32 devices in a mesh: dp: 8 (over y, x, core), tp: 4 (over z).
Axes of the slice: x: 2, y: 2, z: 4, core: 2. Of those that a mesh axis runs over, the one named last changes fastest.
Arguments:
- tokens: bfloat16 [8192, 1536], P('dp'), may hold values from -6 to 6
- lengths: int32 [8], P('dp'), may hold values from 1 to 1024, as said below
- positions: int32 [8192], P('dp'), may hold values from 0 to 2046, as said below
- cotangent: bfloat16 [8192, 1536], P('dp'), may hold values from -6 to 6
- norm_gain: float32 [1536], replicated, may hold values from 0.5 to 1.5
- w_query: bfloat16 [1536, 1536], P(None, 'tp'), may hold values from -0.15625 to 0.15625
- w_key: bfloat16 [1536, 768], P(None, 'tp'), may hold values from -0.15625 to 0.15625
- w_value: bfloat16 [1536, 768], P(None, 'tp'), may hold values from -0.15625 to 0.15625
- w_out: bfloat16 [1536, 1536], P('tp'), may hold values from -0.625 to 0.625
- mlp_gain: float32 [1536], replicated, may hold values from 0.5 to 1.5
- w_gate: bfloat16 [1536, 4096], P(None, 'tp'), may hold values from -0.15625 to 0.15625
- w_up: bfloat16 [1536, 4096], P(None, 'tp'), may hold values from -0.15625 to 0.15625
- w_down: bfloat16 [4096, 1536], P('tp'), may hold values from -0.09375 to 0.09375
Outputs:
- layer_out: bfloat16 [8192, 1536], P(('dp', 'tp'))
- input_grad: bfloat16 [8192, 1536], P('dp')
- norm_gain_grad: float32 [1536], P('dp')
- w_query_grad: float32 [1536, 1536], P('dp', 'tp')
- w_key_grad: float32 [1536, 768], P('dp', 'tp')
- w_value_grad: float32 [1536, 768], P('dp', 'tp')
- w_out_grad: float32 [1536, 1536], P('tp', 'dp')
- mlp_gain_grad: float32 [1536], P('dp')
- w_gate_grad: float32 [1536, 4096], P('dp', 'tp')
- w_up_grad: float32 [1536, 4096], P('dp', 'tp')
- w_down_grad: float32 [4096, 1536], P('tp', 'dp')
The draws below stay inside these ranges and needn't reach their ends.
Inputs may be any that keep to these rules, and one draw needn't show every extreme that they name: `lengths`: each sequence's length; at least one sequence has exactly 1024. Within each sequence positions start at 0 and rise by 1 or 2 from one token to the next; in one sequence every step is 2.
All inputs are finite; a program needn't handle non-finite values.
Results may differ from the reference program's by a relative error of at most 0.015.
Values sent between devices are 32-bit elements; how exact they have to be, the bound alone decides.
No kernel may reach another device: no remote copies, remote signals or barrier semaphores. Data moves between devices by JAX's collectives and lax.ppermute only.
A program may use at most 192 MiB of HBM per device.

```python
import jax
import jax.numpy as jnp
from jax import lax

D = 1536
HEADS = 16
KV = 8
HD = 96
FF = 4096
SEQ = 1024
TOKENS = 8192
N_DP = 8


def draw_lengths(key, part):
    key = jax.random.fold_in(key, 11)
    key_kind, key_long, key_short, key_pick = jax.random.split(key, 4)
    kinds = jax.random.randint(key_kind, (N_DP,), 0, 4)
    long_len = jax.random.randint(key_long, (N_DP,), SEQ * 3 // 4, SEQ + 1)
    short_len = jax.random.randint(key_short, (N_DP,), max(1, SEQ * 300 // 8192), SEQ + 1)
    picked = jax.random.randint(key_pick, (), 0, N_DP)
    result = jnp.where(kinds > 0, long_len, short_len)
    result = jnp.where(jnp.arange(N_DP) == picked, SEQ, result)
    return result.astype(jnp.int32)


def draw_positions(key, part):
    key = jax.random.fold_in(key, 23)
    key_coins, key_pick = jax.random.split(key, 2)
    coins = jax.random.randint(key_coins, (N_DP, SEQ), 0, 4)
    picked = jax.random.randint(key_pick, (), 0, N_DP)
    increments = jnp.where(coins == 0, 2, 1)
    increments = jnp.where((jnp.arange(N_DP) == picked)[:, None], 2, increments)
    increments = jnp.where(jnp.arange(SEQ)[None, :] == 0, 0, increments)
    return jnp.cumsum(increments, axis=1).reshape(TOKENS).astype(jnp.int32)


def shard_levels(key, shape, shards, smallest, high):
    factor_of = 1.0
    for position, blocks in shards:
        heights = jax.random.uniform(jax.random.fold_in(jax.random.fold_in(key, 6), position), (blocks,), jnp.float32, smallest / len(shards), high / len(shards))
        factor_of = factor_of * jnp.repeat(jnp.exp(heights), shape[position] // blocks).reshape((-1,) + (1,) * (len(shape) - 1 - position))
    return factor_of


def gaussian(key, dims, deviation, bound, shards=(), held_as=jnp.bfloat16):
    array = jax.random.normal(key, dims, jnp.float32) * deviation
    if len(shards) > 0:
        array = shard_levels(key, dims, shards, -0.22, 0.18) * array
    return jnp.clip(array, min=-bound, max=bound).astype(held_as)


def setup_inputs(seed: int = 0) -> dict:
    arg_keys = jax.random.split(jax.random.key(seed), 14)
    tokens = gaussian(arg_keys[0], (TOKENS, D), 1.0, 6.0, ((0, 8),))
    lengths = draw_lengths(jax.random.fold_in(arg_keys[13], 71), 0)
    positions = draw_positions(jax.random.fold_in(arg_keys[13], 71), 0)
    cotangent = gaussian(arg_keys[3], (TOKENS, D), 1.0, 6.0, ((0, 8),))
    norm_gain = jnp.clip(1.0 + 0.1 * jax.random.normal(arg_keys[4], (D,), jnp.float32), 0.5, 1.5)
    w_query = gaussian(arg_keys[5], (D, HEADS * HD), D ** -0.5, 0.15625, ((1, 4),))
    w_key = gaussian(arg_keys[6], (D, KV * HD), D ** -0.5, 0.15625, ((1, 4),))
    w_value = gaussian(arg_keys[7], (D, KV * HD), D ** -0.5, 0.15625, ((1, 4),))
    w_out = gaussian(arg_keys[8], (HEADS * HD, D), (HEADS * HD // 16) ** -0.5, 0.625, ((0, 4),))
    mlp_gain = jnp.clip(1.0 + 0.1 * jax.random.normal(arg_keys[9], (D,), jnp.float32), 0.5, 1.5)
    w_gate = gaussian(arg_keys[10], (D, FF), D ** -0.5, 0.15625, ((1, 4),))
    w_up = gaussian(arg_keys[11], (D, FF), D ** -0.5, 0.15625, ((1, 4),))
    w_down = gaussian(arg_keys[12], (FF, D), FF ** -0.5, 0.09375, ((0, 4),))
    return {"tokens": tokens, "lengths": lengths, "positions": positions, "cotangent": cotangent, "norm_gain": norm_gain, "w_query": w_query, "w_key": w_key, "w_value": w_value, "w_out": w_out, "mlp_gain": mlp_gain, "w_gate": w_gate, "w_up": w_up, "w_down": w_down}


rope_base = 100000.0
norm_eps = 1e-05
masked_score = -1e+30

@jax.custom_vjp
def low(v):
    return lax.optimization_barrier(v.astype(jnp.bfloat16)).astype(jnp.float32)

@jax.custom_vjp
def low_back(v):
    return v

def low_keep(v):
    return (low(v), None)

def low_pass(kept, grad):
    return (grad,)

def back_keep(v):
    return (v, None)

def back_low(kept, grad):
    return (low(grad),)
low.defvjp(low_keep, low_pass)
low_back.defvjp(back_keep, back_low)

def rope_tables(places):
    half_dim = HD // 2
    freqs = rope_base ** (-(jnp.arange(half_dim).astype(jnp.float32) * 2.0 / HD))
    angles = places.astype(jnp.float32)[:, None] * freqs[None, :]
    cosines = jnp.cos(angles)
    sines = jnp.sin(angles)
    return (jnp.concatenate([cosines, cosines], -1), jnp.concatenate([sines, sines], -1))

def rotate(values, cosines, sines):
    half_dim = HD // 2
    turned = jnp.concatenate([-values[..., half_dim:], values[..., :half_dim]], -1)
    return values * cosines[:, None, :] + turned * sines[:, None, :]

def layer(inputs, norm_gain, w_query, w_key, w_value, w_out, mlp_gain, w_gate, w_up, w_down, cosines, sines, length):
    highest = lax.Precision.HIGHEST
    rows = inputs.shape[0]
    rms_one = lax.rsqrt(lax.optimization_barrier(jnp.mean(inputs * inputs, -1, keepdims=True)) + norm_eps)
    normed_one = low(inputs * rms_one * norm_gain)
    queries = low(rotate(low_back(jnp.dot(normed_one, w_query, precision=highest)).reshape(rows, HEADS, HD), cosines, sines))
    keys_rot = low(rotate(low_back(jnp.dot(normed_one, w_key, precision=highest)).reshape(rows, KV, HD), cosines, sines))
    values_kv = low(low_back(jnp.dot(normed_one, w_value, precision=highest))).reshape(rows, KV, HD)
    grouped = queries.reshape(rows, KV, HEADS // KV, HD)
    raw_scores = jnp.einsum('qkgd,tkd->kgqt', grouped, keys_rot, precision=highest)
    scores = low_back(raw_scores) * HD ** (-0.5)
    places = jnp.arange(rows)
    allowed = (places[None, :] <= places[:, None]) & (places < length)[None, :]
    scores = jnp.where(allowed, scores, masked_score)
    probs = low(jax.nn.softmax(scores, axis=-1))
    mixed = jnp.einsum('kgqt,tkd->qkgd', probs, values_kv, precision=highest).reshape(rows, HEADS * HD)
    mixed = low_back(low(mixed))
    hidden = inputs + low_back(jnp.dot(mixed, w_out, precision=highest))
    rms_two = lax.rsqrt(lax.optimization_barrier(jnp.mean(hidden * hidden, -1, keepdims=True)) + norm_eps)
    normed_two = low(hidden * rms_two * mlp_gain)
    gate_val = low_back(jnp.dot(normed_two, w_gate, precision=highest))
    up_val = low_back(jnp.dot(normed_two, w_up, precision=highest))
    activ = low(jax.nn.silu(gate_val) * up_val)
    return hidden + low_back(jnp.dot(activ, w_down, precision=highest))

def reference(tokens, lengths, positions, cotangent, norm_gain, w_query, w_key, w_value, w_out, mlp_gain, w_gate, w_up, w_down):
    weights = tuple((item.astype(jnp.float32) for item in (norm_gain, w_query, w_key, w_value, w_out, mlp_gain, w_gate, w_up, w_down)))
    inputs = tokens.astype(jnp.float32).reshape(N_DP, SEQ, D)
    cotans = cotangent.astype(jnp.float32).reshape(N_DP, SEQ, D)
    places = positions.reshape(N_DP, SEQ)

    def one_sequence(totals, item):
        seq_in, seq_cot, seq_places, length = item
        cosines, sines = rope_tables(seq_places)

        def forward(seq_x, *params):
            return layer(seq_x, *params, cosines, sines, length)
        output, pull = jax.vjp(forward, seq_in, *weights)
        live = (jnp.arange(SEQ) < length).astype(jnp.float32)
        grads = pull(seq_cot * live[:, None])
        totals = tuple((acc + grad for acc, grad in zip(totals, grads[1:])))
        return (totals, (output.astype(jnp.bfloat16), grads[0].astype(jnp.bfloat16)))
    start = tuple((jnp.zeros(item.shape, jnp.float32) for item in weights))
    finals, (outputs, input_grads) = lax.scan(one_sequence, start, (inputs, cotans, places, lengths))
    return (outputs.reshape(TOKENS, D), input_grads.reshape(TOKENS, D), finals[0], finals[1], finals[2], finals[3], finals[4], finals[5], finals[6], finals[7], finals[8])
```

```python
import functools

import jax
import jax.numpy as jnp
from jax import lax
from jax.experimental import pallas as pl
from jax.experimental.pallas import tpu as pltpu
from jax.sharding import PartitionSpec as P

HD = 96
LANES = 128
rope_base = 100000.0
norm_eps = 1e-05
masked_score = -1e30
score_scale = HD ** (-0.5)
score_scale_log2 = score_scale * 1.4426950408889634
CHUNKS = 4
VMEM_BYTES = 48 * 1024 * 1024
NT = (((1,), (1,)), ((), ()))


def params():
    return pltpu.CompilerParams(vmem_limit_bytes=VMEM_BYTES)


def dot32(a, b):
    return jnp.dot(a, b, preferred_element_type=jnp.float32)


def dot32_nt(a, b):
    return lax.dot_general(a, b, NT, preferred_element_type=jnp.float32)


def place_halves(heads):
    source = jnp.arange(heads * HD)
    entry = source % HD
    half_dim = HD // 2
    lane = (entry // half_dim) * (LANES // 2) + entry % half_dim
    return (source // HD) * LANES + lane


def place_plain(heads):
    source = jnp.arange(heads * HD)
    return (source // HD) * LANES + source % HD


def placement(lanes, width):
    return (lanes[:, None] == jnp.arange(width)[None, :]).astype(jnp.bfloat16)


def line_flags():
    level = lax.axis_index("tp")
    return level % 2 == 1, level < 2, (level == 1) | (level == 2)


def line_sum(part):
    _, _, inner = line_flags()
    total = part + lax.ppermute(part, "tp", [(0, 1), (3, 2)])
    total = total + lax.ppermute(total, "tp", [(1, 2), (2, 1)])
    outer = lax.ppermute(total, "tp", [(1, 0), (2, 3)])
    return jnp.where(inner, total, outer)


def line_gather(part):
    odd, _, inner = line_flags()
    other = lax.ppermute(part, "tp", [(0, 1), (1, 0), (2, 3), (3, 2)])
    pair = jnp.where(
        odd, jnp.concatenate([other, part], 1), jnp.concatenate([part, other], 1)
    )
    across = lax.ppermute(pair, "tp", [(1, 2), (2, 1)])
    outer = lax.ppermute(across, "tp", [(1, 0), (2, 3)])
    return pair, across, outer


def line_scatter(parts):
    _, low, inner = line_flags()
    rows = parts[0].shape[0]
    away = jnp.where(
        low,
        jnp.concatenate([parts[2], parts[3]], 0),
        jnp.concatenate([parts[1], parts[0]], 0),
    )
    total = away + lax.ppermute(away, "tp", [(0, 1), (3, 2)])
    across = lax.ppermute(total, "tp", [(1, 2), (2, 1)])
    near = jnp.where(low, parts[1], parts[2])
    edge = jnp.where(low, parts[0], parts[3])
    last = lax.ppermute(
        jnp.where(inner, edge + across[rows:], near), "tp", [(0, 1), (1, 0), (2, 3), (3, 2)]
    )
    return jnp.where(inner, near + across[:rows], edge) + last


def spread_kernel(keep_plain, source_ref, place_ref, *out_refs):
    parts, _, rows, width = source_ref.shape
    block = source_ref[...].reshape(parts * rows, width).astype(jnp.bfloat16)
    out_refs[0][...] = dot32(block, place_ref[...]).astype(jnp.bfloat16)
    if keep_plain:
        out_refs[1][...] = block


def spread(gathered, place, keep_plain):
    dp, tp, rows, width = gathered.shape
    parts = max(1, dp // 4)
    wide = place.shape[1]
    shapes = [jax.ShapeDtypeStruct((dp * rows, tp * wide), jnp.bfloat16)]
    specs = [pl.BlockSpec((parts * rows, wide), lambda i, t: (i, t))]
    if keep_plain:
        shapes.append(jax.ShapeDtypeStruct((dp * rows, tp * width), jnp.bfloat16))
        specs.append(pl.BlockSpec((parts * rows, width), lambda i, t: (i, t)))
    return pl.pallas_call(
        functools.partial(spread_kernel, keep_plain),
        out_shape=shapes,
        grid=(dp // parts, tp),
        in_specs=[
            pl.BlockSpec((parts, 1, rows, width), lambda i, t: (i, t, 0, 0)),
            pl.BlockSpec((width, wide), lambda i, t: (0, 0)),
        ],
        out_specs=specs,
        compiler_params=params(),
        cost_estimate=pl.CostEstimate(
            flops=2 * dp * rows * tp * width * wide,
            bytes_accessed=dp * rows * tp * (4 * width + 2 * wide),
            transcendentals=0,
        ),
    )(gathered, place)


def project_kernel(x_ref, w_ref, cos_ref, sin_ref, out_ref):
    lin = dot32(x_ref[...], w_ref[...])
    cosines = cos_ref[0]
    sines = sin_ref[0]
    for h in range(lin.shape[1] // LANES):
        here = slice(h * LANES, (h + 1) * LANES)
        one = lin[:, here]
        turned = one * cosines + pltpu.roll(one, LANES // 2, 1) * sines
        out_ref[:, here] = turned.astype(jnp.bfloat16)


def project(normed, weights, cosines, sines):
    rows, depth = normed.shape
    width = weights.shape[1]
    block = 2 * LANES
    table = lambda i: (jnp.where(i % 4 == 3, 1, 0), 0, 0)
    return pl.pallas_call(
        project_kernel,
        out_shape=jax.ShapeDtypeStruct((rows, width), jnp.bfloat16),
        grid=(width // block,),
        in_specs=[
            pl.BlockSpec((rows, depth), lambda i: (0, 0)),
            pl.BlockSpec((depth, block), lambda i: (0, i)),
            pl.BlockSpec((1, rows, LANES), table),
            pl.BlockSpec((1, rows, LANES), table),
        ],
        out_specs=pl.BlockSpec((rows, block), lambda i: (0, i)),
        compiler_params=params(),
        cost_estimate=pl.CostEstimate(
            flops=2 * rows * depth * width,
            bytes_accessed=2 * (rows * depth + depth * width + rows * width),
            transcendentals=0,
        ),
    )(normed, weights, cosines, sines)


def allowed_mask(length_ref, start, keys, rows):
    row_ids = start + lax.broadcasted_iota(jnp.int32, (1, rows), 1)
    limit = jnp.minimum(row_ids, length_ref[0] - 1)
    return lax.broadcasted_iota(jnp.int32, (keys, rows), 0) <= limit


def softmax_columns(keys, query, allowed):
    raw = jnp.where(allowed, dot32_nt(keys, query), masked_score)
    peak = jnp.max(raw, axis=0, keepdims=True)
    expo = jnp.exp2((raw - peak) * score_scale_log2)
    return expo * (1.0 / jnp.sum(expo, axis=0, keepdims=True))


def attend_kernel(start, length_ref, q_ref, k_ref, v_ref, strip_ref, out_ref):
    rows = q_ref.shape[0]
    keys = k_ref.shape[0]
    kv_heads = k_ref.shape[1] // LANES
    group = q_ref.shape[1] // LANES // kv_heads
    allowed = allowed_mask(length_ref, start, keys, rows)
    mixed = []
    for kv in range(kv_heads):
        key = k_ref[:, kv * LANES : (kv + 1) * LANES]
        value_t = v_ref[:, kv * LANES : (kv + 1) * LANES].T
        for g in range(group):
            h = kv * group + g
            query = q_ref[:, h * LANES : (h + 1) * LANES]
            probs = softmax_columns(key, query, allowed).astype(jnp.bfloat16)
            mixed.append(dot32(value_t, probs).T.astype(jnp.bfloat16))
    out_ref[...] = dot32(jnp.concatenate(mixed, 1), strip_ref[...])


def attend(length, qkv, strip, index, rows):
    keys = (index + 1) * rows
    width = qkv.shape[1]
    heads = width // 2 // LANES
    return pl.pallas_call(
        functools.partial(attend_kernel, index * rows),
        out_shape=jax.ShapeDtypeStruct((rows, strip.shape[1]), jnp.float32),
        grid=(1,),
        in_specs=[
            pl.BlockSpec(memory_space=pltpu.SMEM),
            pl.BlockSpec((rows, width // 2), lambda i: (index, 0)),
            pl.BlockSpec((keys, width // 4), lambda i: (0, 2)),
            pl.BlockSpec((keys, width // 4), lambda i: (0, 3)),
            pl.BlockSpec(strip.shape, lambda i: (0, 0)),
        ],
        out_specs=pl.BlockSpec((rows, strip.shape[1]), lambda i: (0, 0)),
        compiler_params=params(),
        cost_estimate=pl.CostEstimate(
            flops=4 * heads * rows * keys * LANES,
            bytes_accessed=2 * (rows + keys) * width,
            transcendentals=heads * rows * keys,
        ),
    )(length, qkv, qkv, qkv, strip)


def residual_kernel(level_ref, pair_ref, across_ref, outer_ref, x_ref, w_ref, gain_ref, *outs):
    hidden_ref, rms_ref, normed_ref = outs
    level = level_ref[0]
    inner = (level == 1) | (level == 2)
    far = jnp.where(inner, across_ref[...], outer_ref[...])
    pair = pair_ref[...]
    low = level < 2
    mixed = jnp.concatenate(
        [jnp.where(low, pair, far), jnp.where(low, far, pair)], axis=1
    ).astype(jnp.bfloat16)
    hidden = x_ref[...].astype(jnp.float32) + dot32_nt(mixed, w_ref[...])
    hidden_ref[...] = hidden
    rms = lax.rsqrt(jnp.mean(hidden * hidden, -1, keepdims=True) + norm_eps)
    rms_ref[...] = rms
    normed_ref[...] = (hidden * rms * gain_ref[...]).astype(jnp.bfloat16)


def residual(level, gathered, tokens, weights, gain, index, rows):
    depth = tokens.shape[1]
    whole = lambda array: pl.BlockSpec(array.shape, lambda i: (0, 0))
    gain = gain[None, :]
    return pl.pallas_call(
        residual_kernel,
        out_shape=(
            jax.ShapeDtypeStruct((rows, depth), jnp.float32),
            jax.ShapeDtypeStruct((rows, 1), jnp.float32),
            jax.ShapeDtypeStruct((rows, depth), jnp.bfloat16),
        ),
        grid=(1,),
        in_specs=[pl.BlockSpec(memory_space=pltpu.SMEM)]
        + [whole(array) for array in gathered]
        + [pl.BlockSpec((rows, depth), lambda i: (index, 0)), whole(weights), whole(gain)],
        out_specs=(
            pl.BlockSpec((rows, depth), lambda i: (0, 0)),
            pl.BlockSpec((rows, 1), lambda i: (0, 0)),
            pl.BlockSpec((rows, depth), lambda i: (0, 0)),
        ),
        compiler_params=params(),
        cost_estimate=pl.CostEstimate(
            flops=2 * rows * depth * weights.shape[1],
            bytes_accessed=2 * depth * weights.shape[1] + 14 * rows * depth,
            transcendentals=0,
        ),
    )(level, *gathered, tokens, weights, gain)


def attend_back_kernel(start, length_ref, q_ref, k_ref, v_ref, dm_ref, cos_ref, sin_ref, *refs):
    rows = q_ref.shape[0]
    keys = k_ref.shape[0]
    kv_heads = k_ref.shape[1] // LANES
    group = q_ref.shape[1] // LANES // kv_heads
    last = keys == rows + start and len(refs) == (2 if start > 0 else 1)
    acc_ref = None if last else refs[0]
    out_ref = refs[0] if last else refs[1]
    acc_out_ref = refs[-1]
    allowed = allowed_mask(length_ref, start, keys, rows)
    cosines = cos_ref[0]
    sines = sin_ref[0]

    def rotate_back(grads):
        return (grads * cosines - pltpu.roll(grads, LANES // 2, 1) * sines).astype(jnp.bfloat16)

    wide = kv_heads * LANES
    for kv in range(kv_heads):
        here = slice(kv * LANES, (kv + 1) * LANES)
        there = slice(wide + kv * LANES, wide + (kv + 1) * LANES)
        key = k_ref[:, here]
        value = v_ref[:, here]
        key_t = key.T
        dkey = None
        dvalue = None
        for g in range(group):
            h = kv * group + g
            lanes = slice(h * LANES, (h + 1) * LANES)
            query = q_ref[:, lanes]
            dmixed = dm_ref[:, lanes]
            probs = softmax_columns(key, query, allowed)
            dprobs = dot32_nt(value, dmixed)
            row_dot = jnp.sum(dprobs * probs, axis=0, keepdims=True)
            dscores = (probs * (dprobs - row_dot)).astype(jnp.bfloat16)
            dquery = dot32(key_t, dscores).T * score_scale
            out_ref[:, lanes] = rotate_back(dquery)
            dkey_one = dot32(dscores, query)
            dvalue_one = dot32(probs.astype(jnp.bfloat16), dmixed)
            dkey = dkey_one if dkey is None else dkey + dkey_one
            dvalue = dvalue_one if dvalue is None else dvalue + dvalue_one
        if acc_ref is not None:
            dkey = dkey + acc_ref[:, here]
            dvalue = dvalue + acc_ref[:, there]
        if start > 0:
            acc_out_ref[:, here] = dkey[:start]
            acc_out_ref[:, there] = dvalue[:start]
        base = kv_heads * group * LANES
        out_ref[:, base + kv * LANES : base + (kv + 1) * LANES] = rotate_back(
            dkey[start:] * score_scale
        )
        out_ref[:, base + wide + kv * LANES : base + wide + (kv + 1) * LANES] = dvalue[
            start:
        ].astype(jnp.bfloat16)


def attend_back(length, qkv, dmixed, cosines, sines, sums, index, rows, shards):
    start = index * rows
    keys = start + rows
    width = qkv.shape[1] // shards
    in_specs = [
        pl.BlockSpec(memory_space=pltpu.SMEM),
        pl.BlockSpec((rows, width // 2), lambda t: (index, 2 * t)),
        pl.BlockSpec((keys, width // 4), lambda t: (0, 4 * t + 2)),
        pl.BlockSpec((keys, width // 4), lambda t: (0, 4 * t + 3)),
        pl.BlockSpec((rows, width // 2), lambda t: (0, t)),
        pl.BlockSpec((1, rows, LANES), lambda t: (0, index, 0)),
        pl.BlockSpec((1, rows, LANES), lambda t: (0, index, 0)),
    ]
    args = [length, qkv, qkv, qkv, dmixed, cosines, sines]
    if sums is not None:
        in_specs.append(pl.BlockSpec((keys, width // 2), lambda t: (0, t)))
        args.append(sums)
    shapes = [jax.ShapeDtypeStruct((rows, qkv.shape[1]), jnp.bfloat16)]
    out_specs = [pl.BlockSpec((rows, width), lambda t: (0, t))]
    if start > 0:
        shapes.append(jax.ShapeDtypeStruct((start, qkv.shape[1] // 2), jnp.float32))
        out_specs.append(pl.BlockSpec((start, width // 2), lambda t: (0, t)))
    heads = qkv.shape[1] // 2 // LANES
    outs = pl.pallas_call(
        functools.partial(attend_back_kernel, start),
        out_shape=shapes,
        grid=(shards,),
        in_specs=in_specs,
        out_specs=out_specs,
        compiler_params=params(),
        cost_estimate=pl.CostEstimate(
            flops=10 * heads * rows * keys * LANES,
            bytes_accessed=2 * (rows + keys) * qkv.shape[1] + 8 * keys * qkv.shape[1] // 2,
            transcendentals=heads * rows * keys,
        ),
    )(*args)
    return outs[0], (outs[1] if start > 0 else None)


def norm_back(inputs, rms_vals, gain, dnormed):
    scaled = dnormed * gain
    dinputs = rms_vals * scaled - inputs * rms_vals**3 * jnp.mean(
        scaled * inputs, -1, keepdims=True
    )
    dgain = jnp.sum(dnormed * inputs * rms_vals, 0)
    return (dinputs, dgain)


def shards(
    tokens,
    lengths,
    positions,
    cotangent,
    norm_gain,
    w_query,
    w_key,
    w_value,
    w_out,
    mlp_gain,
    w_gate,
    w_up,
    w_down,
):
    seq_rows, depth = tokens.shape
    dp = lax.axis_size("dp")
    tp = lax.axis_size("tp")
    dp_index = lax.axis_index("dp")
    tp_index = lax.axis_index("tp")
    heads_here = w_query.shape[1] // HD
    kv_here = w_key.shape[1] // HD
    rows = seq_rows // CHUNKS
    slice_rows = depth // dp
    q_wide = heads_here * LANES
    kv_wide = kv_here * LANES
    shard_wide = q_wide + 2 * kv_wide

    place_qkv = placement(
        jnp.concatenate(
            [
                place_halves(heads_here),
                q_wide + place_halves(kv_here),
                q_wide + kv_wide + place_plain(kv_here),
            ]
        ),
        shard_wide,
    )
    place_out = placement(place_plain(heads_here), q_wide)

    w_qkv = jnp.concatenate([w_query, w_key, w_value], 1)
    out_slice = lax.dynamic_slice_in_dim(w_out, dp_index * slice_rows, slice_rows, 1).T
    out_all = lax.all_gather(out_slice.astype(jnp.float32), ("dp", "tp"))
    qkv_slice = lax.dynamic_slice_in_dim(w_qkv, dp_index * slice_rows, slice_rows, 0)
    qkv_all_w = lax.all_gather(qkv_slice.astype(jnp.float32), ("dp", "tp"))
    out_pad, out_t = spread(
        out_all.reshape(dp, tp, slice_rows, heads_here * HD), place_out, True
    )
    (qkv_pad,) = spread(qkv_all_w.reshape(dp, tp, slice_rows, -1), place_qkv, False)

    half_dim = HD // 2
    freqs = rope_base ** (-(jnp.arange(half_dim).astype(jnp.float32) * 2.0 / HD))
    freqs = jnp.pad(freqs, (0, LANES // 2 - half_dim))
    angles = positions.astype(jnp.float32)[:, None] * jnp.concatenate([freqs, freqs])[None, :]
    sign = jnp.where(jnp.arange(LANES) < LANES // 2, -1.0, 1.0)
    cosines = jnp.cos(angles)
    sines = jnp.sin(angles) * sign
    cosines = jnp.stack([cosines, jnp.ones_like(cosines)])
    sines = jnp.stack([sines, jnp.zeros_like(sines)])

    inputs = tokens.astype(jnp.float32)
    rms_one = lax.rsqrt(jnp.mean(inputs * inputs, -1, keepdims=True) + norm_eps)
    normed_one = (inputs * rms_one * norm_gain).astype(jnp.bfloat16)
    own_pad = dot32(w_qkv, place_qkv).astype(jnp.bfloat16)
    qkv_own = project(normed_one, own_pad, cosines, sines)

    live = (jnp.arange(seq_rows) < lengths[0]).astype(jnp.float32)
    dout = cotangent.astype(jnp.float32) * live[:, None]
    dout_low = dout.astype(jnp.bfloat16)

    order = list(reversed(range(CHUNKS)))
    cut = lambda array, j: array[j * rows : (j + 1) * rows]

    level = tp_index.astype(jnp.int32).reshape(1)
    mixed_own = {}
    mixed = {}
    for j in order:
        mixed_own[j] = attend(lengths, qkv_own, place_out.T, j, rows)
        mixed[j] = line_gather(mixed_own[j])

    dactiv = dot32_nt(dout_low, w_down)
    hidden = {}
    rms_two = {}
    normed_two = {}
    activ = {}
    dgate = {}
    dup = {}
    mlp_part = {}
    dnormed_two = {}
    for j in order:
        hidden[j], rms_two[j], normed_two[j] = residual(
            level, mixed[j], tokens, out_t, mlp_gain, j, rows
        )
        gate_val = dot32(normed_two[j], w_gate)
        up_val = dot32(normed_two[j], w_up)
        sigmoid_gate = jax.nn.sigmoid(gate_val)
        silu_gate = gate_val * sigmoid_gate
        activ[j] = (silu_gate * up_val).astype(jnp.bfloat16)
        mlp_part[j] = dot32(activ[j], w_down)
        dact = cut(dactiv, j)
        dgate[j] = (dact * up_val * sigmoid_gate * (1.0 + gate_val * (1.0 - sigmoid_gate))).astype(
            jnp.bfloat16
        )
        dup[j] = (dact * silu_gate).astype(jnp.bfloat16)
        part = dot32_nt(dgate[j], w_gate) + dot32_nt(dup[j], w_up)
        half = rows // 2
        dnormed_two[j] = jnp.concatenate([line_sum(part[:half]), line_sum(part[half:])], 0)

    join = lambda pieces: jnp.concatenate([pieces[j] for j in range(CHUNKS)], 0)

    normed_two_all = join(normed_two)
    scatter = lambda array: lax.psum_scatter(array, "dp", scatter_dimension=0, tiled=True)
    grad_gate = scatter(dot32(normed_two_all.T, join(dgate)))
    grad_up = scatter(dot32(normed_two_all.T, join(dup)))
    grad_down = scatter(dot32(dout_low.T, join(activ))).T

    mlp_rows = line_scatter([mlp_part[j] for j in range(CHUNKS)])
    hidden_rows = lax.dynamic_slice_in_dim(
        join(hidden), tp_index * (seq_rows // tp), seq_rows // tp, 0
    )
    layer_out = (hidden_rows + mlp_rows).astype(jnp.bfloat16)

    qkv = project(normed_one, qkv_pad, cosines, sines)
    sums = None
    dhidden_low = {}
    dqkv_own = {}
    input_grad = {}
    gain_one = jnp.zeros((depth,), jnp.float32)
    gain_two = jnp.zeros((depth,), jnp.float32)
    for j in order:
        dnorm, gain_part = norm_back(hidden[j], rms_two[j], mlp_gain, dnormed_two[j])
        gain_two = gain_two + gain_part
        dhidden = cut(dout, j) + dnorm
        dhidden_low[j] = dhidden.astype(jnp.bfloat16)
        dmixed = dot32(dhidden_low[j], out_pad).astype(jnp.bfloat16)
        dqkv, sums = attend_back(lengths, qkv, dmixed, cosines, sines, sums, j, rows, tp)
        dqkv_own[j] = lax.dynamic_slice_in_dim(dqkv, tp_index * shard_wide, shard_wide, 1)
        dnormed_one = dot32_nt(dqkv, qkv_pad)
        dnorm, gain_part = norm_back(cut(inputs, j), cut(rms_one, j), norm_gain, dnormed_one)
        gain_one = gain_one + gain_part
        input_grad[j] = (dhidden + dnorm).astype(jnp.bfloat16)

    dqkv_low = dot32(join(dqkv_own), place_qkv.T).astype(jnp.bfloat16)
    grad_qkv = dot32(normed_one.T, dqkv_low)
    grad_out = dot32(join(dhidden_low).T, join(mixed_own).astype(jnp.bfloat16))
    gains = jnp.pad(jnp.stack([gain_one, gain_two], 1), ((0, 0), (0, LANES - 2)))
    attn = scatter(jnp.concatenate([grad_qkv, grad_out, gains], 1))
    q_cols = heads_here * HD
    kv_cols = kv_here * HD
    ends = [q_cols, q_cols + kv_cols, q_cols + 2 * kv_cols, 2 * q_cols + 2 * kv_cols]
    return (
        layer_out,
        join(input_grad),
        attn[:, ends[3]],
        attn[:, : ends[0]],
        attn[:, ends[0] : ends[1]],
        attn[:, ends[1] : ends[2]],
        attn[:, ends[2] : ends[3]].T,
        attn[:, ends[3] + 1],
        grad_gate,
        grad_up,
        grad_down,
    )


def solution(mesh):
    return jax.shard_map(
        shards,
        mesh=mesh,
        in_specs=(
            P("dp", None),
            P("dp"),
            P("dp"),
            P("dp", None),
            P(),
            P(None, "tp"),
            P(None, "tp"),
            P(None, "tp"),
            P("tp", None),
            P(),
            P(None, "tp"),
            P(None, "tp"),
            P("tp", None),
        ),
        out_specs=(
            P(("dp", "tp"), None),
            P("dp", None),
            P("dp"),
            P("dp", "tp"),
            P("dp", "tp"),
            P("dp", "tp"),
            P("tp", "dp"),
            P("dp"),
            P("dp", "tp"),
            P("dp", "tp"),
            P("tp", "dp"),
        ),
        check_vma=False,
    )
```

```python
import functools

import jax
import jax.numpy as jnp
from jax import lax
from jax.experimental import pallas as pl
from jax.experimental.pallas import tpu as pltpu
from jax.sharding import Mesh
from jax.sharding import PartitionSpec as P

HD = 96
LANES = 128
rope_base = 100000.0
norm_eps = 1e-05
masked_score = -1e30
far_away = 1e30
score_scale = HD ** (-0.5)
score_scale_log2 = score_scale * 1.4426950408889634
CHUNKS = 4
EXTRA = 8
VMEM_BYTES = 48 * 1024 * 1024
NT = (((1,), (1,)), ((), ()))


def params():
    return pltpu.CompilerParams(vmem_limit_bytes=VMEM_BYTES)


def dot32(a, b):
    return jnp.dot(a, b, preferred_element_type=jnp.float32)


def dot32_nt(a, b):
    return lax.dot_general(a, b, NT, preferred_element_type=jnp.float32)


def dot_split(a, places):
    high = a.astype(jnp.bfloat16)
    rest = (a - high.astype(jnp.float32)).astype(jnp.bfloat16)
    return dot32(high, places) + dot32(rest, places)


def fence(tree):
    return lax.optimization_barrier(tree)


def place_halves(heads):
    source = jnp.arange(heads * HD)
    entry = source % HD
    half_dim = HD // 2
    lane = (entry // half_dim) * (LANES // 2) + entry % half_dim
    return (source // HD) * LANES + lane


def place_plain(heads):
    source = jnp.arange(heads * HD)
    return (source // HD) * LANES + source % HD


def placement(lanes, width):
    return (lanes[:, None] == jnp.arange(width)[None, :]).astype(jnp.bfloat16)


PAIRS = [(0, 1), (1, 0), (2, 3), (3, 2)]
INWARD = [(0, 1), (3, 2)]
MIDDLE = [(1, 2), (2, 1)]
OUTWARD = [(1, 0), (2, 3)]


def along(part, pairs):
    return lax.ppermute(part, "tp", pairs)


def spread_kernel(meta_ref, mine_ref, theirs_ref, own_ref, place_ref, *out_refs):
    side = pl.program_id(0)
    shard = pl.program_id(2)
    far = jnp.where(side == 0, mine_ref[0, 0], theirs_ref[0, 0]).astype(jnp.bfloat16)
    block = jnp.where(shard == 0, own_ref[...], far)
    out_refs[0][...] = dot32(block, place_ref[...]).astype(jnp.bfloat16)
    if len(out_refs) > 1:
        out_refs[1][...] = block


def spread(meta, mine, theirs, own, place, keep_plain):
    chips, others, rows, width = mine.shape
    wide = place.shape[1]
    total = own.shape[0]

    def row_block(c, m, meta):
        return (meta[0] ^ m) * 2 + (meta[1] ^ c)

    def far_map(side):
        def index(c, m, s, meta):
            here = c == side
            hold = (chips - 1, others - 1) if side == 0 else (0, 0)
            return (
                jnp.where(here, m, hold[0]),
                jnp.where(here, jnp.maximum(s - 1, 0), hold[1]),
                0,
                0,
            )

        return index

    out_map = lambda c, m, s, meta: (row_block(c, m, meta), meta[2 + s])
    shapes = [jax.ShapeDtypeStruct((total, 4 * wide), jnp.bfloat16)]
    specs = [pl.BlockSpec((rows, wide), out_map)]
    if keep_plain:
        shapes.append(jax.ShapeDtypeStruct((total, 4 * width), jnp.bfloat16))
        specs.append(pl.BlockSpec((rows, width), out_map))
    return pl.pallas_call(
        spread_kernel,
        out_shape=shapes,
        grid_spec=pltpu.PrefetchScalarGridSpec(
            num_scalar_prefetch=1,
            grid=(2, chips, 4),
            in_specs=[
                pl.BlockSpec((1, 1, rows, width), far_map(0)),
                pl.BlockSpec((1, 1, rows, width), far_map(1)),
                pl.BlockSpec((rows, width), lambda c, m, s, meta: (row_block(c, m, meta), 0)),
                pl.BlockSpec((width, wide), lambda c, m, s, meta: (0, 0)),
            ],
            out_specs=specs,
        ),
        compiler_params=params(),
        cost_estimate=pl.CostEstimate(
            flops=8 * total * width * wide,
            bytes_accessed=total * (16 * width + 8 * wide),
            transcendentals=0,
        ),
    )(meta, mine, theirs, own, place)


def spread_all_kernel(source_ref, place_ref, *out_refs):
    parts, _, rows, width = source_ref.shape
    block = source_ref[...].reshape(parts * rows, width).astype(jnp.bfloat16)
    out_refs[0][...] = dot32(block, place_ref[...]).astype(jnp.bfloat16)
    if len(out_refs) > 1:
        out_refs[1][...] = block


def spread_all(gathered, place, keep_plain):
    dp, tp, rows, width = gathered.shape
    parts = max(1, dp // 4)
    wide = place.shape[1]
    shapes = [jax.ShapeDtypeStruct((dp * rows, tp * wide), jnp.bfloat16)]
    specs = [pl.BlockSpec((parts * rows, wide), lambda i, t: (i, t))]
    if keep_plain:
        shapes.append(jax.ShapeDtypeStruct((dp * rows, tp * width), jnp.bfloat16))
        specs.append(pl.BlockSpec((parts * rows, width), lambda i, t: (i, t)))
    return pl.pallas_call(
        spread_all_kernel,
        out_shape=shapes,
        grid=(dp // parts, tp),
        in_specs=[
            pl.BlockSpec((parts, 1, rows, width), lambda i, t: (i, t, 0, 0)),
            pl.BlockSpec((width, wide), lambda i, t: (0, 0)),
        ],
        out_specs=specs,
        compiler_params=params(),
        cost_estimate=pl.CostEstimate(
            flops=2 * dp * rows * tp * width * wide,
            bytes_accessed=dp * rows * tp * (4 * width + 2 * wide),
            transcendentals=0,
        ),
    )(gathered, place)


def project_kernel(x_ref, w_ref, cos_ref, sin_ref, out_ref):
    part = 256
    for r in range(x_ref.shape[0] // part):
        rows = slice(r * part, (r + 1) * part)
        lin = dot32(x_ref[rows, :], w_ref[...])
        cosines = cos_ref[0, rows, :]
        sines = sin_ref[0, rows, :]
        for h in range(lin.shape[1] // LANES):
            here = slice(h * LANES, (h + 1) * LANES)
            one = lin[:, here]
            turned = one * cosines + pltpu.roll(one, LANES // 2, 1) * sines
            out_ref[rows, here] = turned.astype(jnp.bfloat16)


def project(normed, weights, cosines, sines):
    rows, depth = normed.shape
    width = weights.shape[1]
    block = 2 * LANES
    table = lambda i: (jnp.where(i % 4 == 3, 1, 0), 0, 0)
    return pl.pallas_call(
        project_kernel,
        out_shape=jax.ShapeDtypeStruct((rows, width), jnp.bfloat16),
        grid=(width // block,),
        in_specs=[
            pl.BlockSpec((rows, depth), lambda i: (0, 0)),
            pl.BlockSpec((depth, block), lambda i: (0, i)),
            pl.BlockSpec((1, rows, LANES), table),
            pl.BlockSpec((1, rows, LANES), table),
        ],
        out_specs=pl.BlockSpec((rows, block), lambda i: (0, i)),
        compiler_params=params(),
        cost_estimate=pl.CostEstimate(
            flops=2 * rows * depth * width,
            bytes_accessed=2 * (rows * depth + depth * width + rows * width),
            transcendentals=0,
        ),
    )(normed, weights, cosines, sines)


def attend_kernel(start, length_ref, q_ref, k_ref, v_ref, strip_ref, out_ref):
    rows = q_ref.shape[0]
    keys = k_ref.shape[0]
    kv_heads = k_ref.shape[1] // LANES
    group = q_ref.shape[1] // LANES // kv_heads
    length = length_ref[0]
    row_ids = start + lax.broadcasted_iota(jnp.int32, (1, rows), 1)
    limit = jnp.minimum(row_ids, length - 1)
    allowed = lax.broadcasted_iota(jnp.int32, (keys, rows), 0) <= limit
    mixed = []
    sums = []
    for kv in range(kv_heads):
        key = k_ref[:, kv * LANES : (kv + 1) * LANES]
        value_t = v_ref[:, kv * LANES : (kv + 1) * LANES].T
        for g in range(group):
            h = kv * group + g
            query = q_ref[:, h * LANES : (h + 1) * LANES]
            raw = jnp.where(allowed, dot32_nt(key, query), masked_score)
            peak = jnp.max(raw, axis=0, keepdims=True)
            expo = jnp.exp2((raw - peak) * score_scale_log2)
            total = jnp.sum(expo, axis=0, keepdims=True)
            probs = (expo * (1.0 / total)).astype(jnp.bfloat16)
            mixed.append(dot32(value_t, probs).T)
            log_sum = peak * score_scale_log2 + jnp.log2(total)
            sums.append(jnp.where(row_ids < length, log_sum, far_away))
    out_ref[:rows, :] = dot_split(jnp.concatenate(mixed, 1), strip_ref[...])
    out_ref[rows:, :] = jnp.zeros((EXTRA, out_ref.shape[1]), jnp.float32)
    out_ref[rows : rows + len(sums), :rows] = jnp.concatenate(sums, 0)


def attend(length, qkv, strip, index, rows):
    keys = (index + 1) * rows
    width = qkv.shape[1]
    heads = width // 2 // LANES
    return pl.pallas_call(
        functools.partial(attend_kernel, index * rows),
        out_shape=jax.ShapeDtypeStruct((rows + EXTRA, strip.shape[1]), jnp.float32),
        grid=(1,),
        in_specs=[
            pl.BlockSpec(memory_space=pltpu.SMEM),
            pl.BlockSpec((rows, width // 2), lambda i: (index, 0)),
            pl.BlockSpec((keys, width // 4), lambda i: (0, 2)),
            pl.BlockSpec((keys, width // 4), lambda i: (0, 3)),
            pl.BlockSpec(strip.shape, lambda i: (0, 0)),
        ],
        out_specs=pl.BlockSpec((rows + EXTRA, strip.shape[1]), lambda i: (0, 0)),
        compiler_params=params(),
        cost_estimate=pl.CostEstimate(
            flops=4 * heads * rows * keys * LANES,
            bytes_accessed=2 * (rows + keys) * width,
            transcendentals=heads * rows * keys,
        ),
    )(length, qkv, qkv, qkv, strip)


def residual_kernel(level_ref, pair_ref, across_ref, outer_ref, x_ref, w_ref, gain_ref, *outs):
    hidden_ref, rms_ref, normed_ref, mixed_ref = outs
    rows = x_ref.shape[0]
    level = level_ref[0]
    inner = (level == 1) | (level == 2)
    far = jnp.where(inner, across_ref[...], outer_ref[...])
    pair = pair_ref[...]
    low = level < 2
    half = pair.shape[1]
    mixed_ref[:, :half] = jnp.where(low, pair, far)
    mixed_ref[:, half:] = jnp.where(low, far, pair)
    mixed = mixed_ref[:rows, :].astype(jnp.bfloat16)
    hidden = x_ref[...].astype(jnp.float32) + dot32_nt(mixed, w_ref[...])
    hidden_ref[...] = hidden
    rms = lax.rsqrt(jnp.mean(hidden * hidden, -1, keepdims=True) + norm_eps)
    rms_ref[...] = rms
    normed_ref[...] = (hidden * rms * gain_ref[...]).astype(jnp.bfloat16)


def residual(level, gathered, tokens, weights, gain, index, rows):
    depth = tokens.shape[1]
    whole = lambda array: pl.BlockSpec(array.shape, lambda i: (0, 0))
    gain = gain[None, :]
    shapes = (
        jax.ShapeDtypeStruct((rows, depth), jnp.float32),
        jax.ShapeDtypeStruct((rows, 1), jnp.float32),
        jax.ShapeDtypeStruct((rows, depth), jnp.bfloat16),
        jax.ShapeDtypeStruct((rows + EXTRA, weights.shape[1]), jnp.float32),
    )
    return pl.pallas_call(
        residual_kernel,
        out_shape=shapes,
        grid=(1,),
        in_specs=[pl.BlockSpec(memory_space=pltpu.SMEM)]
        + [whole(array) for array in gathered]
        + [pl.BlockSpec((rows, depth), lambda i: (index, 0)), whole(weights), whole(gain)],
        out_specs=[whole(shape) for shape in shapes],
        compiler_params=params(),
        cost_estimate=pl.CostEstimate(
            flops=2 * rows * depth * weights.shape[1],
            bytes_accessed=2 * depth * weights.shape[1] + 14 * rows * depth,
            transcendentals=0,
        ),
    )(level, *gathered, tokens, weights, gain)


def attend_back_kernel(
    start, q_ref, k_ref, v_ref, dm_ref, mixed_ref, place_ref, cos_ref, sin_ref, *refs
):
    rows = q_ref.shape[0]
    keys = k_ref.shape[0]
    kv_heads = k_ref.shape[1] // LANES
    group = q_ref.shape[1] // LANES // kv_heads
    outs = 2 if start > 0 else 1
    acc_ref = refs[0] if len(refs) > outs else None
    out_ref = refs[-outs]
    acc_out_ref = refs[-1]
    cosines = cos_ref[0]
    sines = sin_ref[0]

    def rotate_back(grads):
        return (grads * cosines - pltpu.roll(grads, LANES // 2, 1) * sines).astype(jnp.bfloat16)

    products = dm_ref[...].astype(jnp.float32) * dot_split(mixed_ref[:rows, :], place_ref[...])
    causal = lax.broadcasted_iota(jnp.int32, (rows, rows), 0) <= lax.broadcasted_iota(
        jnp.int32, (rows, rows), 1
    )
    wide = kv_heads * LANES
    base = kv_heads * group * LANES
    for kv in range(kv_heads):
        here = slice(kv * LANES, (kv + 1) * LANES)
        there = slice(wide + kv * LANES, wide + (kv + 1) * LANES)
        heads = range(kv * group, (kv + 1) * group)
        lanes = {h: slice(h * LANES, (h + 1) * LANES) for h in heads}
        row_dots = {h: jnp.sum(products[:, lanes[h]].T, axis=0, keepdims=True) for h in heads}
        log_sums = {h: mixed_ref[rows + h : rows + h + 1, :rows] for h in heads}
        dqueries = {h: None for h in heads}
        for tile in range(keys // rows):
            span = slice(tile * rows, (tile + 1) * rows)
            key = k_ref[span, here]
            value = v_ref[span, here]
            key_t = key.T
            dkey = None if acc_ref is None else acc_ref[span, here]
            dvalue = None if acc_ref is None else acc_ref[span, there]
            last = tile * rows == start
            for h in heads:
                query = q_ref[:, lanes[h]]
                dmixed = dm_ref[:, lanes[h]]
                raw = dot32_nt(key, query)
                probs = jnp.exp2(raw * score_scale_log2 - log_sums[h])
                if last:
                    probs = jnp.where(causal, probs, 0.0)
                dprobs = dot32_nt(value, dmixed)
                dscores = (probs * (dprobs - row_dots[h])).astype(jnp.bfloat16)
                dquery = dot32(key_t, dscores)
                dqueries[h] = dquery if dqueries[h] is None else dqueries[h] + dquery
                dkey_one = dot32(dscores, query)
                dvalue_one = dot32(probs.astype(jnp.bfloat16), dmixed)
                dkey = dkey_one if dkey is None else dkey + dkey_one
                dvalue = dvalue_one if dvalue is None else dvalue + dvalue_one
            if last:
                out_ref[:, base + kv * LANES : base + (kv + 1) * LANES] = rotate_back(
                    dkey * score_scale
                )
                out_ref[:, base + wide + kv * LANES : base + wide + (kv + 1) * LANES] = (
                    dvalue.astype(jnp.bfloat16)
                )
            else:
                acc_out_ref[span, here] = dkey
                acc_out_ref[span, there] = dvalue
        for h in heads:
            out_ref[:, lanes[h]] = rotate_back(dqueries[h].T * score_scale)


def attend_back(qkv, dmixed, mixed, place, cosines, sines, sums, index, rows, shards):
    start = index * rows
    keys = start + rows
    width = qkv.shape[1] // shards
    own = mixed.shape[1] // shards
    in_specs = [
        pl.BlockSpec((rows, width // 2), lambda t: (index, 2 * t)),
        pl.BlockSpec((keys, width // 4), lambda t: (0, 4 * t + 2)),
        pl.BlockSpec((keys, width // 4), lambda t: (0, 4 * t + 3)),
        pl.BlockSpec((rows, width // 2), lambda t: (0, t)),
        pl.BlockSpec((mixed.shape[0], own), lambda t: (0, t)),
        pl.BlockSpec(place.shape, lambda t: (0, 0)),
        pl.BlockSpec((1, rows, LANES), lambda t: (0, index, 0)),
        pl.BlockSpec((1, rows, LANES), lambda t: (0, index, 0)),
    ]
    args = [qkv, qkv, qkv, dmixed, mixed, place, cosines, sines]
    if sums is not None:
        in_specs.append(pl.BlockSpec((keys, width // 2), lambda t: (0, t)))
        args.append(sums)
    shapes = [jax.ShapeDtypeStruct((rows, qkv.shape[1]), jnp.bfloat16)]
    out_specs = [pl.BlockSpec((rows, width), lambda t: (0, t))]
    if start > 0:
        shapes.append(jax.ShapeDtypeStruct((start, qkv.shape[1] // 2), jnp.float32))
        out_specs.append(pl.BlockSpec((start, width // 2), lambda t: (0, t)))
    heads = qkv.shape[1] // 2 // LANES
    outs = pl.pallas_call(
        functools.partial(attend_back_kernel, start),
        out_shape=shapes,
        grid=(shards,),
        in_specs=in_specs,
        out_specs=out_specs,
        compiler_params=params(),
        cost_estimate=pl.CostEstimate(
            flops=10 * heads * rows * keys * LANES,
            bytes_accessed=2 * (rows + keys) * qkv.shape[1] + 4 * keys * qkv.shape[1],
            transcendentals=heads * rows * keys,
        ),
    )(*args)
    return outs[0], (outs[1] if start > 0 else None)


def norm_back(inputs, rms_vals, gain, dnormed):
    scaled = dnormed * gain
    dinputs = rms_vals * scaled - inputs * rms_vals**3 * jnp.mean(
        scaled * inputs, -1, keepdims=True
    )
    dgain = jnp.sum(dnormed * inputs * rms_vals, 0)
    return (dinputs, dgain)


def shards(
    tokens,
    lengths,
    positions,
    cotangent,
    norm_gain,
    w_query,
    w_key,
    w_value,
    w_out,
    mlp_gain,
    w_gate,
    w_up,
    w_down,
):
    seq_rows, depth = tokens.shape
    chips = lax.axis_size("chip")
    dp = chips * 2
    tp = lax.axis_size("tp")
    chip = lax.axis_index("chip")
    core = lax.axis_index("core")
    level = lax.axis_index("tp")
    odd = level % 2 == 1
    low = level < 2
    inner = (level == 1) | (level == 2)
    heads_here = w_query.shape[1] // HD
    kv_here = w_key.shape[1] // HD
    rows = seq_rows // CHUNKS
    slice_rows = depth // dp
    q_wide = heads_here * LANES
    kv_wide = kv_here * LANES
    shard_wide = q_wide + 2 * kv_wide
    level_ref = level.astype(jnp.int32).reshape(1)
    swap = lambda array: lax.ppermute(array, "core", [(0, 1), (1, 0)])

    place_qkv = placement(
        jnp.concatenate(
            [
                place_halves(heads_here),
                q_wide + place_halves(kv_here),
                q_wide + kv_wide + place_plain(kv_here),
            ]
        ),
        shard_wide,
    )
    place_out = placement(place_plain(heads_here), q_wide)

    w_qkv = jnp.concatenate([w_query, w_key, w_value], 1)
    w_out_t = w_out.T
    at_row = (chip * 2 + core) * slice_rows
    sliced = lambda array: lax.dynamic_slice_in_dim(array, at_row, slice_rows, 0).astype(
        jnp.float32
    )
    out_slice, qkv_slice = fence((sliced(w_out_t), sliced(w_qkv)))

    by_hand = dp == 8
    if by_hand:
        far0 = jnp.where(low, 2, 0)
        meta = jnp.stack([chip, core, level, level ^ 1, far0, far0 + 1]).astype(jnp.int32)

        def over_line_1(piece):
            other = along(piece, PAIRS)
            pair = jnp.where(odd, jnp.stack([other, piece]), jnp.stack([piece, other]))
            return other, pair

        def over_line_3(other, across, outer):
            return jnp.concatenate([other[None], jnp.where(inner, across, outer)], 0)

        def over_chips(piece):
            pieces = [piece]
            for m in range(1, chips):
                pieces.append(lax.ppermute(piece, "chip", [(i, i ^ m) for i in range(chips)]))
            return jnp.stack(pieces)

    half_dim = HD // 2
    freqs = rope_base ** (-(jnp.arange(half_dim).astype(jnp.float32) * 2.0 / HD))
    freqs = jnp.pad(freqs, (0, LANES // 2 - half_dim))
    angles = positions.astype(jnp.float32)[:, None] * jnp.concatenate([freqs, freqs])[None, :]
    sign = jnp.where(jnp.arange(LANES) < LANES // 2, -1.0, 1.0)
    cosines = jnp.cos(angles)
    sines = jnp.sin(angles) * sign
    cosines = jnp.stack([cosines, jnp.ones_like(cosines)])
    sines = jnp.stack([sines, jnp.zeros_like(sines)])

    inputs = tokens.astype(jnp.float32)
    rms_one = lax.rsqrt(jnp.mean(inputs * inputs, -1, keepdims=True) + norm_eps)
    normed_one = (inputs * rms_one * norm_gain).astype(jnp.bfloat16)
    own_pad = dot32(w_qkv, place_qkv).astype(jnp.bfloat16)
    live = (jnp.arange(seq_rows) < lengths[0]).astype(jnp.float32)[:, None]
    dout_low = (cotangent.astype(jnp.float32) * live).astype(jnp.bfloat16)

    order = list(reversed(range(CHUNKS)))
    cut = lambda array, j: array[j * rows : (j + 1) * rows]
    join = lambda pieces: jnp.concatenate([pieces[j] for j in range(CHUNKS)], 0)
    c0, c1, c2, c3 = order

    if by_hand:
        out_1 = over_line_1(out_slice)
        qkv_1 = over_line_1(qkv_slice)
    qkv_own = project(normed_one, own_pad, cosines, sines)
    strip = place_out.T
    if by_hand:
        qkv_own, out_1, qkv_1, normed_one, dout_low = fence(
            (qkv_own, out_1, qkv_1, normed_one, dout_low)
        )
        out_2 = along(out_1[1], MIDDLE)
        qkv_2 = along(qkv_1[1], MIDDLE)
    else:
        out_all = lax.all_gather(out_slice, ("chip", "core", "tp"))
        qkv_all = lax.all_gather(qkv_slice, ("chip", "core", "tp"))
    own = {}
    own[c0] = attend(lengths, qkv_own, strip, c0, rows)

    def gather_1(part):
        other = along(part, PAIRS)
        return jnp.where(
            odd, jnp.concatenate([other, part], 1), jnp.concatenate([part, other], 1)
        )

    if by_hand:
        own[c0], qkv_own, out_2 = fence((own[c0], qkv_own, out_2))
        out_piece = over_line_3(out_1[0], out_2, along(out_2, OUTWARD))
    pair = {}
    across = {}
    outer = {}
    pair[c0] = gather_1(own[c0])
    for j in (c1, c2, c3):
        own[j] = attend(lengths, qkv_own, strip, j, rows)
    pair, own, dout_low = fence((pair, own, dout_low))
    if by_hand:
        out_piece, qkv_2 = fence((out_piece, qkv_2))
        out_mine = over_chips(out_piece)
    across[c0] = along(pair[c0], MIDDLE)
    pair[c1] = gather_1(own[c1])
    dactiv = dot32_nt(dout_low, w_down)
    pair, across, own, dactiv = fence((pair, across, own, dactiv))
    outer[c0] = along(across[c0], OUTWARD)
    across[c1] = along(pair[c1], MIDDLE)
    pair[c2] = gather_1(own[c2])
    if by_hand:
        out_mine = fence(out_mine)
        out_theirs = swap(out_mine)
    pair, across, outer, own = fence((pair, across, outer, own))
    outer[c1] = along(across[c1], OUTWARD)
    across[c2] = along(pair[c2], MIDDLE)
    pair[c3] = gather_1(own[c3])
    if by_hand:
        out_pad, out_plain = spread(meta, out_mine, out_theirs, w_out_t, place_out, True)
    else:
        out_pad, out_plain = spread_all(
            out_all.reshape(dp, tp, slice_rows, heads_here * HD), place_out, True
        )

    hidden = {}
    rms_two = {}
    normed_two = {}
    mixed = {}
    activ = {}
    dgate = {}
    dup = {}
    mlp_part = {}

    def mlp_chunk(j):
        hidden[j], rms_two[j], normed_two[j], mixed[j] = residual(
            level_ref, (pair[j], across[j], outer[j]), tokens, out_plain, mlp_gain, j, rows
        )
        gate_val = dot32(normed_two[j], w_gate)
        up_val = dot32(normed_two[j], w_up)
        sigmoid_gate = jax.nn.sigmoid(gate_val)
        silu_gate = gate_val * sigmoid_gate
        activ[j] = (silu_gate * up_val).astype(jnp.bfloat16)
        mlp_part[j] = dot32(activ[j], w_down)
        dact = cut(dactiv, j)
        dgate[j] = (dact * up_val * sigmoid_gate * (1.0 + gate_val * (1.0 - sigmoid_gate))).astype(
            jnp.bfloat16
        )
        dup[j] = (dact * silu_gate).astype(jnp.bfloat16)
        return dot32_nt(dgate[j], w_gate) + dot32_nt(dup[j], w_up)

    part = {}
    total = {}
    final = {}
    part[c0] = mlp_chunk(c0)

    def add_hop(j, pairs):
        return total.get(j, part.get(j)) + along(total.get(j, part.get(j)), pairs)

    pair, across, outer, part, hidden = fence((pair, across, outer, part, hidden))
    total[c0] = add_hop(c0, INWARD)
    outer[c2] = along(across[c2], OUTWARD)
    across[c3] = along(pair[c3], MIDDLE)
    part[c1] = mlp_chunk(c1)
    if by_hand:
        qkv_2 = fence((qkv_2, part[c0]))[0]
        qkv_piece = over_line_3(qkv_1[0], qkv_2, along(qkv_2, OUTWARD))
    across, outer, part, total, hidden = fence((across, outer, part, total, hidden))
    total[c0] = add_hop(c0, MIDDLE)
    total[c1] = add_hop(c1, INWARD)
    outer[c3] = along(across[c3], OUTWARD)
    part[c2] = mlp_chunk(c2)
    if by_hand:
        qkv_piece = fence((qkv_piece, part[c1]))[0]
        qkv_mine = over_chips(qkv_piece)
    across, outer, part, total, hidden = fence((across, outer, part, total, hidden))
    final[c0] = along(total[c0], OUTWARD)
    total[c1] = add_hop(c1, MIDDLE)
    total[c2] = add_hop(c2, INWARD)
    part[c3] = mlp_chunk(c3)
    if by_hand:
        qkv_mine = fence((qkv_mine, part[c2]))[0]
        qkv_theirs = swap(qkv_mine)
    part, total, final, hidden, normed_two, activ, dgate, dup = fence(
        (part, total, final, hidden, normed_two, activ, dgate, dup)
    )
    final[c1] = along(total[c1], OUTWARD)
    total[c2] = add_hop(c2, MIDDLE)
    total[c3] = add_hop(c3, INWARD)
    if by_hand:
        qkv_mine, qkv_theirs, _ = fence((qkv_mine, qkv_theirs, part[c3]))
        (qkv_pad,) = spread(meta, qkv_mine, qkv_theirs, w_qkv, place_qkv, False)
    else:
        (qkv_pad,) = spread_all(qkv_all.reshape(dp, tp, slice_rows, -1), place_qkv, False)
    qkv = project(normed_one, qkv_pad, cosines, sines)

    def scatter_rows(array):
        blocks = array.reshape(chips, 2, slice_rows, array.shape[1])
        keep = lax.dynamic_index_in_dim(blocks, core, 1, False)
        send = lax.dynamic_index_in_dim(blocks, 1 - core, 1, False)
        half = keep + swap(send)
        return lax.psum_scatter(
            half.reshape(chips * slice_rows, array.shape[1]),
            "chip",
            scatter_dimension=0,
            tiled=True,
        )

    normed_two_t = join(normed_two).T
    grad_gate = dot32(normed_two_t, join(dgate))
    grad_up = dot32(normed_two_t, join(dup))
    grad_down = dot32(dout_low.T, join(activ))

    sums = None
    dhidden_low = {}
    dqkv_own = {}
    input_grad = {}
    gain_one = jnp.zeros((depth,), jnp.float32)
    gain_two = jnp.zeros((depth,), jnp.float32)

    def back_chunk(j):
        nonlocal sums, gain_one, gain_two
        dnormed_two = jnp.where(inner, total[j], final[j])
        dnorm, gain_part = norm_back(hidden[j], rms_two[j], mlp_gain, dnormed_two)
        gain_two = gain_two + gain_part
        dhidden = cut(dout_low, j).astype(jnp.float32) + dnorm
        dhidden_low[j] = dhidden.astype(jnp.bfloat16)
        dmixed = dot32(dhidden_low[j], out_pad).astype(jnp.bfloat16)
        dqkv, sums = attend_back(
            qkv, dmixed, mixed[j], place_out, cosines, sines, sums, j, rows, tp
        )
        dqkv_own[j] = lax.dynamic_slice_in_dim(dqkv, level * shard_wide, shard_wide, 1)
        dnormed_one = dot32_nt(dqkv, qkv_pad)
        dnorm, gain_part = norm_back(cut(inputs, j), cut(rms_one, j), norm_gain, dnormed_one)
        gain_one = gain_one + gain_part
        input_grad[j] = (dhidden + dnorm).astype(jnp.bfloat16)

    total, final, hidden, mlp_part, grad_gate, grad_up, grad_down, qkv = fence(
        (total, final, hidden, mlp_part, grad_gate, grad_up, grad_down, qkv)
    )
    final[c2] = along(total[c2], OUTWARD)
    total[c3] = add_hop(c3, MIDDLE)
    grad_gate = scatter_rows(grad_gate)
    grad_up = scatter_rows(grad_up)
    grad_down = scatter_rows(grad_down)
    back_chunk(c0)
    away = jnp.where(
        low,
        jnp.concatenate([mlp_part[2], mlp_part[3]], 0),
        jnp.concatenate([mlp_part[1], mlp_part[0]], 0),
    )
    away = away + along(away, INWARD)
    total, final, hidden, mlp_part, away, sums, input_grad = fence(
        (total, final, hidden, mlp_part, away, sums, input_grad)
    )
    final[c3] = along(total[c3], OUTWARD)
    coming = along(away, MIDDLE)
    back_chunk(c1)
    total, final, hidden, coming, sums, input_grad = fence(
        (total, final, hidden, coming, sums, input_grad)
    )
    near = jnp.where(low, mlp_part[1], mlp_part[2])
    edge = jnp.where(low, mlp_part[0], mlp_part[3])
    last = along(jnp.where(inner, edge + coming[rows:], near), PAIRS)
    mlp_rows = jnp.where(inner, near + coming[:rows], edge) + last
    hidden_rows = lax.dynamic_slice_in_dim(
        join(hidden), level * (seq_rows // tp), seq_rows // tp, 0
    )
    layer_out = (hidden_rows + mlp_rows).astype(jnp.bfloat16)
    back_chunk(c2)
    total, final, hidden, sums, input_grad = fence((total, final, hidden, sums, input_grad))
    back_chunk(c3)

    dqkv_low = dot32(join(dqkv_own), place_qkv.T).astype(jnp.bfloat16)
    grad_qkv = dot32(normed_one.T, dqkv_low)
    own_low = {j: own[j][:rows].astype(jnp.bfloat16) for j in order}
    grad_out = dot32(join(dhidden_low).T, join(own_low))
    gains = jnp.pad(jnp.stack([gain_one, gain_two], 1), ((0, 0), (0, LANES - 2)))
    attn = scatter_rows(jnp.concatenate([grad_qkv, grad_out, gains], 1))
    q_cols = heads_here * HD
    kv_cols = kv_here * HD
    ends = [q_cols, q_cols + kv_cols, q_cols + 2 * kv_cols, 2 * q_cols + 2 * kv_cols]
    return (
        layer_out,
        join(input_grad),
        attn[:, ends[3]],
        attn[:, : ends[0]],
        attn[:, ends[0] : ends[1]],
        attn[:, ends[1] : ends[2]],
        attn[:, ends[2] : ends[3]].T,
        attn[:, ends[3] + 1],
        grad_gate,
        grad_up,
        grad_down.T,
    )


def solution(mesh):
    devices = mesh.devices
    dp, tp = devices.shape
    split = Mesh(devices.reshape(dp // 2, 2, tp), ("chip", "core", "tp"))
    data = ("chip", "core")
    return jax.shard_map(
        shards,
        mesh=split,
        in_specs=(
            P(data, None),
            P(data),
            P(data),
            P(data, None),
            P(),
            P(None, "tp"),
            P(None, "tp"),
            P(None, "tp"),
            P("tp", None),
            P(),
            P(None, "tp"),
            P(None, "tp"),
            P("tp", None),
        ),
        out_specs=(
            P(("chip", "core", "tp"), None),
            P(data, None),
            P(data),
            P(data, "tp"),
            P(data, "tp"),
            P(data, "tp"),
            P("tp", data),
            P(data),
            P(data, "tp"),
            P(data, "tp"),
            P("tp", data),
        ),
        check_vma=False,
    )
```

```python
import functools

import jax
import jax.numpy as jnp
from jax import lax
from jax.experimental import pallas as pl
from jax.experimental.pallas import tpu as pltpu
from jax.sharding import Mesh
from jax.sharding import PartitionSpec as P

HD = 96
LANES = 128
GROUP = 2
KV_WIDE = (GROUP + 2) * LANES
rope_base = 100000.0
norm_eps = 1e-05
masked_score = -1e30
far_away = 1e30
score_scale = HD ** (-0.5)
score_scale_log2 = score_scale * 1.4426950408889634
CHUNKS = 4
EXTRA = 8
VMEM_BYTES = 56 * 1024 * 1024
NT = (((1,), (1,)), ((), ()))


def params():
    return pltpu.CompilerParams(vmem_limit_bytes=VMEM_BYTES)


def cost(flops, moved, exps=0):
    return pl.CostEstimate(flops=flops, bytes_accessed=moved, transcendentals=exps)


def dot32(a, b):
    return jnp.dot(a, b, preferred_element_type=jnp.float32)


def dot32_nt(a, b):
    return lax.dot_general(a, b, NT, preferred_element_type=jnp.float32)


def dot_split(a, places):
    high = a.astype(jnp.bfloat16)
    rest = (a - high.astype(jnp.float32)).astype(jnp.bfloat16)
    return dot32(high, places) + dot32(rest, places)


def fence(*trees):
    return lax.optimization_barrier(trees)


def whole(array, buffers=None):
    zeros = (0,) * len(array.shape)
    return pl.BlockSpec(array.shape, lambda *_: zeros)


SCALAR = pl.BlockSpec(memory_space=pltpu.SMEM)


def halves(entry):
    half_dim = HD // 2
    return (entry // half_dim) * (LANES // 2) + entry % half_dim


def placement(lanes, width):
    return (lanes[:, None] == jnp.arange(width)[None, :]).astype(jnp.bfloat16)


def place_query(heads):
    source = jnp.arange(heads * HD)
    return placement((source // HD) * LANES + halves(source % HD), heads * LANES)


def place_key_value(kv_heads):
    source = jnp.arange(kv_heads * HD)
    head = source // HD
    keys = head * 2 * LANES + halves(source % HD)
    values = head * 2 * LANES + LANES + source % HD
    return placement(jnp.concatenate([keys, values]), kv_heads * 2 * LANES)


def place_all(heads, kv_heads):
    source = jnp.arange(heads * HD)
    head = source // HD
    query = (head // GROUP) * KV_WIDE + (head % GROUP) * LANES + halves(source % HD)
    source = jnp.arange(kv_heads * HD)
    base = (source // HD) * KV_WIDE + GROUP * LANES
    keys = base + halves(source % HD)
    values = base + LANES + source % HD
    return placement(jnp.concatenate([query, keys, values]), kv_heads * KV_WIDE)


def place_plain(heads):
    source = jnp.arange(heads * HD)
    return placement((source // HD) * LANES + source % HD, heads * LANES)


PAIRS = [(0, 1), (1, 0), (2, 3), (3, 2)]
INWARD = [(0, 1), (3, 2)]
MIDDLE = [(1, 2), (2, 1)]
OUTWARD = [(1, 0), (2, 3)]


def along(part, pairs):
    return lax.ppermute(part, "tp", pairs)


def store_qkv(out_ref, base, query, key_value):
    wide = GROUP * LANES
    for kv in range(key_value.shape[1] // (2 * LANES)):
        at = base + kv * KV_WIDE
        out_ref[:, at : at + wide] = query[:, kv * wide : (kv + 1) * wide]
        out_ref[:, at + wide : at + KV_WIDE] = key_value[:, kv * 2 * LANES : (kv + 1) * 2 * LANES]


def place_own_kernel(q_ref, k_ref, v_ref, pq_ref, pkv_ref, out_ref):
    query = dot32(q_ref[...], pq_ref[...]).astype(jnp.bfloat16)
    split = k_ref.shape[1]
    key_value = dot32(k_ref[...], pkv_ref[:split, :]) + dot32(v_ref[...], pkv_ref[split:, :])
    store_qkv(out_ref, 0, query, key_value.astype(jnp.bfloat16))


def place_own(w_query, w_key, w_value, pq, pkv):
    total = w_query.shape[0]
    rows = total // 4
    wide = pq.shape[1] + pkv.shape[1]
    by_rows = lambda array: pl.BlockSpec((rows, array.shape[1]), lambda i: (i, 0))
    return pl.pallas_call(
        place_own_kernel,
        out_shape=jax.ShapeDtypeStruct((total, wide), jnp.bfloat16),
        grid=(4,),
        in_specs=[by_rows(w_query), by_rows(w_key), by_rows(w_value), whole(pq), whole(pkv)],
        out_specs=pl.BlockSpec((rows, wide), lambda i: (i, 0)),
        compiler_params=params(),
        cost_estimate=cost(2 * total * wide * pq.shape[0], 4 * total * wide),
    )(w_query, w_key, w_value, pq, pkv)


def spread_out_kernel(meta_ref, own_ref, p_ref, *refs):
    mine, theirs, (pad_ref, plain_ref) = refs[:3], refs[3:6], refs[6:]
    side = pl.program_id(0)
    width = own_ref.shape[1]
    wide = p_ref.shape[1]
    for s in range(4):
        if s == 0:
            block = own_ref[...]
        else:
            block = jnp.where(side == 0, mine[s - 1][0], theirs[s - 1][0]).astype(jnp.bfloat16)
        plain_ref[:, s * width : (s + 1) * width] = block
        pad_ref[:, s * wide : (s + 1) * wide] = dot32(block, p_ref[...]).astype(jnp.bfloat16)


def spread_qkv_kernel(meta_ref, own_ref, pq_ref, pkv_ref, *refs):
    mine, theirs, (out_ref,) = refs[:3], refs[3:6], refs[6:]
    side = pl.program_id(0)
    wide = own_ref.shape[1]
    split = pq_ref.shape[0]
    out_ref[:, :wide] = own_ref[...]
    for s in range(1, 4):
        block = jnp.where(side == 0, mine[s - 1][0], theirs[s - 1][0]).astype(jnp.bfloat16)
        query = dot32(block[:, :split], pq_ref[...]).astype(jnp.bfloat16)
        key_value = dot32(block[:, split:], pkv_ref[...]).astype(jnp.bfloat16)
        store_qkv(out_ref, s * wide, query, key_value)


def spread(kernel, meta, own, places, mine, theirs, widths):
    chips, rows, width = mine[0].shape
    total = own.shape[0]
    row_block = lambda c, m, meta: ((meta[0] ^ m) * 2 + (meta[1] ^ c), 0)

    def far(side):
        hold = chips - 1 if side == 0 else 0
        return pl.BlockSpec(
            (1, rows, width), lambda c, m, meta: (jnp.where(c == side, m, hold), 0, 0)
        )

    return pl.pallas_call(
        kernel,
        out_shape=[jax.ShapeDtypeStruct((total, wide), jnp.bfloat16) for wide in widths],
        grid_spec=pltpu.PrefetchScalarGridSpec(
            num_scalar_prefetch=1,
            grid=(2, chips),
            in_specs=[pl.BlockSpec((rows, own.shape[1]), row_block)]
            + [whole(place) for place in places]
            + [far(0)] * 3
            + [far(1)] * 3,
            out_specs=[pl.BlockSpec((rows, wide), row_block) for wide in widths],
        ),
        compiler_params=params(),
        cost_estimate=cost(
            8 * total * width * 512, total * (12 * width + 2 * sum(widths))
        ),
    )(meta, own, *places, *mine, *theirs)


def project_kernel(x_ref, w_ref, cos_ref, sin_ref, out_ref):
    lin = dot32(x_ref[...], w_ref[...])
    for h in range(GROUP + 2):
        here = slice(h * LANES, (h + 1) * LANES)
        one = lin[:, here]
        if h < GROUP + 1:
            one = one * cos_ref[...] + pltpu.roll(one, LANES // 2, 1) * sin_ref[...]
        out_ref[:, here] = one.astype(jnp.bfloat16)


def project(normed, weights, cosines, sines):
    rows, depth = normed.shape
    width = weights.shape[1]
    return pl.pallas_call(
        project_kernel,
        out_shape=jax.ShapeDtypeStruct((rows, width), jnp.bfloat16),
        grid=(width // KV_WIDE,),
        in_specs=[
            whole(normed),
            pl.BlockSpec((depth, KV_WIDE), lambda i: (0, i)),
            whole(cosines),
            whole(sines),
        ],
        out_specs=pl.BlockSpec((rows, KV_WIDE), lambda i: (0, i)),
        compiler_params=params(),
        cost_estimate=cost(
            2 * rows * depth * width, 2 * (rows * depth + depth * width + rows * width)
        ),
    )(normed, weights, cosines, sines)


def attend_kernel(start, length_ref, q_ref, kv_ref, strip_ref, out_ref):
    rows = q_ref.shape[0]
    keys = kv_ref.shape[0]
    length = length_ref[0]
    row_ids = start + lax.broadcasted_iota(jnp.int32, (1, rows), 1)
    limit = jnp.minimum(row_ids, length - 1)
    allowed = lax.broadcasted_iota(jnp.int32, (keys, rows), 0) <= limit
    mixed = []
    sums = []
    for kv in range(kv_ref.shape[1] // KV_WIDE):
        base = kv * KV_WIDE
        at = base + GROUP * LANES
        key = kv_ref[:, at : at + LANES]
        value_t = kv_ref[:, at + LANES : at + 2 * LANES].T
        for g in range(GROUP):
            query = q_ref[:, base + g * LANES : base + (g + 1) * LANES]
            raw = jnp.where(allowed, dot32_nt(key, query), masked_score)
            peak = jnp.max(raw, axis=0, keepdims=True)
            expo = jnp.exp2((raw - peak) * score_scale_log2)
            total = jnp.sum(expo, axis=0, keepdims=True)
            probs = (expo * (1.0 / total)).astype(jnp.bfloat16)
            mixed.append(dot32(value_t, probs).T)
            log_sum = peak * score_scale_log2 + jnp.log2(total)
            sums.append(jnp.where(row_ids < length, log_sum, far_away))
    out_ref[:rows, :] = dot_split(jnp.concatenate(mixed, 1), strip_ref[...])
    out_ref[rows:, :] = jnp.zeros((EXTRA, out_ref.shape[1]), jnp.float32)
    out_ref[rows : rows + len(sums), :rows] = jnp.concatenate(sums, 0)


def attend(length, qkv, strip, index, rows):
    keys = (index + 1) * rows
    width = qkv.shape[1]
    heads = width // KV_WIDE * GROUP
    shape = (rows + EXTRA, strip.shape[1])
    return pl.pallas_call(
        functools.partial(attend_kernel, index * rows),
        out_shape=jax.ShapeDtypeStruct(shape, jnp.float32),
        grid=(1,),
        in_specs=[
            SCALAR,
            pl.BlockSpec((rows, width), lambda i: (index, 0)),
            pl.BlockSpec((keys, width), lambda i: (0, 0)),
            whole(strip),
        ],
        out_specs=pl.BlockSpec(shape, lambda i: (0, 0)),
        compiler_params=params(),
        cost_estimate=cost(
            4 * heads * rows * keys * LANES, 2 * (rows + keys) * width, heads * rows * keys
        ),
    )(length, qkv, qkv, strip)


def forward_kernel(level_ref, part_ref, other_ref, across_ref, outer_ref, *refs):
    x_ref, dout_ref, wo_ref, gain_ref, wg_ref, wu_ref, wd_ref = refs[:7]
    hidden_ref, normed_t_ref, activ_ref, dgate_ref, dup_ref, mlp_ref, dn_ref = refs[7:14]
    normed_ref = refs[14]
    rows = x_ref.shape[0]

    @pl.when(pl.program_id(0) == 0)
    def _():
        level = level_ref[0]
        inner = (level == 1) | (level == 2)
        width = part_ref.shape[1]
        second = jnp.where(inner, across_ref[:rows, width:], outer_ref[:rows, :width])
        third = jnp.where(inner, across_ref[:rows, :width], outer_ref[:rows, width:])
        mixed = jnp.concatenate([part_ref[:rows, :], other_ref[:rows, :], second, third], 1)
        hidden = x_ref[...].astype(jnp.float32) + dot32_nt(mixed.astype(jnp.bfloat16), wo_ref[...])
        hidden_ref[...] = hidden
        rms = lax.rsqrt(jnp.mean(hidden * hidden, -1, keepdims=True) + norm_eps)
        normed = (hidden * rms * gain_ref[...]).astype(jnp.bfloat16)
        normed_ref[...] = normed
        normed_t_ref[...] = normed.T
        mlp_ref[...] = jnp.zeros_like(mlp_ref)
        dn_ref[...] = jnp.zeros_like(dn_ref)

    normed = normed_ref[...]
    gate = dot32(normed, wg_ref[...])
    up = dot32(normed, wu_ref[...])
    dact = dot32_nt(dout_ref[...], wd_ref[...])
    sigmoid = jax.nn.sigmoid(gate)
    silu = gate * sigmoid
    activ = (silu * up).astype(jnp.bfloat16)
    dgate = (dact * up * sigmoid * (1.0 + gate * (1.0 - sigmoid))).astype(jnp.bfloat16)
    dup = (dact * silu).astype(jnp.bfloat16)
    activ_ref[...] = activ
    dgate_ref[...] = dgate
    dup_ref[...] = dup
    mlp_ref[...] += dot32(activ, wd_ref[...])
    dn_ref[...] += dot32_nt(dgate, wg_ref[...]) + dot32_nt(dup, wu_ref[...])


def forward_chunk(level, gathered, tokens, dout, w_out, gain, w_gate, w_up, w_down, index, rows):
    depth = tokens.shape[1]
    units = w_gate.shape[1]
    block = 256
    own_rows = pl.BlockSpec((rows, depth), lambda i: (index, 0))
    by_units = pl.BlockSpec((depth, block), lambda i: (0, i))
    gain = gain[None, :]
    f32, bf16 = jnp.float32, jnp.bfloat16
    outs = [
        jax.ShapeDtypeStruct((rows, depth), f32),
        jax.ShapeDtypeStruct((depth, rows), bf16),
        jax.ShapeDtypeStruct((rows, units), bf16),
        jax.ShapeDtypeStruct((rows, units), bf16),
        jax.ShapeDtypeStruct((rows, units), bf16),
        jax.ShapeDtypeStruct((rows, depth), f32),
        jax.ShapeDtypeStruct((rows, depth), f32),
    ]
    unit_out = pl.BlockSpec((rows, block), lambda i: (0, i))
    return pl.pallas_call(
        forward_kernel,
        out_shape=outs,
        grid=(units // block,),
        in_specs=[SCALAR]
        + [whole(array) for array in gathered]
        + [own_rows, own_rows, whole(w_out), whole(gain), by_units, by_units]
        + [pl.BlockSpec((block, depth), lambda i: (i, 0))],
        out_specs=[
            whole(outs[0]),
            whole(outs[1]),
            unit_out,
            unit_out,
            unit_out,
            whole(outs[5]),
            whole(outs[6]),
        ],
        scratch_shapes=[pltpu.VMEM((rows, depth), bf16)],
        compiler_params=params(),
        cost_estimate=cost(
            2 * rows * depth * (6 * units + w_out.shape[1]),
            2 * depth * (3 * units + w_out.shape[1]) + 22 * rows * depth,
            rows * units,
        ),
    )(level, *gathered, tokens, dout, w_out, gain, w_gate, w_up, w_down)


def backward_kernel(start, level_ref, total_ref, final_ref, hidden_ref, dout_ref, x_ref, *refs):
    gain_one_ref, gain_two_ref, wo_ref, w_ref, q_ref, k_ref, v_ref = refs[:7]
    part_ref, other_ref, across_ref, outer_ref, place_ref, strip_ref = refs[7:13]
    cos_ref, sin_ref = refs[13:15]
    dhid_ref, low_ref, dn_ref, own_ref = refs[-4:]
    outs = refs[15:-4]
    count = 5 if start > 0 else 4
    acc_ref = outs[0] if len(outs) > count else None
    outs = outs[-count:]
    dhid_t_ref, dqkv_ref, input_grad_ref, gains_ref = outs[:4]
    rows = q_ref.shape[0]
    keys = k_ref.shape[0]
    head = pl.program_id(0)
    level = level_ref[0]
    inner = (level == 1) | (level == 2)
    kv_here = own_ref.shape[1] // KV_WIDE
    shard = head // kv_here
    kv = head % kv_here

    @pl.when(head == 0)
    def _():
        dnormed = jnp.where(inner, total_ref[...], final_ref[...])
        hidden = hidden_ref[...]
        rms = lax.rsqrt(jnp.mean(hidden * hidden, -1, keepdims=True) + norm_eps)
        scaled = dnormed * gain_two_ref[...]
        shift = jnp.mean(scaled * hidden, -1, keepdims=True)
        dhid = dout_ref[...].astype(jnp.float32) + (rms * scaled - hidden * (rms**3 * shift))
        dhid_ref[...] = dhid
        low = dhid.astype(jnp.bfloat16)
        low_ref[...] = low
        dhid_t_ref[...] = low.T
        gains_ref[...] = jnp.zeros_like(gains_ref)
        gains_ref[1:2, :] = jnp.sum(dnormed * (hidden * rms), 0, keepdims=True)
        dn_ref[...] = jnp.zeros_like(dn_ref)

    def rotate_back(grads):
        turned = grads * cos_ref[...] - pltpu.roll(grads, LANES // 2, 1) * sin_ref[...]
        return turned.astype(jnp.bfloat16)

    dmixed_all = dot32(low_ref[...], wo_ref[...]).astype(jnp.bfloat16)
    mixed = jnp.where(
        shard == 0,
        part_ref[...],
        jnp.where(shard == 1, other_ref[...], jnp.where(inner, across_ref[...], outer_ref[...])),
    )
    products = dmixed_all.astype(jnp.float32) * dot_split(mixed[:rows], place_ref[...])
    all_sums = mixed[rows:, :rows]
    sum_rows = lax.broadcasted_iota(jnp.int32, all_sums.shape, 0)
    causal = lax.broadcasted_iota(jnp.int32, (rows, rows), 0) <= lax.broadcasted_iota(
        jnp.int32, (rows, rows), 1
    )
    row_dots = []
    log_sums = []
    for g in range(GROUP):
        here = slice(g * LANES, (g + 1) * LANES)
        row_dots.append(jnp.sum(products[:, here].T, axis=0, keepdims=True))
        picked = jnp.where(sum_rows == kv * GROUP + g, all_sums, 0.0)
        log_sums.append(jnp.sum(picked, axis=0, keepdims=True))
    dqueries = [None] * GROUP
    for tile in range(keys // rows):
        span = slice(tile * rows, (tile + 1) * rows)
        key = k_ref[span, :]
        value = v_ref[span, :]
        key_t = key.T
        dkey = None if acc_ref is None else acc_ref[span, :LANES]
        dvalue = None if acc_ref is None else acc_ref[span, LANES:]
        last = tile * rows == start
        for g in range(GROUP):
            here = slice(g * LANES, (g + 1) * LANES)
            query = q_ref[:, here]
            dmixed = dmixed_all[:, here]
            raw = dot32_nt(key, query)
            probs = jnp.exp2(raw * score_scale_log2 - log_sums[g])
            if last:
                probs = jnp.where(causal, probs, 0.0)
            dprobs = dot32_nt(value, dmixed)
            dscores = (probs * (dprobs - row_dots[g])).astype(jnp.bfloat16)
            dquery = dot32(key_t, dscores)
            dqueries[g] = dquery if dqueries[g] is None else dqueries[g] + dquery
            dkey_one = dot32(dscores, query)
            dvalue_one = dot32(probs.astype(jnp.bfloat16), dmixed)
            dkey = dkey_one if dkey is None else dkey + dkey_one
            dvalue = dvalue_one if dvalue is None else dvalue + dvalue_one
        if not last:
            outs[4][span, :LANES] = dkey
            outs[4][span, LANES:] = dvalue
    grads = [rotate_back(dquery.T * score_scale) for dquery in dqueries]
    grads.append(rotate_back(dkey * score_scale))
    grads.append(dvalue.astype(jnp.bfloat16))
    grads = jnp.concatenate(grads, 1)
    dn_ref[...] += dot32_nt(grads, w_ref[...])
    for i in range(kv_here):

        @pl.when(head == i)
        def _(i=i):
            own_ref[:, i * KV_WIDE : (i + 1) * KV_WIDE] = grads

    @pl.when(head == kv_here - 1)
    def _():
        dqkv_ref[...] = dot32(own_ref[...], strip_ref[...]).astype(jnp.bfloat16)

    @pl.when(head == pl.num_programs(0) - 1)
    def _():
        dnormed = dn_ref[...]
        inputs = x_ref[...].astype(jnp.float32)
        rms = lax.rsqrt(jnp.mean(inputs * inputs, -1, keepdims=True) + norm_eps)
        scaled = dnormed * gain_one_ref[...]
        shift = jnp.mean(scaled * inputs, -1, keepdims=True)
        grad = dhid_ref[...] + (rms * scaled - inputs * (rms**3 * shift))
        input_grad_ref[...] = grad.astype(jnp.bfloat16)
        gains_ref[0:1, :] = jnp.sum(dnormed * (inputs * rms), 0, keepdims=True)


def backward_chunk(level, sums_two, hidden, dout, tokens, gains, weights, qkv, gathered, places,
                   tables, acc, index, rows):
    start = index * rows
    keys = start + rows
    depth = tokens.shape[1]
    out_pad, qkv_pad = weights
    place_out, strip = places
    heads = qkv.shape[1] // KV_WIDE
    kv_here = place_out.shape[1] // (GROUP * LANES)
    width = gathered[0].shape[1]
    far_rows = gathered[0].shape[0]
    wide = GROUP * LANES
    own_rows = pl.BlockSpec((rows, depth), lambda h: (index, 0))
    table = pl.BlockSpec((rows, LANES), lambda h: (index, 0))
    gains = [gain[None, :] for gain in gains]
    across = pl.BlockSpec((far_rows, width), lambda h: (0, jnp.where(h < 3 * kv_here, 1, 0)))
    outer = pl.BlockSpec((far_rows, width), lambda h: (0, jnp.where(h < 3 * kv_here, 0, 1)))
    in_specs = [
        SCALAR,
        whole(sums_two[0]),
        whole(sums_two[1]),
        whole(hidden),
        own_rows,
        own_rows,
        whole(gains[0]),
        whole(gains[1]),
        pl.BlockSpec((depth, wide), lambda h: (0, h)),
        pl.BlockSpec((depth, KV_WIDE), lambda h: (0, h)),
        pl.BlockSpec((rows, wide), lambda h: (index, 2 * h)),
        pl.BlockSpec((keys, LANES), lambda h: (0, 4 * h + 2)),
        pl.BlockSpec((keys, LANES), lambda h: (0, 4 * h + 3)),
        whole(gathered[0]),
        whole(gathered[1]),
        across,
        outer,
        pl.BlockSpec((width, wide), lambda h: (0, h % kv_here)),
        whole(strip),
        table,
        table,
    ]
    args = [level, *sums_two, hidden, dout, tokens, *gains, out_pad, qkv_pad, qkv, qkv, qkv]
    args += [*gathered, place_out, strip, *tables]
    if acc is not None:
        in_specs.append(pl.BlockSpec((keys, 2 * LANES), lambda h: (0, h)))
        args.append(acc)
    f32, bf16 = jnp.float32, jnp.bfloat16
    outs = [
        jax.ShapeDtypeStruct((depth, rows), bf16),
        jax.ShapeDtypeStruct((rows, strip.shape[1]), bf16),
        jax.ShapeDtypeStruct((rows, depth), bf16),
        jax.ShapeDtypeStruct((8, depth), f32),
    ]
    out_specs = [whole(out) for out in outs]
    if start > 0:
        outs.append(jax.ShapeDtypeStruct((start, heads * 2 * LANES), f32))
        out_specs.append(pl.BlockSpec((start, 2 * LANES), lambda h: (0, h)))
    results = pl.pallas_call(
        functools.partial(backward_kernel, start),
        out_shape=outs,
        grid=(heads,),
        in_specs=in_specs,
        out_specs=out_specs,
        scratch_shapes=[
            pltpu.VMEM((rows, depth), f32),
            pltpu.VMEM((rows, depth), bf16),
            pltpu.VMEM((rows, depth), f32),
            pltpu.VMEM((rows, kv_here * KV_WIDE), bf16),
        ],
        compiler_params=params(),
        cost_estimate=cost(
            heads * rows * (20 * keys * LANES + 2 * depth * (wide + KV_WIDE)),
            2 * depth * heads * (wide + KV_WIDE) + 16 * keys * heads * LANES + 16 * rows * depth,
            heads * GROUP * rows * keys,
        ),
    )(*args)
    return results[:4], (results[4] if start > 0 else None)


def rows_kernel(groups, extra, adding, side_ref, *refs):
    refs = list(refs)
    out_ref = refs.pop()
    recv_ref = refs.pop() if adding else None
    extra_ref = refs.pop() if extra else None
    at = 0

    def put(value):
        nonlocal at
        here = slice(at, at + value.shape[1])
        out_ref[:, here] = value if recv_ref is None else value + recv_ref[:, here]
        at += value.shape[1]

    for _ in range(groups):
        lefts, rights, refs = refs[:CHUNKS], refs[CHUNKS : 2 * CHUNKS], refs[2 * CHUNKS :]
        total = None
        for left, right in zip(lefts, rights):
            length = left.shape[1]
            one = dot32(left[...], right[:length, :].astype(jnp.bfloat16))
            total = one if total is None else total + one
        put(total)
    if extra_ref is not None:
        put(extra_ref[...])


def rows_of(groups, side, rows, count, extra=None, recv=None):
    specs = []
    args = []
    width = 0
    flops = 0
    for left, rights in groups:
        if isinstance(left, list):
            specs += [
                pl.BlockSpec((rows, one.shape[1]), lambda m, side: (m * side[1] + side[0], 0))
                for one in left
            ]
            args += left
        else:
            chunk = left.shape[1] // CHUNKS
            specs += [
                pl.BlockSpec(
                    (rows, chunk), lambda m, side, j=j: (m * side[1] + side[0], j)
                )
                for j in range(CHUNKS)
            ]
            args += [left] * CHUNKS
        specs += [whole(right) for right in rights]
        args += rights
        width += rights[0].shape[1]
        flops += 2 * rows * count * CHUNKS * rights[0].shape[0] * rights[0].shape[1]
    if extra is not None:
        specs.append(
            pl.BlockSpec((rows, extra.shape[1]), lambda m, side: (m * side[1] + side[0], 0))
        )
        args.append(extra)
        width += extra.shape[1]
    block = pl.BlockSpec((rows, width), lambda m, side: (m, 0))
    if recv is not None:
        specs.append(block)
        args.append(recv)
    return pl.pallas_call(
        functools.partial(rows_kernel, len(groups), extra is not None, recv is not None),
        out_shape=jax.ShapeDtypeStruct((rows * count, width), jnp.float32),
        grid_spec=pltpu.PrefetchScalarGridSpec(
            num_scalar_prefetch=1, grid=(count,), in_specs=specs, out_specs=block
        ),
        compiler_params=params(),
        cost_estimate=cost(flops, 4 * rows * count * width + 2 * 1024 * (width + rows * count)),
    )(side, *args)


def shards(
    tokens,
    lengths,
    positions,
    cotangent,
    norm_gain,
    w_query,
    w_key,
    w_value,
    w_out,
    mlp_gain,
    w_gate,
    w_up,
    w_down,
):
    seq_rows, depth = tokens.shape
    chips = lax.axis_size("chip")
    dp = chips * 2
    tp = lax.axis_size("tp")
    chip = lax.axis_index("chip")
    core = lax.axis_index("core")
    level = lax.axis_index("tp")
    low = level < 2
    inner = (level == 1) | (level == 2)
    heads_here = w_query.shape[1] // HD
    kv_here = w_key.shape[1] // HD
    rows = seq_rows // CHUNKS
    slice_rows = depth // dp
    level_ref = level.astype(jnp.int32).reshape(1)
    by_hand = dp == 8
    swap = lambda array: lax.ppermute(array, "core", [(0, 1), (1, 0)])
    to_level = lambda array, s: along(array, [(t, t ^ s) for t in range(tp)])

    def over_chips(piece):
        pieces = [piece]
        for m in range(1, chips):
            pieces.append(lax.ppermute(piece, "chip", [(i, i ^ m) for i in range(chips)]))
        return jnp.stack(pieces)

    at_row = (chip * 2 + core) * slice_rows
    out_slice = lax.dynamic_slice_in_dim(w_out, at_row, slice_rows, 1).astype(jnp.float32).T
    row_slice = lambda w: lax.dynamic_slice_in_dim(w, at_row, slice_rows, 0)
    qkv_slice = jnp.concatenate(
        [row_slice(w_query), row_slice(w_key), row_slice(w_value)], 1
    ).astype(jnp.float32)
    out_slice, qkv_slice = fence(out_slice, qkv_slice)
    if by_hand:
        out_far = [to_level(out_slice, s) for s in (1, 2, 3)]
    meta = jnp.stack([chip, core]).astype(jnp.int32)

    pq = place_query(heads_here)
    pkv = place_key_value(kv_here)
    p_all = place_all(heads_here, kv_here)
    p_out = place_plain(heads_here)
    strip_out = p_out.T

    half_dim = HD // 2
    freqs = rope_base ** (-(jnp.arange(half_dim).astype(jnp.float32) * 2.0 / HD))
    freqs = jnp.pad(freqs, (0, LANES // 2 - half_dim))
    angles = positions.astype(jnp.float32)[:, None] * jnp.concatenate([freqs, freqs])[None, :]
    cosines = jnp.cos(angles)
    sines = jnp.sin(angles) * jnp.where(jnp.arange(LANES) < LANES // 2, -1.0, 1.0)

    inputs = tokens.astype(jnp.float32)
    rms_one = lax.rsqrt(jnp.mean(inputs * inputs, -1, keepdims=True) + norm_eps)
    normed_one = (inputs * rms_one * norm_gain).astype(jnp.bfloat16)
    own_pad = place_own(w_query, w_key, w_value, pq, pkv)
    qkv_own = project(normed_one, own_pad, cosines, sines)
    live = (jnp.arange(seq_rows) < lengths[0]).astype(jnp.float32)[:, None]

    order = list(reversed(range(CHUNKS)))
    c0, c1, c2, c3 = order
    own, other, pair, across, outer = {}, {}, {}, {}, {}
    part, total, final = {}, {}, {}

    def hop_1(j):
        other[j] = along(own[j], PAIRS)
        pair[j] = jnp.concatenate([own[j], other[j]], 1)

    def hop_2(j):
        across[j] = along(pair[j], MIDDLE)

    def hop_3(j):
        outer[j] = along(across[j], OUTWARD)

    def add_1(j):
        total[j] = part[j] + along(part[j], INWARD)

    def add_2(j):
        total[j] = total[j] + along(total[j], MIDDLE)

    def add_3(j):
        final[j] = along(total[j], OUTWARD)

    if by_hand:
        out_far, qkv_own = fence(out_far, qkv_own)
        out_mine = [over_chips(piece) for piece in [jnp.stack(out_far)]][0]
        qkv_far = [to_level(qkv_slice, 1)]
    else:
        gathered_out = lax.all_gather(out_slice, ("chip", "core", "tp"))
        gathered_qkv = lax.all_gather(qkv_slice, ("chip", "core", "tp"))
    own[c0] = attend(lengths, qkv_own, strip_out, c0, rows)
    own, qkv_own = fence(own, qkv_own)
    hop_1(c0)
    for j in (c1, c2, c3):
        own[j] = attend(lengths, qkv_own, strip_out, j, rows)
    own, other, pair, normed_one = fence(own, other, pair, normed_one)
    hop_2(c0)
    hop_1(c1)
    dout = (cotangent.astype(jnp.float32) * live).astype(jnp.bfloat16)
    dout_t = dout.T
    normed_one_t = normed_one.T
    w_out_t = w_out.T
    own, other, pair, across, dout_t, normed_one_t, w_out_t = fence(
        own, other, pair, across, dout_t, normed_one_t, w_out_t
    )
    hop_3(c0)
    hop_2(c1)
    hop_1(c2)
    if by_hand:
        out_mine, qkv_far, own_pad = fence(out_mine, qkv_far, own_pad)
        out_theirs = swap(out_mine)
        qkv_mine = [over_chips(qkv_far[0])]
    own, other, pair, across, outer = fence(own, other, pair, across, outer)
    hop_3(c1)
    hop_2(c2)
    hop_1(c3)
    if by_hand:
        qkv_slice, _ = fence(qkv_slice, outer)
        qkv_far.append(to_level(qkv_slice, 2))
        out_pad, out_plain = spread(
            spread_out_kernel,
            meta,
            w_out_t,
            [p_out],
            [out_mine[:, s] for s in range(3)],
            [out_theirs[:, s] for s in range(3)],
            [4 * p_out.shape[1], 4 * p_out.shape[0]],
        )
    else:
        by_shard = lambda g, s: lax.dynamic_index_in_dim(
            g.reshape(dp, tp, slice_rows, -1), level ^ s, 1, False
        ).reshape(depth, -1)
        plain = [fence(by_shard(gathered_out, s))[0].astype(jnp.bfloat16) for s in range(4)]
        out_plain = jnp.concatenate(plain, 1)
        out_pad = jnp.concatenate([dot32(w, p_out).astype(jnp.bfloat16) for w in plain], 1)

    hidden, normed_t, activ, dgate, dup, mlp_part = {}, {}, {}, {}, {}, {}

    def feed(j):
        gathered = (own[j], other[j], across[j], outer[j])
        (hidden[j], normed_t[j], activ[j], dgate[j], dup[j], mlp_part[j], part[j]) = forward_chunk(
            level_ref, gathered, tokens, dout, out_plain, mlp_gain, w_gate, w_up, w_down, j, rows
        )

    feed(c0)
    own, other, pair, across, outer, part, hidden = fence(
        own, other, pair, across, outer, part, hidden
    )
    add_1(c0)
    hop_3(c2)
    hop_2(c3)
    feed(c1)
    if by_hand:
        qkv_far, _ = fence(qkv_far, part[c0])
        qkv_far.append(to_level(qkv_slice, 3))
        qkv_mine.append(over_chips(qkv_far[1]))
    own, other, across, outer, part, total, hidden = fence(
        own, other, across, outer, part, total, hidden
    )
    add_2(c0)
    add_1(c1)
    hop_3(c3)
    feed(c2)
    if by_hand:
        qkv_far, qkv_mine, _ = fence(qkv_far, qkv_mine, part[c1])
        qkv_mine.append(over_chips(qkv_far[2]))
    own, other, across, outer, part, total, hidden = fence(
        own, other, across, outer, part, total, hidden
    )
    add_3(c0)
    add_2(c1)
    add_1(c2)
    feed(c3)
    if by_hand:
        qkv_mine, _ = fence(qkv_mine, part[c2])
        qkv_theirs = [swap(mine) for mine in qkv_mine]
    part, total, final, hidden, normed_t, activ, dgate, dup, mlp_part = fence(
        part, total, final, hidden, normed_t, activ, dgate, dup, mlp_part
    )
    add_3(c1)
    add_2(c2)
    add_1(c3)
    if by_hand:
        qkv_mine, qkv_theirs, _ = fence(qkv_mine, qkv_theirs, part[c3])
        (qkv_pad,) = spread(
            spread_qkv_kernel,
            meta,
            own_pad,
            [pq, pkv],
            qkv_mine,
            qkv_theirs,
            [4 * own_pad.shape[1]],
        )
    else:
        plain = [
            fence(by_shard(gathered_qkv, s))[0].astype(jnp.bfloat16) for s in range(4)
        ]
        qkv_pad = jnp.concatenate([dot32(w, p_all).astype(jnp.bfloat16) for w in plain], 1)
    qkv = project(normed_one, qkv_pad, cosines, sines)

    listed = lambda pieces: [pieces[j] for j in range(CHUNKS)]
    keep_side = jnp.stack([core, 2]).astype(jnp.int32)
    send_side = jnp.stack([1 - core, 2]).astype(jnp.int32)
    all_rows = jnp.array([0, 1], jnp.int32)

    def send_rows(groups, extra=None):
        if not by_hand:
            return rows_of(groups, all_rows, depth // 4, 4, extra)
        return swap(rows_of(groups, send_side, slice_rows, chips, extra))

    def keep_rows(groups, received, extra=None):
        if not by_hand:
            return received
        return rows_of(groups, keep_side, slice_rows, chips, extra, received)

    def scatter(array):
        axes = "chip" if by_hand else ("chip", "core")
        return lax.psum_scatter(array, axes, scatter_dimension=0, tiled=True)

    gate_groups = lambda: [(listed(normed_t), listed(dgate))]
    up_groups = lambda: [(listed(normed_t), listed(dup))]
    down_groups = lambda: [(dout_t, listed(activ))]
    received = [send_rows(gate_groups()), send_rows(up_groups()), send_rows(down_groups())]

    acc = None
    dhid_t, dqkv_own, input_grad, gains = {}, {}, {}, {}

    def back(j):
        nonlocal acc
        (dhid_t[j], dqkv_own[j], input_grad[j], gains[j]), acc = backward_chunk(
            level_ref,
            (total[j], final[j]),
            hidden[j],
            dout,
            tokens,
            (norm_gain, mlp_gain),
            (out_pad, qkv_pad),
            qkv,
            (own[j], other[j], across[j], outer[j]),
            (p_out, p_all.T),
            (cosines, sines),
            acc,
            j,
            rows,
        )

    total, final, hidden, qkv, received, mlp_part = fence(
        total, final, hidden, qkv, received, mlp_part
    )
    add_3(c2)
    add_2(c3)
    grad_gate = keep_rows(gate_groups(), received[0])
    grad_up = keep_rows(up_groups(), received[1])
    grad_down = keep_rows(down_groups(), received[2])
    back(c0)
    total, final, hidden, grad_gate, grad_up, grad_down, mlp_part, acc, dhid_t = fence(
        total, final, hidden, grad_gate, grad_up, grad_down, mlp_part, acc, dhid_t
    )
    add_3(c3)
    grad_gate = scatter(grad_gate)
    away = jnp.where(
        low,
        jnp.concatenate([mlp_part[2], mlp_part[3]], 0),
        jnp.concatenate([mlp_part[1], mlp_part[0]], 0),
    )
    away = away + along(away, INWARD)
    back(c1)
    total, final, hidden, away, acc, dhid_t, grad_gate, grad_up = fence(
        total, final, hidden, away, acc, dhid_t, grad_gate, grad_up
    )
    grad_up = scatter(grad_up)
    coming = along(away, MIDDLE)
    back(c2)
    total, final, hidden, coming, acc, dhid_t, grad_up, grad_down = fence(
        total, final, hidden, coming, acc, dhid_t, grad_up, grad_down
    )
    grad_down = scatter(grad_down)
    near = jnp.where(low, mlp_part[1], mlp_part[2])
    edge = jnp.where(low, mlp_part[0], mlp_part[3])
    last = along(jnp.where(inner, edge + coming[rows:], near), PAIRS)
    back(c3)

    dhid_t, dqkv_own, last = fence(dhid_t, dqkv_own, last)
    gain_sums = gains[0] + gains[1] + gains[2] + gains[3]
    extra = jnp.pad(gain_sums.T, ((0, 0), (0, LANES - 8)))
    attn_groups = [
        (listed(dhid_t), listed(own)),
        (normed_one_t, listed(dqkv_own)),
    ]
    attn = scatter(keep_rows(attn_groups, send_rows(attn_groups, extra), extra))
    mlp_rows = jnp.where(inner, near + coming[:rows], edge) + last
    hidden_rows = jnp.where(
        low,
        jnp.where(level == 0, hidden[0], hidden[1]),
        jnp.where(level == 2, hidden[2], hidden[3]),
    )
    layer_out = (hidden_rows + mlp_rows).astype(jnp.bfloat16)
    q_cols = heads_here * HD
    kv_cols = kv_here * HD
    ends = [q_cols, 2 * q_cols, 2 * q_cols + kv_cols, 2 * q_cols + 2 * kv_cols]
    return (
        layer_out,
        jnp.concatenate(listed(input_grad), 0),
        attn[:, ends[3]],
        attn[:, ends[0] : ends[1]],
        attn[:, ends[1] : ends[2]],
        attn[:, ends[2] : ends[3]],
        attn[:, : ends[0]].T,
        attn[:, ends[3] + 1],
        grad_gate,
        grad_up,
        grad_down.T,
    )


def solution(mesh):
    devices = mesh.devices
    dp, tp = devices.shape
    split = Mesh(devices.reshape(dp // 2, 2, tp), ("chip", "core", "tp"))
    data = ("chip", "core")
    return jax.shard_map(
        shards,
        mesh=split,
        in_specs=(
            P(data, None),
            P(data),
            P(data),
            P(data, None),
            P(),
            P(None, "tp"),
            P(None, "tp"),
            P(None, "tp"),
            P("tp", None),
            P(),
            P(None, "tp"),
            P(None, "tp"),
            P("tp", None),
        ),
        out_specs=(
            P(("chip", "core", "tp"), None),
            P(data, None),
            P(data),
            P(data, "tp"),
            P(data, "tp"),
            P(data, "tp"),
            P("tp", data),
            P(data),
            P(data, "tp"),
            P(data, "tp"),
            P("tp", data),
        ),
        check_vma=False,
    )
```

```python
import functools

import jax
import jax.numpy as jnp
from jax import lax
from jax.experimental import pallas as pl
from jax.experimental.pallas import tpu as pltpu
from jax.sharding import Mesh
from jax.sharding import PartitionSpec as P

HD = 96
LANES = 128
GROUP = 2
KV_WIDE = (GROUP + 2) * LANES
rope_base = 100000.0
norm_eps = 1e-05
masked_score = -1e30
far_away = 1e30
score_scale = HD ** (-0.5)
score_scale_log2 = score_scale * 1.4426950408889634
CHUNKS = 4
EXTRA = 8
VMEM_BYTES = 56 * 1024 * 1024
NT = (((1,), (1,)), ((), ()))


def params():
    return pltpu.CompilerParams(vmem_limit_bytes=VMEM_BYTES)


def cost(flops, moved, exps=0):
    return pl.CostEstimate(flops=flops, bytes_accessed=moved, transcendentals=exps)


def dot32(a, b):
    return jnp.dot(a, b, preferred_element_type=jnp.float32)


def dot32_nt(a, b):
    return lax.dot_general(a, b, NT, preferred_element_type=jnp.float32)


def dot_split(a, places):
    high = a.astype(jnp.bfloat16)
    rest = (a - high.astype(jnp.float32)).astype(jnp.bfloat16)
    return dot32(high, places) + dot32(rest, places)


def fence(*trees):
    return lax.optimization_barrier(trees)


def whole(array, buffers=None):
    zeros = (0,) * len(array.shape)
    return pl.BlockSpec(array.shape, lambda *_: zeros)


SCALAR = pl.BlockSpec(memory_space=pltpu.SMEM)


def halves(entry):
    half_dim = HD // 2
    return (entry // half_dim) * (LANES // 2) + entry % half_dim


def placement(lanes, width):
    return (lanes[:, None] == jnp.arange(width)[None, :]).astype(jnp.bfloat16)


def place_query(heads):
    source = jnp.arange(heads * HD)
    return placement((source // HD) * LANES + halves(source % HD), heads * LANES)


def place_key_value(kv_heads):
    source = jnp.arange(kv_heads * HD)
    head = source // HD
    keys = head * 2 * LANES + halves(source % HD)
    values = head * 2 * LANES + LANES + source % HD
    return placement(jnp.concatenate([keys, values]), kv_heads * 2 * LANES)


def place_all(heads, kv_heads):
    source = jnp.arange(heads * HD)
    head = source // HD
    query = (head // GROUP) * KV_WIDE + (head % GROUP) * LANES + halves(source % HD)
    source = jnp.arange(kv_heads * HD)
    base = (source // HD) * KV_WIDE + GROUP * LANES
    keys = base + halves(source % HD)
    values = base + LANES + source % HD
    return placement(jnp.concatenate([query, keys, values]), kv_heads * KV_WIDE)


def place_plain(heads):
    source = jnp.arange(heads * HD)
    return placement((source // HD) * LANES + source % HD, heads * LANES)


PAIRS = [(0, 1), (1, 0), (2, 3), (3, 2)]
INWARD = [(0, 1), (3, 2)]
MIDDLE = [(1, 2), (2, 1)]
OUTWARD = [(1, 0), (2, 3)]


def along(part, pairs):
    return lax.ppermute(part, "tp", pairs)


def store_qkv(out_ref, here, base, query, key_value):
    wide = GROUP * LANES
    for kv in range(key_value.shape[1] // (2 * LANES)):
        at = base + kv * KV_WIDE
        there = slice(kv * 2 * LANES, (kv + 1) * 2 * LANES)
        out_ref[here, at : at + wide] = query[:, kv * wide : (kv + 1) * wide]
        out_ref[here, at + wide : at + KV_WIDE] = key_value[:, there]


def store_turned(out_ref, at, lin, cos_ref, sin_ref):
    for h in range(GROUP + 2):
        one = lin[:, h * LANES : (h + 1) * LANES]
        if h < GROUP + 1:
            one = one * cos_ref[...] + pltpu.roll(one, LANES // 2, 1) * sin_ref[...]
        out_ref[:, at + h * LANES : at + (h + 1) * LANES] = one.astype(jnp.bfloat16)


def spread_out_kernel(meta_ref, own_ref, p_ref, mine_ref, theirs_ref, pad_ref, plain_ref):
    rows, width = mine_ref.shape[2:]
    wide = p_ref.shape[1]
    for side, ref in enumerate((mine_ref, theirs_ref)):
        here = pl.ds(pl.multiple_of((meta_ref[1] ^ side) * rows, rows), rows)
        for s in range(4):
            block = own_ref[here, :] if s == 0 else ref[0, s - 1].astype(jnp.bfloat16)
            plain_ref[here, s * width : (s + 1) * width] = block
            pad_ref[here, s * wide : (s + 1) * wide] = dot32(block, p_ref[...]).astype(
                jnp.bfloat16
            )


def spread_qkv_kernel(meta_ref, own_ref, pq_ref, pkv_ref, mine_ref, theirs_ref, out_ref):
    rows = mine_ref.shape[2]
    wide = own_ref.shape[1]
    split = pq_ref.shape[0]
    out_ref[:, :wide] = own_ref[...]
    for side, ref in enumerate((mine_ref, theirs_ref)):
        here = pl.ds(pl.multiple_of((meta_ref[1] ^ side) * rows, rows), rows)
        for s in range(1, 4):
            block = ref[0, s - 1].astype(jnp.bfloat16)
            query = dot32(block[:, :split], pq_ref[...]).astype(jnp.bfloat16)
            key_value = dot32(block[:, split:], pkv_ref[...]).astype(jnp.bfloat16)
            store_qkv(out_ref, here, s * wide, query, key_value)


def spread(kernel, meta, own, places, mine, theirs, widths):
    chips, others, rows, width = mine.shape
    total = own.shape[0]
    row_block = lambda m, meta: (meta[0] ^ m, 0)
    piece = pl.BlockSpec((1, others, rows, width), lambda m, meta: (m, 0, 0, 0))
    return pl.pallas_call(
        kernel,
        out_shape=[jax.ShapeDtypeStruct((total, wide), jnp.bfloat16) for wide in widths],
        grid_spec=pltpu.PrefetchScalarGridSpec(
            num_scalar_prefetch=1,
            grid=(chips,),
            in_specs=[pl.BlockSpec((2 * rows, own.shape[1]), row_block)]
            + [whole(place) for place in places]
            + [piece, piece],
            out_specs=[pl.BlockSpec((2 * rows, wide), row_block) for wide in widths],
        ),
        compiler_params=params(),
        cost_estimate=cost(
            8 * total * width * 512, total * (12 * width + 2 * sum(widths))
        ),
    )(meta, own, *places, mine, theirs)


def start_kernel(x_ref, gain_ref, q_ref, k_ref, v_ref, pq_ref, pkv_ref, cos_ref, sin_ref, *outs):
    qkv_ref, normed_ref, pad_ref = outs

    @pl.when(pl.program_id(0) == 0)
    def _():
        split = k_ref.shape[0]
        query = dot32(q_ref[...], pq_ref[...]).astype(jnp.bfloat16)
        key_value = dot32(k_ref[...].T, pkv_ref[:split, :])
        key_value = key_value + dot32(v_ref[...].T, pkv_ref[split:, :])
        store_qkv(pad_ref, slice(None), 0, query, key_value.astype(jnp.bfloat16))

    inputs = x_ref[...].astype(jnp.float32)
    rms = lax.rsqrt(jnp.mean(inputs * inputs, -1, keepdims=True) + norm_eps)
    normed = (inputs * rms * gain_ref[...]).astype(jnp.bfloat16)
    normed_ref[...] = normed
    for kv in range(pad_ref.shape[1] // KV_WIDE):
        at = kv * KV_WIDE
        store_turned(qkv_ref, at, dot32(normed, pad_ref[:, at : at + KV_WIDE]), cos_ref, sin_ref)


def start(tokens, gain, w_query, w_key_t, w_value_t, pq, pkv, cosines, sines):
    total, depth = tokens.shape
    rows = total // CHUNKS
    wide = pq.shape[1] + pkv.shape[1]
    gain = gain[None, :]
    by_rows = lambda width: pl.BlockSpec((rows, width), lambda i: (i, 0))
    arrays = [w_query, w_key_t, w_value_t, pq, pkv]
    shapes = [
        jax.ShapeDtypeStruct((total, wide), jnp.bfloat16),
        jax.ShapeDtypeStruct((total, depth), jnp.bfloat16),
        jax.ShapeDtypeStruct((depth, wide), jnp.bfloat16),
    ]
    return pl.pallas_call(
        start_kernel,
        out_shape=shapes,
        grid=(CHUNKS,),
        in_specs=[by_rows(depth), whole(gain)]
        + [whole(array) for array in arrays]
        + [by_rows(LANES), by_rows(LANES)],
        out_specs=[by_rows(wide), by_rows(depth), whole(shapes[2])],
        compiler_params=params(),
        cost_estimate=cost(2 * total * depth * wide, 12 * total * depth),
    )(tokens, gain, *arrays, cosines, sines)


def turn_kernel(length_ref, cot_ref, normed_ref, dout_ref, dout_t_ref, normed_t_ref):
    rows = cot_ref.shape[0]
    at = pl.program_id(0) * rows + lax.broadcasted_iota(jnp.int32, cot_ref.shape, 0)
    dout = jnp.where(at < length_ref[0], cot_ref[...].astype(jnp.float32), 0.0)
    dout = dout.astype(jnp.bfloat16)
    dout_ref[...] = dout
    dout_t_ref[...] = dout.T
    normed_t_ref[...] = normed_ref[...].T


def turn(length, cotangent, normed):
    total, depth = cotangent.shape
    rows = total // CHUNKS
    by_rows = pl.BlockSpec((rows, depth), lambda i: (i, 0))
    by_columns = pl.BlockSpec((depth, rows), lambda i: (0, i))
    turned = jax.ShapeDtypeStruct((depth, total), jnp.bfloat16)
    return pl.pallas_call(
        turn_kernel,
        out_shape=[jax.ShapeDtypeStruct((total, depth), jnp.bfloat16), turned, turned],
        grid=(CHUNKS,),
        in_specs=[SCALAR, by_rows, by_rows],
        out_specs=[by_rows, by_columns, by_columns],
        compiler_params=params(),
        cost_estimate=cost(total * depth, 10 * total * depth),
    )(length, cotangent, normed)


def project_kernel(x_ref, w_ref, cos_ref, sin_ref, out_ref):
    store_turned(out_ref, 0, dot32(x_ref[...], w_ref[...]), cos_ref, sin_ref)


def project(normed, weights, cosines, sines):
    rows, depth = normed.shape
    width = weights.shape[1]
    return pl.pallas_call(
        project_kernel,
        out_shape=jax.ShapeDtypeStruct((rows, width), jnp.bfloat16),
        grid=(width // KV_WIDE,),
        in_specs=[
            whole(normed),
            pl.BlockSpec((depth, KV_WIDE), lambda i: (0, i)),
            whole(cosines),
            whole(sines),
        ],
        out_specs=pl.BlockSpec((rows, KV_WIDE), lambda i: (0, i)),
        compiler_params=params(),
        cost_estimate=cost(
            2 * rows * depth * width, 2 * (rows * depth + depth * width + rows * width)
        ),
    )(normed, weights, cosines, sines)


def attend_kernel(start, length_ref, q_ref, kv_ref, strip_ref, out_ref):
    rows = q_ref.shape[0]
    keys = kv_ref.shape[0]
    length = length_ref[0]
    row_ids = start + lax.broadcasted_iota(jnp.int32, (1, rows), 1)
    limit = jnp.minimum(row_ids, length - 1)
    allowed = lax.broadcasted_iota(jnp.int32, (keys, rows), 0) <= limit
    mixed = []
    sums = []
    for kv in range(kv_ref.shape[1] // KV_WIDE):
        base = kv * KV_WIDE
        at = base + GROUP * LANES
        key = kv_ref[:, at : at + LANES]
        value_t = kv_ref[:, at + LANES : at + 2 * LANES].T
        for g in range(GROUP):
            query = q_ref[:, base + g * LANES : base + (g + 1) * LANES]
            raw = jnp.where(allowed, dot32_nt(key, query), masked_score)
            peak = jnp.max(raw, axis=0, keepdims=True)
            expo = jnp.exp2((raw - peak) * score_scale_log2)
            total = jnp.sum(expo, axis=0, keepdims=True)
            probs = (expo * (1.0 / total)).astype(jnp.bfloat16)
            mixed.append(dot32(value_t, probs).T)
            log_sum = peak * score_scale_log2 + jnp.log2(total)
            sums.append(jnp.where(row_ids < length, log_sum, far_away))
    out_ref[:rows, :] = dot_split(jnp.concatenate(mixed, 1), strip_ref[...])
    out_ref[rows:, :] = jnp.zeros((EXTRA, out_ref.shape[1]), jnp.float32)
    out_ref[rows : rows + len(sums), :rows] = jnp.concatenate(sums, 0)


def attend(length, qkv, strip, index, rows):
    keys = (index + 1) * rows
    width = qkv.shape[1]
    heads = width // KV_WIDE * GROUP
    shape = (rows + EXTRA, strip.shape[1])
    return pl.pallas_call(
        functools.partial(attend_kernel, index * rows),
        out_shape=jax.ShapeDtypeStruct(shape, jnp.float32),
        grid=(1,),
        in_specs=[
            SCALAR,
            pl.BlockSpec((rows, width), lambda i: (index, 0)),
            pl.BlockSpec((keys, width), lambda i: (0, 0)),
            whole(strip),
        ],
        out_specs=pl.BlockSpec(shape, lambda i: (0, 0)),
        compiler_params=params(),
        cost_estimate=cost(
            4 * heads * rows * keys * LANES, 2 * (rows + keys) * width, heads * rows * keys
        ),
    )(length, qkv, qkv, strip)


def forward_kernel(level_ref, part_ref, other_ref, across_ref, outer_ref, *refs):
    x_ref, dout_ref, wo_ref, gain_ref, wg_ref, wu_ref, wd_ref = refs[:7]
    hidden_ref, normed_t_ref, activ_ref, dgate_ref, dup_ref, mlp_ref, dn_ref = refs[7:14]
    normed_ref = refs[14]
    rows = x_ref.shape[0]

    @pl.when(pl.program_id(0) == 0)
    def _():
        level = level_ref[0]
        inner = (level == 1) | (level == 2)
        width = part_ref.shape[1]
        second = jnp.where(inner, across_ref[:rows, width:], outer_ref[:rows, :width])
        third = jnp.where(inner, across_ref[:rows, :width], outer_ref[:rows, width:])
        mixed = jnp.concatenate([part_ref[:rows, :], other_ref[:rows, :], second, third], 1)
        hidden = x_ref[...].astype(jnp.float32) + dot32_nt(mixed.astype(jnp.bfloat16), wo_ref[...])
        hidden_ref[...] = hidden
        rms = lax.rsqrt(jnp.mean(hidden * hidden, -1, keepdims=True) + norm_eps)
        normed = (hidden * rms * gain_ref[...]).astype(jnp.bfloat16)
        normed_ref[...] = normed
        normed_t_ref[...] = normed.T
        mlp_ref[...] = jnp.zeros_like(mlp_ref)
        dn_ref[...] = jnp.zeros_like(dn_ref)

    normed = normed_ref[...]
    gate = dot32(normed, wg_ref[...])
    up = dot32(normed, wu_ref[...])
    dact = dot32_nt(dout_ref[...], wd_ref[...])
    sigmoid = jax.nn.sigmoid(gate)
    silu = gate * sigmoid
    activ = (silu * up).astype(jnp.bfloat16)
    dgate = (dact * up * sigmoid * (1.0 + gate * (1.0 - sigmoid))).astype(jnp.bfloat16)
    dup = (dact * silu).astype(jnp.bfloat16)
    activ_ref[...] = activ
    dgate_ref[...] = dgate
    dup_ref[...] = dup
    mlp_ref[...] += dot32(activ, wd_ref[...])
    dn_ref[...] += dot32_nt(dgate, wg_ref[...]) + dot32_nt(dup, wu_ref[...])


def forward_chunk(level, gathered, tokens, dout, w_out, gain, w_gate, w_up, w_down, index, rows):
    depth = tokens.shape[1]
    units = w_gate.shape[1]
    block = 256
    own_rows = pl.BlockSpec((rows, depth), lambda i: (index, 0))
    by_units = pl.BlockSpec((depth, block), lambda i: (0, i))
    gain = gain[None, :]
    f32, bf16 = jnp.float32, jnp.bfloat16
    outs = [
        jax.ShapeDtypeStruct((rows, depth), f32),
        jax.ShapeDtypeStruct((depth, rows), bf16),
        jax.ShapeDtypeStruct((rows, units), bf16),
        jax.ShapeDtypeStruct((rows, units), bf16),
        jax.ShapeDtypeStruct((rows, units), bf16),
        jax.ShapeDtypeStruct((rows, depth), f32),
        jax.ShapeDtypeStruct((rows, depth), f32),
    ]
    unit_out = pl.BlockSpec((rows, block), lambda i: (0, i))
    return pl.pallas_call(
        forward_kernel,
        out_shape=outs,
        grid=(units // block,),
        in_specs=[SCALAR]
        + [whole(array) for array in gathered]
        + [own_rows, own_rows, whole(w_out), whole(gain), by_units, by_units]
        + [pl.BlockSpec((block, depth), lambda i: (i, 0))],
        out_specs=[
            whole(outs[0]),
            whole(outs[1]),
            unit_out,
            unit_out,
            unit_out,
            whole(outs[5]),
            whole(outs[6]),
        ],
        scratch_shapes=[pltpu.VMEM((rows, depth), bf16)],
        compiler_params=params(),
        cost_estimate=cost(
            2 * rows * depth * (6 * units + w_out.shape[1]),
            2 * depth * (3 * units + w_out.shape[1]) + 22 * rows * depth,
            rows * units,
        ),
    )(level, *gathered, tokens, dout, w_out, gain, w_gate, w_up, w_down)


def backward_kernel(start, kv_here, level_ref, total_ref, final_ref, hidden_ref, dout_ref, x_ref, *refs):
    gain_one_ref, gain_two_ref, wo_ref, w_ref, q_ref, k_ref, v_ref = refs[:7]
    part_ref, other_ref, across_ref, outer_ref, place_ref, strip_ref = refs[7:13]
    cos_ref, sin_ref = refs[13:15]
    dhid_ref, low_ref, dn_ref = refs[-3:]
    outs = refs[15:-3]
    count = 5 if start > 0 else 4
    acc_ref = outs[0] if len(outs) > count else None
    outs = outs[-count:]
    dhid_t_ref, dqkv_ref, input_grad_ref, gains_ref = outs[:4]
    rows = q_ref.shape[0]
    keys = k_ref.shape[0]
    head = pl.program_id(0)
    level = level_ref[0]
    inner = (level == 1) | (level == 2)
    shard = head // kv_here
    kv = head % kv_here

    @pl.when(head == 0)
    def _():
        dnormed = jnp.where(inner, total_ref[...], final_ref[...])
        hidden = hidden_ref[...]
        rms = lax.rsqrt(jnp.mean(hidden * hidden, -1, keepdims=True) + norm_eps)
        scaled = dnormed * gain_two_ref[...]
        shift = jnp.mean(scaled * hidden, -1, keepdims=True)
        dhid = dout_ref[...].astype(jnp.float32) + (rms * scaled - hidden * (rms**3 * shift))
        dhid_ref[...] = dhid
        low = dhid.astype(jnp.bfloat16)
        low_ref[...] = low
        dhid_t_ref[...] = low.T
        gains_ref[...] = jnp.zeros_like(gains_ref)
        gains_ref[1:2, :] = jnp.sum(dnormed * (hidden * rms), 0, keepdims=True)
        dn_ref[...] = jnp.zeros_like(dn_ref)

    def rotate_back(grads):
        turned = grads * cos_ref[...] - pltpu.roll(grads, LANES // 2, 1) * sin_ref[...]
        return turned.astype(jnp.bfloat16)

    dmixed_all = dot32(low_ref[...], wo_ref[...]).astype(jnp.bfloat16)
    mixed = jnp.where(
        shard == 0,
        part_ref[...],
        jnp.where(shard == 1, other_ref[...], jnp.where(inner, across_ref[...], outer_ref[...])),
    )
    products = dmixed_all.astype(jnp.float32) * dot_split(mixed[:rows], place_ref[...])
    all_sums = mixed[rows:, :rows]
    sum_rows = lax.broadcasted_iota(jnp.int32, all_sums.shape, 0)
    causal = lax.broadcasted_iota(jnp.int32, (rows, rows), 0) <= lax.broadcasted_iota(
        jnp.int32, (rows, rows), 1
    )
    row_dots = []
    log_sums = []
    for g in range(GROUP):
        here = slice(g * LANES, (g + 1) * LANES)
        row_dots.append(jnp.sum(products[:, here].T, axis=0, keepdims=True))
        picked = jnp.where(sum_rows == kv * GROUP + g, all_sums, 0.0)
        log_sums.append(jnp.sum(picked, axis=0, keepdims=True))
    dqueries = [None] * GROUP
    for tile in range(keys // rows):
        span = slice(tile * rows, (tile + 1) * rows)
        key = k_ref[span, :]
        value = v_ref[span, :]
        key_t = key.T
        dkey = None if acc_ref is None else acc_ref[span, :LANES]
        dvalue = None if acc_ref is None else acc_ref[span, LANES:]
        last = tile * rows == start
        for g in range(GROUP):
            here = slice(g * LANES, (g + 1) * LANES)
            query = q_ref[:, here]
            dmixed = dmixed_all[:, here]
            raw = dot32_nt(key, query)
            probs = jnp.exp2(raw * score_scale_log2 - log_sums[g])
            if last:
                probs = jnp.where(causal, probs, 0.0)
            dprobs = dot32_nt(value, dmixed)
            dscores = (probs * (dprobs - row_dots[g])).astype(jnp.bfloat16)
            dquery = dot32(key_t, dscores)
            dqueries[g] = dquery if dqueries[g] is None else dqueries[g] + dquery
            dkey_one = dot32(dscores, query)
            dvalue_one = dot32(probs.astype(jnp.bfloat16), dmixed)
            dkey = dkey_one if dkey is None else dkey + dkey_one
            dvalue = dvalue_one if dvalue is None else dvalue + dvalue_one
        if not last:
            outs[4][span, :LANES] = dkey
            outs[4][span, LANES:] = dvalue
    grads = [rotate_back(dquery.T * score_scale) for dquery in dqueries]
    grads.append(rotate_back(dkey * score_scale))
    grads.append(dvalue.astype(jnp.bfloat16))
    grads = jnp.concatenate(grads, 1)
    dn_ref[...] += dot32_nt(grads, w_ref[...])

    @pl.when(head < kv_here)
    def _():
        dqkv_ref[...] = dot32(grads, strip_ref[...]).astype(jnp.bfloat16)

    @pl.when(head == pl.num_programs(0) - 1)
    def _():
        dnormed = dn_ref[...]
        inputs = x_ref[...].astype(jnp.float32)
        rms = lax.rsqrt(jnp.mean(inputs * inputs, -1, keepdims=True) + norm_eps)
        scaled = dnormed * gain_one_ref[...]
        shift = jnp.mean(scaled * inputs, -1, keepdims=True)
        grad = dhid_ref[...] + (rms * scaled - inputs * (rms**3 * shift))
        input_grad_ref[...] = grad.astype(jnp.bfloat16)
        gains_ref[0:1, :] = jnp.sum(dnormed * (inputs * rms), 0, keepdims=True)


def backward_chunk(level, sums_two, hidden, dout, tokens, gains, weights, qkv, gathered, places,
                   tables, acc, index, rows):
    start = index * rows
    keys = start + rows
    depth = tokens.shape[1]
    out_pad, qkv_pad = weights
    place_out, strip = places
    heads = qkv.shape[1] // KV_WIDE
    kv_here = place_out.shape[1] // (GROUP * LANES)
    width = gathered[0].shape[1]
    far_rows = gathered[0].shape[0]
    wide = GROUP * LANES
    own_rows = pl.BlockSpec((rows, depth), lambda h: (index, 0))
    table = pl.BlockSpec((rows, LANES), lambda h: (index, 0))
    gains = [gain[None, :] for gain in gains]
    across = pl.BlockSpec((far_rows, width), lambda h: (0, jnp.where(h < 3 * kv_here, 1, 0)))
    outer = pl.BlockSpec((far_rows, width), lambda h: (0, jnp.where(h < 3 * kv_here, 0, 1)))
    in_specs = [
        SCALAR,
        whole(sums_two[0]),
        whole(sums_two[1]),
        whole(hidden),
        own_rows,
        own_rows,
        whole(gains[0]),
        whole(gains[1]),
        pl.BlockSpec((depth, wide), lambda h: (0, h)),
        pl.BlockSpec((depth, KV_WIDE), lambda h: (0, h)),
        pl.BlockSpec((rows, wide), lambda h: (index, 2 * h)),
        pl.BlockSpec((keys, LANES), lambda h: (0, 4 * h + 2)),
        pl.BlockSpec((keys, LANES), lambda h: (0, 4 * h + 3)),
        whole(gathered[0]),
        whole(gathered[1]),
        across,
        outer,
        pl.BlockSpec((width, wide), lambda h: (0, h % kv_here)),
        whole(strip),
        table,
        table,
    ]
    args = [level, *sums_two, hidden, dout, tokens, *gains, out_pad, qkv_pad, qkv, qkv, qkv]
    args += [*gathered, place_out, strip, *tables]
    if acc is not None:
        in_specs.append(pl.BlockSpec((keys, 2 * LANES), lambda h: (0, h)))
        args.append(acc)
    f32, bf16 = jnp.float32, jnp.bfloat16
    outs = [
        jax.ShapeDtypeStruct((depth, rows), bf16),
        jax.ShapeDtypeStruct((rows, kv_here * strip.shape[1]), bf16),
        jax.ShapeDtypeStruct((rows, depth), bf16),
        jax.ShapeDtypeStruct((8, depth), f32),
    ]
    out_specs = [whole(out) for out in outs]
    out_specs[1] = pl.BlockSpec(
        (rows, strip.shape[1]), lambda h: (0, jnp.minimum(h, kv_here - 1))
    )
    if start > 0:
        outs.append(jax.ShapeDtypeStruct((start, heads * 2 * LANES), f32))
        out_specs.append(pl.BlockSpec((start, 2 * LANES), lambda h: (0, h)))
    results = pl.pallas_call(
        functools.partial(backward_kernel, start, kv_here),
        out_shape=outs,
        grid=(heads,),
        in_specs=in_specs,
        out_specs=out_specs,
        scratch_shapes=[
            pltpu.VMEM((rows, depth), f32),
            pltpu.VMEM((rows, depth), bf16),
            pltpu.VMEM((rows, depth), f32),
        ],
        compiler_params=params(),
        cost_estimate=cost(
            heads * rows * (20 * keys * LANES + 2 * depth * (wide + KV_WIDE)),
            2 * depth * heads * (wide + KV_WIDE) + 16 * keys * heads * LANES + 16 * rows * depth,
            heads * GROUP * rows * keys,
        ),
    )(*args)
    return results[:4], (results[4] if start > 0 else None)


def rows_kernel(lefts, extras, adding, side_ref, *refs):
    refs = list(refs)
    held_ref = refs.pop()
    out_ref = refs.pop()
    recv_ref = refs.pop() if adding else None
    left_refs, refs = refs[:lefts], refs[lefts:]
    rights, extra_refs = refs[:CHUNKS], refs[CHUNKS:]
    rows = left_refs[0].shape[0]
    blocks = held_ref.shape[0] // rows

    @pl.when(pl.program_id(0) == 0)
    def _():
        for n, ref in enumerate(left_refs):
            m, j = n % blocks, n // blocks
            wide = ref.shape[1]
            held_ref[m * rows : (m + 1) * rows, j * wide : (j + 1) * wide] = ref[...]

    chunk = held_ref.shape[1] // CHUNKS
    right = jnp.concatenate([ref[:chunk, :].astype(jnp.bfloat16) for ref in rights], 0)
    total = dot32(held_ref[...], right)
    width = total.shape[1]
    out_ref[:, :width] = total if recv_ref is None else total + recv_ref[:, :width]
    for m in range(extras):
        here = slice(m * rows, (m + 1) * rows)
        more = extra_refs[m][...]
        out_ref[here, width:] = more if recv_ref is None else more + recv_ref[here, width:]


def rows_of(left, rights, side, rows, blocks, steps, extra=None, recv=None):
    pieces = left if isinstance(left, list) else [left]
    at = lambda m: lambda i, side: (m * side[1] + side[0], 0)
    specs = []
    args = []
    for piece in pieces:
        for m in range(blocks):
            specs.append(pl.BlockSpec((rows, piece.shape[1]), at(m)))
            args.append(piece)
    lefts = len(args)
    width = rights[0].shape[1]
    step = width // steps
    for right in rights:
        specs.append(pl.BlockSpec((right.shape[0], step), lambda i, side: (0, i)))
        args.append(right)
    total = width
    if extra is not None:
        for m in range(blocks):
            specs.append(pl.BlockSpec((rows, extra.shape[1]), at(m)))
            args.append(extra)
        total += extra.shape[1]
        step += extra.shape[1]
    block = pl.BlockSpec((rows * blocks, step), lambda i, side: (0, i))
    if recv is not None:
        specs.append(block)
        args.append(recv)
    tokens = sum(piece.shape[1] for piece in pieces)
    return pl.pallas_call(
        functools.partial(rows_kernel, lefts, 0 if extra is None else blocks, recv is not None),
        out_shape=jax.ShapeDtypeStruct((rows * blocks, total), jnp.float32),
        grid_spec=pltpu.PrefetchScalarGridSpec(
            num_scalar_prefetch=1,
            grid=(steps,),
            in_specs=specs,
            out_specs=block,
            scratch_shapes=[pltpu.VMEM((rows * blocks, tokens), jnp.bfloat16)],
        ),
        compiler_params=params(),
        cost_estimate=cost(
            2 * rows * blocks * tokens * width,
            4 * rows * blocks * total + 2 * tokens * (width + rows * blocks),
        ),
    )(side, *args)


def shards(
    tokens,
    lengths,
    positions,
    cotangent,
    norm_gain,
    w_query,
    w_key,
    w_value,
    w_out,
    mlp_gain,
    w_gate,
    w_up,
    w_down,
):
    seq_rows, depth = tokens.shape
    chips = lax.axis_size("chip")
    dp = chips * 2
    tp = lax.axis_size("tp")
    chip = lax.axis_index("chip")
    core = lax.axis_index("core")
    level = lax.axis_index("tp")
    low = level < 2
    inner = (level == 1) | (level == 2)
    heads_here = w_query.shape[1] // HD
    kv_here = w_key.shape[1] // HD
    rows = seq_rows // CHUNKS
    slice_rows = depth // dp
    level_ref = level.astype(jnp.int32).reshape(1)
    by_hand = dp == 8
    swap = lambda array: lax.ppermute(array, "core", [(0, 1), (1, 0)])
    to_level = lambda array, s: along(array, [(t, t ^ s) for t in range(tp)])

    at_row = (chip * 2 + core) * slice_rows
    cols = lambda w: lax.dynamic_slice_in_dim(w, at_row, slice_rows, 1).astype(jnp.float32).T
    (out_slice,) = fence(cols(w_out))
    if by_hand:
        out_far = [to_level(out_slice, s) for s in (1, 2, 3)]
    qkv_slice = jnp.concatenate(
        [
            lax.dynamic_slice_in_dim(w_query, at_row, slice_rows, 0).astype(jnp.float32),
            cols(w_key.T),
            cols(w_value.T),
        ],
        1,
    )
    meta = jnp.stack([chip, core]).astype(jnp.int32)

    pq = place_query(heads_here)
    pkv = place_key_value(kv_here)
    p_all = place_all(heads_here, kv_here)
    strip_one = place_all(GROUP, 1).T
    p_out = place_plain(heads_here)
    strip_out = p_out.T

    half_dim = HD // 2
    freqs = rope_base ** (-(jnp.arange(half_dim).astype(jnp.float32) * 2.0 / HD))
    freqs = jnp.pad(freqs, (0, LANES // 2 - half_dim))
    angles = positions.astype(jnp.float32)[:, None] * jnp.concatenate([freqs, freqs])[None, :]
    cosines = jnp.cos(angles)
    sines = jnp.sin(angles) * jnp.where(jnp.arange(LANES) < LANES // 2, -1.0, 1.0)

    qkv_own, normed_one, own_pad = start(
        tokens, norm_gain, w_query, w_key.T, w_value.T, pq, pkv, cosines, sines
    )

    order = list(reversed(range(CHUNKS)))
    c0, c1, c2, c3 = order
    own, other, pair, across, outer = {}, {}, {}, {}, {}
    part, total, final = {}, {}, {}

    def hop_1(j):
        other[j] = along(own[j], PAIRS)
        pair[j] = jnp.concatenate([own[j], other[j]], 1)

    def hop_2(j):
        across[j] = along(pair[j], MIDDLE)

    def hop_3(j):
        outer[j] = along(across[j], OUTWARD)

    def add_1(j):
        total[j] = part[j] + along(part[j], INWARD)

    def add_2(j):
        total[j] = total[j] + along(total[j], MIDDLE)

    def add_3(j):
        final[j] = along(total[j], OUTWARD)

    def over_chips(piece):
        return [piece] + [
            lax.ppermute(piece, "chip", [(i, i ^ m) for i in range(chips)])
            for m in range(1, chips)
        ]

    qkv_own, qkv_slice = fence(qkv_own, qkv_slice)
    if by_hand:
        (out_far,) = fence(out_far)
        out_mine = over_chips(jnp.stack(out_far))
        qkv_far = [to_level(qkv_slice, s) for s in (1, 2, 3)]
    else:
        gathered_out = lax.all_gather(out_slice, ("chip", "core", "tp"))
        gathered_qkv = lax.all_gather(qkv_slice, ("chip", "core", "tp"))
    own[c0] = attend(lengths, qkv_own, strip_out, c0, rows)
    own, qkv_own = fence(own, qkv_own)
    hop_1(c0)
    for j in (c1, c2, c3):
        own[j] = attend(lengths, qkv_own, strip_out, j, rows)
    own, other, pair, normed_one, w_out = fence(own, other, pair, normed_one, w_out)
    hop_2(c0)
    hop_1(c1)
    dout, dout_t, normed_one_t = turn(lengths, cotangent, normed_one)
    w_out_t = w_out.T
    own, other, pair, across, dout, w_out_t = fence(own, other, pair, across, dout, w_out_t)
    hop_3(c0)
    hop_2(c1)
    hop_1(c2)
    if by_hand:
        out_mine, _ = fence(out_mine, across)
        out_mine = jnp.stack(out_mine)
        out_theirs = swap(out_mine)
    own, other, pair, across, outer = fence(own, other, pair, across, outer)
    hop_3(c1)
    hop_2(c2)
    hop_1(c3)
    if by_hand:
        out_mine, out_theirs, qkv_far, _ = fence(out_mine, out_theirs, qkv_far, outer)
        qkv_mine = over_chips(jnp.stack(qkv_far))
        out_pad, out_plain = spread(
            spread_out_kernel,
            meta,
            w_out_t,
            [p_out],
            out_mine,
            out_theirs,
            [4 * p_out.shape[1], 4 * p_out.shape[0]],
        )
    else:
        by_shard = lambda g, s: lax.dynamic_index_in_dim(
            g.reshape(dp, tp, slice_rows, -1), level ^ s, 1, False
        ).reshape(depth, -1)
        plain = [fence(by_shard(gathered_out, s))[0].astype(jnp.bfloat16) for s in range(4)]
        out_plain = jnp.concatenate(plain, 1)
        out_pad = jnp.concatenate([dot32(w, p_out).astype(jnp.bfloat16) for w in plain], 1)

    hidden, normed_t, activ, dgate, dup, mlp_part = {}, {}, {}, {}, {}, {}

    def feed(j):
        gathered = (own[j], other[j], across[j], outer[j])
        (hidden[j], normed_t[j], activ[j], dgate[j], dup[j], mlp_part[j], part[j]) = forward_chunk(
            level_ref, gathered, tokens, dout, out_plain, mlp_gain, w_gate, w_up, w_down, j, rows
        )

    feed(c0)
    own, other, pair, across, outer, part, hidden = fence(
        own, other, pair, across, outer, part, hidden
    )
    add_1(c0)
    hop_3(c2)
    hop_2(c3)
    feed(c1)
    own, other, across, outer, part, total, hidden = fence(
        own, other, across, outer, part, total, hidden
    )
    add_2(c0)
    add_1(c1)
    hop_3(c3)
    feed(c2)
    if by_hand:
        qkv_mine, _ = fence(qkv_mine, part[c2])
        qkv_mine = jnp.stack(qkv_mine)
        qkv_theirs = swap(qkv_mine)
    own, other, across, outer, part, total, hidden = fence(
        own, other, across, outer, part, total, hidden
    )
    add_3(c0)
    add_2(c1)
    add_1(c2)
    feed(c3)
    if by_hand:
        qkv_mine, qkv_theirs, _ = fence(qkv_mine, qkv_theirs, part[c3])
        (qkv_pad,) = spread(
            spread_qkv_kernel,
            meta,
            own_pad,
            [pq, pkv],
            qkv_mine,
            qkv_theirs,
            [4 * own_pad.shape[1]],
        )
    else:
        plain = [
            fence(by_shard(gathered_qkv, s))[0].astype(jnp.bfloat16) for s in range(4)
        ]
        qkv_pad = jnp.concatenate([dot32(w, p_all).astype(jnp.bfloat16) for w in plain], 1)
    qkv = project(normed_one, qkv_pad, cosines, sines)

    listed = lambda pieces: [pieces[j] for j in range(CHUNKS)]
    keep_side = jnp.stack([core, 2]).astype(jnp.int32)
    send_side = jnp.stack([1 - core, 2]).astype(jnp.int32)
    all_rows = jnp.array([0, 1], jnp.int32)

    def send_rows(left, rights, steps, extra=None):
        if not by_hand:
            return rows_of(left, rights, all_rows, depth // 4, 4, steps, extra)
        return swap(rows_of(left, rights, send_side, slice_rows, chips, steps, extra))

    def keep_rows(left, rights, received, steps, extra=None):
        if not by_hand:
            return received
        return rows_of(left, rights, keep_side, slice_rows, chips, steps, extra, received)

    def scatter(array):
        axes = "chip" if by_hand else ("chip", "core")
        return lax.psum_scatter(array, axes, scatter_dimension=0, tiled=True)

    acc = None
    dhid_t, dqkv_own, input_grad, gains = {}, {}, {}, {}

    def back(j):
        nonlocal acc
        (dhid_t[j], dqkv_own[j], input_grad[j], gains[j]), acc = backward_chunk(
            level_ref,
            (total[j], final[j]),
            hidden[j],
            dout,
            tokens,
            (norm_gain, mlp_gain),
            (out_pad, qkv_pad),
            qkv,
            (own[j], other[j], across[j], outer[j]),
            (p_out, strip_one),
            (cosines, sines),
            acc,
            j,
            rows,
        )

    part, total, final, hidden, normed_t, activ, dgate, dup, mlp_part, qkv = fence(
        part, total, final, hidden, normed_t, activ, dgate, dup, mlp_part, qkv
    )
    add_3(c1)
    add_2(c2)
    add_1(c3)
    send_gate = send_rows(listed(normed_t), listed(dgate), 4)
    send_up = send_rows(listed(normed_t), listed(dup), 4)
    send_down = send_rows(dout_t, listed(activ), 4)
    back(c0)

    near = lambda: jnp.where(low, mlp_part[1], mlp_part[2])
    edge = lambda: jnp.where(low, mlp_part[0], mlp_part[3])
    total, final, hidden, send_gate, send_up, send_down, mlp_part, acc, dhid_t = fence(
        total, final, hidden, send_gate, send_up, send_down, mlp_part, acc, dhid_t
    )
    add_3(c2)
    add_2(c3)
    leave = jnp.where(low, mlp_part[3], mlp_part[0])
    far_sum = leave + along(leave, INWARD)
    grad_gate = scatter(keep_rows(listed(normed_t), listed(dgate), send_gate, 4))
    grad_up = keep_rows(listed(normed_t), listed(dup), send_up, 4)
    grad_down = keep_rows(dout_t, listed(activ), send_down, 4)
    back(c1)
    total, final, hidden, grad_up, grad_down, mlp_part, far_sum, acc, dhid_t = fence(
        total, final, hidden, grad_up, grad_down, mlp_part, far_sum, acc, dhid_t
    )
    add_3(c3)
    leave = jnp.where(low, mlp_part[2], mlp_part[1])
    near_sum = leave + along(leave, INWARD)
    far_in = along(far_sum, MIDDLE)
    grad_up = scatter(grad_up)
    back(c2)
    total, final, hidden, mlp_part, near_sum, far_in, acc, dhid_t, grad_gate = fence(
        total, final, hidden, mlp_part, near_sum, far_in, acc, dhid_t, grad_gate
    )
    grad_down = scatter(grad_down)
    near_in = along(near_sum, MIDDLE)
    last = along(jnp.where(inner, edge() + far_in, near()), PAIRS)
    back(c3)

    dhid_t, dqkv_own, last, near_in, grad_up = fence(dhid_t, dqkv_own, last, near_in, grad_up)
    gain_sums = gains[0] + gains[1] + gains[2] + gains[3]
    extra = jnp.pad(gain_sums.T, ((0, 0), (0, LANES - 8)))
    out_args = (listed(dhid_t), listed(own))
    qkv_args = (normed_one_t, listed(dqkv_own))
    send_out = send_rows(*out_args, 1, extra)
    send_qkv = send_rows(*qkv_args, 2)
    grad_out = keep_rows(*out_args, send_out, 1, extra)
    grad_qkv = keep_rows(*qkv_args, send_qkv, 2)
    grad_out, grad_qkv, grad_down = fence(grad_out, grad_qkv, grad_down)
    grad_out = scatter(grad_out)
    grad_qkv = scatter(grad_qkv)
    mlp_rows = jnp.where(inner, near() + near_in, edge()) + last
    hidden_rows = jnp.where(
        low,
        jnp.where(level == 0, hidden[0], hidden[1]),
        jnp.where(level == 2, hidden[2], hidden[3]),
    )
    layer_out = (hidden_rows + mlp_rows).astype(jnp.bfloat16)
    one = strip_one.shape[1]
    picked = lambda at, width: jnp.concatenate(
        [grad_qkv[:, kv * one + at : kv * one + at + width] for kv in range(kv_here)], 1
    )
    q_cols = heads_here * HD
    return (
        layer_out,
        jnp.concatenate(listed(input_grad), 0),
        grad_out[:, q_cols],
        picked(0, GROUP * HD),
        picked(GROUP * HD, HD),
        picked((GROUP + 1) * HD, HD),
        grad_out[:, :q_cols].T,
        grad_out[:, q_cols + 1],
        grad_gate,
        grad_up,
        grad_down.T,
    )


def solution(mesh):
    devices = mesh.devices
    dp, tp = devices.shape
    split = Mesh(devices.reshape(dp // 2, 2, tp), ("chip", "core", "tp"))
    data = ("chip", "core")
    return jax.shard_map(
        shards,
        mesh=split,
        in_specs=(
            P(data, None),
            P(data),
            P(data),
            P(data, None),
            P(),
            P(None, "tp"),
            P(None, "tp"),
            P(None, "tp"),
            P("tp", None),
            P(),
            P(None, "tp"),
            P(None, "tp"),
            P("tp", None),
        ),
        out_specs=(
            P(("chip", "core", "tp"), None),
            P(data, None),
            P(data),
            P(data, "tp"),
            P(data, "tp"),
            P(data, "tp"),
            P("tp", data),
            P(data),
            P(data, "tp"),
            P(data, "tp"),
            P("tp", data),
        ),
        check_vma=False,
    )
```

```python
import functools

import jax
import jax.numpy as jnp
from jax import lax
from jax.experimental import pallas as pl
from jax.experimental.pallas import tpu as pltpu
from jax.sharding import Mesh
from jax.sharding import PartitionSpec as P

HD = 96
LANES = 128
GROUP = 2
KV_WIDE = (GROUP + 2) * LANES
rope_base = 100000.0
norm_eps = 1e-05
masked_score = -1e30
far_away = 1e30
score_scale = HD ** (-0.5)
score_scale_log2 = score_scale * 1.4426950408889634
CHUNKS = 4
EXTRA = 8
VMEM_BYTES = 56 * 1024 * 1024
NT = (((1,), (1,)), ((), ()))


def params():
    return pltpu.CompilerParams(vmem_limit_bytes=VMEM_BYTES)


def cost(flops, moved, exps=0):
    return pl.CostEstimate(
        flops=flops // 1024, bytes_accessed=moved // 1024, transcendentals=exps // 1024
    )


def dot32(a, b):
    return jnp.dot(a, b, preferred_element_type=jnp.float32)


def dot32_nt(a, b):
    return lax.dot_general(a, b, NT, preferred_element_type=jnp.float32)


def dot_split(a, places):
    high = a.astype(jnp.bfloat16)
    rest = (a - high.astype(jnp.float32)).astype(jnp.bfloat16)
    return dot32(high, places) + dot32(rest, places)


def fence(*trees):
    return lax.optimization_barrier(trees)


def whole(array, buffers=None):
    zeros = (0,) * len(array.shape)
    return pl.BlockSpec(array.shape, lambda *_: zeros)


SCALAR = pl.BlockSpec(memory_space=pltpu.SMEM)


def halves(entry):
    half_dim = HD // 2
    return (entry // half_dim) * (LANES // 2) + entry % half_dim


def placement(lanes, width):
    return (lanes[:, None] == jnp.arange(width)[None, :]).astype(jnp.bfloat16)


def place_query(heads):
    source = jnp.arange(heads * HD)
    return placement((source // HD) * LANES + halves(source % HD), heads * LANES)


def place_key_value(kv_heads):
    source = jnp.arange(kv_heads * HD)
    head = source // HD
    keys = head * 2 * LANES + halves(source % HD)
    values = head * 2 * LANES + LANES + source % HD
    return placement(jnp.concatenate([keys, values]), kv_heads * 2 * LANES)


def place_all(heads, kv_heads):
    source = jnp.arange(heads * HD)
    head = source // HD
    query = (head // GROUP) * KV_WIDE + (head % GROUP) * LANES + halves(source % HD)
    source = jnp.arange(kv_heads * HD)
    base = (source // HD) * KV_WIDE + GROUP * LANES
    keys = base + halves(source % HD)
    values = base + LANES + source % HD
    return placement(jnp.concatenate([query, keys, values]), kv_heads * KV_WIDE)


def place_plain(heads):
    source = jnp.arange(heads * HD)
    return placement((source // HD) * LANES + source % HD, heads * LANES)


PAIRS = [(0, 1), (1, 0), (2, 3), (3, 2)]
INWARD = [(0, 1), (3, 2)]
MIDDLE = [(1, 2), (2, 1)]
OUTWARD = [(1, 0), (2, 3)]


def along(part, pairs):
    return lax.ppermute(part, "tp", pairs)


def store_qkv(out_ref, here, base, query, key_value):
    wide = GROUP * LANES
    for kv in range(key_value.shape[1] // (2 * LANES)):
        at = base + kv * KV_WIDE
        there = slice(kv * 2 * LANES, (kv + 1) * 2 * LANES)
        out_ref[here, at : at + wide] = query[:, kv * wide : (kv + 1) * wide]
        out_ref[here, at + wide : at + KV_WIDE] = key_value[:, there]


def store_turned(out_ref, at, lin, cos_ref, sin_ref):
    for h in range(GROUP + 2):
        one = lin[:, h * LANES : (h + 1) * LANES]
        if h < GROUP + 1:
            one = one * cos_ref[...] + pltpu.roll(one, LANES // 2, 1) * sin_ref[...]
        out_ref[:, at + h * LANES : at + (h + 1) * LANES] = one.astype(jnp.bfloat16)


def spread_out_kernel(meta_ref, own_ref, p_ref, mine_ref, theirs_ref, pad_ref, plain_ref):
    rows, width = mine_ref.shape[2:]
    wide = p_ref.shape[1]
    for side, ref in enumerate((mine_ref, theirs_ref)):
        here = pl.ds(pl.multiple_of((meta_ref[1] ^ side) * rows, rows), rows)
        for s in range(4):
            block = own_ref[here, :] if s == 0 else ref[0, s - 1].astype(jnp.bfloat16)
            plain_ref[here, s * width : (s + 1) * width] = block
            pad_ref[here, s * wide : (s + 1) * wide] = dot32(block, p_ref[...]).astype(
                jnp.bfloat16
            )


def spread_qkv_kernel(meta_ref, own_ref, pq_ref, pkv_ref, mine_ref, theirs_ref, out_ref):
    rows = mine_ref.shape[2]
    wide = own_ref.shape[1]
    split = pq_ref.shape[0]
    out_ref[:, :wide] = own_ref[...]
    for side, ref in enumerate((mine_ref, theirs_ref)):
        here = pl.ds(pl.multiple_of((meta_ref[1] ^ side) * rows, rows), rows)
        for s in range(1, 4):
            block = ref[0, s - 1].astype(jnp.bfloat16)
            query = dot32(block[:, :split], pq_ref[...]).astype(jnp.bfloat16)
            key_value = dot32(block[:, split:], pkv_ref[...]).astype(jnp.bfloat16)
            store_qkv(out_ref, here, s * wide, query, key_value)


def spread(kernel, meta, own, places, mine, theirs, widths):
    chips, others, rows, width = mine.shape
    total = own.shape[0]
    row_block = lambda m, meta: (meta[0] ^ m, 0)
    piece = pl.BlockSpec((1, others, rows, width), lambda m, meta: (m, 0, 0, 0))
    return pl.pallas_call(
        kernel,
        out_shape=[jax.ShapeDtypeStruct((total, wide), jnp.bfloat16) for wide in widths],
        grid_spec=pltpu.PrefetchScalarGridSpec(
            num_scalar_prefetch=1,
            grid=(chips,),
            in_specs=[pl.BlockSpec((2 * rows, own.shape[1]), row_block)]
            + [whole(place) for place in places]
            + [piece, piece],
            out_specs=[pl.BlockSpec((2 * rows, wide), row_block) for wide in widths],
        ),
        compiler_params=params(),
        cost_estimate=cost(
            8 * total * width * 512, total * (12 * width + 2 * sum(widths))
        ),
    )(meta, own, *places, mine, theirs)


def start_kernel(x_ref, gain_ref, q_ref, k_ref, v_ref, pq_ref, pkv_ref, cos_ref, sin_ref, *outs):
    qkv_ref, normed_ref, pad_ref = outs

    @pl.when(pl.program_id(0) == 0)
    def _():
        split = k_ref.shape[0]
        query = dot32(q_ref[...], pq_ref[...]).astype(jnp.bfloat16)
        key_value = dot32(k_ref[...].T, pkv_ref[:split, :])
        key_value = key_value + dot32(v_ref[...].T, pkv_ref[split:, :])
        store_qkv(pad_ref, slice(None), 0, query, key_value.astype(jnp.bfloat16))

    inputs = x_ref[...].astype(jnp.float32)
    rms = lax.rsqrt(jnp.mean(inputs * inputs, -1, keepdims=True) + norm_eps)
    normed = (inputs * rms * gain_ref[...]).astype(jnp.bfloat16)
    normed_ref[...] = normed
    for kv in range(pad_ref.shape[1] // KV_WIDE):
        at = kv * KV_WIDE
        store_turned(qkv_ref, at, dot32(normed, pad_ref[:, at : at + KV_WIDE]), cos_ref, sin_ref)


def start(tokens, gain, w_query, w_key_t, w_value_t, pq, pkv, cosines, sines):
    total, depth = tokens.shape
    rows = total // CHUNKS
    wide = pq.shape[1] + pkv.shape[1]
    gain = gain[None, :]
    by_rows = lambda width: pl.BlockSpec((rows, width), lambda i: (i, 0))
    arrays = [w_query, w_key_t, w_value_t, pq, pkv]
    shapes = [
        jax.ShapeDtypeStruct((total, wide), jnp.bfloat16),
        jax.ShapeDtypeStruct((total, depth), jnp.bfloat16),
        jax.ShapeDtypeStruct((depth, wide), jnp.bfloat16),
    ]
    return pl.pallas_call(
        start_kernel,
        out_shape=shapes,
        grid=(CHUNKS,),
        in_specs=[by_rows(depth), whole(gain)]
        + [whole(array) for array in arrays]
        + [by_rows(LANES), by_rows(LANES)],
        out_specs=[by_rows(wide), by_rows(depth), whole(shapes[2])],
        compiler_params=params(),
        cost_estimate=cost(2 * total * depth * wide, 12 * total * depth),
    )(tokens, gain, *arrays, cosines, sines)


def turn_kernel(length_ref, cot_ref, normed_ref, dout_ref, dout_t_ref, normed_t_ref):
    rows = cot_ref.shape[0]
    at = pl.program_id(0) * rows + lax.broadcasted_iota(jnp.int32, cot_ref.shape, 0)
    dout = jnp.where(at < length_ref[0], cot_ref[...].astype(jnp.float32), 0.0)
    dout = dout.astype(jnp.bfloat16)
    dout_ref[...] = dout
    dout_t_ref[...] = dout.T
    normed_t_ref[...] = normed_ref[...].T


def turn(length, cotangent, normed):
    total, depth = cotangent.shape
    rows = total // CHUNKS
    by_rows = pl.BlockSpec((rows, depth), lambda i: (i, 0))
    by_columns = pl.BlockSpec((depth, rows), lambda i: (0, i))
    turned = jax.ShapeDtypeStruct((depth, total), jnp.bfloat16)
    return pl.pallas_call(
        turn_kernel,
        out_shape=[jax.ShapeDtypeStruct((total, depth), jnp.bfloat16), turned, turned],
        grid=(CHUNKS,),
        in_specs=[SCALAR, by_rows, by_rows],
        out_specs=[by_rows, by_columns, by_columns],
        compiler_params=params(),
        cost_estimate=cost(total * depth, 10 * total * depth),
    )(length, cotangent, normed)


def project_kernel(x_ref, w_ref, cos_ref, sin_ref, out_ref):
    store_turned(out_ref, 0, dot32(x_ref[...], w_ref[...]), cos_ref, sin_ref)


def project(normed, weights, cosines, sines):
    rows, depth = normed.shape
    width = weights.shape[1]
    return pl.pallas_call(
        project_kernel,
        out_shape=jax.ShapeDtypeStruct((rows, width), jnp.bfloat16),
        grid=(width // KV_WIDE,),
        in_specs=[
            whole(normed),
            pl.BlockSpec((depth, KV_WIDE), lambda i: (0, i)),
            whole(cosines),
            whole(sines),
        ],
        out_specs=pl.BlockSpec((rows, KV_WIDE), lambda i: (0, i)),
        compiler_params=params(),
        cost_estimate=cost(
            2 * rows * depth * width, 2 * (rows * depth + depth * width + rows * width)
        ),
    )(normed, weights, cosines, sines)


def attend_kernel(start, length_ref, q_ref, kv_ref, strip_ref, out_ref):
    rows = q_ref.shape[0]
    keys = kv_ref.shape[0]
    length = length_ref[0]
    row_ids = start + lax.broadcasted_iota(jnp.int32, (1, rows), 1)
    limit = jnp.minimum(row_ids, length - 1)
    allowed = lax.broadcasted_iota(jnp.int32, (keys, rows), 0) <= limit
    mixed = []
    sums = []
    for kv in range(kv_ref.shape[1] // KV_WIDE):
        base = kv * KV_WIDE
        at = base + GROUP * LANES
        key = kv_ref[:, at : at + LANES]
        value_t = kv_ref[:, at + LANES : at + 2 * LANES].T
        for g in range(GROUP):
            query = q_ref[:, base + g * LANES : base + (g + 1) * LANES]
            raw = jnp.where(allowed, dot32_nt(key, query), masked_score)
            peak = jnp.max(raw, axis=0, keepdims=True)
            expo = jnp.exp2((raw - peak) * score_scale_log2)
            total = jnp.sum(expo, axis=0, keepdims=True)
            probs = (expo * (1.0 / total)).astype(jnp.bfloat16)
            mixed.append(dot32(value_t, probs).T)
            log_sum = peak * score_scale_log2 + jnp.log2(total)
            sums.append(jnp.where(row_ids < length, log_sum, far_away))
    out_ref[:rows, :] = dot_split(jnp.concatenate(mixed, 1), strip_ref[...])
    out_ref[rows:, :] = jnp.zeros((EXTRA, out_ref.shape[1]), jnp.float32)
    out_ref[rows : rows + len(sums), :rows] = jnp.concatenate(sums, 0)


def attend(length, qkv, strip, index, rows):
    keys = (index + 1) * rows
    width = qkv.shape[1]
    heads = width // KV_WIDE * GROUP
    shape = (rows + EXTRA, strip.shape[1])
    return pl.pallas_call(
        functools.partial(attend_kernel, index * rows),
        out_shape=jax.ShapeDtypeStruct(shape, jnp.float32),
        grid=(1,),
        in_specs=[
            SCALAR,
            pl.BlockSpec((rows, width), lambda i: (index, 0)),
            pl.BlockSpec((keys, width), lambda i: (0, 0)),
            whole(strip),
        ],
        out_specs=pl.BlockSpec(shape, lambda i: (0, 0)),
        compiler_params=params(),
        cost_estimate=cost(
            4 * heads * rows * keys * LANES, 2 * (rows + keys) * width, heads * rows * keys
        ),
    )(length, qkv, qkv, strip)


def forward_kernel(level_ref, part_ref, other_ref, across_ref, outer_ref, *refs):
    x_ref, dout_ref, wo_ref, gain_ref, wg_ref, wu_ref, wd_ref = refs[:7]
    hidden_ref, normed_t_ref, activ_ref, dgate_ref, dup_ref, mlp_ref, dn_ref = refs[7:14]
    normed_ref = refs[14]
    rows = x_ref.shape[0]

    @pl.when(pl.program_id(0) == 0)
    def _():
        level = level_ref[0]
        inner = (level == 1) | (level == 2)
        width = part_ref.shape[1]
        second = jnp.where(inner, across_ref[:rows, width:], outer_ref[:rows, :width])
        third = jnp.where(inner, across_ref[:rows, :width], outer_ref[:rows, width:])
        mixed = jnp.concatenate([part_ref[:rows, :], other_ref[:rows, :], second, third], 1)
        hidden = x_ref[...].astype(jnp.float32) + dot32_nt(mixed.astype(jnp.bfloat16), wo_ref[...])
        hidden_ref[...] = hidden
        rms = lax.rsqrt(jnp.mean(hidden * hidden, -1, keepdims=True) + norm_eps)
        normed = (hidden * rms * gain_ref[...]).astype(jnp.bfloat16)
        normed_ref[...] = normed
        normed_t_ref[...] = normed.T
        mlp_ref[...] = jnp.zeros_like(mlp_ref)
        dn_ref[...] = jnp.zeros_like(dn_ref)

    normed = normed_ref[...]
    gate = dot32(normed, wg_ref[...])
    up = dot32(normed, wu_ref[...])
    dact = dot32_nt(dout_ref[...], wd_ref[...])
    sigmoid = jax.nn.sigmoid(gate)
    silu = gate * sigmoid
    activ = (silu * up).astype(jnp.bfloat16)
    dgate = (dact * up * sigmoid * (1.0 + gate * (1.0 - sigmoid))).astype(jnp.bfloat16)
    dup = (dact * silu).astype(jnp.bfloat16)
    activ_ref[...] = activ
    dgate_ref[...] = dgate
    dup_ref[...] = dup
    mlp_ref[...] += dot32(activ, wd_ref[...])
    dn_ref[...] += dot32_nt(dgate, wg_ref[...]) + dot32_nt(dup, wu_ref[...])


def forward_chunk(level, gathered, tokens, dout, w_out, gain, w_gate, w_up, w_down, index, rows):
    depth = tokens.shape[1]
    units = w_gate.shape[1]
    block = 512
    own_rows = pl.BlockSpec((rows, depth), lambda i: (index, 0))
    by_units = pl.BlockSpec((depth, block), lambda i: (0, i))
    gain = gain[None, :]
    f32, bf16 = jnp.float32, jnp.bfloat16
    outs = [
        jax.ShapeDtypeStruct((rows, depth), f32),
        jax.ShapeDtypeStruct((depth, rows), bf16),
        jax.ShapeDtypeStruct((rows, units), bf16),
        jax.ShapeDtypeStruct((rows, units), bf16),
        jax.ShapeDtypeStruct((rows, units), bf16),
        jax.ShapeDtypeStruct((rows, depth), f32),
        jax.ShapeDtypeStruct((rows, depth), f32),
    ]
    unit_out = pl.BlockSpec((rows, block), lambda i: (0, i))
    return pl.pallas_call(
        forward_kernel,
        out_shape=outs,
        grid=(units // block,),
        in_specs=[SCALAR]
        + [whole(array) for array in gathered]
        + [own_rows, own_rows, whole(w_out), whole(gain), by_units, by_units]
        + [pl.BlockSpec((block, depth), lambda i: (i, 0))],
        out_specs=[
            whole(outs[0]),
            whole(outs[1]),
            unit_out,
            unit_out,
            unit_out,
            whole(outs[5]),
            whole(outs[6]),
        ],
        scratch_shapes=[pltpu.VMEM((rows, depth), bf16)],
        compiler_params=params(),
        cost_estimate=cost(
            2 * rows * depth * (6 * units + w_out.shape[1]),
            2 * depth * (3 * units + w_out.shape[1]) + 22 * rows * depth,
            rows * units,
        ),
    )(level, *gathered, tokens, dout, w_out, gain, w_gate, w_up, w_down)


def backward_kernel(start, level_ref, total_ref, final_ref, hidden_ref, dout_ref, x_ref, *refs):
    gain_one_ref, gain_two_ref, wo_ref, w_ref, q_ref = refs[:5]
    kv_here = q_ref.shape[1] // KV_WIDE
    refs = refs[5:]
    kv_refs, refs = refs[: 2 * kv_here], refs[2 * kv_here :]
    part_ref, other_ref, across_ref, outer_ref, place_ref, strip_ref = refs[:6]
    cos_ref, sin_ref = refs[6:8]
    dhid_ref, low_ref, dn_ref = refs[-3:]
    outs = refs[8:-3]
    count = 5 if start > 0 else 4
    acc_ref = outs[0] if len(outs) > count else None
    outs = outs[-count:]
    dhid_t_ref, dqkv_ref, input_grad_ref, gains_ref = outs[:4]
    rows = q_ref.shape[0]
    keys = kv_refs[0].shape[0]
    shard = pl.program_id(0)
    level = level_ref[0]
    inner = (level == 1) | (level == 2)

    @pl.when(shard == 0)
    def _():
        dnormed = jnp.where(inner, total_ref[...], final_ref[...])
        hidden = hidden_ref[...]
        rms = lax.rsqrt(jnp.mean(hidden * hidden, -1, keepdims=True) + norm_eps)
        scaled = dnormed * gain_two_ref[...]
        shift = jnp.mean(scaled * hidden, -1, keepdims=True)
        dhid = dout_ref[...].astype(jnp.float32) + (rms * scaled - hidden * (rms**3 * shift))
        dhid_ref[...] = dhid
        low = dhid.astype(jnp.bfloat16)
        low_ref[...] = low
        dhid_t_ref[...] = low.T
        gains_ref[...] = jnp.zeros_like(gains_ref)
        gains_ref[1:2, :] = jnp.sum(dnormed * (hidden * rms), 0, keepdims=True)
        dn_ref[...] = jnp.zeros_like(dn_ref)

    def rotate_back(grads):
        turned = grads * cos_ref[...] - pltpu.roll(grads, LANES // 2, 1) * sin_ref[...]
        return turned.astype(jnp.bfloat16)

    dmixed_all = dot32(low_ref[...], wo_ref[...]).astype(jnp.bfloat16)
    mixed = jnp.where(
        shard == 0,
        part_ref[...],
        jnp.where(shard == 1, other_ref[...], jnp.where(inner, across_ref[...], outer_ref[...])),
    )
    products = dmixed_all.astype(jnp.float32) * dot_split(mixed[:rows], place_ref[...])
    causal = lax.broadcasted_iota(jnp.int32, (rows, rows), 0) <= lax.broadcasted_iota(
        jnp.int32, (rows, rows), 1
    )
    grads = []
    for kv in range(kv_here):
        key_ref, value_ref = kv_refs[2 * kv : 2 * kv + 2]
        heads = range(kv * GROUP, (kv + 1) * GROUP)
        lanes = {h: slice(h * LANES, (h + 1) * LANES) for h in heads}
        row_dots = {h: jnp.sum(products[:, lanes[h]].T, axis=0, keepdims=True) for h in heads}
        log_sums = {h: mixed[rows + h : rows + h + 1, :rows] for h in heads}
        dqueries = dict.fromkeys(heads)
        here = slice(2 * kv * LANES, (2 * kv + 1) * LANES)
        there = slice((2 * kv + 1) * LANES, (2 * kv + 2) * LANES)
        for tile in range(keys // rows):
            span = slice(tile * rows, (tile + 1) * rows)
            key = key_ref[span, :]
            value = value_ref[span, :]
            key_t = key.T
            dkey = None if acc_ref is None else acc_ref[span, here]
            dvalue = None if acc_ref is None else acc_ref[span, there]
            last = tile * rows == start
            for h in heads:
                at = kv * KV_WIDE + (h % GROUP) * LANES
                query = q_ref[:, at : at + LANES]
                dmixed = dmixed_all[:, lanes[h]]
                raw = dot32_nt(key, query)
                probs = jnp.exp2(raw * score_scale_log2 - log_sums[h])
                if last:
                    probs = jnp.where(causal, probs, 0.0)
                dprobs = dot32_nt(value, dmixed)
                dscores = (probs * (dprobs - row_dots[h])).astype(jnp.bfloat16)
                dquery = dot32(key_t, dscores)
                dqueries[h] = dquery if dqueries[h] is None else dqueries[h] + dquery
                dkey_one = dot32(dscores, query)
                dvalue_one = dot32(probs.astype(jnp.bfloat16), dmixed)
                dkey = dkey_one if dkey is None else dkey + dkey_one
                dvalue = dvalue_one if dvalue is None else dvalue + dvalue_one
            if not last:
                outs[4][span, here] = dkey
                outs[4][span, there] = dvalue
        grads += [rotate_back(dqueries[h].T * score_scale) for h in heads]
        grads.append(rotate_back(dkey * score_scale))
        grads.append(dvalue.astype(jnp.bfloat16))
    grads = jnp.concatenate(grads, 1)
    dn_ref[...] += dot32_nt(grads, w_ref[...])

    @pl.when(shard == 0)
    def _():
        wide = strip_ref.shape[1]
        for kv in range(kv_here):
            dqkv_ref[:, kv * wide : (kv + 1) * wide] = dot32(
                grads[:, kv * KV_WIDE : (kv + 1) * KV_WIDE], strip_ref[...]
            ).astype(jnp.bfloat16)

    @pl.when(shard == pl.num_programs(0) - 1)
    def _():
        dnormed = dn_ref[...]
        inputs = x_ref[...].astype(jnp.float32)
        rms = lax.rsqrt(jnp.mean(inputs * inputs, -1, keepdims=True) + norm_eps)
        scaled = dnormed * gain_one_ref[...]
        shift = jnp.mean(scaled * inputs, -1, keepdims=True)
        grad = dhid_ref[...] + (rms * scaled - inputs * (rms**3 * shift))
        input_grad_ref[...] = grad.astype(jnp.bfloat16)
        gains_ref[0:1, :] = jnp.sum(dnormed * (inputs * rms), 0, keepdims=True)


def backward_chunk(
    level, sums_two, hidden, dout, tokens, gains, weights, qkv, gathered, places, tables, acc,
    index, rows
):
    start = index * rows
    keys = start + rows
    depth = tokens.shape[1]
    out_pad, qkv_pad = weights
    place_out, strip = places
    far_rows, width = gathered[0].shape
    out_wide = place_out.shape[1]
    kv_here = out_wide // (GROUP * LANES)
    wide = kv_here * KV_WIDE
    levels = qkv.shape[1] // wide
    own_rows = pl.BlockSpec((rows, depth), lambda t: (index, 0))
    table = pl.BlockSpec((rows, LANES), lambda t: (index, 0))
    gains = [gain[None, :] for gain in gains]
    key_value = lambda at: pl.BlockSpec(
        (keys, LANES), lambda t: (0, (wide // LANES) * t + at)
    )
    across = pl.BlockSpec((far_rows, width), lambda t: (0, jnp.where(t == 2, 1, 0)))
    outer = pl.BlockSpec((far_rows, width), lambda t: (0, jnp.where(t == 3, 1, 0)))
    in_specs = [
        SCALAR,
        whole(sums_two[0]),
        whole(sums_two[1]),
        whole(hidden),
        own_rows,
        own_rows,
        whole(gains[0]),
        whole(gains[1]),
        pl.BlockSpec((depth, out_wide), lambda t: (0, t)),
        pl.BlockSpec((depth, wide), lambda t: (0, t)),
        pl.BlockSpec((rows, wide), lambda t: (index, t)),
    ]
    for kv in range(kv_here):
        at = kv * (KV_WIDE // LANES) + GROUP
        in_specs += [key_value(at), key_value(at + 1)]
    in_specs += [
        whole(gathered[0]),
        whole(gathered[1]),
        across,
        outer,
        whole(place_out),
        whole(strip),
        table,
        table,
    ]
    args = [level, *sums_two, hidden, dout, tokens, *gains, out_pad, qkv_pad]
    args += [qkv] * (1 + 2 * kv_here)
    args += [*gathered, place_out, strip, *tables]
    sums_wide = 2 * kv_here * LANES
    if acc is not None:
        in_specs.append(pl.BlockSpec((keys, sums_wide), lambda t: (0, t)))
        args.append(acc)
    f32, bf16 = jnp.float32, jnp.bfloat16
    outs = [
        jax.ShapeDtypeStruct((depth, rows), bf16),
        jax.ShapeDtypeStruct((rows, kv_here * strip.shape[1]), bf16),
        jax.ShapeDtypeStruct((rows, depth), bf16),
        jax.ShapeDtypeStruct((8, depth), f32),
    ]
    out_specs = [whole(out) for out in outs]
    if start > 0:
        outs.append(jax.ShapeDtypeStruct((start, levels * sums_wide), f32))
        out_specs.append(pl.BlockSpec((start, sums_wide), lambda t: (0, t)))
    results = pl.pallas_call(
        functools.partial(backward_kernel, start),
        out_shape=outs,
        grid=(levels,),
        in_specs=in_specs,
        out_specs=out_specs,
        scratch_shapes=[
            pltpu.VMEM((rows, depth), f32),
            pltpu.VMEM((rows, depth), bf16),
            pltpu.VMEM((rows, depth), f32),
        ],
        compiler_params=params(),
        cost_estimate=cost(
            levels * rows * (20 * kv_here * keys * LANES + 2 * depth * (out_wide + wide)),
            2 * depth * levels * (out_wide + wide) + 16 * rows * depth,
            levels * kv_here * GROUP * rows * keys,
        ),
    )(*args)
    return results[:4], (results[4] if start > 0 else None)


def rows_kernel(lefts, groups, extras, adding, side_ref, *refs):
    refs = list(refs)
    held_ref = refs.pop()
    out_ref = refs.pop()
    recv_ref = refs.pop() if adding else None
    step = pl.program_id(0)
    left_refs = []
    for count in lefts:
        left_refs.append(refs[:count])
        refs = refs[count:]
    rights = []
    for _ in groups:
        rights.append(refs[:CHUNKS])
        refs = refs[CHUNKS:]
    rows = left_refs[0][0].shape[0]
    blocks = held_ref.shape[1] // rows

    @pl.when(step == 0)
    def _():
        for which, pieces in enumerate(left_refs):
            for n, ref in enumerate(pieces):
                m, j = n % blocks, n // blocks
                wide = ref.shape[1]
                held_ref[which, m * rows : (m + 1) * rows, j * wide : (j + 1) * wide] = ref[...]

    chunk = held_ref.shape[2] // CHUNKS
    right = None
    which = 0
    for group, (left, first, _) in zip(rights, groups):
        one = jnp.concatenate([ref[:chunk, :].astype(jnp.bfloat16) for ref in group], 0)
        right = one if right is None else jnp.where(step >= first, one, right)
        which = jnp.where(step >= first, left, which)
    total = dot32(held_ref[which], right)
    width = total.shape[1]
    out_ref[:, :width] = total if recv_ref is None else total + recv_ref[:, :width]
    for m in range(extras):
        here = slice(m * rows, (m + 1) * rows)
        more = refs[m][...]
        out_ref[here, width:] = more if recv_ref is None else more + recv_ref[here, width:]


def rows_of(lefts, groups, side, rows, blocks, step, extra=None, recv=None):
    at = lambda m: lambda i, side: (m * side[1] + side[0], 0)
    specs = []
    args = []
    counts = []
    for left in lefts:
        pieces = left if isinstance(left, list) else [left]
        counts.append(len(pieces) * blocks)
        for piece in pieces:
            for m in range(blocks):
                specs.append(pl.BlockSpec((rows, piece.shape[1]), at(m)))
                args.append(piece)
    tokens = sum(piece.shape[1] for piece in pieces)
    first = 0
    plan = []
    for which, rights in groups:
        steps = rights[0].shape[1] // step
        plan.append((which, first, steps))
        for right in rights:
            pick = lambda i, side, first=first, steps=steps: (0, jnp.clip(i - first, 0, steps - 1))
            specs.append(pl.BlockSpec((right.shape[0], step), pick))
            args.append(right)
        first += steps
    total = first * step
    if extra is not None:
        for m in range(blocks):
            specs.append(pl.BlockSpec((rows, extra.shape[1]), at(m)))
            args.append(extra)
        total += extra.shape[1]
        step += extra.shape[1]
    block = pl.BlockSpec((rows * blocks, step), lambda i, side: (0, i))
    if recv is not None:
        specs.append(block)
        args.append(recv)
    return pl.pallas_call(
        functools.partial(
            rows_kernel, counts, plan, 0 if extra is None else blocks, recv is not None
        ),
        out_shape=jax.ShapeDtypeStruct((rows * blocks, total), jnp.float32),
        grid_spec=pltpu.PrefetchScalarGridSpec(
            num_scalar_prefetch=1,
            grid=(first,),
            in_specs=specs,
            out_specs=block,
            scratch_shapes=[pltpu.VMEM((len(lefts), rows * blocks, tokens), jnp.bfloat16)],
        ),
        compiler_params=params(),
        cost_estimate=cost(
            2 * rows * blocks * tokens * total,
            4 * rows * blocks * total + 2 * tokens * (total + rows * blocks),
        ),
    )(side, *args)


def shards(
    tokens,
    lengths,
    positions,
    cotangent,
    norm_gain,
    w_query,
    w_key,
    w_value,
    w_out,
    mlp_gain,
    w_gate,
    w_up,
    w_down,
):
    seq_rows, depth = tokens.shape
    chips = lax.axis_size("chip")
    dp = chips * 2
    tp = lax.axis_size("tp")
    chip = lax.axis_index("chip")
    core = lax.axis_index("core")
    level = lax.axis_index("tp")
    low = level < 2
    inner = (level == 1) | (level == 2)
    heads_here = w_query.shape[1] // HD
    kv_here = w_key.shape[1] // HD
    rows = seq_rows // CHUNKS
    slice_rows = depth // dp
    level_ref = level.astype(jnp.int32).reshape(1)
    by_hand = dp == 8
    swap = lambda array: lax.ppermute(array, "core", [(0, 1), (1, 0)])
    to_level = lambda array, s: along(array, [(t, t ^ s) for t in range(tp)])

    at_row = (chip * 2 + core) * slice_rows
    cols = lambda w: lax.dynamic_slice_in_dim(w, at_row, slice_rows, 1).astype(jnp.float32).T
    (out_slice,) = fence(cols(w_out))
    qkv_slice = jnp.concatenate(
        [
            lax.dynamic_slice_in_dim(w_query, at_row, slice_rows, 0).astype(jnp.float32),
            cols(w_key.T),
            cols(w_value.T),
        ],
        1,
    )
    out_slice, qkv_slice = fence(out_slice, qkv_slice)
    if by_hand:
        out_far = [to_level(out_slice, s) for s in (1, 2, 3)]
        qkv_near = along(qkv_slice, PAIRS)
    meta = jnp.stack([chip, core]).astype(jnp.int32)

    pq = place_query(heads_here)
    pkv = place_key_value(kv_here)
    p_all = place_all(heads_here, kv_here)
    strip_one = place_all(GROUP, 1).T
    p_out = place_plain(heads_here)
    strip_out = p_out.T

    half_dim = HD // 2
    freqs = rope_base ** (-(jnp.arange(half_dim).astype(jnp.float32) * 2.0 / HD))
    freqs = jnp.pad(freqs, (0, LANES // 2 - half_dim))
    angles = positions.astype(jnp.float32)[:, None] * jnp.concatenate([freqs, freqs])[None, :]
    cosines = jnp.cos(angles)
    sines = jnp.sin(angles) * jnp.where(jnp.arange(LANES) < LANES // 2, -1.0, 1.0)

    qkv_own, normed_one, own_pad = start(
        tokens, norm_gain, w_query, w_key.T, w_value.T, pq, pkv, cosines, sines
    )

    order = list(reversed(range(CHUNKS)))
    c0, c1, c2, c3 = order
    own, other, pair, across, outer = {}, {}, {}, {}, {}
    part, total, final = {}, {}, {}

    def hop_1(j):
        other[j] = along(own[j], PAIRS)
        pair[j] = jnp.concatenate([own[j], other[j]], 1)

    def hop_2(j):
        across[j] = along(pair[j], MIDDLE)

    def hop_3(j):
        outer[j] = along(across[j], OUTWARD)

    def add_1(j):
        total[j] = part[j] + along(part[j], INWARD)

    def add_2(j):
        total[j] = total[j] + along(total[j], MIDDLE)

    def add_3(j):
        final[j] = along(total[j], OUTWARD)

    def to_chip(array, m):
        return lax.ppermute(array, "chip", [(i, i ^ m) for i in range(chips)])

    def over_chips_1(piece):
        cut = piece.shape[1] // 2
        one, two = piece[:, :cut], piece[:, cut:]
        return jnp.stack([one, to_chip(one, 1)]), jnp.stack([two, to_chip(two, 2)])

    def over_chips_2(one, two):
        return one, to_chip(one, 2), two, to_chip(two, 1)

    def over_chips_3(one, one_far, two, two_far):
        upper = jnp.stack([one[0], one[1], one_far[0], one_far[1]])
        lower = jnp.stack([two[0], two_far[0], two[1], two_far[1]])
        return jnp.concatenate([upper, lower], 2)

    if by_hand:
        qkv_own, qkv_near, out_far = fence(qkv_own, qkv_near, out_far)
        out_mine = over_chips_1(jnp.stack(out_far))
        qkv_across = along(jnp.stack([qkv_slice, qkv_near]), MIDDLE)
    else:
        gathered_out = lax.all_gather(out_slice, ("chip", "core", "tp"))
        gathered_qkv = lax.all_gather(qkv_slice, ("chip", "core", "tp"))
    own[c0] = attend(lengths, qkv_own, strip_out, c0, rows)
    if by_hand:
        own, qkv_own, out_mine = fence(own, qkv_own, out_mine)
        out_mine = over_chips_2(*out_mine)
    else:
        own, qkv_own = fence(own, qkv_own)
    hop_1(c0)
    for j in (c1, c2, c3):
        own[j] = attend(lengths, qkv_own, strip_out, j, rows)
    if by_hand:
        own, other, pair, qkv_across = fence(own, other, pair, qkv_across)
        qkv_outer = along(qkv_across, OUTWARD)
    own, other, pair, normed_one, w_out = fence(own, other, pair, normed_one, w_out)
    hop_2(c0)
    hop_1(c1)
    dout, dout_t, normed_one_t = turn(lengths, cotangent, normed_one)
    w_out_t = w_out.T
    own, other, pair, across, dout, dout_t, normed_one_t, w_out_t = fence(
        own, other, pair, across, dout, dout_t, normed_one_t, w_out_t
    )
    if by_hand:
        out_mine, across = fence(out_mine, across)
        out_mine = over_chips_3(*out_mine)
        out_theirs = swap(out_mine)
    hop_3(c0)
    hop_2(c1)
    hop_1(c2)
    own, other, pair, across, outer = fence(own, other, pair, across, outer)
    if by_hand:
        out_mine, out_theirs, qkv_outer, qkv_near, qkv_across, outer = fence(
            out_mine, out_theirs, qkv_outer, qkv_near, qkv_across, outer
        )
        qkv_far = [
            qkv_near,
            jnp.where(inner, qkv_across[1], qkv_outer[0]),
            jnp.where(inner, qkv_across[0], qkv_outer[1]),
        ]
        qkv_mine = over_chips_1(jnp.stack(qkv_far))
    hop_3(c1)
    hop_2(c2)
    hop_1(c3)
    if by_hand:
        out_pad, out_plain = spread(
            spread_out_kernel,
            meta,
            w_out_t,
            [p_out],
            out_mine,
            out_theirs,
            [4 * p_out.shape[1], 4 * p_out.shape[0]],
        )
    else:
        by_shard = lambda g, s: lax.dynamic_index_in_dim(
            g.reshape(dp, tp, slice_rows, -1), level ^ s, 1, False
        ).reshape(depth, -1)
        plain = [fence(by_shard(gathered_out, s))[0].astype(jnp.bfloat16) for s in range(4)]
        out_plain = jnp.concatenate(plain, 1)
        out_pad = jnp.concatenate([dot32(w, p_out).astype(jnp.bfloat16) for w in plain], 1)

    hidden, normed_t, activ, dgate, dup, mlp_part = {}, {}, {}, {}, {}, {}

    def feed(j):
        gathered = (own[j], other[j], across[j], outer[j])
        (hidden[j], normed_t[j], activ[j], dgate[j], dup[j], mlp_part[j], part[j]) = forward_chunk(
            level_ref, gathered, tokens, dout, out_plain, mlp_gain, w_gate, w_up, w_down, j, rows
        )

    feed(c0)
    own, other, pair, across, outer, part, hidden = fence(
        own, other, pair, across, outer, part, hidden
    )
    add_1(c0)
    hop_3(c2)
    hop_2(c3)
    if by_hand:
        qkv_mine, part = fence(qkv_mine, part)
        qkv_mine = over_chips_2(*qkv_mine)
    feed(c1)
    own, other, across, outer, part, total, hidden = fence(
        own, other, across, outer, part, total, hidden
    )
    add_2(c0)
    add_1(c1)
    hop_3(c3)
    feed(c2)
    if by_hand:
        qkv_mine, _ = fence(qkv_mine, hidden[c1])
        qkv_mine = over_chips_3(*qkv_mine)
        qkv_theirs = swap(qkv_mine)
    own, other, across, outer, part, total, hidden = fence(
        own, other, across, outer, part, total, hidden
    )
    add_3(c0)
    add_2(c1)
    add_1(c2)
    feed(c3)
    if by_hand:
        qkv_mine, qkv_theirs, _ = fence(qkv_mine, qkv_theirs, part[c3])
        (qkv_pad,) = spread(
            spread_qkv_kernel,
            meta,
            own_pad,
            [pq, pkv],
            qkv_mine,
            qkv_theirs,
            [4 * own_pad.shape[1]],
        )
    else:
        plain = [
            fence(by_shard(gathered_qkv, s))[0].astype(jnp.bfloat16) for s in range(4)
        ]
        qkv_pad = jnp.concatenate([dot32(w, p_all).astype(jnp.bfloat16) for w in plain], 1)
    qkv = project(normed_one, qkv_pad, cosines, sines)

    listed = lambda pieces: [pieces[j] for j in range(CHUNKS)]
    keep_side = jnp.stack([core, 2]).astype(jnp.int32)
    send_side = jnp.stack([1 - core, 2]).astype(jnp.int32)
    all_rows = jnp.array([0, 1], jnp.int32)

    def send_rows(lefts, groups, step, extra=None):
        if not by_hand:
            return rows_of(lefts, groups, all_rows, depth // 4, 4, step, extra)
        return swap(rows_of(lefts, groups, send_side, slice_rows, chips, step, extra))

    def keep_rows(lefts, groups, received, step, extra=None):
        if not by_hand:
            return received
        return rows_of(lefts, groups, keep_side, slice_rows, chips, step, extra, received)

    def scatter(array):
        axes = "chip" if by_hand else ("chip", "core")
        return lax.psum_scatter(array, axes, scatter_dimension=0, tiled=True)

    acc = None
    dhid_t, dqkv_own, input_grad, gains = {}, {}, {}, {}

    def back(j):
        nonlocal acc
        (dhid_t[j], dqkv_own[j], input_grad[j], gains[j]), acc = backward_chunk(
            level_ref,
            (total[j], final[j]),
            hidden[j],
            dout,
            tokens,
            (norm_gain, mlp_gain),
            (out_pad, qkv_pad),
            qkv,
            (own[j], other[j], across[j], outer[j]),
            (p_out, strip_one),
            (cosines, sines),
            acc,
            j,
            rows,
        )

    part, total, final, hidden, normed_t, activ, dgate, dup, mlp_part, qkv = fence(
        part, total, final, hidden, normed_t, activ, dgate, dup, mlp_part, qkv
    )
    add_3(c1)
    add_2(c2)
    add_1(c3)
    units = w_gate.shape[1]
    mlp_args = (
        [listed(normed_t), dout_t],
        [(0, listed(dgate)), (0, listed(dup)), (1, listed(activ))],
    )
    sent = send_rows(*mlp_args, units // 2)
    hidden, sent = fence(hidden, sent)
    grad_mlp = keep_rows(*mlp_args, sent, units // 2)
    hidden, grad_mlp = fence(hidden, grad_mlp)
    grad_mlp = scatter(grad_mlp)
    back(c0)

    near = lambda: jnp.where(low, mlp_part[1], mlp_part[2])
    edge = lambda: jnp.where(low, mlp_part[0], mlp_part[3])
    total, final, hidden, mlp_part, acc, dhid_t = fence(
        total, final, hidden, mlp_part, acc, dhid_t
    )
    add_3(c2)
    add_2(c3)
    leave = jnp.where(low, mlp_part[3], mlp_part[0])
    far_sum = leave + along(leave, INWARD)
    back(c1)
    total, final, hidden, mlp_part, far_sum, acc, dhid_t = fence(
        total, final, hidden, mlp_part, far_sum, acc, dhid_t
    )
    add_3(c3)
    leave = jnp.where(low, mlp_part[2], mlp_part[1])
    near_sum = leave + along(leave, INWARD)
    far_in = along(far_sum, MIDDLE)
    back(c2)
    total, final, hidden, mlp_part, near_sum, far_in, acc, dhid_t = fence(
        total, final, hidden, mlp_part, near_sum, far_in, acc, dhid_t
    )
    near_in = along(near_sum, MIDDLE)
    last = along(jnp.where(inner, edge() + far_in, near()), PAIRS)
    back(c3)

    dhid_t, dqkv_own, last, near_in = fence(dhid_t, dqkv_own, last, near_in)
    gain_sums = gains[0] + gains[1] + gains[2] + gains[3]
    extra = jnp.pad(gain_sums.T, ((0, 0), (0, LANES - 8)))
    out_args = ([listed(dhid_t)], [(0, listed(own))])
    qkv_args = ([normed_one_t], [(0, listed(dqkv_own))])
    q_cols = heads_here * HD
    send_qkv = send_rows(*qkv_args, q_cols)
    send_out = send_rows(*out_args, q_cols, extra)
    grad_qkv = keep_rows(*qkv_args, send_qkv, q_cols)
    grad_out = keep_rows(*out_args, send_out, q_cols, extra)
    grad_out, grad_qkv, grad_mlp = fence(grad_out, grad_qkv, grad_mlp)
    grad_qkv = scatter(grad_qkv)
    grad_out = scatter(grad_out)
    mlp_rows = jnp.where(inner, near() + near_in, edge()) + last
    hidden_rows = jnp.where(
        low,
        jnp.where(level == 0, hidden[0], hidden[1]),
        jnp.where(level == 2, hidden[2], hidden[3]),
    )
    layer_out = (hidden_rows + mlp_rows).astype(jnp.bfloat16)
    one = strip_one.shape[1]
    picked = lambda at, width: jnp.concatenate(
        [grad_qkv[:, kv * one + at : kv * one + at + width] for kv in range(kv_here)], 1
    )
    return (
        layer_out,
        jnp.concatenate(listed(input_grad), 0),
        grad_out[:, q_cols],
        picked(0, GROUP * HD),
        picked(GROUP * HD, HD),
        picked((GROUP + 1) * HD, HD),
        grad_out[:, :q_cols].T,
        grad_out[:, q_cols + 1],
        grad_mlp[:, :units],
        grad_mlp[:, units : 2 * units],
        grad_mlp[:, 2 * units :].T,
    )


def solution(mesh):
    devices = mesh.devices
    dp, tp = devices.shape
    split = Mesh(devices.reshape(dp // 2, 2, tp), ("chip", "core", "tp"))
    data = ("chip", "core")
    return jax.shard_map(
        shards,
        mesh=split,
        in_specs=(
            P(data, None),
            P(data),
            P(data),
            P(data, None),
            P(),
            P(None, "tp"),
            P(None, "tp"),
            P(None, "tp"),
            P("tp", None),
            P(),
            P(None, "tp"),
            P(None, "tp"),
            P("tp", None),
        ),
        out_specs=(
            P(("chip", "core", "tp"), None),
            P(data, None),
            P(data),
            P(data, "tp"),
            P(data, "tp"),
            P(data, "tp"),
            P("tp", data),
            P(data),
            P(data, "tp"),
            P(data, "tp"),
            P("tp", data),
        ),
        check_vma=False,
    )
```

```python
import functools

import jax
import jax.numpy as jnp
from jax import lax
from jax.experimental import pallas as pl
from jax.experimental.pallas import tpu as pltpu
from jax.sharding import Mesh
from jax.sharding import PartitionSpec as P

HD = 96
LANES = 128
GROUP = 2
KV_WIDE = (GROUP + 2) * LANES
rope_base = 100000.0
norm_eps = 1e-05
masked_score = -1e30
far_away = 1e30
score_scale = HD ** (-0.5)
score_scale_log2 = score_scale * 1.4426950408889634
CHUNKS = 4
EXTRA = 8
VMEM_BYTES = 56 * 1024 * 1024
NT = (((1,), (1,)), ((), ()))


def params():
    return pltpu.CompilerParams(vmem_limit_bytes=VMEM_BYTES)


def cost(flops, moved, exps=0):
    return pl.CostEstimate(
        flops=flops // 1024, bytes_accessed=moved // 1024, transcendentals=exps // 1024
    )


def dot32(a, b):
    return jnp.dot(a, b, preferred_element_type=jnp.float32)


def dot32_nt(a, b):
    return lax.dot_general(a, b, NT, preferred_element_type=jnp.float32)


def dot_split(a, places):
    high = a.astype(jnp.bfloat16)
    rest = (a - high.astype(jnp.float32)).astype(jnp.bfloat16)
    return dot32(high, places) + dot32(rest, places)


def fence(*trees):
    return lax.optimization_barrier(trees)


def whole(array, buffers=None):
    zeros = (0,) * len(array.shape)
    return pl.BlockSpec(array.shape, lambda *_: zeros)


SCALAR = pl.BlockSpec(memory_space=pltpu.SMEM)


def halves(entry):
    half_dim = HD // 2
    return (entry // half_dim) * (LANES // 2) + entry % half_dim


def placement(lanes, width):
    return (lanes[:, None] == jnp.arange(width)[None, :]).astype(jnp.bfloat16)


def place_query(heads):
    source = jnp.arange(heads * HD)
    return placement((source // HD) * LANES + halves(source % HD), heads * LANES)


def place_key_value(kv_heads):
    source = jnp.arange(kv_heads * HD)
    head = source // HD
    keys = head * 2 * LANES + halves(source % HD)
    values = head * 2 * LANES + LANES + source % HD
    return placement(jnp.concatenate([keys, values]), kv_heads * 2 * LANES)


def place_all(heads, kv_heads):
    source = jnp.arange(heads * HD)
    head = source // HD
    query = (head // GROUP) * KV_WIDE + (head % GROUP) * LANES + halves(source % HD)
    source = jnp.arange(kv_heads * HD)
    base = (source // HD) * KV_WIDE + GROUP * LANES
    keys = base + halves(source % HD)
    values = base + LANES + source % HD
    return placement(jnp.concatenate([query, keys, values]), kv_heads * KV_WIDE)


def place_plain(heads):
    source = jnp.arange(heads * HD)
    return placement((source // HD) * LANES + source % HD, heads * LANES)


PAIRS = [(0, 1), (1, 0), (2, 3), (3, 2)]
INWARD = [(0, 1), (3, 2)]
MIDDLE = [(1, 2), (2, 1)]
OUTWARD = [(1, 0), (2, 3)]


def along(part, pairs):
    return lax.ppermute(part, "tp", pairs)


def store_qkv(out_ref, here, base, query, key_value):
    wide = GROUP * LANES
    for kv in range(key_value.shape[1] // (2 * LANES)):
        at = base + kv * KV_WIDE
        there = slice(kv * 2 * LANES, (kv + 1) * 2 * LANES)
        out_ref[here, at : at + wide] = query[:, kv * wide : (kv + 1) * wide]
        out_ref[here, at + wide : at + KV_WIDE] = key_value[:, there]


def store_turned(out_ref, at, lin, cos_ref, sin_ref):
    for h in range(GROUP + 2):
        one = lin[:, h * LANES : (h + 1) * LANES]
        if h < GROUP + 1:
            one = one * cos_ref[...] + pltpu.roll(one, LANES // 2, 1) * sin_ref[...]
        out_ref[:, at + h * LANES : at + (h + 1) * LANES] = one.astype(jnp.bfloat16)


def spread_out_kernel(meta_ref, own_ref, p_ref, mine_ref, theirs_ref, pad_ref, plain_ref):
    rows, width = mine_ref.shape[2:]
    wide = p_ref.shape[1]
    for side, ref in enumerate((mine_ref, theirs_ref)):
        here = pl.ds(pl.multiple_of((meta_ref[1] ^ side) * rows, rows), rows)
        for s in range(4):
            block = own_ref[here, :] if s == 0 else ref[0, s - 1].astype(jnp.bfloat16)
            plain_ref[here, s * width : (s + 1) * width] = block
            pad_ref[here, s * wide : (s + 1) * wide] = dot32(block, p_ref[...]).astype(
                jnp.bfloat16
            )


def spread_qkv_kernel(meta_ref, own_ref, pq_ref, pkv_ref, mine_ref, theirs_ref, out_ref):
    rows = mine_ref.shape[2]
    wide = own_ref.shape[1]
    split = pq_ref.shape[0]
    out_ref[:, :wide] = own_ref[...]
    for side, ref in enumerate((mine_ref, theirs_ref)):
        here = pl.ds(pl.multiple_of((meta_ref[1] ^ side) * rows, rows), rows)
        for s in range(1, 4):
            block = ref[0, s - 1].astype(jnp.bfloat16)
            query = dot32(block[:, :split], pq_ref[...]).astype(jnp.bfloat16)
            key_value = dot32(block[:, split:], pkv_ref[...]).astype(jnp.bfloat16)
            store_qkv(out_ref, here, s * wide, query, key_value)


def spread(kernel, meta, own, places, mine, theirs, widths):
    chips, others, rows, width = mine.shape
    total = own.shape[0]
    row_block = lambda m, meta: (meta[0] ^ m, 0)
    piece = pl.BlockSpec((1, others, rows, width), lambda m, meta: (m, 0, 0, 0))
    return pl.pallas_call(
        kernel,
        out_shape=[jax.ShapeDtypeStruct((total, wide), jnp.bfloat16) for wide in widths],
        grid_spec=pltpu.PrefetchScalarGridSpec(
            num_scalar_prefetch=1,
            grid=(chips,),
            in_specs=[pl.BlockSpec((2 * rows, own.shape[1]), row_block)]
            + [whole(place) for place in places]
            + [piece, piece],
            out_specs=[pl.BlockSpec((2 * rows, wide), row_block) for wide in widths],
        ),
        compiler_params=params(),
        cost_estimate=cost(
            8 * total * width * 512, total * (12 * width + 2 * sum(widths))
        ),
    )(meta, own, *places, mine, theirs)


def start_kernel(x_ref, gain_ref, q_ref, k_ref, v_ref, pq_ref, pkv_ref, cos_ref, sin_ref, *outs):
    qkv_ref, normed_ref, pad_ref = outs

    @pl.when(pl.program_id(0) == 0)
    def _():
        split = k_ref.shape[0]
        query = dot32(q_ref[...], pq_ref[...]).astype(jnp.bfloat16)
        key_value = dot32(k_ref[...].T, pkv_ref[:split, :])
        key_value = key_value + dot32(v_ref[...].T, pkv_ref[split:, :])
        store_qkv(pad_ref, slice(None), 0, query, key_value.astype(jnp.bfloat16))

    inputs = x_ref[...].astype(jnp.float32)
    rms = lax.rsqrt(jnp.mean(inputs * inputs, -1, keepdims=True) + norm_eps)
    normed = (inputs * rms * gain_ref[...]).astype(jnp.bfloat16)
    normed_ref[...] = normed
    for kv in range(pad_ref.shape[1] // KV_WIDE):
        at = kv * KV_WIDE
        store_turned(qkv_ref, at, dot32(normed, pad_ref[:, at : at + KV_WIDE]), cos_ref, sin_ref)


def start(tokens, gain, w_query, w_key_t, w_value_t, pq, pkv, cosines, sines):
    total, depth = tokens.shape
    rows = total // CHUNKS
    wide = pq.shape[1] + pkv.shape[1]
    gain = gain[None, :]
    by_rows = lambda width: pl.BlockSpec((rows, width), lambda i: (i, 0))
    arrays = [w_query, w_key_t, w_value_t, pq, pkv]
    shapes = [
        jax.ShapeDtypeStruct((total, wide), jnp.bfloat16),
        jax.ShapeDtypeStruct((total, depth), jnp.bfloat16),
        jax.ShapeDtypeStruct((depth, wide), jnp.bfloat16),
    ]
    return pl.pallas_call(
        start_kernel,
        out_shape=shapes,
        grid=(CHUNKS,),
        in_specs=[by_rows(depth), whole(gain)]
        + [whole(array) for array in arrays]
        + [by_rows(LANES), by_rows(LANES)],
        out_specs=[by_rows(wide), by_rows(depth), whole(shapes[2])],
        compiler_params=params(),
        cost_estimate=cost(2 * total * depth * wide, 12 * total * depth),
    )(tokens, gain, *arrays, cosines, sines)


def turn_kernel(length_ref, cot_ref, normed_ref, dout_ref, dout_t_ref, normed_t_ref):
    rows = cot_ref.shape[0]
    at = pl.program_id(0) * rows + lax.broadcasted_iota(jnp.int32, cot_ref.shape, 0)
    dout = jnp.where(at < length_ref[0], cot_ref[...].astype(jnp.float32), 0.0)
    dout = dout.astype(jnp.bfloat16)
    dout_ref[...] = dout
    dout_t_ref[...] = dout.T
    normed_t_ref[...] = normed_ref[...].T


def turn(length, cotangent, normed):
    total, depth = cotangent.shape
    rows = total // CHUNKS
    by_rows = pl.BlockSpec((rows, depth), lambda i: (i, 0))
    by_columns = pl.BlockSpec((depth, rows), lambda i: (0, i))
    turned = jax.ShapeDtypeStruct((depth, total), jnp.bfloat16)
    return pl.pallas_call(
        turn_kernel,
        out_shape=[jax.ShapeDtypeStruct((total, depth), jnp.bfloat16), turned, turned],
        grid=(CHUNKS,),
        in_specs=[SCALAR, by_rows, by_rows],
        out_specs=[by_rows, by_columns, by_columns],
        compiler_params=params(),
        cost_estimate=cost(total * depth, 10 * total * depth),
    )(length, cotangent, normed)


def project_kernel(x_ref, w_ref, cos_ref, sin_ref, out_ref):
    store_turned(out_ref, 0, dot32(x_ref[...], w_ref[...]), cos_ref, sin_ref)


def project(normed, weights, cosines, sines):
    rows, depth = normed.shape
    width = weights.shape[1]
    return pl.pallas_call(
        project_kernel,
        out_shape=jax.ShapeDtypeStruct((rows, width), jnp.bfloat16),
        grid=(width // KV_WIDE,),
        in_specs=[
            whole(normed),
            pl.BlockSpec((depth, KV_WIDE), lambda i: (0, i)),
            whole(cosines),
            whole(sines),
        ],
        out_specs=pl.BlockSpec((rows, KV_WIDE), lambda i: (0, i)),
        compiler_params=params(),
        cost_estimate=cost(
            2 * rows * depth * width, 2 * (rows * depth + depth * width + rows * width)
        ),
    )(normed, weights, cosines, sines)


def attend_kernel(start, length_ref, q_ref, kv_ref, strip_ref, out_ref):
    rows = q_ref.shape[0]
    keys = kv_ref.shape[0]
    length = length_ref[0]
    row_ids = start + lax.broadcasted_iota(jnp.int32, (1, rows), 1)
    limit = jnp.minimum(row_ids, length - 1)
    allowed = lax.broadcasted_iota(jnp.int32, (keys, rows), 0) <= limit
    mixed = []
    sums = []
    for kv in range(kv_ref.shape[1] // KV_WIDE):
        base = kv * KV_WIDE
        at = base + GROUP * LANES
        key = kv_ref[:, at : at + LANES]
        value_t = kv_ref[:, at + LANES : at + 2 * LANES].T
        for g in range(GROUP):
            query = q_ref[:, base + g * LANES : base + (g + 1) * LANES]
            raw = jnp.where(allowed, dot32_nt(key, query), masked_score)
            peak = jnp.max(raw, axis=0, keepdims=True)
            expo = jnp.exp2((raw - peak) * score_scale_log2)
            total = jnp.sum(expo, axis=0, keepdims=True)
            probs = (expo * (1.0 / total)).astype(jnp.bfloat16)
            mixed.append(dot32(value_t, probs).T)
            log_sum = peak * score_scale_log2 + jnp.log2(total)
            sums.append(jnp.where(row_ids < length, log_sum, far_away))
    out_ref[:rows, :] = dot_split(jnp.concatenate(mixed, 1), strip_ref[...])
    out_ref[rows:, :] = jnp.zeros((EXTRA, out_ref.shape[1]), jnp.float32)
    out_ref[rows : rows + len(sums), :rows] = jnp.concatenate(sums, 0)


def attend(length, qkv, strip, index, rows):
    keys = (index + 1) * rows
    width = qkv.shape[1]
    heads = width // KV_WIDE * GROUP
    shape = (rows + EXTRA, strip.shape[1])
    return pl.pallas_call(
        functools.partial(attend_kernel, index * rows),
        out_shape=jax.ShapeDtypeStruct(shape, jnp.float32),
        grid=(1,),
        in_specs=[
            SCALAR,
            pl.BlockSpec((rows, width), lambda i: (index, 0)),
            pl.BlockSpec((keys, width), lambda i: (0, 0)),
            whole(strip),
        ],
        out_specs=pl.BlockSpec(shape, lambda i: (0, 0)),
        compiler_params=params(),
        cost_estimate=cost(
            4 * heads * rows * keys * LANES, 2 * (rows + keys) * width, heads * rows * keys
        ),
    )(length, qkv, qkv, strip)


def forward_kernel(level_ref, part_ref, other_ref, across_ref, outer_ref, *refs):
    x_ref, dout_ref, wo_ref, gain_ref, wg_ref, wu_ref, wd_ref = refs[:7]
    hidden_ref, normed_t_ref, activ_ref, dgate_ref, dup_ref, mlp_ref, dn_ref = refs[7:14]
    normed_ref = refs[14]
    rows = x_ref.shape[0]

    @pl.when(pl.program_id(0) == 0)
    def _():
        level = level_ref[0]
        inner = (level == 1) | (level == 2)
        width = part_ref.shape[1]
        second = jnp.where(inner, across_ref[:rows, width:], outer_ref[:rows, :width])
        third = jnp.where(inner, across_ref[:rows, :width], outer_ref[:rows, width:])
        mixed = jnp.concatenate([part_ref[:rows, :], other_ref[:rows, :], second, third], 1)
        hidden = x_ref[...].astype(jnp.float32) + dot32_nt(mixed.astype(jnp.bfloat16), wo_ref[...])
        hidden_ref[...] = hidden
        rms = lax.rsqrt(jnp.mean(hidden * hidden, -1, keepdims=True) + norm_eps)
        normed = (hidden * rms * gain_ref[...]).astype(jnp.bfloat16)
        normed_ref[...] = normed
        normed_t_ref[...] = normed.T
        mlp_ref[...] = jnp.zeros_like(mlp_ref)
        dn_ref[...] = jnp.zeros_like(dn_ref)

    normed = normed_ref[...]
    gate = dot32(normed, wg_ref[...])
    up = dot32(normed, wu_ref[...])
    dact = dot32_nt(dout_ref[...], wd_ref[...])
    sigmoid = jax.nn.sigmoid(gate)
    silu = gate * sigmoid
    activ = (silu * up).astype(jnp.bfloat16)
    dgate = (dact * up * sigmoid * (1.0 + gate * (1.0 - sigmoid))).astype(jnp.bfloat16)
    dup = (dact * silu).astype(jnp.bfloat16)
    activ_ref[...] = activ
    dgate_ref[...] = dgate
    dup_ref[...] = dup
    mlp_ref[...] += dot32(activ, wd_ref[...])
    dn_ref[...] += dot32_nt(dgate, wg_ref[...]) + dot32_nt(dup, wu_ref[...])


def forward_chunk(level, gathered, tokens, dout, w_out, gain, w_gate, w_up, w_down, index, rows):
    depth = tokens.shape[1]
    units = w_gate.shape[1]
    block = 512
    own_rows = pl.BlockSpec((rows, depth), lambda i: (index, 0))
    by_units = pl.BlockSpec((depth, block), lambda i: (0, i))
    gain = gain[None, :]
    f32, bf16 = jnp.float32, jnp.bfloat16
    outs = [
        jax.ShapeDtypeStruct((rows, depth), f32),
        jax.ShapeDtypeStruct((depth, rows), bf16),
        jax.ShapeDtypeStruct((rows, units), bf16),
        jax.ShapeDtypeStruct((rows, units), bf16),
        jax.ShapeDtypeStruct((rows, units), bf16),
        jax.ShapeDtypeStruct((rows, depth), f32),
        jax.ShapeDtypeStruct((rows, depth), f32),
    ]
    unit_out = pl.BlockSpec((rows, block), lambda i: (0, i))
    return pl.pallas_call(
        forward_kernel,
        out_shape=outs,
        grid=(units // block,),
        in_specs=[SCALAR]
        + [whole(array) for array in gathered]
        + [own_rows, own_rows, whole(w_out), whole(gain), by_units, by_units]
        + [pl.BlockSpec((block, depth), lambda i: (i, 0))],
        out_specs=[
            whole(outs[0]),
            whole(outs[1]),
            unit_out,
            unit_out,
            unit_out,
            whole(outs[5]),
            whole(outs[6]),
        ],
        scratch_shapes=[pltpu.VMEM((rows, depth), bf16)],
        compiler_params=params(),
        cost_estimate=cost(
            2 * rows * depth * (6 * units + w_out.shape[1]),
            2 * depth * (3 * units + w_out.shape[1]) + 22 * rows * depth,
            rows * units,
        ),
    )(level, *gathered, tokens, dout, w_out, gain, w_gate, w_up, w_down)


def hidden_grad(inner, total_ref, final_ref, hidden_ref, dout_ref, gain_ref):
    dnormed = jnp.where(inner, total_ref[...], final_ref[...])
    hidden = hidden_ref[...]
    rms = lax.rsqrt(jnp.mean(hidden * hidden, -1, keepdims=True) + norm_eps)
    scaled = dnormed * gain_ref[...]
    shift = jnp.mean(scaled * hidden, -1, keepdims=True)
    dhid = dout_ref[...].astype(jnp.float32) + (rms * scaled - hidden * (rms**3 * shift))
    return dhid, dnormed * (hidden * rms)


def hidden_grad_kernel(level_ref, total_ref, final_ref, hidden_ref, dout_ref, gain_ref, out_ref):
    inner = (level_ref[0] == 1) | (level_ref[0] == 2)
    dhid, _ = hidden_grad(inner, total_ref, final_ref, hidden_ref, dout_ref, gain_ref)
    out_ref[...] = dhid.astype(jnp.bfloat16).T


def hidden_grad_t(level, sums_two, hidden, dout, gain, index):
    rows, depth = hidden.shape
    gain = gain[None, :]
    return pl.pallas_call(
        hidden_grad_kernel,
        out_shape=jax.ShapeDtypeStruct((depth, rows), jnp.bfloat16),
        grid=(1,),
        in_specs=[SCALAR, whole(hidden), whole(hidden), whole(hidden)]
        + [pl.BlockSpec((rows, depth), lambda i: (index, 0)), whole(gain)],
        out_specs=pl.BlockSpec((depth, rows), lambda i: (0, 0)),
        compiler_params=params(),
        cost_estimate=cost(20 * rows * depth, 16 * rows * depth),
    )(level, *sums_two, hidden, dout, gain)


def backward_kernel(start, level_ref, total_ref, final_ref, hidden_ref, dout_ref, x_ref, *refs):
    gain_one_ref, gain_two_ref, wo_ref, w_ref, q_ref = refs[:5]
    kv_here = q_ref.shape[1] // KV_WIDE
    refs = refs[5:]
    kv_refs, refs = refs[: 2 * kv_here], refs[2 * kv_here :]
    part_ref, other_ref, across_ref, outer_ref, place_ref, strip_ref = refs[:6]
    cos_ref, sin_ref = refs[6:8]
    dhid_ref, low_ref, dn_ref = refs[-3:]
    outs = refs[8:-3]
    count = 5 if start > 0 else 4
    acc_ref = outs[0] if len(outs) > count else None
    outs = outs[-count:]
    dhid_t_ref, dqkv_ref, input_grad_ref, gains_ref = outs[:4]
    rows = q_ref.shape[0]
    keys = kv_refs[0].shape[0]
    shard = pl.program_id(0)
    level = level_ref[0]
    inner = (level == 1) | (level == 2)

    @pl.when(shard == 0)
    def _():
        dhid, dgain = hidden_grad(
            inner, total_ref, final_ref, hidden_ref, dout_ref, gain_two_ref
        )
        dhid_ref[...] = dhid
        low = dhid.astype(jnp.bfloat16)
        low_ref[...] = low
        dhid_t_ref[...] = low.T
        gains_ref[...] = jnp.zeros_like(gains_ref)
        gains_ref[1:2, :] = jnp.sum(dgain, 0, keepdims=True)
        dn_ref[...] = jnp.zeros_like(dn_ref)

    def rotate_back(grads):
        turned = grads * cos_ref[...] - pltpu.roll(grads, LANES // 2, 1) * sin_ref[...]
        return turned.astype(jnp.bfloat16)

    dmixed_all = dot32(low_ref[...], wo_ref[...]).astype(jnp.bfloat16)
    mixed = jnp.where(
        shard == 0,
        part_ref[...],
        jnp.where(shard == 1, other_ref[...], jnp.where(inner, across_ref[...], outer_ref[...])),
    )
    products = dmixed_all.astype(jnp.float32) * dot_split(mixed[:rows], place_ref[...])
    causal = lax.broadcasted_iota(jnp.int32, (rows, rows), 0) <= lax.broadcasted_iota(
        jnp.int32, (rows, rows), 1
    )
    grads = []
    for kv in range(kv_here):
        key_ref, value_ref = kv_refs[2 * kv : 2 * kv + 2]
        heads = range(kv * GROUP, (kv + 1) * GROUP)
        lanes = {h: slice(h * LANES, (h + 1) * LANES) for h in heads}
        row_dots = {h: jnp.sum(products[:, lanes[h]].T, axis=0, keepdims=True) for h in heads}
        log_sums = {h: mixed[rows + h : rows + h + 1, :rows] for h in heads}
        dqueries = dict.fromkeys(heads)
        here = slice(2 * kv * LANES, (2 * kv + 1) * LANES)
        there = slice((2 * kv + 1) * LANES, (2 * kv + 2) * LANES)
        for tile in range(keys // rows):
            span = slice(tile * rows, (tile + 1) * rows)
            key = key_ref[span, :]
            value = value_ref[span, :]
            key_t = key.T
            dkey = None if acc_ref is None else acc_ref[span, here]
            dvalue = None if acc_ref is None else acc_ref[span, there]
            last = tile * rows == start
            for h in heads:
                at = kv * KV_WIDE + (h % GROUP) * LANES
                query = q_ref[:, at : at + LANES]
                dmixed = dmixed_all[:, lanes[h]]
                raw = dot32_nt(key, query)
                probs = jnp.exp2(raw * score_scale_log2 - log_sums[h])
                if last:
                    probs = jnp.where(causal, probs, 0.0)
                dprobs = dot32_nt(value, dmixed)
                dscores = (probs * (dprobs - row_dots[h])).astype(jnp.bfloat16)
                dquery = dot32(key_t, dscores)
                dqueries[h] = dquery if dqueries[h] is None else dqueries[h] + dquery
                dkey_one = dot32(dscores, query)
                dvalue_one = dot32(probs.astype(jnp.bfloat16), dmixed)
                dkey = dkey_one if dkey is None else dkey + dkey_one
                dvalue = dvalue_one if dvalue is None else dvalue + dvalue_one
            if not last:
                outs[4][span, here] = dkey
                outs[4][span, there] = dvalue
        grads += [rotate_back(dqueries[h].T * score_scale) for h in heads]
        grads.append(rotate_back(dkey * score_scale))
        grads.append(dvalue.astype(jnp.bfloat16))
    grads = jnp.concatenate(grads, 1)
    dn_ref[...] += dot32_nt(grads, w_ref[...])

    @pl.when(shard == 0)
    def _():
        wide = strip_ref.shape[1]
        for kv in range(kv_here):
            dqkv_ref[:, kv * wide : (kv + 1) * wide] = dot32(
                grads[:, kv * KV_WIDE : (kv + 1) * KV_WIDE], strip_ref[...]
            ).astype(jnp.bfloat16)

    @pl.when(shard == pl.num_programs(0) - 1)
    def _():
        dnormed = dn_ref[...]
        inputs = x_ref[...].astype(jnp.float32)
        rms = lax.rsqrt(jnp.mean(inputs * inputs, -1, keepdims=True) + norm_eps)
        scaled = dnormed * gain_one_ref[...]
        shift = jnp.mean(scaled * inputs, -1, keepdims=True)
        grad = dhid_ref[...] + (rms * scaled - inputs * (rms**3 * shift))
        input_grad_ref[...] = grad.astype(jnp.bfloat16)
        gains_ref[0:1, :] = jnp.sum(dnormed * (inputs * rms), 0, keepdims=True)


def backward_chunk(
    level, sums_two, hidden, dout, tokens, gains, weights, qkv, gathered, places, tables, acc,
    index, rows
):
    start = index * rows
    keys = start + rows
    depth = tokens.shape[1]
    out_pad, qkv_pad = weights
    place_out, strip = places
    far_rows, width = gathered[0].shape
    out_wide = place_out.shape[1]
    kv_here = out_wide // (GROUP * LANES)
    wide = kv_here * KV_WIDE
    levels = qkv.shape[1] // wide
    own_rows = pl.BlockSpec((rows, depth), lambda t: (index, 0))
    table = pl.BlockSpec((rows, LANES), lambda t: (index, 0))
    gains = [gain[None, :] for gain in gains]
    key_value = lambda at: pl.BlockSpec(
        (keys, LANES), lambda t: (0, (wide // LANES) * t + at)
    )
    across = pl.BlockSpec((far_rows, width), lambda t: (0, jnp.where(t == 2, 1, 0)))
    outer = pl.BlockSpec((far_rows, width), lambda t: (0, jnp.where(t == 3, 1, 0)))
    in_specs = [
        SCALAR,
        whole(sums_two[0]),
        whole(sums_two[1]),
        whole(hidden),
        own_rows,
        own_rows,
        whole(gains[0]),
        whole(gains[1]),
        pl.BlockSpec((depth, out_wide), lambda t: (0, t)),
        pl.BlockSpec((depth, wide), lambda t: (0, t)),
        pl.BlockSpec((rows, wide), lambda t: (index, t)),
    ]
    for kv in range(kv_here):
        at = kv * (KV_WIDE // LANES) + GROUP
        in_specs += [key_value(at), key_value(at + 1)]
    in_specs += [
        whole(gathered[0]),
        whole(gathered[1]),
        across,
        outer,
        whole(place_out),
        whole(strip),
        table,
        table,
    ]
    args = [level, *sums_two, hidden, dout, tokens, *gains, out_pad, qkv_pad]
    args += [qkv] * (1 + 2 * kv_here)
    args += [*gathered, place_out, strip, *tables]
    sums_wide = 2 * kv_here * LANES
    if acc is not None:
        in_specs.append(pl.BlockSpec((keys, sums_wide), lambda t: (0, t)))
        args.append(acc)
    f32, bf16 = jnp.float32, jnp.bfloat16
    outs = [
        jax.ShapeDtypeStruct((depth, rows), bf16),
        jax.ShapeDtypeStruct((rows, kv_here * strip.shape[1]), bf16),
        jax.ShapeDtypeStruct((rows, depth), bf16),
        jax.ShapeDtypeStruct((8, depth), f32),
    ]
    out_specs = [whole(out) for out in outs]
    if start > 0:
        outs.append(jax.ShapeDtypeStruct((start, levels * sums_wide), f32))
        out_specs.append(pl.BlockSpec((start, sums_wide), lambda t: (0, t)))
    results = pl.pallas_call(
        functools.partial(backward_kernel, start),
        out_shape=outs,
        grid=(levels,),
        in_specs=in_specs,
        out_specs=out_specs,
        scratch_shapes=[
            pltpu.VMEM((rows, depth), f32),
            pltpu.VMEM((rows, depth), bf16),
            pltpu.VMEM((rows, depth), f32),
        ],
        compiler_params=params(),
        cost_estimate=cost(
            levels * rows * (20 * kv_here * keys * LANES + 2 * depth * (out_wide + wide)),
            2 * depth * levels * (out_wide + wide) + 16 * rows * depth,
            levels * kv_here * GROUP * rows * keys,
        ),
    )(*args)
    return results[:4], (results[4] if start > 0 else None)


def rows_kernel(lefts, groups, extras, adding, apart, side_ref, *refs):
    refs = list(refs)
    held_ref = refs.pop()
    out_refs = refs[-apart:]
    refs = refs[:-apart]
    recv_ref = refs.pop() if adding else None
    step = pl.program_id(0)
    left_refs = []
    for count in lefts:
        left_refs.append(refs[:count])
        refs = refs[count:]
    rights = []
    for _ in groups:
        rights.append(refs[:CHUNKS])
        refs = refs[CHUNKS:]
    rows = left_refs[0][0].shape[0]
    blocks = held_ref.shape[1] // rows

    @pl.when(step == 0)
    def _():
        for which, pieces in enumerate(left_refs):
            for n, ref in enumerate(pieces):
                m, j = n % blocks, n // blocks
                wide = ref.shape[1]
                held_ref[which, m * rows : (m + 1) * rows, j * wide : (j + 1) * wide] = ref[...]

    chunk = held_ref.shape[2] // CHUNKS
    right = None
    which = 0
    for group, (left, first, _) in zip(rights, groups):
        one = jnp.concatenate([ref[:chunk, :].astype(jnp.bfloat16) for ref in group], 0)
        right = one if right is None else jnp.where(step >= first, one, right)
        which = jnp.where(step >= first, left, which)
    total = dot32(held_ref[which], right)
    width = total.shape[1]
    held = total.shape[0] // apart
    if recv_ref is not None:
        total = total + recv_ref[:, :width]
    for n, out_ref in enumerate(out_refs):
        out_ref[:, :width] = total[n * held : (n + 1) * held]
    for m in range(extras):
        more = refs[m][...]
        if recv_ref is not None:
            more = more + recv_ref[m * rows : (m + 1) * rows, width:]
        at = m * rows % held
        out_refs[m * rows // held][at : at + rows, width:] = more


def rows_of(lefts, groups, side, rows, blocks, step, extra=None, recv=None, apart=1):
    at = lambda m: lambda i, side: ((m ^ side[2]) * side[1] + side[0], 0)
    specs = []
    args = []
    counts = []
    for left in lefts:
        pieces = left if isinstance(left, list) else [left]
        counts.append(len(pieces) * blocks)
        for piece in pieces:
            for m in range(blocks):
                specs.append(pl.BlockSpec((rows, piece.shape[1]), at(m)))
                args.append(piece)
    tokens = sum(piece.shape[1] for piece in pieces)
    first = 0
    plan = []
    for which, rights in groups:
        steps = rights[0].shape[1] // step
        plan.append((which, first, steps))
        for right in rights:
            pick = lambda i, side, first=first, steps=steps: (0, jnp.clip(i - first, 0, steps - 1))
            specs.append(pl.BlockSpec((right.shape[0], step), pick))
            args.append(right)
        first += steps
    total = first * step
    if extra is not None:
        for m in range(blocks):
            specs.append(pl.BlockSpec((rows, extra.shape[1]), at(m)))
            args.append(extra)
        total += extra.shape[1]
        step += extra.shape[1]
    block = lambda parts: pl.BlockSpec((rows * blocks // parts, step), lambda i, side: (0, i))
    if recv is not None:
        specs.append(block(1))
        args.append(recv)
    extras = 0 if extra is None else blocks
    results = pl.pallas_call(
        functools.partial(rows_kernel, counts, plan, extras, recv is not None, apart),
        out_shape=[jax.ShapeDtypeStruct((rows * blocks // apart, total), jnp.float32)] * apart,
        grid_spec=pltpu.PrefetchScalarGridSpec(
            num_scalar_prefetch=1,
            grid=(first,),
            in_specs=specs,
            out_specs=[block(apart)] * apart,
            scratch_shapes=[pltpu.VMEM((len(lefts), rows * blocks, tokens), jnp.bfloat16)],
        ),
        compiler_params=params(),
        cost_estimate=cost(
            2 * rows * blocks * tokens * total,
            4 * rows * blocks * total + 2 * tokens * (total + rows * blocks),
        ),
    )(side, *args)
    return results[0] if apart == 1 else results


def shards(
    tokens,
    lengths,
    positions,
    cotangent,
    norm_gain,
    w_query,
    w_key,
    w_value,
    w_out,
    mlp_gain,
    w_gate,
    w_up,
    w_down,
):
    seq_rows, depth = tokens.shape
    chips = lax.axis_size("chip")
    dp = chips * 2
    tp = lax.axis_size("tp")
    chip = lax.axis_index("chip")
    core = lax.axis_index("core")
    level = lax.axis_index("tp")
    low = level < 2
    inner = (level == 1) | (level == 2)
    heads_here = w_query.shape[1] // HD
    kv_here = w_key.shape[1] // HD
    rows = seq_rows // CHUNKS
    slice_rows = depth // dp
    level_ref = level.astype(jnp.int32).reshape(1)
    by_hand = dp == 8
    swap = lambda array: lax.ppermute(array, "core", [(0, 1), (1, 0)])
    to_level = lambda array, s: along(array, [(t, t ^ s) for t in range(tp)])

    at_row = (chip * 2 + core) * slice_rows
    cols = lambda w: lax.dynamic_slice_in_dim(w, at_row, slice_rows, 1).astype(jnp.float32).T
    (out_slice,) = fence(cols(w_out))
    qkv_slice = jnp.concatenate(
        [
            lax.dynamic_slice_in_dim(w_query, at_row, slice_rows, 0).astype(jnp.float32),
            cols(w_key.T),
            cols(w_value.T),
        ],
        1,
    )
    out_slice, qkv_slice = fence(out_slice, qkv_slice)
    if by_hand:
        out_far = [to_level(out_slice, s) for s in (1, 2, 3)]
        qkv_near = along(qkv_slice, PAIRS)
    meta = jnp.stack([chip, core]).astype(jnp.int32)

    pq = place_query(heads_here)
    pkv = place_key_value(kv_here)
    p_all = place_all(heads_here, kv_here)
    strip_one = place_all(GROUP, 1).T
    p_out = place_plain(heads_here)
    strip_out = p_out.T

    half_dim = HD // 2
    freqs = rope_base ** (-(jnp.arange(half_dim).astype(jnp.float32) * 2.0 / HD))
    freqs = jnp.pad(freqs, (0, LANES // 2 - half_dim))
    angles = positions.astype(jnp.float32)[:, None] * jnp.concatenate([freqs, freqs])[None, :]
    cosines = jnp.cos(angles)
    sines = jnp.sin(angles) * jnp.where(jnp.arange(LANES) < LANES // 2, -1.0, 1.0)

    qkv_own, normed_one, own_pad = start(
        tokens, norm_gain, w_query, w_key.T, w_value.T, pq, pkv, cosines, sines
    )

    order = list(reversed(range(CHUNKS)))
    c0, c1, c2, c3 = order
    own, other, pair, across, outer = {}, {}, {}, {}, {}
    part, total, final = {}, {}, {}

    def hop_1(j):
        other[j] = along(own[j], PAIRS)
        pair[j] = jnp.concatenate([own[j], other[j]], 1)

    def hop_2(j):
        across[j] = along(pair[j], MIDDLE)

    def hop_3(j):
        outer[j] = along(across[j], OUTWARD)

    coming = {}

    def add_1(j):
        coming[j] = along(part[j], INWARD)

    def add_2(j):
        total[j] = part[j] + coming[j]
        coming[j] = along(total[j], MIDDLE)

    def add_3(j):
        total[j] = total[j] + coming[j]
        final[j] = along(total[j], OUTWARD)

    def to_chip(array, m):
        return lax.ppermute(array, "chip", [(i, i ^ m) for i in range(chips)])

    def over_chips_1(piece):
        cut = piece.shape[1] // 2
        one, two = piece[:, :cut], piece[:, cut:]
        return jnp.stack([one, to_chip(one, 1)]), jnp.stack([two, to_chip(two, 2)])

    def over_chips_2(one, two):
        return one, to_chip(one, 2), two, to_chip(two, 1)

    def over_chips_3(one, one_far, two, two_far):
        upper = jnp.stack([one[0], one[1], one_far[0], one_far[1]])
        lower = jnp.stack([two[0], two_far[0], two[1], two_far[1]])
        return jnp.concatenate([upper, lower], 2)

    if by_hand:
        qkv_own, qkv_near, out_far = fence(qkv_own, qkv_near, out_far)
        out_mine = over_chips_1(jnp.stack(out_far))
        qkv_across = along(jnp.stack([qkv_slice, qkv_near]), MIDDLE)
    else:
        gathered_out = lax.all_gather(out_slice, ("chip", "core", "tp"))
        gathered_qkv = lax.all_gather(qkv_slice, ("chip", "core", "tp"))
    own[c0] = attend(lengths, qkv_own, strip_out, c0, rows)
    if by_hand:
        own, qkv_own, out_mine = fence(own, qkv_own, out_mine)
        out_mine = over_chips_2(*out_mine)
    else:
        own, qkv_own = fence(own, qkv_own)
    hop_1(c0)
    for j in (c1, c2, c3):
        own[j] = attend(lengths, qkv_own, strip_out, j, rows)
    if by_hand:
        own, other, pair, qkv_across = fence(own, other, pair, qkv_across)
    own, other, pair, normed_one, w_out = fence(own, other, pair, normed_one, w_out)
    hop_2(c0)
    hop_1(c1)
    dout, dout_t, normed_one_t = turn(lengths, cotangent, normed_one)
    w_out_t = w_out.T
    own, other, pair, across, dout, dout_t, normed_one_t, w_out_t = fence(
        own, other, pair, across, dout, dout_t, normed_one_t, w_out_t
    )
    if by_hand:
        out_mine, _ = fence(out_mine, own[c1])
        out_mine = over_chips_3(*out_mine)
        out_theirs = swap(out_mine)
        out_pad, out_plain = spread(
            spread_out_kernel,
            meta,
            w_out_t,
            [p_out],
            out_mine,
            out_theirs,
            [4 * p_out.shape[1], 4 * p_out.shape[0]],
        )
    else:
        by_shard = lambda g, s: lax.dynamic_index_in_dim(
            g.reshape(dp, tp, slice_rows, -1), level ^ s, 1, False
        ).reshape(depth, -1)
        plain = [fence(by_shard(gathered_out, s))[0].astype(jnp.bfloat16) for s in range(4)]
        out_plain = jnp.concatenate(plain, 1)
        out_pad = jnp.concatenate([dot32(w, p_out).astype(jnp.bfloat16) for w in plain], 1)
    hop_3(c0)
    hop_2(c1)
    hop_1(c2)
    own, other, pair, across, outer, out_pad, out_plain = fence(
        own, other, pair, across, outer, out_pad, out_plain
    )
    hidden, normed_t, activ, dgate, dup, mlp_part = {}, {}, {}, {}, {}, {}

    def feed(j):
        gathered = (own[j], other[j], across[j], outer[j])
        (hidden[j], normed_t[j], activ[j], dgate[j], dup[j], mlp_part[j], part[j]) = forward_chunk(
            level_ref, gathered, tokens, dout, out_plain, mlp_gain, w_gate, w_up, w_down, j, rows
        )

    feed(c0)
    hop_3(c1)
    hop_2(c2)
    hop_1(c3)
    own, other, pair, across, outer, part, hidden = fence(
        own, other, pair, across, outer, part, hidden
    )
    add_1(c0)
    hop_3(c2)
    hop_2(c3)
    if by_hand:
        qkv_across, _ = fence(qkv_across, own[c0])
        qkv_outer = along(qkv_across, OUTWARD)
    feed(c1)
    own, other, across, outer, part, total, coming, hidden = fence(
        own, other, across, outer, part, total, coming, hidden
    )
    add_2(c0)
    add_1(c1)
    hop_3(c3)
    if by_hand:
        qkv_outer, qkv_near, qkv_across, _ = fence(
            qkv_outer, qkv_near, qkv_across, hidden[c1]
        )
        qkv_far = [
            qkv_near,
            jnp.where(inner, qkv_across[1], qkv_outer[0]),
            jnp.where(inner, qkv_across[0], qkv_outer[1]),
        ]
        qkv_mine = over_chips_1(jnp.stack(qkv_far))
    feed(c2)
    own, other, across, outer, part, total, coming, hidden = fence(
        own, other, across, outer, part, total, coming, hidden
    )
    add_3(c0)
    add_2(c1)
    add_1(c2)
    if by_hand:
        qkv_mine, _ = fence(qkv_mine, hidden[c2])
        qkv_mine = over_chips_2(*qkv_mine)
    feed(c3)

    listed = lambda pieces: [pieces[j] for j in range(CHUNKS)]
    keep_side = jnp.stack([core, 2, 0]).astype(jnp.int32)
    keep_turned = jnp.stack([core, 2, chip]).astype(jnp.int32)
    send_side = jnp.stack([1 - core, 2, 0]).astype(jnp.int32)
    send_turned = jnp.stack([1 - core, 2, chip]).astype(jnp.int32)
    all_rows = jnp.array([0, 1, 0], jnp.int32)

    def send_rows(lefts, groups, step, extra=None, side=send_side):
        if not by_hand:
            return rows_of(lefts, groups, all_rows, depth // 4, 4, step, extra)
        return rows_of(lefts, groups, side, slice_rows, chips, step, extra)

    def keep_rows(lefts, groups, received, step, extra=None, side=keep_side, apart=1):
        if not by_hand:
            return received
        return rows_of(
            lefts, groups, side, slice_rows, chips, step, extra, received, apart
        )

    def swap_rows(array):
        return swap(array) if by_hand else array

    def scatter(array):
        axes = "chip" if by_hand else ("chip", "core")
        return lax.psum_scatter(array, axes, scatter_dimension=0, tiled=True)

    units = w_gate.shape[1]
    mlp_args = (
        [listed(normed_t), dout_t],
        [(0, listed(dgate)), (0, listed(dup)), (1, listed(activ))],
    )
    sent = send_rows(*mlp_args, units // 2)

    acc = None
    dhid_t, dqkv_own, input_grad, gains = {}, {}, {}, {}

    def back(j):
        nonlocal acc
        (dhid_t[j], dqkv_own[j], input_grad[j], gains[j]), acc = backward_chunk(
            level_ref,
            (total[j], final[j]),
            hidden[j],
            dout,
            tokens,
            (norm_gain, mlp_gain),
            (out_pad, qkv_pad),
            qkv,
            (own[j], other[j], across[j], outer[j]),
            (p_out, strip_one),
            (cosines, sines),
            acc,
            j,
            rows,
        )

    part, total, coming, final, hidden, mlp_part, sent = fence(
        part, total, coming, final, hidden, mlp_part, sent
    )
    sent = swap_rows(sent)
    add_3(c1)
    add_2(c2)
    add_1(c3)
    if by_hand:
        qkv_mine, _ = fence(qkv_mine, hidden[c3])
        qkv_mine = over_chips_3(*qkv_mine)
        qkv_theirs = swap(qkv_mine)
        (qkv_pad,) = spread(
            spread_qkv_kernel,
            meta,
            own_pad,
            [pq, pkv],
            qkv_mine,
            qkv_theirs,
            [4 * own_pad.shape[1]],
        )
    else:
        plain = [
            fence(by_shard(gathered_qkv, s))[0].astype(jnp.bfloat16) for s in range(4)
        ]
        qkv_pad = jnp.concatenate([dot32(w, p_all).astype(jnp.bfloat16) for w in plain], 1)
    qkv = project(normed_one, qkv_pad, cosines, sines)

    near = lambda: jnp.where(low, mlp_part[1], mlp_part[2])
    edge = lambda: jnp.where(low, mlp_part[0], mlp_part[3])
    part, total, coming, final, hidden, mlp_part, sent, qkv = fence(
        part, total, coming, final, hidden, mlp_part, sent, qkv
    )
    add_3(c2)
    add_2(c3)
    leave_far = jnp.where(low, mlp_part[3], mlp_part[0])
    leave_near = jnp.where(low, mlp_part[2], mlp_part[1])
    far_sum = along(leave_far, INWARD)
    grad_mlp = keep_rows(*mlp_args, sent, units // 2)
    hidden, grad_mlp = fence(hidden, grad_mlp)
    grad_mlp = scatter(grad_mlp)
    back(c0)
    total, coming, final, hidden, mlp_part, far_sum, acc, dhid_t = fence(
        total, coming, final, hidden, mlp_part, far_sum, acc, dhid_t
    )
    add_3(c3)
    near_sum = along(leave_near, INWARD)
    far_in = along(leave_far + far_sum, MIDDLE)
    back(c1)
    total, final, hidden, mlp_part, near_sum, far_in, acc, dhid_t = fence(
        total, final, hidden, mlp_part, near_sum, far_in, acc, dhid_t
    )
    near_in = along(leave_near + near_sum, MIDDLE)
    last = along(jnp.where(inner, edge() + far_in, near()), PAIRS)
    last_hidden_t = hidden_grad_t(
        level_ref, (total[c3], final[c3]), hidden[c3], dout, mlp_gain, c3
    )
    back(c2)
    q_cols = heads_here * HD
    out_args = (
        [[last_hidden_t if j == c3 else dhid_t[j] for j in range(CHUNKS)]],
        [(0, listed(own))],
    )
    sent = send_rows(*out_args, q_cols)
    total, final, hidden, acc, sent, last, near_in = fence(
        total, final, hidden, acc, sent, last, near_in
    )
    sent, hidden = fence(swap_rows(sent), hidden)
    grad_out, hidden = fence(keep_rows(*out_args, sent, q_cols), hidden)
    grad_out = scatter(grad_out)
    back(c3)
    dqkv_own, gains = fence(dqkv_own, gains)
    gain_sums = gains[0] + gains[1] + gains[2] + gains[3]
    extra = jnp.pad(gain_sums.T, ((0, 0), (0, LANES - 8)))
    qkv_args = ([normed_one_t], [(0, listed(dqkv_own))])
    qkv_wide = 2 * q_cols
    send_qkv = swap_rows(send_rows(*qkv_args, qkv_wide, extra, send_turned))
    send_qkv, grad_mlp, grad_out = fence(send_qkv, grad_mlp, grad_out)
    if by_hand:
        pieces = keep_rows(*qkv_args, send_qkv, qkv_wide, extra, keep_turned, chips)
        grad_qkv = pieces[0]
        for m in range(1, chips):
            grad_qkv = grad_qkv + to_chip(pieces[m], m)
    else:
        grad_qkv = scatter(send_qkv)
    mlp_rows = jnp.where(inner, near() + near_in, edge()) + last
    hidden_rows = jnp.where(
        low,
        jnp.where(level == 0, hidden[0], hidden[1]),
        jnp.where(level == 2, hidden[2], hidden[3]),
    )
    layer_out = (hidden_rows + mlp_rows).astype(jnp.bfloat16)
    one = strip_one.shape[1]
    picked = lambda at, width: jnp.concatenate(
        [grad_qkv[:, kv * one + at : kv * one + at + width] for kv in range(kv_here)], 1
    )
    return (
        layer_out,
        jnp.concatenate(listed(input_grad), 0),
        grad_qkv[:, qkv_wide],
        picked(0, GROUP * HD),
        picked(GROUP * HD, HD),
        picked((GROUP + 1) * HD, HD),
        grad_out.T,
        grad_qkv[:, qkv_wide + 1],
        grad_mlp[:, :units],
        grad_mlp[:, units : 2 * units],
        grad_mlp[:, 2 * units :].T,
    )


def solution(mesh):
    devices = mesh.devices
    dp, tp = devices.shape
    split = Mesh(devices.reshape(dp // 2, 2, tp), ("chip", "core", "tp"))
    data = ("chip", "core")
    return jax.shard_map(
        shards,
        mesh=split,
        in_specs=(
            P(data, None),
            P(data),
            P(data),
            P(data, None),
            P(),
            P(None, "tp"),
            P(None, "tp"),
            P(None, "tp"),
            P("tp", None),
            P(),
            P(None, "tp"),
            P(None, "tp"),
            P("tp", None),
        ),
        out_specs=(
            P(("chip", "core", "tp"), None),
            P(data, None),
            P(data),
            P(data, "tp"),
            P(data, "tp"),
            P(data, "tp"),
            P("tp", data),
            P(data),
            P(data, "tp"),
            P(data, "tp"),
            P("tp", data),
        ),
        check_vma=False,
    )
```

```python
import functools

import jax
import jax.numpy as jnp
from jax import lax
from jax.experimental import pallas as pl
from jax.experimental.pallas import tpu as pltpu
from jax.sharding import Mesh
from jax.sharding import PartitionSpec as P

HD = 96
LANES = 128
GROUP = 2
KV_WIDE = (GROUP + 2) * LANES
rope_base = 100000.0
norm_eps = 1e-05
masked_score = -1e30
far_away = 1e30
score_scale = HD ** (-0.5)
score_scale_log2 = score_scale * 1.4426950408889634
CHUNKS = 4
EXTRA = 8
VMEM_BYTES = 56 * 1024 * 1024
NT = (((1,), (1,)), ((), ()))


def params():
    return pltpu.CompilerParams(vmem_limit_bytes=VMEM_BYTES)


def cost(flops, moved, exps=0):
    return pl.CostEstimate(
        flops=flops // 1024, bytes_accessed=moved // 1024, transcendentals=exps // 1024
    )


def dot32(a, b):
    return jnp.dot(a, b, preferred_element_type=jnp.float32)


def dot32_nt(a, b):
    return lax.dot_general(a, b, NT, preferred_element_type=jnp.float32)


def dot_split(a, places):
    high = a.astype(jnp.bfloat16)
    rest = (a - high.astype(jnp.float32)).astype(jnp.bfloat16)
    return dot32(high, places) + dot32(rest, places)


def fence(*trees):
    return lax.optimization_barrier(trees)


def whole(array, buffers=None):
    zeros = (0,) * len(array.shape)
    return pl.BlockSpec(array.shape, lambda *_: zeros)


SCALAR = pl.BlockSpec(memory_space=pltpu.SMEM)


def halves(entry):
    half_dim = HD // 2
    return (entry // half_dim) * (LANES // 2) + entry % half_dim


def placement(lanes, width):
    return (lanes[:, None] == jnp.arange(width)[None, :]).astype(jnp.bfloat16)


def place_query(heads):
    source = jnp.arange(heads * HD)
    return placement((source // HD) * LANES + halves(source % HD), heads * LANES)


def place_key_value(kv_heads):
    source = jnp.arange(kv_heads * HD)
    head = source // HD
    keys = head * 2 * LANES + halves(source % HD)
    values = head * 2 * LANES + LANES + source % HD
    return placement(jnp.concatenate([keys, values]), kv_heads * 2 * LANES)


def place_all(heads, kv_heads):
    source = jnp.arange(heads * HD)
    head = source // HD
    query = (head // GROUP) * KV_WIDE + (head % GROUP) * LANES + halves(source % HD)
    source = jnp.arange(kv_heads * HD)
    base = (source // HD) * KV_WIDE + GROUP * LANES
    keys = base + halves(source % HD)
    values = base + LANES + source % HD
    return placement(jnp.concatenate([query, keys, values]), kv_heads * KV_WIDE)


def place_plain(heads):
    source = jnp.arange(heads * HD)
    return placement((source // HD) * LANES + source % HD, heads * LANES)


PAIRS = [(0, 1), (1, 0), (2, 3), (3, 2)]
INWARD = [(0, 1), (3, 2)]
MIDDLE = [(1, 2), (2, 1)]
OUTWARD = [(1, 0), (2, 3)]


def along(part, pairs):
    return lax.ppermute(part, "tp", pairs)


def store_qkv(out_ref, here, base, query, key_value):
    wide = GROUP * LANES
    for kv in range(key_value.shape[1] // (2 * LANES)):
        at = base + kv * KV_WIDE
        there = slice(kv * 2 * LANES, (kv + 1) * 2 * LANES)
        out_ref[here, at : at + wide] = query[:, kv * wide : (kv + 1) * wide]
        out_ref[here, at + wide : at + KV_WIDE] = key_value[:, there]


def store_turned(out_ref, at, lin, cos_ref, sin_ref):
    for h in range(GROUP + 2):
        one = lin[:, h * LANES : (h + 1) * LANES]
        if h < GROUP + 1:
            one = one * cos_ref[...] + pltpu.roll(one, LANES // 2, 1) * sin_ref[...]
        out_ref[:, at + h * LANES : at + (h + 1) * LANES] = one.astype(jnp.bfloat16)


def spread_out_kernel(meta_ref, own_ref, p_ref, mine_ref, theirs_ref, pad_ref, plain_ref):
    rows, width = mine_ref.shape[2:]
    wide = p_ref.shape[1]
    for side, ref in enumerate((mine_ref, theirs_ref)):
        here = pl.ds(pl.multiple_of((meta_ref[1] ^ side) * rows, rows), rows)
        for s in range(4):
            block = own_ref[here, :] if s == 0 else ref[0, s - 1].astype(jnp.bfloat16)
            plain_ref[here, s * width : (s + 1) * width] = block
            pad_ref[here, s * wide : (s + 1) * wide] = dot32(block, p_ref[...]).astype(
                jnp.bfloat16
            )


def spread_qkv_kernel(meta_ref, own_ref, pq_ref, pkv_ref, mine_ref, theirs_ref, out_ref):
    rows = mine_ref.shape[2]
    wide = own_ref.shape[1]
    split = pq_ref.shape[0]
    out_ref[:, :wide] = own_ref[...]
    for side, ref in enumerate((mine_ref, theirs_ref)):
        here = pl.ds(pl.multiple_of((meta_ref[1] ^ side) * rows, rows), rows)
        for s in range(1, 4):
            block = ref[0, s - 1].astype(jnp.bfloat16)
            query = dot32(block[:, :split], pq_ref[...]).astype(jnp.bfloat16)
            key_value = dot32(block[:, split:], pkv_ref[...]).astype(jnp.bfloat16)
            store_qkv(out_ref, here, s * wide, query, key_value)


def spread(kernel, meta, own, places, mine, theirs, widths):
    chips, others, rows, width = mine.shape
    total = own.shape[0]
    row_block = lambda m, meta: (meta[0] ^ m, 0)
    piece = pl.BlockSpec((1, others, rows, width), lambda m, meta: (m, 0, 0, 0))
    return pl.pallas_call(
        kernel,
        out_shape=[jax.ShapeDtypeStruct((total, wide), jnp.bfloat16) for wide in widths],
        grid_spec=pltpu.PrefetchScalarGridSpec(
            num_scalar_prefetch=1,
            grid=(chips,),
            in_specs=[pl.BlockSpec((2 * rows, own.shape[1]), row_block)]
            + [whole(place) for place in places]
            + [piece, piece],
            out_specs=[pl.BlockSpec((2 * rows, wide), row_block) for wide in widths],
        ),
        compiler_params=params(),
        cost_estimate=cost(
            8 * total * width * 512, total * (12 * width + 2 * sum(widths))
        ),
    )(meta, own, *places, mine, theirs)


def start_kernel(x_ref, gain_ref, q_ref, k_ref, v_ref, pq_ref, pkv_ref, cos_ref, sin_ref, *outs):
    qkv_ref, normed_ref, pad_ref = outs

    @pl.when(pl.program_id(0) == 0)
    def _():
        split = k_ref.shape[0]
        query = dot32(q_ref[...], pq_ref[...]).astype(jnp.bfloat16)
        key_value = dot32(k_ref[...].T, pkv_ref[:split, :])
        key_value = key_value + dot32(v_ref[...].T, pkv_ref[split:, :])
        store_qkv(pad_ref, slice(None), 0, query, key_value.astype(jnp.bfloat16))

    inputs = x_ref[...].astype(jnp.float32)
    rms = lax.rsqrt(jnp.mean(inputs * inputs, -1, keepdims=True) + norm_eps)
    normed = (inputs * rms * gain_ref[...]).astype(jnp.bfloat16)
    normed_ref[...] = normed
    for kv in range(pad_ref.shape[1] // KV_WIDE):
        at = kv * KV_WIDE
        store_turned(qkv_ref, at, dot32(normed, pad_ref[:, at : at + KV_WIDE]), cos_ref, sin_ref)


def start(tokens, gain, w_query, w_key_t, w_value_t, pq, pkv, cosines, sines):
    total, depth = tokens.shape
    rows = total // CHUNKS
    wide = pq.shape[1] + pkv.shape[1]
    gain = gain[None, :]
    by_rows = lambda width: pl.BlockSpec((rows, width), lambda i: (i, 0))
    arrays = [w_query, w_key_t, w_value_t, pq, pkv]
    shapes = [
        jax.ShapeDtypeStruct((total, wide), jnp.bfloat16),
        jax.ShapeDtypeStruct((total, depth), jnp.bfloat16),
        jax.ShapeDtypeStruct((depth, wide), jnp.bfloat16),
    ]
    return pl.pallas_call(
        start_kernel,
        out_shape=shapes,
        grid=(CHUNKS,),
        in_specs=[by_rows(depth), whole(gain)]
        + [whole(array) for array in arrays]
        + [by_rows(LANES), by_rows(LANES)],
        out_specs=[by_rows(wide), by_rows(depth), whole(shapes[2])],
        compiler_params=params(),
        cost_estimate=cost(2 * total * depth * wide, 12 * total * depth),
    )(tokens, gain, *arrays, cosines, sines)


def turn_kernel(length_ref, cot_ref, normed_ref, dout_ref, dout_t_ref, normed_t_ref):
    rows = cot_ref.shape[0]
    at = pl.program_id(0) * rows + lax.broadcasted_iota(jnp.int32, cot_ref.shape, 0)
    dout = jnp.where(at < length_ref[0], cot_ref[...].astype(jnp.float32), 0.0)
    dout = dout.astype(jnp.bfloat16)
    dout_ref[...] = dout
    dout_t_ref[...] = dout.T
    normed_t_ref[...] = normed_ref[...].T


def turn(length, cotangent, normed):
    total, depth = cotangent.shape
    rows = total // CHUNKS
    by_rows = pl.BlockSpec((rows, depth), lambda i: (i, 0))
    by_columns = pl.BlockSpec((depth, rows), lambda i: (0, i))
    turned = jax.ShapeDtypeStruct((depth, total), jnp.bfloat16)
    return pl.pallas_call(
        turn_kernel,
        out_shape=[jax.ShapeDtypeStruct((total, depth), jnp.bfloat16), turned, turned],
        grid=(CHUNKS,),
        in_specs=[SCALAR, by_rows, by_rows],
        out_specs=[by_rows, by_columns, by_columns],
        compiler_params=params(),
        cost_estimate=cost(total * depth, 10 * total * depth),
    )(length, cotangent, normed)


def project_kernel(x_ref, w_ref, cos_ref, sin_ref, out_ref):
    store_turned(out_ref, 0, dot32(x_ref[...], w_ref[...]), cos_ref, sin_ref)


def project(normed, weights, cosines, sines):
    rows, depth = normed.shape
    width = weights.shape[1]
    return pl.pallas_call(
        project_kernel,
        out_shape=jax.ShapeDtypeStruct((rows, width), jnp.bfloat16),
        grid=(width // KV_WIDE,),
        in_specs=[
            whole(normed),
            pl.BlockSpec((depth, KV_WIDE), lambda i: (0, i)),
            whole(cosines),
            whole(sines),
        ],
        out_specs=pl.BlockSpec((rows, KV_WIDE), lambda i: (0, i)),
        compiler_params=params(),
        cost_estimate=cost(
            2 * rows * depth * width, 2 * (rows * depth + depth * width + rows * width)
        ),
    )(normed, weights, cosines, sines)


def attend_kernel(start, length_ref, q_ref, kv_ref, strip_ref, out_ref):
    rows = q_ref.shape[0]
    keys = kv_ref.shape[0]
    length = length_ref[0]
    row_ids = start + lax.broadcasted_iota(jnp.int32, (1, rows), 1)
    limit = jnp.minimum(row_ids, length - 1)
    allowed = lax.broadcasted_iota(jnp.int32, (keys, rows), 0) <= limit
    mixed = []
    sums = []
    for kv in range(kv_ref.shape[1] // KV_WIDE):
        base = kv * KV_WIDE
        at = base + GROUP * LANES
        key = kv_ref[:, at : at + LANES]
        value_t = kv_ref[:, at + LANES : at + 2 * LANES].T
        for g in range(GROUP):
            query = q_ref[:, base + g * LANES : base + (g + 1) * LANES]
            raw = jnp.where(allowed, dot32_nt(key, query), masked_score)
            peak = jnp.max(raw, axis=0, keepdims=True)
            expo = jnp.exp2((raw - peak) * score_scale_log2)
            total = jnp.sum(expo, axis=0, keepdims=True)
            probs = (expo * (1.0 / total)).astype(jnp.bfloat16)
            mixed.append(dot32(value_t, probs).T)
            log_sum = peak * score_scale_log2 + jnp.log2(total)
            sums.append(jnp.where(row_ids < length, log_sum, far_away))
    out_ref[:rows, :] = dot_split(jnp.concatenate(mixed, 1), strip_ref[...])
    out_ref[rows:, :] = jnp.zeros((EXTRA, out_ref.shape[1]), jnp.float32)
    out_ref[rows : rows + len(sums), :rows] = jnp.concatenate(sums, 0)


def attend(length, qkv, strip, index, rows):
    keys = (index + 1) * rows
    width = qkv.shape[1]
    heads = width // KV_WIDE * GROUP
    shape = (rows + EXTRA, strip.shape[1])
    return pl.pallas_call(
        functools.partial(attend_kernel, index * rows),
        out_shape=jax.ShapeDtypeStruct(shape, jnp.float32),
        grid=(1,),
        in_specs=[
            SCALAR,
            pl.BlockSpec((rows, width), lambda i: (index, 0)),
            pl.BlockSpec((keys, width), lambda i: (0, 0)),
            whole(strip),
        ],
        out_specs=pl.BlockSpec(shape, lambda i: (0, 0)),
        compiler_params=params(),
        cost_estimate=cost(
            4 * heads * rows * keys * LANES, 2 * (rows + keys) * width, heads * rows * keys
        ),
    )(length, qkv, qkv, strip)


def forward_kernel(level_ref, part_ref, other_ref, across_ref, outer_ref, *refs):
    x_ref, dout_ref, wo_ref, gain_ref, wg_ref, wu_ref, wd_ref = refs[:7]
    hidden_ref, normed_t_ref, activ_ref, dgate_ref, dup_ref, mlp_ref, dn_ref = refs[7:14]
    normed_ref = refs[14]
    rows = x_ref.shape[0]

    @pl.when(pl.program_id(0) == 0)
    def _():
        level = level_ref[0]
        inner = (level == 1) | (level == 2)
        width = part_ref.shape[1]
        second = jnp.where(inner, across_ref[:rows, width:], outer_ref[:rows, :width])
        third = jnp.where(inner, across_ref[:rows, :width], outer_ref[:rows, width:])
        mixed = jnp.concatenate([part_ref[:rows, :], other_ref[:rows, :], second, third], 1)
        hidden = x_ref[...].astype(jnp.float32) + dot32_nt(mixed.astype(jnp.bfloat16), wo_ref[...])
        hidden_ref[...] = hidden
        rms = lax.rsqrt(jnp.mean(hidden * hidden, -1, keepdims=True) + norm_eps)
        normed = (hidden * rms * gain_ref[...]).astype(jnp.bfloat16)
        normed_ref[...] = normed
        normed_t_ref[...] = normed.T
        mlp_ref[...] = jnp.zeros_like(mlp_ref)
        dn_ref[...] = jnp.zeros_like(dn_ref)

    normed = normed_ref[...]
    gate = dot32(normed, wg_ref[...])
    up = dot32(normed, wu_ref[...])
    dact = dot32_nt(dout_ref[...], wd_ref[...])
    sigmoid = jax.nn.sigmoid(gate)
    silu = gate * sigmoid
    activ = (silu * up).astype(jnp.bfloat16)
    dgate = (dact * up * sigmoid * (1.0 + gate * (1.0 - sigmoid))).astype(jnp.bfloat16)
    dup = (dact * silu).astype(jnp.bfloat16)
    activ_ref[...] = activ
    dgate_ref[...] = dgate
    dup_ref[...] = dup
    mlp_ref[...] += dot32(activ, wd_ref[...])
    dn_ref[...] += dot32_nt(dgate, wg_ref[...]) + dot32_nt(dup, wu_ref[...])


def forward_chunk(level, gathered, tokens, dout, w_out, gain, w_gate, w_up, w_down, index, rows):
    depth = tokens.shape[1]
    units = w_gate.shape[1]
    block = 512
    own_rows = pl.BlockSpec((rows, depth), lambda i: (index, 0))
    by_units = pl.BlockSpec((depth, block), lambda i: (0, i))
    gain = gain[None, :]
    f32, bf16 = jnp.float32, jnp.bfloat16
    outs = [
        jax.ShapeDtypeStruct((rows, depth), f32),
        jax.ShapeDtypeStruct((depth, rows), bf16),
        jax.ShapeDtypeStruct((rows, units), bf16),
        jax.ShapeDtypeStruct((rows, units), bf16),
        jax.ShapeDtypeStruct((rows, units), bf16),
        jax.ShapeDtypeStruct((rows, depth), f32),
        jax.ShapeDtypeStruct((rows, depth), f32),
    ]
    unit_out = pl.BlockSpec((rows, block), lambda i: (0, i))
    return pl.pallas_call(
        forward_kernel,
        out_shape=outs,
        grid=(units // block,),
        in_specs=[SCALAR]
        + [whole(array) for array in gathered]
        + [own_rows, own_rows, whole(w_out), whole(gain), by_units, by_units]
        + [pl.BlockSpec((block, depth), lambda i: (i, 0))],
        out_specs=[
            whole(outs[0]),
            whole(outs[1]),
            unit_out,
            unit_out,
            unit_out,
            whole(outs[5]),
            whole(outs[6]),
        ],
        scratch_shapes=[pltpu.VMEM((rows, depth), bf16)],
        compiler_params=params(),
        cost_estimate=cost(
            2 * rows * depth * (6 * units + w_out.shape[1]),
            2 * depth * (3 * units + w_out.shape[1]) + 22 * rows * depth,
            rows * units,
        ),
    )(level, *gathered, tokens, dout, w_out, gain, w_gate, w_up, w_down)


def hidden_grad(inner, total_ref, final_ref, hidden_ref, dout_ref, gain_ref):
    dnormed = jnp.where(inner, total_ref[...], final_ref[...])
    hidden = hidden_ref[...]
    rms = lax.rsqrt(jnp.mean(hidden * hidden, -1, keepdims=True) + norm_eps)
    scaled = dnormed * gain_ref[...]
    shift = jnp.mean(scaled * hidden, -1, keepdims=True)
    dhid = dout_ref[...].astype(jnp.float32) + (rms * scaled - hidden * (rms**3 * shift))
    return dhid, dnormed * (hidden * rms)


def hidden_grad_kernel(level_ref, total_ref, final_ref, hidden_ref, dout_ref, gain_ref, out_ref):
    inner = (level_ref[0] == 1) | (level_ref[0] == 2)
    dhid, _ = hidden_grad(inner, total_ref, final_ref, hidden_ref, dout_ref, gain_ref)
    out_ref[...] = dhid.astype(jnp.bfloat16).T


def hidden_grad_t(level, sums_two, hidden, dout, gain, index):
    rows, depth = hidden.shape
    gain = gain[None, :]
    return pl.pallas_call(
        hidden_grad_kernel,
        out_shape=jax.ShapeDtypeStruct((depth, rows), jnp.bfloat16),
        grid=(1,),
        in_specs=[SCALAR, whole(hidden), whole(hidden), whole(hidden)]
        + [pl.BlockSpec((rows, depth), lambda i: (index, 0)), whole(gain)],
        out_specs=pl.BlockSpec((depth, rows), lambda i: (0, 0)),
        compiler_params=params(),
        cost_estimate=cost(20 * rows * depth, 16 * rows * depth),
    )(level, *sums_two, hidden, dout, gain)


def backward_kernel(start, level_ref, total_ref, final_ref, hidden_ref, dout_ref, x_ref, *refs):
    gain_one_ref, gain_two_ref, wo_ref, w_ref, q_ref = refs[:5]
    kv_here = q_ref.shape[1] // KV_WIDE
    refs = refs[5:]
    kv_refs, refs = refs[: 2 * kv_here], refs[2 * kv_here :]
    part_ref, other_ref, across_ref, outer_ref, place_ref, strip_ref = refs[:6]
    cos_ref, sin_ref = refs[6:8]
    dhid_ref, low_ref, dn_ref = refs[-3:]
    outs = refs[8:-3]
    count = 5 if start > 0 else 4
    acc_ref = outs[0] if len(outs) > count else None
    outs = outs[-count:]
    dhid_t_ref, dqkv_ref, input_grad_ref, gains_ref = outs[:4]
    rows = q_ref.shape[0]
    keys = kv_refs[0].shape[0]
    shard = pl.program_id(0)
    level = level_ref[0]
    inner = (level == 1) | (level == 2)

    @pl.when(shard == 0)
    def _():
        dhid, dgain = hidden_grad(
            inner, total_ref, final_ref, hidden_ref, dout_ref, gain_two_ref
        )
        dhid_ref[...] = dhid
        low = dhid.astype(jnp.bfloat16)
        low_ref[...] = low
        dhid_t_ref[...] = low.T
        gains_ref[...] = jnp.zeros_like(gains_ref)
        gains_ref[1:2, :] = jnp.sum(dgain, 0, keepdims=True)
        dn_ref[...] = jnp.zeros_like(dn_ref)

    def rotate_back(grads):
        turned = grads * cos_ref[...] - pltpu.roll(grads, LANES // 2, 1) * sin_ref[...]
        return turned.astype(jnp.bfloat16)

    dmixed_all = dot32(low_ref[...], wo_ref[...]).astype(jnp.bfloat16)
    mixed = jnp.where(
        shard == 0,
        part_ref[...],
        jnp.where(shard == 1, other_ref[...], jnp.where(inner, across_ref[...], outer_ref[...])),
    )
    products = dmixed_all.astype(jnp.float32) * dot_split(mixed[:rows], place_ref[...])
    causal = lax.broadcasted_iota(jnp.int32, (rows, rows), 0) <= lax.broadcasted_iota(
        jnp.int32, (rows, rows), 1
    )
    grads = []
    for kv in range(kv_here):
        key_ref, value_ref = kv_refs[2 * kv : 2 * kv + 2]
        heads = range(kv * GROUP, (kv + 1) * GROUP)
        lanes = {h: slice(h * LANES, (h + 1) * LANES) for h in heads}
        row_dots = {h: jnp.sum(products[:, lanes[h]].T, axis=0, keepdims=True) for h in heads}
        log_sums = {h: mixed[rows + h : rows + h + 1, :rows] for h in heads}
        dqueries = dict.fromkeys(heads)
        here = slice(2 * kv * LANES, (2 * kv + 1) * LANES)
        there = slice((2 * kv + 1) * LANES, (2 * kv + 2) * LANES)
        for tile in range(keys // rows):
            span = slice(tile * rows, (tile + 1) * rows)
            key = key_ref[span, :]
            value = value_ref[span, :]
            key_t = key.T
            dkey = None if acc_ref is None else acc_ref[span, here]
            dvalue = None if acc_ref is None else acc_ref[span, there]
            last = tile * rows == start
            for h in heads:
                at = kv * KV_WIDE + (h % GROUP) * LANES
                query = q_ref[:, at : at + LANES]
                dmixed = dmixed_all[:, lanes[h]]
                raw = dot32_nt(key, query)
                probs = jnp.exp2(raw * score_scale_log2 - log_sums[h])
                if last:
                    probs = jnp.where(causal, probs, 0.0)
                dprobs = dot32_nt(value, dmixed)
                dscores = (probs * (dprobs - row_dots[h])).astype(jnp.bfloat16)
                dquery = dot32(key_t, dscores)
                dqueries[h] = dquery if dqueries[h] is None else dqueries[h] + dquery
                dkey_one = dot32(dscores, query)
                dvalue_one = dot32(probs.astype(jnp.bfloat16), dmixed)
                dkey = dkey_one if dkey is None else dkey + dkey_one
                dvalue = dvalue_one if dvalue is None else dvalue + dvalue_one
            if not last:
                outs[4][span, here] = dkey
                outs[4][span, there] = dvalue
        grads += [rotate_back(dqueries[h].T * score_scale) for h in heads]
        grads.append(rotate_back(dkey * score_scale))
        grads.append(dvalue.astype(jnp.bfloat16))
    grads = jnp.concatenate(grads, 1)
    dn_ref[...] += dot32_nt(grads, w_ref[...])

    @pl.when(shard == 0)
    def _():
        wide = strip_ref.shape[1]
        for kv in range(kv_here):
            dqkv_ref[:, kv * wide : (kv + 1) * wide] = dot32(
                grads[:, kv * KV_WIDE : (kv + 1) * KV_WIDE], strip_ref[...]
            ).astype(jnp.bfloat16)

    @pl.when(shard == pl.num_programs(0) - 1)
    def _():
        dnormed = dn_ref[...]
        inputs = x_ref[...].astype(jnp.float32)
        rms = lax.rsqrt(jnp.mean(inputs * inputs, -1, keepdims=True) + norm_eps)
        scaled = dnormed * gain_one_ref[...]
        shift = jnp.mean(scaled * inputs, -1, keepdims=True)
        grad = dhid_ref[...] + (rms * scaled - inputs * (rms**3 * shift))
        input_grad_ref[...] = grad.astype(jnp.bfloat16)
        gains_ref[0:1, :] = jnp.sum(dnormed * (inputs * rms), 0, keepdims=True)


def backward_chunk(
    level, sums_two, hidden, dout, tokens, gains, weights, qkv, gathered, places, tables, acc,
    index, rows
):
    start = index * rows
    keys = start + rows
    depth = tokens.shape[1]
    out_pad, qkv_pad = weights
    place_out, strip = places
    far_rows, width = gathered[0].shape
    out_wide = place_out.shape[1]
    kv_here = out_wide // (GROUP * LANES)
    wide = kv_here * KV_WIDE
    levels = qkv.shape[1] // wide
    own_rows = pl.BlockSpec((rows, depth), lambda t: (index, 0))
    table = pl.BlockSpec((rows, LANES), lambda t: (index, 0))
    gains = [gain[None, :] for gain in gains]
    key_value = lambda at: pl.BlockSpec(
        (keys, LANES), lambda t: (0, (wide // LANES) * t + at)
    )
    across = pl.BlockSpec((far_rows, width), lambda t: (0, jnp.where(t == 2, 1, 0)))
    outer = pl.BlockSpec((far_rows, width), lambda t: (0, jnp.where(t == 3, 1, 0)))
    in_specs = [
        SCALAR,
        whole(sums_two[0]),
        whole(sums_two[1]),
        whole(hidden),
        own_rows,
        own_rows,
        whole(gains[0]),
        whole(gains[1]),
        pl.BlockSpec((depth, out_wide), lambda t: (0, t)),
        pl.BlockSpec((depth, wide), lambda t: (0, t)),
        pl.BlockSpec((rows, wide), lambda t: (index, t)),
    ]
    for kv in range(kv_here):
        at = kv * (KV_WIDE // LANES) + GROUP
        in_specs += [key_value(at), key_value(at + 1)]
    in_specs += [
        whole(gathered[0]),
        whole(gathered[1]),
        across,
        outer,
        whole(place_out),
        whole(strip),
        table,
        table,
    ]
    args = [level, *sums_two, hidden, dout, tokens, *gains, out_pad, qkv_pad]
    args += [qkv] * (1 + 2 * kv_here)
    args += [*gathered, place_out, strip, *tables]
    sums_wide = 2 * kv_here * LANES
    if acc is not None:
        in_specs.append(pl.BlockSpec((keys, sums_wide), lambda t: (0, t)))
        args.append(acc)
    f32, bf16 = jnp.float32, jnp.bfloat16
    outs = [
        jax.ShapeDtypeStruct((depth, rows), bf16),
        jax.ShapeDtypeStruct((rows, kv_here * strip.shape[1]), bf16),
        jax.ShapeDtypeStruct((rows, depth), bf16),
        jax.ShapeDtypeStruct((8, depth), f32),
    ]
    out_specs = [whole(out) for out in outs]
    if start > 0:
        outs.append(jax.ShapeDtypeStruct((start, levels * sums_wide), f32))
        out_specs.append(pl.BlockSpec((start, sums_wide), lambda t: (0, t)))
    results = pl.pallas_call(
        functools.partial(backward_kernel, start),
        out_shape=outs,
        grid=(levels,),
        in_specs=in_specs,
        out_specs=out_specs,
        scratch_shapes=[
            pltpu.VMEM((rows, depth), f32),
            pltpu.VMEM((rows, depth), bf16),
            pltpu.VMEM((rows, depth), f32),
        ],
        compiler_params=params(),
        cost_estimate=cost(
            levels * rows * (20 * kv_here * keys * LANES + 2 * depth * (out_wide + wide)),
            2 * depth * levels * (out_wide + wide) + 16 * rows * depth,
            levels * kv_here * GROUP * rows * keys,
        ),
    )(*args)
    return results[:4], (results[4] if start > 0 else None)


def rows_kernel(lefts, groups, extras, adding, apart, side_ref, *refs):
    refs = list(refs)
    held_ref = refs.pop()
    out_refs = refs[-apart:]
    refs = refs[:-apart]
    recv_ref = refs.pop() if adding else None
    step = pl.program_id(0)
    left_refs = []
    for count in lefts:
        left_refs.append(refs[:count])
        refs = refs[count:]
    rights = []
    for _ in groups:
        rights.append(refs[:CHUNKS])
        refs = refs[CHUNKS:]
    rows = left_refs[0][0].shape[0]
    blocks = held_ref.shape[1] // rows

    @pl.when(step == 0)
    def _():
        for which, pieces in enumerate(left_refs):
            for n, ref in enumerate(pieces):
                m, j = n % blocks, n // blocks
                wide = ref.shape[1]
                held_ref[which, m * rows : (m + 1) * rows, j * wide : (j + 1) * wide] = ref[...]

    chunk = held_ref.shape[2] // CHUNKS
    right = None
    which = 0
    for group, (left, first, _) in zip(rights, groups):
        one = jnp.concatenate([ref[:chunk, :].astype(jnp.bfloat16) for ref in group], 0)
        right = one if right is None else jnp.where(step >= first, one, right)
        which = jnp.where(step >= first, left, which)
    total = dot32(held_ref[which], right)
    width = total.shape[1]
    held = total.shape[0] // apart
    if recv_ref is not None:
        total = total + recv_ref[:, :width]
    for n, out_ref in enumerate(out_refs):
        out_ref[:, :width] = total[n * held : (n + 1) * held]
    for m in range(extras):
        more = refs[m][...]
        if recv_ref is not None:
            more = more + recv_ref[m * rows : (m + 1) * rows, width:]
        at = m * rows % held
        out_refs[m * rows // held][at : at + rows, width:] = more


def rows_of(lefts, groups, side, rows, blocks, step, extra=None, recv=None, apart=1):
    at = lambda m: lambda i, side: ((m ^ side[2]) * side[1] + side[0], 0)
    specs = []
    args = []
    counts = []
    for left in lefts:
        pieces = left if isinstance(left, list) else [left]
        counts.append(len(pieces) * blocks)
        for piece in pieces:
            for m in range(blocks):
                specs.append(pl.BlockSpec((rows, piece.shape[1]), at(m)))
                args.append(piece)
    tokens = sum(piece.shape[1] for piece in pieces)
    first = 0
    plan = []
    for which, rights in groups:
        steps = rights[0].shape[1] // step
        plan.append((which, first, steps))
        for right in rights:
            pick = lambda i, side, first=first, steps=steps: (0, jnp.clip(i - first, 0, steps - 1))
            specs.append(pl.BlockSpec((right.shape[0], step), pick))
            args.append(right)
        first += steps
    total = first * step
    if extra is not None:
        for m in range(blocks):
            specs.append(pl.BlockSpec((rows, extra.shape[1]), at(m)))
            args.append(extra)
        total += extra.shape[1]
        step += extra.shape[1]
    block = lambda parts: pl.BlockSpec((rows * blocks // parts, step), lambda i, side: (0, i))
    if recv is not None:
        specs.append(block(1))
        args.append(recv)
    extras = 0 if extra is None else blocks
    results = pl.pallas_call(
        functools.partial(rows_kernel, counts, plan, extras, recv is not None, apart),
        out_shape=[jax.ShapeDtypeStruct((rows * blocks // apart, total), jnp.float32)] * apart,
        grid_spec=pltpu.PrefetchScalarGridSpec(
            num_scalar_prefetch=1,
            grid=(first,),
            in_specs=specs,
            out_specs=[block(apart)] * apart,
            scratch_shapes=[pltpu.VMEM((len(lefts), rows * blocks, tokens), jnp.bfloat16)],
        ),
        compiler_params=params(),
        cost_estimate=cost(
            2 * rows * blocks * tokens * total,
            4 * rows * blocks * total + 2 * tokens * (total + rows * blocks),
        ),
    )(side, *args)
    return results[0] if apart == 1 else results


def shards(
    tokens,
    lengths,
    positions,
    cotangent,
    norm_gain,
    w_query,
    w_key,
    w_value,
    w_out,
    mlp_gain,
    w_gate,
    w_up,
    w_down,
):
    seq_rows, depth = tokens.shape
    chips = lax.axis_size("chip")
    dp = chips * 2
    tp = lax.axis_size("tp")
    chip = lax.axis_index("chip")
    core = lax.axis_index("core")
    level = lax.axis_index("tp")
    low = level < 2
    inner = (level == 1) | (level == 2)
    heads_here = w_query.shape[1] // HD
    kv_here = w_key.shape[1] // HD
    rows = seq_rows // CHUNKS
    slice_rows = depth // dp
    level_ref = level.astype(jnp.int32).reshape(1)
    by_hand = dp == 8
    swap = lambda array: lax.ppermute(array, "core", [(0, 1), (1, 0)])
    to_level = lambda array, s: along(array, [(t, t ^ s) for t in range(tp)])

    at_row = (chip * 2 + core) * slice_rows
    cols = lambda w: lax.dynamic_slice_in_dim(w, at_row, slice_rows, 1).astype(jnp.float32).T
    (out_slice,) = fence(cols(w_out))
    qkv_slice = jnp.concatenate(
        [
            lax.dynamic_slice_in_dim(w_query, at_row, slice_rows, 0).astype(jnp.float32),
            cols(w_key.T),
            cols(w_value.T),
        ],
        1,
    )
    out_slice, qkv_slice = fence(out_slice, qkv_slice)
    if by_hand:
        out_far = [to_level(out_slice, s) for s in (1, 2, 3)]
        qkv_near = along(qkv_slice, PAIRS)
    meta = jnp.stack([chip, core]).astype(jnp.int32)

    pq = place_query(heads_here)
    pkv = place_key_value(kv_here)
    p_all = place_all(heads_here, kv_here)
    strip_one = place_all(GROUP, 1).T
    p_out = place_plain(heads_here)
    strip_out = p_out.T

    half_dim = HD // 2
    freqs = rope_base ** (-(jnp.arange(half_dim).astype(jnp.float32) * 2.0 / HD))
    freqs = jnp.pad(freqs, (0, LANES // 2 - half_dim))
    angles = positions.astype(jnp.float32)[:, None] * jnp.concatenate([freqs, freqs])[None, :]
    cosines = jnp.cos(angles)
    sines = jnp.sin(angles) * jnp.where(jnp.arange(LANES) < LANES // 2, -1.0, 1.0)

    qkv_own, normed_one, own_pad = start(
        tokens, norm_gain, w_query, w_key.T, w_value.T, pq, pkv, cosines, sines
    )

    order = list(reversed(range(CHUNKS)))
    c0, c1, c2, c3 = order
    own, other, across, outer = {}, {}, {}, {}
    part, total, final = {}, {}, {}

    def hop_1(j):
        other[j] = along(own[j], PAIRS)

    def hop_2(j):
        across[j] = along(jnp.concatenate([own[j], other[j]], 1), MIDDLE)

    def hop_3(j):
        outer[j] = along(across[j], OUTWARD)

    coming = {}

    def add_1(j):
        coming[j] = along(part[j], INWARD)

    def add_2(j):
        total[j] = part[j] + coming[j]
        coming[j] = along(total[j], MIDDLE)

    def add_3(j):
        total[j] = total[j] + coming[j]
        final[j] = along(total[j], OUTWARD)

    def to_chip(array, m):
        return lax.ppermute(array, "chip", [(i, i ^ m) for i in range(chips)])

    def over_chips_1(piece):
        cut = piece.shape[1] // 2
        one, two = piece[:, :cut], piece[:, cut:]
        return jnp.stack([one, to_chip(one, 1)]), jnp.stack([two, to_chip(two, 2)])

    def over_chips_2(one, two):
        return one, to_chip(one, 2), two, to_chip(two, 1)

    def over_chips_3(one, one_far, two, two_far):
        upper = jnp.stack([one[0], one[1], one_far[0], one_far[1]])
        lower = jnp.stack([two[0], two_far[0], two[1], two_far[1]])
        return jnp.concatenate([upper, lower], 2)

    if by_hand:
        qkv_own, qkv_near, out_far = fence(qkv_own, qkv_near, out_far)
        out_mine = over_chips_1(jnp.stack(out_far))
        qkv_across = along(jnp.stack([qkv_slice, qkv_near]), MIDDLE)
    else:
        gathered_out = lax.all_gather(out_slice, ("chip", "core", "tp"))
        gathered_qkv = lax.all_gather(qkv_slice, ("chip", "core", "tp"))
    own[c0] = attend(lengths, qkv_own, strip_out, c0, rows)
    if by_hand:
        own, qkv_own, out_mine = fence(own, qkv_own, out_mine)
        out_mine = over_chips_2(*out_mine)
    else:
        own, qkv_own = fence(own, qkv_own)
    hop_1(c0)
    for j in (c1, c2, c3):
        own[j] = attend(lengths, qkv_own, strip_out, j, rows)
    chain = (qkv_across, out_mine) if by_hand else ()
    own, other, normed_one, w_out, chain = fence(own, other, normed_one, w_out, chain)
    if by_hand:
        qkv_across, out_mine = chain
        out_mine = over_chips_3(*out_mine)
        out_theirs = swap(out_mine)
    hop_2(c0)
    hop_1(c1)
    dout, dout_t, normed_one_t = turn(lengths, cotangent, normed_one)
    w_out_t = w_out.T
    own, other, across, dout, dout_t, normed_one_t, w_out_t = fence(
        own, other, across, dout, dout_t, normed_one_t, w_out_t
    )
    hop_3(c0)
    hop_2(c1)
    hop_1(c2)
    if by_hand:
        out_mine, out_theirs, _ = fence(out_mine, out_theirs, w_out_t)
        out_pad, out_plain = spread(
            spread_out_kernel,
            meta,
            w_out_t,
            [p_out],
            out_mine,
            out_theirs,
            [4 * p_out.shape[1], 4 * p_out.shape[0]],
        )
    else:
        by_shard = lambda g, s: lax.dynamic_index_in_dim(
            g.reshape(dp, tp, slice_rows, -1), level ^ s, 1, False
        ).reshape(depth, -1)
        plain = [fence(by_shard(gathered_out, s))[0].astype(jnp.bfloat16) for s in range(4)]
        out_plain = jnp.concatenate(plain, 1)
        out_pad = jnp.concatenate([dot32(w, p_out).astype(jnp.bfloat16) for w in plain], 1)
    hidden, normed_t, activ, dgate, dup, mlp_part = {}, {}, {}, {}, {}, {}

    def feed(j):
        gathered = (own[j], other[j], across[j], outer[j])
        (hidden[j], normed_t[j], activ[j], dgate[j], dup[j], mlp_part[j], part[j]) = forward_chunk(
            level_ref, gathered, tokens, dout, out_plain, mlp_gain, w_gate, w_up, w_down, j, rows
        )

    feed(c0)
    own, other, across, outer, part, hidden = fence(own, other, across, outer, part, hidden)
    add_1(c0)
    hop_3(c1)
    hop_2(c2)
    hop_1(c3)
    feed(c1)
    own, other, across, outer, part, total, coming, hidden = fence(
        own, other, across, outer, part, total, coming, hidden
    )
    add_2(c0)
    add_1(c1)
    hop_3(c2)
    hop_2(c3)
    if by_hand:
        qkv_across, outer = fence(qkv_across, outer)
        qkv_outer = along(qkv_across, OUTWARD)
    feed(c2)
    far_slices = (qkv_outer, qkv_near, qkv_across) if by_hand else ()
    own, other, across, outer, part, total, coming, hidden, far_slices = fence(
        own, other, across, outer, part, total, coming, hidden, far_slices
    )
    add_3(c0)
    add_2(c1)
    hop_3(c3)
    if by_hand:
        qkv_outer, qkv_near, qkv_across = far_slices
        qkv_far = [
            qkv_near,
            jnp.where(inner, qkv_across[1], qkv_outer[0]),
            jnp.where(inner, qkv_across[0], qkv_outer[1]),
        ]
        qkv_mine = over_chips_1(jnp.stack(qkv_far))
    feed(c3)

    listed = lambda pieces: [pieces[j] for j in range(CHUNKS)]
    keep_side = jnp.stack([core, 2, 0]).astype(jnp.int32)
    keep_turned = jnp.stack([core, 2, chip]).astype(jnp.int32)
    send_side = jnp.stack([1 - core, 2, 0]).astype(jnp.int32)
    send_turned = jnp.stack([1 - core, 2, chip]).astype(jnp.int32)
    all_rows = jnp.array([0, 1, 0], jnp.int32)

    def send_rows(lefts, groups, step, extra=None, side=send_side):
        if not by_hand:
            return rows_of(lefts, groups, all_rows, depth // 4, 4, step, extra)
        return rows_of(lefts, groups, side, slice_rows, chips, step, extra)

    def keep_rows(lefts, groups, received, step, extra=None, side=keep_side, apart=1):
        if not by_hand:
            return received
        return rows_of(
            lefts, groups, side, slice_rows, chips, step, extra, received, apart
        )

    def swap_rows(array):
        return swap(array) if by_hand else array

    def scatter(array):
        axes = "chip" if by_hand else ("chip", "core")
        return lax.psum_scatter(array, axes, scatter_dimension=0, tiled=True)

    units = w_gate.shape[1]
    mlp_args = (
        [listed(normed_t), dout_t],
        [(0, listed(dgate)), (0, listed(dup)), (1, listed(activ))],
    )
    acc = None
    dhid_t, dqkv_own, input_grad, gains = {}, {}, {}, {}

    def back(j):
        nonlocal acc
        (dhid_t[j], dqkv_own[j], input_grad[j], gains[j]), acc = backward_chunk(
            level_ref,
            (total[j], final[j]),
            hidden[j],
            dout,
            tokens,
            (norm_gain, mlp_gain),
            (out_pad, qkv_pad),
            qkv,
            (own[j], other[j], across[j], outer[j]),
            (p_out, strip_one),
            (cosines, sines),
            acc,
            j,
            rows,
        )

    if not by_hand:
        qkv_mine = ()
    own, other, across, outer, part, total, coming, final, hidden, mlp_in, qkv_mine = fence(
        own, other, across, outer, part, total, coming, final, hidden,
        (normed_t, activ, dgate, dup), qkv_mine,
    )
    normed_t, activ, dgate, dup = mlp_in
    add_3(c1)
    add_1(c2)
    if by_hand:
        qkv_mine = over_chips_2(*qkv_mine)
    units = w_gate.shape[1]
    mlp_args = (
        [listed(normed_t), dout_t],
        [(0, listed(dgate)), (0, listed(dup)), (1, listed(activ))],
    )
    sent = send_rows(*mlp_args, units // 2)
    part, total, coming, final, hidden, mlp_part, sent, qkv_mine = fence(
        part, total, coming, final, hidden, mlp_part, sent, qkv_mine
    )
    sent = swap_rows(sent)
    add_2(c2)
    add_1(c3)
    if by_hand:
        qkv_mine = over_chips_3(*qkv_mine)
        qkv_theirs = swap(qkv_mine)
        (qkv_pad,) = spread(
            spread_qkv_kernel,
            meta,
            own_pad,
            [pq, pkv],
            qkv_mine,
            qkv_theirs,
            [4 * own_pad.shape[1]],
        )
    else:
        plain = [
            fence(by_shard(gathered_qkv, s))[0].astype(jnp.bfloat16) for s in range(4)
        ]
        qkv_pad = jnp.concatenate([dot32(w, p_all).astype(jnp.bfloat16) for w in plain], 1)
    qkv = project(normed_one, qkv_pad, cosines, sines)

    near = lambda: jnp.where(low, mlp_part[1], mlp_part[2])
    edge = lambda: jnp.where(low, mlp_part[0], mlp_part[3])
    back(c0)
    total, coming, final, hidden, mlp_part, acc, dhid_t, sent = fence(
        total, coming, final, hidden, mlp_part, acc, dhid_t, sent
    )
    add_3(c2)
    add_2(c3)
    leave_far = jnp.where(low, mlp_part[3], mlp_part[0])
    leave_near = jnp.where(low, mlp_part[2], mlp_part[1])
    far_sum = along(leave_far, INWARD)
    grad_mlp = keep_rows(*mlp_args, sent, units // 2)
    hidden, grad_mlp = fence(hidden, grad_mlp)
    grad_mlp = scatter(grad_mlp)
    back(c1)
    total, coming, final, hidden, mlp_part, far_sum, acc, dhid_t = fence(
        total, coming, final, hidden, mlp_part, far_sum, acc, dhid_t
    )
    add_3(c3)
    near_sum = along(leave_near, INWARD)
    far_in = along(leave_far + far_sum, MIDDLE)
    back(c2)
    total, final, hidden, mlp_part, near_sum, far_in, acc, dhid_t = fence(
        total, final, hidden, mlp_part, near_sum, far_in, acc, dhid_t
    )
    near_in = along(leave_near + near_sum, MIDDLE)
    last = along(jnp.where(inner, edge() + far_in, near()), PAIRS)
    last_hidden_t = hidden_grad_t(
        level_ref, (total[c3], final[c3]), hidden[c3], dout, mlp_gain, c3
    )
    q_cols = heads_here * HD
    out_args = (
        [[last_hidden_t if j == c3 else dhid_t[j] for j in range(CHUNKS)]],
        [(0, listed(own))],
    )
    sent = swap_rows(send_rows(*out_args, q_cols))
    sent, hidden, grad_mlp = fence(sent, hidden, grad_mlp)
    grad_out, hidden = fence(keep_rows(*out_args, sent, q_cols), hidden)
    grad_out = scatter(grad_out)
    back(c3)
    dqkv_own, gains, last, near_in = fence(dqkv_own, gains, last, near_in)
    gain_sums = gains[0] + gains[1] + gains[2] + gains[3]
    extra = jnp.pad(gain_sums.T, ((0, 0), (0, LANES - 8)))
    qkv_args = ([normed_one_t], [(0, listed(dqkv_own))])
    qkv_wide = 2 * q_cols
    send_qkv = swap_rows(send_rows(*qkv_args, qkv_wide, extra, send_turned))
    if by_hand:
        pieces = keep_rows(*qkv_args, send_qkv, qkv_wide, extra, keep_turned, chips)
        grad_qkv = pieces[0]
        for m in range(1, chips):
            grad_qkv = grad_qkv + to_chip(pieces[m], m)
    else:
        grad_qkv = scatter(send_qkv)
    mlp_rows = jnp.where(inner, near() + near_in, edge()) + last
    hidden_rows = jnp.where(
        low,
        jnp.where(level == 0, hidden[0], hidden[1]),
        jnp.where(level == 2, hidden[2], hidden[3]),
    )
    layer_out = (hidden_rows + mlp_rows).astype(jnp.bfloat16)
    one = strip_one.shape[1]
    picked = lambda at, width: jnp.concatenate(
        [grad_qkv[:, kv * one + at : kv * one + at + width] for kv in range(kv_here)], 1
    )
    return (
        layer_out,
        jnp.concatenate(listed(input_grad), 0),
        grad_qkv[:, qkv_wide],
        picked(0, GROUP * HD),
        picked(GROUP * HD, HD),
        picked((GROUP + 1) * HD, HD),
        grad_out.T,
        grad_qkv[:, qkv_wide + 1],
        grad_mlp[:, :units],
        grad_mlp[:, units : 2 * units],
        grad_mlp[:, 2 * units :].T,
    )


def solution(mesh):
    devices = mesh.devices
    dp, tp = devices.shape
    split = Mesh(devices.reshape(dp // 2, 2, tp), ("chip", "core", "tp"))
    data = ("chip", "core")
    return jax.shard_map(
        shards,
        mesh=split,
        in_specs=(
            P(data, None),
            P(data),
            P(data),
            P(data, None),
            P(),
            P(None, "tp"),
            P(None, "tp"),
            P(None, "tp"),
            P("tp", None),
            P(),
            P(None, "tp"),
            P(None, "tp"),
            P("tp", None),
        ),
        out_specs=(
            P(("chip", "core", "tp"), None),
            P(data, None),
            P(data),
            P(data, "tp"),
            P(data, "tp"),
            P(data, "tp"),
            P("tp", data),
            P(data),
            P(data, "tp"),
            P(data, "tp"),
            P("tp", data),
        ),
        check_vma=False,
    )
```

```python
import functools

import jax
import jax.numpy as jnp
from jax import lax
from jax.experimental import pallas as pl
from jax.experimental.pallas import tpu as pltpu
from jax.sharding import Mesh
from jax.sharding import PartitionSpec as P

HD = 96
LANES = 128
GROUP = 2
KV_WIDE = (GROUP + 2) * LANES
rope_base = 100000.0
norm_eps = 1e-05
masked_score = -1e30
far_away = 1e30
score_scale = HD ** (-0.5)
score_scale_log2 = score_scale * 1.4426950408889634
CHUNKS = 4
EXTRA = 8
VMEM_BYTES = 56 * 1024 * 1024
NT = (((1,), (1,)), ((), ()))


def params():
    return pltpu.CompilerParams(vmem_limit_bytes=VMEM_BYTES)


def cost(flops, moved, exps=0):
    return pl.CostEstimate(
        flops=flops // 1024, bytes_accessed=moved // 1024, transcendentals=exps // 1024
    )


def dot32(a, b):
    return jnp.dot(a, b, preferred_element_type=jnp.float32)


def dot32_nt(a, b):
    return lax.dot_general(a, b, NT, preferred_element_type=jnp.float32)


def dot_split(a, places):
    high = a.astype(jnp.bfloat16)
    rest = (a - high.astype(jnp.float32)).astype(jnp.bfloat16)
    return dot32(high, places) + dot32(rest, places)


def fence(*trees):
    return lax.optimization_barrier(trees)


def whole(array, buffers=None):
    zeros = (0,) * len(array.shape)
    return pl.BlockSpec(array.shape, lambda *_: zeros)


SCALAR = pl.BlockSpec(memory_space=pltpu.SMEM)


def halves(entry):
    half_dim = HD // 2
    return (entry // half_dim) * (LANES // 2) + entry % half_dim


def placement(lanes, width):
    return (lanes[:, None] == jnp.arange(width)[None, :]).astype(jnp.bfloat16)


def place_query(heads):
    source = jnp.arange(heads * HD)
    return placement((source // HD) * LANES + halves(source % HD), heads * LANES)


def place_key_value(kv_heads):
    source = jnp.arange(kv_heads * HD)
    head = source // HD
    keys = head * 2 * LANES + halves(source % HD)
    values = head * 2 * LANES + LANES + source % HD
    return placement(jnp.concatenate([keys, values]), kv_heads * 2 * LANES)


def place_all(heads, kv_heads):
    source = jnp.arange(heads * HD)
    head = source // HD
    query = (head // GROUP) * KV_WIDE + (head % GROUP) * LANES + halves(source % HD)
    source = jnp.arange(kv_heads * HD)
    base = (source // HD) * KV_WIDE + GROUP * LANES
    keys = base + halves(source % HD)
    values = base + LANES + source % HD
    return placement(jnp.concatenate([query, keys, values]), kv_heads * KV_WIDE)


def place_plain(heads):
    source = jnp.arange(heads * HD)
    return placement((source // HD) * LANES + source % HD, heads * LANES)


PAIRS = [(0, 1), (1, 0), (2, 3), (3, 2)]
INWARD = [(0, 1), (3, 2)]
MIDDLE = [(1, 2), (2, 1)]
OUTWARD = [(1, 0), (2, 3)]


def along(part, pairs):
    return lax.ppermute(part, "tp", pairs)


def store_qkv(out_ref, here, base, query, key_value):
    wide = GROUP * LANES
    for kv in range(key_value.shape[1] // (2 * LANES)):
        at = base + kv * KV_WIDE
        there = slice(kv * 2 * LANES, (kv + 1) * 2 * LANES)
        out_ref[here, at : at + wide] = query[:, kv * wide : (kv + 1) * wide]
        out_ref[here, at + wide : at + KV_WIDE] = key_value[:, there]


def store_turned(out_ref, at, lin, cos_ref, sin_ref):
    for h in range(GROUP + 2):
        one = lin[:, h * LANES : (h + 1) * LANES]
        if h < GROUP + 1:
            one = one * cos_ref[...] + pltpu.roll(one, LANES // 2, 1) * sin_ref[...]
        out_ref[:, at + h * LANES : at + (h + 1) * LANES] = one.astype(jnp.bfloat16)


def spread_out_kernel(meta_ref, own_ref, p_ref, mine_ref, theirs_ref, pad_ref, plain_ref):
    rows, width = mine_ref.shape[2:]
    wide = p_ref.shape[1]
    for side, ref in enumerate((mine_ref, theirs_ref)):
        here = pl.ds(pl.multiple_of((meta_ref[1] ^ side) * rows, rows), rows)
        for s in range(4):
            block = own_ref[here, :] if s == 0 else ref[0, s - 1].astype(jnp.bfloat16)
            plain_ref[here, s * width : (s + 1) * width] = block
            pad_ref[here, s * wide : (s + 1) * wide] = dot32(block, p_ref[...]).astype(
                jnp.bfloat16
            )


def spread_qkv_kernel(own_ref, pq_ref, pkv_ref, far_ref, out_ref):
    parts, others, rows, width = far_ref.shape
    wide = own_ref.shape[1]
    split = pq_ref.shape[0]
    out_ref[:, :wide] = own_ref[...]
    for s in range(others):
        block = far_ref[:, s].reshape(parts * rows, width).astype(jnp.bfloat16)
        query = dot32(block[:, :split], pq_ref[...]).astype(jnp.bfloat16)
        key_value = dot32(block[:, split:], pkv_ref[...]).astype(jnp.bfloat16)
        store_qkv(out_ref, slice(None), (s + 1) * wide, query, key_value)


def spread_qkv(own, pq, pkv, far):
    total, wide = own.shape
    dp, others, rows, width = far.shape
    parts = max(1, dp // 4)
    block = parts * rows
    return pl.pallas_call(
        spread_qkv_kernel,
        out_shape=jax.ShapeDtypeStruct((total, (others + 1) * wide), jnp.bfloat16),
        grid=(total // block,),
        in_specs=[
            pl.BlockSpec((block, wide), lambda i: (i, 0)),
            whole(pq),
            whole(pkv),
            pl.BlockSpec((parts, others, rows, width), lambda i: (i, 0, 0, 0)),
        ],
        out_specs=pl.BlockSpec((block, (others + 1) * wide), lambda i: (i, 0)),
        compiler_params=params(),
        cost_estimate=cost(8 * total * width * 512, 20 * total * wide),
    )(own, pq, pkv, far)


def spread(kernel, meta, own, places, mine, theirs, widths):
    chips, others, rows, width = mine.shape
    total = own.shape[0]
    row_block = lambda m, meta: (meta[0] ^ m, 0)
    piece = pl.BlockSpec((1, others, rows, width), lambda m, meta: (m, 0, 0, 0))
    return pl.pallas_call(
        kernel,
        out_shape=[jax.ShapeDtypeStruct((total, wide), jnp.bfloat16) for wide in widths],
        grid_spec=pltpu.PrefetchScalarGridSpec(
            num_scalar_prefetch=1,
            grid=(chips,),
            in_specs=[pl.BlockSpec((2 * rows, own.shape[1]), row_block)]
            + [whole(place) for place in places]
            + [piece, piece],
            out_specs=[pl.BlockSpec((2 * rows, wide), row_block) for wide in widths],
        ),
        compiler_params=params(),
        cost_estimate=cost(
            8 * total * width * 512, total * (12 * width + 2 * sum(widths))
        ),
    )(meta, own, *places, mine, theirs)


def start_kernel(x_ref, gain_ref, q_ref, k_ref, v_ref, pq_ref, pkv_ref, cos_ref, sin_ref, *outs):
    qkv_ref, normed_ref, pad_ref = outs

    @pl.when(pl.program_id(0) == 0)
    def _():
        split = k_ref.shape[0]
        query = dot32(q_ref[...], pq_ref[...]).astype(jnp.bfloat16)
        key_value = dot32(k_ref[...].T, pkv_ref[:split, :])
        key_value = key_value + dot32(v_ref[...].T, pkv_ref[split:, :])
        store_qkv(pad_ref, slice(None), 0, query, key_value.astype(jnp.bfloat16))

    inputs = x_ref[...].astype(jnp.float32)
    rms = lax.rsqrt(jnp.mean(inputs * inputs, -1, keepdims=True) + norm_eps)
    normed = (inputs * rms * gain_ref[...]).astype(jnp.bfloat16)
    normed_ref[...] = normed
    for kv in range(pad_ref.shape[1] // KV_WIDE):
        at = kv * KV_WIDE
        store_turned(qkv_ref, at, dot32(normed, pad_ref[:, at : at + KV_WIDE]), cos_ref, sin_ref)


def start(tokens, gain, w_query, w_key_t, w_value_t, pq, pkv, cosines, sines):
    total, depth = tokens.shape
    rows = total // CHUNKS
    wide = pq.shape[1] + pkv.shape[1]
    gain = gain[None, :]
    by_rows = lambda width: pl.BlockSpec((rows, width), lambda i: (i, 0))
    arrays = [w_query, w_key_t, w_value_t, pq, pkv]
    shapes = [
        jax.ShapeDtypeStruct((total, wide), jnp.bfloat16),
        jax.ShapeDtypeStruct((total, depth), jnp.bfloat16),
        jax.ShapeDtypeStruct((depth, wide), jnp.bfloat16),
    ]
    return pl.pallas_call(
        start_kernel,
        out_shape=shapes,
        grid=(CHUNKS,),
        in_specs=[by_rows(depth), whole(gain)]
        + [whole(array) for array in arrays]
        + [by_rows(LANES), by_rows(LANES)],
        out_specs=[by_rows(wide), by_rows(depth), whole(shapes[2])],
        compiler_params=params(),
        cost_estimate=cost(2 * total * depth * wide, 12 * total * depth),
    )(tokens, gain, *arrays, cosines, sines)


def turn_kernel(length_ref, cot_ref, normed_ref, dout_ref, dout_t_ref, normed_t_ref):
    rows = cot_ref.shape[0]
    at = pl.program_id(0) * rows + lax.broadcasted_iota(jnp.int32, cot_ref.shape, 0)
    dout = jnp.where(at < length_ref[0], cot_ref[...].astype(jnp.float32), 0.0)
    dout = dout.astype(jnp.bfloat16)
    dout_ref[...] = dout
    dout_t_ref[...] = dout.T
    normed_t_ref[...] = normed_ref[...].T


def turn(length, cotangent, normed):
    total, depth = cotangent.shape
    rows = total // CHUNKS
    by_rows = pl.BlockSpec((rows, depth), lambda i: (i, 0))
    by_columns = pl.BlockSpec((depth, rows), lambda i: (0, i))
    turned = jax.ShapeDtypeStruct((depth, total), jnp.bfloat16)
    return pl.pallas_call(
        turn_kernel,
        out_shape=[jax.ShapeDtypeStruct((total, depth), jnp.bfloat16), turned, turned],
        grid=(CHUNKS,),
        in_specs=[SCALAR, by_rows, by_rows],
        out_specs=[by_rows, by_columns, by_columns],
        compiler_params=params(),
        cost_estimate=cost(total * depth, 10 * total * depth),
    )(length, cotangent, normed)


def project_kernel(x_ref, w_ref, cos_ref, sin_ref, out_ref):
    store_turned(out_ref, 0, dot32(x_ref[...], w_ref[...]), cos_ref, sin_ref)


def project(normed, weights, cosines, sines):
    rows, depth = normed.shape
    width = weights.shape[1]
    return pl.pallas_call(
        project_kernel,
        out_shape=jax.ShapeDtypeStruct((rows, width), jnp.bfloat16),
        grid=(width // KV_WIDE,),
        in_specs=[
            whole(normed),
            pl.BlockSpec((depth, KV_WIDE), lambda i: (0, i)),
            whole(cosines),
            whole(sines),
        ],
        out_specs=pl.BlockSpec((rows, KV_WIDE), lambda i: (0, i)),
        compiler_params=params(),
        cost_estimate=cost(
            2 * rows * depth * width, 2 * (rows * depth + depth * width + rows * width)
        ),
    )(normed, weights, cosines, sines)


def attend_kernel(start, length_ref, q_ref, kv_ref, strip_ref, out_ref):
    rows = q_ref.shape[0]
    keys = kv_ref.shape[0]
    length = length_ref[0]
    row_ids = start + lax.broadcasted_iota(jnp.int32, (1, rows), 1)
    limit = jnp.minimum(row_ids, length - 1)
    allowed = lax.broadcasted_iota(jnp.int32, (keys, rows), 0) <= limit
    mixed = []
    sums = []
    for kv in range(kv_ref.shape[1] // KV_WIDE):
        base = kv * KV_WIDE
        at = base + GROUP * LANES
        key = kv_ref[:, at : at + LANES]
        value_t = kv_ref[:, at + LANES : at + 2 * LANES].T
        for g in range(GROUP):
            query = q_ref[:, base + g * LANES : base + (g + 1) * LANES]
            raw = jnp.where(allowed, dot32_nt(key, query), masked_score)
            peak = jnp.max(raw, axis=0, keepdims=True)
            expo = jnp.exp2((raw - peak) * score_scale_log2)
            total = jnp.sum(expo, axis=0, keepdims=True)
            probs = (expo * (1.0 / total)).astype(jnp.bfloat16)
            mixed.append(dot32(value_t, probs).T)
            log_sum = peak * score_scale_log2 + jnp.log2(total)
            sums.append(jnp.where(row_ids < length, log_sum, far_away))
    out_ref[:rows, :] = dot_split(jnp.concatenate(mixed, 1), strip_ref[...])
    out_ref[rows:, :] = jnp.zeros((EXTRA, out_ref.shape[1]), jnp.float32)
    out_ref[rows : rows + len(sums), :rows] = jnp.concatenate(sums, 0)


def attend(length, qkv, strip, index, rows):
    keys = (index + 1) * rows
    width = qkv.shape[1]
    heads = width // KV_WIDE * GROUP
    shape = (rows + EXTRA, strip.shape[1])
    return pl.pallas_call(
        functools.partial(attend_kernel, index * rows),
        out_shape=jax.ShapeDtypeStruct(shape, jnp.float32),
        grid=(1,),
        in_specs=[
            SCALAR,
            pl.BlockSpec((rows, width), lambda i: (index, 0)),
            pl.BlockSpec((keys, width), lambda i: (0, 0)),
            whole(strip),
        ],
        out_specs=pl.BlockSpec(shape, lambda i: (0, 0)),
        compiler_params=params(),
        cost_estimate=cost(
            4 * heads * rows * keys * LANES, 2 * (rows + keys) * width, heads * rows * keys
        ),
    )(length, qkv, qkv, strip)


def forward_kernel(level_ref, part_ref, other_ref, across_ref, outer_ref, *refs):
    x_ref, dout_ref, wo_ref, gain_ref, wg_ref, wu_ref, wd_ref = refs[:7]
    hidden_ref, normed_t_ref, activ_ref, dgate_ref, dup_ref, mlp_ref, dn_ref = refs[7:14]
    normed_ref = refs[14]
    rows = x_ref.shape[0]

    @pl.when(pl.program_id(0) == 0)
    def _():
        level = level_ref[0]
        inner = (level == 1) | (level == 2)
        width = part_ref.shape[1]
        second = jnp.where(inner, across_ref[:rows, width:], outer_ref[:rows, :width])
        third = jnp.where(inner, across_ref[:rows, :width], outer_ref[:rows, width:])
        mixed = jnp.concatenate([part_ref[:rows, :], other_ref[:rows, :], second, third], 1)
        hidden = x_ref[...].astype(jnp.float32) + dot32_nt(mixed.astype(jnp.bfloat16), wo_ref[...])
        hidden_ref[...] = hidden
        rms = lax.rsqrt(jnp.mean(hidden * hidden, -1, keepdims=True) + norm_eps)
        normed = (hidden * rms * gain_ref[...]).astype(jnp.bfloat16)
        normed_ref[...] = normed
        normed_t_ref[...] = normed.T
        mlp_ref[...] = jnp.zeros_like(mlp_ref)
        dn_ref[...] = jnp.zeros_like(dn_ref)

    normed = normed_ref[...]
    gate = dot32(normed, wg_ref[...])
    up = dot32(normed, wu_ref[...])
    dact = dot32_nt(dout_ref[...], wd_ref[...])
    sigmoid = jax.nn.sigmoid(gate)
    silu = gate * sigmoid
    activ = (silu * up).astype(jnp.bfloat16)
    dgate = (dact * up * sigmoid * (1.0 + gate * (1.0 - sigmoid))).astype(jnp.bfloat16)
    dup = (dact * silu).astype(jnp.bfloat16)
    activ_ref[...] = activ
    dgate_ref[...] = dgate
    dup_ref[...] = dup
    mlp_ref[...] += dot32(activ, wd_ref[...])
    dn_ref[...] += dot32_nt(dgate, wg_ref[...]) + dot32_nt(dup, wu_ref[...])


def forward_chunk(level, gathered, tokens, dout, w_out, gain, w_gate, w_up, w_down, index, rows):
    depth = tokens.shape[1]
    units = w_gate.shape[1]
    block = 512
    own_rows = pl.BlockSpec((rows, depth), lambda i: (index, 0))
    by_units = pl.BlockSpec((depth, block), lambda i: (0, i))
    gain = gain[None, :]
    f32, bf16 = jnp.float32, jnp.bfloat16
    outs = [
        jax.ShapeDtypeStruct((rows, depth), f32),
        jax.ShapeDtypeStruct((depth, rows), bf16),
        jax.ShapeDtypeStruct((rows, units), bf16),
        jax.ShapeDtypeStruct((rows, units), bf16),
        jax.ShapeDtypeStruct((rows, units), bf16),
        jax.ShapeDtypeStruct((rows, depth), f32),
        jax.ShapeDtypeStruct((rows, depth), f32),
    ]
    unit_out = pl.BlockSpec((rows, block), lambda i: (0, i))
    return pl.pallas_call(
        forward_kernel,
        out_shape=outs,
        grid=(units // block,),
        in_specs=[SCALAR]
        + [whole(array) for array in gathered]
        + [own_rows, own_rows, whole(w_out), whole(gain), by_units, by_units]
        + [pl.BlockSpec((block, depth), lambda i: (i, 0))],
        out_specs=[
            whole(outs[0]),
            whole(outs[1]),
            unit_out,
            unit_out,
            unit_out,
            whole(outs[5]),
            whole(outs[6]),
        ],
        scratch_shapes=[pltpu.VMEM((rows, depth), bf16)],
        compiler_params=params(),
        cost_estimate=cost(
            2 * rows * depth * (6 * units + w_out.shape[1]),
            2 * depth * (3 * units + w_out.shape[1]) + 22 * rows * depth,
            rows * units,
        ),
    )(level, *gathered, tokens, dout, w_out, gain, w_gate, w_up, w_down)


def hidden_grad(inner, total_ref, final_ref, hidden_ref, dout_ref, gain_ref):
    dnormed = jnp.where(inner, total_ref[...], final_ref[...])
    hidden = hidden_ref[...]
    rms = lax.rsqrt(jnp.mean(hidden * hidden, -1, keepdims=True) + norm_eps)
    scaled = dnormed * gain_ref[...]
    shift = jnp.mean(scaled * hidden, -1, keepdims=True)
    dhid = dout_ref[...].astype(jnp.float32) + (rms * scaled - hidden * (rms**3 * shift))
    return dhid, dnormed * (hidden * rms)


def backward_kernel(start, full, level_ref, total_ref, final_ref, hidden_ref, dout_ref, x_ref, *refs):
    gain_one_ref, gain_two_ref, wo_ref, q_ref = refs[:4]
    kv_here = q_ref.shape[1] // KV_WIDE
    refs = refs[4:]
    kv_refs, refs = refs[: 2 * kv_here], refs[2 * kv_here :]
    part_ref, other_ref, across_ref, outer_ref, place_ref, strip_ref = refs[:6]
    cos_ref, sin_ref = refs[6:8]
    dhid_ref, low_ref, dn_ref = refs[-3:]
    outs = refs[8:-3]
    if full:
        w_ref, outs = outs[0], outs[1:]
    count = (5 if start > 0 else 4) if full else 2
    acc_ref = outs[0] if len(outs) > count else None
    outs = outs[-count:]
    dhid_t_ref, dqkv_ref = outs[:2]
    if full:
        input_grad_ref, gains_ref = outs[2:4]
    rows = q_ref.shape[0]
    keys = kv_refs[0].shape[0]
    shard = pl.program_id(0)
    level = level_ref[0]
    inner = (level == 1) | (level == 2)

    @pl.when(shard == 0)
    def _():
        dhid, dgain = hidden_grad(
            inner, total_ref, final_ref, hidden_ref, dout_ref, gain_two_ref
        )
        dhid_ref[...] = dhid
        low = dhid.astype(jnp.bfloat16)
        low_ref[...] = low
        dhid_t_ref[...] = low.T
        if full:
            gains_ref[...] = jnp.zeros_like(gains_ref)
            gains_ref[1:2, :] = jnp.sum(dgain, 0, keepdims=True)
            dn_ref[...] = jnp.zeros_like(dn_ref)

    def rotate_back(grads):
        turned = grads * cos_ref[...] - pltpu.roll(grads, LANES // 2, 1) * sin_ref[...]
        return turned.astype(jnp.bfloat16)

    dmixed_all = dot32(low_ref[...], wo_ref[...]).astype(jnp.bfloat16)
    mixed = jnp.where(
        shard == 0,
        part_ref[...],
        jnp.where(shard == 1, other_ref[...], jnp.where(inner, across_ref[...], outer_ref[...])),
    )
    products = dmixed_all.astype(jnp.float32) * dot_split(mixed[:rows], place_ref[...])
    causal = lax.broadcasted_iota(jnp.int32, (rows, rows), 0) <= lax.broadcasted_iota(
        jnp.int32, (rows, rows), 1
    )
    grads = []
    for kv in range(kv_here):
        key_ref, value_ref = kv_refs[2 * kv : 2 * kv + 2]
        heads = range(kv * GROUP, (kv + 1) * GROUP)
        lanes = {h: slice(h * LANES, (h + 1) * LANES) for h in heads}
        row_dots = {h: jnp.sum(products[:, lanes[h]].T, axis=0, keepdims=True) for h in heads}
        log_sums = {h: mixed[rows + h : rows + h + 1, :rows] for h in heads}
        dqueries = dict.fromkeys(heads)
        here = slice(2 * kv * LANES, (2 * kv + 1) * LANES)
        there = slice((2 * kv + 1) * LANES, (2 * kv + 2) * LANES)
        for tile in range(keys // rows):
            span = slice(tile * rows, (tile + 1) * rows)
            key = key_ref[span, :]
            value = value_ref[span, :]
            key_t = key.T
            dkey = None if acc_ref is None else acc_ref[span, here]
            dvalue = None if acc_ref is None else acc_ref[span, there]
            last = tile * rows == start
            for h in heads:
                at = kv * KV_WIDE + (h % GROUP) * LANES
                query = q_ref[:, at : at + LANES]
                dmixed = dmixed_all[:, lanes[h]]
                raw = dot32_nt(key, query)
                probs = jnp.exp2(raw * score_scale_log2 - log_sums[h])
                if last:
                    probs = jnp.where(causal, probs, 0.0)
                dprobs = dot32_nt(value, dmixed)
                dscores = (probs * (dprobs - row_dots[h])).astype(jnp.bfloat16)
                dquery = dot32(key_t, dscores)
                dqueries[h] = dquery if dqueries[h] is None else dqueries[h] + dquery
                dkey_one = dot32(dscores, query)
                dvalue_one = dot32(probs.astype(jnp.bfloat16), dmixed)
                dkey = dkey_one if dkey is None else dkey + dkey_one
                dvalue = dvalue_one if dvalue is None else dvalue + dvalue_one
            if full and not last:
                outs[4][span, here] = dkey
                outs[4][span, there] = dvalue
        grads += [rotate_back(dqueries[h].T * score_scale) for h in heads]
        grads.append(rotate_back(dkey * score_scale))
        grads.append(dvalue.astype(jnp.bfloat16))
    grads = jnp.concatenate(grads, 1)
    if full:
        dn_ref[...] += dot32_nt(grads, w_ref[...])

    @pl.when(shard == 0)
    def _():
        wide = strip_ref.shape[1]
        for kv in range(kv_here):
            dqkv_ref[:, kv * wide : (kv + 1) * wide] = dot32(
                grads[:, kv * KV_WIDE : (kv + 1) * KV_WIDE], strip_ref[...]
            ).astype(jnp.bfloat16)

    if not full:
        return

    @pl.when(shard == pl.num_programs(0) - 1)
    def _():
        dnormed = dn_ref[...]
        inputs = x_ref[...].astype(jnp.float32)
        rms = lax.rsqrt(jnp.mean(inputs * inputs, -1, keepdims=True) + norm_eps)
        scaled = dnormed * gain_one_ref[...]
        shift = jnp.mean(scaled * inputs, -1, keepdims=True)
        grad = dhid_ref[...] + (rms * scaled - inputs * (rms**3 * shift))
        input_grad_ref[...] = grad.astype(jnp.bfloat16)
        gains_ref[0:1, :] = jnp.sum(dnormed * (inputs * rms), 0, keepdims=True)


def backward_chunk(
    level, sums_two, hidden, dout, tokens, gains, weights, qkv, gathered, places, tables, acc,
    index, rows, full=True
):
    start = index * rows
    keys = start + rows
    depth = tokens.shape[1]
    out_pad, qkv_pad = weights
    place_out, strip = places
    far_rows, width = gathered[0].shape
    out_wide = place_out.shape[1]
    kv_here = out_wide // (GROUP * LANES)
    wide = kv_here * KV_WIDE
    levels = qkv.shape[1] // wide
    own_rows = pl.BlockSpec((rows, depth), lambda t: (index, 0))
    table = pl.BlockSpec((rows, LANES), lambda t: (index, 0))
    gains = [gain[None, :] for gain in gains]
    key_value = lambda at: pl.BlockSpec(
        (keys, LANES), lambda t: (0, (wide // LANES) * t + at)
    )
    across = pl.BlockSpec((far_rows, width), lambda t: (0, jnp.where(t == 2, 1, 0)))
    outer = pl.BlockSpec((far_rows, width), lambda t: (0, jnp.where(t == 3, 1, 0)))
    in_specs = [
        SCALAR,
        whole(sums_two[0]),
        whole(sums_two[1]),
        whole(hidden),
        own_rows,
        own_rows,
        whole(gains[0]),
        whole(gains[1]),
        pl.BlockSpec((depth, out_wide), lambda t: (0, t)),
        pl.BlockSpec((rows, wide), lambda t: (index, t)),
    ]
    for kv in range(kv_here):
        at = kv * (KV_WIDE // LANES) + GROUP
        in_specs += [key_value(at), key_value(at + 1)]
    in_specs += [
        whole(gathered[0]),
        whole(gathered[1]),
        across,
        outer,
        whole(place_out),
        whole(strip),
        table,
        table,
    ]
    args = [level, *sums_two, hidden, dout, tokens, *gains, out_pad]
    args += [qkv] * (1 + 2 * kv_here)
    args += [*gathered, place_out, strip, *tables]
    sums_wide = 2 * kv_here * LANES
    if full:
        in_specs.append(pl.BlockSpec((depth, wide), lambda t: (0, t)))
        args.append(qkv_pad)
    if acc is not None:
        in_specs.append(pl.BlockSpec((keys, sums_wide), lambda t: (0, t)))
        args.append(acc)
    f32, bf16 = jnp.float32, jnp.bfloat16
    outs = [
        jax.ShapeDtypeStruct((depth, rows), bf16),
        jax.ShapeDtypeStruct((rows, kv_here * strip.shape[1]), bf16),
        jax.ShapeDtypeStruct((rows, depth), bf16),
        jax.ShapeDtypeStruct((8, depth), f32),
    ]
    outs = outs if full else outs[:2]
    out_specs = [whole(out) for out in outs]
    if full and start > 0:
        outs.append(jax.ShapeDtypeStruct((start, levels * sums_wide), f32))
        out_specs.append(pl.BlockSpec((start, sums_wide), lambda t: (0, t)))
    results = pl.pallas_call(
        functools.partial(backward_kernel, start, full),
        out_shape=outs,
        grid=(levels if full else 1,),
        in_specs=in_specs,
        out_specs=out_specs,
        scratch_shapes=[
            pltpu.VMEM((rows, depth), f32),
            pltpu.VMEM((rows, depth), bf16),
            pltpu.VMEM((rows, depth), f32),
        ],
        compiler_params=params(),
        cost_estimate=cost(
            levels * rows * (20 * kv_here * keys * LANES + 2 * depth * (out_wide + wide)),
            2 * depth * levels * (out_wide + wide) + 16 * rows * depth,
            levels * kv_here * GROUP * rows * keys,
        ),
    )(*args)
    return results[:4], (results[4] if full and start > 0 else None)


def rows_kernel(lefts, groups, extras, adding, apart, side_ref, *refs):
    refs = list(refs)
    held_ref = refs.pop()
    out_refs = refs[-apart:]
    refs = refs[:-apart]
    recv_ref = refs.pop() if adding else None
    step = pl.program_id(0)
    left_refs = []
    for count in lefts:
        left_refs.append(refs[:count])
        refs = refs[count:]
    rights = []
    for _ in groups:
        rights.append(refs[:CHUNKS])
        refs = refs[CHUNKS:]
    rows = left_refs[0][0].shape[0]
    blocks = held_ref.shape[1] // rows

    @pl.when(step == 0)
    def _():
        for which, pieces in enumerate(left_refs):
            for n, ref in enumerate(pieces):
                m, j = n % blocks, n // blocks
                wide = ref.shape[1]
                held_ref[which, m * rows : (m + 1) * rows, j * wide : (j + 1) * wide] = ref[...]

    chunk = held_ref.shape[2] // CHUNKS
    right = None
    which = 0
    for group, (left, first, _) in zip(rights, groups):
        one = jnp.concatenate([ref[:chunk, :].astype(jnp.bfloat16) for ref in group], 0)
        right = one if right is None else jnp.where(step >= first, one, right)
        which = jnp.where(step >= first, left, which)
    total = dot32(held_ref[which], right)
    width = total.shape[1]
    held = total.shape[0] // apart
    if recv_ref is not None:
        total = total + recv_ref[:, :width]
    for n, out_ref in enumerate(out_refs):
        out_ref[:, :width] = total[n * held : (n + 1) * held]
    for m in range(extras):
        more = refs[m][...]
        if recv_ref is not None:
            more = more + recv_ref[m * rows : (m + 1) * rows, width:]
        at = m * rows % held
        out_refs[m * rows // held][at : at + rows, width:] = more


def rows_of(lefts, groups, side, rows, blocks, step, extra=None, recv=None, apart=1):
    at = lambda m: lambda i, side: ((m ^ side[2]) * side[1] + side[0], 0)
    specs = []
    args = []
    counts = []
    for left in lefts:
        pieces = left if isinstance(left, list) else [left]
        counts.append(len(pieces) * blocks)
        for piece in pieces:
            for m in range(blocks):
                specs.append(pl.BlockSpec((rows, piece.shape[1]), at(m)))
                args.append(piece)
    tokens = sum(piece.shape[1] for piece in pieces)
    first = 0
    plan = []
    for which, rights in groups:
        steps = rights[0].shape[1] // step
        plan.append((which, first, steps))
        for right in rights:
            pick = lambda i, side, first=first, steps=steps: (0, jnp.clip(i - first, 0, steps - 1))
            specs.append(pl.BlockSpec((right.shape[0], step), pick))
            args.append(right)
        first += steps
    total = first * step
    if extra is not None:
        for m in range(blocks):
            specs.append(pl.BlockSpec((rows, extra.shape[1]), at(m)))
            args.append(extra)
        total += extra.shape[1]
        step += extra.shape[1]
    block = lambda parts: pl.BlockSpec((rows * blocks // parts, step), lambda i, side: (0, i))
    if recv is not None:
        specs.append(block(1))
        args.append(recv)
    extras = 0 if extra is None else blocks
    results = pl.pallas_call(
        functools.partial(rows_kernel, counts, plan, extras, recv is not None, apart),
        out_shape=[jax.ShapeDtypeStruct((rows * blocks // apart, total), jnp.float32)] * apart,
        grid_spec=pltpu.PrefetchScalarGridSpec(
            num_scalar_prefetch=1,
            grid=(first,),
            in_specs=specs,
            out_specs=[block(apart)] * apart,
            scratch_shapes=[pltpu.VMEM((len(lefts), rows * blocks, tokens), jnp.bfloat16)],
        ),
        compiler_params=params(),
        cost_estimate=cost(
            2 * rows * blocks * tokens * total,
            4 * rows * blocks * total + 2 * tokens * (total + rows * blocks),
        ),
    )(side, *args)
    return results[0] if apart == 1 else results


def shards(
    tokens,
    lengths,
    positions,
    cotangent,
    norm_gain,
    w_query,
    w_key,
    w_value,
    w_out,
    mlp_gain,
    w_gate,
    w_up,
    w_down,
):
    seq_rows, depth = tokens.shape
    chips = lax.axis_size("chip")
    dp = chips * 2
    tp = lax.axis_size("tp")
    chip = lax.axis_index("chip")
    core = lax.axis_index("core")
    level = lax.axis_index("tp")
    low = level < 2
    inner = (level == 1) | (level == 2)
    heads_here = w_query.shape[1] // HD
    kv_here = w_key.shape[1] // HD
    rows = seq_rows // CHUNKS
    slice_rows = depth // dp
    level_ref = level.astype(jnp.int32).reshape(1)
    by_hand = dp == 8
    swap = lambda array: lax.ppermute(array, "core", [(0, 1), (1, 0)])
    to_level = lambda array, s: along(array, [(t, t ^ s) for t in range(tp)])

    at_row = (chip * 2 + core) * slice_rows
    cols = lambda w: lax.dynamic_slice_in_dim(w, at_row, slice_rows, 1).astype(jnp.float32).T
    (out_slice,) = fence(cols(w_out))
    qkv_slice = jnp.concatenate(
        [
            lax.dynamic_slice_in_dim(w_query, at_row, slice_rows, 0).astype(jnp.float32),
            cols(w_key.T),
            cols(w_value.T),
        ],
        1,
    )
    out_slice, qkv_slice = fence(out_slice, qkv_slice)
    out_near = along(out_slice, PAIRS)
    qkv_near = along(qkv_slice, PAIRS)
    meta = jnp.stack([chip, core]).astype(jnp.int32)

    pq = place_query(heads_here)
    pkv = place_key_value(kv_here)
    p_all = place_all(heads_here, kv_here)
    strip_one = place_all(GROUP, 1).T
    p_out = place_plain(heads_here)
    strip_out = p_out.T

    half_dim = HD // 2
    freqs = rope_base ** (-(jnp.arange(half_dim).astype(jnp.float32) * 2.0 / HD))
    freqs = jnp.pad(freqs, (0, LANES // 2 - half_dim))
    angles = positions.astype(jnp.float32)[:, None] * jnp.concatenate([freqs, freqs])[None, :]
    cosines = jnp.cos(angles)
    sines = jnp.sin(angles) * jnp.where(jnp.arange(LANES) < LANES // 2, -1.0, 1.0)

    cosines, sines, out_near = fence(cosines, sines, out_near)
    out_across = along(jnp.stack([out_slice, out_near]), MIDDLE)
    qkv_own, normed_one, own_pad = start(
        tokens, norm_gain, w_query, w_key.T, w_value.T, pq, pkv, cosines, sines
    )

    def far_slices(near, across, outer):
        return jnp.stack(
            [
                near,
                jnp.where(inner, across[1], outer[0]),
                jnp.where(inner, across[0], outer[1]),
            ]
        )

    order = list(reversed(range(CHUNKS)))
    c0, c1, c2, c3 = order
    own, other, across, outer = {}, {}, {}, {}
    part, total, final = {}, {}, {}

    def hop_1(j):
        other[j] = along(own[j], PAIRS)

    def hop_2(j):
        across[j] = along(jnp.concatenate([own[j], other[j]], 1), MIDDLE)

    def hop_3(j):
        outer[j] = along(across[j], OUTWARD)

    coming = {}

    def add_1(j):
        coming[j] = along(part[j], INWARD)

    def add_2(j):
        total[j] = part[j] + coming[j]
        coming[j] = along(total[j], MIDDLE)

    def add_3(j):
        total[j] = total[j] + coming[j]
        final[j] = along(total[j], OUTWARD)

    def to_chip(array, m):
        return lax.ppermute(array, "chip", [(i, i ^ m) for i in range(chips)])

    def over_chips_1(piece):
        cut = piece.shape[1] // 2
        one, two = piece[:, :cut], piece[:, cut:]
        return jnp.stack([one, to_chip(one, 1)]), jnp.stack([two, to_chip(two, 2)])

    def over_chips_2(one, two):
        return one, to_chip(one, 2), two, to_chip(two, 1)

    def over_chips_3(one, one_far, two, two_far):
        upper = jnp.stack([one[0], one[1], one_far[0], one_far[1]])
        lower = jnp.stack([two[0], two_far[0], two[1], two_far[1]])
        return jnp.concatenate([upper, lower], 2)

    qkv_own, out_across, qkv_near = fence(qkv_own, out_across, qkv_near)
    out_outer = along(out_across, OUTWARD)
    qkv_across = along(jnp.stack([qkv_slice, qkv_near]), MIDDLE)
    own[c0] = attend(lengths, qkv_own, strip_out, c0, rows)
    own, qkv_own, out_outer = fence(own, qkv_own, out_outer)
    hop_1(c0)
    out_far = far_slices(out_near, out_across, out_outer)
    out_mine = over_chips_1(out_far) if by_hand else out_far
    for j in (c1, c2, c3):
        own[j] = attend(lengths, qkv_own, strip_out, j, rows)
    own, other, normed_one, w_out, out_mine, qkv_across = fence(
        own, other, normed_one, w_out, out_mine, qkv_across
    )
    if by_hand:
        out_mine = over_chips_2(*out_mine)
    else:
        out_mine = lax.all_gather(out_mine, ("chip", "core"))
    qkv_outer = along(qkv_across, OUTWARD)
    hop_2(c0)
    hop_1(c1)
    dout, dout_t, normed_one_t = turn(lengths, cotangent, normed_one)
    w_out_t = w_out.T
    own, other, across, dout, dout_t, normed_one_t, w_out_t, out_mine, qkv_outer = fence(
        own, other, across, dout, dout_t, normed_one_t, w_out_t, out_mine, qkv_outer
    )
    hop_3(c0)
    hop_2(c1)
    hop_1(c2)
    qkv_far = lax.all_gather(far_slices(qkv_near, qkv_across, qkv_outer), ("chip", "core"))
    if by_hand:
        out_mine = over_chips_3(*out_mine)
        out_theirs = swap(out_mine)
        out_pad, out_plain = spread(
            spread_out_kernel,
            meta,
            w_out_t,
            [p_out],
            out_mine,
            out_theirs,
            [4 * p_out.shape[1], 4 * p_out.shape[0]],
        )
    else:
        plain = [w_out_t] + [
            out_mine[:, s].reshape(depth, -1).astype(jnp.bfloat16) for s in range(tp - 1)
        ]
        out_plain = jnp.concatenate(plain, 1)
        out_pad = jnp.concatenate([dot32(w, p_out).astype(jnp.bfloat16) for w in plain], 1)
    hidden, normed_t, activ, dgate, dup, mlp_part = {}, {}, {}, {}, {}, {}

    def feed(j):
        gathered = (own[j], other[j], across[j], outer[j])
        (hidden[j], normed_t[j], activ[j], dgate[j], dup[j], mlp_part[j], part[j]) = forward_chunk(
            level_ref, gathered, tokens, dout, out_plain, mlp_gain, w_gate, w_up, w_down, j, rows
        )

    feed(c0)
    own, other, across, outer, part, hidden = fence(own, other, across, outer, part, hidden)
    add_1(c0)
    hop_3(c1)
    hop_2(c2)
    hop_1(c3)
    feed(c1)
    own, other, across, outer, part, total, coming, hidden = fence(
        own, other, across, outer, part, total, coming, hidden
    )
    add_2(c0)
    add_1(c1)
    hop_3(c2)
    hop_2(c3)
    feed(c2)
    own, other, across, outer, part, total, coming, hidden = fence(
        own, other, across, outer, part, total, coming, hidden
    )
    add_3(c0)
    add_2(c1)
    add_1(c2)
    hop_3(c3)
    feed(c3)
    qkv_far, _ = fence(qkv_far, part[c3])
    qkv_pad = spread_qkv(own_pad, pq, pkv, qkv_far)
    qkv = project(normed_one, qkv_pad, cosines, sines)

    listed = lambda pieces: [pieces[j] for j in range(CHUNKS)]
    keep_side = jnp.stack([core, 2, 0]).astype(jnp.int32)
    keep_turned = jnp.stack([core, 2, chip]).astype(jnp.int32)
    send_side = jnp.stack([1 - core, 2, 0]).astype(jnp.int32)
    send_turned = jnp.stack([1 - core, 2, chip]).astype(jnp.int32)
    all_rows = jnp.array([0, 1, 0], jnp.int32)

    def send_rows(lefts, groups, step, extra=None, side=send_side):
        if not by_hand:
            return rows_of(lefts, groups, all_rows, depth // 4, 4, step, extra)
        return rows_of(lefts, groups, side, slice_rows, chips, step, extra)

    def keep_rows(lefts, groups, received, step, extra=None, side=keep_side, apart=1):
        if not by_hand:
            return received
        return rows_of(
            lefts, groups, side, slice_rows, chips, step, extra, received, apart
        )

    def swap_rows(array):
        return swap(array) if by_hand else array

    def scatter(array):
        axes = "chip" if by_hand else ("chip", "core")
        return lax.psum_scatter(array, axes, scatter_dimension=0, tiled=True)

    units = w_gate.shape[1]
    mlp_args = (
        [listed(normed_t), dout_t],
        [(0, listed(dgate)), (0, listed(dup)), (1, listed(activ))],
    )
    acc = None
    dhid_t, dqkv_own, input_grad, gains = {}, {}, {}, {}

    def back(j):
        nonlocal acc
        (dhid_t[j], dqkv_own[j], input_grad[j], gains[j]), acc = back_some(j, True)

    def back_own(j):
        return back_some(j, False)[0]

    def back_some(j, full):
        return backward_chunk(
            level_ref,
            (total[j], final[j]),
            hidden[j],
            dout,
            tokens,
            (norm_gain, mlp_gain),
            (out_pad, qkv_pad),
            qkv,
            (own[j], other[j], across[j], outer[j]),
            (p_out, strip_one),
            (cosines, sines),
            acc,
            j,
            rows,
            full,
        )

    own, other, across, outer, part, total, coming, final, hidden, mlp_in, qkv = fence(
        own, other, across, outer, part, total, coming, final, hidden,
        (normed_t, activ, dgate, dup), qkv,
    )
    normed_t, activ, dgate, dup = mlp_in
    add_3(c1)
    add_2(c2)
    add_1(c3)
    units = w_gate.shape[1]
    mlp_args = (
        [listed(normed_t), dout_t],
        [(0, listed(dgate)), (0, listed(dup)), (1, listed(activ))],
    )
    sent = swap_rows(send_rows(*mlp_args, units // 2))
    back(c0)

    near = lambda: jnp.where(low, mlp_part[1], mlp_part[2])
    edge = lambda: jnp.where(low, mlp_part[0], mlp_part[3])
    total, coming, final, hidden, mlp_part, acc, dhid_t, sent = fence(
        total, coming, final, hidden, mlp_part, acc, dhid_t, sent
    )
    add_3(c2)
    add_2(c3)
    leave_far = jnp.where(low, mlp_part[3], mlp_part[0])
    leave_near = jnp.where(low, mlp_part[2], mlp_part[1])
    far_sum = along(leave_far, INWARD)
    grad_mlp = keep_rows(*mlp_args, sent, units // 2)
    hidden, grad_mlp = fence(hidden, grad_mlp)
    grad_mlp = scatter(grad_mlp)
    back(c1)
    total, coming, final, hidden, mlp_part, far_sum, acc, dhid_t = fence(
        total, coming, final, hidden, mlp_part, far_sum, acc, dhid_t
    )
    add_3(c3)
    near_sum = along(leave_near, INWARD)
    far_in = along(leave_far + far_sum, MIDDLE)
    back(c2)
    total, final, hidden, mlp_part, near_sum, far_in, acc, dhid_t = fence(
        total, final, hidden, mlp_part, near_sum, far_in, acc, dhid_t
    )
    near_in = along(leave_near + near_sum, MIDDLE)
    last = along(jnp.where(inner, edge() + far_in, near()), PAIRS)
    dhid_t[c3], dqkv_own[c3] = back_own(c3)
    q_cols = heads_here * HD
    attn_args = (
        [listed(dhid_t), normed_one_t],
        [(0, listed(own)), (1, listed(dqkv_own))],
    )
    sent = swap_rows(send_rows(*attn_args, q_cols, None, send_turned))
    total, final, hidden, acc, sent = fence(total, final, hidden, acc, sent)
    if by_hand:
        pieces = keep_rows(*attn_args, sent, q_cols, None, keep_turned, chips)
        pieces, hidden = fence(pieces, hidden)
        pieces = [pieces[0]] + [to_chip(pieces[m], m) for m in range(1, chips)]
    else:
        pieces = [scatter(sent)]
    back(c3)
    pieces, gains, input_grad, last, near_in = fence(pieces, gains, input_grad, last, near_in)
    gain_sums = gains[0] + gains[1] + gains[2] + gains[3]
    gain_sums = gain_sums + swap(gain_sums)
    if by_hand:
        others = [to_chip(gain_sums, m) for m in range(1, chips)]
        gain_sums = sum(others, gain_sums)
    else:
        gain_sums = lax.psum(gain_sums, "chip")
    gain_rows = lax.dynamic_slice_in_dim(gain_sums, at_row, slice_rows, 1)
    attn = sum(pieces[1:], pieces[0])
    grad_out, grad_qkv = attn[:, :q_cols], attn[:, q_cols:]
    mlp_rows = jnp.where(inner, near() + near_in, edge()) + last
    hidden_rows = jnp.where(
        low,
        jnp.where(level == 0, hidden[0], hidden[1]),
        jnp.where(level == 2, hidden[2], hidden[3]),
    )
    layer_out = (hidden_rows + mlp_rows).astype(jnp.bfloat16)
    one = strip_one.shape[1]
    picked = lambda at, width: jnp.concatenate(
        [grad_qkv[:, kv * one + at : kv * one + at + width] for kv in range(kv_here)], 1
    )
    return (
        layer_out,
        jnp.concatenate(listed(input_grad), 0),
        gain_rows[0],
        picked(0, GROUP * HD),
        picked(GROUP * HD, HD),
        picked((GROUP + 1) * HD, HD),
        grad_out.T,
        gain_rows[1],
        grad_mlp[:, :units],
        grad_mlp[:, units : 2 * units],
        grad_mlp[:, 2 * units :].T,
    )


def solution(mesh):
    devices = mesh.devices
    dp, tp = devices.shape
    split = Mesh(devices.reshape(dp // 2, 2, tp), ("chip", "core", "tp"))
    data = ("chip", "core")
    return jax.shard_map(
        shards,
        mesh=split,
        in_specs=(
            P(data, None),
            P(data),
            P(data),
            P(data, None),
            P(),
            P(None, "tp"),
            P(None, "tp"),
            P(None, "tp"),
            P("tp", None),
            P(),
            P(None, "tp"),
            P(None, "tp"),
            P("tp", None),
        ),
        out_specs=(
            P(("chip", "core", "tp"), None),
            P(data, None),
            P(data),
            P(data, "tp"),
            P(data, "tp"),
            P(data, "tp"),
            P("tp", data),
            P(data),
            P(data, "tp"),
            P(data, "tp"),
            P("tp", data),
        ),
        check_vma=False,
    )
```

```python
import functools

import jax
import jax.numpy as jnp
from jax import lax
from jax.experimental import pallas as pl
from jax.experimental.pallas import tpu as pltpu
from jax.sharding import Mesh
from jax.sharding import PartitionSpec as P

HD = 96
LANES = 128
GROUP = 2
KV_WIDE = (GROUP + 2) * LANES
rope_base = 100000.0
norm_eps = 1e-05
masked_score = -1e30
far_away = 1e30
score_scale = HD ** (-0.5)
score_scale_log2 = score_scale * 1.4426950408889634
CHUNKS = 4
EXTRA = 8
VMEM_BYTES = 56 * 1024 * 1024
NT = (((1,), (1,)), ((), ()))


def params():
    return pltpu.CompilerParams(vmem_limit_bytes=VMEM_BYTES)


def cost(flops, moved, exps=0):
    return pl.CostEstimate(
        flops=flops // 1024, bytes_accessed=moved // 1024, transcendentals=exps // 1024
    )


def dot32(a, b):
    return jnp.dot(a, b, preferred_element_type=jnp.float32)


def dot32_nt(a, b):
    return lax.dot_general(a, b, NT, preferred_element_type=jnp.float32)


def dot_split(a, places):
    high = a.astype(jnp.bfloat16)
    rest = (a - high.astype(jnp.float32)).astype(jnp.bfloat16)
    return dot32(high, places) + dot32(rest, places)


def fence(*trees):
    return lax.optimization_barrier(trees)


def whole(array, buffers=None):
    zeros = (0,) * len(array.shape)
    return pl.BlockSpec(array.shape, lambda *_: zeros)


SCALAR = pl.BlockSpec(memory_space=pltpu.SMEM)


def halves(entry):
    half_dim = HD // 2
    return (entry // half_dim) * (LANES // 2) + entry % half_dim


def placement(lanes, width):
    return (lanes[:, None] == jnp.arange(width)[None, :]).astype(jnp.bfloat16)


def place_query(heads):
    source = jnp.arange(heads * HD)
    return placement((source // HD) * LANES + halves(source % HD), heads * LANES)


def place_key_value(kv_heads):
    source = jnp.arange(kv_heads * HD)
    head = source // HD
    keys = head * 2 * LANES + halves(source % HD)
    values = head * 2 * LANES + LANES + source % HD
    return placement(jnp.concatenate([keys, values]), kv_heads * 2 * LANES)


def place_all(heads, kv_heads):
    source = jnp.arange(heads * HD)
    head = source // HD
    query = (head // GROUP) * KV_WIDE + (head % GROUP) * LANES + halves(source % HD)
    source = jnp.arange(kv_heads * HD)
    base = (source // HD) * KV_WIDE + GROUP * LANES
    keys = base + halves(source % HD)
    values = base + LANES + source % HD
    return placement(jnp.concatenate([query, keys, values]), kv_heads * KV_WIDE)


def place_plain(heads):
    source = jnp.arange(heads * HD)
    return placement((source // HD) * LANES + source % HD, heads * LANES)


PAIRS = [(0, 1), (1, 0), (2, 3), (3, 2)]
INWARD = [(0, 1), (3, 2)]
MIDDLE = [(1, 2), (2, 1)]
OUTWARD = [(1, 0), (2, 3)]


def along(part, pairs):
    return lax.ppermute(part, "tp", pairs)


def store_qkv(out_ref, here, base, query, key_value):
    wide = GROUP * LANES
    for kv in range(key_value.shape[1] // (2 * LANES)):
        at = base + kv * KV_WIDE
        there = slice(kv * 2 * LANES, (kv + 1) * 2 * LANES)
        out_ref[here, at : at + wide] = query[:, kv * wide : (kv + 1) * wide]
        out_ref[here, at + wide : at + KV_WIDE] = key_value[:, there]


def store_turned(out_ref, at, lin, cos_ref, sin_ref):
    for h in range(GROUP + 2):
        one = lin[:, h * LANES : (h + 1) * LANES]
        if h < GROUP + 1:
            one = one * cos_ref[...] + pltpu.roll(one, LANES // 2, 1) * sin_ref[...]
        out_ref[:, at + h * LANES : at + (h + 1) * LANES] = one.astype(jnp.bfloat16)


def spread_out_kernel(meta_ref, own_ref, p_ref, mine_ref, theirs_ref, pad_ref, plain_ref):
    rows, width = mine_ref.shape[2:]
    wide = p_ref.shape[1]
    for side, ref in enumerate((mine_ref, theirs_ref)):
        here = pl.ds(pl.multiple_of((meta_ref[1] ^ side) * rows, rows), rows)
        for s in range(4):
            block = own_ref[here, :] if s == 0 else ref[0, s - 1].astype(jnp.bfloat16)
            plain_ref[here, s * width : (s + 1) * width] = block
            pad_ref[here, s * wide : (s + 1) * wide] = dot32(block, p_ref[...]).astype(
                jnp.bfloat16
            )


def spread_qkv_kernel(own_ref, pq_ref, pkv_ref, far_ref, out_ref):
    parts, others, rows, width = far_ref.shape
    wide = own_ref.shape[1]
    split = pq_ref.shape[0]
    out_ref[:, :wide] = own_ref[...]
    for s in range(others):
        block = far_ref[:, s].reshape(parts * rows, width).astype(jnp.bfloat16)
        query = dot32(block[:, :split], pq_ref[...]).astype(jnp.bfloat16)
        key_value = dot32(block[:, split:], pkv_ref[...]).astype(jnp.bfloat16)
        store_qkv(out_ref, slice(None), (s + 1) * wide, query, key_value)


def spread_qkv(own, pq, pkv, far):
    total, wide = own.shape
    dp, others, rows, width = far.shape
    parts = max(1, dp // 4)
    block = parts * rows
    return pl.pallas_call(
        spread_qkv_kernel,
        out_shape=jax.ShapeDtypeStruct((total, (others + 1) * wide), jnp.bfloat16),
        grid=(total // block,),
        in_specs=[
            pl.BlockSpec((block, wide), lambda i: (i, 0)),
            whole(pq),
            whole(pkv),
            pl.BlockSpec((parts, others, rows, width), lambda i: (i, 0, 0, 0)),
        ],
        out_specs=pl.BlockSpec((block, (others + 1) * wide), lambda i: (i, 0)),
        compiler_params=params(),
        cost_estimate=cost(8 * total * width * 512, 20 * total * wide),
    )(own, pq, pkv, far)


def spread(kernel, meta, own, places, mine, theirs, widths):
    chips, others, rows, width = mine.shape
    total = own.shape[0]
    row_block = lambda m, meta: (meta[0] ^ m, 0)
    piece = pl.BlockSpec((1, others, rows, width), lambda m, meta: (m, 0, 0, 0))
    return pl.pallas_call(
        kernel,
        out_shape=[jax.ShapeDtypeStruct((total, wide), jnp.bfloat16) for wide in widths],
        grid_spec=pltpu.PrefetchScalarGridSpec(
            num_scalar_prefetch=1,
            grid=(chips,),
            in_specs=[pl.BlockSpec((2 * rows, own.shape[1]), row_block)]
            + [whole(place) for place in places]
            + [piece, piece],
            out_specs=[pl.BlockSpec((2 * rows, wide), row_block) for wide in widths],
        ),
        compiler_params=params(),
        cost_estimate=cost(
            8 * total * width * 512, total * (12 * width + 2 * sum(widths))
        ),
    )(meta, own, *places, mine, theirs)


def start_kernel(x_ref, gain_ref, q_ref, k_ref, v_ref, pq_ref, pkv_ref, cos_ref, sin_ref, *outs):
    qkv_ref, normed_ref, pad_ref = outs

    @pl.when(pl.program_id(0) == 0)
    def _():
        split = k_ref.shape[0]
        query = dot32(q_ref[...], pq_ref[...]).astype(jnp.bfloat16)
        key_value = dot32(k_ref[...].T, pkv_ref[:split, :])
        key_value = key_value + dot32(v_ref[...].T, pkv_ref[split:, :])
        store_qkv(pad_ref, slice(None), 0, query, key_value.astype(jnp.bfloat16))

    inputs = x_ref[...].astype(jnp.float32)
    rms = lax.rsqrt(jnp.mean(inputs * inputs, -1, keepdims=True) + norm_eps)
    normed = (inputs * rms * gain_ref[...]).astype(jnp.bfloat16)
    normed_ref[...] = normed
    for kv in range(pad_ref.shape[1] // KV_WIDE):
        at = kv * KV_WIDE
        store_turned(qkv_ref, at, dot32(normed, pad_ref[:, at : at + KV_WIDE]), cos_ref, sin_ref)


def start(tokens, gain, w_query, w_key_t, w_value_t, pq, pkv, cosines, sines):
    total, depth = tokens.shape
    rows = total // CHUNKS
    wide = pq.shape[1] + pkv.shape[1]
    gain = gain[None, :]
    by_rows = lambda width: pl.BlockSpec((rows, width), lambda i: (i, 0))
    arrays = [w_query, w_key_t, w_value_t, pq, pkv]
    shapes = [
        jax.ShapeDtypeStruct((total, wide), jnp.bfloat16),
        jax.ShapeDtypeStruct((total, depth), jnp.bfloat16),
        jax.ShapeDtypeStruct((depth, wide), jnp.bfloat16),
    ]
    return pl.pallas_call(
        start_kernel,
        out_shape=shapes,
        grid=(CHUNKS,),
        in_specs=[by_rows(depth), whole(gain)]
        + [whole(array) for array in arrays]
        + [by_rows(LANES), by_rows(LANES)],
        out_specs=[by_rows(wide), by_rows(depth), whole(shapes[2])],
        compiler_params=params(),
        cost_estimate=cost(2 * total * depth * wide, 12 * total * depth),
    )(tokens, gain, *arrays, cosines, sines)


def turn_kernel(length_ref, cot_ref, normed_ref, dout_ref, dout_t_ref, normed_t_ref):
    rows = cot_ref.shape[0]
    at = pl.program_id(0) * rows + lax.broadcasted_iota(jnp.int32, cot_ref.shape, 0)
    dout = jnp.where(at < length_ref[0], cot_ref[...].astype(jnp.float32), 0.0)
    dout = dout.astype(jnp.bfloat16)
    dout_ref[...] = dout
    dout_t_ref[...] = dout.T
    normed_t_ref[...] = normed_ref[...].T


def turn(length, cotangent, normed):
    total, depth = cotangent.shape
    rows = total // CHUNKS
    by_rows = pl.BlockSpec((rows, depth), lambda i: (i, 0))
    by_columns = pl.BlockSpec((depth, rows), lambda i: (0, i))
    turned = jax.ShapeDtypeStruct((depth, total), jnp.bfloat16)
    return pl.pallas_call(
        turn_kernel,
        out_shape=[jax.ShapeDtypeStruct((total, depth), jnp.bfloat16), turned, turned],
        grid=(CHUNKS,),
        in_specs=[SCALAR, by_rows, by_rows],
        out_specs=[by_rows, by_columns, by_columns],
        compiler_params=params(),
        cost_estimate=cost(total * depth, 10 * total * depth),
    )(length, cotangent, normed)


def project_kernel(x_ref, w_ref, cos_ref, sin_ref, out_ref):
    store_turned(out_ref, 0, dot32(x_ref[...], w_ref[...]), cos_ref, sin_ref)


def project(normed, weights, cosines, sines):
    rows, depth = normed.shape
    width = weights.shape[1]
    return pl.pallas_call(
        project_kernel,
        out_shape=jax.ShapeDtypeStruct((rows, width), jnp.bfloat16),
        grid=(width // KV_WIDE,),
        in_specs=[
            whole(normed),
            pl.BlockSpec((depth, KV_WIDE), lambda i: (0, i)),
            whole(cosines),
            whole(sines),
        ],
        out_specs=pl.BlockSpec((rows, KV_WIDE), lambda i: (0, i)),
        compiler_params=params(),
        cost_estimate=cost(
            2 * rows * depth * width, 2 * (rows * depth + depth * width + rows * width)
        ),
    )(normed, weights, cosines, sines)


def attend_kernel(start, length_ref, q_ref, kv_ref, strip_ref, out_ref):
    rows = q_ref.shape[0]
    keys = kv_ref.shape[0]
    length = length_ref[0]
    row_ids = start + lax.broadcasted_iota(jnp.int32, (1, rows), 1)
    limit = jnp.minimum(row_ids, length - 1)
    allowed = lax.broadcasted_iota(jnp.int32, (keys, rows), 0) <= limit
    mixed = []
    sums = []
    for kv in range(kv_ref.shape[1] // KV_WIDE):
        base = kv * KV_WIDE
        at = base + GROUP * LANES
        key = kv_ref[:, at : at + LANES]
        value_t = kv_ref[:, at + LANES : at + 2 * LANES].T
        for g in range(GROUP):
            query = q_ref[:, base + g * LANES : base + (g + 1) * LANES]
            raw = jnp.where(allowed, dot32_nt(key, query), masked_score)
            peak = jnp.max(raw, axis=0, keepdims=True)
            expo = jnp.exp2((raw - peak) * score_scale_log2)
            total = jnp.sum(expo, axis=0, keepdims=True)
            probs = (expo * (1.0 / total)).astype(jnp.bfloat16)
            mixed.append(dot32(value_t, probs).T)
            log_sum = peak * score_scale_log2 + jnp.log2(total)
            sums.append(jnp.where(row_ids < length, log_sum, far_away))
    out_ref[:rows, :] = dot_split(jnp.concatenate(mixed, 1), strip_ref[...])
    out_ref[rows:, :] = jnp.zeros((EXTRA, out_ref.shape[1]), jnp.float32)
    out_ref[rows : rows + len(sums), :rows] = jnp.concatenate(sums, 0)


def attend(length, qkv, strip, index, rows):
    keys = (index + 1) * rows
    width = qkv.shape[1]
    heads = width // KV_WIDE * GROUP
    shape = (rows + EXTRA, strip.shape[1])
    return pl.pallas_call(
        functools.partial(attend_kernel, index * rows),
        out_shape=jax.ShapeDtypeStruct(shape, jnp.float32),
        grid=(1,),
        in_specs=[
            SCALAR,
            pl.BlockSpec((rows, width), lambda i: (index, 0)),
            pl.BlockSpec((keys, width), lambda i: (0, 0)),
            whole(strip),
        ],
        out_specs=pl.BlockSpec(shape, lambda i: (0, 0)),
        compiler_params=params(),
        cost_estimate=cost(
            4 * heads * rows * keys * LANES, 2 * (rows + keys) * width, heads * rows * keys
        ),
    )(length, qkv, qkv, strip)


def forward_kernel(level_ref, part_ref, other_ref, across_ref, outer_ref, *refs):
    x_ref, dout_ref, wo_ref, gain_ref, wg_ref, wu_ref, wd_ref = refs[:7]
    hidden_ref, normed_t_ref, activ_ref, dgate_ref, dup_ref, mlp_ref, dn_ref = refs[7:14]
    normed_ref = refs[14]
    rows = x_ref.shape[0]

    @pl.when(pl.program_id(0) == 0)
    def _():
        level = level_ref[0]
        inner = (level == 1) | (level == 2)
        width = part_ref.shape[1]
        second = jnp.where(inner, across_ref[:rows, width:], outer_ref[:rows, :width])
        third = jnp.where(inner, across_ref[:rows, :width], outer_ref[:rows, width:])
        mixed = jnp.concatenate([part_ref[:rows, :], other_ref[:rows, :], second, third], 1)
        hidden = x_ref[...].astype(jnp.float32) + dot32_nt(mixed.astype(jnp.bfloat16), wo_ref[...])
        hidden_ref[...] = hidden
        rms = lax.rsqrt(jnp.mean(hidden * hidden, -1, keepdims=True) + norm_eps)
        normed = (hidden * rms * gain_ref[...]).astype(jnp.bfloat16)
        normed_ref[...] = normed
        normed_t_ref[...] = normed.T
        mlp_ref[...] = jnp.zeros_like(mlp_ref)
        dn_ref[...] = jnp.zeros_like(dn_ref)

    normed = normed_ref[...]
    gate = dot32(normed, wg_ref[...])
    up = dot32(normed, wu_ref[...])
    dact = dot32_nt(dout_ref[...], wd_ref[...])
    sigmoid = jax.nn.sigmoid(gate)
    silu = gate * sigmoid
    activ = (silu * up).astype(jnp.bfloat16)
    dgate = (dact * up * sigmoid * (1.0 + gate * (1.0 - sigmoid))).astype(jnp.bfloat16)
    dup = (dact * silu).astype(jnp.bfloat16)
    activ_ref[...] = activ
    dgate_ref[...] = dgate
    dup_ref[...] = dup
    mlp_ref[...] += dot32(activ, wd_ref[...])
    dn_ref[...] += dot32_nt(dgate, wg_ref[...]) + dot32_nt(dup, wu_ref[...])


def forward_chunk(level, gathered, tokens, dout, w_out, gain, w_gate, w_up, w_down, index, rows):
    depth = tokens.shape[1]
    units = w_gate.shape[1]
    block = 512
    own_rows = pl.BlockSpec((rows, depth), lambda i: (index, 0))
    by_units = pl.BlockSpec((depth, block), lambda i: (0, i))
    gain = gain[None, :]
    f32, bf16 = jnp.float32, jnp.bfloat16
    outs = [
        jax.ShapeDtypeStruct((rows, depth), f32),
        jax.ShapeDtypeStruct((depth, rows), bf16),
        jax.ShapeDtypeStruct((rows, units), bf16),
        jax.ShapeDtypeStruct((rows, units), bf16),
        jax.ShapeDtypeStruct((rows, units), bf16),
        jax.ShapeDtypeStruct((rows, depth), f32),
        jax.ShapeDtypeStruct((rows, depth), f32),
    ]
    unit_out = pl.BlockSpec((rows, block), lambda i: (0, i))
    return pl.pallas_call(
        forward_kernel,
        out_shape=outs,
        grid=(units // block,),
        in_specs=[SCALAR]
        + [whole(array) for array in gathered]
        + [own_rows, own_rows, whole(w_out), whole(gain), by_units, by_units]
        + [pl.BlockSpec((block, depth), lambda i: (i, 0))],
        out_specs=[
            whole(outs[0]),
            whole(outs[1]),
            unit_out,
            unit_out,
            unit_out,
            whole(outs[5]),
            whole(outs[6]),
        ],
        scratch_shapes=[pltpu.VMEM((rows, depth), bf16)],
        compiler_params=params(),
        cost_estimate=cost(
            2 * rows * depth * (6 * units + w_out.shape[1]),
            2 * depth * (3 * units + w_out.shape[1]) + 22 * rows * depth,
            rows * units,
        ),
    )(level, *gathered, tokens, dout, w_out, gain, w_gate, w_up, w_down)


def hidden_grad(inner, total_ref, final_ref, hidden_ref, dout_ref, gain_ref):
    dnormed = jnp.where(inner, total_ref[...], final_ref[...])
    hidden = hidden_ref[...]
    rms = lax.rsqrt(jnp.mean(hidden * hidden, -1, keepdims=True) + norm_eps)
    scaled = dnormed * gain_ref[...]
    shift = jnp.mean(scaled * hidden, -1, keepdims=True)
    dhid = dout_ref[...].astype(jnp.float32) + (rms * scaled - hidden * (rms**3 * shift))
    return dhid, dnormed * (hidden * rms)


def backward_kernel(start, full, level_ref, total_ref, final_ref, hidden_ref, dout_ref, x_ref, *refs):
    gain_one_ref, gain_two_ref, wo_ref, q_ref = refs[:4]
    kv_here = q_ref.shape[1] // KV_WIDE
    refs = refs[4:]
    kv_refs, refs = refs[: 2 * kv_here], refs[2 * kv_here :]
    part_ref, other_ref, across_ref, outer_ref, place_ref, strip_ref = refs[:6]
    cos_ref, sin_ref = refs[6:8]
    dhid_ref, low_ref, dn_ref = refs[-3:]
    outs = refs[8:-3]
    if full:
        w_ref, outs = outs[0], outs[1:]
    count = (5 if start > 0 else 4) if full else 2
    acc_ref = outs[0] if len(outs) > count else None
    outs = outs[-count:]
    dhid_t_ref, dqkv_ref = outs[:2]
    if full:
        input_grad_ref, gains_ref = outs[2:4]
    rows = q_ref.shape[0]
    keys = kv_refs[0].shape[0]
    shard = pl.program_id(0)
    level = level_ref[0]
    inner = (level == 1) | (level == 2)

    @pl.when(shard == 0)
    def _():
        dhid, dgain = hidden_grad(
            inner, total_ref, final_ref, hidden_ref, dout_ref, gain_two_ref
        )
        dhid_ref[...] = dhid
        low = dhid.astype(jnp.bfloat16)
        low_ref[...] = low
        dhid_t_ref[...] = low.T
        if full:
            gains_ref[...] = jnp.zeros_like(gains_ref)
            gains_ref[1:2, :] = jnp.sum(dgain, 0, keepdims=True)
            dn_ref[...] = jnp.zeros_like(dn_ref)

    def rotate_back(grads):
        turned = grads * cos_ref[...] - pltpu.roll(grads, LANES // 2, 1) * sin_ref[...]
        return turned.astype(jnp.bfloat16)

    dmixed_all = dot32(low_ref[...], wo_ref[...]).astype(jnp.bfloat16)
    mixed = jnp.where(
        shard == 0,
        part_ref[...],
        jnp.where(shard == 1, other_ref[...], jnp.where(inner, across_ref[...], outer_ref[...])),
    )
    products = dmixed_all.astype(jnp.float32) * dot_split(mixed[:rows], place_ref[...])
    causal = lax.broadcasted_iota(jnp.int32, (rows, rows), 0) <= lax.broadcasted_iota(
        jnp.int32, (rows, rows), 1
    )
    grads = []
    for kv in range(kv_here):
        key_ref, value_ref = kv_refs[2 * kv : 2 * kv + 2]
        heads = range(kv * GROUP, (kv + 1) * GROUP)
        lanes = {h: slice(h * LANES, (h + 1) * LANES) for h in heads}
        row_dots = {h: jnp.sum(products[:, lanes[h]].T, axis=0, keepdims=True) for h in heads}
        log_sums = {h: mixed[rows + h : rows + h + 1, :rows] for h in heads}
        dqueries = dict.fromkeys(heads)
        here = slice(2 * kv * LANES, (2 * kv + 1) * LANES)
        there = slice((2 * kv + 1) * LANES, (2 * kv + 2) * LANES)
        for tile in range(keys // rows):
            span = slice(tile * rows, (tile + 1) * rows)
            key = key_ref[span, :]
            value = value_ref[span, :]
            key_t = key.T
            dkey = None if acc_ref is None else acc_ref[span, here]
            dvalue = None if acc_ref is None else acc_ref[span, there]
            last = tile * rows == start
            for h in heads:
                at = kv * KV_WIDE + (h % GROUP) * LANES
                query = q_ref[:, at : at + LANES]
                dmixed = dmixed_all[:, lanes[h]]
                raw = dot32_nt(key, query)
                probs = jnp.exp2(raw * score_scale_log2 - log_sums[h])
                if last:
                    probs = jnp.where(causal, probs, 0.0)
                dprobs = dot32_nt(value, dmixed)
                dscores = (probs * (dprobs - row_dots[h])).astype(jnp.bfloat16)
                dquery = dot32(key_t, dscores)
                dqueries[h] = dquery if dqueries[h] is None else dqueries[h] + dquery
                dkey_one = dot32(dscores, query)
                dvalue_one = dot32(probs.astype(jnp.bfloat16), dmixed)
                dkey = dkey_one if dkey is None else dkey + dkey_one
                dvalue = dvalue_one if dvalue is None else dvalue + dvalue_one
            if full and not last:
                outs[4][span, here] = dkey
                outs[4][span, there] = dvalue
        grads += [rotate_back(dqueries[h].T * score_scale) for h in heads]
        grads.append(rotate_back(dkey * score_scale))
        grads.append(dvalue.astype(jnp.bfloat16))
    grads = jnp.concatenate(grads, 1)
    if full:
        dn_ref[...] += dot32_nt(grads, w_ref[...])

    @pl.when(shard == 0)
    def _():
        wide = strip_ref.shape[1]
        for kv in range(kv_here):
            dqkv_ref[:, kv * wide : (kv + 1) * wide] = dot32(
                grads[:, kv * KV_WIDE : (kv + 1) * KV_WIDE], strip_ref[...]
            ).astype(jnp.bfloat16)

    if not full:
        return

    @pl.when(shard == pl.num_programs(0) - 1)
    def _():
        dnormed = dn_ref[...]
        inputs = x_ref[...].astype(jnp.float32)
        rms = lax.rsqrt(jnp.mean(inputs * inputs, -1, keepdims=True) + norm_eps)
        scaled = dnormed * gain_one_ref[...]
        shift = jnp.mean(scaled * inputs, -1, keepdims=True)
        grad = dhid_ref[...] + (rms * scaled - inputs * (rms**3 * shift))
        input_grad_ref[...] = grad.astype(jnp.bfloat16)
        gains_ref[0:1, :] = jnp.sum(dnormed * (inputs * rms), 0, keepdims=True)


def backward_chunk(
    level, sums_two, hidden, dout, tokens, gains, weights, qkv, gathered, places, tables, acc,
    index, rows, full=True
):
    start = index * rows
    keys = start + rows
    depth = tokens.shape[1]
    out_pad, qkv_pad = weights
    place_out, strip = places
    far_rows, width = gathered[0].shape
    out_wide = place_out.shape[1]
    kv_here = out_wide // (GROUP * LANES)
    wide = kv_here * KV_WIDE
    levels = qkv.shape[1] // wide
    own_rows = pl.BlockSpec((rows, depth), lambda t: (index, 0))
    table = pl.BlockSpec((rows, LANES), lambda t: (index, 0))
    gains = [gain[None, :] for gain in gains]
    key_value = lambda at: pl.BlockSpec(
        (keys, LANES), lambda t: (0, (wide // LANES) * t + at)
    )
    across = pl.BlockSpec((far_rows, width), lambda t: (0, jnp.where(t == 2, 1, 0)))
    outer = pl.BlockSpec((far_rows, width), lambda t: (0, jnp.where(t == 3, 1, 0)))
    in_specs = [
        SCALAR,
        whole(sums_two[0]),
        whole(sums_two[1]),
        whole(hidden),
        own_rows,
        own_rows,
        whole(gains[0]),
        whole(gains[1]),
        pl.BlockSpec((depth, out_wide), lambda t: (0, t)),
        pl.BlockSpec((rows, wide), lambda t: (index, t)),
    ]
    for kv in range(kv_here):
        at = kv * (KV_WIDE // LANES) + GROUP
        in_specs += [key_value(at), key_value(at + 1)]
    in_specs += [
        whole(gathered[0]),
        whole(gathered[1]),
        across,
        outer,
        whole(place_out),
        whole(strip),
        table,
        table,
    ]
    args = [level, *sums_two, hidden, dout, tokens, *gains, out_pad]
    args += [qkv] * (1 + 2 * kv_here)
    args += [*gathered, place_out, strip, *tables]
    sums_wide = 2 * kv_here * LANES
    if full:
        in_specs.append(pl.BlockSpec((depth, wide), lambda t: (0, t)))
        args.append(qkv_pad)
    if acc is not None:
        in_specs.append(pl.BlockSpec((keys, sums_wide), lambda t: (0, t)))
        args.append(acc)
    f32, bf16 = jnp.float32, jnp.bfloat16
    outs = [
        jax.ShapeDtypeStruct((depth, rows), bf16),
        jax.ShapeDtypeStruct((rows, kv_here * strip.shape[1]), bf16),
        jax.ShapeDtypeStruct((rows, depth), bf16),
        jax.ShapeDtypeStruct((8, depth), f32),
    ]
    outs = outs if full else outs[:2]
    out_specs = [whole(out) for out in outs]
    if full and start > 0:
        outs.append(jax.ShapeDtypeStruct((start, levels * sums_wide), f32))
        out_specs.append(pl.BlockSpec((start, sums_wide), lambda t: (0, t)))
    results = pl.pallas_call(
        functools.partial(backward_kernel, start, full),
        out_shape=outs,
        grid=(levels if full else 1,),
        in_specs=in_specs,
        out_specs=out_specs,
        scratch_shapes=[
            pltpu.VMEM((rows, depth), f32),
            pltpu.VMEM((rows, depth), bf16),
            pltpu.VMEM((rows, depth), f32),
        ],
        compiler_params=params(),
        cost_estimate=cost(
            levels * rows * (20 * kv_here * keys * LANES + 2 * depth * (out_wide + wide)),
            2 * depth * levels * (out_wide + wide) + 16 * rows * depth,
            levels * kv_here * GROUP * rows * keys,
        ),
    )(*args)
    return results[:4], (results[4] if full and start > 0 else None)


def rows_kernel(lefts, groups, adding, picked, side_ref, *refs):
    refs = list(refs)
    held_ref = refs.pop()
    out_refs = refs[-len(picked) :]
    refs = refs[: -len(picked)]
    recv_ref = refs.pop() if adding else None
    step = pl.program_id(0)
    left_refs = []
    for count in lefts:
        left_refs.append(refs[:count])
        refs = refs[count:]
    rights = []
    for _ in groups:
        rights.append(refs[:CHUNKS])
        refs = refs[CHUNKS:]
    rows = left_refs[0][0].shape[0]
    blocks = held_ref.shape[1] // rows

    @pl.when(step == 0)
    def _():
        for which, pieces in enumerate(left_refs):
            for n, ref in enumerate(pieces):
                m, j = n % blocks, n // blocks
                wide = ref.shape[1]
                held_ref[which, m * rows : (m + 1) * rows, j * wide : (j + 1) * wide] = ref[...]

    chunk = held_ref.shape[2] // CHUNKS
    right = None
    which = 0
    for group, (left, first, _) in zip(rights, groups):
        one = jnp.concatenate([ref[:chunk, :].astype(jnp.bfloat16) for ref in group], 0)
        right = one if right is None else jnp.where(step >= first, one, right)
        which = jnp.where(step >= first, left, which)
    total = dot32(held_ref[which], right)
    if recv_ref is not None:
        total = total + recv_ref[...]
    for out_ref, parts in zip(out_refs, picked):
        at = 0
        for start, size in parts:
            out_ref[at : at + size, :] = total[start : start + size]
            at += size


def rows_of(lefts, groups, side, rows, blocks, step, recv=None, picked=None):
    if picked is None:
        picked = [[(0, rows * blocks)]]
    at = lambda m: lambda i, side: ((m ^ side[2]) * side[1] + side[0], 0)
    specs = []
    args = []
    counts = []
    for left in lefts:
        pieces = left if isinstance(left, list) else [left]
        counts.append(len(pieces) * blocks)
        for piece in pieces:
            for m in range(blocks):
                specs.append(pl.BlockSpec((rows, piece.shape[1]), at(m)))
                args.append(piece)
    tokens = sum(piece.shape[1] for piece in pieces)
    first = 0
    plan = []
    for which, rights in groups:
        steps = rights[0].shape[1] // step
        plan.append((which, first, steps))
        for right in rights:
            pick = lambda i, side, first=first, steps=steps: (0, jnp.clip(i - first, 0, steps - 1))
            specs.append(pl.BlockSpec((right.shape[0], step), pick))
            args.append(right)
        first += steps
    total = first * step
    block = lambda height: pl.BlockSpec((height, step), lambda i, side: (0, i))
    if recv is not None:
        specs.append(block(rows * blocks))
        args.append(recv)
    heights = [sum(size for _, size in parts) for parts in picked]
    results = pl.pallas_call(
        functools.partial(rows_kernel, counts, plan, recv is not None, picked),
        out_shape=[jax.ShapeDtypeStruct((height, total), jnp.float32) for height in heights],
        grid_spec=pltpu.PrefetchScalarGridSpec(
            num_scalar_prefetch=1,
            grid=(first,),
            in_specs=specs,
            out_specs=[block(height) for height in heights],
            scratch_shapes=[pltpu.VMEM((len(lefts), rows * blocks, tokens), jnp.bfloat16)],
        ),
        compiler_params=params(),
        cost_estimate=cost(
            2 * rows * blocks * tokens * total,
            4 * rows * blocks * total + 2 * tokens * (total + rows * blocks),
        ),
    )(side, *args)
    return results[0] if len(picked) == 1 else results


def shards(
    tokens,
    lengths,
    positions,
    cotangent,
    norm_gain,
    w_query,
    w_key,
    w_value,
    w_out,
    mlp_gain,
    w_gate,
    w_up,
    w_down,
):
    seq_rows, depth = tokens.shape
    chips = lax.axis_size("chip")
    dp = chips * 2
    tp = lax.axis_size("tp")
    chip = lax.axis_index("chip")
    core = lax.axis_index("core")
    level = lax.axis_index("tp")
    low = level < 2
    inner = (level == 1) | (level == 2)
    heads_here = w_query.shape[1] // HD
    kv_here = w_key.shape[1] // HD
    rows = seq_rows // CHUNKS
    slice_rows = depth // dp
    level_ref = level.astype(jnp.int32).reshape(1)
    by_hand = dp == 8
    swap = lambda array: lax.ppermute(array, "core", [(0, 1), (1, 0)])
    to_level = lambda array, s: along(array, [(t, t ^ s) for t in range(tp)])

    at_row = (chip * 2 + core) * slice_rows
    cols = lambda w: lax.dynamic_slice_in_dim(w, at_row, slice_rows, 1).astype(jnp.float32).T
    (out_slice,) = fence(cols(w_out))
    qkv_slice = jnp.concatenate(
        [
            lax.dynamic_slice_in_dim(w_query, at_row, slice_rows, 0).astype(jnp.float32),
            cols(w_key.T),
            cols(w_value.T),
        ],
        1,
    )
    out_slice, qkv_slice = fence(out_slice, qkv_slice)
    out_near = along(out_slice, PAIRS)
    qkv_near = along(qkv_slice, PAIRS)
    meta = jnp.stack([chip, core]).astype(jnp.int32)

    pq = place_query(heads_here)
    pkv = place_key_value(kv_here)
    p_all = place_all(heads_here, kv_here)
    strip_one = place_all(GROUP, 1).T
    p_out = place_plain(heads_here)
    strip_out = p_out.T

    half_dim = HD // 2
    freqs = rope_base ** (-(jnp.arange(half_dim).astype(jnp.float32) * 2.0 / HD))
    freqs = jnp.pad(freqs, (0, LANES // 2 - half_dim))
    angles = positions.astype(jnp.float32)[:, None] * jnp.concatenate([freqs, freqs])[None, :]
    cosines = jnp.cos(angles)
    sines = jnp.sin(angles) * jnp.where(jnp.arange(LANES) < LANES // 2, -1.0, 1.0)

    cosines, sines, out_near = fence(cosines, sines, out_near)
    out_across = along(jnp.stack([out_slice, out_near]), MIDDLE)
    qkv_own, normed_one, own_pad = start(
        tokens, norm_gain, w_query, w_key.T, w_value.T, pq, pkv, cosines, sines
    )

    def far_slices(near, across, outer):
        return jnp.stack(
            [
                near,
                jnp.where(inner, across[1], outer[0]),
                jnp.where(inner, across[0], outer[1]),
            ]
        )

    order = list(reversed(range(CHUNKS)))
    c0, c1, c2, c3 = order
    own, other, across, outer = {}, {}, {}, {}
    part, total, final = {}, {}, {}

    def hop_1(j):
        other[j] = along(own[j], PAIRS)

    def hop_2(j):
        across[j] = along(jnp.concatenate([own[j], other[j]], 1), MIDDLE)

    def hop_3(j):
        outer[j] = along(across[j], OUTWARD)

    coming = {}

    def add_1(j):
        coming[j] = along(part[j], INWARD)

    def add_2(j):
        total[j] = part[j] + coming[j]
        coming[j] = along(total[j], MIDDLE)

    def add_3(j):
        total[j] = total[j] + coming[j]
        final[j] = along(total[j], OUTWARD)

    def to_chip(array, m):
        return lax.ppermute(array, "chip", [(i, i ^ m) for i in range(chips)])

    def over_chips_1(piece):
        cut = piece.shape[1] // 2
        one, two = piece[:, :cut], piece[:, cut:]
        return jnp.stack([one, to_chip(one, 1)]), jnp.stack([two, to_chip(two, 2)])

    def over_chips_2(one, two):
        return one, to_chip(one, 2), two, to_chip(two, 1)

    def over_chips_3(one, one_far, two, two_far):
        upper = jnp.stack([one[0], one[1], one_far[0], one_far[1]])
        lower = jnp.stack([two[0], two_far[0], two[1], two_far[1]])
        return jnp.concatenate([upper, lower], 2)

    qkv_own, out_across, qkv_near = fence(qkv_own, out_across, qkv_near)
    out_outer = along(out_across, OUTWARD)
    qkv_across = along(jnp.stack([qkv_slice, qkv_near]), MIDDLE)
    own[c0] = attend(lengths, qkv_own, strip_out, c0, rows)
    own, qkv_own, out_outer = fence(own, qkv_own, out_outer)
    hop_1(c0)
    out_far = far_slices(out_near, out_across, out_outer)
    out_mine = over_chips_1(out_far) if by_hand else out_far
    for j in (c1, c2, c3):
        own[j] = attend(lengths, qkv_own, strip_out, j, rows)
    own, other, normed_one, w_out, out_mine, qkv_across = fence(
        own, other, normed_one, w_out, out_mine, qkv_across
    )
    if by_hand:
        out_mine = over_chips_2(*out_mine)
    else:
        out_mine = lax.all_gather(out_mine, ("chip", "core"))
    qkv_outer = along(qkv_across, OUTWARD)
    hop_2(c0)
    hop_1(c1)
    dout, dout_t, normed_one_t = turn(lengths, cotangent, normed_one)
    w_out_t = w_out.T
    own, other, across, dout, dout_t, normed_one_t, w_out_t, out_mine, qkv_outer = fence(
        own, other, across, dout, dout_t, normed_one_t, w_out_t, out_mine, qkv_outer
    )
    hop_3(c0)
    hop_2(c1)
    hop_1(c2)
    qkv_far = lax.all_gather(far_slices(qkv_near, qkv_across, qkv_outer), ("chip", "core"))
    if by_hand:
        out_mine = over_chips_3(*out_mine)
        out_theirs = swap(out_mine)
        out_pad, out_plain = spread(
            spread_out_kernel,
            meta,
            w_out_t,
            [p_out],
            out_mine,
            out_theirs,
            [4 * p_out.shape[1], 4 * p_out.shape[0]],
        )
    else:
        plain = [w_out_t] + [
            out_mine[:, s].reshape(depth, -1).astype(jnp.bfloat16) for s in range(tp - 1)
        ]
        out_plain = jnp.concatenate(plain, 1)
        out_pad = jnp.concatenate([dot32(w, p_out).astype(jnp.bfloat16) for w in plain], 1)
    hidden, normed_t, activ, dgate, dup, mlp_part = {}, {}, {}, {}, {}, {}

    def feed(j):
        gathered = (own[j], other[j], across[j], outer[j])
        (hidden[j], normed_t[j], activ[j], dgate[j], dup[j], mlp_part[j], part[j]) = forward_chunk(
            level_ref, gathered, tokens, dout, out_plain, mlp_gain, w_gate, w_up, w_down, j, rows
        )

    own, other, across, outer, out_pad, out_plain = fence(
        own, other, across, outer, out_pad, out_plain
    )
    hop_3(c1)
    hop_2(c2)
    hop_1(c3)
    feed(c0)
    own, other, across, outer, part, hidden = fence(own, other, across, outer, part, hidden)
    add_1(c0)
    hop_3(c2)
    hop_2(c3)
    feed(c1)
    own, other, across, outer, part, total, coming, hidden = fence(
        own, other, across, outer, part, total, coming, hidden
    )
    add_2(c0)
    add_1(c1)
    hop_3(c3)
    feed(c2)
    qkv_far, part = fence(qkv_far, part)
    qkv_pad = spread_qkv(own_pad, pq, pkv, qkv_far)
    own, other, across, outer, part, total, coming, hidden, qkv_pad = fence(
        own, other, across, outer, part, total, coming, hidden, qkv_pad
    )
    add_3(c0)
    add_2(c1)
    add_1(c2)
    qkv = project(normed_one, qkv_pad, cosines, sines)
    feed(c3)

    listed = lambda pieces: [pieces[j] for j in range(CHUNKS)]
    keep_side = jnp.stack([core, 2, 0]).astype(jnp.int32)
    keep_turned = jnp.stack([core, 2, chip]).astype(jnp.int32)
    send_side = jnp.stack([1 - core, 2, 0]).astype(jnp.int32)
    send_turned = jnp.stack([1 - core, 2, chip]).astype(jnp.int32)
    all_rows = jnp.array([0, 1, 0], jnp.int32)

    def send_rows(lefts, groups, step, side=send_side):
        if not by_hand:
            return rows_of(lefts, groups, all_rows, depth // 4, 4, step)
        return rows_of(lefts, groups, side, slice_rows, chips, step)

    def keep_rows(lefts, groups, received, step, side=keep_side, picked=None):
        if not by_hand:
            return received
        return rows_of(lefts, groups, side, slice_rows, chips, step, received, picked)

    def swap_rows(array):
        return swap(array) if by_hand else array

    def scatter(array):
        axes = "chip" if by_hand else ("chip", "core")
        return lax.psum_scatter(array, axes, scatter_dimension=0, tiled=True)

    units = w_gate.shape[1]
    mlp_args = (
        [listed(normed_t), dout_t],
        [(0, listed(dgate)), (0, listed(dup)), (1, listed(activ))],
    )
    acc = None
    dhid_t, dqkv_own, input_grad, gains = {}, {}, {}, {}

    def back(j):
        nonlocal acc
        (dhid_t[j], dqkv_own[j], input_grad[j], gains[j]), acc = back_some(j, True)

    def back_own(j):
        return back_some(j, False)[0]

    def back_some(j, full):
        return backward_chunk(
            level_ref,
            (total[j], final[j]),
            hidden[j],
            dout,
            tokens,
            (norm_gain, mlp_gain),
            (out_pad, qkv_pad),
            qkv,
            (own[j], other[j], across[j], outer[j]),
            (p_out, strip_one),
            (cosines, sines),
            acc,
            j,
            rows,
            full,
        )

    own, other, across, outer, part, total, coming, final, hidden, mlp_in, qkv = fence(
        own, other, across, outer, part, total, coming, final, hidden,
        (normed_t, activ, dgate, dup), qkv,
    )
    normed_t, activ, dgate, dup = mlp_in
    add_3(c1)
    add_2(c2)
    add_1(c3)
    units = w_gate.shape[1]
    mlp_args = (
        [listed(normed_t), dout_t],
        [(0, listed(dgate)), (0, listed(dup)), (1, listed(activ))],
    )
    sent = swap_rows(send_rows(*mlp_args, units // 2))
    back(c0)

    near = lambda: jnp.where(low, mlp_part[1], mlp_part[2])
    edge = lambda: jnp.where(low, mlp_part[0], mlp_part[3])
    total, coming, final, hidden, mlp_part, acc, dhid_t, sent = fence(
        total, coming, final, hidden, mlp_part, acc, dhid_t, sent
    )
    add_3(c2)
    add_2(c3)
    leave_far = jnp.where(low, mlp_part[3], mlp_part[0])
    leave_near = jnp.where(low, mlp_part[2], mlp_part[1])
    far_sum = along(leave_far, INWARD)
    grad_mlp = keep_rows(*mlp_args, sent, units // 2)
    hidden, grad_mlp = fence(hidden, grad_mlp)
    grad_mlp = scatter(grad_mlp)
    back(c1)
    total, coming, final, hidden, mlp_part, far_sum, acc, dhid_t = fence(
        total, coming, final, hidden, mlp_part, far_sum, acc, dhid_t
    )
    add_3(c3)
    near_sum = along(leave_near, INWARD)
    far_in = along(leave_far + far_sum, MIDDLE)
    back(c2)
    total, final, hidden, mlp_part, near_sum, far_in, acc, dhid_t = fence(
        total, final, hidden, mlp_part, near_sum, far_in, acc, dhid_t
    )
    near_in = along(leave_near + near_sum, MIDDLE)
    last = along(jnp.where(inner, edge() + far_in, near()), PAIRS)
    dhid_t[c3], dqkv_own[c3] = back_own(c3)
    q_cols = heads_here * HD
    attn_args = (
        [listed(dhid_t), normed_one_t],
        [(0, listed(own)), (1, listed(dqkv_own))],
    )
    sent = swap_rows(send_rows(*attn_args, q_cols, send_turned))
    total, final, hidden, acc, sent = fence(total, final, hidden, acc, sent)
    if by_hand:
        half = slice_rows // 2
        upper = lambda m: (m * slice_rows, half)
        lower = lambda m: (m * slice_rows + half, half)
        picked = [
            [upper(1), upper(3)],
            [upper(0), upper(2)],
            [lower(2), lower(3)],
            [lower(0), lower(1)],
        ]
        pieces = keep_rows(*attn_args, sent, q_cols, keep_turned, picked)
        pieces, hidden = fence(pieces, hidden)
        one_away, one, two_away, two = pieces
        pieces = (one, to_chip(one_away, 1), two, to_chip(two_away, 2))
    else:
        pieces = scatter(sent)
    back(c3)
    pieces, gains, input_grad, last, near_in = fence(pieces, gains, input_grad, last, near_in)
    gain_sums = gains[0] + gains[1] + gains[2] + gains[3]
    gain_sums = gain_sums + swap(gain_sums)
    if by_hand:
        others = [to_chip(gain_sums, m) for m in range(1, chips)]
        gain_sums = sum(others, gain_sums)
        one = pieces[0] + pieces[1]
        two = pieces[2] + pieces[3]
        one = one[:half] + to_chip(one[half:], 2)
        two = two[:half] + to_chip(two[half:], 1)
        attn = jnp.concatenate([one, two], 0)
    else:
        gain_sums = lax.psum(gain_sums, "chip")
        attn = pieces
    gain_rows = lax.dynamic_slice_in_dim(gain_sums, at_row, slice_rows, 1)
    grad_out, grad_qkv = attn[:, :q_cols], attn[:, q_cols:]
    mlp_rows = jnp.where(inner, near() + near_in, edge()) + last
    hidden_rows = jnp.where(
        low,
        jnp.where(level == 0, hidden[0], hidden[1]),
        jnp.where(level == 2, hidden[2], hidden[3]),
    )
    layer_out = (hidden_rows + mlp_rows).astype(jnp.bfloat16)
    one = strip_one.shape[1]
    picked = lambda at, width: jnp.concatenate(
        [grad_qkv[:, kv * one + at : kv * one + at + width] for kv in range(kv_here)], 1
    )
    return (
        layer_out,
        jnp.concatenate(listed(input_grad), 0),
        gain_rows[0],
        picked(0, GROUP * HD),
        picked(GROUP * HD, HD),
        picked((GROUP + 1) * HD, HD),
        grad_out.T,
        gain_rows[1],
        grad_mlp[:, :units],
        grad_mlp[:, units : 2 * units],
        grad_mlp[:, 2 * units :].T,
    )


def solution(mesh):
    devices = mesh.devices
    dp, tp = devices.shape
    split = Mesh(devices.reshape(dp // 2, 2, tp), ("chip", "core", "tp"))
    data = ("chip", "core")
    return jax.shard_map(
        shards,
        mesh=split,
        in_specs=(
            P(data, None),
            P(data),
            P(data),
            P(data, None),
            P(),
            P(None, "tp"),
            P(None, "tp"),
            P(None, "tp"),
            P("tp", None),
            P(),
            P(None, "tp"),
            P(None, "tp"),
            P("tp", None),
        ),
        out_specs=(
            P(("chip", "core", "tp"), None),
            P(data, None),
            P(data),
            P(data, "tp"),
            P(data, "tp"),
            P(data, "tp"),
            P("tp", data),
            P(data),
            P(data, "tp"),
            P(data, "tp"),
            P("tp", data),
        ),
        check_vma=False,
    )
```

```python
import functools

import jax
import jax.numpy as jnp
from jax import lax
from jax.experimental import pallas as pl
from jax.experimental.pallas import tpu as pltpu
from jax.sharding import Mesh
from jax.sharding import PartitionSpec as P

HD = 96
LANES = 128
GROUP = 2
KV_WIDE = (GROUP + 2) * LANES
rope_base = 100000.0
norm_eps = 1e-05
masked_score = -1e30
far_away = 1e30
score_scale = HD ** (-0.5)
score_scale_log2 = score_scale * 1.4426950408889634
CHUNKS = 4
EXTRA = 8
VMEM_BYTES = 56 * 1024 * 1024
NT = (((1,), (1,)), ((), ()))


def params():
    return pltpu.CompilerParams(vmem_limit_bytes=VMEM_BYTES)


def cost(flops, moved, exps=0):
    return pl.CostEstimate(
        flops=flops // 1024, bytes_accessed=moved // 1024, transcendentals=exps // 1024
    )


def dot32(a, b):
    return jnp.dot(a, b, preferred_element_type=jnp.float32)


def dot32_nt(a, b):
    return lax.dot_general(a, b, NT, preferred_element_type=jnp.float32)


def dot_split(a, places):
    high = a.astype(jnp.bfloat16)
    rest = (a - high.astype(jnp.float32)).astype(jnp.bfloat16)
    return dot32(high, places) + dot32(rest, places)


def fence(*trees):
    return lax.optimization_barrier(trees)


def whole(array, buffers=None):
    zeros = (0,) * len(array.shape)
    return pl.BlockSpec(array.shape, lambda *_: zeros)


SCALAR = pl.BlockSpec(memory_space=pltpu.SMEM)


def halves(entry):
    half_dim = HD // 2
    return (entry // half_dim) * (LANES // 2) + entry % half_dim


def placement(lanes, width):
    return (lanes[:, None] == jnp.arange(width)[None, :]).astype(jnp.bfloat16)


def place_query(heads):
    source = jnp.arange(heads * HD)
    return placement((source // HD) * LANES + halves(source % HD), heads * LANES)


def place_key_value(kv_heads):
    source = jnp.arange(kv_heads * HD)
    head = source // HD
    keys = head * 2 * LANES + halves(source % HD)
    values = head * 2 * LANES + LANES + source % HD
    return placement(jnp.concatenate([keys, values]), kv_heads * 2 * LANES)


def place_all(heads, kv_heads):
    source = jnp.arange(heads * HD)
    head = source // HD
    query = (head // GROUP) * KV_WIDE + (head % GROUP) * LANES + halves(source % HD)
    source = jnp.arange(kv_heads * HD)
    base = (source // HD) * KV_WIDE + GROUP * LANES
    keys = base + halves(source % HD)
    values = base + LANES + source % HD
    return placement(jnp.concatenate([query, keys, values]), kv_heads * KV_WIDE)


def place_plain(heads):
    source = jnp.arange(heads * HD)
    return placement((source // HD) * LANES + source % HD, heads * LANES)


PAIRS = [(0, 1), (1, 0), (2, 3), (3, 2)]
INWARD = [(0, 1), (3, 2)]
MIDDLE = [(1, 2), (2, 1)]
OUTWARD = [(1, 0), (2, 3)]


def along(part, pairs):
    return lax.ppermute(part, "tp", pairs)


def store_qkv(out_ref, here, base, query, key_value):
    wide = GROUP * LANES
    for kv in range(key_value.shape[1] // (2 * LANES)):
        at = base + kv * KV_WIDE
        there = slice(kv * 2 * LANES, (kv + 1) * 2 * LANES)
        out_ref[here, at : at + wide] = query[:, kv * wide : (kv + 1) * wide]
        out_ref[here, at + wide : at + KV_WIDE] = key_value[:, there]


def store_turned(out_ref, at, lin, cos_ref, sin_ref):
    for h in range(GROUP + 2):
        one = lin[:, h * LANES : (h + 1) * LANES]
        if h < GROUP + 1:
            one = one * cos_ref[...] + pltpu.roll(one, LANES // 2, 1) * sin_ref[...]
        out_ref[:, at + h * LANES : at + (h + 1) * LANES] = one.astype(jnp.bfloat16)


def spread_out_kernel(meta_ref, own_ref, p_ref, mine_ref, theirs_ref, pad_ref, plain_ref):
    rows, width = mine_ref.shape[2:]
    wide = p_ref.shape[1]
    for side, ref in enumerate((mine_ref, theirs_ref)):
        here = pl.ds(pl.multiple_of((meta_ref[1] ^ side) * rows, rows), rows)
        for s in range(4):
            block = own_ref[here, :] if s == 0 else ref[0, s - 1].astype(jnp.bfloat16)
            plain_ref[here, s * width : (s + 1) * width] = block
            pad_ref[here, s * wide : (s + 1) * wide] = dot32(block, p_ref[...]).astype(
                jnp.bfloat16
            )


def spread_qkv_kernel(own_ref, pq_ref, pkv_ref, far_ref, out_ref):
    parts, others, rows, width = far_ref.shape
    wide = own_ref.shape[1]
    split = pq_ref.shape[0]
    out_ref[:, :wide] = own_ref[...]
    for s in range(others):
        block = far_ref[:, s].reshape(parts * rows, width).astype(jnp.bfloat16)
        query = dot32(block[:, :split], pq_ref[...]).astype(jnp.bfloat16)
        key_value = dot32(block[:, split:], pkv_ref[...]).astype(jnp.bfloat16)
        store_qkv(out_ref, slice(None), (s + 1) * wide, query, key_value)


def spread_qkv(own, pq, pkv, far):
    total, wide = own.shape
    dp, others, rows, width = far.shape
    parts = max(1, dp // 4)
    block = parts * rows
    return pl.pallas_call(
        spread_qkv_kernel,
        out_shape=jax.ShapeDtypeStruct((total, (others + 1) * wide), jnp.bfloat16),
        grid=(total // block,),
        in_specs=[
            pl.BlockSpec((block, wide), lambda i: (i, 0)),
            whole(pq),
            whole(pkv),
            pl.BlockSpec((parts, others, rows, width), lambda i: (i, 0, 0, 0)),
        ],
        out_specs=pl.BlockSpec((block, (others + 1) * wide), lambda i: (i, 0)),
        compiler_params=params(),
        cost_estimate=cost(8 * total * width * 512, 20 * total * wide),
    )(own, pq, pkv, far)


def spread(kernel, meta, own, places, mine, theirs, widths):
    chips, others, rows, width = mine.shape
    total = own.shape[0]
    row_block = lambda m, meta: (meta[0] ^ m, 0)
    piece = pl.BlockSpec((1, others, rows, width), lambda m, meta: (m, 0, 0, 0))
    return pl.pallas_call(
        kernel,
        out_shape=[jax.ShapeDtypeStruct((total, wide), jnp.bfloat16) for wide in widths],
        grid_spec=pltpu.PrefetchScalarGridSpec(
            num_scalar_prefetch=1,
            grid=(chips,),
            in_specs=[pl.BlockSpec((2 * rows, own.shape[1]), row_block)]
            + [whole(place) for place in places]
            + [piece, piece],
            out_specs=[pl.BlockSpec((2 * rows, wide), row_block) for wide in widths],
        ),
        compiler_params=params(),
        cost_estimate=cost(
            8 * total * width * 512, total * (12 * width + 2 * sum(widths))
        ),
    )(meta, own, *places, mine, theirs)


def start_kernel(x_ref, gain_ref, q_ref, k_ref, v_ref, pq_ref, pkv_ref, cos_ref, sin_ref, *outs):
    qkv_ref, normed_ref, pad_ref = outs

    @pl.when(pl.program_id(0) == 0)
    def _():
        split = k_ref.shape[0]
        query = dot32(q_ref[...], pq_ref[...]).astype(jnp.bfloat16)
        key_value = dot32(k_ref[...].T, pkv_ref[:split, :])
        key_value = key_value + dot32(v_ref[...].T, pkv_ref[split:, :])
        store_qkv(pad_ref, slice(None), 0, query, key_value.astype(jnp.bfloat16))

    inputs = x_ref[...].astype(jnp.float32)
    rms = lax.rsqrt(jnp.mean(inputs * inputs, -1, keepdims=True) + norm_eps)
    normed = (inputs * rms * gain_ref[...]).astype(jnp.bfloat16)
    normed_ref[...] = normed
    for kv in range(pad_ref.shape[1] // KV_WIDE):
        at = kv * KV_WIDE
        store_turned(qkv_ref, at, dot32(normed, pad_ref[:, at : at + KV_WIDE]), cos_ref, sin_ref)


def start(tokens, gain, w_query, w_key_t, w_value_t, pq, pkv, cosines, sines):
    total, depth = tokens.shape
    rows = total // CHUNKS
    wide = pq.shape[1] + pkv.shape[1]
    gain = gain[None, :]
    by_rows = lambda width: pl.BlockSpec((rows, width), lambda i: (i, 0))
    arrays = [w_query, w_key_t, w_value_t, pq, pkv]
    shapes = [
        jax.ShapeDtypeStruct((total, wide), jnp.bfloat16),
        jax.ShapeDtypeStruct((total, depth), jnp.bfloat16),
        jax.ShapeDtypeStruct((depth, wide), jnp.bfloat16),
    ]
    return pl.pallas_call(
        start_kernel,
        out_shape=shapes,
        grid=(CHUNKS,),
        in_specs=[by_rows(depth), whole(gain)]
        + [whole(array) for array in arrays]
        + [by_rows(LANES), by_rows(LANES)],
        out_specs=[by_rows(wide), by_rows(depth), whole(shapes[2])],
        compiler_params=params(),
        cost_estimate=cost(2 * total * depth * wide, 12 * total * depth),
    )(tokens, gain, *arrays, cosines, sines)


def turn_kernel(length_ref, cot_ref, normed_ref, dout_ref, dout_t_ref, normed_t_ref):
    rows = cot_ref.shape[0]
    at = pl.program_id(0) * rows + lax.broadcasted_iota(jnp.int32, cot_ref.shape, 0)
    dout = jnp.where(at < length_ref[0], cot_ref[...].astype(jnp.float32), 0.0)
    dout = dout.astype(jnp.bfloat16)
    dout_ref[...] = dout
    dout_t_ref[...] = dout.T
    normed_t_ref[...] = normed_ref[...].T


def turn(length, cotangent, normed):
    total, depth = cotangent.shape
    rows = total // CHUNKS
    by_rows = pl.BlockSpec((rows, depth), lambda i: (i, 0))
    by_columns = pl.BlockSpec((depth, rows), lambda i: (0, i))
    turned = jax.ShapeDtypeStruct((depth, total), jnp.bfloat16)
    return pl.pallas_call(
        turn_kernel,
        out_shape=[jax.ShapeDtypeStruct((total, depth), jnp.bfloat16), turned, turned],
        grid=(CHUNKS,),
        in_specs=[SCALAR, by_rows, by_rows],
        out_specs=[by_rows, by_columns, by_columns],
        compiler_params=params(),
        cost_estimate=cost(total * depth, 10 * total * depth),
    )(length, cotangent, normed)


def project_kernel(x_ref, w_ref, cos_ref, sin_ref, out_ref):
    store_turned(out_ref, 0, dot32(x_ref[...], w_ref[...]), cos_ref, sin_ref)


def project(normed, weights, cosines, sines):
    rows, depth = normed.shape
    width = weights.shape[1]
    return pl.pallas_call(
        project_kernel,
        out_shape=jax.ShapeDtypeStruct((rows, width), jnp.bfloat16),
        grid=(width // KV_WIDE,),
        in_specs=[
            whole(normed),
            pl.BlockSpec((depth, KV_WIDE), lambda i: (0, i)),
            whole(cosines),
            whole(sines),
        ],
        out_specs=pl.BlockSpec((rows, KV_WIDE), lambda i: (0, i)),
        compiler_params=params(),
        cost_estimate=cost(
            2 * rows * depth * width, 2 * (rows * depth + depth * width + rows * width)
        ),
    )(normed, weights, cosines, sines)


def attend_kernel(start, length_ref, q_ref, kv_ref, strip_ref, out_ref):
    rows = q_ref.shape[0]
    keys = kv_ref.shape[0]
    length = length_ref[0]
    row_ids = start + lax.broadcasted_iota(jnp.int32, (1, rows), 1)
    limit = jnp.minimum(row_ids, length - 1)
    allowed = lax.broadcasted_iota(jnp.int32, (keys, rows), 0) <= limit
    mixed = []
    sums = []
    for kv in range(kv_ref.shape[1] // KV_WIDE):
        base = kv * KV_WIDE
        at = base + GROUP * LANES
        key = kv_ref[:, at : at + LANES]
        value_t = kv_ref[:, at + LANES : at + 2 * LANES].T
        for g in range(GROUP):
            query = q_ref[:, base + g * LANES : base + (g + 1) * LANES]
            raw = jnp.where(allowed, dot32_nt(key, query), masked_score)
            peak = jnp.max(raw, axis=0, keepdims=True)
            expo = jnp.exp2((raw - peak) * score_scale_log2)
            total = jnp.sum(expo, axis=0, keepdims=True)
            probs = (expo * (1.0 / total)).astype(jnp.bfloat16)
            mixed.append(dot32(value_t, probs).T)
            log_sum = peak * score_scale_log2 + jnp.log2(total)
            sums.append(jnp.where(row_ids < length, log_sum, far_away))
    out_ref[:rows, :] = dot_split(jnp.concatenate(mixed, 1), strip_ref[...])
    out_ref[rows:, :] = jnp.zeros((EXTRA, out_ref.shape[1]), jnp.float32)
    out_ref[rows : rows + len(sums), :rows] = jnp.concatenate(sums, 0)


def attend(length, qkv, strip, index, rows):
    keys = (index + 1) * rows
    width = qkv.shape[1]
    heads = width // KV_WIDE * GROUP
    shape = (rows + EXTRA, strip.shape[1])
    return pl.pallas_call(
        functools.partial(attend_kernel, index * rows),
        out_shape=jax.ShapeDtypeStruct(shape, jnp.float32),
        grid=(1,),
        in_specs=[
            SCALAR,
            pl.BlockSpec((rows, width), lambda i: (index, 0)),
            pl.BlockSpec((keys, width), lambda i: (0, 0)),
            whole(strip),
        ],
        out_specs=pl.BlockSpec(shape, lambda i: (0, 0)),
        compiler_params=params(),
        cost_estimate=cost(
            4 * heads * rows * keys * LANES, 2 * (rows + keys) * width, heads * rows * keys
        ),
    )(length, qkv, qkv, strip)


def forward_kernel(level_ref, part_ref, other_ref, across_ref, outer_ref, *refs):
    x_ref, dout_ref, wo_ref, gain_ref, wg_ref, wu_ref, wd_ref = refs[:7]
    hidden_ref, normed_t_ref, activ_ref, dgate_ref, dup_ref, mlp_ref, dn_ref = refs[7:14]
    normed_ref = refs[14]
    rows = x_ref.shape[0]

    @pl.when(pl.program_id(0) == 0)
    def _():
        level = level_ref[0]
        inner = (level == 1) | (level == 2)
        width = part_ref.shape[1]
        second = jnp.where(inner, across_ref[:rows, width:], outer_ref[:rows, :width])
        third = jnp.where(inner, across_ref[:rows, :width], outer_ref[:rows, width:])
        mixed = jnp.concatenate([part_ref[:rows, :], other_ref[:rows, :], second, third], 1)
        hidden = x_ref[...].astype(jnp.float32) + dot32_nt(mixed.astype(jnp.bfloat16), wo_ref[...])
        hidden_ref[...] = hidden
        rms = lax.rsqrt(jnp.mean(hidden * hidden, -1, keepdims=True) + norm_eps)
        normed = (hidden * rms * gain_ref[...]).astype(jnp.bfloat16)
        normed_ref[...] = normed
        normed_t_ref[...] = normed.T
        mlp_ref[...] = jnp.zeros_like(mlp_ref)
        dn_ref[...] = jnp.zeros_like(dn_ref)

    normed = normed_ref[...]
    gate = dot32(normed, wg_ref[...])
    up = dot32(normed, wu_ref[...])
    dact = dot32_nt(dout_ref[...], wd_ref[...])
    sigmoid = jax.nn.sigmoid(gate)
    silu = gate * sigmoid
    activ = (silu * up).astype(jnp.bfloat16)
    dgate = (dact * up * sigmoid * (1.0 + gate * (1.0 - sigmoid))).astype(jnp.bfloat16)
    dup = (dact * silu).astype(jnp.bfloat16)
    activ_ref[...] = activ
    dgate_ref[...] = dgate
    dup_ref[...] = dup
    mlp_ref[...] += dot32(activ, wd_ref[...])
    dn_ref[...] += dot32_nt(dgate, wg_ref[...]) + dot32_nt(dup, wu_ref[...])


def forward_chunk(level, gathered, tokens, dout, w_out, gain, w_gate, w_up, w_down, index, rows):
    depth = tokens.shape[1]
    units = w_gate.shape[1]
    block = 512
    own_rows = pl.BlockSpec((rows, depth), lambda i: (index, 0))
    by_units = pl.BlockSpec((depth, block), lambda i: (0, i))
    gain = gain[None, :]
    f32, bf16 = jnp.float32, jnp.bfloat16
    outs = [
        jax.ShapeDtypeStruct((rows, depth), f32),
        jax.ShapeDtypeStruct((depth, rows), bf16),
        jax.ShapeDtypeStruct((rows, units), bf16),
        jax.ShapeDtypeStruct((rows, units), bf16),
        jax.ShapeDtypeStruct((rows, units), bf16),
        jax.ShapeDtypeStruct((rows, depth), f32),
        jax.ShapeDtypeStruct((rows, depth), f32),
    ]
    unit_out = pl.BlockSpec((rows, block), lambda i: (0, i))
    return pl.pallas_call(
        forward_kernel,
        out_shape=outs,
        grid=(units // block,),
        in_specs=[SCALAR]
        + [whole(array) for array in gathered]
        + [own_rows, own_rows, whole(w_out), whole(gain), by_units, by_units]
        + [pl.BlockSpec((block, depth), lambda i: (i, 0))],
        out_specs=[
            whole(outs[0]),
            whole(outs[1]),
            unit_out,
            unit_out,
            unit_out,
            whole(outs[5]),
            whole(outs[6]),
        ],
        scratch_shapes=[pltpu.VMEM((rows, depth), bf16)],
        compiler_params=params(),
        cost_estimate=cost(
            2 * rows * depth * (6 * units + w_out.shape[1]),
            2 * depth * (3 * units + w_out.shape[1]) + 22 * rows * depth,
            rows * units,
        ),
    )(level, *gathered, tokens, dout, w_out, gain, w_gate, w_up, w_down)


def hidden_grad(inner, total_ref, final_ref, hidden_ref, dout_ref, gain_ref):
    dnormed = jnp.where(inner, total_ref[...], final_ref[...])
    hidden = hidden_ref[...]
    rms = lax.rsqrt(jnp.mean(hidden * hidden, -1, keepdims=True) + norm_eps)
    scaled = dnormed * gain_ref[...]
    shift = jnp.mean(scaled * hidden, -1, keepdims=True)
    dhid = dout_ref[...].astype(jnp.float32) + (rms * scaled - hidden * (rms**3 * shift))
    return dhid, dnormed * (hidden * rms)


def backward_kernel(start, full, level_ref, total_ref, final_ref, hidden_ref, dout_ref, x_ref, *refs):
    gain_one_ref, gain_two_ref, wo_ref, q_ref = refs[:4]
    kv_here = q_ref.shape[1] // KV_WIDE
    refs = refs[4:]
    kv_refs, refs = refs[: 2 * kv_here], refs[2 * kv_here :]
    part_ref, other_ref, across_ref, outer_ref, place_ref, strip_ref = refs[:6]
    cos_ref, sin_ref = refs[6:8]
    dhid_ref, low_ref, dn_ref = refs[-3:]
    outs = refs[8:-3]
    if full:
        w_ref, outs = outs[0], outs[1:]
    count = (5 if start > 0 else 4) if full else 2
    acc_ref = outs[0] if len(outs) > count else None
    outs = outs[-count:]
    dhid_t_ref, dqkv_ref = outs[:2]
    if full:
        input_grad_ref, gains_ref = outs[2:4]
    rows = q_ref.shape[0]
    keys = kv_refs[0].shape[0]
    shard = pl.program_id(0)
    level = level_ref[0]
    inner = (level == 1) | (level == 2)

    @pl.when(shard == 0)
    def _():
        dhid, dgain = hidden_grad(
            inner, total_ref, final_ref, hidden_ref, dout_ref, gain_two_ref
        )
        dhid_ref[...] = dhid
        low = dhid.astype(jnp.bfloat16)
        low_ref[...] = low
        dhid_t_ref[...] = low.T
        if full:
            gains_ref[...] = jnp.zeros_like(gains_ref)
            gains_ref[1:2, :] = jnp.sum(dgain, 0, keepdims=True)
            dn_ref[...] = jnp.zeros_like(dn_ref)

    def rotate_back(grads):
        turned = grads * cos_ref[...] - pltpu.roll(grads, LANES // 2, 1) * sin_ref[...]
        return turned.astype(jnp.bfloat16)

    dmixed_all = dot32(low_ref[...], wo_ref[...]).astype(jnp.bfloat16)
    mixed = jnp.where(
        shard == 0,
        part_ref[...],
        jnp.where(shard == 1, other_ref[...], jnp.where(inner, across_ref[...], outer_ref[...])),
    )
    products = dmixed_all.astype(jnp.float32) * dot_split(mixed[:rows], place_ref[...])
    causal = lax.broadcasted_iota(jnp.int32, (rows, rows), 0) <= lax.broadcasted_iota(
        jnp.int32, (rows, rows), 1
    )
    grads = []
    for kv in range(kv_here):
        key_ref, value_ref = kv_refs[2 * kv : 2 * kv + 2]
        heads = range(kv * GROUP, (kv + 1) * GROUP)
        lanes = {h: slice(h * LANES, (h + 1) * LANES) for h in heads}
        row_dots = {h: jnp.sum(products[:, lanes[h]].T, axis=0, keepdims=True) for h in heads}
        log_sums = {h: mixed[rows + h : rows + h + 1, :rows] for h in heads}
        dqueries = dict.fromkeys(heads)
        here = slice(2 * kv * LANES, (2 * kv + 1) * LANES)
        there = slice((2 * kv + 1) * LANES, (2 * kv + 2) * LANES)
        for tile in range(keys // rows):
            span = slice(tile * rows, (tile + 1) * rows)
            key = key_ref[span, :]
            value = value_ref[span, :]
            key_t = key.T
            dkey = None if acc_ref is None else acc_ref[span, here]
            dvalue = None if acc_ref is None else acc_ref[span, there]
            last = tile * rows == start
            for h in heads:
                at = kv * KV_WIDE + (h % GROUP) * LANES
                query = q_ref[:, at : at + LANES]
                dmixed = dmixed_all[:, lanes[h]]
                raw = dot32_nt(key, query)
                probs = jnp.exp2(raw * score_scale_log2 - log_sums[h])
                if last:
                    probs = jnp.where(causal, probs, 0.0)
                dprobs = dot32_nt(value, dmixed)
                dscores = (probs * (dprobs - row_dots[h])).astype(jnp.bfloat16)
                dquery = dot32(key_t, dscores)
                dqueries[h] = dquery if dqueries[h] is None else dqueries[h] + dquery
                dkey_one = dot32(dscores, query)
                dvalue_one = dot32(probs.astype(jnp.bfloat16), dmixed)
                dkey = dkey_one if dkey is None else dkey + dkey_one
                dvalue = dvalue_one if dvalue is None else dvalue + dvalue_one
            if full and not last:
                outs[4][span, here] = dkey
                outs[4][span, there] = dvalue
        grads += [rotate_back(dqueries[h].T * score_scale) for h in heads]
        grads.append(rotate_back(dkey * score_scale))
        grads.append(dvalue.astype(jnp.bfloat16))
    grads = jnp.concatenate(grads, 1)
    if full:
        dn_ref[...] += dot32_nt(grads, w_ref[...])

    @pl.when(shard == 0)
    def _():
        wide = strip_ref.shape[1]
        for kv in range(kv_here):
            dqkv_ref[:, kv * wide : (kv + 1) * wide] = dot32(
                grads[:, kv * KV_WIDE : (kv + 1) * KV_WIDE], strip_ref[...]
            ).astype(jnp.bfloat16)

    if not full:
        return

    @pl.when(shard == pl.num_programs(0) - 1)
    def _():
        dnormed = dn_ref[...]
        inputs = x_ref[...].astype(jnp.float32)
        rms = lax.rsqrt(jnp.mean(inputs * inputs, -1, keepdims=True) + norm_eps)
        scaled = dnormed * gain_one_ref[...]
        shift = jnp.mean(scaled * inputs, -1, keepdims=True)
        grad = dhid_ref[...] + (rms * scaled - inputs * (rms**3 * shift))
        input_grad_ref[...] = grad.astype(jnp.bfloat16)
        gains_ref[0:1, :] = jnp.sum(dnormed * (inputs * rms), 0, keepdims=True)


def backward_chunk(
    level, sums_two, hidden, dout, tokens, gains, weights, qkv, gathered, places, tables, acc,
    index, rows, full=True
):
    start = index * rows
    keys = start + rows
    depth = tokens.shape[1]
    out_pad, qkv_pad = weights
    place_out, strip = places
    far_rows, width = gathered[0].shape
    out_wide = place_out.shape[1]
    kv_here = out_wide // (GROUP * LANES)
    wide = kv_here * KV_WIDE
    levels = qkv.shape[1] // wide
    own_rows = pl.BlockSpec((rows, depth), lambda t: (index, 0))
    table = pl.BlockSpec((rows, LANES), lambda t: (index, 0))
    gains = [gain[None, :] for gain in gains]
    key_value = lambda at: pl.BlockSpec(
        (keys, LANES), lambda t: (0, (wide // LANES) * t + at)
    )
    across = pl.BlockSpec((far_rows, width), lambda t: (0, jnp.where(t == 2, 1, 0)))
    outer = pl.BlockSpec((far_rows, width), lambda t: (0, jnp.where(t == 3, 1, 0)))
    in_specs = [
        SCALAR,
        whole(sums_two[0]),
        whole(sums_two[1]),
        whole(hidden),
        own_rows,
        own_rows,
        whole(gains[0]),
        whole(gains[1]),
        pl.BlockSpec((depth, out_wide), lambda t: (0, t)),
        pl.BlockSpec((rows, wide), lambda t: (index, t)),
    ]
    for kv in range(kv_here):
        at = kv * (KV_WIDE // LANES) + GROUP
        in_specs += [key_value(at), key_value(at + 1)]
    in_specs += [
        whole(gathered[0]),
        whole(gathered[1]),
        across,
        outer,
        whole(place_out),
        whole(strip),
        table,
        table,
    ]
    args = [level, *sums_two, hidden, dout, tokens, *gains, out_pad]
    args += [qkv] * (1 + 2 * kv_here)
    args += [*gathered, place_out, strip, *tables]
    sums_wide = 2 * kv_here * LANES
    if full:
        in_specs.append(pl.BlockSpec((depth, wide), lambda t: (0, t)))
        args.append(qkv_pad)
    if acc is not None:
        in_specs.append(pl.BlockSpec((keys, sums_wide), lambda t: (0, t)))
        args.append(acc)
    f32, bf16 = jnp.float32, jnp.bfloat16
    outs = [
        jax.ShapeDtypeStruct((depth, rows), bf16),
        jax.ShapeDtypeStruct((rows, kv_here * strip.shape[1]), bf16),
        jax.ShapeDtypeStruct((rows, depth), bf16),
        jax.ShapeDtypeStruct((8, depth), f32),
    ]
    outs = outs if full else outs[:2]
    out_specs = [whole(out) for out in outs]
    if full and start > 0:
        outs.append(jax.ShapeDtypeStruct((start, levels * sums_wide), f32))
        out_specs.append(pl.BlockSpec((start, sums_wide), lambda t: (0, t)))
    results = pl.pallas_call(
        functools.partial(backward_kernel, start, full),
        out_shape=outs,
        grid=(levels if full else 1,),
        in_specs=in_specs,
        out_specs=out_specs,
        scratch_shapes=[
            pltpu.VMEM((rows, depth), f32),
            pltpu.VMEM((rows, depth), bf16),
            pltpu.VMEM((rows, depth), f32),
        ],
        compiler_params=params(),
        cost_estimate=cost(
            levels * rows * (20 * kv_here * keys * LANES + 2 * depth * (out_wide + wide)),
            2 * depth * levels * (out_wide + wide) + 16 * rows * depth,
            levels * kv_here * GROUP * rows * keys,
        ),
    )(*args)
    return results[:4], (results[4] if full and start > 0 else None)


def rows_kernel(lefts, groups, adding, picked, side_ref, *refs):
    refs = list(refs)
    held_ref = refs.pop()
    out_refs = refs[-len(picked) :]
    refs = refs[: -len(picked)]
    recv_ref = refs.pop() if adding else None
    step = pl.program_id(0)
    left_refs = []
    for count in lefts:
        left_refs.append(refs[:count])
        refs = refs[count:]
    rights = []
    for _ in groups:
        rights.append(refs[:CHUNKS])
        refs = refs[CHUNKS:]
    rows = left_refs[0][0].shape[0]
    blocks = held_ref.shape[1] // rows

    @pl.when(step == 0)
    def _():
        for which, pieces in enumerate(left_refs):
            for n, ref in enumerate(pieces):
                m, j = n % blocks, n // blocks
                wide = ref.shape[1]
                held_ref[which, m * rows : (m + 1) * rows, j * wide : (j + 1) * wide] = ref[...]

    chunk = held_ref.shape[2] // CHUNKS
    for group, (left, first, steps) in zip(rights, groups):

        @pl.when((step >= first) & (step < first + steps))
        def _(group=group, left=left):
            right = jnp.concatenate([ref[:chunk, :].astype(jnp.bfloat16) for ref in group], 0)
            total = dot32(held_ref[left], right)
            if recv_ref is not None:
                total = total + recv_ref[...]
            for out_ref, parts in zip(out_refs, picked):
                at = 0
                for start, size in parts:
                    out_ref[at : at + size, :] = total[start : start + size]
                    at += size


def rows_of(lefts, groups, side, rows, blocks, step, recv=None, picked=None):
    if picked is None:
        picked = [[(0, rows * blocks)]]
    at = lambda m: lambda i, side: ((m ^ side[2]) * side[1] + side[0], 0)
    specs = []
    args = []
    counts = []
    for left in lefts:
        pieces = left if isinstance(left, list) else [left]
        counts.append(len(pieces) * blocks)
        for piece in pieces:
            for m in range(blocks):
                specs.append(pl.BlockSpec((rows, piece.shape[1]), at(m)))
                args.append(piece)
    tokens = sum(piece.shape[1] for piece in pieces)
    first = 0
    plan = []
    for which, rights in groups:
        steps = rights[0].shape[1] // step
        plan.append((which, first, steps))
        for right in rights:
            pick = lambda i, side, first=first, steps=steps: (0, jnp.clip(i - first, 0, steps - 1))
            specs.append(pl.BlockSpec((right.shape[0], step), pick))
            args.append(right)
        first += steps
    total = first * step
    block = lambda height: pl.BlockSpec((height, step), lambda i, side: (0, i))
    if recv is not None:
        specs.append(block(rows * blocks))
        args.append(recv)
    heights = [sum(size for _, size in parts) for parts in picked]
    results = pl.pallas_call(
        functools.partial(rows_kernel, counts, plan, recv is not None, picked),
        out_shape=[jax.ShapeDtypeStruct((height, total), jnp.float32) for height in heights],
        grid_spec=pltpu.PrefetchScalarGridSpec(
            num_scalar_prefetch=1,
            grid=(first,),
            in_specs=specs,
            out_specs=[block(height) for height in heights],
            scratch_shapes=[pltpu.VMEM((len(lefts), rows * blocks, tokens), jnp.bfloat16)],
        ),
        compiler_params=params(),
        cost_estimate=cost(
            2 * rows * blocks * tokens * total,
            4 * rows * blocks * total + 2 * tokens * (total + rows * blocks),
        ),
    )(side, *args)
    return results[0] if len(picked) == 1 else results


def shards(
    tokens,
    lengths,
    positions,
    cotangent,
    norm_gain,
    w_query,
    w_key,
    w_value,
    w_out,
    mlp_gain,
    w_gate,
    w_up,
    w_down,
):
    seq_rows, depth = tokens.shape
    chips = lax.axis_size("chip")
    dp = chips * 2
    tp = lax.axis_size("tp")
    chip = lax.axis_index("chip")
    core = lax.axis_index("core")
    level = lax.axis_index("tp")
    low = level < 2
    inner = (level == 1) | (level == 2)
    heads_here = w_query.shape[1] // HD
    kv_here = w_key.shape[1] // HD
    rows = seq_rows // CHUNKS
    slice_rows = depth // dp
    level_ref = level.astype(jnp.int32).reshape(1)
    by_hand = dp == 8
    swap = lambda array: lax.ppermute(array, "core", [(0, 1), (1, 0)])
    to_level = lambda array, s: along(array, [(t, t ^ s) for t in range(tp)])

    at_row = (chip * 2 + core) * slice_rows
    cols = lambda w: lax.dynamic_slice_in_dim(w, at_row, slice_rows, 1).astype(jnp.float32).T
    (out_slice,) = fence(cols(w_out))
    qkv_slice = jnp.concatenate(
        [
            lax.dynamic_slice_in_dim(w_query, at_row, slice_rows, 0).astype(jnp.float32),
            cols(w_key.T),
            cols(w_value.T),
        ],
        1,
    )
    out_slice, qkv_slice = fence(out_slice, qkv_slice)
    out_near = along(out_slice, PAIRS)
    qkv_near = along(qkv_slice, PAIRS)
    meta = jnp.stack([chip, core]).astype(jnp.int32)

    pq = place_query(heads_here)
    pkv = place_key_value(kv_here)
    p_all = place_all(heads_here, kv_here)
    strip_one = place_all(GROUP, 1).T
    p_out = place_plain(heads_here)
    strip_out = p_out.T

    half_dim = HD // 2
    freqs = rope_base ** (-(jnp.arange(half_dim).astype(jnp.float32) * 2.0 / HD))
    freqs = jnp.pad(freqs, (0, LANES // 2 - half_dim))
    angles = positions.astype(jnp.float32)[:, None] * jnp.concatenate([freqs, freqs])[None, :]
    cosines = jnp.cos(angles)
    sines = jnp.sin(angles) * jnp.where(jnp.arange(LANES) < LANES // 2, -1.0, 1.0)

    cosines, sines, out_near = fence(cosines, sines, out_near)
    out_across = along(jnp.stack([out_slice, out_near]), MIDDLE)
    qkv_own, normed_one, own_pad = start(
        tokens, norm_gain, w_query, w_key.T, w_value.T, pq, pkv, cosines, sines
    )

    def far_slices(near, across, outer):
        return jnp.stack(
            [
                near,
                jnp.where(inner, across[1], outer[0]),
                jnp.where(inner, across[0], outer[1]),
            ]
        )

    order = list(reversed(range(CHUNKS)))
    c0, c1, c2, c3 = order
    own, other, across, outer = {}, {}, {}, {}
    part, total, final = {}, {}, {}

    def hop_1(j):
        other[j] = along(own[j], PAIRS)

    def hop_2(j):
        across[j] = along(jnp.concatenate([own[j], other[j]], 1), MIDDLE)

    def hop_3(j):
        outer[j] = along(across[j], OUTWARD)

    coming = {}

    def add_1(j):
        coming[j] = along(part[j], INWARD)

    def add_2(j):
        total[j] = part[j] + coming[j]
        coming[j] = along(total[j], MIDDLE)

    def add_3(j):
        total[j] = total[j] + coming[j]
        final[j] = along(total[j], OUTWARD)

    def to_chip(array, m):
        return lax.ppermute(array, "chip", [(i, i ^ m) for i in range(chips)])

    def over_chips_1(piece):
        cut = piece.shape[1] // 2
        one, two = piece[:, :cut], piece[:, cut:]
        return jnp.stack([one, to_chip(one, 1)]), jnp.stack([two, to_chip(two, 2)])

    def over_chips_2(one, two):
        return one, to_chip(one, 2), two, to_chip(two, 1)

    def over_chips_3(one, one_far, two, two_far):
        upper = jnp.stack([one[0], one[1], one_far[0], one_far[1]])
        lower = jnp.stack([two[0], two_far[0], two[1], two_far[1]])
        return jnp.concatenate([upper, lower], 2)

    qkv_own, out_across, qkv_near = fence(qkv_own, out_across, qkv_near)
    out_outer = along(out_across, OUTWARD)
    qkv_across = along(jnp.stack([qkv_slice, qkv_near]), MIDDLE)
    own[c0] = attend(lengths, qkv_own, strip_out, c0, rows)
    own, qkv_own, out_outer = fence(own, qkv_own, out_outer)
    hop_1(c0)
    out_far = far_slices(out_near, out_across, out_outer)
    out_mine = over_chips_1(out_far) if by_hand else out_far
    for j in (c1, c2):
        own[j] = attend(lengths, qkv_own, strip_out, j, rows)
    own, other, normed_one, w_out, out_mine, qkv_across, qkv_own = fence(
        own, other, normed_one, w_out, out_mine, qkv_across, qkv_own
    )
    own[c3] = attend(lengths, qkv_own, strip_out, c3, rows)
    if by_hand:
        out_mine = over_chips_2(*out_mine)
    else:
        out_mine = lax.all_gather(out_mine, ("chip", "core"))
    qkv_outer = along(qkv_across, OUTWARD)
    hop_2(c0)
    hop_1(c1)
    dout, dout_t, normed_one_t = turn(lengths, cotangent, normed_one)
    w_out_t = w_out.T
    own, other, across, dout, dout_t, normed_one_t, w_out_t, out_mine, qkv_outer = fence(
        own, other, across, dout, dout_t, normed_one_t, w_out_t, out_mine, qkv_outer
    )
    hop_3(c0)
    hop_2(c1)
    hop_1(c2)
    hop_1(c3)
    qkv_far = lax.all_gather(far_slices(qkv_near, qkv_across, qkv_outer), ("chip", "core"))
    if by_hand:
        out_mine = over_chips_3(*out_mine)
        out_theirs = swap(out_mine)
        out_pad, out_plain = spread(
            spread_out_kernel,
            meta,
            w_out_t,
            [p_out],
            out_mine,
            out_theirs,
            [4 * p_out.shape[1], 4 * p_out.shape[0]],
        )
    else:
        plain = [w_out_t] + [
            out_mine[:, s].reshape(depth, -1).astype(jnp.bfloat16) for s in range(tp - 1)
        ]
        out_plain = jnp.concatenate(plain, 1)
        out_pad = jnp.concatenate([dot32(w, p_out).astype(jnp.bfloat16) for w in plain], 1)
    hidden, normed_t, activ, dgate, dup, mlp_part = {}, {}, {}, {}, {}, {}

    def feed(j):
        gathered = (own[j], other[j], across[j], outer[j])
        (hidden[j], normed_t[j], activ[j], dgate[j], dup[j], mlp_part[j], part[j]) = forward_chunk(
            level_ref, gathered, tokens, dout, out_plain, mlp_gain, w_gate, w_up, w_down, j, rows
        )

    feed(c0)
    own, other, across, outer, part, hidden = fence(own, other, across, outer, part, hidden)
    add_1(c0)
    hop_3(c1)
    hop_2(c2)
    hop_2(c3)
    feed(c1)
    own, other, across, outer, part, total, coming, hidden = fence(
        own, other, across, outer, part, total, coming, hidden
    )
    add_2(c0)
    add_1(c1)
    hop_3(c2)
    hop_3(c3)
    qkv_far, part = fence(qkv_far, part)
    qkv_pad = spread_qkv(own_pad, pq, pkv, qkv_far)
    feed(c2)
    own, other, across, outer, part, total, coming, hidden, qkv_pad = fence(
        own, other, across, outer, part, total, coming, hidden, qkv_pad
    )
    add_3(c0)
    add_2(c1)
    add_1(c2)
    qkv = project(normed_one, qkv_pad, cosines, sines)
    feed(c3)

    listed = lambda pieces: [pieces[j] for j in range(CHUNKS)]
    keep_side = jnp.stack([core, 2, 0]).astype(jnp.int32)
    keep_turned = jnp.stack([core, 2, chip]).astype(jnp.int32)
    send_side = jnp.stack([1 - core, 2, 0]).astype(jnp.int32)
    send_turned = jnp.stack([1 - core, 2, chip]).astype(jnp.int32)
    all_rows = jnp.array([0, 1, 0], jnp.int32)

    def send_rows(lefts, groups, step, side=send_side):
        if not by_hand:
            return rows_of(lefts, groups, all_rows, depth // 4, 4, step)
        return rows_of(lefts, groups, side, slice_rows, chips, step)

    def keep_rows(lefts, groups, received, step, side=keep_side, picked=None):
        if not by_hand:
            return received
        return rows_of(lefts, groups, side, slice_rows, chips, step, received, picked)

    def swap_rows(array):
        return swap(array) if by_hand else array

    def scatter(array):
        axes = "chip" if by_hand else ("chip", "core")
        return lax.psum_scatter(array, axes, scatter_dimension=0, tiled=True)

    units = w_gate.shape[1]
    mlp_args = (
        [listed(normed_t), dout_t],
        [(0, listed(dgate)), (0, listed(dup)), (1, listed(activ))],
    )
    acc = None
    dhid_t, dqkv_own, input_grad, gains = {}, {}, {}, {}

    def back(j):
        nonlocal acc
        (dhid_t[j], dqkv_own[j], input_grad[j], gains[j]), acc = back_some(j, True)

    def back_own(j):
        return back_some(j, False)[0]

    def back_some(j, full):
        return backward_chunk(
            level_ref,
            (total[j], final[j]),
            hidden[j],
            dout,
            tokens,
            (norm_gain, mlp_gain),
            (out_pad, qkv_pad),
            qkv,
            (own[j], other[j], across[j], outer[j]),
            (p_out, strip_one),
            (cosines, sines),
            acc,
            j,
            rows,
            full,
        )

    own, other, across, outer, part, total, coming, final, hidden, mlp_in, qkv = fence(
        own, other, across, outer, part, total, coming, final, hidden,
        (normed_t, activ, dgate, dup), qkv,
    )
    normed_t, activ, dgate, dup = mlp_in
    add_3(c1)
    add_2(c2)
    add_1(c3)
    units = w_gate.shape[1]
    mlp_args = (
        [listed(normed_t), dout_t],
        [(0, listed(dgate)), (0, listed(dup)), (1, listed(activ))],
    )
    sent = swap_rows(send_rows(*mlp_args, units // 2))
    back(c0)

    near = lambda: jnp.where(low, mlp_part[1], mlp_part[2])
    edge = lambda: jnp.where(low, mlp_part[0], mlp_part[3])
    total, coming, final, hidden, mlp_part, acc, dhid_t, sent = fence(
        total, coming, final, hidden, mlp_part, acc, dhid_t, sent
    )
    add_3(c2)
    add_2(c3)
    leave_far = jnp.where(low, mlp_part[3], mlp_part[0])
    leave_near = jnp.where(low, mlp_part[2], mlp_part[1])
    far_sum = along(leave_far, INWARD)
    grad_mlp = keep_rows(*mlp_args, sent, units // 2)
    hidden, grad_mlp = fence(hidden, grad_mlp)
    grad_mlp = scatter(grad_mlp)
    back(c1)
    total, coming, final, hidden, mlp_part, far_sum, acc, dhid_t = fence(
        total, coming, final, hidden, mlp_part, far_sum, acc, dhid_t
    )
    add_3(c3)
    near_sum = along(leave_near, INWARD)
    far_in = along(leave_far + far_sum, MIDDLE)
    back(c2)
    total, final, hidden, mlp_part, near_sum, far_in, acc, dhid_t = fence(
        total, final, hidden, mlp_part, near_sum, far_in, acc, dhid_t
    )
    near_in = along(leave_near + near_sum, MIDDLE)
    last = along(jnp.where(inner, edge() + far_in, near()), PAIRS)
    dhid_t[c3], dqkv_own[c3] = back_own(c3)
    q_cols = heads_here * HD
    attn_args = (
        [listed(dhid_t), normed_one_t],
        [(0, listed(own)), (1, listed(dqkv_own))],
    )
    sent = swap_rows(send_rows(*attn_args, q_cols, send_turned))
    total, final, hidden, acc, sent = fence(total, final, hidden, acc, sent)
    if by_hand:
        half = slice_rows // 2
        upper = lambda m: (m * slice_rows, half)
        lower = lambda m: (m * slice_rows + half, half)
        picked = [
            [upper(1), upper(3)],
            [upper(0), upper(2)],
            [lower(2), lower(3)],
            [lower(0), lower(1)],
        ]
        pieces = keep_rows(*attn_args, sent, q_cols, keep_turned, picked)
        pieces, hidden = fence(pieces, hidden)
        one_away, one, two_away, two = pieces
        pieces = (one, to_chip(one_away, 1), two, to_chip(two_away, 2))
    else:
        pieces = scatter(sent)
    back(c3)
    pieces, gains, input_grad, last, near_in = fence(pieces, gains, input_grad, last, near_in)
    gain_sums = gains[0] + gains[1] + gains[2] + gains[3]
    gain_sums = gain_sums + swap(gain_sums)
    if by_hand:
        others = [to_chip(gain_sums, m) for m in range(1, chips)]
        gain_sums = sum(others, gain_sums)
        one = pieces[0] + pieces[1]
        two = pieces[2] + pieces[3]
        one = one[:half] + to_chip(one[half:], 2)
        two = two[:half] + to_chip(two[half:], 1)
        attn = jnp.concatenate([one, two], 0)
    else:
        gain_sums = lax.psum(gain_sums, "chip")
        attn = pieces
    gain_rows = lax.dynamic_slice_in_dim(gain_sums, at_row, slice_rows, 1)
    grad_out, grad_qkv = attn[:, :q_cols], attn[:, q_cols:]
    mlp_rows = jnp.where(inner, near() + near_in, edge()) + last
    hidden_rows = jnp.where(
        low,
        jnp.where(level == 0, hidden[0], hidden[1]),
        jnp.where(level == 2, hidden[2], hidden[3]),
    )
    layer_out = (hidden_rows + mlp_rows).astype(jnp.bfloat16)
    one = strip_one.shape[1]
    picked = lambda at, width: jnp.concatenate(
        [grad_qkv[:, kv * one + at : kv * one + at + width] for kv in range(kv_here)], 1
    )
    return (
        layer_out,
        jnp.concatenate(listed(input_grad), 0),
        gain_rows[0],
        picked(0, GROUP * HD),
        picked(GROUP * HD, HD),
        picked((GROUP + 1) * HD, HD),
        grad_out.T,
        gain_rows[1],
        grad_mlp[:, :units],
        grad_mlp[:, units : 2 * units],
        grad_mlp[:, 2 * units :].T,
    )


def solution(mesh):
    devices = mesh.devices
    dp, tp = devices.shape
    split = Mesh(devices.reshape(dp // 2, 2, tp), ("chip", "core", "tp"))
    data = ("chip", "core")
    return jax.shard_map(
        shards,
        mesh=split,
        in_specs=(
            P(data, None),
            P(data),
            P(data),
            P(data, None),
            P(),
            P(None, "tp"),
            P(None, "tp"),
            P(None, "tp"),
            P("tp", None),
            P(),
            P(None, "tp"),
            P(None, "tp"),
            P("tp", None),
        ),
        out_specs=(
            P(("chip", "core", "tp"), None),
            P(data, None),
            P(data),
            P(data, "tp"),
            P(data, "tp"),
            P(data, "tp"),
            P("tp", data),
            P(data),
            P(data, "tp"),
            P(data, "tp"),
            P("tp", data),
        ),
        check_vma=False,
    )
```

```python
import functools

import jax
import jax.numpy as jnp
from jax import lax
from jax.experimental import pallas as pl
from jax.experimental.pallas import tpu as pltpu
from jax.sharding import Mesh
from jax.sharding import PartitionSpec as P

HD = 96
LANES = 128
GROUP = 2
KV_WIDE = (GROUP + 2) * LANES
rope_base = 100000.0
norm_eps = 1e-05
masked_score = -1e30
far_away = 1e30
score_scale = HD ** (-0.5)
score_scale_log2 = score_scale * 1.4426950408889634
CHUNKS = 4
EXTRA = 8
VMEM_BYTES = 56 * 1024 * 1024
NT = (((1,), (1,)), ((), ()))


def params():
    return pltpu.CompilerParams(vmem_limit_bytes=VMEM_BYTES)


def cost(flops, moved, exps=0):
    return pl.CostEstimate(
        flops=flops // 1024, bytes_accessed=moved // 1024, transcendentals=exps // 1024
    )


def dot32(a, b):
    return jnp.dot(a, b, preferred_element_type=jnp.float32)


def dot32_nt(a, b):
    return lax.dot_general(a, b, NT, preferred_element_type=jnp.float32)


def dot_split(a, places):
    high = a.astype(jnp.bfloat16)
    rest = (a - high.astype(jnp.float32)).astype(jnp.bfloat16)
    return dot32(high, places) + dot32(rest, places)


def fence(*trees):
    return lax.optimization_barrier(trees)


def whole(array, buffers=None):
    zeros = (0,) * len(array.shape)
    return pl.BlockSpec(array.shape, lambda *_: zeros)


SCALAR = pl.BlockSpec(memory_space=pltpu.SMEM)


def halves(entry):
    half_dim = HD // 2
    return (entry // half_dim) * (LANES // 2) + entry % half_dim


def placement(lanes, width):
    return (lanes[:, None] == jnp.arange(width)[None, :]).astype(jnp.bfloat16)


def place_query(heads):
    source = jnp.arange(heads * HD)
    return placement((source // HD) * LANES + halves(source % HD), heads * LANES)


def place_key_value(kv_heads):
    source = jnp.arange(kv_heads * HD)
    head = source // HD
    keys = head * 2 * LANES + halves(source % HD)
    values = head * 2 * LANES + LANES + source % HD
    return placement(jnp.concatenate([keys, values]), kv_heads * 2 * LANES)


def place_all(heads, kv_heads):
    source = jnp.arange(heads * HD)
    head = source // HD
    query = (head // GROUP) * KV_WIDE + (head % GROUP) * LANES + halves(source % HD)
    source = jnp.arange(kv_heads * HD)
    base = (source // HD) * KV_WIDE + GROUP * LANES
    keys = base + halves(source % HD)
    values = base + LANES + source % HD
    return placement(jnp.concatenate([query, keys, values]), kv_heads * KV_WIDE)


def place_plain(heads):
    source = jnp.arange(heads * HD)
    return placement((source // HD) * LANES + source % HD, heads * LANES)


PAIRS = [(0, 1), (1, 0), (2, 3), (3, 2)]
INWARD = [(0, 1), (3, 2)]
MIDDLE = [(1, 2), (2, 1)]
OUTWARD = [(1, 0), (2, 3)]


def along(part, pairs):
    return lax.ppermute(part, "tp", pairs)


def store_qkv(out_ref, here, base, query, key_value):
    wide = GROUP * LANES
    for kv in range(key_value.shape[1] // (2 * LANES)):
        at = base + kv * KV_WIDE
        there = slice(kv * 2 * LANES, (kv + 1) * 2 * LANES)
        out_ref[here, at : at + wide] = query[:, kv * wide : (kv + 1) * wide]
        out_ref[here, at + wide : at + KV_WIDE] = key_value[:, there]


def store_turned(out_ref, at, lin, cos_ref, sin_ref):
    for h in range(GROUP + 2):
        one = lin[:, h * LANES : (h + 1) * LANES]
        if h < GROUP + 1:
            one = one * cos_ref[...] + pltpu.roll(one, LANES // 2, 1) * sin_ref[...]
        out_ref[:, at + h * LANES : at + (h + 1) * LANES] = one.astype(jnp.bfloat16)


def spread_out_kernel(meta_ref, own_ref, p_ref, mine_ref, theirs_ref, pad_ref, plain_ref):
    rows, width = mine_ref.shape[2:]
    wide = p_ref.shape[1]
    for side, ref in enumerate((mine_ref, theirs_ref)):
        here = pl.ds(pl.multiple_of((meta_ref[1] ^ side) * rows, rows), rows)
        for s in range(4):
            block = own_ref[here, :] if s == 0 else ref[0, s - 1].astype(jnp.bfloat16)
            plain_ref[here, s * width : (s + 1) * width] = block
            pad_ref[here, s * wide : (s + 1) * wide] = dot32(block, p_ref[...]).astype(
                jnp.bfloat16
            )


def spread_qkv_kernel(own_ref, pq_ref, pkv_ref, far_ref, out_ref):
    parts, others, rows, width = far_ref.shape
    wide = own_ref.shape[1]
    split = pq_ref.shape[0]
    out_ref[:, :wide] = own_ref[...]
    for s in range(others):
        block = far_ref[:, s].reshape(parts * rows, width).astype(jnp.bfloat16)
        query = dot32(block[:, :split], pq_ref[...]).astype(jnp.bfloat16)
        key_value = dot32(block[:, split:], pkv_ref[...]).astype(jnp.bfloat16)
        store_qkv(out_ref, slice(None), (s + 1) * wide, query, key_value)


def spread_qkv(own, pq, pkv, far):
    total, wide = own.shape
    dp, others, rows, width = far.shape
    parts = max(1, dp // 4)
    block = parts * rows
    return pl.pallas_call(
        spread_qkv_kernel,
        out_shape=jax.ShapeDtypeStruct((total, (others + 1) * wide), jnp.bfloat16),
        grid=(total // block,),
        in_specs=[
            pl.BlockSpec((block, wide), lambda i: (i, 0)),
            whole(pq),
            whole(pkv),
            pl.BlockSpec((parts, others, rows, width), lambda i: (i, 0, 0, 0)),
        ],
        out_specs=pl.BlockSpec((block, (others + 1) * wide), lambda i: (i, 0)),
        compiler_params=params(),
        cost_estimate=cost(8 * total * width * 512, 20 * total * wide),
    )(own, pq, pkv, far)


def spread(kernel, meta, own, places, mine, theirs, widths):
    chips, others, rows, width = mine.shape
    total = own.shape[0]
    row_block = lambda m, meta: (meta[0] ^ m, 0)
    piece = pl.BlockSpec((1, others, rows, width), lambda m, meta: (m, 0, 0, 0))
    return pl.pallas_call(
        kernel,
        out_shape=[jax.ShapeDtypeStruct((total, wide), jnp.bfloat16) for wide in widths],
        grid_spec=pltpu.PrefetchScalarGridSpec(
            num_scalar_prefetch=1,
            grid=(chips,),
            in_specs=[pl.BlockSpec((2 * rows, own.shape[1]), row_block)]
            + [whole(place) for place in places]
            + [piece, piece],
            out_specs=[pl.BlockSpec((2 * rows, wide), row_block) for wide in widths],
        ),
        compiler_params=params(),
        cost_estimate=cost(
            8 * total * width * 512, total * (12 * width + 2 * sum(widths))
        ),
    )(meta, own, *places, mine, theirs)


def start_kernel(x_ref, gain_ref, q_ref, k_ref, v_ref, pq_ref, pkv_ref, cos_ref, sin_ref, *outs):
    qkv_ref, normed_ref, pad_ref = outs

    @pl.when(pl.program_id(0) == 0)
    def _():
        split = k_ref.shape[0]
        query = dot32(q_ref[...], pq_ref[...]).astype(jnp.bfloat16)
        key_value = dot32(k_ref[...].T, pkv_ref[:split, :])
        key_value = key_value + dot32(v_ref[...].T, pkv_ref[split:, :])
        store_qkv(pad_ref, slice(None), 0, query, key_value.astype(jnp.bfloat16))

    inputs = x_ref[...].astype(jnp.float32)
    rms = lax.rsqrt(jnp.mean(inputs * inputs, -1, keepdims=True) + norm_eps)
    normed = (inputs * rms * gain_ref[...]).astype(jnp.bfloat16)
    normed_ref[...] = normed
    for kv in range(pad_ref.shape[1] // KV_WIDE):
        at = kv * KV_WIDE
        store_turned(qkv_ref, at, dot32(normed, pad_ref[:, at : at + KV_WIDE]), cos_ref, sin_ref)


def start(tokens, gain, w_query, w_key_t, w_value_t, pq, pkv, cosines, sines):
    total, depth = tokens.shape
    rows = total // CHUNKS
    wide = pq.shape[1] + pkv.shape[1]
    gain = gain[None, :]
    by_rows = lambda width: pl.BlockSpec((rows, width), lambda i: (i, 0))
    arrays = [w_query, w_key_t, w_value_t, pq, pkv]
    shapes = [
        jax.ShapeDtypeStruct((total, wide), jnp.bfloat16),
        jax.ShapeDtypeStruct((total, depth), jnp.bfloat16),
        jax.ShapeDtypeStruct((depth, wide), jnp.bfloat16),
    ]
    return pl.pallas_call(
        start_kernel,
        out_shape=shapes,
        grid=(CHUNKS,),
        in_specs=[by_rows(depth), whole(gain)]
        + [whole(array) for array in arrays]
        + [by_rows(LANES), by_rows(LANES)],
        out_specs=[by_rows(wide), by_rows(depth), whole(shapes[2])],
        compiler_params=params(),
        cost_estimate=cost(2 * total * depth * wide, 12 * total * depth),
    )(tokens, gain, *arrays, cosines, sines)


def turn_kernel(length_ref, cot_ref, normed_ref, dout_ref, dout_t_ref, normed_t_ref):
    rows = cot_ref.shape[0]
    at = pl.program_id(0) * rows + lax.broadcasted_iota(jnp.int32, cot_ref.shape, 0)
    dout = jnp.where(at < length_ref[0], cot_ref[...].astype(jnp.float32), 0.0)
    dout = dout.astype(jnp.bfloat16)
    dout_ref[...] = dout
    dout_t_ref[...] = dout.T
    normed_t_ref[...] = normed_ref[...].T


def turn(length, cotangent, normed):
    total, depth = cotangent.shape
    rows = total // CHUNKS
    by_rows = pl.BlockSpec((rows, depth), lambda i: (i, 0))
    by_columns = pl.BlockSpec((depth, rows), lambda i: (0, i))
    turned = jax.ShapeDtypeStruct((depth, total), jnp.bfloat16)
    return pl.pallas_call(
        turn_kernel,
        out_shape=[jax.ShapeDtypeStruct((total, depth), jnp.bfloat16), turned, turned],
        grid=(CHUNKS,),
        in_specs=[SCALAR, by_rows, by_rows],
        out_specs=[by_rows, by_columns, by_columns],
        compiler_params=params(),
        cost_estimate=cost(total * depth, 10 * total * depth),
    )(length, cotangent, normed)


def project_kernel(x_ref, w_ref, cos_ref, sin_ref, out_ref):
    store_turned(out_ref, 0, dot32(x_ref[...], w_ref[...]), cos_ref, sin_ref)


def project(normed, weights, cosines, sines):
    rows, depth = normed.shape
    width = weights.shape[1]
    return pl.pallas_call(
        project_kernel,
        out_shape=jax.ShapeDtypeStruct((rows, width), jnp.bfloat16),
        grid=(width // KV_WIDE,),
        in_specs=[
            whole(normed),
            pl.BlockSpec((depth, KV_WIDE), lambda i: (0, i)),
            whole(cosines),
            whole(sines),
        ],
        out_specs=pl.BlockSpec((rows, KV_WIDE), lambda i: (0, i)),
        compiler_params=params(),
        cost_estimate=cost(
            2 * rows * depth * width, 2 * (rows * depth + depth * width + rows * width)
        ),
    )(normed, weights, cosines, sines)


def attend_kernel(start, length_ref, q_ref, kv_ref, strip_ref, out_ref):
    rows = q_ref.shape[0]
    keys = kv_ref.shape[0]
    length = length_ref[0]
    row_ids = start + lax.broadcasted_iota(jnp.int32, (1, rows), 1)
    limit = jnp.minimum(row_ids, length - 1)
    allowed = lax.broadcasted_iota(jnp.int32, (keys, rows), 0) <= limit
    mixed = []
    sums = []
    for kv in range(kv_ref.shape[1] // KV_WIDE):
        base = kv * KV_WIDE
        at = base + GROUP * LANES
        key = kv_ref[:, at : at + LANES]
        value_t = kv_ref[:, at + LANES : at + 2 * LANES].T
        for g in range(GROUP):
            query = q_ref[:, base + g * LANES : base + (g + 1) * LANES]
            raw = jnp.where(allowed, dot32_nt(key, query), masked_score)
            peak = jnp.max(raw, axis=0, keepdims=True)
            expo = jnp.exp2((raw - peak) * score_scale_log2)
            total = jnp.sum(expo, axis=0, keepdims=True)
            probs = (expo * (1.0 / total)).astype(jnp.bfloat16)
            mixed.append(dot32(value_t, probs).T)
            log_sum = peak * score_scale_log2 + jnp.log2(total)
            sums.append(jnp.where(row_ids < length, log_sum, far_away))
    out_ref[:rows, :] = dot_split(jnp.concatenate(mixed, 1), strip_ref[...])
    out_ref[rows:, :] = jnp.zeros((EXTRA, out_ref.shape[1]), jnp.float32)
    out_ref[rows : rows + len(sums), :rows] = jnp.concatenate(sums, 0)


def attend(length, qkv, strip, index, rows):
    keys = (index + 1) * rows
    width = qkv.shape[1]
    heads = width // KV_WIDE * GROUP
    shape = (rows + EXTRA, strip.shape[1])
    return pl.pallas_call(
        functools.partial(attend_kernel, index * rows),
        out_shape=jax.ShapeDtypeStruct(shape, jnp.float32),
        grid=(1,),
        in_specs=[
            SCALAR,
            pl.BlockSpec((rows, width), lambda i: (index, 0)),
            pl.BlockSpec((keys, width), lambda i: (0, 0)),
            whole(strip),
        ],
        out_specs=pl.BlockSpec(shape, lambda i: (0, 0)),
        compiler_params=params(),
        cost_estimate=cost(
            4 * heads * rows * keys * LANES, 2 * (rows + keys) * width, heads * rows * keys
        ),
    )(length, qkv, qkv, strip)


def forward_kernel(level_ref, part_ref, other_ref, across_ref, outer_ref, *refs):
    x_ref, dout_ref, wo_ref, gain_ref, wg_ref, wu_ref, wd_ref = refs[:7]
    hidden_ref, normed_t_ref, activ_ref, dgate_ref, dup_ref, mlp_ref, dn_ref = refs[7:14]
    normed_ref = refs[14]
    rows = x_ref.shape[0]

    @pl.when(pl.program_id(0) == 0)
    def _():
        level = level_ref[0]
        inner = (level == 1) | (level == 2)
        width = part_ref.shape[1]
        second = jnp.where(inner, across_ref[:rows, width:], outer_ref[:rows, :width])
        third = jnp.where(inner, across_ref[:rows, :width], outer_ref[:rows, width:])
        mixed = jnp.concatenate([part_ref[:rows, :], other_ref[:rows, :], second, third], 1)
        hidden = x_ref[...].astype(jnp.float32) + dot32_nt(mixed.astype(jnp.bfloat16), wo_ref[...])
        hidden_ref[...] = hidden
        rms = lax.rsqrt(jnp.mean(hidden * hidden, -1, keepdims=True) + norm_eps)
        normed = (hidden * rms * gain_ref[...]).astype(jnp.bfloat16)
        normed_ref[...] = normed
        normed_t_ref[...] = normed.T
        mlp_ref[...] = jnp.zeros_like(mlp_ref)
        dn_ref[...] = jnp.zeros_like(dn_ref)

    normed = normed_ref[...]
    gate = dot32(normed, wg_ref[...])
    up = dot32(normed, wu_ref[...])
    dact = dot32_nt(dout_ref[...], wd_ref[...])
    sigmoid = jax.nn.sigmoid(gate)
    silu = gate * sigmoid
    activ = (silu * up).astype(jnp.bfloat16)
    dgate = (dact * up * sigmoid * (1.0 + gate * (1.0 - sigmoid))).astype(jnp.bfloat16)
    dup = (dact * silu).astype(jnp.bfloat16)
    activ_ref[...] = activ
    dgate_ref[...] = dgate
    dup_ref[...] = dup
    mlp_ref[...] += dot32(activ, wd_ref[...])
    dn_ref[:rows, :] += dot32_nt(dgate, wg_ref[...]) + dot32_nt(dup, wu_ref[...])


def forward_chunk(level, gathered, tokens, dout, w_out, gain, w_gate, w_up, w_down, index, rows):
    depth = tokens.shape[1]
    units = w_gate.shape[1]
    block = 512
    own_rows = pl.BlockSpec((rows, depth), lambda i: (index, 0))
    by_units = pl.BlockSpec((depth, block), lambda i: (0, i))
    gain = gain[None, :]
    f32, bf16 = jnp.float32, jnp.bfloat16
    outs = [
        jax.ShapeDtypeStruct((rows, depth), f32),
        jax.ShapeDtypeStruct((depth, rows), bf16),
        jax.ShapeDtypeStruct((rows, units), bf16),
        jax.ShapeDtypeStruct((rows, units), bf16),
        jax.ShapeDtypeStruct((rows, units), bf16),
        jax.ShapeDtypeStruct((rows, depth), f32),
        jax.ShapeDtypeStruct((rows + EXTRA, depth), f32),
    ]
    unit_out = pl.BlockSpec((rows, block), lambda i: (0, i))
    return pl.pallas_call(
        forward_kernel,
        out_shape=outs,
        grid=(units // block,),
        in_specs=[SCALAR]
        + [whole(array) for array in gathered]
        + [own_rows, own_rows, whole(w_out), whole(gain), by_units, by_units]
        + [pl.BlockSpec((block, depth), lambda i: (i, 0))],
        out_specs=[
            whole(outs[0]),
            whole(outs[1]),
            unit_out,
            unit_out,
            unit_out,
            whole(outs[5]),
            whole(outs[6]),
        ],
        scratch_shapes=[pltpu.VMEM((rows, depth), bf16)],
        compiler_params=params(),
        cost_estimate=cost(
            2 * rows * depth * (6 * units + w_out.shape[1]),
            2 * depth * (3 * units + w_out.shape[1]) + 22 * rows * depth,
            rows * units,
        ),
    )(level, *gathered, tokens, dout, w_out, gain, w_gate, w_up, w_down)


def hidden_grad(inner, total_ref, final_ref, hidden_ref, dout_ref, gain_ref):
    dnormed = jnp.where(inner, total_ref[...], final_ref[...])
    hidden = hidden_ref[...]
    rms = lax.rsqrt(jnp.mean(hidden * hidden, -1, keepdims=True) + norm_eps)
    scaled = dnormed * gain_ref[...]
    shift = jnp.mean(scaled * hidden, -1, keepdims=True)
    dhid = dout_ref[...].astype(jnp.float32) + (rms * scaled - hidden * (rms**3 * shift))
    return dhid, dnormed * (hidden * rms)


def backward_kernel(start, full, level_ref, total_ref, final_ref, hidden_ref, dout_ref, x_ref, *refs):
    gain_one_ref, gain_two_ref, wo_ref, q_ref = refs[:4]
    kv_here = q_ref.shape[1] // KV_WIDE
    refs = refs[4:]
    kv_refs, refs = refs[: 2 * kv_here], refs[2 * kv_here :]
    part_ref, other_ref, across_ref, outer_ref, place_ref, strip_ref = refs[:6]
    cos_ref, sin_ref = refs[6:8]
    dhid_ref, low_ref, dn_ref = refs[-3:]
    outs = refs[8:-3]
    if full:
        w_ref, outs = outs[0], outs[1:]
    count = (5 if start > 0 else 4) if full else 2
    acc_ref = outs[0] if len(outs) > count else None
    outs = outs[-count:]
    dhid_t_ref, dqkv_ref = outs[:2]
    if full:
        input_grad_ref, gains_ref = outs[2:4]
    rows = q_ref.shape[0]
    keys = kv_refs[0].shape[0]
    shard = pl.program_id(0)
    level = level_ref[0]
    inner = (level == 1) | (level == 2)

    @pl.when(shard == 0)
    def _():
        dhid, dgain = hidden_grad(
            inner, total_ref, final_ref, hidden_ref, dout_ref, gain_two_ref
        )
        dhid_ref[...] = dhid
        low = dhid.astype(jnp.bfloat16)
        low_ref[...] = low
        dhid_t_ref[...] = low.T
        if full:
            gains_ref[...] = jnp.zeros_like(gains_ref)
            gains_ref[1:2, :] = jnp.sum(dgain, 0, keepdims=True)
            dn_ref[...] = jnp.zeros_like(dn_ref)

    def rotate_back(grads):
        turned = grads * cos_ref[...] - pltpu.roll(grads, LANES // 2, 1) * sin_ref[...]
        return turned.astype(jnp.bfloat16)

    dmixed_all = dot32(low_ref[...], wo_ref[...]).astype(jnp.bfloat16)
    mixed = jnp.where(
        shard == 0,
        part_ref[...],
        jnp.where(shard == 1, other_ref[...], jnp.where(inner, across_ref[...], outer_ref[...])),
    )
    products = dmixed_all.astype(jnp.float32) * dot_split(mixed[:rows], place_ref[...])
    causal = lax.broadcasted_iota(jnp.int32, (rows, rows), 0) <= lax.broadcasted_iota(
        jnp.int32, (rows, rows), 1
    )
    grads = []
    for kv in range(kv_here):
        key_ref, value_ref = kv_refs[2 * kv : 2 * kv + 2]
        heads = range(kv * GROUP, (kv + 1) * GROUP)
        lanes = {h: slice(h * LANES, (h + 1) * LANES) for h in heads}
        row_dots = {h: jnp.sum(products[:, lanes[h]].T, axis=0, keepdims=True) for h in heads}
        log_sums = {h: mixed[rows + h : rows + h + 1, :rows] for h in heads}
        dqueries = dict.fromkeys(heads)
        here = slice(2 * kv * LANES, (2 * kv + 1) * LANES)
        there = slice((2 * kv + 1) * LANES, (2 * kv + 2) * LANES)
        for tile in range(keys // rows):
            span = slice(tile * rows, (tile + 1) * rows)
            key = key_ref[span, :]
            value = value_ref[span, :]
            key_t = key.T
            dkey = None if acc_ref is None else acc_ref[span, here]
            dvalue = None if acc_ref is None else acc_ref[span, there]
            last = tile * rows == start
            for h in heads:
                at = kv * KV_WIDE + (h % GROUP) * LANES
                query = q_ref[:, at : at + LANES]
                dmixed = dmixed_all[:, lanes[h]]
                raw = dot32_nt(key, query)
                probs = jnp.exp2(raw * score_scale_log2 - log_sums[h])
                if last:
                    probs = jnp.where(causal, probs, 0.0)
                dprobs = dot32_nt(value, dmixed)
                dscores = (probs * (dprobs - row_dots[h])).astype(jnp.bfloat16)
                dquery = dot32(key_t, dscores)
                dqueries[h] = dquery if dqueries[h] is None else dqueries[h] + dquery
                dkey_one = dot32(dscores, query)
                dvalue_one = dot32(probs.astype(jnp.bfloat16), dmixed)
                dkey = dkey_one if dkey is None else dkey + dkey_one
                dvalue = dvalue_one if dvalue is None else dvalue + dvalue_one
            if full and not last:
                outs[4][span, here] = dkey
                outs[4][span, there] = dvalue
        grads += [rotate_back(dqueries[h].T * score_scale) for h in heads]
        grads.append(rotate_back(dkey * score_scale))
        grads.append(dvalue.astype(jnp.bfloat16))
    grads = jnp.concatenate(grads, 1)
    if full:
        dn_ref[...] += dot32_nt(grads, w_ref[...])

    @pl.when(shard == 0)
    def _():
        wide = strip_ref.shape[1]
        for kv in range(kv_here):
            dqkv_ref[:, kv * wide : (kv + 1) * wide] = dot32(
                grads[:, kv * KV_WIDE : (kv + 1) * KV_WIDE], strip_ref[...]
            ).astype(jnp.bfloat16)

    if not full:
        return

    @pl.when(shard == pl.num_programs(0) - 1)
    def _():
        dnormed = dn_ref[...]
        inputs = x_ref[...].astype(jnp.float32)
        rms = lax.rsqrt(jnp.mean(inputs * inputs, -1, keepdims=True) + norm_eps)
        scaled = dnormed * gain_one_ref[...]
        shift = jnp.mean(scaled * inputs, -1, keepdims=True)
        grad = dhid_ref[...] + (rms * scaled - inputs * (rms**3 * shift))
        input_grad_ref[...] = grad.astype(jnp.bfloat16)
        gains_ref[0:1, :] = jnp.sum(dnormed * (inputs * rms), 0, keepdims=True)


def backward_chunk(
    level, sums_two, hidden, dout, tokens, gains, weights, qkv, gathered, places, tables, acc,
    index, rows, full=True
):
    start = index * rows
    keys = start + rows
    depth = tokens.shape[1]
    out_pad, qkv_pad = weights
    place_out, strip = places
    far_rows, width = gathered[0].shape
    out_wide = place_out.shape[1]
    kv_here = out_wide // (GROUP * LANES)
    wide = kv_here * KV_WIDE
    levels = qkv.shape[1] // wide
    own_rows = pl.BlockSpec((rows, depth), lambda t: (index, 0))
    table = pl.BlockSpec((rows, LANES), lambda t: (index, 0))
    gains = [gain[None, :] for gain in gains]
    key_value = lambda at: pl.BlockSpec(
        (keys, LANES), lambda t: (0, (wide // LANES) * t + at)
    )
    across = pl.BlockSpec((far_rows, width), lambda t: (0, jnp.where(t == 2, 1, 0)))
    outer = pl.BlockSpec((far_rows, width), lambda t: (0, jnp.where(t == 3, 1, 0)))
    in_specs = [
        SCALAR,
        whole(sums_two[0]),
        whole(sums_two[1]),
        whole(hidden),
        own_rows,
        own_rows,
        whole(gains[0]),
        whole(gains[1]),
        pl.BlockSpec((depth, out_wide), lambda t: (0, t)),
        pl.BlockSpec((rows, wide), lambda t: (index, t)),
    ]
    for kv in range(kv_here):
        at = kv * (KV_WIDE // LANES) + GROUP
        in_specs += [key_value(at), key_value(at + 1)]
    in_specs += [
        whole(gathered[0]),
        whole(gathered[1]),
        across,
        outer,
        whole(place_out),
        whole(strip),
        table,
        table,
    ]
    args = [level, *sums_two, hidden, dout, tokens, *gains, out_pad]
    args += [qkv] * (1 + 2 * kv_here)
    args += [*gathered, place_out, strip, *tables]
    sums_wide = 2 * kv_here * LANES
    if full:
        in_specs.append(pl.BlockSpec((depth, wide), lambda t: (0, t)))
        args.append(qkv_pad)
    if acc is not None:
        in_specs.append(pl.BlockSpec((keys, sums_wide), lambda t: (0, t)))
        args.append(acc)
    f32, bf16 = jnp.float32, jnp.bfloat16
    outs = [
        jax.ShapeDtypeStruct((depth, rows), bf16),
        jax.ShapeDtypeStruct((rows, kv_here * strip.shape[1]), bf16),
        jax.ShapeDtypeStruct((rows, depth), bf16),
        jax.ShapeDtypeStruct((8, depth), f32),
    ]
    outs = outs if full else outs[:2]
    out_specs = [whole(out) for out in outs]
    if full and start > 0:
        outs.append(jax.ShapeDtypeStruct((start, levels * sums_wide), f32))
        out_specs.append(pl.BlockSpec((start, sums_wide), lambda t: (0, t)))
    results = pl.pallas_call(
        functools.partial(backward_kernel, start, full),
        out_shape=outs,
        grid=(levels if full else 1,),
        in_specs=in_specs,
        out_specs=out_specs,
        scratch_shapes=[
            pltpu.VMEM((rows, depth), f32),
            pltpu.VMEM((rows, depth), bf16),
            pltpu.VMEM((rows, depth), f32),
        ],
        compiler_params=params(),
        cost_estimate=cost(
            levels * rows * (20 * kv_here * keys * LANES + 2 * depth * (out_wide + wide)),
            2 * depth * levels * (out_wide + wide) + 16 * rows * depth,
            levels * kv_here * GROUP * rows * keys,
        ),
    )(*args)
    return results[:4], (results[4] if full and start > 0 else None)


def rows_kernel(lefts, groups, adding, picked, side_ref, *refs):
    refs = list(refs)
    held_ref = refs.pop()
    out_refs = refs[-len(picked) :]
    refs = refs[: -len(picked)]
    recv_ref = refs.pop() if adding else None
    step = pl.program_id(0)
    left_refs = []
    for count in lefts:
        left_refs.append(refs[:count])
        refs = refs[count:]
    rights = []
    for _ in groups:
        rights.append(refs[:CHUNKS])
        refs = refs[CHUNKS:]
    rows = left_refs[0][0].shape[0]
    blocks = held_ref.shape[1] // rows

    @pl.when(step == 0)
    def _():
        for which, pieces in enumerate(left_refs):
            for n, ref in enumerate(pieces):
                m, j = n % blocks, n // blocks
                wide = ref.shape[1]
                held_ref[which, m * rows : (m + 1) * rows, j * wide : (j + 1) * wide] = ref[...]

    chunk = held_ref.shape[2] // CHUNKS
    for group, (left, first, steps) in zip(rights, groups):

        @pl.when((step >= first) & (step < first + steps))
        def _(group=group, left=left):
            right = jnp.concatenate([ref[:chunk, :].astype(jnp.bfloat16) for ref in group], 0)
            total = dot32(held_ref[left], right)
            if recv_ref is not None:
                total = total + recv_ref[...]
            for out_ref, parts in zip(out_refs, picked):
                at = 0
                for start, size in parts:
                    out_ref[at : at + size, :] = total[start : start + size]
                    at += size


def rows_of(lefts, groups, side, rows, blocks, step, recv=None, picked=None):
    if picked is None:
        picked = [[(0, rows * blocks)]]
    at = lambda m: lambda i, side: ((m ^ side[2]) * side[1] + side[0], 0)
    specs = []
    args = []
    counts = []
    for left in lefts:
        pieces = left if isinstance(left, list) else [left]
        counts.append(len(pieces) * blocks)
        for piece in pieces:
            for m in range(blocks):
                specs.append(pl.BlockSpec((rows, piece.shape[1]), at(m)))
                args.append(piece)
    tokens = sum(piece.shape[1] for piece in pieces)
    first = 0
    plan = []
    for which, rights in groups:
        steps = rights[0].shape[1] // step
        plan.append((which, first, steps))
        for right in rights:
            pick = lambda i, side, first=first, steps=steps: (0, jnp.clip(i - first, 0, steps - 1))
            specs.append(pl.BlockSpec((right.shape[0], step), pick))
            args.append(right)
        first += steps
    total = first * step
    block = lambda height: pl.BlockSpec((height, step), lambda i, side: (0, i))
    if recv is not None:
        specs.append(block(rows * blocks))
        args.append(recv)
    heights = [sum(size for _, size in parts) for parts in picked]
    results = pl.pallas_call(
        functools.partial(rows_kernel, counts, plan, recv is not None, picked),
        out_shape=[jax.ShapeDtypeStruct((height, total), jnp.float32) for height in heights],
        grid_spec=pltpu.PrefetchScalarGridSpec(
            num_scalar_prefetch=1,
            grid=(first,),
            in_specs=specs,
            out_specs=[block(height) for height in heights],
            scratch_shapes=[pltpu.VMEM((len(lefts), rows * blocks, tokens), jnp.bfloat16)],
        ),
        compiler_params=params(),
        cost_estimate=cost(
            2 * rows * blocks * tokens * total,
            4 * rows * blocks * total + 2 * tokens * (total + rows * blocks),
        ),
    )(side, *args)
    return results[0] if len(picked) == 1 else results


def shards(
    tokens,
    lengths,
    positions,
    cotangent,
    norm_gain,
    w_query,
    w_key,
    w_value,
    w_out,
    mlp_gain,
    w_gate,
    w_up,
    w_down,
):
    seq_rows, depth = tokens.shape
    chips = lax.axis_size("chip")
    dp = chips * 2
    tp = lax.axis_size("tp")
    chip = lax.axis_index("chip")
    core = lax.axis_index("core")
    level = lax.axis_index("tp")
    low = level < 2
    inner = (level == 1) | (level == 2)
    heads_here = w_query.shape[1] // HD
    kv_here = w_key.shape[1] // HD
    rows = seq_rows // CHUNKS
    slice_rows = depth // dp
    level_ref = level.astype(jnp.int32).reshape(1)
    by_hand = dp == 8
    swap = lambda array: lax.ppermute(array, "core", [(0, 1), (1, 0)])
    to_level = lambda array, s: along(array, [(t, t ^ s) for t in range(tp)])

    at_row = (chip * 2 + core) * slice_rows
    cols = lambda w: lax.dynamic_slice_in_dim(w, at_row, slice_rows, 1).astype(jnp.float32).T
    (out_slice,) = fence(cols(w_out))
    qkv_slice = jnp.concatenate(
        [
            lax.dynamic_slice_in_dim(w_query, at_row, slice_rows, 0).astype(jnp.float32),
            cols(w_key.T),
            cols(w_value.T),
        ],
        1,
    )
    out_slice, qkv_slice = fence(out_slice, qkv_slice)
    out_near = along(out_slice, PAIRS)
    qkv_near = along(qkv_slice, PAIRS)
    meta = jnp.stack([chip, core]).astype(jnp.int32)

    pq = place_query(heads_here)
    pkv = place_key_value(kv_here)
    p_all = place_all(heads_here, kv_here)
    strip_one = place_all(GROUP, 1).T
    p_out = place_plain(heads_here)
    strip_out = p_out.T

    half_dim = HD // 2
    freqs = rope_base ** (-(jnp.arange(half_dim).astype(jnp.float32) * 2.0 / HD))
    freqs = jnp.pad(freqs, (0, LANES // 2 - half_dim))
    angles = positions.astype(jnp.float32)[:, None] * jnp.concatenate([freqs, freqs])[None, :]
    cosines = jnp.cos(angles)
    sines = jnp.sin(angles) * jnp.where(jnp.arange(LANES) < LANES // 2, -1.0, 1.0)

    cosines, sines, out_near = fence(cosines, sines, out_near)
    out_across = along(jnp.stack([out_slice, out_near]), MIDDLE)
    qkv_own, normed_one, own_pad = start(
        tokens, norm_gain, w_query, w_key.T, w_value.T, pq, pkv, cosines, sines
    )

    def far_slices(near, across, outer):
        return jnp.stack(
            [
                near,
                jnp.where(inner, across[1], outer[0]),
                jnp.where(inner, across[0], outer[1]),
            ]
        )

    order = list(reversed(range(CHUNKS)))
    c0, c1, c2, c3 = order
    own, other, across, outer = {}, {}, {}, {}
    part, total, final = {}, {}, {}

    def hop_1(j):
        other[j] = along(own[j], PAIRS)

    def hop_2(j):
        across[j] = along(jnp.concatenate([own[j], other[j]], 1), MIDDLE)

    def hop_3(j):
        outer[j] = along(across[j], OUTWARD)

    coming = {}

    def add_1(j):
        coming[j] = along(part[j], INWARD)

    def add_2(j):
        total[j] = part[j][:rows] + coming[j][:rows]
        coming[j] = along(total[j], MIDDLE)

    def add_3(j):
        total[j] = total[j] + coming[j]
        final[j] = along(total[j], OUTWARD)

    def to_chip(array, m):
        return lax.ppermute(array, "chip", [(i, i ^ m) for i in range(chips)])

    def over_chips_1(piece):
        cut = piece.shape[1] // 2
        one, two = piece[:, :cut], piece[:, cut:]
        return jnp.stack([one, to_chip(one, 1)]), jnp.stack([two, to_chip(two, 2)])

    def over_chips_2(one, two):
        return one, to_chip(one, 2), two, to_chip(two, 1)

    def over_chips_3(one, one_far, two, two_far):
        upper = jnp.stack([one[0], one[1], one_far[0], one_far[1]])
        lower = jnp.stack([two[0], two_far[0], two[1], two_far[1]])
        return jnp.concatenate([upper, lower], 2)

    qkv_own, out_across, qkv_near = fence(qkv_own, out_across, qkv_near)
    out_outer = along(out_across, OUTWARD)
    qkv_across = along(jnp.stack([qkv_slice, qkv_near]), MIDDLE)
    own[c0] = attend(lengths, qkv_own, strip_out, c0, rows)
    own, qkv_own, out_outer = fence(own, qkv_own, out_outer)
    hop_1(c0)
    out_far = far_slices(out_near, out_across, out_outer)
    out_mine = over_chips_1(out_far) if by_hand else out_far
    for j in (c1, c2):
        own[j] = attend(lengths, qkv_own, strip_out, j, rows)
    own, other, normed_one, w_out, out_mine, qkv_across, qkv_own = fence(
        own, other, normed_one, w_out, out_mine, qkv_across, qkv_own
    )
    own[c3] = attend(lengths, qkv_own, strip_out, c3, rows)
    hop_1(c1)
    qkv_outer = along(qkv_across, OUTWARD)
    if by_hand:
        out_mine = over_chips_2(*out_mine)
    else:
        out_mine = lax.all_gather(out_mine, ("chip", "core"))
    hop_2(c0)
    dout, dout_t, normed_one_t = turn(lengths, cotangent, normed_one)
    w_out_t = w_out.T
    own, other, across, dout, dout_t, normed_one_t, w_out_t, out_mine, qkv_outer = fence(
        own, other, across, dout, dout_t, normed_one_t, w_out_t, out_mine, qkv_outer
    )
    hop_1(c2)
    hop_1(c3)
    hop_3(c0)
    hop_2(c1)
    qkv_far = lax.all_gather(far_slices(qkv_near, qkv_across, qkv_outer), ("chip", "core"))
    if by_hand:
        out_mine = over_chips_3(*out_mine)
        out_theirs = swap(out_mine)
        out_pad, out_plain = spread(
            spread_out_kernel,
            meta,
            w_out_t,
            [p_out],
            out_mine,
            out_theirs,
            [4 * p_out.shape[1], 4 * p_out.shape[0]],
        )
    else:
        plain = [w_out_t] + [
            out_mine[:, s].reshape(depth, -1).astype(jnp.bfloat16) for s in range(tp - 1)
        ]
        out_plain = jnp.concatenate(plain, 1)
        out_pad = jnp.concatenate([dot32(w, p_out).astype(jnp.bfloat16) for w in plain], 1)
    hidden, normed_t, activ, dgate, dup, mlp_part = {}, {}, {}, {}, {}, {}

    def feed(j):
        gathered = (own[j], other[j], across[j], outer[j])
        (hidden[j], normed_t[j], activ[j], dgate[j], dup[j], mlp_part[j], part[j]) = forward_chunk(
            level_ref, gathered, tokens, dout, out_plain, mlp_gain, w_gate, w_up, w_down, j, rows
        )

    feed(c0)
    own, other, across, outer, part, hidden = fence(own, other, across, outer, part, hidden)
    add_1(c0)
    hop_3(c1)
    hop_2(c2)
    hop_2(c3)
    feed(c1)
    own, other, across, outer, part, total, coming, hidden = fence(
        own, other, across, outer, part, total, coming, hidden
    )
    add_1(c1)
    hop_3(c2)
    hop_3(c3)
    add_2(c0)
    qkv_far, part = fence(qkv_far, part)
    qkv_pad = spread_qkv(own_pad, pq, pkv, qkv_far)
    outer[c2], qkv_pad = fence(outer[c2], qkv_pad)
    outer[c3], qkv_pad = fence(outer[c3], qkv_pad)
    feed(c2)
    feed(c3)
    own, other, across, outer, part, total, coming, hidden, mlp_in, qkv_pad = fence(
        own, other, across, outer, part, total, coming, hidden,
        (normed_t, activ, dgate, dup), qkv_pad,
    )
    normed_t, activ, dgate, dup = mlp_in
    add_1(c2)
    add_3(c0)
    add_2(c1)
    qkv = project(normed_one, qkv_pad, cosines, sines)

    listed = lambda pieces: [pieces[j] for j in range(CHUNKS)]
    keep_side = jnp.stack([core, 2, 0]).astype(jnp.int32)
    keep_turned = jnp.stack([core, 2, chip]).astype(jnp.int32)
    send_side = jnp.stack([1 - core, 2, 0]).astype(jnp.int32)
    send_turned = jnp.stack([1 - core, 2, chip]).astype(jnp.int32)
    all_rows = jnp.array([0, 1, 0], jnp.int32)

    def send_rows(lefts, groups, step, side=send_side):
        if not by_hand:
            return rows_of(lefts, groups, all_rows, depth // 4, 4, step)
        return rows_of(lefts, groups, side, slice_rows, chips, step)

    def keep_rows(lefts, groups, received, step, side=keep_side, picked=None):
        if not by_hand:
            return received
        return rows_of(lefts, groups, side, slice_rows, chips, step, received, picked)

    def swap_rows(array):
        return swap(array) if by_hand else array

    def scatter(array):
        axes = "chip" if by_hand else ("chip", "core")
        return lax.psum_scatter(array, axes, scatter_dimension=0, tiled=True)

    units = w_gate.shape[1]
    mlp_args = (
        [listed(normed_t), dout_t],
        [(0, listed(dgate)), (0, listed(dup)), (1, listed(activ))],
    )
    acc = None
    dhid_t, dqkv_own, input_grad, gains = {}, {}, {}, {}

    def back(j):
        nonlocal acc
        (dhid_t[j], dqkv_own[j], input_grad[j], gains[j]), acc = back_some(j, True)

    def back_own(j):
        return back_some(j, False)[0]

    def back_some(j, full):
        return backward_chunk(
            level_ref,
            (total[j], final[j]),
            hidden[j],
            dout,
            tokens,
            (norm_gain, mlp_gain),
            (out_pad, qkv_pad),
            qkv,
            (own[j], other[j], across[j], outer[j]),
            (p_out, strip_one),
            (cosines, sines),
            acc,
            j,
            rows,
            full,
        )

    sent = send_rows(*mlp_args, units // 2)
    own, other, across, outer, part, total, coming, final, hidden, sent, qkv = fence(
        own, other, across, outer, part, total, coming, final, hidden, sent, qkv
    )
    sent = swap_rows(sent)
    add_1(c3)
    add_3(c1)
    add_2(c2)
    back(c0)

    near = lambda: jnp.where(low, mlp_part[1], mlp_part[2])
    edge = lambda: jnp.where(low, mlp_part[0], mlp_part[3])
    total, coming, final, hidden, mlp_part, acc, dhid_t, sent = fence(
        total, coming, final, hidden, mlp_part, acc, dhid_t, sent
    )
    leave_far = jnp.where(low, mlp_part[3], mlp_part[0])
    leave_near = jnp.where(low, mlp_part[2], mlp_part[1])
    far_sum = along(leave_far, INWARD)
    add_3(c2)
    add_2(c3)
    grad_mlp = keep_rows(*mlp_args, sent, units // 2)
    hidden, grad_mlp = fence(hidden, grad_mlp)
    grad_mlp = scatter(grad_mlp)
    back(c1)
    total, coming, final, hidden, mlp_part, far_sum, acc, dhid_t = fence(
        total, coming, final, hidden, mlp_part, far_sum, acc, dhid_t
    )
    near_sum = along(leave_near, INWARD)
    add_3(c3)
    far_in = along(leave_far + far_sum, MIDDLE)
    back(c2)
    total, final, hidden, mlp_part, near_sum, far_in, acc, dhid_t = fence(
        total, final, hidden, mlp_part, near_sum, far_in, acc, dhid_t
    )
    last = along(jnp.where(inner, edge() + far_in, near()), PAIRS)
    near_in = along(leave_near + near_sum, MIDDLE)
    dhid_t[c3], dqkv_own[c3] = back_own(c3)
    q_cols = heads_here * HD
    attn_args = (
        [listed(dhid_t), normed_one_t],
        [(0, listed(own)), (1, listed(dqkv_own))],
    )
    sent = swap_rows(send_rows(*attn_args, q_cols, send_turned))
    total, final, hidden, acc, sent = fence(total, final, hidden, acc, sent)
    if by_hand:
        half = slice_rows // 2
        upper = lambda m: (m * slice_rows, half)
        lower = lambda m: (m * slice_rows + half, half)
        picked = [
            [upper(1), upper(3)],
            [upper(0), upper(2)],
            [lower(2), lower(3)],
            [lower(0), lower(1)],
        ]
        pieces = keep_rows(*attn_args, sent, q_cols, keep_turned, picked)
        pieces, hidden = fence(pieces, hidden)
        one_away, one, two_away, two = pieces
        pieces = (one, to_chip(one_away, 1), two, to_chip(two_away, 2))
    else:
        pieces = scatter(sent)
    back(c3)
    pieces, gains, input_grad, last, near_in = fence(pieces, gains, input_grad, last, near_in)
    gain_sums = gains[0] + gains[1] + gains[2] + gains[3]
    gain_sums = gain_sums + swap(gain_sums)
    if by_hand:
        others = [to_chip(gain_sums, m) for m in range(1, chips)]
        gain_sums = sum(others, gain_sums)
        one = pieces[0] + pieces[1]
        two = pieces[2] + pieces[3]
        one = one[:half] + to_chip(one[half:], 2)
        two = two[:half] + to_chip(two[half:], 1)
        attn = jnp.concatenate([one, two], 0)
    else:
        gain_sums = lax.psum(gain_sums, "chip")
        attn = pieces
    gain_rows = lax.dynamic_slice_in_dim(gain_sums, at_row, slice_rows, 1)
    grad_out, grad_qkv = attn[:, :q_cols], attn[:, q_cols:]
    mlp_rows = jnp.where(inner, near() + near_in, edge()) + last
    hidden_rows = jnp.where(
        low,
        jnp.where(level == 0, hidden[0], hidden[1]),
        jnp.where(level == 2, hidden[2], hidden[3]),
    )
    layer_out = (hidden_rows + mlp_rows).astype(jnp.bfloat16)
    one = strip_one.shape[1]
    picked = lambda at, width: jnp.concatenate(
        [grad_qkv[:, kv * one + at : kv * one + at + width] for kv in range(kv_here)], 1
    )
    return (
        layer_out,
        jnp.concatenate(listed(input_grad), 0),
        gain_rows[0],
        picked(0, GROUP * HD),
        picked(GROUP * HD, HD),
        picked((GROUP + 1) * HD, HD),
        grad_out.T,
        gain_rows[1],
        grad_mlp[:, :units],
        grad_mlp[:, units : 2 * units],
        grad_mlp[:, 2 * units :].T,
    )


def solution(mesh):
    devices = mesh.devices
    dp, tp = devices.shape
    split = Mesh(devices.reshape(dp // 2, 2, tp), ("chip", "core", "tp"))
    data = ("chip", "core")
    return jax.shard_map(
        shards,
        mesh=split,
        in_specs=(
            P(data, None),
            P(data),
            P(data),
            P(data, None),
            P(),
            P(None, "tp"),
            P(None, "tp"),
            P(None, "tp"),
            P("tp", None),
            P(),
            P(None, "tp"),
            P(None, "tp"),
            P("tp", None),
        ),
        out_specs=(
            P(("chip", "core", "tp"), None),
            P(data, None),
            P(data),
            P(data, "tp"),
            P(data, "tp"),
            P(data, "tp"),
            P("tp", data),
            P(data),
            P(data, "tp"),
            P(data, "tp"),
            P("tp", data),
        ),
        check_vma=False,
    )
```

```python
import functools

import jax
import jax.numpy as jnp
from jax import lax
from jax.experimental import pallas as pl
from jax.experimental.pallas import tpu as pltpu
from jax.sharding import Mesh
from jax.sharding import PartitionSpec as P

HD = 96
LANES = 128
GROUP = 2
KV_WIDE = (GROUP + 2) * LANES
rope_base = 100000.0
norm_eps = 1e-05
masked_score = -1e30
far_away = 1e30
score_scale = HD ** (-0.5)
score_scale_log2 = score_scale * 1.4426950408889634
CHUNKS = 4
EXTRA = 8
VMEM_BYTES = 56 * 1024 * 1024
NT = (((1,), (1,)), ((), ()))


def params():
    return pltpu.CompilerParams(vmem_limit_bytes=VMEM_BYTES)


def cost(flops, moved, exps=0):
    return pl.CostEstimate(
        flops=flops // 1024, bytes_accessed=moved // 1024, transcendentals=exps // 1024
    )


def dot32(a, b):
    return jnp.dot(a, b, preferred_element_type=jnp.float32)


def dot32_nt(a, b):
    return lax.dot_general(a, b, NT, preferred_element_type=jnp.float32)


def dot_split(a, places):
    high = a.astype(jnp.bfloat16)
    rest = (a - high.astype(jnp.float32)).astype(jnp.bfloat16)
    return dot32(high, places) + dot32(rest, places)


def fence(*trees):
    return lax.optimization_barrier(trees)


def whole(array, buffers=None):
    zeros = (0,) * len(array.shape)
    return pl.BlockSpec(array.shape, lambda *_: zeros)


SCALAR = pl.BlockSpec(memory_space=pltpu.SMEM)


def halves(entry):
    half_dim = HD // 2
    return (entry // half_dim) * (LANES // 2) + entry % half_dim


def placement(lanes, width):
    return (lanes[:, None] == jnp.arange(width)[None, :]).astype(jnp.bfloat16)


def place_query(heads):
    source = jnp.arange(heads * HD)
    return placement((source // HD) * LANES + halves(source % HD), heads * LANES)


def place_key_value(kv_heads):
    source = jnp.arange(kv_heads * HD)
    head = source // HD
    keys = head * 2 * LANES + halves(source % HD)
    values = head * 2 * LANES + LANES + source % HD
    return placement(jnp.concatenate([keys, values]), kv_heads * 2 * LANES)


def place_all(heads, kv_heads):
    source = jnp.arange(heads * HD)
    head = source // HD
    query = (head // GROUP) * KV_WIDE + (head % GROUP) * LANES + halves(source % HD)
    source = jnp.arange(kv_heads * HD)
    base = (source // HD) * KV_WIDE + GROUP * LANES
    keys = base + halves(source % HD)
    values = base + LANES + source % HD
    return placement(jnp.concatenate([query, keys, values]), kv_heads * KV_WIDE)


def place_plain(heads):
    source = jnp.arange(heads * HD)
    return placement((source // HD) * LANES + source % HD, heads * LANES)


PAIRS = [(0, 1), (1, 0), (2, 3), (3, 2)]
INWARD = [(0, 1), (3, 2)]
MIDDLE = [(1, 2), (2, 1)]
OUTWARD = [(1, 0), (2, 3)]


def along(part, pairs):
    return lax.ppermute(part, "tp", pairs)


def store_qkv(out_ref, here, base, query, key_value):
    wide = GROUP * LANES
    for kv in range(key_value.shape[1] // (2 * LANES)):
        at = base + kv * KV_WIDE
        there = slice(kv * 2 * LANES, (kv + 1) * 2 * LANES)
        out_ref[here, at : at + wide] = query[:, kv * wide : (kv + 1) * wide]
        out_ref[here, at + wide : at + KV_WIDE] = key_value[:, there]


def store_turned(out_ref, at, lin, cos_ref, sin_ref):
    for h in range(GROUP + 2):
        one = lin[:, h * LANES : (h + 1) * LANES]
        if h < GROUP + 1:
            one = one * cos_ref[...] + pltpu.roll(one, LANES // 2, 1) * sin_ref[...]
        out_ref[:, at + h * LANES : at + (h + 1) * LANES] = one.astype(jnp.bfloat16)


def spread_out_kernel(meta_ref, own_ref, p_ref, mine_ref, theirs_ref, pad_ref, plain_ref):
    rows, width = mine_ref.shape[2:]
    wide = p_ref.shape[1]
    for side, ref in enumerate((mine_ref, theirs_ref)):
        here = pl.ds(pl.multiple_of((meta_ref[1] ^ side) * rows, rows), rows)
        for s in range(4):
            block = own_ref[here, :] if s == 0 else ref[0, s - 1].astype(jnp.bfloat16)
            plain_ref[here, s * width : (s + 1) * width] = block
            pad_ref[here, s * wide : (s + 1) * wide] = dot32(block, p_ref[...]).astype(
                jnp.bfloat16
            )


def spread_qkv_kernel(own_ref, pq_ref, pkv_ref, far_ref, out_ref):
    parts, others, rows, width = far_ref.shape
    wide = own_ref.shape[1]
    split = pq_ref.shape[0]
    out_ref[:, :wide] = own_ref[...]
    for s in range(others):
        block = far_ref[:, s].reshape(parts * rows, width).astype(jnp.bfloat16)
        query = dot32(block[:, :split], pq_ref[...]).astype(jnp.bfloat16)
        key_value = dot32(block[:, split:], pkv_ref[...]).astype(jnp.bfloat16)
        store_qkv(out_ref, slice(None), (s + 1) * wide, query, key_value)


def spread_qkv(own, pq, pkv, far):
    total, wide = own.shape
    dp, others, rows, width = far.shape
    parts = max(1, dp // 4)
    block = parts * rows
    return pl.pallas_call(
        spread_qkv_kernel,
        out_shape=jax.ShapeDtypeStruct((total, (others + 1) * wide), jnp.bfloat16),
        grid=(total // block,),
        in_specs=[
            pl.BlockSpec((block, wide), lambda i: (i, 0)),
            whole(pq),
            whole(pkv),
            pl.BlockSpec((parts, others, rows, width), lambda i: (i, 0, 0, 0)),
        ],
        out_specs=pl.BlockSpec((block, (others + 1) * wide), lambda i: (i, 0)),
        compiler_params=params(),
        cost_estimate=cost(8 * total * width * 512, 20 * total * wide),
    )(own, pq, pkv, far)


def spread(kernel, meta, own, places, mine, theirs, widths):
    chips, others, rows, width = mine.shape
    total = own.shape[0]
    row_block = lambda m, meta: (meta[0] ^ m, 0)
    piece = pl.BlockSpec((1, others, rows, width), lambda m, meta: (m, 0, 0, 0))
    return pl.pallas_call(
        kernel,
        out_shape=[jax.ShapeDtypeStruct((total, wide), jnp.bfloat16) for wide in widths],
        grid_spec=pltpu.PrefetchScalarGridSpec(
            num_scalar_prefetch=1,
            grid=(chips,),
            in_specs=[pl.BlockSpec((2 * rows, own.shape[1]), row_block)]
            + [whole(place) for place in places]
            + [piece, piece],
            out_specs=[pl.BlockSpec((2 * rows, wide), row_block) for wide in widths],
        ),
        compiler_params=params(),
        cost_estimate=cost(
            8 * total * width * 512, total * (12 * width + 2 * sum(widths))
        ),
    )(meta, own, *places, mine, theirs)


def start_kernel(x_ref, gain_ref, q_ref, k_ref, v_ref, pq_ref, pkv_ref, cos_ref, sin_ref, *outs):
    qkv_ref, normed_ref, pad_ref = outs

    @pl.when(pl.program_id(0) == 0)
    def _():
        split = k_ref.shape[0]
        query = dot32(q_ref[...], pq_ref[...]).astype(jnp.bfloat16)
        key_value = dot32(k_ref[...].T, pkv_ref[:split, :])
        key_value = key_value + dot32(v_ref[...].T, pkv_ref[split:, :])
        store_qkv(pad_ref, slice(None), 0, query, key_value.astype(jnp.bfloat16))

    inputs = x_ref[...].astype(jnp.float32)
    rms = lax.rsqrt(jnp.mean(inputs * inputs, -1, keepdims=True) + norm_eps)
    normed = (inputs * rms * gain_ref[...]).astype(jnp.bfloat16)
    normed_ref[...] = normed
    for kv in range(pad_ref.shape[1] // KV_WIDE):
        at = kv * KV_WIDE
        store_turned(qkv_ref, at, dot32(normed, pad_ref[:, at : at + KV_WIDE]), cos_ref, sin_ref)


def start(tokens, gain, w_query, w_key_t, w_value_t, pq, pkv, cosines, sines):
    total, depth = tokens.shape
    rows = total // CHUNKS
    wide = pq.shape[1] + pkv.shape[1]
    gain = gain[None, :]
    by_rows = lambda width: pl.BlockSpec((rows, width), lambda i: (i, 0))
    arrays = [w_query, w_key_t, w_value_t, pq, pkv]
    shapes = [
        jax.ShapeDtypeStruct((total, wide), jnp.bfloat16),
        jax.ShapeDtypeStruct((total, depth), jnp.bfloat16),
        jax.ShapeDtypeStruct((depth, wide), jnp.bfloat16),
    ]
    return pl.pallas_call(
        start_kernel,
        out_shape=shapes,
        grid=(CHUNKS,),
        in_specs=[by_rows(depth), whole(gain)]
        + [whole(array) for array in arrays]
        + [by_rows(LANES), by_rows(LANES)],
        out_specs=[by_rows(wide), by_rows(depth), whole(shapes[2])],
        compiler_params=params(),
        cost_estimate=cost(2 * total * depth * wide, 12 * total * depth),
    )(tokens, gain, *arrays, cosines, sines)


def turn_kernel(length_ref, cot_ref, normed_ref, dout_ref, dout_t_ref, normed_t_ref):
    rows = cot_ref.shape[0]
    at = pl.program_id(0) * rows + lax.broadcasted_iota(jnp.int32, cot_ref.shape, 0)
    dout = jnp.where(at < length_ref[0], cot_ref[...].astype(jnp.float32), 0.0)
    dout = dout.astype(jnp.bfloat16)
    dout_ref[...] = dout
    dout_t_ref[...] = dout.T
    normed_t_ref[...] = normed_ref[...].T


def turn(length, cotangent, normed):
    total, depth = cotangent.shape
    rows = total // CHUNKS
    by_rows = pl.BlockSpec((rows, depth), lambda i: (i, 0))
    by_columns = pl.BlockSpec((depth, rows), lambda i: (0, i))
    turned = jax.ShapeDtypeStruct((depth, total), jnp.bfloat16)
    return pl.pallas_call(
        turn_kernel,
        out_shape=[jax.ShapeDtypeStruct((total, depth), jnp.bfloat16), turned, turned],
        grid=(CHUNKS,),
        in_specs=[SCALAR, by_rows, by_rows],
        out_specs=[by_rows, by_columns, by_columns],
        compiler_params=params(),
        cost_estimate=cost(total * depth, 10 * total * depth),
    )(length, cotangent, normed)


def project_kernel(x_ref, w_ref, cos_ref, sin_ref, out_ref):
    store_turned(out_ref, 0, dot32(x_ref[...], w_ref[...]), cos_ref, sin_ref)


def project(normed, weights, cosines, sines):
    rows, depth = normed.shape
    width = weights.shape[1]
    return pl.pallas_call(
        project_kernel,
        out_shape=jax.ShapeDtypeStruct((rows, width), jnp.bfloat16),
        grid=(width // KV_WIDE,),
        in_specs=[
            whole(normed),
            pl.BlockSpec((depth, KV_WIDE), lambda i: (0, i)),
            whole(cosines),
            whole(sines),
        ],
        out_specs=pl.BlockSpec((rows, KV_WIDE), lambda i: (0, i)),
        compiler_params=params(),
        cost_estimate=cost(
            2 * rows * depth * width, 2 * (rows * depth + depth * width + rows * width)
        ),
    )(normed, weights, cosines, sines)


def attend_kernel(start, length_ref, q_ref, kv_ref, strip_ref, out_ref):
    rows = q_ref.shape[0]
    keys = kv_ref.shape[0]
    length = length_ref[0]
    row_ids = start + lax.broadcasted_iota(jnp.int32, (1, rows), 1)
    limit = jnp.minimum(row_ids, length - 1)
    allowed = lax.broadcasted_iota(jnp.int32, (keys, rows), 0) <= limit
    mixed = []
    sums = []
    for kv in range(kv_ref.shape[1] // KV_WIDE):
        base = kv * KV_WIDE
        at = base + GROUP * LANES
        key = kv_ref[:, at : at + LANES]
        value_t = kv_ref[:, at + LANES : at + 2 * LANES].T
        for g in range(GROUP):
            query = q_ref[:, base + g * LANES : base + (g + 1) * LANES]
            raw = jnp.where(allowed, dot32_nt(key, query), masked_score)
            peak = jnp.max(raw, axis=0, keepdims=True)
            expo = jnp.exp2((raw - peak) * score_scale_log2)
            total = jnp.sum(expo, axis=0, keepdims=True)
            probs = (expo * (1.0 / total)).astype(jnp.bfloat16)
            mixed.append(dot32(value_t, probs).T)
            log_sum = peak * score_scale_log2 + jnp.log2(total)
            sums.append(jnp.where(row_ids < length, log_sum, far_away))
    out_ref[:rows, :] = dot_split(jnp.concatenate(mixed, 1), strip_ref[...])
    out_ref[rows:, :] = jnp.zeros((EXTRA, out_ref.shape[1]), jnp.float32)
    out_ref[rows : rows + len(sums), :rows] = jnp.concatenate(sums, 0)


def attend(length, qkv, strip, index, rows):
    keys = (index + 1) * rows
    width = qkv.shape[1]
    heads = width // KV_WIDE * GROUP
    shape = (rows + EXTRA, strip.shape[1])
    return pl.pallas_call(
        functools.partial(attend_kernel, index * rows),
        out_shape=jax.ShapeDtypeStruct(shape, jnp.float32),
        grid=(1,),
        in_specs=[
            SCALAR,
            pl.BlockSpec((rows, width), lambda i: (index, 0)),
            pl.BlockSpec((keys, width), lambda i: (0, 0)),
            whole(strip),
        ],
        out_specs=pl.BlockSpec(shape, lambda i: (0, 0)),
        compiler_params=params(),
        cost_estimate=cost(
            4 * heads * rows * keys * LANES, 2 * (rows + keys) * width, heads * rows * keys
        ),
    )(length, qkv, qkv, strip)


def forward_kernel(level_ref, part_ref, other_ref, across_ref, outer_ref, *refs):
    x_ref, dout_ref, wo_ref, gain_ref, wg_ref, wu_ref, wd_ref = refs[:7]
    hidden_ref, normed_t_ref, activ_ref, dgate_ref, dup_ref, mlp_ref, dn_ref = refs[7:14]
    normed_ref = refs[14]
    rows = x_ref.shape[0]

    @pl.when(pl.program_id(0) == 0)
    def _():
        level = level_ref[0]
        inner = (level == 1) | (level == 2)
        width = part_ref.shape[1]
        second = jnp.where(inner, across_ref[:rows, width:], outer_ref[:rows, :width])
        third = jnp.where(inner, across_ref[:rows, :width], outer_ref[:rows, width:])
        mixed = jnp.concatenate([part_ref[:rows, :], other_ref[:rows, :], second, third], 1)
        hidden = x_ref[...].astype(jnp.float32) + dot32_nt(mixed.astype(jnp.bfloat16), wo_ref[...])
        hidden_ref[...] = hidden
        rms = lax.rsqrt(jnp.mean(hidden * hidden, -1, keepdims=True) + norm_eps)
        normed = (hidden * rms * gain_ref[...]).astype(jnp.bfloat16)
        normed_ref[...] = normed
        normed_t_ref[...] = normed.T
        mlp_ref[...] = jnp.zeros_like(mlp_ref)
        dn_ref[...] = jnp.zeros_like(dn_ref)

    normed = normed_ref[...]
    gate = dot32(normed, wg_ref[...])
    up = dot32(normed, wu_ref[...])
    dact = dot32_nt(dout_ref[...], wd_ref[...])
    sigmoid = jax.nn.sigmoid(gate)
    silu = gate * sigmoid
    activ = (silu * up).astype(jnp.bfloat16)
    dgate = (dact * up * sigmoid * (1.0 + gate * (1.0 - sigmoid))).astype(jnp.bfloat16)
    dup = (dact * silu).astype(jnp.bfloat16)
    activ_ref[...] = activ
    dgate_ref[...] = dgate
    dup_ref[...] = dup
    mlp_ref[...] += dot32(activ, wd_ref[...])
    dn_ref[:rows, :] += dot32_nt(dgate, wg_ref[...]) + dot32_nt(dup, wu_ref[...])


def forward_chunk(level, gathered, tokens, dout, w_out, gain, w_gate, w_up, w_down, index, rows):
    depth = tokens.shape[1]
    units = w_gate.shape[1]
    block = 512
    own_rows = pl.BlockSpec((rows, depth), lambda i: (index, 0))
    by_units = pl.BlockSpec((depth, block), lambda i: (0, i))
    gain = gain[None, :]
    f32, bf16 = jnp.float32, jnp.bfloat16
    outs = [
        jax.ShapeDtypeStruct((rows, depth), f32),
        jax.ShapeDtypeStruct((depth, rows), bf16),
        jax.ShapeDtypeStruct((rows, units), bf16),
        jax.ShapeDtypeStruct((rows, units), bf16),
        jax.ShapeDtypeStruct((rows, units), bf16),
        jax.ShapeDtypeStruct((rows, depth), f32),
        jax.ShapeDtypeStruct((rows + EXTRA, depth), f32),
    ]
    unit_out = pl.BlockSpec((rows, block), lambda i: (0, i))
    return pl.pallas_call(
        forward_kernel,
        out_shape=outs,
        grid=(units // block,),
        in_specs=[SCALAR]
        + [whole(array) for array in gathered]
        + [own_rows, own_rows, whole(w_out), whole(gain), by_units, by_units]
        + [pl.BlockSpec((block, depth), lambda i: (i, 0))],
        out_specs=[
            whole(outs[0]),
            whole(outs[1]),
            unit_out,
            unit_out,
            unit_out,
            whole(outs[5]),
            whole(outs[6]),
        ],
        scratch_shapes=[pltpu.VMEM((rows, depth), bf16)],
        compiler_params=params(),
        cost_estimate=cost(
            2 * rows * depth * (6 * units + w_out.shape[1]),
            2 * depth * (3 * units + w_out.shape[1]) + 22 * rows * depth,
            rows * units,
        ),
    )(level, *gathered, tokens, dout, w_out, gain, w_gate, w_up, w_down)


def hidden_grad(inner, total_ref, final_ref, hidden_ref, dout_ref, gain_ref):
    dnormed = jnp.where(inner, total_ref[...], final_ref[...])
    hidden = hidden_ref[...]
    rms = lax.rsqrt(jnp.mean(hidden * hidden, -1, keepdims=True) + norm_eps)
    scaled = dnormed * gain_ref[...]
    shift = jnp.mean(scaled * hidden, -1, keepdims=True)
    dhid = dout_ref[...].astype(jnp.float32) + (rms * scaled - hidden * (rms**3 * shift))
    return dhid, dnormed * (hidden * rms)


def backward_kernel(start, full, level_ref, total_ref, final_ref, hidden_ref, dout_ref, x_ref, *refs):
    gain_one_ref, gain_two_ref, wo_ref, q_ref = refs[:4]
    kv_here = q_ref.shape[1] // KV_WIDE
    refs = refs[4:]
    kv_refs, refs = refs[: 2 * kv_here], refs[2 * kv_here :]
    part_ref, other_ref, across_ref, outer_ref, place_ref, strip_ref = refs[:6]
    cos_ref, sin_ref = refs[6:8]
    dhid_ref, low_ref, dn_ref = refs[-3:]
    outs = refs[8:-3]
    if full:
        w_ref, outs = outs[0], outs[1:]
    count = (5 if start > 0 else 4) if full else 2
    acc_ref = outs[0] if len(outs) > count else None
    outs = outs[-count:]
    dhid_t_ref, dqkv_ref = outs[:2]
    if full:
        input_grad_ref, gains_ref = outs[2:4]
    rows = q_ref.shape[0]
    keys = kv_refs[0].shape[0]
    shard = pl.program_id(0)
    level = level_ref[0]
    inner = (level == 1) | (level == 2)

    @pl.when(shard == 0)
    def _():
        dhid, dgain = hidden_grad(
            inner, total_ref, final_ref, hidden_ref, dout_ref, gain_two_ref
        )
        dhid_ref[...] = dhid
        low = dhid.astype(jnp.bfloat16)
        low_ref[...] = low
        dhid_t_ref[...] = low.T
        if full:
            gains_ref[...] = jnp.zeros_like(gains_ref)
            gains_ref[1:2, :] = jnp.sum(dgain, 0, keepdims=True)
            dn_ref[...] = jnp.zeros_like(dn_ref)

    def rotate_back(grads):
        turned = grads * cos_ref[...] - pltpu.roll(grads, LANES // 2, 1) * sin_ref[...]
        return turned.astype(jnp.bfloat16)

    dmixed_all = dot32(low_ref[...], wo_ref[...]).astype(jnp.bfloat16)
    mixed = jnp.where(
        shard == 0,
        part_ref[...],
        jnp.where(shard == 1, other_ref[...], jnp.where(inner, across_ref[...], outer_ref[...])),
    )
    products = dmixed_all.astype(jnp.float32) * dot_split(mixed[:rows], place_ref[...])
    causal = lax.broadcasted_iota(jnp.int32, (rows, rows), 0) <= lax.broadcasted_iota(
        jnp.int32, (rows, rows), 1
    )
    grads = []
    for kv in range(kv_here):
        key_ref, value_ref = kv_refs[2 * kv : 2 * kv + 2]
        heads = range(kv * GROUP, (kv + 1) * GROUP)
        lanes = {h: slice(h * LANES, (h + 1) * LANES) for h in heads}
        row_dots = {h: jnp.sum(products[:, lanes[h]].T, axis=0, keepdims=True) for h in heads}
        log_sums = {h: mixed[rows + h : rows + h + 1, :rows] for h in heads}
        dqueries = dict.fromkeys(heads)
        here = slice(2 * kv * LANES, (2 * kv + 1) * LANES)
        there = slice((2 * kv + 1) * LANES, (2 * kv + 2) * LANES)
        for tile in range(keys // rows):
            span = slice(tile * rows, (tile + 1) * rows)
            key = key_ref[span, :]
            value = value_ref[span, :]
            key_t = key.T
            dkey = None if acc_ref is None else acc_ref[span, here]
            dvalue = None if acc_ref is None else acc_ref[span, there]
            last = tile * rows == start
            for h in heads:
                at = kv * KV_WIDE + (h % GROUP) * LANES
                query = q_ref[:, at : at + LANES]
                dmixed = dmixed_all[:, lanes[h]]
                raw = dot32_nt(key, query)
                probs = jnp.exp2(raw * score_scale_log2 - log_sums[h])
                if last:
                    probs = jnp.where(causal, probs, 0.0)
                dprobs = dot32_nt(value, dmixed)
                dscores = (probs * (dprobs - row_dots[h])).astype(jnp.bfloat16)
                dquery = dot32(key_t, dscores)
                dqueries[h] = dquery if dqueries[h] is None else dqueries[h] + dquery
                dkey_one = dot32(dscores, query)
                dvalue_one = dot32(probs.astype(jnp.bfloat16), dmixed)
                dkey = dkey_one if dkey is None else dkey + dkey_one
                dvalue = dvalue_one if dvalue is None else dvalue + dvalue_one
            if full and not last:
                outs[4][span, here] = dkey
                outs[4][span, there] = dvalue
        grads += [rotate_back(dqueries[h].T * score_scale) for h in heads]
        grads.append(rotate_back(dkey * score_scale))
        grads.append(dvalue.astype(jnp.bfloat16))
    grads = jnp.concatenate(grads, 1)
    if full:
        dn_ref[...] += dot32_nt(grads, w_ref[...])

    @pl.when(shard == 0)
    def _():
        wide = strip_ref.shape[1]
        for kv in range(kv_here):
            dqkv_ref[:, kv * wide : (kv + 1) * wide] = dot32(
                grads[:, kv * KV_WIDE : (kv + 1) * KV_WIDE], strip_ref[...]
            ).astype(jnp.bfloat16)

    if not full:
        return

    @pl.when(shard == pl.num_programs(0) - 1)
    def _():
        dnormed = dn_ref[...]
        inputs = x_ref[...].astype(jnp.float32)
        rms = lax.rsqrt(jnp.mean(inputs * inputs, -1, keepdims=True) + norm_eps)
        scaled = dnormed * gain_one_ref[...]
        shift = jnp.mean(scaled * inputs, -1, keepdims=True)
        grad = dhid_ref[...] + (rms * scaled - inputs * (rms**3 * shift))
        input_grad_ref[...] = grad.astype(jnp.bfloat16)
        gains_ref[0:1, :] = jnp.sum(dnormed * (inputs * rms), 0, keepdims=True)


def backward_chunk(
    level, sums_two, hidden, dout, tokens, gains, weights, qkv, gathered, places, tables, acc,
    index, rows, full=True
):
    start = index * rows
    keys = start + rows
    depth = tokens.shape[1]
    out_pad, qkv_pad = weights
    place_out, strip = places
    far_rows, width = gathered[0].shape
    out_wide = place_out.shape[1]
    kv_here = out_wide // (GROUP * LANES)
    wide = kv_here * KV_WIDE
    levels = qkv.shape[1] // wide
    own_rows = pl.BlockSpec((rows, depth), lambda t: (index, 0))
    table = pl.BlockSpec((rows, LANES), lambda t: (index, 0))
    gains = [gain[None, :] for gain in gains]
    key_value = lambda at: pl.BlockSpec(
        (keys, LANES), lambda t: (0, (wide // LANES) * t + at)
    )
    across = pl.BlockSpec((far_rows, width), lambda t: (0, jnp.where(t == 2, 1, 0)))
    outer = pl.BlockSpec((far_rows, width), lambda t: (0, jnp.where(t == 3, 1, 0)))
    in_specs = [
        SCALAR,
        whole(sums_two[0]),
        whole(sums_two[1]),
        whole(hidden),
        own_rows,
        own_rows,
        whole(gains[0]),
        whole(gains[1]),
        pl.BlockSpec((depth, out_wide), lambda t: (0, t)),
        pl.BlockSpec((rows, wide), lambda t: (index, t)),
    ]
    for kv in range(kv_here):
        at = kv * (KV_WIDE // LANES) + GROUP
        in_specs += [key_value(at), key_value(at + 1)]
    in_specs += [
        whole(gathered[0]),
        whole(gathered[1]),
        across,
        outer,
        whole(place_out),
        whole(strip),
        table,
        table,
    ]
    args = [level, *sums_two, hidden, dout, tokens, *gains, out_pad]
    args += [qkv] * (1 + 2 * kv_here)
    args += [*gathered, place_out, strip, *tables]
    sums_wide = 2 * kv_here * LANES
    if full:
        in_specs.append(pl.BlockSpec((depth, wide), lambda t: (0, t)))
        args.append(qkv_pad)
    if acc is not None:
        in_specs.append(pl.BlockSpec((keys, sums_wide), lambda t: (0, t)))
        args.append(acc)
    f32, bf16 = jnp.float32, jnp.bfloat16
    outs = [
        jax.ShapeDtypeStruct((depth, rows), bf16),
        jax.ShapeDtypeStruct((rows, kv_here * strip.shape[1]), bf16),
        jax.ShapeDtypeStruct((rows, depth), bf16),
        jax.ShapeDtypeStruct((8, depth), f32),
    ]
    outs = outs if full else outs[:2]
    out_specs = [whole(out) for out in outs]
    if full and start > 0:
        outs.append(jax.ShapeDtypeStruct((start, levels * sums_wide), f32))
        out_specs.append(pl.BlockSpec((start, sums_wide), lambda t: (0, t)))
    results = pl.pallas_call(
        functools.partial(backward_kernel, start, full),
        out_shape=outs,
        grid=(levels if full else 1,),
        in_specs=in_specs,
        out_specs=out_specs,
        scratch_shapes=[
            pltpu.VMEM((rows, depth), f32),
            pltpu.VMEM((rows, depth), bf16),
            pltpu.VMEM((rows, depth), f32),
        ],
        compiler_params=params(),
        cost_estimate=cost(
            levels * rows * (20 * kv_here * keys * LANES + 2 * depth * (out_wide + wide)),
            2 * depth * levels * (out_wide + wide) + 16 * rows * depth,
            levels * kv_here * GROUP * rows * keys,
        ),
    )(*args)
    return results[:4], (results[4] if full and start > 0 else None)


def rows_kernel(lefts, groups, adding, picked, side_ref, *refs):
    refs = list(refs)
    held_ref = refs.pop()
    out_refs = refs[-len(picked) :]
    refs = refs[: -len(picked)]
    recv_ref = refs.pop() if adding else None
    step = pl.program_id(0)
    left_refs = []
    for count in lefts:
        left_refs.append(refs[:count])
        refs = refs[count:]
    rights = []
    for _ in groups:
        rights.append(refs[:CHUNKS])
        refs = refs[CHUNKS:]
    rows = left_refs[0][0].shape[0]
    blocks = held_ref.shape[1] // rows

    @pl.when(step == 0)
    def _():
        for which, pieces in enumerate(left_refs):
            for n, ref in enumerate(pieces):
                m, j = n % blocks, n // blocks
                wide = ref.shape[1]
                held_ref[which, m * rows : (m + 1) * rows, j * wide : (j + 1) * wide] = ref[...]

    chunk = held_ref.shape[2] // CHUNKS
    for group, (left, first, steps) in zip(rights, groups):

        @pl.when((step >= first) & (step < first + steps))
        def _(group=group, left=left):
            right = jnp.concatenate([ref[:chunk, :].astype(jnp.bfloat16) for ref in group], 0)
            total = dot32(held_ref[left], right)
            if recv_ref is not None:
                total = total + recv_ref[...]
            for out_ref, parts in zip(out_refs, picked):
                at = 0
                for start, size in parts:
                    out_ref[at : at + size, :] = total[start : start + size]
                    at += size


def rows_of(lefts, groups, side, rows, blocks, step, recv=None, picked=None):
    if picked is None:
        picked = [[(0, rows * blocks)]]
    at = lambda m: lambda i, side: ((m ^ side[2]) * side[1] + side[0], 0)
    specs = []
    args = []
    counts = []
    for left in lefts:
        pieces = left if isinstance(left, list) else [left]
        counts.append(len(pieces) * blocks)
        for piece in pieces:
            for m in range(blocks):
                specs.append(pl.BlockSpec((rows, piece.shape[1]), at(m)))
                args.append(piece)
    tokens = sum(piece.shape[1] for piece in pieces)
    first = 0
    plan = []
    for which, rights in groups:
        steps = rights[0].shape[1] // step
        plan.append((which, first, steps))
        for right in rights:
            pick = lambda i, side, first=first, steps=steps: (0, jnp.clip(i - first, 0, steps - 1))
            specs.append(pl.BlockSpec((right.shape[0], step), pick))
            args.append(right)
        first += steps
    total = first * step
    block = lambda height: pl.BlockSpec((height, step), lambda i, side: (0, i))
    if recv is not None:
        specs.append(block(rows * blocks))
        args.append(recv)
    heights = [sum(size for _, size in parts) for parts in picked]
    results = pl.pallas_call(
        functools.partial(rows_kernel, counts, plan, recv is not None, picked),
        out_shape=[jax.ShapeDtypeStruct((height, total), jnp.float32) for height in heights],
        grid_spec=pltpu.PrefetchScalarGridSpec(
            num_scalar_prefetch=1,
            grid=(first,),
            in_specs=specs,
            out_specs=[block(height) for height in heights],
            scratch_shapes=[pltpu.VMEM((len(lefts), rows * blocks, tokens), jnp.bfloat16)],
        ),
        compiler_params=params(),
        cost_estimate=cost(
            2 * rows * blocks * tokens * total,
            4 * rows * blocks * total + 2 * tokens * (total + rows * blocks),
        ),
    )(side, *args)
    return results[0] if len(picked) == 1 else results


def shards(
    tokens,
    lengths,
    positions,
    cotangent,
    norm_gain,
    w_query,
    w_key,
    w_value,
    w_out,
    mlp_gain,
    w_gate,
    w_up,
    w_down,
):
    seq_rows, depth = tokens.shape
    chips = lax.axis_size("chip")
    dp = chips * 2
    tp = lax.axis_size("tp")
    chip = lax.axis_index("chip")
    core = lax.axis_index("core")
    level = lax.axis_index("tp")
    low = level < 2
    inner = (level == 1) | (level == 2)
    heads_here = w_query.shape[1] // HD
    kv_here = w_key.shape[1] // HD
    rows = seq_rows // CHUNKS
    slice_rows = depth // dp
    level_ref = level.astype(jnp.int32).reshape(1)
    by_hand = dp == 8
    swap = lambda array: lax.ppermute(array, "core", [(0, 1), (1, 0)])
    to_level = lambda array, s: along(array, [(t, t ^ s) for t in range(tp)])

    at_row = (chip * 2 + core) * slice_rows
    cols = lambda w: lax.dynamic_slice_in_dim(w, at_row, slice_rows, 1).astype(jnp.float32).T
    (out_slice,) = fence(cols(w_out))
    qkv_slice = jnp.concatenate(
        [
            lax.dynamic_slice_in_dim(w_query, at_row, slice_rows, 0).astype(jnp.float32),
            cols(w_key.T),
            cols(w_value.T),
        ],
        1,
    )
    out_slice, qkv_slice = fence(out_slice, qkv_slice)
    out_near = along(out_slice, PAIRS)
    qkv_near = along(qkv_slice, PAIRS)
    meta = jnp.stack([chip, core]).astype(jnp.int32)

    pq = place_query(heads_here)
    pkv = place_key_value(kv_here)
    p_all = place_all(heads_here, kv_here)
    strip_one = place_all(GROUP, 1).T
    p_out = place_plain(heads_here)
    strip_out = p_out.T

    half_dim = HD // 2
    freqs = rope_base ** (-(jnp.arange(half_dim).astype(jnp.float32) * 2.0 / HD))
    freqs = jnp.pad(freqs, (0, LANES // 2 - half_dim))
    angles = positions.astype(jnp.float32)[:, None] * jnp.concatenate([freqs, freqs])[None, :]
    cosines = jnp.cos(angles)
    sines = jnp.sin(angles) * jnp.where(jnp.arange(LANES) < LANES // 2, -1.0, 1.0)

    cosines, sines, out_near = fence(cosines, sines, out_near)
    out_across = along(jnp.stack([out_slice, out_near]), MIDDLE)
    qkv_own, normed_one, own_pad = start(
        tokens, norm_gain, w_query, w_key.T, w_value.T, pq, pkv, cosines, sines
    )

    def far_slices(near, across, outer):
        return jnp.stack(
            [
                near,
                jnp.where(inner, across[1], outer[0]),
                jnp.where(inner, across[0], outer[1]),
            ]
        )

    order = list(reversed(range(CHUNKS)))
    c0, c1, c2, c3 = order
    own, other, across, outer = {}, {}, {}, {}
    part, total, final = {}, {}, {}

    def hop_1(j):
        other[j] = along(own[j], PAIRS)

    def hop_2(j):
        across[j] = along(jnp.concatenate([own[j], other[j]], 1), MIDDLE)

    def hop_3(j):
        outer[j] = along(across[j], OUTWARD)

    coming = {}

    def add_1(j):
        coming[j] = along(part[j], INWARD)

    def add_2(j):
        total[j] = part[j][:rows] + coming[j][:rows]
        coming[j] = along(total[j], MIDDLE)

    def add_3(j, inward):
        total[j] = jnp.where(inner, total[j] + coming[j], inward)
        final[j] = along(total[j], PAIRS)
        return final[j]

    def to_chip(array, m):
        return lax.ppermute(array, "chip", [(i, i ^ m) for i in range(chips)])

    def over_chips_1(piece):
        cut = piece.shape[1] // 2
        one, two = piece[:, :cut], piece[:, cut:]
        return jnp.stack([one, to_chip(one, 1)]), jnp.stack([two, to_chip(two, 2)])

    def over_chips_2(one, two):
        return one, to_chip(one, 2), two, to_chip(two, 1)

    def over_chips_3(one, one_far, two, two_far):
        upper = jnp.stack([one[0], one[1], one_far[0], one_far[1]])
        lower = jnp.stack([two[0], two_far[0], two[1], two_far[1]])
        return jnp.concatenate([upper, lower], 2)

    qkv_own, out_across, qkv_near = fence(qkv_own, out_across, qkv_near)
    out_outer = along(out_across, OUTWARD)
    qkv_across = along(jnp.stack([qkv_slice, qkv_near]), MIDDLE)
    own[c0] = attend(lengths, qkv_own, strip_out, c0, rows)
    own, qkv_own, out_outer = fence(own, qkv_own, out_outer)
    hop_1(c0)
    out_far = far_slices(out_near, out_across, out_outer)
    out_mine = over_chips_1(out_far) if by_hand else out_far
    for j in (c1, c2):
        own[j] = attend(lengths, qkv_own, strip_out, j, rows)
    own, other, normed_one, w_out, out_mine, qkv_across, qkv_own = fence(
        own, other, normed_one, w_out, out_mine, qkv_across, qkv_own
    )
    own[c3] = attend(lengths, qkv_own, strip_out, c3, rows)
    hop_1(c1)
    qkv_outer = along(qkv_across, OUTWARD)
    if by_hand:
        out_mine = over_chips_2(*out_mine)
    else:
        out_mine = lax.all_gather(out_mine, ("chip", "core"))
    hop_2(c0)
    dout, dout_t, normed_one_t = turn(lengths, cotangent, normed_one)
    w_out_t = w_out.T
    own, other, across, dout, dout_t, normed_one_t, w_out_t, out_mine, qkv_outer = fence(
        own, other, across, dout, dout_t, normed_one_t, w_out_t, out_mine, qkv_outer
    )
    hop_1(c2)
    hop_3(c0)
    hop_2(c1)
    qkv_far = lax.all_gather(far_slices(qkv_near, qkv_across, qkv_outer), ("chip", "core"))
    if by_hand:
        out_mine = over_chips_3(*out_mine)
        out_theirs = swap(out_mine)
        out_pad, out_plain = spread(
            spread_out_kernel,
            meta,
            w_out_t,
            [p_out],
            out_mine,
            out_theirs,
            [4 * p_out.shape[1], 4 * p_out.shape[0]],
        )
    else:
        plain = [w_out_t] + [
            out_mine[:, s].reshape(depth, -1).astype(jnp.bfloat16) for s in range(tp - 1)
        ]
        out_plain = jnp.concatenate(plain, 1)
        out_pad = jnp.concatenate([dot32(w, p_out).astype(jnp.bfloat16) for w in plain], 1)
    hidden, normed_t, activ, dgate, dup, mlp_part = {}, {}, {}, {}, {}, {}

    def feed(j):
        gathered = (own[j], other[j], across[j], outer[j])
        (hidden[j], normed_t[j], activ[j], dgate[j], dup[j], mlp_part[j], part[j]) = forward_chunk(
            level_ref, gathered, tokens, dout, out_plain, mlp_gain, w_gate, w_up, w_down, j, rows
        )

    own, other, across, outer, out_pad, out_plain = fence(
        own, other, across, outer, out_pad, out_plain
    )
    hop_1(c3)
    hop_3(c1)
    hop_2(c2)
    feed(c0)
    own, other, across, outer, part, hidden = fence(own, other, across, outer, part, hidden)
    add_1(c0)
    hop_3(c2)
    hop_2(c3)
    feed(c1)
    outer[c2], hidden[c1] = fence(outer[c2], hidden[c1])
    feed(c2)
    own, other, across, outer, part, total, coming, hidden = fence(
        own, other, across, outer, part, total, coming, hidden
    )
    add_1(c1)
    hop_3(c3)
    add_2(c0)
    qkv_far, part = fence(qkv_far, part)
    qkv_pad = spread_qkv(own_pad, pq, pkv, qkv_far)
    qkv = project(normed_one, qkv_pad, cosines, sines)
    own, other, across, outer, part, total, coming, hidden, qkv = fence(
        own, other, across, outer, part, total, coming, hidden, qkv
    )
    coming[c2] = add_3(c0, part[c2][:rows])
    add_2(c1)
    feed(c3)

    listed = lambda pieces: [pieces[j] for j in range(CHUNKS)]
    keep_side = jnp.stack([core, 2, 0]).astype(jnp.int32)
    keep_turned = jnp.stack([core, 2, chip]).astype(jnp.int32)
    send_side = jnp.stack([1 - core, 2, 0]).astype(jnp.int32)
    send_turned = jnp.stack([1 - core, 2, chip]).astype(jnp.int32)
    all_rows = jnp.array([0, 1, 0], jnp.int32)

    def send_rows(lefts, groups, step, side=send_side):
        if not by_hand:
            return rows_of(lefts, groups, all_rows, depth // 4, 4, step)
        return rows_of(lefts, groups, side, slice_rows, chips, step)

    def keep_rows(lefts, groups, received, step, side=keep_side, picked=None):
        if not by_hand:
            return received
        return rows_of(lefts, groups, side, slice_rows, chips, step, received, picked)

    def swap_rows(array):
        return swap(array) if by_hand else array

    def scatter(array):
        axes = "chip" if by_hand else ("chip", "core")
        return lax.psum_scatter(array, axes, scatter_dimension=0, tiled=True)

    units = w_gate.shape[1]
    mlp_args = (
        [listed(normed_t), dout_t],
        [(0, listed(dgate)), (0, listed(dup)), (1, listed(activ))],
    )
    acc = None
    dhid_t, dqkv_own, input_grad, gains = {}, {}, {}, {}

    def back(j):
        nonlocal acc
        (dhid_t[j], dqkv_own[j], input_grad[j], gains[j]), acc = back_some(j, True)

    def back_own(j):
        return back_some(j, False)[0]

    def back_some(j, full):
        return backward_chunk(
            level_ref,
            (total[j], final[j]),
            hidden[j],
            dout,
            tokens,
            (norm_gain, mlp_gain),
            (out_pad, qkv_pad),
            qkv,
            (own[j], other[j], across[j], outer[j]),
            (p_out, strip_one),
            (cosines, sines),
            acc,
            j,
            rows,
            full,
        )

    sent = send_rows(*mlp_args, units // 2)
    own, other, across, outer, part, total, coming, final, hidden, sent = fence(
        own, other, across, outer, part, total, coming, final, hidden, sent
    )
    sent = swap_rows(sent)
    coming[c3] = add_3(c1, part[c3][:rows])
    add_2(c2)
    back(c0)

    near = lambda: jnp.where(low, mlp_part[1], mlp_part[2])
    edge = lambda: jnp.where(low, mlp_part[0], mlp_part[3])
    leave_far = lambda: jnp.where(low, mlp_part[3], mlp_part[0])
    leave_near = lambda: jnp.where(low, mlp_part[2], mlp_part[1])
    total, coming, final, hidden, mlp_part, acc, dhid_t, sent = fence(
        total, coming, final, hidden, mlp_part, acc, dhid_t, sent
    )
    far_sum = add_3(c2, leave_far())
    add_2(c3)
    grad_mlp = keep_rows(*mlp_args, sent, units // 2)
    hidden, grad_mlp = fence(hidden, grad_mlp)
    grad_mlp = scatter(grad_mlp)
    back(c1)
    total, coming, final, hidden, mlp_part, far_sum, acc, dhid_t = fence(
        total, coming, final, hidden, mlp_part, far_sum, acc, dhid_t
    )
    near_sum = add_3(c3, leave_near())
    far_in = along(leave_far() + far_sum, MIDDLE)
    back(c2)
    total, final, hidden, mlp_part, near_sum, far_in, acc, dhid_t = fence(
        total, final, hidden, mlp_part, near_sum, far_in, acc, dhid_t
    )
    last = along(jnp.where(inner, edge() + far_in, near()), PAIRS)
    near_in = along(leave_near() + near_sum, MIDDLE)
    dhid_t[c3], dqkv_own[c3] = back_own(c3)
    q_cols = heads_here * HD
    attn_args = (
        [listed(dhid_t), normed_one_t],
        [(0, listed(own)), (1, listed(dqkv_own))],
    )
    sent = swap_rows(send_rows(*attn_args, q_cols, send_turned))
    total, final, hidden, acc, sent = fence(total, final, hidden, acc, sent)
    if by_hand:
        half = slice_rows // 2
        upper = lambda m: (m * slice_rows, half)
        lower = lambda m: (m * slice_rows + half, half)
        picked = [
            [upper(1), upper(3)],
            [upper(0), upper(2)],
            [lower(2), lower(3)],
            [lower(0), lower(1)],
        ]
        pieces = keep_rows(*attn_args, sent, q_cols, keep_turned, picked)
        pieces, hidden = fence(pieces, hidden)
        one_away, one, two_away, two = pieces
        pieces = (one, to_chip(one_away, 1), two, to_chip(two_away, 2))
    else:
        pieces = scatter(sent)
    back(c3)
    pieces, gains, input_grad, last, near_in = fence(pieces, gains, input_grad, last, near_in)
    gain_sums = gains[0] + gains[1] + gains[2] + gains[3]
    gain_sums = gain_sums + swap(gain_sums)
    if by_hand:
        others = [to_chip(gain_sums, m) for m in range(1, chips)]
        gain_sums = sum(others, gain_sums)
        one = pieces[0] + pieces[1]
        two = pieces[2] + pieces[3]
        one = one[:half] + to_chip(one[half:], 2)
        two = two[:half] + to_chip(two[half:], 1)
        attn = jnp.concatenate([one, two], 0)
    else:
        gain_sums = lax.psum(gain_sums, "chip")
        attn = pieces
    gain_rows = lax.dynamic_slice_in_dim(gain_sums, at_row, slice_rows, 1)
    grad_out, grad_qkv = attn[:, :q_cols], attn[:, q_cols:]
    mlp_rows = jnp.where(inner, near() + near_in, edge()) + last
    hidden_rows = jnp.where(
        low,
        jnp.where(level == 0, hidden[0], hidden[1]),
        jnp.where(level == 2, hidden[2], hidden[3]),
    )
    layer_out = (hidden_rows + mlp_rows).astype(jnp.bfloat16)
    one = strip_one.shape[1]
    picked = lambda at, width: jnp.concatenate(
        [grad_qkv[:, kv * one + at : kv * one + at + width] for kv in range(kv_here)], 1
    )
    return (
        layer_out,
        jnp.concatenate(listed(input_grad), 0),
        gain_rows[0],
        picked(0, GROUP * HD),
        picked(GROUP * HD, HD),
        picked((GROUP + 1) * HD, HD),
        grad_out.T,
        gain_rows[1],
        grad_mlp[:, :units],
        grad_mlp[:, units : 2 * units],
        grad_mlp[:, 2 * units :].T,
    )


def solution(mesh):
    devices = mesh.devices
    dp, tp = devices.shape
    split = Mesh(devices.reshape(dp // 2, 2, tp), ("chip", "core", "tp"))
    data = ("chip", "core")
    return jax.shard_map(
        shards,
        mesh=split,
        in_specs=(
            P(data, None),
            P(data),
            P(data),
            P(data, None),
            P(),
            P(None, "tp"),
            P(None, "tp"),
            P(None, "tp"),
            P("tp", None),
            P(),
            P(None, "tp"),
            P(None, "tp"),
            P("tp", None),
        ),
        out_specs=(
            P(("chip", "core", "tp"), None),
            P(data, None),
            P(data),
            P(data, "tp"),
            P(data, "tp"),
            P(data, "tp"),
            P("tp", data),
            P(data),
            P(data, "tp"),
            P(data, "tp"),
            P("tp", data),
        ),
        check_vma=False,
    )
```

```python
import functools

import jax
import jax.numpy as jnp
from jax import lax
from jax.experimental import pallas as pl
from jax.experimental.pallas import tpu as pltpu
from jax.sharding import Mesh
from jax.sharding import PartitionSpec as P

HD = 96
LANES = 128
GROUP = 2
KV_WIDE = (GROUP + 2) * LANES
rope_base = 100000.0
norm_eps = 1e-05
masked_score = -1e30
far_away = 1e30
score_scale = HD ** (-0.5)
score_scale_log2 = score_scale * 1.4426950408889634
CHUNKS = 4
EXTRA = 8
VMEM_BYTES = 56 * 1024 * 1024
NT = (((1,), (1,)), ((), ()))


def params():
    return pltpu.CompilerParams(vmem_limit_bytes=VMEM_BYTES)


def cost(flops, moved, exps=0):
    return pl.CostEstimate(
        flops=flops // 1024, bytes_accessed=moved // 1024, transcendentals=exps // 1024
    )


def dot32(a, b):
    return jnp.dot(a, b, preferred_element_type=jnp.float32)


def dot32_nt(a, b):
    return lax.dot_general(a, b, NT, preferred_element_type=jnp.float32)


def dot_split(a, places):
    high = a.astype(jnp.bfloat16)
    rest = (a - high.astype(jnp.float32)).astype(jnp.bfloat16)
    return dot32(high, places) + dot32(rest, places)


def fence(*trees):
    return lax.optimization_barrier(trees)


def whole(array, buffers=None):
    zeros = (0,) * len(array.shape)
    return pl.BlockSpec(array.shape, lambda *_: zeros)


SCALAR = pl.BlockSpec(memory_space=pltpu.SMEM)


def halves(entry):
    half_dim = HD // 2
    return (entry // half_dim) * (LANES // 2) + entry % half_dim


def placement(lanes, width):
    return (lanes[:, None] == jnp.arange(width)[None, :]).astype(jnp.bfloat16)


def place_query(heads):
    source = jnp.arange(heads * HD)
    return placement((source // HD) * LANES + halves(source % HD), heads * LANES)


def place_key_value(kv_heads):
    source = jnp.arange(kv_heads * HD)
    head = source // HD
    keys = head * 2 * LANES + halves(source % HD)
    values = head * 2 * LANES + LANES + source % HD
    return placement(jnp.concatenate([keys, values]), kv_heads * 2 * LANES)


def place_all(heads, kv_heads):
    source = jnp.arange(heads * HD)
    head = source // HD
    query = (head // GROUP) * KV_WIDE + (head % GROUP) * LANES + halves(source % HD)
    source = jnp.arange(kv_heads * HD)
    base = (source // HD) * KV_WIDE + GROUP * LANES
    keys = base + halves(source % HD)
    values = base + LANES + source % HD
    return placement(jnp.concatenate([query, keys, values]), kv_heads * KV_WIDE)


def place_plain(heads):
    source = jnp.arange(heads * HD)
    return placement((source // HD) * LANES + source % HD, heads * LANES)


PAIRS = [(0, 1), (1, 0), (2, 3), (3, 2)]
INWARD = [(0, 1), (3, 2)]
MIDDLE = [(1, 2), (2, 1)]
OUTWARD = [(1, 0), (2, 3)]


def along(part, pairs):
    return lax.ppermute(part, "tp", pairs)


def store_qkv(out_ref, here, base, query, key_value):
    wide = GROUP * LANES
    for kv in range(key_value.shape[1] // (2 * LANES)):
        at = base + kv * KV_WIDE
        there = slice(kv * 2 * LANES, (kv + 1) * 2 * LANES)
        out_ref[here, at : at + wide] = query[:, kv * wide : (kv + 1) * wide]
        out_ref[here, at + wide : at + KV_WIDE] = key_value[:, there]


def store_turned(out_ref, at, lin, cos_ref, sin_ref):
    for h in range(GROUP + 2):
        one = lin[:, h * LANES : (h + 1) * LANES]
        if h < GROUP + 1:
            one = one * cos_ref[...] + pltpu.roll(one, LANES // 2, 1) * sin_ref[...]
        out_ref[:, at + h * LANES : at + (h + 1) * LANES] = one.astype(jnp.bfloat16)


def spread_out_kernel(meta_ref, own_ref, p_ref, mine_ref, theirs_ref, pad_ref, plain_ref):
    rows, width = mine_ref.shape[2:]
    wide = p_ref.shape[1]
    for side, ref in enumerate((mine_ref, theirs_ref)):
        here = pl.ds(pl.multiple_of((meta_ref[1] ^ side) * rows, rows), rows)
        for s in range(4):
            block = own_ref[here, :] if s == 0 else ref[0, s - 1].astype(jnp.bfloat16)
            plain_ref[here, s * width : (s + 1) * width] = block
            pad_ref[here, s * wide : (s + 1) * wide] = dot32(block, p_ref[...]).astype(
                jnp.bfloat16
            )


def spread_qkv_kernel(own_ref, pq_ref, pkv_ref, far_ref, out_ref):
    parts, others, rows, width = far_ref.shape
    wide = own_ref.shape[1]
    split = pq_ref.shape[0]
    out_ref[:, :wide] = own_ref[...]
    for s in range(others):
        block = far_ref[:, s].reshape(parts * rows, width).astype(jnp.bfloat16)
        query = dot32(block[:, :split], pq_ref[...]).astype(jnp.bfloat16)
        key_value = dot32(block[:, split:], pkv_ref[...]).astype(jnp.bfloat16)
        store_qkv(out_ref, slice(None), (s + 1) * wide, query, key_value)


def spread_qkv(own, pq, pkv, far):
    total, wide = own.shape
    dp, others, rows, width = far.shape
    parts = max(1, dp // 4)
    block = parts * rows
    return pl.pallas_call(
        spread_qkv_kernel,
        out_shape=jax.ShapeDtypeStruct((total, (others + 1) * wide), jnp.bfloat16),
        grid=(total // block,),
        in_specs=[
            pl.BlockSpec((block, wide), lambda i: (i, 0)),
            whole(pq),
            whole(pkv),
            pl.BlockSpec((parts, others, rows, width), lambda i: (i, 0, 0, 0)),
        ],
        out_specs=pl.BlockSpec((block, (others + 1) * wide), lambda i: (i, 0)),
        compiler_params=params(),
        cost_estimate=cost(8 * total * width * 512, 20 * total * wide),
    )(own, pq, pkv, far)


def spread(kernel, meta, own, places, mine, theirs, widths):
    chips, others, rows, width = mine.shape
    total = own.shape[0]
    row_block = lambda m, meta: (meta[0] ^ m, 0)
    piece = pl.BlockSpec((1, others, rows, width), lambda m, meta: (m, 0, 0, 0))
    return pl.pallas_call(
        kernel,
        out_shape=[jax.ShapeDtypeStruct((total, wide), jnp.bfloat16) for wide in widths],
        grid_spec=pltpu.PrefetchScalarGridSpec(
            num_scalar_prefetch=1,
            grid=(chips,),
            in_specs=[pl.BlockSpec((2 * rows, own.shape[1]), row_block)]
            + [whole(place) for place in places]
            + [piece, piece],
            out_specs=[pl.BlockSpec((2 * rows, wide), row_block) for wide in widths],
        ),
        compiler_params=params(),
        cost_estimate=cost(
            8 * total * width * 512, total * (12 * width + 2 * sum(widths))
        ),
    )(meta, own, *places, mine, theirs)


def start_kernel(x_ref, gain_ref, q_ref, k_ref, v_ref, pq_ref, pkv_ref, cos_ref, sin_ref, *outs):
    qkv_ref, normed_ref, pad_ref = outs

    @pl.when(pl.program_id(0) == 0)
    def _():
        split = k_ref.shape[0]
        query = dot32(q_ref[...], pq_ref[...]).astype(jnp.bfloat16)
        key_value = dot32(k_ref[...].T, pkv_ref[:split, :])
        key_value = key_value + dot32(v_ref[...].T, pkv_ref[split:, :])
        store_qkv(pad_ref, slice(None), 0, query, key_value.astype(jnp.bfloat16))

    inputs = x_ref[...].astype(jnp.float32)
    rms = lax.rsqrt(jnp.mean(inputs * inputs, -1, keepdims=True) + norm_eps)
    normed = (inputs * rms * gain_ref[...]).astype(jnp.bfloat16)
    normed_ref[...] = normed
    for kv in range(pad_ref.shape[1] // KV_WIDE):
        at = kv * KV_WIDE
        store_turned(qkv_ref, at, dot32(normed, pad_ref[:, at : at + KV_WIDE]), cos_ref, sin_ref)


def start(tokens, gain, w_query, w_key_t, w_value_t, pq, pkv, cosines, sines):
    total, depth = tokens.shape
    rows = total // CHUNKS
    wide = pq.shape[1] + pkv.shape[1]
    gain = gain[None, :]
    by_rows = lambda width: pl.BlockSpec((rows, width), lambda i: (i, 0))
    arrays = [w_query, w_key_t, w_value_t, pq, pkv]
    shapes = [
        jax.ShapeDtypeStruct((total, wide), jnp.bfloat16),
        jax.ShapeDtypeStruct((total, depth), jnp.bfloat16),
        jax.ShapeDtypeStruct((depth, wide), jnp.bfloat16),
    ]
    return pl.pallas_call(
        start_kernel,
        out_shape=shapes,
        grid=(CHUNKS,),
        in_specs=[by_rows(depth), whole(gain)]
        + [whole(array) for array in arrays]
        + [by_rows(LANES), by_rows(LANES)],
        out_specs=[by_rows(wide), by_rows(depth), whole(shapes[2])],
        compiler_params=params(),
        cost_estimate=cost(2 * total * depth * wide, 12 * total * depth),
    )(tokens, gain, *arrays, cosines, sines)


def turn_kernel(length_ref, cot_ref, normed_ref, dout_ref, dout_t_ref, normed_t_ref):
    rows = cot_ref.shape[0]
    at = pl.program_id(0) * rows + lax.broadcasted_iota(jnp.int32, cot_ref.shape, 0)
    dout = jnp.where(at < length_ref[0], cot_ref[...].astype(jnp.float32), 0.0)
    dout = dout.astype(jnp.bfloat16)
    dout_ref[...] = dout
    dout_t_ref[...] = dout.T
    normed_t_ref[...] = normed_ref[...].T


def turn(length, cotangent, normed):
    total, depth = cotangent.shape
    rows = total // CHUNKS
    by_rows = pl.BlockSpec((rows, depth), lambda i: (i, 0))
    by_columns = pl.BlockSpec((depth, rows), lambda i: (0, i))
    turned = jax.ShapeDtypeStruct((depth, total), jnp.bfloat16)
    return pl.pallas_call(
        turn_kernel,
        out_shape=[jax.ShapeDtypeStruct((total, depth), jnp.bfloat16), turned, turned],
        grid=(CHUNKS,),
        in_specs=[SCALAR, by_rows, by_rows],
        out_specs=[by_rows, by_columns, by_columns],
        compiler_params=params(),
        cost_estimate=cost(total * depth, 10 * total * depth),
    )(length, cotangent, normed)


def project_kernel(x_ref, w_ref, cos_ref, sin_ref, out_ref):
    store_turned(out_ref, 0, dot32(x_ref[...], w_ref[...]), cos_ref, sin_ref)


def project(normed, weights, cosines, sines):
    rows, depth = normed.shape
    width = weights.shape[1]
    return pl.pallas_call(
        project_kernel,
        out_shape=jax.ShapeDtypeStruct((rows, width), jnp.bfloat16),
        grid=(width // KV_WIDE,),
        in_specs=[
            whole(normed),
            pl.BlockSpec((depth, KV_WIDE), lambda i: (0, i)),
            whole(cosines),
            whole(sines),
        ],
        out_specs=pl.BlockSpec((rows, KV_WIDE), lambda i: (0, i)),
        compiler_params=params(),
        cost_estimate=cost(
            2 * rows * depth * width, 2 * (rows * depth + depth * width + rows * width)
        ),
    )(normed, weights, cosines, sines)


def attend_kernel(start, length_ref, q_ref, kv_ref, strip_ref, out_ref):
    rows = q_ref.shape[0]
    keys = kv_ref.shape[0]
    length = length_ref[0]
    row_ids = start + lax.broadcasted_iota(jnp.int32, (1, rows), 1)
    limit = jnp.minimum(row_ids, length - 1)
    allowed = lax.broadcasted_iota(jnp.int32, (keys, rows), 0) <= limit
    mixed = []
    sums = []
    for kv in range(kv_ref.shape[1] // KV_WIDE):
        base = kv * KV_WIDE
        at = base + GROUP * LANES
        key = kv_ref[:, at : at + LANES]
        value_t = kv_ref[:, at + LANES : at + 2 * LANES].T
        for g in range(GROUP):
            query = q_ref[:, base + g * LANES : base + (g + 1) * LANES]
            raw = jnp.where(allowed, dot32_nt(key, query), masked_score)
            peak = jnp.max(raw, axis=0, keepdims=True)
            expo = jnp.exp2((raw - peak) * score_scale_log2)
            total = jnp.sum(expo, axis=0, keepdims=True)
            probs = (expo * (1.0 / total)).astype(jnp.bfloat16)
            mixed.append(dot32(value_t, probs).T)
            log_sum = peak * score_scale_log2 + jnp.log2(total)
            sums.append(jnp.where(row_ids < length, log_sum, far_away))
    out_ref[:rows, :] = dot_split(jnp.concatenate(mixed, 1), strip_ref[...])
    out_ref[rows:, :] = jnp.zeros((EXTRA, out_ref.shape[1]), jnp.float32)
    out_ref[rows : rows + len(sums), :rows] = jnp.concatenate(sums, 0)


def attend(length, qkv, strip, index, rows):
    keys = (index + 1) * rows
    width = qkv.shape[1]
    heads = width // KV_WIDE * GROUP
    shape = (rows + EXTRA, strip.shape[1])
    return pl.pallas_call(
        functools.partial(attend_kernel, index * rows),
        out_shape=jax.ShapeDtypeStruct(shape, jnp.float32),
        grid=(1,),
        in_specs=[
            SCALAR,
            pl.BlockSpec((rows, width), lambda i: (index, 0)),
            pl.BlockSpec((keys, width), lambda i: (0, 0)),
            whole(strip),
        ],
        out_specs=pl.BlockSpec(shape, lambda i: (0, 0)),
        compiler_params=params(),
        cost_estimate=cost(
            4 * heads * rows * keys * LANES, 2 * (rows + keys) * width, heads * rows * keys
        ),
    )(length, qkv, qkv, strip)


def forward_kernel(level_ref, part_ref, other_ref, across_ref, outer_ref, *refs):
    x_ref, dout_ref, wo_ref, gain_ref, wg_ref, wu_ref, wd_ref = refs[:7]
    hidden_ref, normed_t_ref, activ_ref, dgate_ref, dup_ref, mlp_ref, dn_ref = refs[7:14]
    normed_ref = refs[14]
    rows = x_ref.shape[0]
    width = part_ref.shape[1]
    step = pl.program_id(0)
    level = level_ref[0]
    inner = (level == 1) | (level == 2)

    def mixed_of(s):
        if s < 2:
            return (part_ref, other_ref)[s][:rows, :]
        first, second = slice(0, width), slice(width, 2 * width)
        one, two = (second, first) if s == 2 else (first, second)
        return jnp.where(inner, across_ref[:rows, one], outer_ref[:rows, two])

    for s in range(4):

        @pl.when(step == s)
        def _(s=s):
            product = dot32_nt(mixed_of(s).astype(jnp.bfloat16), wo_ref[...])
            if s == 0:
                hidden_ref[...] = x_ref[...].astype(jnp.float32) + product
            else:
                hidden_ref[...] += product

    @pl.when(step == 3)
    def _():
        hidden = hidden_ref[...]
        rms = lax.rsqrt(jnp.mean(hidden * hidden, -1, keepdims=True) + norm_eps)
        normed = (hidden * rms * gain_ref[...]).astype(jnp.bfloat16)
        normed_ref[...] = normed
        normed_t_ref[...] = normed.T
        mlp_ref[...] = jnp.zeros_like(mlp_ref)
        dn_ref[...] = jnp.zeros_like(dn_ref)

    @pl.when(step >= 4)
    def _():
        normed = normed_ref[...]
        gate = dot32(normed, wg_ref[...])
        up = dot32(normed, wu_ref[...])
        dact = dot32_nt(dout_ref[...], wd_ref[...])
        sigmoid = jax.nn.sigmoid(gate)
        silu = gate * sigmoid
        activ = (silu * up).astype(jnp.bfloat16)
        dgate = (dact * up * sigmoid * (1.0 + gate * (1.0 - sigmoid))).astype(jnp.bfloat16)
        dup = (dact * silu).astype(jnp.bfloat16)
        activ_ref[...] = activ
        dgate_ref[...] = dgate
        dup_ref[...] = dup
        mlp_ref[...] += dot32(activ, wd_ref[...])
        dn_ref[:rows, :] += dot32_nt(dgate, wg_ref[...]) + dot32_nt(dup, wu_ref[...])


def forward_chunk(level, gathered, tokens, dout, w_out, gain, w_gate, w_up, w_down, index, rows):
    depth = tokens.shape[1]
    units = w_gate.shape[1]
    block = 256
    own_rows = pl.BlockSpec((rows, depth), lambda i: (index, 0))
    unit = lambda i: jnp.maximum(i - 4, 0)
    by_units = pl.BlockSpec((depth, block), lambda i: (0, unit(i)))
    by_level = pl.BlockSpec((depth, w_out.shape[1] // 4), lambda i: (0, jnp.minimum(i, 3)))
    gain = gain[None, :]
    f32, bf16 = jnp.float32, jnp.bfloat16
    outs = [
        jax.ShapeDtypeStruct((rows, depth), f32),
        jax.ShapeDtypeStruct((depth, rows), bf16),
        jax.ShapeDtypeStruct((rows, units), bf16),
        jax.ShapeDtypeStruct((rows, units), bf16),
        jax.ShapeDtypeStruct((rows, units), bf16),
        jax.ShapeDtypeStruct((rows, depth), f32),
        jax.ShapeDtypeStruct((rows + EXTRA, depth), f32),
    ]
    unit_out = pl.BlockSpec((rows, block), lambda i: (0, unit(i)))
    return pl.pallas_call(
        forward_kernel,
        out_shape=outs,
        grid=(4 + units // block,),
        in_specs=[SCALAR]
        + [whole(array) for array in gathered]
        + [own_rows, own_rows, by_level, whole(gain), by_units, by_units]
        + [pl.BlockSpec((block, depth), lambda i: (unit(i), 0))],
        out_specs=[
            whole(outs[0]),
            whole(outs[1]),
            unit_out,
            unit_out,
            unit_out,
            whole(outs[5]),
            whole(outs[6]),
        ],
        scratch_shapes=[pltpu.VMEM((rows, depth), bf16)],
        compiler_params=params(),
        cost_estimate=cost(
            2 * rows * depth * (6 * units + w_out.shape[1]),
            2 * depth * (3 * units + w_out.shape[1]) + 22 * rows * depth,
            rows * units,
        ),
    )(level, *gathered, tokens, dout, w_out, gain, w_gate, w_up, w_down)


def hidden_grad(inner, total_ref, final_ref, hidden_ref, dout_ref, gain_ref):
    dnormed = jnp.where(inner, total_ref[...], final_ref[...])
    hidden = hidden_ref[...]
    rms = lax.rsqrt(jnp.mean(hidden * hidden, -1, keepdims=True) + norm_eps)
    scaled = dnormed * gain_ref[...]
    shift = jnp.mean(scaled * hidden, -1, keepdims=True)
    dhid = dout_ref[...].astype(jnp.float32) + (rms * scaled - hidden * (rms**3 * shift))
    return dhid, dnormed * (hidden * rms)


def backward_kernel(start, full, level_ref, total_ref, final_ref, hidden_ref, dout_ref, x_ref, *refs):
    gain_one_ref, gain_two_ref, wo_ref, q_ref = refs[:4]
    kv_here = q_ref.shape[1] // KV_WIDE
    refs = refs[4:]
    kv_refs, refs = refs[: 2 * kv_here], refs[2 * kv_here :]
    part_ref, other_ref, across_ref, outer_ref, place_ref, strip_ref = refs[:6]
    cos_ref, sin_ref = refs[6:8]
    dhid_ref, low_ref, dn_ref = refs[-3:]
    outs = refs[8:-3]
    if full:
        w_ref, outs = outs[0], outs[1:]
    count = (5 if start > 0 else 4) if full else 2
    acc_ref = outs[0] if len(outs) > count else None
    outs = outs[-count:]
    dhid_t_ref, dqkv_ref = outs[:2]
    if full:
        input_grad_ref, gains_ref = outs[2:4]
    rows = q_ref.shape[0]
    keys = kv_refs[0].shape[0]
    shard = pl.program_id(0)
    level = level_ref[0]
    inner = (level == 1) | (level == 2)

    @pl.when(shard == 0)
    def _():
        dhid, dgain = hidden_grad(
            inner, total_ref, final_ref, hidden_ref, dout_ref, gain_two_ref
        )
        dhid_ref[...] = dhid
        low = dhid.astype(jnp.bfloat16)
        low_ref[...] = low
        dhid_t_ref[...] = low.T
        if full:
            gains_ref[...] = jnp.zeros_like(gains_ref)
            gains_ref[1:2, :] = jnp.sum(dgain, 0, keepdims=True)
            dn_ref[...] = jnp.zeros_like(dn_ref)

    def rotate_back(grads):
        turned = grads * cos_ref[...] - pltpu.roll(grads, LANES // 2, 1) * sin_ref[...]
        return turned.astype(jnp.bfloat16)

    dmixed_all = dot32(low_ref[...], wo_ref[...]).astype(jnp.bfloat16)
    mixed = jnp.where(
        shard == 0,
        part_ref[...],
        jnp.where(shard == 1, other_ref[...], jnp.where(inner, across_ref[...], outer_ref[...])),
    )
    products = dmixed_all.astype(jnp.float32) * dot_split(mixed[:rows], place_ref[...])
    causal = lax.broadcasted_iota(jnp.int32, (rows, rows), 0) <= lax.broadcasted_iota(
        jnp.int32, (rows, rows), 1
    )
    grads = []
    for kv in range(kv_here):
        key_ref, value_ref = kv_refs[2 * kv : 2 * kv + 2]
        heads = range(kv * GROUP, (kv + 1) * GROUP)
        lanes = {h: slice(h * LANES, (h + 1) * LANES) for h in heads}
        row_dots = {h: jnp.sum(products[:, lanes[h]].T, axis=0, keepdims=True) for h in heads}
        log_sums = {h: mixed[rows + h : rows + h + 1, :rows] for h in heads}
        dqueries = dict.fromkeys(heads)
        here = slice(2 * kv * LANES, (2 * kv + 1) * LANES)
        there = slice((2 * kv + 1) * LANES, (2 * kv + 2) * LANES)
        for tile in range(keys // rows):
            span = slice(tile * rows, (tile + 1) * rows)
            key = key_ref[span, :]
            value = value_ref[span, :]
            key_t = key.T
            dkey = None if acc_ref is None else acc_ref[span, here]
            dvalue = None if acc_ref is None else acc_ref[span, there]
            last = tile * rows == start
            for h in heads:
                at = kv * KV_WIDE + (h % GROUP) * LANES
                query = q_ref[:, at : at + LANES]
                dmixed = dmixed_all[:, lanes[h]]
                raw = dot32_nt(key, query)
                probs = jnp.exp2(raw * score_scale_log2 - log_sums[h])
                if last:
                    probs = jnp.where(causal, probs, 0.0)
                dprobs = dot32_nt(value, dmixed)
                dscores = (probs * (dprobs - row_dots[h])).astype(jnp.bfloat16)
                dquery = dot32(key_t, dscores)
                dqueries[h] = dquery if dqueries[h] is None else dqueries[h] + dquery
                dkey_one = dot32(dscores, query)
                dvalue_one = dot32(probs.astype(jnp.bfloat16), dmixed)
                dkey = dkey_one if dkey is None else dkey + dkey_one
                dvalue = dvalue_one if dvalue is None else dvalue + dvalue_one
            if full and not last:
                outs[4][span, here] = dkey
                outs[4][span, there] = dvalue
        grads += [rotate_back(dqueries[h].T * score_scale) for h in heads]
        grads.append(rotate_back(dkey * score_scale))
        grads.append(dvalue.astype(jnp.bfloat16))
    grads = jnp.concatenate(grads, 1)
    if full:
        dn_ref[...] += dot32_nt(grads, w_ref[...])

    @pl.when(shard == 0)
    def _():
        dqkv_ref[...] = dot32(grads, strip_ref[...]).astype(jnp.bfloat16)

    if not full:
        return

    @pl.when(shard == pl.num_programs(0) - 1)
    def _():
        dnormed = dn_ref[...]
        inputs = x_ref[...].astype(jnp.float32)
        rms = lax.rsqrt(jnp.mean(inputs * inputs, -1, keepdims=True) + norm_eps)
        scaled = dnormed * gain_one_ref[...]
        shift = jnp.mean(scaled * inputs, -1, keepdims=True)
        grad = dhid_ref[...] + (rms * scaled - inputs * (rms**3 * shift))
        input_grad_ref[...] = grad.astype(jnp.bfloat16)
        gains_ref[0:1, :] = jnp.sum(dnormed * (inputs * rms), 0, keepdims=True)


def backward_chunk(
    level, sums_two, hidden, dout, tokens, gains, weights, qkv, gathered, places, tables, acc,
    index, rows, full=True
):
    start = index * rows
    keys = start + rows
    depth = tokens.shape[1]
    out_pad, qkv_pad = weights
    place_out, strip = places
    far_rows, width = gathered[0].shape
    out_wide = place_out.shape[1]
    kv_here = out_wide // (GROUP * LANES)
    wide = kv_here * KV_WIDE
    levels = qkv.shape[1] // wide
    own_rows = pl.BlockSpec((rows, depth), lambda t: (index, 0))
    table = pl.BlockSpec((rows, LANES), lambda t: (index, 0))
    gains = [gain[None, :] for gain in gains]
    key_value = lambda at: pl.BlockSpec(
        (keys, LANES), lambda t: (0, (wide // LANES) * t + at)
    )
    across = pl.BlockSpec((far_rows, width), lambda t: (0, jnp.where(t == 2, 1, 0)))
    outer = pl.BlockSpec((far_rows, width), lambda t: (0, jnp.where(t == 3, 1, 0)))
    in_specs = [
        SCALAR,
        whole(sums_two[0]),
        whole(sums_two[1]),
        whole(hidden),
        own_rows,
        own_rows,
        whole(gains[0]),
        whole(gains[1]),
        pl.BlockSpec((depth, out_wide), lambda t: (0, t)),
        pl.BlockSpec((rows, wide), lambda t: (index, t)),
    ]
    for kv in range(kv_here):
        at = kv * (KV_WIDE // LANES) + GROUP
        in_specs += [key_value(at), key_value(at + 1)]
    in_specs += [
        whole(gathered[0]),
        whole(gathered[1]),
        across,
        outer,
        whole(place_out),
        whole(strip),
        table,
        table,
    ]
    args = [level, *sums_two, hidden, dout, tokens, *gains, out_pad]
    args += [qkv] * (1 + 2 * kv_here)
    args += [*gathered, place_out, strip, *tables]
    sums_wide = 2 * kv_here * LANES
    if full:
        in_specs.append(pl.BlockSpec((depth, wide), lambda t: (0, t)))
        args.append(qkv_pad)
    if acc is not None:
        in_specs.append(pl.BlockSpec((keys, sums_wide), lambda t: (0, t)))
        args.append(acc)
    f32, bf16 = jnp.float32, jnp.bfloat16
    outs = [
        jax.ShapeDtypeStruct((depth, rows), bf16),
        jax.ShapeDtypeStruct((rows, strip.shape[1]), bf16),
        jax.ShapeDtypeStruct((rows, depth), bf16),
        jax.ShapeDtypeStruct((8, depth), f32),
    ]
    outs = outs if full else outs[:2]
    out_specs = [whole(out) for out in outs]
    if full and start > 0:
        outs.append(jax.ShapeDtypeStruct((start, levels * sums_wide), f32))
        out_specs.append(pl.BlockSpec((start, sums_wide), lambda t: (0, t)))
    results = pl.pallas_call(
        functools.partial(backward_kernel, start, full),
        out_shape=outs,
        grid=(levels if full else 1,),
        in_specs=in_specs,
        out_specs=out_specs,
        scratch_shapes=[
            pltpu.VMEM((rows, depth), f32),
            pltpu.VMEM((rows, depth), bf16),
            pltpu.VMEM((rows, depth), f32),
        ],
        compiler_params=params(),
        cost_estimate=cost(
            levels * rows * (20 * kv_here * keys * LANES + 2 * depth * (out_wide + wide)),
            2 * depth * levels * (out_wide + wide) + 16 * rows * depth,
            levels * kv_here * GROUP * rows * keys,
        ),
    )(*args)
    return results[:4], (results[4] if full and start > 0 else None)


def rows_kernel(lefts, groups, adding, picked, together, side_ref, *refs):
    refs = list(refs)
    held_ref = refs.pop()
    out_refs = refs[-len(picked) :]
    refs = refs[: -len(picked)]
    recv_ref = refs.pop() if adding else None
    step = pl.program_id(0)
    left_refs = []
    for count in lefts:
        left_refs.append(refs[:count])
        refs = refs[count:]
    rights = []
    for _ in groups:
        rights.append(refs[:CHUNKS])
        refs = refs[CHUNKS:]
    rows = left_refs[0][0].shape[0]
    blocks = held_ref.shape[1] // rows

    @pl.when(step == 0)
    def _():
        for which, pieces in enumerate(left_refs):
            for n, ref in enumerate(pieces):
                m, j = n % blocks, n // blocks
                wide = ref.shape[1]
                held_ref[which, m * rows : (m + 1) * rows, j * wide : (j + 1) * wide] = ref[...]

    chunk = held_ref.shape[2] // CHUNKS
    whole_columns = slice(0, out_refs[0].shape[1])

    def give(group, left, columns):
        right = jnp.concatenate([ref[:chunk, :].astype(jnp.bfloat16) for ref in group], 0)
        total = dot32(held_ref[left], right)
        if recv_ref is not None:
            total = total + recv_ref[:, columns]
        for out_ref, parts in zip(out_refs, picked):
            at = 0
            for start, size in parts:
                out_ref[at : at + size, columns] = total[start : start + size]
                at += size

    begin = 0
    for group, (left, first, steps) in zip(rights, groups):
        if together:
            width = group[0].shape[1]
            give(group, left, slice(begin, begin + width))
            begin += width
        else:

            @pl.when((step >= first) & (step < first + steps))
            def _(group=group, left=left):
                give(group, left, whole_columns)


def rows_of(lefts, groups, side, rows, blocks, step, recv=None, picked=None):
    if picked is None:
        picked = [[(0, rows * blocks)]]
    at = lambda m: lambda i, side: ((m ^ side[2]) * side[1] + side[0], 0)
    specs = []
    args = []
    counts = []
    for left in lefts:
        pieces = left if isinstance(left, list) else [left]
        counts.append(len(pieces) * blocks)
        for piece in pieces:
            for m in range(blocks):
                specs.append(pl.BlockSpec((rows, piece.shape[1]), at(m)))
                args.append(piece)
    tokens = sum(piece.shape[1] for piece in pieces)
    first = 0
    plan = []
    together = step is None
    for which, rights in groups:
        if together:
            plan.append((which, 0, 1))
            specs += [whole(right) for right in rights]
            args += rights
            first += rights[0].shape[1]
            continue
        steps = rights[0].shape[1] // step
        plan.append((which, first, steps))
        for right in rights:
            pick = lambda i, side, first=first, steps=steps: (0, jnp.clip(i - first, 0, steps - 1))
            specs.append(pl.BlockSpec((right.shape[0], step), pick))
            args.append(right)
        first += steps
    if together:
        first, step = 1, first
    total = first * step
    block = lambda height: pl.BlockSpec((height, step), lambda i, side: (0, i))
    if recv is not None:
        specs.append(block(rows * blocks))
        args.append(recv)
    heights = [sum(size for _, size in parts) for parts in picked]
    results = pl.pallas_call(
        functools.partial(rows_kernel, counts, plan, recv is not None, picked, together),
        out_shape=[jax.ShapeDtypeStruct((height, total), jnp.float32) for height in heights],
        grid_spec=pltpu.PrefetchScalarGridSpec(
            num_scalar_prefetch=1,
            grid=(first,),
            in_specs=specs,
            out_specs=[block(height) for height in heights],
            scratch_shapes=[pltpu.VMEM((len(lefts), rows * blocks, tokens), jnp.bfloat16)],
        ),
        compiler_params=params(),
        cost_estimate=cost(
            2 * rows * blocks * tokens * total,
            4 * rows * blocks * total + 2 * tokens * (total + rows * blocks),
        ),
    )(side, *args)
    return results[0] if len(picked) == 1 else results


def shards(
    tokens,
    lengths,
    positions,
    cotangent,
    norm_gain,
    w_query,
    w_key,
    w_value,
    w_out,
    mlp_gain,
    w_gate,
    w_up,
    w_down,
):
    seq_rows, depth = tokens.shape
    chips = lax.axis_size("chip")
    dp = chips * 2
    tp = lax.axis_size("tp")
    chip = lax.axis_index("chip")
    core = lax.axis_index("core")
    level = lax.axis_index("tp")
    low = level < 2
    inner = (level == 1) | (level == 2)
    heads_here = w_query.shape[1] // HD
    kv_here = w_key.shape[1] // HD
    rows = seq_rows // CHUNKS
    slice_rows = depth // dp
    level_ref = level.astype(jnp.int32).reshape(1)
    by_hand = dp == 8
    swap = lambda array: lax.ppermute(array, "core", [(0, 1), (1, 0)])
    to_level = lambda array, s: along(array, [(t, t ^ s) for t in range(tp)])

    at_row = (chip * 2 + core) * slice_rows
    cols = lambda w: lax.dynamic_slice_in_dim(w, at_row, slice_rows, 1).astype(jnp.float32).T
    (out_slice,) = fence(cols(w_out))
    qkv_slice = jnp.concatenate(
        [
            lax.dynamic_slice_in_dim(w_query, at_row, slice_rows, 0).astype(jnp.float32),
            cols(w_key.T),
            cols(w_value.T),
        ],
        1,
    )
    out_slice, qkv_slice = fence(out_slice, qkv_slice)
    out_near = along(out_slice, PAIRS)
    qkv_near = along(qkv_slice, PAIRS)
    meta = jnp.stack([chip, core]).astype(jnp.int32)

    pq = place_query(heads_here)
    pkv = place_key_value(kv_here)
    p_all = place_all(heads_here, kv_here)
    p_out = place_plain(heads_here)
    strip_out = p_out.T

    half_dim = HD // 2
    freqs = rope_base ** (-(jnp.arange(half_dim).astype(jnp.float32) * 2.0 / HD))
    freqs = jnp.pad(freqs, (0, LANES // 2 - half_dim))
    angles = positions.astype(jnp.float32)[:, None] * jnp.concatenate([freqs, freqs])[None, :]
    cosines = jnp.cos(angles)
    sines = jnp.sin(angles) * jnp.where(jnp.arange(LANES) < LANES // 2, -1.0, 1.0)

    cosines, sines, out_near = fence(cosines, sines, out_near)
    out_across = along(jnp.stack([out_slice, out_near]), MIDDLE)
    qkv_own, normed_one, own_pad = start(
        tokens, norm_gain, w_query, w_key.T, w_value.T, pq, pkv, cosines, sines
    )

    def far_slices(near, across, outer):
        return jnp.stack(
            [
                near,
                jnp.where(inner, across[1], outer[0]),
                jnp.where(inner, across[0], outer[1]),
            ]
        )

    order = list(reversed(range(CHUNKS)))
    c0, c1, c2, c3 = order
    own, other, across, outer = {}, {}, {}, {}
    part, total, final = {}, {}, {}

    def hop_1(j):
        other[j] = along(own[j], PAIRS)

    def hop_2(j):
        across[j] = along(jnp.concatenate([own[j], other[j]], 1), MIDDLE)

    def hop_3(j):
        outer[j] = along(across[j], OUTWARD)

    coming = {}

    def add_1(j):
        coming[j] = along(part[j], INWARD)

    def add_2(j):
        total[j] = part[j][:rows] + coming[j][:rows]
        coming[j] = along(total[j], MIDDLE)

    def add_3(j, inward):
        total[j] = jnp.where(inner, total[j] + coming[j], inward)
        final[j] = along(total[j], PAIRS)
        return final[j]

    def to_chip(array, m):
        return lax.ppermute(array, "chip", [(i, i ^ m) for i in range(chips)])

    def over_chips_1(piece):
        cut = piece.shape[1] // 2
        one, two = piece[:, :cut], piece[:, cut:]
        return jnp.stack([one, to_chip(one, 1)]), jnp.stack([two, to_chip(two, 2)])

    def over_chips_2(one, two):
        return one, to_chip(one, 2), two, to_chip(two, 1)

    def over_chips_3(one, one_far, two, two_far):
        upper = jnp.stack([one[0], one[1], one_far[0], one_far[1]])
        lower = jnp.stack([two[0], two_far[0], two[1], two_far[1]])
        return jnp.concatenate([upper, lower], 2)

    qkv_own, out_across, qkv_near = fence(qkv_own, out_across, qkv_near)
    out_outer = along(out_across, OUTWARD)
    qkv_across = along(jnp.stack([qkv_slice, qkv_near]), MIDDLE)
    own[c0] = attend(lengths, qkv_own, strip_out, c0, rows)
    own, qkv_own, out_outer = fence(own, qkv_own, out_outer)
    hop_1(c0)
    out_far = far_slices(out_near, out_across, out_outer)
    out_mine = over_chips_1(out_far) if by_hand else out_far
    for j in (c1, c2):
        own[j] = attend(lengths, qkv_own, strip_out, j, rows)
    own, other, normed_one, w_out, out_mine, qkv_across, qkv_own = fence(
        own, other, normed_one, w_out, out_mine, qkv_across, qkv_own
    )
    own[c3] = attend(lengths, qkv_own, strip_out, c3, rows)
    hop_1(c1)
    qkv_outer = along(qkv_across, OUTWARD)
    if by_hand:
        out_mine = over_chips_2(*out_mine)
    else:
        out_mine = lax.all_gather(out_mine, ("chip", "core"))
    hop_2(c0)
    dout, dout_t, normed_one_t = turn(lengths, cotangent, normed_one)
    w_out_t = w_out.T
    own, other, across, dout, dout_t, normed_one_t, w_out_t, out_mine, qkv_outer = fence(
        own, other, across, dout, dout_t, normed_one_t, w_out_t, out_mine, qkv_outer
    )
    hop_1(c2)
    hop_3(c0)
    hop_2(c1)
    qkv_far = lax.all_gather(far_slices(qkv_near, qkv_across, qkv_outer), ("chip", "core"))
    if by_hand:
        out_mine = over_chips_3(*out_mine)
        out_theirs = swap(out_mine)
        out_pad, out_plain = spread(
            spread_out_kernel,
            meta,
            w_out_t,
            [p_out],
            out_mine,
            out_theirs,
            [4 * p_out.shape[1], 4 * p_out.shape[0]],
        )
    else:
        plain = [w_out_t] + [
            out_mine[:, s].reshape(depth, -1).astype(jnp.bfloat16) for s in range(tp - 1)
        ]
        out_plain = jnp.concatenate(plain, 1)
        out_pad = jnp.concatenate([dot32(w, p_out).astype(jnp.bfloat16) for w in plain], 1)
    hidden, normed_t, activ, dgate, dup, mlp_part = {}, {}, {}, {}, {}, {}

    def feed(j):
        gathered = (own[j], other[j], across[j], outer[j])
        (hidden[j], normed_t[j], activ[j], dgate[j], dup[j], mlp_part[j], part[j]) = forward_chunk(
            level_ref, gathered, tokens, dout, out_plain, mlp_gain, w_gate, w_up, w_down, j, rows
        )

    own, other, across, outer, out_pad, out_plain = fence(
        own, other, across, outer, out_pad, out_plain
    )
    hop_1(c3)
    hop_3(c1)
    hop_2(c2)
    feed(c0)
    own, other, across, outer, part, hidden = fence(own, other, across, outer, part, hidden)
    add_1(c0)
    hop_3(c2)
    hop_2(c3)
    feed(c1)
    outer[c2], hidden[c1] = fence(outer[c2], hidden[c1])
    feed(c2)
    own, other, across, outer, part, total, coming, hidden = fence(
        own, other, across, outer, part, total, coming, hidden
    )
    add_1(c1)
    hop_3(c3)
    add_2(c0)
    qkv_far, part = fence(qkv_far, part)
    qkv_pad = spread_qkv(own_pad, pq, pkv, qkv_far)
    qkv = project(normed_one, qkv_pad, cosines, sines)
    own, other, across, outer, part, total, coming, hidden, qkv = fence(
        own, other, across, outer, part, total, coming, hidden, qkv
    )
    coming[c2] = add_3(c0, part[c2][:rows])
    add_2(c1)
    feed(c3)

    listed = lambda pieces: [pieces[j] for j in range(CHUNKS)]
    keep_side = jnp.stack([core, 2, 0]).astype(jnp.int32)
    keep_turned = jnp.stack([core, 2, chip]).astype(jnp.int32)
    send_side = jnp.stack([1 - core, 2, 0]).astype(jnp.int32)
    send_turned = jnp.stack([1 - core, 2, chip]).astype(jnp.int32)
    all_rows = jnp.array([0, 1, 0], jnp.int32)

    def send_rows(lefts, groups, step, side=send_side):
        if not by_hand:
            return rows_of(lefts, groups, all_rows, depth // 4, 4, step)
        return rows_of(lefts, groups, side, slice_rows, chips, step)

    def keep_rows(lefts, groups, received, step, side=keep_side, picked=None):
        if not by_hand:
            return received
        return rows_of(lefts, groups, side, slice_rows, chips, step, received, picked)

    def swap_rows(array):
        return swap(array) if by_hand else array

    def scatter(array):
        axes = "chip" if by_hand else ("chip", "core")
        return lax.psum_scatter(array, axes, scatter_dimension=0, tiled=True)

    units = w_gate.shape[1]
    mlp_args = (
        [listed(normed_t), dout_t],
        [(0, listed(dgate)), (0, listed(dup)), (1, listed(activ))],
    )
    acc = None
    dhid_t, dqkv_own, input_grad, gains = {}, {}, {}, {}

    def back(j):
        nonlocal acc
        (dhid_t[j], dqkv_own[j], input_grad[j], gains[j]), acc = back_some(j, True)

    def back_own(j):
        return back_some(j, False)[0]

    def back_some(j, full):
        return backward_chunk(
            level_ref,
            (total[j], final[j]),
            hidden[j],
            dout,
            tokens,
            (norm_gain, mlp_gain),
            (out_pad, qkv_pad),
            qkv,
            (own[j], other[j], across[j], outer[j]),
            (p_out, p_all.T),
            (cosines, sines),
            acc,
            j,
            rows,
            full,
        )

    sent = send_rows(*mlp_args, units // 2)
    own, other, across, outer, part, total, coming, final, hidden, sent = fence(
        own, other, across, outer, part, total, coming, final, hidden, sent
    )
    sent = swap_rows(sent)
    coming[c3] = add_3(c1, part[c3][:rows])
    add_2(c2)
    back(c0)

    near = lambda: jnp.where(low, mlp_part[1], mlp_part[2])
    edge = lambda: jnp.where(low, mlp_part[0], mlp_part[3])
    leave_far = lambda: jnp.where(low, mlp_part[3], mlp_part[0])
    leave_near = lambda: jnp.where(low, mlp_part[2], mlp_part[1])
    total, coming, final, hidden, mlp_part, acc, dhid_t, sent = fence(
        total, coming, final, hidden, mlp_part, acc, dhid_t, sent
    )
    far_sum = add_3(c2, leave_far())
    add_2(c3)
    grad_mlp = keep_rows(*mlp_args, sent, units // 2)
    hidden, grad_mlp = fence(hidden, grad_mlp)
    grad_mlp = scatter(grad_mlp)
    back(c1)
    total, coming, final, hidden, mlp_part, far_sum, acc, dhid_t = fence(
        total, coming, final, hidden, mlp_part, far_sum, acc, dhid_t
    )
    near_sum = add_3(c3, leave_near())
    far_in = along(leave_far() + far_sum, MIDDLE)
    back(c2)
    total, final, hidden, mlp_part, near_sum, far_in, acc, dhid_t = fence(
        total, final, hidden, mlp_part, near_sum, far_in, acc, dhid_t
    )
    last = along(jnp.where(inner, edge() + far_in, near()), PAIRS)
    near_in = along(leave_near() + near_sum, MIDDLE)
    dhid_t[c3], dqkv_own[c3] = back_own(c3)
    q_cols = heads_here * HD
    attn_args = (
        [listed(dhid_t), normed_one_t],
        [(0, listed(own)), (1, listed(dqkv_own))],
    )
    sent = swap_rows(send_rows(*attn_args, None, send_turned))
    total, final, hidden, acc, sent = fence(total, final, hidden, acc, sent)
    if by_hand:
        half = slice_rows // 2
        upper = lambda m: (m * slice_rows, half)
        lower = lambda m: (m * slice_rows + half, half)
        picked = [
            [upper(1), upper(3)],
            [upper(0), upper(2)],
            [lower(2), lower(3)],
            [lower(0), lower(1)],
        ]
        pieces = keep_rows(*attn_args, sent, None, keep_turned, picked)
        pieces, hidden = fence(pieces, hidden)
        one_away, one, two_away, two = pieces
        pieces = (one, to_chip(one_away, 1), two, to_chip(two_away, 2))
    else:
        pieces = scatter(sent)
    back(c3)
    pieces, gains, input_grad, last, near_in = fence(pieces, gains, input_grad, last, near_in)
    gain_sums = gains[0] + gains[1] + gains[2] + gains[3]
    gain_sums = gain_sums + swap(gain_sums)
    mlp_rows = jnp.where(inner, near() + near_in, edge()) + last
    hidden_rows = jnp.where(
        low,
        jnp.where(level == 0, hidden[0], hidden[1]),
        jnp.where(level == 2, hidden[2], hidden[3]),
    )
    layer_out = (hidden_rows + mlp_rows).astype(jnp.bfloat16)
    all_input_grad = jnp.concatenate(listed(input_grad), 0)
    grad_gate = grad_mlp[:, :units]
    grad_up = grad_mlp[:, units : 2 * units]
    grad_down = grad_mlp[:, 2 * units :].T
    if by_hand:
        one = pieces[0] + pieces[1]
        two = pieces[2] + pieces[3]
        one_last = to_chip(one[half:], 2)
        two_last = to_chip(two[half:], 1)
        others = [to_chip(gain_sums, m) for m in range(1, chips)]
        gain_sums = sum(others, gain_sums)
        one_last, two_last, gain_sums, layer_out, all_input_grad, grad_gate, grad_up, grad_down = (
            fence(
                one_last, two_last, gain_sums, layer_out, all_input_grad, grad_gate, grad_up,
                grad_down,
            )
        )
        attn = jnp.concatenate([one[:half] + one_last, two[:half] + two_last], 0)
    else:
        gain_sums = lax.psum(gain_sums, "chip")
        attn = pieces
    gain_rows = lax.dynamic_slice_in_dim(gain_sums, at_row, slice_rows, 1)
    grad_out, grad_qkv = attn[:, :q_cols], attn[:, q_cols:]
    kv_cols = kv_here * HD
    return (
        layer_out,
        all_input_grad,
        gain_rows[0],
        grad_qkv[:, :q_cols],
        grad_qkv[:, q_cols : q_cols + kv_cols],
        grad_qkv[:, q_cols + kv_cols :],
        grad_out.T,
        gain_rows[1],
        grad_gate,
        grad_up,
        grad_down,
    )


def solution(mesh):
    devices = mesh.devices
    dp, tp = devices.shape
    split = Mesh(devices.reshape(dp // 2, 2, tp), ("chip", "core", "tp"))
    data = ("chip", "core")
    return jax.shard_map(
        shards,
        mesh=split,
        in_specs=(
            P(data, None),
            P(data),
            P(data),
            P(data, None),
            P(),
            P(None, "tp"),
            P(None, "tp"),
            P(None, "tp"),
            P("tp", None),
            P(),
            P(None, "tp"),
            P(None, "tp"),
            P("tp", None),
        ),
        out_specs=(
            P(("chip", "core", "tp"), None),
            P(data, None),
            P(data),
            P(data, "tp"),
            P(data, "tp"),
            P(data, "tp"),
            P("tp", data),
            P(data),
            P(data, "tp"),
            P(data, "tp"),
            P("tp", data),
        ),
        check_vma=False,
    )
```

```python
import functools

import jax
import jax.numpy as jnp
from jax import lax
from jax.experimental import pallas as pl
from jax.experimental.pallas import tpu as pltpu
from jax.sharding import Mesh
from jax.sharding import PartitionSpec as P

HD = 96
LANES = 128
GROUP = 2
KV_WIDE = (GROUP + 2) * LANES
rope_base = 100000.0
norm_eps = 1e-05
masked_score = -1e30
far_away = 1e30
score_scale = HD ** (-0.5)
score_scale_log2 = score_scale * 1.4426950408889634
CHUNKS = 4
EXTRA = 8
VMEM_BYTES = 56 * 1024 * 1024
NT = (((1,), (1,)), ((), ()))


def params():
    return pltpu.CompilerParams(vmem_limit_bytes=VMEM_BYTES)


def cost(flops, moved, exps=0):
    return pl.CostEstimate(
        flops=flops // 1024, bytes_accessed=moved // 1024, transcendentals=exps // 1024
    )


def dot32(a, b):
    return jnp.dot(a, b, preferred_element_type=jnp.float32)


def dot32_nt(a, b):
    return lax.dot_general(a, b, NT, preferred_element_type=jnp.float32)


def dot_split(a, places):
    high = a.astype(jnp.bfloat16)
    rest = (a - high.astype(jnp.float32)).astype(jnp.bfloat16)
    return dot32(high, places) + dot32(rest, places)


def fence(*trees):
    return lax.optimization_barrier(trees)


def whole(array, buffers=None):
    zeros = (0,) * len(array.shape)
    return pl.BlockSpec(array.shape, lambda *_: zeros)


SCALAR = pl.BlockSpec(memory_space=pltpu.SMEM)


def halves(entry):
    half_dim = HD // 2
    return (entry // half_dim) * (LANES // 2) + entry % half_dim


def placement(lanes, width):
    return (lanes[:, None] == jnp.arange(width)[None, :]).astype(jnp.bfloat16)


def place_query(heads):
    source = jnp.arange(heads * HD)
    return placement((source // HD) * LANES + halves(source % HD), heads * LANES)


def place_key_value(kv_heads):
    source = jnp.arange(kv_heads * HD)
    head = source // HD
    keys = head * 2 * LANES + halves(source % HD)
    values = head * 2 * LANES + LANES + source % HD
    return placement(jnp.concatenate([keys, values]), kv_heads * 2 * LANES)


def place_all(heads, kv_heads):
    source = jnp.arange(heads * HD)
    head = source // HD
    query = (head // GROUP) * KV_WIDE + (head % GROUP) * LANES + halves(source % HD)
    source = jnp.arange(kv_heads * HD)
    base = (source // HD) * KV_WIDE + GROUP * LANES
    keys = base + halves(source % HD)
    values = base + LANES + source % HD
    return placement(jnp.concatenate([query, keys, values]), kv_heads * KV_WIDE)


def place_plain(heads):
    source = jnp.arange(heads * HD)
    return placement((source // HD) * LANES + source % HD, heads * LANES)


PAIRS = [(0, 1), (1, 0), (2, 3), (3, 2)]
INWARD = [(0, 1), (3, 2)]
MIDDLE = [(1, 2), (2, 1)]
OUTWARD = [(1, 0), (2, 3)]


def along(part, pairs):
    return lax.ppermute(part, "tp", pairs)


def store_qkv(out_ref, here, base, query, key_value):
    wide = GROUP * LANES
    for kv in range(key_value.shape[1] // (2 * LANES)):
        at = base + kv * KV_WIDE
        there = slice(kv * 2 * LANES, (kv + 1) * 2 * LANES)
        out_ref[here, at : at + wide] = query[:, kv * wide : (kv + 1) * wide]
        out_ref[here, at + wide : at + KV_WIDE] = key_value[:, there]


def store_turned(out_ref, at, lin, cos_ref, sin_ref):
    for h in range(GROUP + 2):
        one = lin[:, h * LANES : (h + 1) * LANES]
        if h < GROUP + 1:
            one = one * cos_ref[...] + pltpu.roll(one, LANES // 2, 1) * sin_ref[...]
        out_ref[:, at + h * LANES : at + (h + 1) * LANES] = one.astype(jnp.bfloat16)


def spread_out_kernel(meta_ref, own_ref, p_ref, mine_ref, theirs_ref, pad_ref, plain_ref):
    rows, width = mine_ref.shape[2:]
    wide = p_ref.shape[1]
    for side, ref in enumerate((mine_ref, theirs_ref)):
        here = pl.ds(pl.multiple_of((meta_ref[1] ^ side) * rows, rows), rows)
        for s in range(4):
            block = own_ref[here, :] if s == 0 else ref[0, s - 1].astype(jnp.bfloat16)
            plain_ref[here, s * width : (s + 1) * width] = block
            pad_ref[here, s * wide : (s + 1) * wide] = dot32(block, p_ref[...]).astype(
                jnp.bfloat16
            )


def spread_qkv_kernel(own_ref, pq_ref, pkv_ref, far_ref, out_ref):
    parts, others, rows, width = far_ref.shape
    wide = own_ref.shape[1]
    split = pq_ref.shape[0]
    out_ref[:, :wide] = own_ref[...]
    for s in range(others):
        block = far_ref[:, s].reshape(parts * rows, width).astype(jnp.bfloat16)
        query = dot32(block[:, :split], pq_ref[...]).astype(jnp.bfloat16)
        key_value = dot32(block[:, split:], pkv_ref[...]).astype(jnp.bfloat16)
        store_qkv(out_ref, slice(None), (s + 1) * wide, query, key_value)


def spread_qkv(own, pq, pkv, far):
    total, wide = own.shape
    dp, others, rows, width = far.shape
    parts = max(1, dp // 4)
    block = parts * rows
    return pl.pallas_call(
        spread_qkv_kernel,
        out_shape=jax.ShapeDtypeStruct((total, (others + 1) * wide), jnp.bfloat16),
        grid=(total // block,),
        in_specs=[
            pl.BlockSpec((block, wide), lambda i: (i, 0)),
            whole(pq),
            whole(pkv),
            pl.BlockSpec((parts, others, rows, width), lambda i: (i, 0, 0, 0)),
        ],
        out_specs=pl.BlockSpec((block, (others + 1) * wide), lambda i: (i, 0)),
        compiler_params=params(),
        cost_estimate=cost(8 * total * width * 512, 20 * total * wide),
    )(own, pq, pkv, far)


def spread(kernel, meta, own, places, mine, theirs, widths):
    chips, others, rows, width = mine.shape
    total = own.shape[0]
    row_block = lambda m, meta: (meta[0] ^ m, 0)
    piece = pl.BlockSpec((1, others, rows, width), lambda m, meta: (m, 0, 0, 0))
    return pl.pallas_call(
        kernel,
        out_shape=[jax.ShapeDtypeStruct((total, wide), jnp.bfloat16) for wide in widths],
        grid_spec=pltpu.PrefetchScalarGridSpec(
            num_scalar_prefetch=1,
            grid=(chips,),
            in_specs=[pl.BlockSpec((2 * rows, own.shape[1]), row_block)]
            + [whole(place) for place in places]
            + [piece, piece],
            out_specs=[pl.BlockSpec((2 * rows, wide), row_block) for wide in widths],
        ),
        compiler_params=params(),
        cost_estimate=cost(
            8 * total * width * 512, total * (12 * width + 2 * sum(widths))
        ),
    )(meta, own, *places, mine, theirs)


def start_kernel(x_ref, gain_ref, q_ref, k_ref, v_ref, pq_ref, pkv_ref, cos_ref, sin_ref, *outs):
    qkv_ref, normed_ref, pad_ref = outs

    @pl.when(pl.program_id(0) == 0)
    def _():
        split = k_ref.shape[0]
        query = dot32(q_ref[...], pq_ref[...]).astype(jnp.bfloat16)
        key_value = dot32(k_ref[...].T, pkv_ref[:split, :])
        key_value = key_value + dot32(v_ref[...].T, pkv_ref[split:, :])
        store_qkv(pad_ref, slice(None), 0, query, key_value.astype(jnp.bfloat16))

    inputs = x_ref[...].astype(jnp.float32)
    rms = lax.rsqrt(jnp.mean(inputs * inputs, -1, keepdims=True) + norm_eps)
    normed = (inputs * rms * gain_ref[...]).astype(jnp.bfloat16)
    normed_ref[...] = normed
    for kv in range(pad_ref.shape[1] // KV_WIDE):
        at = kv * KV_WIDE
        store_turned(qkv_ref, at, dot32(normed, pad_ref[:, at : at + KV_WIDE]), cos_ref, sin_ref)


def start(tokens, gain, w_query, w_key_t, w_value_t, pq, pkv, cosines, sines):
    total, depth = tokens.shape
    rows = total // CHUNKS
    wide = pq.shape[1] + pkv.shape[1]
    gain = gain[None, :]
    by_rows = lambda width: pl.BlockSpec((rows, width), lambda i: (i, 0))
    arrays = [w_query, w_key_t, w_value_t, pq, pkv]
    shapes = [
        jax.ShapeDtypeStruct((total, wide), jnp.bfloat16),
        jax.ShapeDtypeStruct((total, depth), jnp.bfloat16),
        jax.ShapeDtypeStruct((depth, wide), jnp.bfloat16),
    ]
    return pl.pallas_call(
        start_kernel,
        out_shape=shapes,
        grid=(CHUNKS,),
        in_specs=[by_rows(depth), whole(gain)]
        + [whole(array) for array in arrays]
        + [by_rows(LANES), by_rows(LANES)],
        out_specs=[by_rows(wide), by_rows(depth), whole(shapes[2])],
        compiler_params=params(),
        cost_estimate=cost(2 * total * depth * wide, 12 * total * depth),
    )(tokens, gain, *arrays, cosines, sines)


def turn_kernel(length_ref, cot_ref, normed_ref, dout_ref, dout_t_ref, normed_t_ref):
    rows = cot_ref.shape[0]
    at = pl.program_id(0) * rows + lax.broadcasted_iota(jnp.int32, cot_ref.shape, 0)
    dout = jnp.where(at < length_ref[0], cot_ref[...].astype(jnp.float32), 0.0)
    dout = dout.astype(jnp.bfloat16)
    dout_ref[...] = dout
    dout_t_ref[...] = dout.T
    normed_t_ref[...] = normed_ref[...].T


def turn(length, cotangent, normed):
    total, depth = cotangent.shape
    rows = total // CHUNKS
    by_rows = pl.BlockSpec((rows, depth), lambda i: (i, 0))
    by_columns = pl.BlockSpec((depth, rows), lambda i: (0, i))
    turned = jax.ShapeDtypeStruct((depth, total), jnp.bfloat16)
    return pl.pallas_call(
        turn_kernel,
        out_shape=[jax.ShapeDtypeStruct((total, depth), jnp.bfloat16), turned, turned],
        grid=(CHUNKS,),
        in_specs=[SCALAR, by_rows, by_rows],
        out_specs=[by_rows, by_columns, by_columns],
        compiler_params=params(),
        cost_estimate=cost(total * depth, 10 * total * depth),
    )(length, cotangent, normed)


def project_kernel(x_ref, w_ref, cos_ref, sin_ref, out_ref):
    store_turned(out_ref, 0, dot32(x_ref[...], w_ref[...]), cos_ref, sin_ref)


def project(normed, weights, cosines, sines):
    rows, depth = normed.shape
    width = weights.shape[1]
    return pl.pallas_call(
        project_kernel,
        out_shape=jax.ShapeDtypeStruct((rows, width), jnp.bfloat16),
        grid=(width // KV_WIDE,),
        in_specs=[
            whole(normed),
            pl.BlockSpec((depth, KV_WIDE), lambda i: (0, i)),
            whole(cosines),
            whole(sines),
        ],
        out_specs=pl.BlockSpec((rows, KV_WIDE), lambda i: (0, i)),
        compiler_params=params(),
        cost_estimate=cost(
            2 * rows * depth * width, 2 * (rows * depth + depth * width + rows * width)
        ),
    )(normed, weights, cosines, sines)


def attend_kernel(start, length_ref, q_ref, kv_ref, strip_ref, out_ref):
    rows = q_ref.shape[0]
    keys = kv_ref.shape[0]
    length = length_ref[0]
    row_ids = start + lax.broadcasted_iota(jnp.int32, (1, rows), 1)
    limit = jnp.minimum(row_ids, length - 1)
    allowed = lax.broadcasted_iota(jnp.int32, (keys, rows), 0) <= limit
    mixed = []
    sums = []
    for kv in range(kv_ref.shape[1] // KV_WIDE):
        base = kv * KV_WIDE
        at = base + GROUP * LANES
        key = kv_ref[:, at : at + LANES]
        value_t = kv_ref[:, at + LANES : at + 2 * LANES].T
        for g in range(GROUP):
            query = q_ref[:, base + g * LANES : base + (g + 1) * LANES]
            raw = jnp.where(allowed, dot32_nt(key, query), masked_score)
            peak = jnp.max(raw, axis=0, keepdims=True)
            expo = jnp.exp2((raw - peak) * score_scale_log2)
            total = jnp.sum(expo, axis=0, keepdims=True)
            probs = (expo * (1.0 / total)).astype(jnp.bfloat16)
            mixed.append(dot32(value_t, probs).T)
            log_sum = peak * score_scale_log2 + jnp.log2(total)
            sums.append(jnp.where(row_ids < length, log_sum, far_away))
    out_ref[:rows, :] = dot_split(jnp.concatenate(mixed, 1), strip_ref[...])
    out_ref[rows:, :] = jnp.zeros((EXTRA, out_ref.shape[1]), jnp.float32)
    out_ref[rows : rows + len(sums), :rows] = jnp.concatenate(sums, 0)


def attend(length, qkv, strip, index, rows):
    keys = (index + 1) * rows
    width = qkv.shape[1]
    heads = width // KV_WIDE * GROUP
    shape = (rows + EXTRA, strip.shape[1])
    return pl.pallas_call(
        functools.partial(attend_kernel, index * rows),
        out_shape=jax.ShapeDtypeStruct(shape, jnp.float32),
        grid=(1,),
        in_specs=[
            SCALAR,
            pl.BlockSpec((rows, width), lambda i: (index, 0)),
            pl.BlockSpec((keys, width), lambda i: (0, 0)),
            whole(strip),
        ],
        out_specs=pl.BlockSpec(shape, lambda i: (0, 0)),
        compiler_params=params(),
        cost_estimate=cost(
            4 * heads * rows * keys * LANES, 2 * (rows + keys) * width, heads * rows * keys
        ),
    )(length, qkv, qkv, strip)


def forward_kernel(level_ref, part_ref, other_ref, across_ref, outer_ref, *refs):
    x_ref, dout_ref, wo_ref, gain_ref, wg_ref, wu_ref, wd_ref = refs[:7]
    hidden_ref, normed_t_ref, activ_ref, dgate_ref, dup_ref, mlp_ref, dn_ref = refs[7:14]
    normed_ref = refs[14]
    rows = x_ref.shape[0]

    @pl.when(pl.program_id(0) == 0)
    def _():
        level = level_ref[0]
        inner = (level == 1) | (level == 2)
        width = part_ref.shape[1]
        second = jnp.where(inner, across_ref[:rows, width:], outer_ref[:rows, :width])
        third = jnp.where(inner, across_ref[:rows, :width], outer_ref[:rows, width:])
        mixed = jnp.concatenate([part_ref[:rows, :], other_ref[:rows, :], second, third], 1)
        hidden = x_ref[...].astype(jnp.float32) + dot32_nt(mixed.astype(jnp.bfloat16), wo_ref[...])
        hidden_ref[...] = hidden
        rms = lax.rsqrt(jnp.mean(hidden * hidden, -1, keepdims=True) + norm_eps)
        normed = (hidden * rms * gain_ref[...]).astype(jnp.bfloat16)
        normed_ref[...] = normed
        normed_t_ref[...] = normed.T
        mlp_ref[...] = jnp.zeros_like(mlp_ref)
        dn_ref[...] = jnp.zeros_like(dn_ref)

    normed = normed_ref[...]
    gate = dot32(normed, wg_ref[...])
    up = dot32(normed, wu_ref[...])
    dact = dot32_nt(dout_ref[...], wd_ref[...])
    sigmoid = jax.nn.sigmoid(gate)
    silu = gate * sigmoid
    activ = (silu * up).astype(jnp.bfloat16)
    dgate = (dact * up * sigmoid * (1.0 + gate * (1.0 - sigmoid))).astype(jnp.bfloat16)
    dup = (dact * silu).astype(jnp.bfloat16)
    activ_ref[...] = activ
    dgate_ref[...] = dgate
    dup_ref[...] = dup
    mlp_ref[...] += dot32(activ, wd_ref[...])
    dn_ref[:rows, :] += dot32_nt(dgate, wg_ref[...]) + dot32_nt(dup, wu_ref[...])


def forward_chunk(level, gathered, tokens, dout, w_out, gain, w_gate, w_up, w_down, index, rows):
    depth = tokens.shape[1]
    units = w_gate.shape[1]
    block = 512
    own_rows = pl.BlockSpec((rows, depth), lambda i: (index, 0))
    by_units = pl.BlockSpec((depth, block), lambda i: (0, i))
    gain = gain[None, :]
    f32, bf16 = jnp.float32, jnp.bfloat16
    outs = [
        jax.ShapeDtypeStruct((rows, depth), f32),
        jax.ShapeDtypeStruct((depth, rows), bf16),
        jax.ShapeDtypeStruct((rows, units), bf16),
        jax.ShapeDtypeStruct((rows, units), bf16),
        jax.ShapeDtypeStruct((rows, units), bf16),
        jax.ShapeDtypeStruct((rows, depth), f32),
        jax.ShapeDtypeStruct((rows + EXTRA, depth), f32),
    ]
    unit_out = pl.BlockSpec((rows, block), lambda i: (0, i))
    return pl.pallas_call(
        forward_kernel,
        out_shape=outs,
        grid=(units // block,),
        in_specs=[SCALAR]
        + [whole(array) for array in gathered]
        + [own_rows, own_rows, whole(w_out), whole(gain), by_units, by_units]
        + [pl.BlockSpec((block, depth), lambda i: (i, 0))],
        out_specs=[
            whole(outs[0]),
            whole(outs[1]),
            unit_out,
            unit_out,
            unit_out,
            whole(outs[5]),
            whole(outs[6]),
        ],
        scratch_shapes=[pltpu.VMEM((rows, depth), bf16)],
        compiler_params=params(),
        cost_estimate=cost(
            2 * rows * depth * (6 * units + w_out.shape[1]),
            2 * depth * (3 * units + w_out.shape[1]) + 22 * rows * depth,
            rows * units,
        ),
    )(level, *gathered, tokens, dout, w_out, gain, w_gate, w_up, w_down)


def hidden_grad(inner, total_ref, final_ref, hidden_ref, dout_ref, gain_ref):
    dnormed = jnp.where(inner, total_ref[...], final_ref[...])
    hidden = hidden_ref[...]
    rms = lax.rsqrt(jnp.mean(hidden * hidden, -1, keepdims=True) + norm_eps)
    scaled = dnormed * gain_ref[...]
    shift = jnp.mean(scaled * hidden, -1, keepdims=True)
    dhid = dout_ref[...].astype(jnp.float32) + (rms * scaled - hidden * (rms**3 * shift))
    return dhid, dnormed * (hidden * rms)


def backward_kernel(start, full, level_ref, total_ref, final_ref, hidden_ref, dout_ref, x_ref, *refs):
    gain_one_ref, gain_two_ref, wo_ref, q_ref = refs[:4]
    kv_here = q_ref.shape[1] // KV_WIDE
    refs = refs[4:]
    kv_refs, refs = refs[: 2 * kv_here], refs[2 * kv_here :]
    part_ref, other_ref, across_ref, outer_ref, place_ref, strip_ref = refs[:6]
    cos_ref, sin_ref = refs[6:8]
    dhid_ref, low_ref, dn_ref = refs[-3:]
    outs = refs[8:-3]
    if full:
        w_ref, outs = outs[0], outs[1:]
    count = (5 if start > 0 else 4) if full else 2
    acc_ref = outs[0] if len(outs) > count else None
    outs = outs[-count:]
    dhid_t_ref, dqkv_ref = outs[:2]
    if full:
        input_grad_ref, gains_ref = outs[2:4]
    rows = q_ref.shape[0]
    keys = kv_refs[0].shape[0]
    shard = pl.program_id(0)
    level = level_ref[0]
    inner = (level == 1) | (level == 2)

    @pl.when(shard == 0)
    def _():
        dhid, dgain = hidden_grad(
            inner, total_ref, final_ref, hidden_ref, dout_ref, gain_two_ref
        )
        dhid_ref[...] = dhid
        low = dhid.astype(jnp.bfloat16)
        low_ref[...] = low
        dhid_t_ref[...] = low.T
        if full:
            gains_ref[...] = jnp.zeros_like(gains_ref)
            gains_ref[1:2, :] = jnp.sum(dgain, 0, keepdims=True)
            dn_ref[...] = jnp.zeros_like(dn_ref)

    def rotate_back(grads):
        turned = grads * cos_ref[...] - pltpu.roll(grads, LANES // 2, 1) * sin_ref[...]
        return turned.astype(jnp.bfloat16)

    dmixed_all = dot32(low_ref[...], wo_ref[...]).astype(jnp.bfloat16)
    mixed = jnp.where(
        shard == 0,
        part_ref[...],
        jnp.where(shard == 1, other_ref[...], jnp.where(inner, across_ref[...], outer_ref[...])),
    )
    products = dmixed_all.astype(jnp.float32) * dot_split(mixed[:rows], place_ref[...])
    causal = lax.broadcasted_iota(jnp.int32, (rows, rows), 0) <= lax.broadcasted_iota(
        jnp.int32, (rows, rows), 1
    )
    grads = []
    for kv in range(kv_here):
        key_ref, value_ref = kv_refs[2 * kv : 2 * kv + 2]
        heads = range(kv * GROUP, (kv + 1) * GROUP)
        lanes = {h: slice(h * LANES, (h + 1) * LANES) for h in heads}
        row_dots = {h: jnp.sum(products[:, lanes[h]].T, axis=0, keepdims=True) for h in heads}
        log_sums = {h: mixed[rows + h : rows + h + 1, :rows] for h in heads}
        dqueries = dict.fromkeys(heads)
        here = slice(2 * kv * LANES, (2 * kv + 1) * LANES)
        there = slice((2 * kv + 1) * LANES, (2 * kv + 2) * LANES)
        for tile in range(keys // rows):
            span = slice(tile * rows, (tile + 1) * rows)
            key = key_ref[span, :]
            value = value_ref[span, :]
            key_t = key.T
            dkey = None if acc_ref is None else acc_ref[span, here]
            dvalue = None if acc_ref is None else acc_ref[span, there]
            last = tile * rows == start
            for h in heads:
                at = kv * KV_WIDE + (h % GROUP) * LANES
                query = q_ref[:, at : at + LANES]
                dmixed = dmixed_all[:, lanes[h]]
                raw = dot32_nt(key, query)
                probs = jnp.exp2(raw * score_scale_log2 - log_sums[h])
                if last:
                    probs = jnp.where(causal, probs, 0.0)
                dprobs = dot32_nt(value, dmixed)
                dscores = (probs * (dprobs - row_dots[h])).astype(jnp.bfloat16)
                dquery = dot32(key_t, dscores)
                dqueries[h] = dquery if dqueries[h] is None else dqueries[h] + dquery
                dkey_one = dot32(dscores, query)
                dvalue_one = dot32(probs.astype(jnp.bfloat16), dmixed)
                dkey = dkey_one if dkey is None else dkey + dkey_one
                dvalue = dvalue_one if dvalue is None else dvalue + dvalue_one
            if full and not last:
                outs[4][span, here] = dkey
                outs[4][span, there] = dvalue
        grads += [rotate_back(dqueries[h].T * score_scale) for h in heads]
        grads.append(rotate_back(dkey * score_scale))
        grads.append(dvalue.astype(jnp.bfloat16))
    grads = jnp.concatenate(grads, 1)
    if full:
        dn_ref[...] += dot32_nt(grads, w_ref[...])

    @pl.when(shard == 0)
    def _():
        wide = strip_ref.shape[1]
        for kv in range(kv_here):
            dqkv_ref[:, kv * wide : (kv + 1) * wide] = dot32(
                grads[:, kv * KV_WIDE : (kv + 1) * KV_WIDE], strip_ref[...]
            ).astype(jnp.bfloat16)

    if not full:
        return

    @pl.when(shard == pl.num_programs(0) - 1)
    def _():
        dnormed = dn_ref[...]
        inputs = x_ref[...].astype(jnp.float32)
        rms = lax.rsqrt(jnp.mean(inputs * inputs, -1, keepdims=True) + norm_eps)
        scaled = dnormed * gain_one_ref[...]
        shift = jnp.mean(scaled * inputs, -1, keepdims=True)
        grad = dhid_ref[...] + (rms * scaled - inputs * (rms**3 * shift))
        input_grad_ref[...] = grad.astype(jnp.bfloat16)
        gains_ref[0:1, :] = jnp.sum(dnormed * (inputs * rms), 0, keepdims=True)


def backward_chunk(
    level, sums_two, hidden, dout, tokens, gains, weights, qkv, gathered, places, tables, acc,
    index, rows, full=True
):
    start = index * rows
    keys = start + rows
    depth = tokens.shape[1]
    out_pad, qkv_pad = weights
    place_out, strip = places
    far_rows, width = gathered[0].shape
    out_wide = place_out.shape[1]
    kv_here = out_wide // (GROUP * LANES)
    wide = kv_here * KV_WIDE
    levels = qkv.shape[1] // wide
    own_rows = pl.BlockSpec((rows, depth), lambda t: (index, 0))
    table = pl.BlockSpec((rows, LANES), lambda t: (index, 0))
    gains = [gain[None, :] for gain in gains]
    key_value = lambda at: pl.BlockSpec(
        (keys, LANES), lambda t: (0, (wide // LANES) * t + at)
    )
    across = pl.BlockSpec((far_rows, width), lambda t: (0, jnp.where(t == 2, 1, 0)))
    outer = pl.BlockSpec((far_rows, width), lambda t: (0, jnp.where(t == 3, 1, 0)))
    in_specs = [
        SCALAR,
        whole(sums_two[0]),
        whole(sums_two[1]),
        whole(hidden),
        own_rows,
        own_rows,
        whole(gains[0]),
        whole(gains[1]),
        pl.BlockSpec((depth, out_wide), lambda t: (0, t)),
        pl.BlockSpec((rows, wide), lambda t: (index, t)),
    ]
    for kv in range(kv_here):
        at = kv * (KV_WIDE // LANES) + GROUP
        in_specs += [key_value(at), key_value(at + 1)]
    in_specs += [
        whole(gathered[0]),
        whole(gathered[1]),
        across,
        outer,
        whole(place_out),
        whole(strip),
        table,
        table,
    ]
    args = [level, *sums_two, hidden, dout, tokens, *gains, out_pad]
    args += [qkv] * (1 + 2 * kv_here)
    args += [*gathered, place_out, strip, *tables]
    sums_wide = 2 * kv_here * LANES
    if full:
        in_specs.append(pl.BlockSpec((depth, wide), lambda t: (0, t)))
        args.append(qkv_pad)
    if acc is not None:
        in_specs.append(pl.BlockSpec((keys, sums_wide), lambda t: (0, t)))
        args.append(acc)
    f32, bf16 = jnp.float32, jnp.bfloat16
    outs = [
        jax.ShapeDtypeStruct((depth, rows), bf16),
        jax.ShapeDtypeStruct((rows, kv_here * strip.shape[1]), bf16),
        jax.ShapeDtypeStruct((rows, depth), bf16),
        jax.ShapeDtypeStruct((8, depth), f32),
    ]
    outs = outs if full else outs[:2]
    out_specs = [whole(out) for out in outs]
    if full and start > 0:
        outs.append(jax.ShapeDtypeStruct((start, levels * sums_wide), f32))
        out_specs.append(pl.BlockSpec((start, sums_wide), lambda t: (0, t)))
    results = pl.pallas_call(
        functools.partial(backward_kernel, start, full),
        out_shape=outs,
        grid=(levels if full else 1,),
        in_specs=in_specs,
        out_specs=out_specs,
        scratch_shapes=[
            pltpu.VMEM((rows, depth), f32),
            pltpu.VMEM((rows, depth), bf16),
            pltpu.VMEM((rows, depth), f32),
        ],
        compiler_params=params(),
        cost_estimate=cost(
            levels * rows * (20 * kv_here * keys * LANES + 2 * depth * (out_wide + wide)),
            2 * depth * levels * (out_wide + wide) + 16 * rows * depth,
            levels * kv_here * GROUP * rows * keys,
        ),
    )(*args)
    return results[:4], (results[4] if full and start > 0 else None)


def rows_kernel(lefts, groups, adding, picked, together, side_ref, *refs):
    refs = list(refs)
    held_ref = refs.pop()
    out_refs = refs[-len(picked) :]
    refs = refs[: -len(picked)]
    recv_ref = refs.pop() if adding else None
    step = pl.program_id(0)
    left_refs = []
    for count in lefts:
        left_refs.append(refs[:count])
        refs = refs[count:]
    rights = []
    for _ in groups:
        rights.append(refs[:CHUNKS])
        refs = refs[CHUNKS:]
    rows = left_refs[0][0].shape[0]
    blocks = held_ref.shape[1] // rows

    @pl.when(step == 0)
    def _():
        for which, pieces in enumerate(left_refs):
            for n, ref in enumerate(pieces):
                m, j = n % blocks, n // blocks
                wide = ref.shape[1]
                held_ref[which, m * rows : (m + 1) * rows, j * wide : (j + 1) * wide] = ref[...]

    chunk = held_ref.shape[2] // CHUNKS
    whole_columns = slice(0, out_refs[0].shape[1])

    def give(group, left, columns):
        right = jnp.concatenate([ref[:chunk, :].astype(jnp.bfloat16) for ref in group], 0)
        total = dot32(held_ref[left], right)
        if recv_ref is not None:
            total = total + recv_ref[:, columns]
        for out_ref, parts in zip(out_refs, picked):
            at = 0
            for start, size in parts:
                out_ref[at : at + size, columns] = total[start : start + size]
                at += size

    begin = 0
    for group, (left, first, steps) in zip(rights, groups):
        if together:
            width = group[0].shape[1]
            give(group, left, slice(begin, begin + width))
            begin += width
        else:

            @pl.when((step >= first) & (step < first + steps))
            def _(group=group, left=left):
                give(group, left, whole_columns)


def rows_of(lefts, groups, side, rows, blocks, step, recv=None, picked=None):
    if picked is None:
        picked = [[(0, rows * blocks)]]
    at = lambda m: lambda i, side: ((m ^ side[2]) * side[1] + side[0], 0)
    specs = []
    args = []
    counts = []
    for left in lefts:
        pieces = left if isinstance(left, list) else [left]
        counts.append(len(pieces) * blocks)
        for piece in pieces:
            for m in range(blocks):
                specs.append(pl.BlockSpec((rows, piece.shape[1]), at(m)))
                args.append(piece)
    tokens = sum(piece.shape[1] for piece in pieces)
    first = 0
    plan = []
    together = step is None
    for which, rights in groups:
        if together:
            plan.append((which, 0, 1))
            specs += [whole(right) for right in rights]
            args += rights
            first += rights[0].shape[1]
            continue
        steps = rights[0].shape[1] // step
        plan.append((which, first, steps))
        for right in rights:
            pick = lambda i, side, first=first, steps=steps: (0, jnp.clip(i - first, 0, steps - 1))
            specs.append(pl.BlockSpec((right.shape[0], step), pick))
            args.append(right)
        first += steps
    if together:
        first, step = 1, first
    total = first * step
    block = lambda height: pl.BlockSpec((height, step), lambda i, side: (0, i))
    if recv is not None:
        specs.append(block(rows * blocks))
        args.append(recv)
    heights = [sum(size for _, size in parts) for parts in picked]
    results = pl.pallas_call(
        functools.partial(rows_kernel, counts, plan, recv is not None, picked, together),
        out_shape=[jax.ShapeDtypeStruct((height, total), jnp.float32) for height in heights],
        grid_spec=pltpu.PrefetchScalarGridSpec(
            num_scalar_prefetch=1,
            grid=(first,),
            in_specs=specs,
            out_specs=[block(height) for height in heights],
            scratch_shapes=[pltpu.VMEM((len(lefts), rows * blocks, tokens), jnp.bfloat16)],
        ),
        compiler_params=params(),
        cost_estimate=cost(
            2 * rows * blocks * tokens * total,
            4 * rows * blocks * total + 2 * tokens * (total + rows * blocks),
        ),
    )(side, *args)
    return results[0] if len(picked) == 1 else results


def shards(
    tokens,
    lengths,
    positions,
    cotangent,
    norm_gain,
    w_query,
    w_key,
    w_value,
    w_out,
    mlp_gain,
    w_gate,
    w_up,
    w_down,
):
    seq_rows, depth = tokens.shape
    chips = lax.axis_size("chip")
    dp = chips * 2
    tp = lax.axis_size("tp")
    chip = lax.axis_index("chip")
    core = lax.axis_index("core")
    level = lax.axis_index("tp")
    low = level < 2
    inner = (level == 1) | (level == 2)
    heads_here = w_query.shape[1] // HD
    kv_here = w_key.shape[1] // HD
    rows = seq_rows // CHUNKS
    slice_rows = depth // dp
    level_ref = level.astype(jnp.int32).reshape(1)
    by_hand = dp == 8
    swap = lambda array: lax.ppermute(array, "core", [(0, 1), (1, 0)])
    to_level = lambda array, s: along(array, [(t, t ^ s) for t in range(tp)])

    at_row = (chip * 2 + core) * slice_rows
    cols = lambda w: lax.dynamic_slice_in_dim(w, at_row, slice_rows, 1).astype(jnp.float32).T
    (out_slice,) = fence(cols(w_out))
    qkv_slice = jnp.concatenate(
        [
            lax.dynamic_slice_in_dim(w_query, at_row, slice_rows, 0).astype(jnp.float32),
            cols(w_key.T),
            cols(w_value.T),
        ],
        1,
    )
    out_slice, qkv_slice = fence(out_slice, qkv_slice)
    out_near = along(out_slice, PAIRS)
    qkv_near = along(qkv_slice, PAIRS)
    meta = jnp.stack([chip, core]).astype(jnp.int32)

    pq = place_query(heads_here)
    pkv = place_key_value(kv_here)
    p_all = place_all(heads_here, kv_here)
    strip_one = place_all(GROUP, 1).T
    p_out = place_plain(heads_here)
    strip_out = p_out.T

    half_dim = HD // 2
    freqs = rope_base ** (-(jnp.arange(half_dim).astype(jnp.float32) * 2.0 / HD))
    freqs = jnp.pad(freqs, (0, LANES // 2 - half_dim))
    angles = positions.astype(jnp.float32)[:, None] * jnp.concatenate([freqs, freqs])[None, :]
    cosines = jnp.cos(angles)
    sines = jnp.sin(angles) * jnp.where(jnp.arange(LANES) < LANES // 2, -1.0, 1.0)

    cosines, sines, out_near = fence(cosines, sines, out_near)
    out_across = along(jnp.stack([out_slice, out_near]), MIDDLE)
    qkv_own, normed_one, own_pad = start(
        tokens, norm_gain, w_query, w_key.T, w_value.T, pq, pkv, cosines, sines
    )

    def far_slices(near, across, outer):
        return jnp.stack(
            [
                near,
                jnp.where(inner, across[1], outer[0]),
                jnp.where(inner, across[0], outer[1]),
            ]
        )

    order = list(reversed(range(CHUNKS)))
    c0, c1, c2, c3 = order
    own, other, across, outer = {}, {}, {}, {}
    part, total, final = {}, {}, {}

    def hop_1(j):
        other[j] = along(own[j], PAIRS)

    def hop_2(j):
        across[j] = along(jnp.concatenate([own[j], other[j]], 1), MIDDLE)

    def hop_3(j):
        outer[j] = along(across[j], OUTWARD)

    coming = {}

    def add_1(j):
        coming[j] = along(part[j], INWARD)

    def add_2(j):
        total[j] = part[j][:rows] + coming[j][:rows]
        coming[j] = along(total[j], MIDDLE)

    def add_3(j, inward):
        total[j] = jnp.where(inner, total[j] + coming[j], inward)
        final[j] = along(total[j], PAIRS)
        return final[j]

    def to_chip(array, m):
        return lax.ppermute(array, "chip", [(i, i ^ m) for i in range(chips)])

    def over_chips_1(piece):
        cut = piece.shape[1] // 2
        one, two = piece[:, :cut], piece[:, cut:]
        return jnp.stack([one, to_chip(one, 1)]), jnp.stack([two, to_chip(two, 2)])

    def over_chips_2(one, two):
        return one, to_chip(one, 2), two, to_chip(two, 1)

    def over_chips_3(one, one_far, two, two_far):
        upper = jnp.stack([one[0], one[1], one_far[0], one_far[1]])
        lower = jnp.stack([two[0], two_far[0], two[1], two_far[1]])
        return jnp.concatenate([upper, lower], 2)

    qkv_own, out_across, qkv_near = fence(qkv_own, out_across, qkv_near)
    out_outer = along(out_across, OUTWARD)
    qkv_across = along(jnp.stack([qkv_slice, qkv_near]), MIDDLE)
    own[c0] = attend(lengths, qkv_own, strip_out, c0, rows)
    own, qkv_own, out_outer = fence(own, qkv_own, out_outer)
    hop_1(c0)
    out_far = far_slices(out_near, out_across, out_outer)
    out_mine = over_chips_1(out_far) if by_hand else out_far
    own[c1] = attend(lengths, qkv_own, strip_out, c1, rows)
    own[c1], qkv_own = fence(own[c1], qkv_own)
    hop_1(c1)
    own[c2] = attend(lengths, qkv_own, strip_out, c2, rows)
    own, other, normed_one, w_out, out_mine, qkv_across, qkv_own = fence(
        own, other, normed_one, w_out, out_mine, qkv_across, qkv_own
    )
    own[c3] = attend(lengths, qkv_own, strip_out, c3, rows)
    qkv_outer = along(qkv_across, OUTWARD)
    if by_hand:
        out_mine = over_chips_2(*out_mine)
    else:
        out_mine = lax.all_gather(out_mine, ("chip", "core"))
    hop_2(c0)
    dout, dout_t, normed_one_t = turn(lengths, cotangent, normed_one)
    w_out_t = w_out.T
    own, other, across, dout, dout_t, normed_one_t, w_out_t, out_mine, qkv_outer = fence(
        own, other, across, dout, dout_t, normed_one_t, w_out_t, out_mine, qkv_outer
    )
    hop_1(c2)
    hop_3(c0)
    hop_2(c1)
    if by_hand:
        out_mine = over_chips_3(*out_mine)
        out_theirs = swap(out_mine)
        out_pad, out_plain = spread(
            spread_out_kernel,
            meta,
            w_out_t,
            [p_out],
            out_mine,
            out_theirs,
            [4 * p_out.shape[1], 4 * p_out.shape[0]],
        )
    else:
        plain = [w_out_t] + [
            out_mine[:, s].reshape(depth, -1).astype(jnp.bfloat16) for s in range(tp - 1)
        ]
        out_plain = jnp.concatenate(plain, 1)
        out_pad = jnp.concatenate([dot32(w, p_out).astype(jnp.bfloat16) for w in plain], 1)
    qkv_outer, out_pad = fence(qkv_outer, out_pad)
    qkv_far = lax.all_gather(far_slices(qkv_near, qkv_across, qkv_outer), ("chip", "core"))
    hidden, normed_t, activ, dgate, dup, mlp_part = {}, {}, {}, {}, {}, {}

    def feed(j):
        gathered = (own[j], other[j], across[j], outer[j])
        (hidden[j], normed_t[j], activ[j], dgate[j], dup[j], mlp_part[j], part[j]) = forward_chunk(
            level_ref, gathered, tokens, dout, out_plain, mlp_gain, w_gate, w_up, w_down, j, rows
        )

    own, other, across, outer, out_pad, out_plain = fence(
        own, other, across, outer, out_pad, out_plain
    )
    hop_1(c3)
    hop_3(c1)
    hop_2(c2)
    feed(c0)
    own, other, across, outer, part, hidden = fence(own, other, across, outer, part, hidden)
    add_1(c0)
    hop_3(c2)
    hop_2(c3)
    feed(c1)
    outer[c2], hidden[c1] = fence(outer[c2], hidden[c1])
    feed(c2)
    own, other, across, outer, part, total, coming, hidden = fence(
        own, other, across, outer, part, total, coming, hidden
    )
    add_1(c1)
    hop_3(c3)
    add_2(c0)
    qkv_far, part = fence(qkv_far, part)
    qkv_pad = spread_qkv(own_pad, pq, pkv, qkv_far)
    qkv = project(normed_one, qkv_pad, cosines, sines)
    own, other, across, outer, part, total, coming, hidden, qkv = fence(
        own, other, across, outer, part, total, coming, hidden, qkv
    )
    coming[c2] = add_3(c0, part[c2][:rows])
    add_2(c1)
    feed(c3)

    listed = lambda pieces: [pieces[j] for j in range(CHUNKS)]
    keep_side = jnp.stack([core, 2, 0]).astype(jnp.int32)
    keep_turned = jnp.stack([core, 2, chip]).astype(jnp.int32)
    send_side = jnp.stack([1 - core, 2, 0]).astype(jnp.int32)
    send_turned = jnp.stack([1 - core, 2, chip]).astype(jnp.int32)
    all_rows = jnp.array([0, 1, 0], jnp.int32)

    def send_rows(lefts, groups, step, side=send_side):
        if not by_hand:
            return rows_of(lefts, groups, all_rows, depth // 4, 4, step)
        return rows_of(lefts, groups, side, slice_rows, chips, step)

    def keep_rows(lefts, groups, received, step, side=keep_side, picked=None):
        if not by_hand:
            return received
        return rows_of(lefts, groups, side, slice_rows, chips, step, received, picked)

    def swap_rows(array):
        return swap(array) if by_hand else array

    def scatter(array, axes):
        return lax.psum_scatter(array, axes, scatter_dimension=0, tiled=True)

    units = w_gate.shape[1]
    mlp_args = (
        [listed(normed_t), dout_t],
        [(0, listed(dgate)), (0, listed(dup)), (1, listed(activ))],
    )
    acc = None
    dhid_t, dqkv_own, input_grad, gains = {}, {}, {}, {}

    def back(j):
        nonlocal acc
        (dhid_t[j], dqkv_own[j], input_grad[j], gains[j]), acc = back_some(j, True)

    def back_own(j):
        return back_some(j, False)[0]

    def back_some(j, full):
        return backward_chunk(
            level_ref,
            (total[j], final[j]),
            hidden[j],
            dout,
            tokens,
            (norm_gain, mlp_gain),
            (out_pad, qkv_pad),
            qkv,
            (own[j], other[j], across[j], outer[j]),
            (p_out, strip_one),
            (cosines, sines),
            acc,
            j,
            rows,
            full,
        )

    grad_mlp = rows_of(*mlp_args, all_rows, depth // 4, 4, units // 2)
    own, other, across, outer, part, total, coming, final, hidden, grad_mlp = fence(
        own, other, across, outer, part, total, coming, final, hidden, grad_mlp
    )
    grad_mlp = scatter(grad_mlp, ("chip", "core"))
    coming[c3] = add_3(c1, part[c3][:rows])
    add_2(c2)
    back(c0)

    near = lambda: jnp.where(low, mlp_part[1], mlp_part[2])
    edge = lambda: jnp.where(low, mlp_part[0], mlp_part[3])
    leave_far = lambda: jnp.where(low, mlp_part[3], mlp_part[0])
    leave_near = lambda: jnp.where(low, mlp_part[2], mlp_part[1])
    total, coming, final, hidden, mlp_part, acc, dhid_t = fence(
        total, coming, final, hidden, mlp_part, acc, dhid_t
    )
    far_sum = add_3(c2, leave_far())
    add_2(c3)
    back(c1)
    total, coming, final, hidden, mlp_part, far_sum, acc, dhid_t = fence(
        total, coming, final, hidden, mlp_part, far_sum, acc, dhid_t
    )
    near_sum = add_3(c3, leave_near())
    far_in = along(leave_far() + far_sum, MIDDLE)
    back(c2)
    total, final, hidden, mlp_part, near_sum, far_in, acc, dhid_t = fence(
        total, final, hidden, mlp_part, near_sum, far_in, acc, dhid_t
    )
    last = along(jnp.where(inner, edge() + far_in, near()), PAIRS)
    near_in = along(leave_near() + near_sum, MIDDLE)
    dhid_t[c3], dqkv_own[c3] = back_own(c3)
    q_cols = heads_here * HD
    attn_args = (
        [listed(dhid_t), normed_one_t],
        [(0, listed(own)), (1, listed(dqkv_own))],
    )
    sent = swap_rows(send_rows(*attn_args, None, send_turned))
    total, final, hidden, acc, sent = fence(total, final, hidden, acc, sent)
    if by_hand:
        half = slice_rows // 2
        upper = lambda m: (m * slice_rows, half)
        lower = lambda m: (m * slice_rows + half, half)
        picked = [
            [upper(1), upper(3)],
            [upper(0), upper(2)],
            [lower(2), lower(3)],
            [lower(0), lower(1)],
        ]
        pieces = keep_rows(*attn_args, sent, None, keep_turned, picked)
        pieces, hidden = fence(pieces, hidden)
        one_away, one, two_away, two = pieces
        pieces = (one, to_chip(one_away, 1), two, to_chip(two_away, 2))
    else:
        pieces = scatter(sent, ("chip", "core"))
    back(c3)
    pieces, gains, input_grad, last, near_in = fence(pieces, gains, input_grad, last, near_in)
    gain_sums = gains[0] + gains[1] + gains[2] + gains[3]
    gain_sums = gain_sums + swap(gain_sums)
    if by_hand:
        others = [to_chip(gain_sums, m) for m in range(1, chips)]
        gain_sums = sum(others, gain_sums)
        one = pieces[0] + pieces[1]
        two = pieces[2] + pieces[3]
        one = one[:half] + to_chip(one[half:], 2)
        two = two[:half] + to_chip(two[half:], 1)
        attn = jnp.concatenate([one, two], 0)
    else:
        gain_sums = lax.psum(gain_sums, "chip")
        attn = pieces
    gain_rows = lax.dynamic_slice_in_dim(gain_sums, at_row, slice_rows, 1)
    grad_out, grad_qkv = attn[:, :q_cols], attn[:, q_cols:]
    mlp_rows = jnp.where(inner, near() + near_in, edge()) + last
    hidden_rows = jnp.where(
        low,
        jnp.where(level == 0, hidden[0], hidden[1]),
        jnp.where(level == 2, hidden[2], hidden[3]),
    )
    layer_out = (hidden_rows + mlp_rows).astype(jnp.bfloat16)
    one = strip_one.shape[1]
    picked = lambda at, width: jnp.concatenate(
        [grad_qkv[:, kv * one + at : kv * one + at + width] for kv in range(kv_here)], 1
    )
    return (
        layer_out,
        jnp.concatenate(listed(input_grad), 0),
        gain_rows[0],
        picked(0, GROUP * HD),
        picked(GROUP * HD, HD),
        picked((GROUP + 1) * HD, HD),
        grad_out.T,
        gain_rows[1],
        grad_mlp[:, :units],
        grad_mlp[:, units : 2 * units],
        grad_mlp[:, 2 * units :].T,
    )


def solution(mesh):
    devices = mesh.devices
    dp, tp = devices.shape
    split = Mesh(devices.reshape(dp // 2, 2, tp), ("chip", "core", "tp"))
    data = ("chip", "core")
    return jax.shard_map(
        shards,
        mesh=split,
        in_specs=(
            P(data, None),
            P(data),
            P(data),
            P(data, None),
            P(),
            P(None, "tp"),
            P(None, "tp"),
            P(None, "tp"),
            P("tp", None),
            P(),
            P(None, "tp"),
            P(None, "tp"),
            P("tp", None),
        ),
        out_specs=(
            P(("chip", "core", "tp"), None),
            P(data, None),
            P(data),
            P(data, "tp"),
            P(data, "tp"),
            P(data, "tp"),
            P("tp", data),
            P(data),
            P(data, "tp"),
            P(data, "tp"),
            P("tp", data),
        ),
        check_vma=False,
    )
```

```python
import functools

import jax
import jax.numpy as jnp
from jax import lax
from jax.experimental import pallas as pl
from jax.experimental.pallas import tpu as pltpu
from jax.sharding import Mesh
from jax.sharding import PartitionSpec as P

HD = 96
LANES = 128
GROUP = 2
KV_WIDE = (GROUP + 2) * LANES
rope_base = 100000.0
norm_eps = 1e-05
masked_score = -1e30
far_away = 1e30
score_scale = HD ** (-0.5)
score_scale_log2 = score_scale * 1.4426950408889634
CHUNKS = 4
EXTRA = 8
VMEM_BYTES = 56 * 1024 * 1024
NT = (((1,), (1,)), ((), ()))


def params():
    return pltpu.CompilerParams(vmem_limit_bytes=VMEM_BYTES)


def cost(flops, moved, exps=0):
    return pl.CostEstimate(
        flops=flops // 1024, bytes_accessed=moved // 1024, transcendentals=exps // 1024
    )


def dot32(a, b):
    return jnp.dot(a, b, preferred_element_type=jnp.float32)


def dot32_nt(a, b):
    return lax.dot_general(a, b, NT, preferred_element_type=jnp.float32)


def dot_split(a, places):
    high = a.astype(jnp.bfloat16)
    rest = (a - high.astype(jnp.float32)).astype(jnp.bfloat16)
    return dot32(high, places) + dot32(rest, places)


def fence(*trees):
    return lax.optimization_barrier(trees)


def whole(array, buffers=None):
    zeros = (0,) * len(array.shape)
    return pl.BlockSpec(array.shape, lambda *_: zeros)


SCALAR = pl.BlockSpec(memory_space=pltpu.SMEM)


def halves(entry):
    half_dim = HD // 2
    return (entry // half_dim) * (LANES // 2) + entry % half_dim


def placement(lanes, width):
    return (lanes[:, None] == jnp.arange(width)[None, :]).astype(jnp.bfloat16)


def place_query(heads):
    source = jnp.arange(heads * HD)
    return placement((source // HD) * LANES + halves(source % HD), heads * LANES)


def place_key_value(kv_heads):
    source = jnp.arange(kv_heads * HD)
    head = source // HD
    keys = head * 2 * LANES + halves(source % HD)
    values = head * 2 * LANES + LANES + source % HD
    return placement(jnp.concatenate([keys, values]), kv_heads * 2 * LANES)


def place_all(heads, kv_heads):
    source = jnp.arange(heads * HD)
    head = source // HD
    query = (head // GROUP) * KV_WIDE + (head % GROUP) * LANES + halves(source % HD)
    source = jnp.arange(kv_heads * HD)
    base = (source // HD) * KV_WIDE + GROUP * LANES
    keys = base + halves(source % HD)
    values = base + LANES + source % HD
    return placement(jnp.concatenate([query, keys, values]), kv_heads * KV_WIDE)


def place_plain(heads):
    source = jnp.arange(heads * HD)
    return placement((source // HD) * LANES + source % HD, heads * LANES)


PAIRS = [(0, 1), (1, 0), (2, 3), (3, 2)]
INWARD = [(0, 1), (3, 2)]
MIDDLE = [(1, 2), (2, 1)]
OUTWARD = [(1, 0), (2, 3)]


def along(part, pairs):
    return lax.ppermute(part, "tp", pairs)


def store_qkv(out_ref, here, base, query, key_value):
    wide = GROUP * LANES
    for kv in range(key_value.shape[1] // (2 * LANES)):
        at = base + kv * KV_WIDE
        there = slice(kv * 2 * LANES, (kv + 1) * 2 * LANES)
        out_ref[here, at : at + wide] = query[:, kv * wide : (kv + 1) * wide]
        out_ref[here, at + wide : at + KV_WIDE] = key_value[:, there]


def store_turned(out_ref, at, lin, cos_ref, sin_ref):
    for h in range(GROUP + 2):
        one = lin[:, h * LANES : (h + 1) * LANES]
        if h < GROUP + 1:
            one = one * cos_ref[...] + pltpu.roll(one, LANES // 2, 1) * sin_ref[...]
        out_ref[:, at + h * LANES : at + (h + 1) * LANES] = one.astype(jnp.bfloat16)


def spread_out_kernel(meta_ref, own_ref, p_ref, mine_ref, theirs_ref, pad_ref, plain_ref):
    rows, width = mine_ref.shape[2:]
    wide = p_ref.shape[1]
    for side, ref in enumerate((mine_ref, theirs_ref)):
        here = pl.ds(pl.multiple_of((meta_ref[1] ^ side) * rows, rows), rows)
        for s in range(4):
            block = own_ref[here, :] if s == 0 else ref[0, s - 1].astype(jnp.bfloat16)
            plain_ref[here, s * width : (s + 1) * width] = block
            pad_ref[here, s * wide : (s + 1) * wide] = dot32(block, p_ref[...]).astype(
                jnp.bfloat16
            )


def spread_qkv_kernel(own_ref, pq_ref, pkv_ref, far_ref, out_ref):
    parts, others, rows, width = far_ref.shape
    wide = own_ref.shape[1]
    split = pq_ref.shape[0]
    out_ref[:, :wide] = own_ref[...]
    for s in range(others):
        block = far_ref[:, s].reshape(parts * rows, width).astype(jnp.bfloat16)
        query = dot32(block[:, :split], pq_ref[...]).astype(jnp.bfloat16)
        key_value = dot32(block[:, split:], pkv_ref[...]).astype(jnp.bfloat16)
        store_qkv(out_ref, slice(None), (s + 1) * wide, query, key_value)


def spread_qkv(own, pq, pkv, far):
    total, wide = own.shape
    dp, others, rows, width = far.shape
    parts = max(1, dp // 4)
    block = parts * rows
    return pl.pallas_call(
        spread_qkv_kernel,
        out_shape=jax.ShapeDtypeStruct((total, (others + 1) * wide), jnp.bfloat16),
        grid=(total // block,),
        in_specs=[
            pl.BlockSpec((block, wide), lambda i: (i, 0)),
            whole(pq),
            whole(pkv),
            pl.BlockSpec((parts, others, rows, width), lambda i: (i, 0, 0, 0)),
        ],
        out_specs=pl.BlockSpec((block, (others + 1) * wide), lambda i: (i, 0)),
        compiler_params=params(),
        cost_estimate=cost(8 * total * width * 512, 20 * total * wide),
    )(own, pq, pkv, far)


def spread(kernel, meta, own, places, mine, theirs, widths):
    chips, others, rows, width = mine.shape
    total = own.shape[0]
    row_block = lambda m, meta: (meta[0] ^ m, 0)
    piece = pl.BlockSpec((1, others, rows, width), lambda m, meta: (m, 0, 0, 0))
    return pl.pallas_call(
        kernel,
        out_shape=[jax.ShapeDtypeStruct((total, wide), jnp.bfloat16) for wide in widths],
        grid_spec=pltpu.PrefetchScalarGridSpec(
            num_scalar_prefetch=1,
            grid=(chips,),
            in_specs=[pl.BlockSpec((2 * rows, own.shape[1]), row_block)]
            + [whole(place) for place in places]
            + [piece, piece],
            out_specs=[pl.BlockSpec((2 * rows, wide), row_block) for wide in widths],
        ),
        compiler_params=params(),
        cost_estimate=cost(
            8 * total * width * 512, total * (12 * width + 2 * sum(widths))
        ),
    )(meta, own, *places, mine, theirs)


def start_kernel(x_ref, gain_ref, q_ref, k_ref, v_ref, pq_ref, pkv_ref, cos_ref, sin_ref, *outs):
    qkv_ref, normed_ref, pad_ref = outs

    @pl.when(pl.program_id(0) == 0)
    def _():
        split = k_ref.shape[0]
        query = dot32(q_ref[...], pq_ref[...]).astype(jnp.bfloat16)
        key_value = dot32(k_ref[...].T, pkv_ref[:split, :])
        key_value = key_value + dot32(v_ref[...].T, pkv_ref[split:, :])
        store_qkv(pad_ref, slice(None), 0, query, key_value.astype(jnp.bfloat16))

    inputs = x_ref[...].astype(jnp.float32)
    rms = lax.rsqrt(jnp.mean(inputs * inputs, -1, keepdims=True) + norm_eps)
    normed = (inputs * rms * gain_ref[...]).astype(jnp.bfloat16)
    normed_ref[...] = normed
    for kv in range(pad_ref.shape[1] // KV_WIDE):
        at = kv * KV_WIDE
        store_turned(qkv_ref, at, dot32(normed, pad_ref[:, at : at + KV_WIDE]), cos_ref, sin_ref)


def start(tokens, gain, w_query, w_key_t, w_value_t, pq, pkv, cosines, sines):
    total, depth = tokens.shape
    rows = total // CHUNKS
    wide = pq.shape[1] + pkv.shape[1]
    gain = gain[None, :]
    by_rows = lambda width: pl.BlockSpec((rows, width), lambda i: (i, 0))
    arrays = [w_query, w_key_t, w_value_t, pq, pkv]
    shapes = [
        jax.ShapeDtypeStruct((total, wide), jnp.bfloat16),
        jax.ShapeDtypeStruct((total, depth), jnp.bfloat16),
        jax.ShapeDtypeStruct((depth, wide), jnp.bfloat16),
    ]
    return pl.pallas_call(
        start_kernel,
        out_shape=shapes,
        grid=(CHUNKS,),
        in_specs=[by_rows(depth), whole(gain)]
        + [whole(array) for array in arrays]
        + [by_rows(LANES), by_rows(LANES)],
        out_specs=[by_rows(wide), by_rows(depth), whole(shapes[2])],
        compiler_params=params(),
        cost_estimate=cost(2 * total * depth * wide, 12 * total * depth),
    )(tokens, gain, *arrays, cosines, sines)


def turn_kernel(length_ref, cot_ref, normed_ref, dout_ref, dout_t_ref, normed_t_ref):
    rows = cot_ref.shape[0]
    at = pl.program_id(0) * rows + lax.broadcasted_iota(jnp.int32, cot_ref.shape, 0)
    dout = jnp.where(at < length_ref[0], cot_ref[...].astype(jnp.float32), 0.0)
    dout = dout.astype(jnp.bfloat16)
    dout_ref[...] = dout
    dout_t_ref[...] = dout.T
    normed_t_ref[...] = normed_ref[...].T


def turn(length, cotangent, normed):
    total, depth = cotangent.shape
    rows = total // CHUNKS
    by_rows = pl.BlockSpec((rows, depth), lambda i: (i, 0))
    by_columns = pl.BlockSpec((depth, rows), lambda i: (0, i))
    turned = jax.ShapeDtypeStruct((depth, total), jnp.bfloat16)
    return pl.pallas_call(
        turn_kernel,
        out_shape=[jax.ShapeDtypeStruct((total, depth), jnp.bfloat16), turned, turned],
        grid=(CHUNKS,),
        in_specs=[SCALAR, by_rows, by_rows],
        out_specs=[by_rows, by_columns, by_columns],
        compiler_params=params(),
        cost_estimate=cost(total * depth, 10 * total * depth),
    )(length, cotangent, normed)


def project_kernel(x_ref, w_ref, cos_ref, sin_ref, out_ref):
    store_turned(out_ref, 0, dot32(x_ref[...], w_ref[...]), cos_ref, sin_ref)


def project(normed, weights, cosines, sines):
    rows, depth = normed.shape
    width = weights.shape[1]
    return pl.pallas_call(
        project_kernel,
        out_shape=jax.ShapeDtypeStruct((rows, width), jnp.bfloat16),
        grid=(width // KV_WIDE,),
        in_specs=[
            whole(normed),
            pl.BlockSpec((depth, KV_WIDE), lambda i: (0, i)),
            whole(cosines),
            whole(sines),
        ],
        out_specs=pl.BlockSpec((rows, KV_WIDE), lambda i: (0, i)),
        compiler_params=params(),
        cost_estimate=cost(
            2 * rows * depth * width, 2 * (rows * depth + depth * width + rows * width)
        ),
    )(normed, weights, cosines, sines)


def attend_kernel(start, length_ref, q_ref, kv_ref, strip_ref, out_ref):
    rows = q_ref.shape[0]
    keys = kv_ref.shape[0]
    length = length_ref[0]
    row_ids = start + lax.broadcasted_iota(jnp.int32, (1, rows), 1)
    limit = jnp.minimum(row_ids, length - 1)
    allowed = lax.broadcasted_iota(jnp.int32, (keys, rows), 0) <= limit
    mixed = []
    sums = []
    for kv in range(kv_ref.shape[1] // KV_WIDE):
        base = kv * KV_WIDE
        at = base + GROUP * LANES
        key = kv_ref[:, at : at + LANES]
        value_t = kv_ref[:, at + LANES : at + 2 * LANES].T
        for g in range(GROUP):
            query = q_ref[:, base + g * LANES : base + (g + 1) * LANES]
            raw = jnp.where(allowed, dot32_nt(key, query), masked_score)
            peak = jnp.max(raw, axis=0, keepdims=True)
            expo = jnp.exp2((raw - peak) * score_scale_log2)
            total = jnp.sum(expo, axis=0, keepdims=True)
            probs = (expo * (1.0 / total)).astype(jnp.bfloat16)
            mixed.append(dot32(value_t, probs).T)
            log_sum = peak * score_scale_log2 + jnp.log2(total)
            sums.append(jnp.where(row_ids < length, log_sum, far_away))
    out_ref[:rows, :] = dot_split(jnp.concatenate(mixed, 1), strip_ref[...])
    out_ref[rows:, :] = jnp.zeros((EXTRA, out_ref.shape[1]), jnp.float32)
    out_ref[rows : rows + len(sums), :rows] = jnp.concatenate(sums, 0)


def attend(length, qkv, strip, index, rows):
    keys = (index + 1) * rows
    width = qkv.shape[1]
    heads = width // KV_WIDE * GROUP
    shape = (rows + EXTRA, strip.shape[1])
    return pl.pallas_call(
        functools.partial(attend_kernel, index * rows),
        out_shape=jax.ShapeDtypeStruct(shape, jnp.float32),
        grid=(1,),
        in_specs=[
            SCALAR,
            pl.BlockSpec((rows, width), lambda i: (index, 0)),
            pl.BlockSpec((keys, width), lambda i: (0, 0)),
            whole(strip),
        ],
        out_specs=pl.BlockSpec(shape, lambda i: (0, 0)),
        compiler_params=params(),
        cost_estimate=cost(
            4 * heads * rows * keys * LANES, 2 * (rows + keys) * width, heads * rows * keys
        ),
    )(length, qkv, qkv, strip)


def forward_kernel(level_ref, part_ref, other_ref, across_ref, outer_ref, *refs):
    x_ref, dout_ref, wo_ref, gain_ref, wg_ref, wu_ref, wd_ref = refs[:7]
    hidden_ref, normed_t_ref, activ_ref, dgate_ref, dup_ref, mlp_ref, dn_ref = refs[7:14]
    normed_ref = refs[14]
    rows = x_ref.shape[0]

    @pl.when(pl.program_id(0) == 0)
    def _():
        level = level_ref[0]
        inner = (level == 1) | (level == 2)
        width = part_ref.shape[1]
        second = jnp.where(inner, across_ref[:rows, width:], outer_ref[:rows, :width])
        third = jnp.where(inner, across_ref[:rows, :width], outer_ref[:rows, width:])
        mixed = jnp.concatenate([part_ref[:rows, :], other_ref[:rows, :], second, third], 1)
        hidden = x_ref[...].astype(jnp.float32) + dot32_nt(mixed.astype(jnp.bfloat16), wo_ref[...])
        hidden_ref[...] = hidden
        rms = lax.rsqrt(jnp.mean(hidden * hidden, -1, keepdims=True) + norm_eps)
        normed = (hidden * rms * gain_ref[...]).astype(jnp.bfloat16)
        normed_ref[...] = normed
        normed_t_ref[...] = normed.T
        mlp_ref[...] = jnp.zeros_like(mlp_ref)
        dn_ref[...] = jnp.zeros_like(dn_ref)

    normed = normed_ref[...]
    gate = dot32(normed, wg_ref[...])
    up = dot32(normed, wu_ref[...])
    dact = dot32_nt(dout_ref[...], wd_ref[...])
    sigmoid = jax.nn.sigmoid(gate)
    silu = gate * sigmoid
    activ = (silu * up).astype(jnp.bfloat16)
    dgate = (dact * up * sigmoid * (1.0 + gate * (1.0 - sigmoid))).astype(jnp.bfloat16)
    dup = (dact * silu).astype(jnp.bfloat16)
    activ_ref[...] = activ
    dgate_ref[...] = dgate
    dup_ref[...] = dup
    mlp_ref[...] += dot32(activ, wd_ref[...])
    dn_ref[:rows, :] += dot32_nt(dgate, wg_ref[...]) + dot32_nt(dup, wu_ref[...])


def forward_chunk(level, gathered, tokens, dout, w_out, gain, w_gate, w_up, w_down, index, rows):
    depth = tokens.shape[1]
    units = w_gate.shape[1]
    block = 512
    own_rows = pl.BlockSpec((rows, depth), lambda i: (index, 0))
    by_units = pl.BlockSpec((depth, block), lambda i: (0, i))
    gain = gain[None, :]
    f32, bf16 = jnp.float32, jnp.bfloat16
    outs = [
        jax.ShapeDtypeStruct((rows, depth), f32),
        jax.ShapeDtypeStruct((depth, rows), bf16),
        jax.ShapeDtypeStruct((rows, units), bf16),
        jax.ShapeDtypeStruct((rows, units), bf16),
        jax.ShapeDtypeStruct((rows, units), bf16),
        jax.ShapeDtypeStruct((rows, depth), f32),
        jax.ShapeDtypeStruct((rows + EXTRA, depth), f32),
    ]
    unit_out = pl.BlockSpec((rows, block), lambda i: (0, i))
    return pl.pallas_call(
        forward_kernel,
        out_shape=outs,
        grid=(units // block,),
        in_specs=[SCALAR]
        + [whole(array) for array in gathered]
        + [own_rows, own_rows, whole(w_out), whole(gain), by_units, by_units]
        + [pl.BlockSpec((block, depth), lambda i: (i, 0))],
        out_specs=[
            whole(outs[0]),
            whole(outs[1]),
            unit_out,
            unit_out,
            unit_out,
            whole(outs[5]),
            whole(outs[6]),
        ],
        scratch_shapes=[pltpu.VMEM((rows, depth), bf16)],
        compiler_params=params(),
        cost_estimate=cost(
            2 * rows * depth * (6 * units + w_out.shape[1]),
            2 * depth * (3 * units + w_out.shape[1]) + 22 * rows * depth,
            rows * units,
        ),
    )(level, *gathered, tokens, dout, w_out, gain, w_gate, w_up, w_down)


def hidden_grad(inner, total_ref, final_ref, hidden_ref, dout_ref, gain_ref):
    dnormed = jnp.where(inner, total_ref[...], final_ref[...])
    hidden = hidden_ref[...]
    rms = lax.rsqrt(jnp.mean(hidden * hidden, -1, keepdims=True) + norm_eps)
    scaled = dnormed * gain_ref[...]
    shift = jnp.mean(scaled * hidden, -1, keepdims=True)
    dhid = dout_ref[...].astype(jnp.float32) + (rms * scaled - hidden * (rms**3 * shift))
    return dhid, dnormed * (hidden * rms)


def backward_kernel(start, full, level_ref, total_ref, final_ref, hidden_ref, dout_ref, x_ref, *refs):
    gain_one_ref, gain_two_ref, wo_ref, q_ref = refs[:4]
    kv_here = q_ref.shape[1] // KV_WIDE
    refs = refs[4:]
    kv_refs, refs = refs[: 2 * kv_here], refs[2 * kv_here :]
    part_ref, other_ref, across_ref, outer_ref, place_ref, strip_ref = refs[:6]
    cos_ref, sin_ref = refs[6:8]
    dhid_ref, low_ref, dn_ref = refs[-3:]
    outs = refs[8:-3]
    if full:
        w_ref, outs = outs[0], outs[1:]
    count = (5 if start > 0 else 4) if full else 2
    acc_ref = outs[0] if len(outs) > count else None
    outs = outs[-count:]
    dhid_t_ref, dqkv_ref = outs[:2]
    if full:
        input_grad_ref, gains_ref = outs[2:4]
    rows = q_ref.shape[0]
    keys = kv_refs[0].shape[0]
    shard = pl.program_id(0)
    level = level_ref[0]
    inner = (level == 1) | (level == 2)

    @pl.when(shard == 0)
    def _():
        dhid, dgain = hidden_grad(
            inner, total_ref, final_ref, hidden_ref, dout_ref, gain_two_ref
        )
        dhid_ref[...] = dhid
        low = dhid.astype(jnp.bfloat16)
        low_ref[...] = low
        dhid_t_ref[...] = low.T
        if full:
            gains_ref[...] = jnp.zeros_like(gains_ref)
            gains_ref[1:2, :] = jnp.sum(dgain, 0, keepdims=True)
            dn_ref[...] = jnp.zeros_like(dn_ref)

    def rotate_back(grads):
        turned = grads * cos_ref[...] - pltpu.roll(grads, LANES // 2, 1) * sin_ref[...]
        return turned.astype(jnp.bfloat16)

    dmixed_all = dot32(low_ref[...], wo_ref[...]).astype(jnp.bfloat16)
    mixed = jnp.where(
        shard == 0,
        part_ref[...],
        jnp.where(shard == 1, other_ref[...], jnp.where(inner, across_ref[...], outer_ref[...])),
    )
    products = dmixed_all.astype(jnp.float32) * dot_split(mixed[:rows], place_ref[...])
    causal = lax.broadcasted_iota(jnp.int32, (rows, rows), 0) <= lax.broadcasted_iota(
        jnp.int32, (rows, rows), 1
    )
    grads = []
    for kv in range(kv_here):
        key_ref, value_ref = kv_refs[2 * kv : 2 * kv + 2]
        heads = range(kv * GROUP, (kv + 1) * GROUP)
        lanes = {h: slice(h * LANES, (h + 1) * LANES) for h in heads}
        row_dots = {h: jnp.sum(products[:, lanes[h]].T, axis=0, keepdims=True) for h in heads}
        log_sums = {h: mixed[rows + h : rows + h + 1, :rows] for h in heads}
        dqueries = dict.fromkeys(heads)
        here = slice(2 * kv * LANES, (2 * kv + 1) * LANES)
        there = slice((2 * kv + 1) * LANES, (2 * kv + 2) * LANES)
        for tile in range(keys // rows):
            span = slice(tile * rows, (tile + 1) * rows)
            key = key_ref[span, :]
            value = value_ref[span, :]
            key_t = key.T
            dkey = None if acc_ref is None else acc_ref[span, here]
            dvalue = None if acc_ref is None else acc_ref[span, there]
            last = tile * rows == start
            for h in heads:
                at = kv * KV_WIDE + (h % GROUP) * LANES
                query = q_ref[:, at : at + LANES]
                dmixed = dmixed_all[:, lanes[h]]
                raw = dot32_nt(key, query)
                probs = jnp.exp2(raw * score_scale_log2 - log_sums[h])
                if last:
                    probs = jnp.where(causal, probs, 0.0)
                dprobs = dot32_nt(value, dmixed)
                dscores = (probs * (dprobs - row_dots[h])).astype(jnp.bfloat16)
                dquery = dot32(key_t, dscores)
                dqueries[h] = dquery if dqueries[h] is None else dqueries[h] + dquery
                dkey_one = dot32(dscores, query)
                dvalue_one = dot32(probs.astype(jnp.bfloat16), dmixed)
                dkey = dkey_one if dkey is None else dkey + dkey_one
                dvalue = dvalue_one if dvalue is None else dvalue + dvalue_one
            if full and not last:
                outs[4][span, here] = dkey
                outs[4][span, there] = dvalue
        grads += [rotate_back(dqueries[h].T * score_scale) for h in heads]
        grads.append(rotate_back(dkey * score_scale))
        grads.append(dvalue.astype(jnp.bfloat16))
    grads = jnp.concatenate(grads, 1)
    if full:
        dn_ref[...] += dot32_nt(grads, w_ref[...])

    @pl.when(shard == 0)
    def _():
        wide = strip_ref.shape[1]
        for kv in range(kv_here):
            dqkv_ref[:, kv * wide : (kv + 1) * wide] = dot32(
                grads[:, kv * KV_WIDE : (kv + 1) * KV_WIDE], strip_ref[...]
            ).astype(jnp.bfloat16)

    if not full:
        return

    @pl.when(shard == pl.num_programs(0) - 1)
    def _():
        dnormed = dn_ref[...]
        inputs = x_ref[...].astype(jnp.float32)
        rms = lax.rsqrt(jnp.mean(inputs * inputs, -1, keepdims=True) + norm_eps)
        scaled = dnormed * gain_one_ref[...]
        shift = jnp.mean(scaled * inputs, -1, keepdims=True)
        grad = dhid_ref[...] + (rms * scaled - inputs * (rms**3 * shift))
        input_grad_ref[...] = grad.astype(jnp.bfloat16)
        gains_ref[0:1, :] = jnp.sum(dnormed * (inputs * rms), 0, keepdims=True)


def backward_chunk(
    level, sums_two, hidden, dout, tokens, gains, weights, qkv, gathered, places, tables, acc,
    index, rows, full=True
):
    start = index * rows
    keys = start + rows
    depth = tokens.shape[1]
    out_pad, qkv_pad = weights
    place_out, strip = places
    far_rows, width = gathered[0].shape
    out_wide = place_out.shape[1]
    kv_here = out_wide // (GROUP * LANES)
    wide = kv_here * KV_WIDE
    levels = qkv.shape[1] // wide
    own_rows = pl.BlockSpec((rows, depth), lambda t: (index, 0))
    table = pl.BlockSpec((rows, LANES), lambda t: (index, 0))
    gains = [gain[None, :] for gain in gains]
    key_value = lambda at: pl.BlockSpec(
        (keys, LANES), lambda t: (0, (wide // LANES) * t + at)
    )
    across = pl.BlockSpec((far_rows, width), lambda t: (0, jnp.where(t == 2, 1, 0)))
    outer = pl.BlockSpec((far_rows, width), lambda t: (0, jnp.where(t == 3, 1, 0)))
    in_specs = [
        SCALAR,
        whole(sums_two[0]),
        whole(sums_two[1]),
        whole(hidden),
        own_rows,
        own_rows,
        whole(gains[0]),
        whole(gains[1]),
        pl.BlockSpec((depth, out_wide), lambda t: (0, t)),
        pl.BlockSpec((rows, wide), lambda t: (index, t)),
    ]
    for kv in range(kv_here):
        at = kv * (KV_WIDE // LANES) + GROUP
        in_specs += [key_value(at), key_value(at + 1)]
    in_specs += [
        whole(gathered[0]),
        whole(gathered[1]),
        across,
        outer,
        whole(place_out),
        whole(strip),
        table,
        table,
    ]
    args = [level, *sums_two, hidden, dout, tokens, *gains, out_pad]
    args += [qkv] * (1 + 2 * kv_here)
    args += [*gathered, place_out, strip, *tables]
    sums_wide = 2 * kv_here * LANES
    if full:
        in_specs.append(pl.BlockSpec((depth, wide), lambda t: (0, t)))
        args.append(qkv_pad)
    if acc is not None:
        in_specs.append(pl.BlockSpec((keys, sums_wide), lambda t: (0, t)))
        args.append(acc)
    f32, bf16 = jnp.float32, jnp.bfloat16
    outs = [
        jax.ShapeDtypeStruct((depth, rows), bf16),
        jax.ShapeDtypeStruct((rows, kv_here * strip.shape[1]), bf16),
        jax.ShapeDtypeStruct((rows, depth), bf16),
        jax.ShapeDtypeStruct((8, depth), f32),
    ]
    outs = outs if full else outs[:2]
    out_specs = [whole(out) for out in outs]
    if full and start > 0:
        outs.append(jax.ShapeDtypeStruct((start, levels * sums_wide), f32))
        out_specs.append(pl.BlockSpec((start, sums_wide), lambda t: (0, t)))
    results = pl.pallas_call(
        functools.partial(backward_kernel, start, full),
        out_shape=outs,
        grid=(levels if full else 1,),
        in_specs=in_specs,
        out_specs=out_specs,
        scratch_shapes=[
            pltpu.VMEM((rows, depth), f32),
            pltpu.VMEM((rows, depth), bf16),
            pltpu.VMEM((rows, depth), f32),
        ],
        compiler_params=params(),
        cost_estimate=cost(
            levels * rows * (20 * kv_here * keys * LANES + 2 * depth * (out_wide + wide)),
            2 * depth * levels * (out_wide + wide) + 16 * rows * depth,
            levels * kv_here * GROUP * rows * keys,
        ),
    )(*args)
    return results[:4], (results[4] if full and start > 0 else None)


def rows_kernel(lefts, groups, adding, picked, together, side_ref, *refs):
    refs = list(refs)
    held_ref = refs.pop()
    out_refs = refs[-len(picked) :]
    refs = refs[: -len(picked)]
    recv_ref = refs.pop() if adding else None
    step = pl.program_id(0)
    left_refs = []
    for count in lefts:
        left_refs.append(refs[:count])
        refs = refs[count:]
    rights = []
    for _ in groups:
        rights.append(refs[:CHUNKS])
        refs = refs[CHUNKS:]
    rows = left_refs[0][0].shape[0]
    blocks = held_ref.shape[1] // rows

    @pl.when(step == 0)
    def _():
        for which, pieces in enumerate(left_refs):
            for n, ref in enumerate(pieces):
                m, j = n % blocks, n // blocks
                wide = ref.shape[1]
                held_ref[which, m * rows : (m + 1) * rows, j * wide : (j + 1) * wide] = ref[...]

    chunk = held_ref.shape[2] // CHUNKS
    whole_columns = slice(0, out_refs[0].shape[1])

    def give(group, left, columns):
        right = jnp.concatenate([ref[:chunk, :].astype(jnp.bfloat16) for ref in group], 0)
        total = dot32(held_ref[left], right)
        if recv_ref is not None:
            total = total + recv_ref[:, columns]
        for out_ref, parts in zip(out_refs, picked):
            at = 0
            for start, size in parts:
                out_ref[at : at + size, columns] = total[start : start + size]
                at += size

    begin = 0
    for group, (left, first, steps) in zip(rights, groups):
        if together:
            width = group[0].shape[1]
            give(group, left, slice(begin, begin + width))
            begin += width
        else:

            @pl.when((step >= first) & (step < first + steps))
            def _(group=group, left=left):
                give(group, left, whole_columns)


def rows_of(lefts, groups, side, rows, blocks, step, recv=None, picked=None):
    if picked is None:
        picked = [[(0, rows * blocks)]]
    at = lambda m: lambda i, side: ((m ^ side[2]) * side[1] + side[0], 0)
    specs = []
    args = []
    counts = []
    for left in lefts:
        pieces = left if isinstance(left, list) else [left]
        counts.append(len(pieces) * blocks)
        for piece in pieces:
            for m in range(blocks):
                specs.append(pl.BlockSpec((rows, piece.shape[1]), at(m)))
                args.append(piece)
    tokens = sum(piece.shape[1] for piece in pieces)
    first = 0
    plan = []
    together = step is None
    for which, rights in groups:
        if together:
            plan.append((which, 0, 1))
            specs += [whole(right) for right in rights]
            args += rights
            first += rights[0].shape[1]
            continue
        steps = rights[0].shape[1] // step
        plan.append((which, first, steps))
        for right in rights:
            pick = lambda i, side, first=first, steps=steps: (0, jnp.clip(i - first, 0, steps - 1))
            specs.append(pl.BlockSpec((right.shape[0], step), pick))
            args.append(right)
        first += steps
    if together:
        first, step = 1, first
    total = first * step
    block = lambda height: pl.BlockSpec((height, step), lambda i, side: (0, i))
    if recv is not None:
        specs.append(block(rows * blocks))
        args.append(recv)
    heights = [sum(size for _, size in parts) for parts in picked]
    results = pl.pallas_call(
        functools.partial(rows_kernel, counts, plan, recv is not None, picked, together),
        out_shape=[jax.ShapeDtypeStruct((height, total), jnp.float32) for height in heights],
        grid_spec=pltpu.PrefetchScalarGridSpec(
            num_scalar_prefetch=1,
            grid=(first,),
            in_specs=specs,
            out_specs=[block(height) for height in heights],
            scratch_shapes=[pltpu.VMEM((len(lefts), rows * blocks, tokens), jnp.bfloat16)],
        ),
        compiler_params=params(),
        cost_estimate=cost(
            2 * rows * blocks * tokens * total,
            4 * rows * blocks * total + 2 * tokens * (total + rows * blocks),
        ),
    )(side, *args)
    return results[0] if len(picked) == 1 else results


def shards(
    tokens,
    lengths,
    positions,
    cotangent,
    norm_gain,
    w_query,
    w_key,
    w_value,
    w_out,
    mlp_gain,
    w_gate,
    w_up,
    w_down,
):
    seq_rows, depth = tokens.shape
    chips = lax.axis_size("chip")
    dp = chips * 2
    tp = lax.axis_size("tp")
    chip = lax.axis_index("chip")
    core = lax.axis_index("core")
    level = lax.axis_index("tp")
    low = level < 2
    inner = (level == 1) | (level == 2)
    heads_here = w_query.shape[1] // HD
    kv_here = w_key.shape[1] // HD
    rows = seq_rows // CHUNKS
    slice_rows = depth // dp
    level_ref = level.astype(jnp.int32).reshape(1)
    by_hand = dp == 8
    swap = lambda array: lax.ppermute(array, "core", [(0, 1), (1, 0)])
    to_level = lambda array, s: along(array, [(t, t ^ s) for t in range(tp)])

    at_row = (chip * 2 + core) * slice_rows
    cols = lambda w: lax.dynamic_slice_in_dim(w, at_row, slice_rows, 1).astype(jnp.float32).T
    (out_slice,) = fence(cols(w_out))
    qkv_slice = jnp.concatenate(
        [
            lax.dynamic_slice_in_dim(w_query, at_row, slice_rows, 0).astype(jnp.float32),
            cols(w_key.T),
            cols(w_value.T),
        ],
        1,
    )
    out_slice, qkv_slice = fence(out_slice, qkv_slice)
    out_near = along(out_slice, PAIRS)
    qkv_near = along(qkv_slice, PAIRS)
    meta = jnp.stack([chip, core]).astype(jnp.int32)

    pq = place_query(heads_here)
    pkv = place_key_value(kv_here)
    p_all = place_all(heads_here, kv_here)
    strip_one = place_all(GROUP, 1).T
    p_out = place_plain(heads_here)
    strip_out = p_out.T

    half_dim = HD // 2
    freqs = rope_base ** (-(jnp.arange(half_dim).astype(jnp.float32) * 2.0 / HD))
    freqs = jnp.pad(freqs, (0, LANES // 2 - half_dim))
    angles = positions.astype(jnp.float32)[:, None] * jnp.concatenate([freqs, freqs])[None, :]
    cosines = jnp.cos(angles)
    sines = jnp.sin(angles) * jnp.where(jnp.arange(LANES) < LANES // 2, -1.0, 1.0)

    cosines, sines, out_near = fence(cosines, sines, out_near)
    out_across = along(jnp.stack([out_slice, out_near]), MIDDLE)
    qkv_own, normed_one, own_pad = start(
        tokens, norm_gain, w_query, w_key.T, w_value.T, pq, pkv, cosines, sines
    )

    def far_slices(near, across, outer):
        return jnp.stack(
            [
                near,
                jnp.where(inner, across[1], outer[0]),
                jnp.where(inner, across[0], outer[1]),
            ]
        )

    order = list(reversed(range(CHUNKS)))
    c0, c1, c2, c3 = order
    own, other, across, outer = {}, {}, {}, {}
    part, total, final = {}, {}, {}

    def hop_1(j):
        other[j] = along(own[j], PAIRS)

    def hop_2(j):
        across[j] = along(jnp.concatenate([own[j], other[j]], 1), MIDDLE)

    def hop_3(j):
        outer[j] = along(across[j], OUTWARD)

    coming = {}

    def add_1(j):
        coming[j] = along(part[j], INWARD)

    def add_2(j):
        total[j] = part[j][:rows] + coming[j][:rows]
        coming[j] = along(total[j], MIDDLE)

    def add_3(j, inward):
        total[j] = jnp.where(inner, total[j] + coming[j], inward)
        final[j] = along(total[j], PAIRS)
        return final[j]

    def to_chip(array, m):
        return lax.ppermute(array, "chip", [(i, i ^ m) for i in range(chips)])

    def over_chips_1(piece):
        cut = piece.shape[1] // 2
        one, two = piece[:, :cut], piece[:, cut:]
        return jnp.stack([one, to_chip(one, 1)]), jnp.stack([two, to_chip(two, 2)])

    def over_chips_2(one, two):
        return one, to_chip(one, 2), two, to_chip(two, 1)

    def over_chips_3(one, one_far, two, two_far):
        upper = jnp.stack([one[0], one[1], one_far[0], one_far[1]])
        lower = jnp.stack([two[0], two_far[0], two[1], two_far[1]])
        return jnp.concatenate([upper, lower], 2)

    qkv_own, out_across, qkv_near = fence(qkv_own, out_across, qkv_near)
    out_outer = along(out_across, OUTWARD)
    qkv_across = along(jnp.stack([qkv_slice, qkv_near]), MIDDLE)
    own[c0] = attend(lengths, qkv_own, strip_out, c0, rows)
    own, qkv_own, out_outer = fence(own, qkv_own, out_outer)
    hop_1(c0)
    out_far = far_slices(out_near, out_across, out_outer)
    out_mine = over_chips_1(out_far) if by_hand else out_far
    own[c1] = attend(lengths, qkv_own, strip_out, c1, rows)
    own[c1], qkv_own = fence(own[c1], qkv_own)
    hop_1(c1)
    own[c2] = attend(lengths, qkv_own, strip_out, c2, rows)
    own, other[c0], normed_one, w_out, out_mine, qkv_across, qkv_own = fence(
        own, other[c0], normed_one, w_out, out_mine, qkv_across, qkv_own
    )
    own[c3] = attend(lengths, qkv_own, strip_out, c3, rows)
    qkv_outer = along(qkv_across, OUTWARD)
    if by_hand:
        out_mine = over_chips_2(*out_mine)
    else:
        out_mine = lax.all_gather(out_mine, ("chip", "core"))
    hop_2(c0)
    dout, dout_t, normed_one_t = turn(lengths, cotangent, normed_one)
    w_out_t = w_out.T
    own, other, across, dout, dout_t, normed_one_t, w_out_t, out_mine, qkv_outer = fence(
        own, other, across, dout, dout_t, normed_one_t, w_out_t, out_mine, qkv_outer
    )
    hop_1(c2)
    hop_3(c0)
    hop_2(c1)
    qkv_far = lax.all_gather(far_slices(qkv_near, qkv_across, qkv_outer), ("chip", "core"))
    if by_hand:
        out_mine = over_chips_3(*out_mine)
        out_theirs = swap(out_mine)
        out_pad, out_plain = spread(
            spread_out_kernel,
            meta,
            w_out_t,
            [p_out],
            out_mine,
            out_theirs,
            [4 * p_out.shape[1], 4 * p_out.shape[0]],
        )
    else:
        plain = [w_out_t] + [
            out_mine[:, s].reshape(depth, -1).astype(jnp.bfloat16) for s in range(tp - 1)
        ]
        out_plain = jnp.concatenate(plain, 1)
        out_pad = jnp.concatenate([dot32(w, p_out).astype(jnp.bfloat16) for w in plain], 1)
    hidden, normed_t, activ, dgate, dup, mlp_part = {}, {}, {}, {}, {}, {}

    def feed(j):
        gathered = (own[j], other[j], across[j], outer[j])
        (hidden[j], normed_t[j], activ[j], dgate[j], dup[j], mlp_part[j], part[j]) = forward_chunk(
            level_ref, gathered, tokens, dout, out_plain, mlp_gain, w_gate, w_up, w_down, j, rows
        )

    own, other, across, outer, out_pad, out_plain = fence(
        own, other, across, outer, out_pad, out_plain
    )
    hop_1(c3)
    hop_3(c1)
    hop_2(c2)
    feed(c0)
    own, other, across, outer, part, hidden = fence(own, other, across, outer, part, hidden)
    add_1(c0)
    hop_3(c2)
    hop_2(c3)
    feed(c1)
    outer[c2], hidden[c1] = fence(outer[c2], hidden[c1])
    feed(c2)
    own, other, across, outer, part, total, coming, hidden = fence(
        own, other, across, outer, part, total, coming, hidden
    )
    add_1(c1)
    hop_3(c3)
    add_2(c0)
    qkv_far, part = fence(qkv_far, part)
    qkv_pad = spread_qkv(own_pad, pq, pkv, qkv_far)
    qkv = project(normed_one, qkv_pad, cosines, sines)
    own, other, across, outer, part, total, coming, hidden, qkv = fence(
        own, other, across, outer, part, total, coming, hidden, qkv
    )
    coming[c2] = add_3(c0, part[c2][:rows])
    add_2(c1)
    feed(c3)

    listed = lambda pieces: [pieces[j] for j in range(CHUNKS)]
    keep_side = jnp.stack([core, 2, 0]).astype(jnp.int32)
    keep_turned = jnp.stack([core, 2, chip]).astype(jnp.int32)
    send_side = jnp.stack([1 - core, 2, 0]).astype(jnp.int32)
    send_turned = jnp.stack([1 - core, 2, chip]).astype(jnp.int32)
    all_rows = jnp.array([0, 1, 0], jnp.int32)

    def send_rows(lefts, groups, step, side=send_side):
        if not by_hand:
            return rows_of(lefts, groups, all_rows, depth // 4, 4, step)
        return rows_of(lefts, groups, side, slice_rows, chips, step)

    def keep_rows(lefts, groups, received, step, side=keep_side, picked=None):
        if not by_hand:
            return received
        return rows_of(lefts, groups, side, slice_rows, chips, step, received, picked)

    def swap_rows(array):
        return swap(array) if by_hand else array

    def scatter(array, axes):
        return lax.psum_scatter(array, axes, scatter_dimension=0, tiled=True)

    units = w_gate.shape[1]
    mlp_args = (
        [listed(normed_t), dout_t],
        [(0, listed(dgate)), (0, listed(dup)), (1, listed(activ))],
    )
    acc = None
    dhid_t, dqkv_own, input_grad, gains = {}, {}, {}, {}

    def back(j):
        nonlocal acc
        (dhid_t[j], dqkv_own[j], input_grad[j], gains[j]), acc = back_some(j, True)

    def back_own(j):
        return back_some(j, False)[0]

    def back_some(j, full):
        return backward_chunk(
            level_ref,
            (total[j], final[j]),
            hidden[j],
            dout,
            tokens,
            (norm_gain, mlp_gain),
            (out_pad, qkv_pad),
            qkv,
            (own[j], other[j], across[j], outer[j]),
            (p_out, strip_one),
            (cosines, sines),
            acc,
            j,
            rows,
            full,
        )

    grad_mlp = rows_of(*mlp_args, all_rows, depth // 4, 4, units // 2)
    own, other, across, outer, part, total, coming, final, hidden, grad_mlp = fence(
        own, other, across, outer, part, total, coming, final, hidden, grad_mlp
    )
    grad_mlp = scatter(grad_mlp, ("chip", "core"))
    coming[c3] = add_3(c1, part[c3][:rows])
    add_2(c2)
    back(c0)

    near = lambda: jnp.where(low, mlp_part[1], mlp_part[2])
    edge = lambda: jnp.where(low, mlp_part[0], mlp_part[3])
    leave_far = lambda: jnp.where(low, mlp_part[3], mlp_part[0])
    leave_near = lambda: jnp.where(low, mlp_part[2], mlp_part[1])
    total, coming, final, hidden, mlp_part, acc, dhid_t = fence(
        total, coming, final, hidden, mlp_part, acc, dhid_t
    )
    far_sum = add_3(c2, leave_far())
    add_2(c3)
    back(c1)
    total, coming, final, hidden, mlp_part, far_sum, acc, dhid_t = fence(
        total, coming, final, hidden, mlp_part, far_sum, acc, dhid_t
    )
    near_sum = add_3(c3, leave_near())
    far_in = along(leave_far() + far_sum, MIDDLE)
    back(c2)
    total, final, hidden, mlp_part, near_sum, far_in, acc, dhid_t = fence(
        total, final, hidden, mlp_part, near_sum, far_in, acc, dhid_t
    )
    last = along(jnp.where(inner, edge() + far_in, near()), PAIRS)
    near_in = along(leave_near() + near_sum, MIDDLE)
    dhid_t[c3], dqkv_own[c3] = back_own(c3)
    q_cols = heads_here * HD
    attn_args = (
        [listed(dhid_t), normed_one_t],
        [(0, listed(own)), (1, listed(dqkv_own))],
    )
    sent = swap_rows(send_rows(*attn_args, None, send_turned))
    total, final, hidden, acc, sent = fence(total, final, hidden, acc, sent)
    if by_hand:
        half = slice_rows // 2
        upper = lambda m: (m * slice_rows, half)
        lower = lambda m: (m * slice_rows + half, half)
        picked = [
            [upper(1), upper(3)],
            [upper(0), upper(2)],
            [lower(2), lower(3)],
            [lower(0), lower(1)],
        ]
        pieces = keep_rows(*attn_args, sent, None, keep_turned, picked)
        pieces, hidden = fence(pieces, hidden)
        one_away, one, two_away, two = pieces
        pieces = (one, to_chip(one_away, 1), two, to_chip(two_away, 2))
    else:
        pieces = scatter(sent, ("chip", "core"))
    back(c3)
    pieces, gains, input_grad, last, near_in = fence(pieces, gains, input_grad, last, near_in)
    gain_sums = gains[0] + gains[1] + gains[2] + gains[3]
    gain_sums = gain_sums + swap(gain_sums)
    if by_hand:
        others = [to_chip(gain_sums, m) for m in range(1, chips)]
        gain_sums = sum(others, gain_sums)
        one = pieces[0] + pieces[1]
        two = pieces[2] + pieces[3]
        one = one[:half] + to_chip(one[half:], 2)
        two = two[:half] + to_chip(two[half:], 1)
        attn = jnp.concatenate([one, two], 0)
    else:
        gain_sums = lax.psum(gain_sums, "chip")
        attn = pieces
    gain_rows = lax.dynamic_slice_in_dim(gain_sums, at_row, slice_rows, 1)
    grad_out, grad_qkv = attn[:, :q_cols], attn[:, q_cols:]
    mlp_rows = jnp.where(inner, near() + near_in, edge()) + last
    hidden_rows = jnp.where(
        low,
        jnp.where(level == 0, hidden[0], hidden[1]),
        jnp.where(level == 2, hidden[2], hidden[3]),
    )
    layer_out = (hidden_rows + mlp_rows).astype(jnp.bfloat16)
    one = strip_one.shape[1]
    picked = lambda at, width: jnp.concatenate(
        [grad_qkv[:, kv * one + at : kv * one + at + width] for kv in range(kv_here)], 1
    )
    return (
        layer_out,
        jnp.concatenate(listed(input_grad), 0),
        gain_rows[0],
        picked(0, GROUP * HD),
        picked(GROUP * HD, HD),
        picked((GROUP + 1) * HD, HD),
        grad_out.T,
        gain_rows[1],
        grad_mlp[:, :units],
        grad_mlp[:, units : 2 * units],
        grad_mlp[:, 2 * units :].T,
    )


def solution(mesh):
    devices = mesh.devices
    dp, tp = devices.shape
    split = Mesh(devices.reshape(dp // 2, 2, tp), ("chip", "core", "tp"))
    data = ("chip", "core")
    return jax.shard_map(
        shards,
        mesh=split,
        in_specs=(
            P(data, None),
            P(data),
            P(data),
            P(data, None),
            P(),
            P(None, "tp"),
            P(None, "tp"),
            P(None, "tp"),
            P("tp", None),
            P(),
            P(None, "tp"),
            P(None, "tp"),
            P("tp", None),
        ),
        out_specs=(
            P(("chip", "core", "tp"), None),
            P(data, None),
            P(data),
            P(data, "tp"),
            P(data, "tp"),
            P(data, "tp"),
            P("tp", data),
            P(data),
            P(data, "tp"),
            P(data, "tp"),
            P("tp", data),
        ),
        check_vma=False,
    )
```

```python
import functools

import jax
import jax.numpy as jnp
from jax import lax
from jax.experimental import pallas as pl
from jax.experimental.pallas import tpu as pltpu
from jax.sharding import Mesh
from jax.sharding import PartitionSpec as P

HD = 96
LANES = 128
GROUP = 2
KV_WIDE = (GROUP + 2) * LANES
rope_base = 100000.0
norm_eps = 1e-05
masked_score = -1e30
far_away = 1e30
score_scale = HD ** (-0.5)
score_scale_log2 = score_scale * 1.4426950408889634
CHUNKS = 4
EXTRA = 8
VMEM_BYTES = 56 * 1024 * 1024
NT = (((1,), (1,)), ((), ()))


def params():
    return pltpu.CompilerParams(vmem_limit_bytes=VMEM_BYTES)


def cost(flops, moved, exps=0):
    return pl.CostEstimate(
        flops=flops // 1024, bytes_accessed=moved // 1024, transcendentals=exps // 1024
    )


def dot32(a, b):
    return jnp.dot(a, b, preferred_element_type=jnp.float32)


def dot32_nt(a, b):
    return lax.dot_general(a, b, NT, preferred_element_type=jnp.float32)


def dot_split(a, places):
    high = a.astype(jnp.bfloat16)
    rest = (a - high.astype(jnp.float32)).astype(jnp.bfloat16)
    return dot32(high, places) + dot32(rest, places)


def fence(*trees):
    return lax.optimization_barrier(trees)


def whole(array, buffers=None):
    zeros = (0,) * len(array.shape)
    return pl.BlockSpec(array.shape, lambda *_: zeros)


SCALAR = pl.BlockSpec(memory_space=pltpu.SMEM)


def halves(entry):
    half_dim = HD // 2
    return (entry // half_dim) * (LANES // 2) + entry % half_dim


def placement(lanes, width):
    return (lanes[:, None] == jnp.arange(width)[None, :]).astype(jnp.bfloat16)


def place_query(heads):
    source = jnp.arange(heads * HD)
    return placement((source // HD) * LANES + halves(source % HD), heads * LANES)


def place_key_value(kv_heads):
    source = jnp.arange(kv_heads * HD)
    head = source // HD
    keys = head * 2 * LANES + halves(source % HD)
    values = head * 2 * LANES + LANES + source % HD
    return placement(jnp.concatenate([keys, values]), kv_heads * 2 * LANES)


def place_all(heads, kv_heads):
    source = jnp.arange(heads * HD)
    head = source // HD
    query = (head // GROUP) * KV_WIDE + (head % GROUP) * LANES + halves(source % HD)
    source = jnp.arange(kv_heads * HD)
    base = (source // HD) * KV_WIDE + GROUP * LANES
    keys = base + halves(source % HD)
    values = base + LANES + source % HD
    return placement(jnp.concatenate([query, keys, values]), kv_heads * KV_WIDE)


def place_plain(heads):
    source = jnp.arange(heads * HD)
    return placement((source // HD) * LANES + source % HD, heads * LANES)


PAIRS = [(0, 1), (1, 0), (2, 3), (3, 2)]
INWARD = [(0, 1), (3, 2)]
MIDDLE = [(1, 2), (2, 1)]
OUTWARD = [(1, 0), (2, 3)]


def along(part, pairs):
    return lax.ppermute(part, "tp", pairs)


def store_qkv(out_ref, here, base, query, key_value):
    wide = GROUP * LANES
    for kv in range(key_value.shape[1] // (2 * LANES)):
        at = base + kv * KV_WIDE
        there = slice(kv * 2 * LANES, (kv + 1) * 2 * LANES)
        out_ref[here, at : at + wide] = query[:, kv * wide : (kv + 1) * wide]
        out_ref[here, at + wide : at + KV_WIDE] = key_value[:, there]


def store_turned(out_ref, at, lin, cos_ref, sin_ref):
    for h in range(GROUP + 2):
        one = lin[:, h * LANES : (h + 1) * LANES]
        if h < GROUP + 1:
            one = one * cos_ref[...] + pltpu.roll(one, LANES // 2, 1) * sin_ref[...]
        out_ref[:, at + h * LANES : at + (h + 1) * LANES] = one.astype(jnp.bfloat16)


def spread_out_kernel(meta_ref, own_ref, p_ref, mine_ref, theirs_ref, pad_ref, plain_ref):
    rows, width = mine_ref.shape[2:]
    wide = p_ref.shape[1]
    for side, ref in enumerate((mine_ref, theirs_ref)):
        here = pl.ds(pl.multiple_of((meta_ref[1] ^ side) * rows, rows), rows)
        for s in range(4):
            block = own_ref[here, :] if s == 0 else ref[0, s - 1].astype(jnp.bfloat16)
            plain_ref[here, s * width : (s + 1) * width] = block
            pad_ref[here, s * wide : (s + 1) * wide] = dot32(block, p_ref[...]).astype(
                jnp.bfloat16
            )


def spread_qkv_kernel(pq_ref, pkv_ref, far_ref, _, out_ref):
    parts, _, rows, width = far_ref.shape
    split = pq_ref.shape[0]
    block = far_ref[:, 0].reshape(parts * rows, width).astype(jnp.bfloat16)
    query = dot32(block[:, :split], pq_ref[...]).astype(jnp.bfloat16)
    key_value = dot32(block[:, split:], pkv_ref[...]).astype(jnp.bfloat16)
    store_qkv(out_ref, slice(None), 0, query, key_value)


def spread_qkv(padded, pq, pkv, far):
    total = padded.shape[0]
    dp, others, rows, width = far.shape
    wide = padded.shape[1] // (others + 1)
    parts = max(1, dp // 2)
    block = parts * rows
    return pl.pallas_call(
        spread_qkv_kernel,
        out_shape=jax.ShapeDtypeStruct(padded.shape, jnp.bfloat16),
        grid=(total // block, others),
        in_specs=[
            whole(pq),
            whole(pkv),
            pl.BlockSpec((parts, 1, rows, width), lambda i, s: (i, s, 0, 0)),
            pl.BlockSpec(memory_space=pl.ANY),
        ],
        out_specs=pl.BlockSpec((block, wide), lambda i, s: (i, s + 1)),
        input_output_aliases={3: 0},
        compiler_params=params(),
        cost_estimate=cost(8 * total * width * 512, 20 * total * wide),
    )(pq, pkv, far, padded)


def spread(kernel, meta, own, places, mine, theirs, widths):
    chips, others, rows, width = mine.shape
    total = own.shape[0]
    row_block = lambda m, meta: (meta[0] ^ m, 0)
    piece = pl.BlockSpec((1, others, rows, width), lambda m, meta: (m, 0, 0, 0))
    return pl.pallas_call(
        kernel,
        out_shape=[jax.ShapeDtypeStruct((total, wide), jnp.bfloat16) for wide in widths],
        grid_spec=pltpu.PrefetchScalarGridSpec(
            num_scalar_prefetch=1,
            grid=(chips,),
            in_specs=[pl.BlockSpec((2 * rows, own.shape[1]), row_block)]
            + [whole(place) for place in places]
            + [piece, piece],
            out_specs=[pl.BlockSpec((2 * rows, wide), row_block) for wide in widths],
        ),
        compiler_params=params(),
        cost_estimate=cost(
            8 * total * width * 512, total * (12 * width + 2 * sum(widths))
        ),
    )(meta, own, *places, mine, theirs)


def start_kernel(x_ref, gain_ref, q_ref, k_ref, v_ref, pq_ref, pkv_ref, cos_ref, sin_ref, *outs):
    qkv_ref, normed_ref, pad_ref = outs

    @pl.when(pl.program_id(0) == 0)
    def _():
        split = k_ref.shape[0]
        query = dot32(q_ref[...], pq_ref[...]).astype(jnp.bfloat16)
        key_value = dot32(k_ref[...].T, pkv_ref[:split, :])
        key_value = key_value + dot32(v_ref[...].T, pkv_ref[split:, :])
        store_qkv(pad_ref, slice(None), 0, query, key_value.astype(jnp.bfloat16))

    inputs = x_ref[...].astype(jnp.float32)
    rms = lax.rsqrt(jnp.mean(inputs * inputs, -1, keepdims=True) + norm_eps)
    normed = (inputs * rms * gain_ref[...]).astype(jnp.bfloat16)
    normed_ref[...] = normed
    for kv in range(pad_ref.shape[1] // KV_WIDE):
        at = kv * KV_WIDE
        store_turned(qkv_ref, at, dot32(normed, pad_ref[:, at : at + KV_WIDE]), cos_ref, sin_ref)


def start(tokens, gain, w_query, w_key_t, w_value_t, pq, pkv, cosines, sines):
    total, depth = tokens.shape
    rows = total // CHUNKS
    wide = pq.shape[1] + pkv.shape[1]
    gain = gain[None, :]
    by_rows = lambda width: pl.BlockSpec((rows, width), lambda i: (i, 0))
    arrays = [w_query, w_key_t, w_value_t, pq, pkv]
    shapes = [
        jax.ShapeDtypeStruct((total, 4 * wide), jnp.bfloat16),
        jax.ShapeDtypeStruct((total, depth), jnp.bfloat16),
        jax.ShapeDtypeStruct((depth, 4 * wide), jnp.bfloat16),
    ]
    return pl.pallas_call(
        start_kernel,
        out_shape=shapes,
        grid=(CHUNKS,),
        in_specs=[by_rows(depth), whole(gain)]
        + [whole(array) for array in arrays]
        + [by_rows(LANES), by_rows(LANES)],
        out_specs=[
            by_rows(wide),
            by_rows(depth),
            pl.BlockSpec((depth, wide), lambda i: (0, 0)),
        ],
        compiler_params=params(),
        cost_estimate=cost(2 * total * depth * wide, 12 * total * depth),
    )(tokens, gain, *arrays, cosines, sines)


def turn_kernel(length_ref, cot_ref, normed_ref, dout_ref, dout_t_ref, normed_t_ref):
    rows = cot_ref.shape[0]
    at = pl.program_id(0) * rows + lax.broadcasted_iota(jnp.int32, cot_ref.shape, 0)
    dout = jnp.where(at < length_ref[0], cot_ref[...].astype(jnp.float32), 0.0)
    dout = dout.astype(jnp.bfloat16)
    dout_ref[...] = dout
    dout_t_ref[...] = dout.T
    normed_t_ref[...] = normed_ref[...].T


def turn(length, cotangent, normed):
    total, depth = cotangent.shape
    rows = total // CHUNKS
    by_rows = pl.BlockSpec((rows, depth), lambda i: (i, 0))
    by_columns = pl.BlockSpec((depth, rows), lambda i: (0, i))
    turned = jax.ShapeDtypeStruct((depth, total), jnp.bfloat16)
    return pl.pallas_call(
        turn_kernel,
        out_shape=[jax.ShapeDtypeStruct((total, depth), jnp.bfloat16), turned, turned],
        grid=(CHUNKS,),
        in_specs=[SCALAR, by_rows, by_rows],
        out_specs=[by_rows, by_columns, by_columns],
        compiler_params=params(),
        cost_estimate=cost(total * depth, 10 * total * depth),
    )(length, cotangent, normed)


def project_kernel(x_ref, w_ref, cos_ref, sin_ref, _, out_ref):
    store_turned(out_ref, 0, dot32(x_ref[...], w_ref[...]), cos_ref, sin_ref)


def project(normed, weights, cosines, sines, qkv):
    rows, depth = normed.shape
    width = weights.shape[1]
    steps = width // KV_WIDE
    first = steps // 4
    return pl.pallas_call(
        project_kernel,
        out_shape=jax.ShapeDtypeStruct((rows, width), jnp.bfloat16),
        grid=(steps - first,),
        in_specs=[
            whole(normed),
            pl.BlockSpec((depth, KV_WIDE), lambda i: (0, i + first)),
            whole(cosines),
            whole(sines),
            pl.BlockSpec(memory_space=pl.ANY),
        ],
        out_specs=pl.BlockSpec((rows, KV_WIDE), lambda i: (0, i + first)),
        input_output_aliases={4: 0},
        compiler_params=params(),
        cost_estimate=cost(
            2 * rows * depth * width, 2 * (rows * depth + depth * width + rows * width)
        ),
    )(normed, weights, cosines, sines, qkv)


def attend_kernel(start, length_ref, q_ref, kv_ref, strip_ref, out_ref):
    rows = q_ref.shape[0]
    keys = kv_ref.shape[0]
    length = length_ref[0]
    row_ids = start + lax.broadcasted_iota(jnp.int32, (1, rows), 1)
    limit = jnp.minimum(row_ids, length - 1)
    allowed = lax.broadcasted_iota(jnp.int32, (keys, rows), 0) <= limit
    mixed = []
    sums = []
    for kv in range(kv_ref.shape[1] // KV_WIDE):
        base = kv * KV_WIDE
        at = base + GROUP * LANES
        key = kv_ref[:, at : at + LANES]
        value_t = kv_ref[:, at + LANES : at + 2 * LANES].T
        for g in range(GROUP):
            query = q_ref[:, base + g * LANES : base + (g + 1) * LANES]
            raw = jnp.where(allowed, dot32_nt(key, query), masked_score)
            peak = jnp.max(raw, axis=0, keepdims=True)
            expo = jnp.exp2((raw - peak) * score_scale_log2)
            total = jnp.sum(expo, axis=0, keepdims=True)
            probs = (expo * (1.0 / total)).astype(jnp.bfloat16)
            mixed.append(dot32(value_t, probs).T)
            log_sum = peak * score_scale_log2 + jnp.log2(total)
            sums.append(jnp.where(row_ids < length, log_sum, far_away))
    out_ref[:rows, :] = dot_split(jnp.concatenate(mixed, 1), strip_ref[...])
    out_ref[rows:, :] = jnp.zeros((EXTRA, out_ref.shape[1]), jnp.float32)
    out_ref[rows : rows + len(sums), :rows] = jnp.concatenate(sums, 0)


def attend(length, qkv, strip, index, rows):
    keys = (index + 1) * rows
    width = qkv.shape[1] // 4
    heads = width // KV_WIDE * GROUP
    shape = (rows + EXTRA, strip.shape[1])
    return pl.pallas_call(
        functools.partial(attend_kernel, index * rows),
        out_shape=jax.ShapeDtypeStruct(shape, jnp.float32),
        grid=(1,),
        in_specs=[
            SCALAR,
            pl.BlockSpec((rows, width), lambda i: (index, 0)),
            pl.BlockSpec((keys, width), lambda i: (0, 0)),
            whole(strip),
        ],
        out_specs=pl.BlockSpec(shape, lambda i: (0, 0)),
        compiler_params=params(),
        cost_estimate=cost(
            4 * heads * rows * keys * LANES, 2 * (rows + keys) * width, heads * rows * keys
        ),
    )(length, qkv, qkv, strip)


def forward_kernel(level_ref, part_ref, other_ref, across_ref, outer_ref, *refs):
    x_ref, dout_ref, wo_ref, gain_ref, wg_ref, wu_ref, wd_ref = refs[:7]
    hidden_ref, normed_t_ref, activ_ref, dgate_ref, dup_ref, mlp_ref, dn_ref = refs[7:14]
    normed_ref = refs[14]
    rows = x_ref.shape[0]

    @pl.when(pl.program_id(0) == 0)
    def _():
        level = level_ref[0]
        inner = (level == 1) | (level == 2)
        width = part_ref.shape[1]
        second = jnp.where(inner, across_ref[:rows, width:], outer_ref[:rows, :width])
        third = jnp.where(inner, across_ref[:rows, :width], outer_ref[:rows, width:])
        mixed = jnp.concatenate([part_ref[:rows, :], other_ref[:rows, :], second, third], 1)
        hidden = x_ref[...].astype(jnp.float32) + dot32_nt(mixed.astype(jnp.bfloat16), wo_ref[...])
        hidden_ref[...] = hidden
        rms = lax.rsqrt(jnp.mean(hidden * hidden, -1, keepdims=True) + norm_eps)
        normed = (hidden * rms * gain_ref[...]).astype(jnp.bfloat16)
        normed_ref[...] = normed
        normed_t_ref[...] = normed.T
        mlp_ref[...] = jnp.zeros_like(mlp_ref)
        dn_ref[...] = jnp.zeros_like(dn_ref)

    normed = normed_ref[...]
    gate = dot32(normed, wg_ref[...])
    up = dot32(normed, wu_ref[...])
    dact = dot32_nt(dout_ref[...], wd_ref[...])
    sigmoid = jax.nn.sigmoid(gate)
    silu = gate * sigmoid
    activ = (silu * up).astype(jnp.bfloat16)
    dgate = (dact * up * sigmoid * (1.0 + gate * (1.0 - sigmoid))).astype(jnp.bfloat16)
    dup = (dact * silu).astype(jnp.bfloat16)
    activ_ref[...] = activ
    dgate_ref[...] = dgate
    dup_ref[...] = dup
    mlp_ref[...] += dot32(activ, wd_ref[...])
    dn_ref[:rows, :] += dot32_nt(dgate, wg_ref[...]) + dot32_nt(dup, wu_ref[...])


def forward_chunk(level, gathered, tokens, dout, w_out, gain, w_gate, w_up, w_down, index, rows):
    depth = tokens.shape[1]
    units = w_gate.shape[1]
    block = 512
    own_rows = pl.BlockSpec((rows, depth), lambda i: (index, 0))
    by_units = pl.BlockSpec((depth, block), lambda i: (0, i))
    gain = gain[None, :]
    f32, bf16 = jnp.float32, jnp.bfloat16
    outs = [
        jax.ShapeDtypeStruct((rows, depth), f32),
        jax.ShapeDtypeStruct((depth, rows), bf16),
        jax.ShapeDtypeStruct((rows, units), bf16),
        jax.ShapeDtypeStruct((rows, units), bf16),
        jax.ShapeDtypeStruct((rows, units), bf16),
        jax.ShapeDtypeStruct((rows, depth), f32),
        jax.ShapeDtypeStruct((rows + EXTRA, depth), f32),
    ]
    unit_out = pl.BlockSpec((rows, block), lambda i: (0, i))
    return pl.pallas_call(
        forward_kernel,
        out_shape=outs,
        grid=(units // block,),
        in_specs=[SCALAR]
        + [whole(array) for array in gathered]
        + [own_rows, own_rows, whole(w_out), whole(gain), by_units, by_units]
        + [pl.BlockSpec((block, depth), lambda i: (i, 0))],
        out_specs=[
            whole(outs[0]),
            whole(outs[1]),
            unit_out,
            unit_out,
            unit_out,
            whole(outs[5]),
            whole(outs[6]),
        ],
        scratch_shapes=[pltpu.VMEM((rows, depth), bf16)],
        compiler_params=params(),
        cost_estimate=cost(
            2 * rows * depth * (6 * units + w_out.shape[1]),
            2 * depth * (3 * units + w_out.shape[1]) + 22 * rows * depth,
            rows * units,
        ),
    )(level, *gathered, tokens, dout, w_out, gain, w_gate, w_up, w_down)


def hidden_grad(inner, total_ref, final_ref, hidden_ref, dout_ref, gain_ref):
    dnormed = jnp.where(inner, total_ref[...], final_ref[...])
    hidden = hidden_ref[...]
    rms = lax.rsqrt(jnp.mean(hidden * hidden, -1, keepdims=True) + norm_eps)
    scaled = dnormed * gain_ref[...]
    shift = jnp.mean(scaled * hidden, -1, keepdims=True)
    dhid = dout_ref[...].astype(jnp.float32) + (rms * scaled - hidden * (rms**3 * shift))
    return dhid, dnormed * (hidden * rms)


def backward_kernel(start, full, level_ref, total_ref, final_ref, hidden_ref, dout_ref, x_ref, *refs):
    gain_one_ref, gain_two_ref, wo_ref, q_ref = refs[:4]
    kv_here = q_ref.shape[1] // KV_WIDE
    refs = refs[4:]
    kv_refs, refs = refs[: 2 * kv_here], refs[2 * kv_here :]
    part_ref, other_ref, across_ref, outer_ref, place_ref, strip_ref = refs[:6]
    cos_ref, sin_ref = refs[6:8]
    dhid_ref, low_ref, dn_ref = refs[-3:]
    outs = refs[8:-3]
    if full:
        w_ref, outs = outs[0], outs[1:]
    count = (5 if start > 0 else 4) if full else 2
    acc_ref = outs[0] if len(outs) > count else None
    outs = outs[-count:]
    dhid_t_ref, dqkv_ref = outs[:2]
    if full:
        input_grad_ref, gains_ref = outs[2:4]
    rows = q_ref.shape[0]
    keys = kv_refs[0].shape[0]
    shard = pl.program_id(0)
    level = level_ref[0]
    inner = (level == 1) | (level == 2)

    @pl.when(shard == 0)
    def _():
        dhid, dgain = hidden_grad(
            inner, total_ref, final_ref, hidden_ref, dout_ref, gain_two_ref
        )
        dhid_ref[...] = dhid
        low = dhid.astype(jnp.bfloat16)
        low_ref[...] = low
        dhid_t_ref[...] = low.T
        if full:
            gains_ref[...] = jnp.zeros_like(gains_ref)
            gains_ref[1:2, :] = jnp.sum(dgain, 0, keepdims=True)
            dn_ref[...] = jnp.zeros_like(dn_ref)

    def rotate_back(grads):
        turned = grads * cos_ref[...] - pltpu.roll(grads, LANES // 2, 1) * sin_ref[...]
        return turned.astype(jnp.bfloat16)

    dmixed_all = dot32(low_ref[...], wo_ref[...]).astype(jnp.bfloat16)
    mixed = jnp.where(
        shard == 0,
        part_ref[...],
        jnp.where(shard == 1, other_ref[...], jnp.where(inner, across_ref[...], outer_ref[...])),
    )
    products = dmixed_all.astype(jnp.float32) * dot_split(mixed[:rows], place_ref[...])
    causal = lax.broadcasted_iota(jnp.int32, (rows, rows), 0) <= lax.broadcasted_iota(
        jnp.int32, (rows, rows), 1
    )
    grads = []
    for kv in range(kv_here):
        key_ref, value_ref = kv_refs[2 * kv : 2 * kv + 2]
        heads = range(kv * GROUP, (kv + 1) * GROUP)
        lanes = {h: slice(h * LANES, (h + 1) * LANES) for h in heads}
        row_dots = {h: jnp.sum(products[:, lanes[h]].T, axis=0, keepdims=True) for h in heads}
        log_sums = {h: mixed[rows + h : rows + h + 1, :rows] for h in heads}
        dqueries = dict.fromkeys(heads)
        here = slice(2 * kv * LANES, (2 * kv + 1) * LANES)
        there = slice((2 * kv + 1) * LANES, (2 * kv + 2) * LANES)
        for tile in range(keys // rows):
            span = slice(tile * rows, (tile + 1) * rows)
            key = key_ref[span, :]
            value = value_ref[span, :]
            key_t = key.T
            dkey = None if acc_ref is None else acc_ref[span, here]
            dvalue = None if acc_ref is None else acc_ref[span, there]
            last = tile * rows == start
            for h in heads:
                at = kv * KV_WIDE + (h % GROUP) * LANES
                query = q_ref[:, at : at + LANES]
                dmixed = dmixed_all[:, lanes[h]]
                raw = dot32_nt(key, query)
                probs = jnp.exp2(raw * score_scale_log2 - log_sums[h])
                if last:
                    probs = jnp.where(causal, probs, 0.0)
                dprobs = dot32_nt(value, dmixed)
                dscores = (probs * (dprobs - row_dots[h])).astype(jnp.bfloat16)
                dquery = dot32(key_t, dscores)
                dqueries[h] = dquery if dqueries[h] is None else dqueries[h] + dquery
                dkey_one = dot32(dscores, query)
                dvalue_one = dot32(probs.astype(jnp.bfloat16), dmixed)
                dkey = dkey_one if dkey is None else dkey + dkey_one
                dvalue = dvalue_one if dvalue is None else dvalue + dvalue_one
            if full and not last:
                outs[4][span, here] = dkey
                outs[4][span, there] = dvalue
        grads += [rotate_back(dqueries[h].T * score_scale) for h in heads]
        grads.append(rotate_back(dkey * score_scale))
        grads.append(dvalue.astype(jnp.bfloat16))
    grads = jnp.concatenate(grads, 1)
    if full:
        dn_ref[...] += dot32_nt(grads, w_ref[...])

    @pl.when(shard == 0)
    def _():
        wide = strip_ref.shape[1]
        for kv in range(kv_here):
            dqkv_ref[:, kv * wide : (kv + 1) * wide] = dot32(
                grads[:, kv * KV_WIDE : (kv + 1) * KV_WIDE], strip_ref[...]
            ).astype(jnp.bfloat16)

    if not full:
        return

    @pl.when(shard == pl.num_programs(0) - 1)
    def _():
        dnormed = dn_ref[...]
        inputs = x_ref[...].astype(jnp.float32)
        rms = lax.rsqrt(jnp.mean(inputs * inputs, -1, keepdims=True) + norm_eps)
        scaled = dnormed * gain_one_ref[...]
        shift = jnp.mean(scaled * inputs, -1, keepdims=True)
        grad = dhid_ref[...] + (rms * scaled - inputs * (rms**3 * shift))
        input_grad_ref[...] = grad.astype(jnp.bfloat16)
        gains_ref[0:1, :] = jnp.sum(dnormed * (inputs * rms), 0, keepdims=True)


def backward_chunk(
    level, sums_two, hidden, dout, tokens, gains, weights, qkv, gathered, places, tables, acc,
    index, rows, full=True
):
    start = index * rows
    keys = start + rows
    depth = tokens.shape[1]
    out_pad, qkv_pad = weights
    place_out, strip = places
    far_rows, width = gathered[0].shape
    out_wide = place_out.shape[1]
    kv_here = out_wide // (GROUP * LANES)
    wide = kv_here * KV_WIDE
    levels = qkv.shape[1] // wide
    own_rows = pl.BlockSpec((rows, depth), lambda t: (index, 0))
    table = pl.BlockSpec((rows, LANES), lambda t: (index, 0))
    gains = [gain[None, :] for gain in gains]
    key_value = lambda at: pl.BlockSpec(
        (keys, LANES), lambda t: (0, (wide // LANES) * t + at)
    )
    across = pl.BlockSpec((far_rows, width), lambda t: (0, jnp.where(t == 2, 1, 0)))
    outer = pl.BlockSpec((far_rows, width), lambda t: (0, jnp.where(t == 3, 1, 0)))
    in_specs = [
        SCALAR,
        whole(hidden),
        whole(hidden),
        whole(hidden),
        own_rows,
        own_rows,
        whole(gains[0]),
        whole(gains[1]),
        pl.BlockSpec((depth, out_wide), lambda t: (0, t)),
        pl.BlockSpec((rows, wide), lambda t: (index, t)),
    ]
    for kv in range(kv_here):
        at = kv * (KV_WIDE // LANES) + GROUP
        in_specs += [key_value(at), key_value(at + 1)]
    in_specs += [
        whole(gathered[0]),
        whole(gathered[1]),
        across,
        outer,
        whole(place_out),
        whole(strip),
        table,
        table,
    ]
    args = [level, *sums_two, hidden, dout, tokens, *gains, out_pad]
    args += [qkv] * (1 + 2 * kv_here)
    args += [*gathered, place_out, strip, *tables]
    sums_wide = 2 * kv_here * LANES
    if full:
        in_specs.append(pl.BlockSpec((depth, wide), lambda t: (0, t)))
        args.append(qkv_pad)
    if acc is not None:
        in_specs.append(pl.BlockSpec((keys, sums_wide), lambda t: (0, t)))
        args.append(acc)
    f32, bf16 = jnp.float32, jnp.bfloat16
    outs = [
        jax.ShapeDtypeStruct((depth, rows), bf16),
        jax.ShapeDtypeStruct((rows, kv_here * strip.shape[1]), bf16),
        jax.ShapeDtypeStruct((rows, depth), bf16),
        jax.ShapeDtypeStruct((8, depth), f32),
    ]
    outs = outs if full else outs[:2]
    out_specs = [whole(out) for out in outs]
    if full and start > 0:
        outs.append(jax.ShapeDtypeStruct((start, levels * sums_wide), f32))
        out_specs.append(pl.BlockSpec((start, sums_wide), lambda t: (0, t)))
    results = pl.pallas_call(
        functools.partial(backward_kernel, start, full),
        out_shape=outs,
        grid=(levels if full else 1,),
        in_specs=in_specs,
        out_specs=out_specs,
        scratch_shapes=[
            pltpu.VMEM((rows, depth), f32),
            pltpu.VMEM((rows, depth), bf16),
            pltpu.VMEM((rows, depth), f32),
        ],
        compiler_params=params(),
        cost_estimate=cost(
            levels * rows * (20 * kv_here * keys * LANES + 2 * depth * (out_wide + wide)),
            2 * depth * levels * (out_wide + wide) + 16 * rows * depth,
            levels * kv_here * GROUP * rows * keys,
        ),
    )(*args)
    return results[:4], (results[4] if full and start > 0 else None)


def rows_kernel(lefts, groups, adding, picked, together, side_ref, *refs):
    refs = list(refs)
    held_ref = refs.pop()
    out_refs = refs[-len(picked) :]
    refs = refs[: -len(picked)]
    recv_ref = refs.pop() if adding else None
    step = pl.program_id(0)
    left_refs = []
    for count in lefts:
        left_refs.append(refs[:count])
        refs = refs[count:]
    rights = []
    for _ in groups:
        rights.append(refs[:CHUNKS])
        refs = refs[CHUNKS:]
    rows = left_refs[0][0].shape[0]
    blocks = held_ref.shape[1] // rows

    @pl.when(step == 0)
    def _():
        for which, pieces in enumerate(left_refs):
            for n, ref in enumerate(pieces):
                m, j = n % blocks, n // blocks
                wide = ref.shape[1]
                held_ref[which, m * rows : (m + 1) * rows, j * wide : (j + 1) * wide] = ref[...]

    chunk = held_ref.shape[2] // CHUNKS
    whole_columns = slice(0, out_refs[0].shape[1])

    def give(group, left, columns):
        right = jnp.concatenate([ref[:chunk, :].astype(jnp.bfloat16) for ref in group], 0)
        total = dot32(held_ref[left], right)
        if recv_ref is not None:
            total = total + recv_ref[:, columns]
        for out_ref, parts in zip(out_refs, picked):
            at = 0
            for start, size in parts:
                out_ref[at : at + size, columns] = total[start : start + size]
                at += size

    begin = 0
    for group, (left, first, steps) in zip(rights, groups):
        if together:
            width = group[0].shape[1]
            give(group, left, slice(begin, begin + width))
            begin += width
        else:

            @pl.when((step >= first) & (step < first + steps))
            def _(group=group, left=left):
                give(group, left, whole_columns)


def rows_of(lefts, groups, side, rows, blocks, step, recv=None, picked=None):
    if picked is None:
        picked = [[(0, rows * blocks)]]
    at = lambda m: lambda i, side: ((m ^ side[2]) * side[1] + side[0], 0)
    specs = []
    args = []
    counts = []
    for left in lefts:
        pieces = left if isinstance(left, list) else [left]
        counts.append(len(pieces) * blocks)
        for piece in pieces:
            for m in range(blocks):
                specs.append(pl.BlockSpec((rows, piece.shape[1]), at(m)))
                args.append(piece)
    tokens = sum(piece.shape[1] for piece in pieces)
    first = 0
    plan = []
    together = step is None
    for which, rights in groups:
        if together:
            plan.append((which, 0, 1))
            specs += [whole(right) for right in rights]
            args += rights
            first += rights[0].shape[1]
            continue
        steps = rights[0].shape[1] // step
        plan.append((which, first, steps))
        for right in rights:
            pick = lambda i, side, first=first, steps=steps: (0, jnp.clip(i - first, 0, steps - 1))
            specs.append(pl.BlockSpec((right.shape[0], step), pick))
            args.append(right)
        first += steps
    if together:
        first, step = 1, first
    total = first * step
    block = lambda height: pl.BlockSpec((height, step), lambda i, side: (0, i))
    if recv is not None:
        specs.append(block(rows * blocks))
        args.append(recv)
    heights = [sum(size for _, size in parts) for parts in picked]
    results = pl.pallas_call(
        functools.partial(rows_kernel, counts, plan, recv is not None, picked, together),
        out_shape=[jax.ShapeDtypeStruct((height, total), jnp.float32) for height in heights],
        grid_spec=pltpu.PrefetchScalarGridSpec(
            num_scalar_prefetch=1,
            grid=(first,),
            in_specs=specs,
            out_specs=[block(height) for height in heights],
            scratch_shapes=[pltpu.VMEM((len(lefts), rows * blocks, tokens), jnp.bfloat16)],
        ),
        compiler_params=params(),
        cost_estimate=cost(
            2 * rows * blocks * tokens * total,
            4 * rows * blocks * total + 2 * tokens * (total + rows * blocks),
        ),
    )(side, *args)
    return results[0] if len(picked) == 1 else results


def shards(
    tokens,
    lengths,
    positions,
    cotangent,
    norm_gain,
    w_query,
    w_key,
    w_value,
    w_out,
    mlp_gain,
    w_gate,
    w_up,
    w_down,
):
    seq_rows, depth = tokens.shape
    chips = lax.axis_size("chip")
    dp = chips * 2
    tp = lax.axis_size("tp")
    chip = lax.axis_index("chip")
    core = lax.axis_index("core")
    level = lax.axis_index("tp")
    low = level < 2
    inner = (level == 1) | (level == 2)
    heads_here = w_query.shape[1] // HD
    kv_here = w_key.shape[1] // HD
    rows = seq_rows // CHUNKS
    slice_rows = depth // dp
    level_ref = level.astype(jnp.int32).reshape(1)
    by_hand = dp == 8
    swap = lambda array: lax.ppermute(array, "core", [(0, 1), (1, 0)])
    to_level = lambda array, s: along(array, [(t, t ^ s) for t in range(tp)])

    at_row = (chip * 2 + core) * slice_rows
    cols = lambda w: lax.dynamic_slice_in_dim(w, at_row, slice_rows, 1).astype(jnp.float32).T
    (out_slice,) = fence(cols(w_out))
    qkv_slice = jnp.concatenate(
        [
            lax.dynamic_slice_in_dim(w_query, at_row, slice_rows, 0).astype(jnp.float32),
            cols(w_key.T),
            cols(w_value.T),
        ],
        1,
    )
    out_slice, qkv_slice = fence(out_slice, qkv_slice)
    out_near = along(out_slice, PAIRS)
    qkv_near = along(qkv_slice, PAIRS)
    meta = jnp.stack([chip, core]).astype(jnp.int32)

    pq = place_query(heads_here)
    pkv = place_key_value(kv_here)
    p_all = place_all(heads_here, kv_here)
    strip_one = place_all(GROUP, 1).T
    p_out = place_plain(heads_here)
    strip_out = p_out.T

    half_dim = HD // 2
    freqs = rope_base ** (-(jnp.arange(half_dim).astype(jnp.float32) * 2.0 / HD))
    freqs = jnp.pad(freqs, (0, LANES // 2 - half_dim))
    angles = positions.astype(jnp.float32)[:, None] * jnp.concatenate([freqs, freqs])[None, :]
    cosines = jnp.cos(angles)
    sines = jnp.sin(angles) * jnp.where(jnp.arange(LANES) < LANES // 2, -1.0, 1.0)

    cosines, sines, out_near = fence(cosines, sines, out_near)
    out_across = along(jnp.stack([out_slice, out_near]), MIDDLE)
    qkv_own, normed_one, own_pad = start(
        tokens, norm_gain, w_query, w_key.T, w_value.T, pq, pkv, cosines, sines
    )

    def far_slices(near, across, outer):
        return jnp.stack(
            [
                near,
                jnp.where(inner, across[1], outer[0]),
                jnp.where(inner, across[0], outer[1]),
            ]
        )

    order = list(reversed(range(CHUNKS)))
    c0, c1, c2, c3 = order
    own, other, across, outer = {}, {}, {}, {}
    part, total, final = {}, {}, {}

    def hop_1(j):
        other[j] = along(own[j], PAIRS)

    def hop_2(j):
        across[j] = along(jnp.concatenate([own[j], other[j]], 1), MIDDLE)

    def hop_3(j):
        outer[j] = along(across[j], OUTWARD)

    coming = {}

    def add_1(j):
        coming[j] = along(part[j], INWARD)

    def add_2(j):
        total[j] = part[j][:rows] + coming[j][:rows]
        coming[j] = along(total[j], MIDDLE)

    def add_3(j, inward, extra=0):
        both = jnp.where(inner, total[j] + coming[j], inward)
        total[j] = jnp.pad(both, ((0, extra), (0, 0)))
        final[j] = along(total[j], PAIRS)
        return final[j][:rows]

    def to_chip(array, m):
        return lax.ppermute(array, "chip", [(i, i ^ m) for i in range(chips)])

    def over_chips_1(piece):
        cut = piece.shape[1] // 2
        one, two = piece[:, :cut], piece[:, cut:]
        return jnp.stack([one, to_chip(one, 1)]), jnp.stack([two, to_chip(two, 2)])

    def over_chips_2(one, two):
        return one, to_chip(one, 2), two, to_chip(two, 1)

    def over_chips_3(one, one_far, two, two_far):
        upper = jnp.stack([one[0], one[1], one_far[0], one_far[1]])
        lower = jnp.stack([two[0], two_far[0], two[1], two_far[1]])
        return jnp.concatenate([upper, lower], 2)

    qkv_own, out_across, qkv_near = fence(qkv_own, out_across, qkv_near)
    out_outer = along(out_across, OUTWARD)
    qkv_across = along(jnp.stack([qkv_slice, qkv_near]), MIDDLE)
    own[c0] = attend(lengths, qkv_own, strip_out, c0, rows)
    own, qkv_own, out_outer = fence(own, qkv_own, out_outer)
    hop_1(c0)
    out_far = far_slices(out_near, out_across, out_outer)
    out_mine = over_chips_1(out_far) if by_hand else out_far
    own[c1] = attend(lengths, qkv_own, strip_out, c1, rows)
    own[c1], qkv_own = fence(own[c1], qkv_own)
    hop_1(c1)
    own[c2] = attend(lengths, qkv_own, strip_out, c2, rows)
    own, other[c0], normed_one, w_out, out_mine, qkv_across, qkv_own = fence(
        own, other[c0], normed_one, w_out, out_mine, qkv_across, qkv_own
    )
    own[c3] = attend(lengths, qkv_own, strip_out, c3, rows)
    qkv_outer = along(qkv_across, OUTWARD)
    if by_hand:
        out_mine = over_chips_2(*out_mine)
    else:
        out_mine = lax.all_gather(out_mine, ("chip", "core"))
    hop_2(c0)
    dout, dout_t, normed_one_t = turn(lengths, cotangent, normed_one)
    w_out_t = w_out.T
    own, other, across, dout, dout_t, normed_one_t, w_out_t, out_mine, qkv_outer = fence(
        own, other, across, dout, dout_t, normed_one_t, w_out_t, out_mine, qkv_outer
    )
    hop_1(c2)
    hop_3(c0)
    hop_2(c1)
    qkv_far = lax.all_gather(far_slices(qkv_near, qkv_across, qkv_outer), ("chip", "core"))
    if by_hand:
        out_mine = over_chips_3(*out_mine)
        out_theirs = swap(out_mine)
        out_pad, out_plain = spread(
            spread_out_kernel,
            meta,
            w_out_t,
            [p_out],
            out_mine,
            out_theirs,
            [4 * p_out.shape[1], 4 * p_out.shape[0]],
        )
    else:
        plain = [w_out_t] + [
            out_mine[:, s].reshape(depth, -1).astype(jnp.bfloat16) for s in range(tp - 1)
        ]
        out_plain = jnp.concatenate(plain, 1)
        out_pad = jnp.concatenate([dot32(w, p_out).astype(jnp.bfloat16) for w in plain], 1)
    hidden, normed_t, activ, dgate, dup, mlp_part = {}, {}, {}, {}, {}, {}

    def feed(j):
        gathered = (own[j], other[j], across[j], outer[j])
        (hidden[j], normed_t[j], activ[j], dgate[j], dup[j], mlp_part[j], part[j]) = forward_chunk(
            level_ref, gathered, tokens, dout, out_plain, mlp_gain, w_gate, w_up, w_down, j, rows
        )

    own, other, across, outer, out_pad, out_plain = fence(
        own, other, across, outer, out_pad, out_plain
    )
    hop_1(c3)
    hop_3(c1)
    hop_2(c2)
    feed(c0)
    part, other = fence(part, other)
    add_1(c0)
    own, other, across, outer, part, hidden = fence(own, other, across, outer, part, hidden)
    hop_3(c2)
    hop_2(c3)
    feed(c1)
    own, other, across, outer, part, total, coming, hidden = fence(
        own, other, across, outer, part, total, coming, hidden
    )
    add_1(c1)
    hop_3(c3)
    add_2(c0)
    feed(c2)
    qkv_far, hidden[c2] = fence(qkv_far, hidden[c2])
    qkv_pad = spread_qkv(own_pad, pq, pkv, qkv_far)
    qkv = project(normed_one, qkv_pad, cosines, sines, qkv_own)
    own, other, across, outer, part, total, coming, hidden, qkv = fence(
        own, other, across, outer, part, total, coming, hidden, qkv
    )
    coming[c2] = add_3(c0, part[c2][:rows])
    add_2(c1)
    feed(c3)

    listed = lambda pieces: [pieces[j] for j in range(CHUNKS)]
    keep_side = jnp.stack([core, 2, 0]).astype(jnp.int32)
    keep_turned = jnp.stack([core, 2, chip]).astype(jnp.int32)
    send_side = jnp.stack([1 - core, 2, 0]).astype(jnp.int32)
    send_turned = jnp.stack([1 - core, 2, chip]).astype(jnp.int32)
    all_rows = jnp.array([0, 1, 0], jnp.int32)

    def send_rows(lefts, groups, step, side=send_side):
        if not by_hand:
            return rows_of(lefts, groups, all_rows, depth // 4, 4, step)
        return rows_of(lefts, groups, side, slice_rows, chips, step)

    def keep_rows(lefts, groups, received, step, side=keep_side, picked=None):
        if not by_hand:
            return received
        return rows_of(lefts, groups, side, slice_rows, chips, step, received, picked)

    def swap_rows(array):
        return swap(array) if by_hand else array

    def scatter(array, axes):
        return lax.psum_scatter(array, axes, scatter_dimension=0, tiled=True)

    units = w_gate.shape[1]
    mlp_args = (
        [listed(normed_t), dout_t],
        [(0, listed(dgate)), (0, listed(dup)), (1, listed(activ))],
    )
    acc = None
    dhid_t, dqkv_own, input_grad, gains = {}, {}, {}, {}

    def back(j):
        nonlocal acc
        (dhid_t[j], dqkv_own[j], input_grad[j], gains[j]), acc = back_some(j, True)

    def back_own(j):
        return back_some(j, False)[0]

    def back_some(j, full):
        return backward_chunk(
            level_ref,
            (total[j], final[j]),
            hidden[j],
            dout,
            tokens,
            (norm_gain, mlp_gain),
            (out_pad, qkv_pad),
            qkv,
            (own[j], other[j], across[j], outer[j]),
            (p_out, strip_one),
            (cosines, sines),
            acc,
            j,
            rows,
            full,
        )

    grad_mlp = rows_of(*mlp_args, all_rows, depth // 4, 4, units // 2)
    own, other, across, outer, part, total, coming, final, hidden, grad_mlp = fence(
        own, other, across, outer, part, total, coming, final, hidden, grad_mlp
    )
    grad_mlp = scatter(grad_mlp, ("chip", "core"))
    coming[c3] = add_3(c1, part[c3][:rows])
    add_2(c2)
    back(c0)

    near = lambda: jnp.where(low, mlp_part[1], mlp_part[2])
    edge = lambda: jnp.where(low, mlp_part[0], mlp_part[3])
    leave_far = lambda: jnp.where(low, mlp_part[3], mlp_part[0])
    leave_near = lambda: jnp.where(low, mlp_part[2], mlp_part[1])
    total, coming, final, hidden, mlp_part, acc, dhid_t = fence(
        total, coming, final, hidden, mlp_part, acc, dhid_t
    )
    far_sum = add_3(c2, leave_far())
    add_2(c3)
    back(c1)
    total, coming, final, hidden, mlp_part, far_sum, acc, dhid_t = fence(
        total, coming, final, hidden, mlp_part, far_sum, acc, dhid_t
    )
    near_sum = add_3(c3, leave_near(), EXTRA)
    far_in = along(leave_far() + far_sum, MIDDLE)
    back(c2)
    total, final, hidden, mlp_part, near_sum, far_in, acc, dhid_t = fence(
        total, final, hidden, mlp_part, near_sum, far_in, acc, dhid_t
    )
    last = along(jnp.where(inner, edge() + far_in, near()), PAIRS)
    near_in = along(leave_near() + near_sum, MIDDLE)
    dhid_t[c3], dqkv_own[c3] = back_own(c3)
    q_cols = heads_here * HD
    attn_args = (
        [listed(dhid_t), normed_one_t],
        [(0, listed(own)), (1, listed(dqkv_own))],
    )
    sent = swap_rows(send_rows(*attn_args, None, send_turned))
    total, final, hidden, acc, sent = fence(total, final, hidden, acc, sent)
    if by_hand:
        half = slice_rows // 2
        upper = lambda m: (m * slice_rows, half)
        lower = lambda m: (m * slice_rows + half, half)
        picked = [
            [upper(1), upper(3)],
            [upper(0), upper(2)],
            [lower(2), lower(3)],
            [lower(0), lower(1)],
        ]
        pieces = keep_rows(*attn_args, sent, None, keep_turned, picked)
        pieces, hidden = fence(pieces, hidden)
        one_away, one, two_away, two = pieces
        pieces = (one, to_chip(one_away, 1), two, to_chip(two_away, 2))
    else:
        pieces = scatter(sent, ("chip", "core"))
    back(c3)
    pieces, gains, input_grad, last, near_in = fence(pieces, gains, input_grad, last, near_in)
    gain_sums = gains[0] + gains[1] + gains[2] + gains[3]
    gain_sums = gain_sums + swap(gain_sums)
    if by_hand:
        others = [to_chip(gain_sums, m) for m in range(1, chips)]
        gain_sums = sum(others, gain_sums)
        one = pieces[0] + pieces[1]
        two = pieces[2] + pieces[3]
        one = one[:half] + to_chip(one[half:], 2)
        two = two[:half] + to_chip(two[half:], 1)
        attn = jnp.concatenate([one, two], 0)
    else:
        gain_sums = lax.psum(gain_sums, "chip")
        attn = pieces
    gain_rows = lax.dynamic_slice_in_dim(gain_sums, at_row, slice_rows, 1)
    grad_out, grad_qkv = attn[:, :q_cols], attn[:, q_cols:]
    mlp_rows = jnp.where(inner, near() + near_in, edge()) + last
    hidden_rows = jnp.where(
        low,
        jnp.where(level == 0, hidden[0], hidden[1]),
        jnp.where(level == 2, hidden[2], hidden[3]),
    )
    layer_out = (hidden_rows + mlp_rows).astype(jnp.bfloat16)
    one = strip_one.shape[1]
    picked = lambda at, width: jnp.concatenate(
        [grad_qkv[:, kv * one + at : kv * one + at + width] for kv in range(kv_here)], 1
    )
    return (
        layer_out,
        jnp.concatenate(listed(input_grad), 0),
        gain_rows[0],
        picked(0, GROUP * HD),
        picked(GROUP * HD, HD),
        picked((GROUP + 1) * HD, HD),
        grad_out.T,
        gain_rows[1],
        grad_mlp[:, :units],
        grad_mlp[:, units : 2 * units],
        grad_mlp[:, 2 * units :].T,
    )


def solution(mesh):
    devices = mesh.devices
    dp, tp = devices.shape
    split = Mesh(devices.reshape(dp // 2, 2, tp), ("chip", "core", "tp"))
    data = ("chip", "core")
    return jax.shard_map(
        shards,
        mesh=split,
        in_specs=(
            P(data, None),
            P(data),
            P(data),
            P(data, None),
            P(),
            P(None, "tp"),
            P(None, "tp"),
            P(None, "tp"),
            P("tp", None),
            P(),
            P(None, "tp"),
            P(None, "tp"),
            P("tp", None),
        ),
        out_specs=(
            P(("chip", "core", "tp"), None),
            P(data, None),
            P(data),
            P(data, "tp"),
            P(data, "tp"),
            P(data, "tp"),
            P("tp", data),
            P(data),
            P(data, "tp"),
            P(data, "tp"),
            P("tp", data),
        ),
        check_vma=False,
    )
```

```python
import functools

import jax
import jax.numpy as jnp
from jax import lax
from jax.experimental import pallas as pl
from jax.experimental.pallas import tpu as pltpu
from jax.sharding import Mesh
from jax.sharding import PartitionSpec as P

HD = 96
LANES = 128
GROUP = 2
KV_WIDE = (GROUP + 2) * LANES
rope_base = 100000.0
norm_eps = 1e-05
masked_score = -1e30
far_away = 1e30
score_scale = HD ** (-0.5)
score_scale_log2 = score_scale * 1.4426950408889634
CHUNKS = 4
EXTRA = 8
VMEM_BYTES = 56 * 1024 * 1024
NT = (((1,), (1,)), ((), ()))


def params():
    return pltpu.CompilerParams(vmem_limit_bytes=VMEM_BYTES)


def cost(flops, moved, exps=0):
    return pl.CostEstimate(
        flops=flops // 1024, bytes_accessed=moved // 1024, transcendentals=exps // 1024
    )


def dot32(a, b):
    return jnp.dot(a, b, preferred_element_type=jnp.float32)


def dot32_nt(a, b):
    return lax.dot_general(a, b, NT, preferred_element_type=jnp.float32)


def dot_split(a, places):
    high = a.astype(jnp.bfloat16)
    rest = (a - high.astype(jnp.float32)).astype(jnp.bfloat16)
    return dot32(high, places) + dot32(rest, places)


def fence(*trees):
    return lax.optimization_barrier(trees)


def whole(array, buffers=None):
    zeros = (0,) * len(array.shape)
    return pl.BlockSpec(array.shape, lambda *_: zeros)


SCALAR = pl.BlockSpec(memory_space=pltpu.SMEM)


def halves(entry):
    half_dim = HD // 2
    return (entry // half_dim) * (LANES // 2) + entry % half_dim


def placement(lanes, width):
    return (lanes[:, None] == jnp.arange(width)[None, :]).astype(jnp.bfloat16)


def place_query(heads):
    source = jnp.arange(heads * HD)
    return placement((source // HD) * LANES + halves(source % HD), heads * LANES)


def place_key_value(kv_heads):
    source = jnp.arange(kv_heads * HD)
    head = source // HD
    keys = head * 2 * LANES + halves(source % HD)
    values = head * 2 * LANES + LANES + source % HD
    return placement(jnp.concatenate([keys, values]), kv_heads * 2 * LANES)


def place_all(heads, kv_heads):
    source = jnp.arange(heads * HD)
    head = source // HD
    query = (head // GROUP) * KV_WIDE + (head % GROUP) * LANES + halves(source % HD)
    source = jnp.arange(kv_heads * HD)
    base = (source // HD) * KV_WIDE + GROUP * LANES
    keys = base + halves(source % HD)
    values = base + LANES + source % HD
    return placement(jnp.concatenate([query, keys, values]), kv_heads * KV_WIDE)


def place_plain(heads):
    source = jnp.arange(heads * HD)
    return placement((source // HD) * LANES + source % HD, heads * LANES)


PAIRS = [(0, 1), (1, 0), (2, 3), (3, 2)]
INWARD = [(0, 1), (3, 2)]
MIDDLE = [(1, 2), (2, 1)]
OUTWARD = [(1, 0), (2, 3)]


def along(part, pairs):
    return lax.ppermute(part, "tp", pairs)


def store_qkv(out_ref, here, base, query, key_value):
    wide = GROUP * LANES
    for kv in range(key_value.shape[1] // (2 * LANES)):
        at = base + kv * KV_WIDE
        there = slice(kv * 2 * LANES, (kv + 1) * 2 * LANES)
        out_ref[here, at : at + wide] = query[:, kv * wide : (kv + 1) * wide]
        out_ref[here, at + wide : at + KV_WIDE] = key_value[:, there]


def store_turned(out_ref, at, lin, cos_ref, sin_ref):
    for h in range(GROUP + 2):
        one = lin[:, h * LANES : (h + 1) * LANES]
        if h < GROUP + 1:
            one = one * cos_ref[...] + pltpu.roll(one, LANES // 2, 1) * sin_ref[...]
        out_ref[:, at + h * LANES : at + (h + 1) * LANES] = one.astype(jnp.bfloat16)


def spread_out_kernel(meta_ref, own_ref, p_ref, mine_ref, theirs_ref, pad_ref, plain_ref):
    rows, width = mine_ref.shape[2:]
    wide = p_ref.shape[1]
    for side, ref in enumerate((mine_ref, theirs_ref)):
        here = pl.ds(pl.multiple_of((meta_ref[1] ^ side) * rows, rows), rows)
        for s in range(4):
            block = own_ref[here, :] if s == 0 else ref[0, s - 1].astype(jnp.bfloat16)
            plain_ref[here, s * width : (s + 1) * width] = block
            pad_ref[here, s * wide : (s + 1) * wide] = dot32(block, p_ref[...]).astype(
                jnp.bfloat16
            )


def spread_qkv_kernel(pq_ref, pkv_ref, far_ref, _, out_ref):
    parts, _, rows, width = far_ref.shape
    split = pq_ref.shape[0]
    block = far_ref[:, 0].reshape(parts * rows, width).astype(jnp.bfloat16)
    query = dot32(block[:, :split], pq_ref[...]).astype(jnp.bfloat16)
    key_value = dot32(block[:, split:], pkv_ref[...]).astype(jnp.bfloat16)
    store_qkv(out_ref, slice(None), 0, query, key_value)


def spread_qkv(padded, pq, pkv, far):
    total = padded.shape[0]
    dp, others, rows, width = far.shape
    wide = padded.shape[1] // (others + 1)
    parts = max(1, dp // 2)
    block = parts * rows
    return pl.pallas_call(
        spread_qkv_kernel,
        out_shape=jax.ShapeDtypeStruct(padded.shape, jnp.bfloat16),
        grid=(total // block, others),
        in_specs=[
            whole(pq),
            whole(pkv),
            pl.BlockSpec((parts, 1, rows, width), lambda i, s: (i, s, 0, 0)),
            pl.BlockSpec(memory_space=pl.ANY),
        ],
        out_specs=pl.BlockSpec((block, wide), lambda i, s: (i, s + 1)),
        input_output_aliases={3: 0},
        compiler_params=params(),
        cost_estimate=cost(8 * total * width * 512, 20 * total * wide),
    )(pq, pkv, far, padded)


def spread(kernel, meta, own, places, mine, theirs, widths):
    chips, others, rows, width = mine.shape
    total = own.shape[0]
    row_block = lambda m, meta: (meta[0] ^ m, 0)
    piece = pl.BlockSpec((1, others, rows, width), lambda m, meta: (m, 0, 0, 0))
    return pl.pallas_call(
        kernel,
        out_shape=[jax.ShapeDtypeStruct((total, wide), jnp.bfloat16) for wide in widths],
        grid_spec=pltpu.PrefetchScalarGridSpec(
            num_scalar_prefetch=1,
            grid=(chips,),
            in_specs=[pl.BlockSpec((2 * rows, own.shape[1]), row_block)]
            + [whole(place) for place in places]
            + [piece, piece],
            out_specs=[pl.BlockSpec((2 * rows, wide), row_block) for wide in widths],
        ),
        compiler_params=params(),
        cost_estimate=cost(
            8 * total * width * 512, total * (12 * width + 2 * sum(widths))
        ),
    )(meta, own, *places, mine, theirs)


def start_kernel(x_ref, gain_ref, q_ref, k_ref, v_ref, pq_ref, pkv_ref, cos_ref, sin_ref, *outs):
    qkv_ref, normed_ref, pad_ref = outs

    @pl.when(pl.program_id(0) == 0)
    def _():
        split = k_ref.shape[0]
        query = dot32(q_ref[...], pq_ref[...]).astype(jnp.bfloat16)
        key_value = dot32(k_ref[...].T, pkv_ref[:split, :])
        key_value = key_value + dot32(v_ref[...].T, pkv_ref[split:, :])
        store_qkv(pad_ref, slice(None), 0, query, key_value.astype(jnp.bfloat16))

    inputs = x_ref[...].astype(jnp.float32)
    rms = lax.rsqrt(jnp.mean(inputs * inputs, -1, keepdims=True) + norm_eps)
    normed = (inputs * rms * gain_ref[...]).astype(jnp.bfloat16)
    normed_ref[...] = normed
    for kv in range(pad_ref.shape[1] // KV_WIDE):
        at = kv * KV_WIDE
        store_turned(qkv_ref, at, dot32(normed, pad_ref[:, at : at + KV_WIDE]), cos_ref, sin_ref)


def start(tokens, gain, w_query, w_key_t, w_value_t, pq, pkv, cosines, sines):
    total, depth = tokens.shape
    rows = total // CHUNKS
    wide = pq.shape[1] + pkv.shape[1]
    gain = gain[None, :]
    by_rows = lambda width: pl.BlockSpec((rows, width), lambda i: (i, 0))
    arrays = [w_query, w_key_t, w_value_t, pq, pkv]
    shapes = [
        jax.ShapeDtypeStruct((total, 4 * wide), jnp.bfloat16),
        jax.ShapeDtypeStruct((total, depth), jnp.bfloat16),
        jax.ShapeDtypeStruct((depth, 4 * wide), jnp.bfloat16),
    ]
    return pl.pallas_call(
        start_kernel,
        out_shape=shapes,
        grid=(CHUNKS,),
        in_specs=[by_rows(depth), whole(gain)]
        + [whole(array) for array in arrays]
        + [by_rows(LANES), by_rows(LANES)],
        out_specs=[
            by_rows(wide),
            by_rows(depth),
            pl.BlockSpec((depth, wide), lambda i: (0, 0)),
        ],
        compiler_params=params(),
        cost_estimate=cost(2 * total * depth * wide, 12 * total * depth),
    )(tokens, gain, *arrays, cosines, sines)


def turn_kernel(length_ref, cot_ref, normed_ref, dout_ref, dout_t_ref, normed_t_ref):
    rows = cot_ref.shape[0]
    at = pl.program_id(0) * rows + lax.broadcasted_iota(jnp.int32, cot_ref.shape, 0)
    dout = jnp.where(at < length_ref[0], cot_ref[...].astype(jnp.float32), 0.0)
    dout = dout.astype(jnp.bfloat16)
    dout_ref[...] = dout
    dout_t_ref[...] = dout.T
    normed_t_ref[...] = normed_ref[...].T


def turn(length, cotangent, normed):
    total, depth = cotangent.shape
    rows = total // CHUNKS
    by_rows = pl.BlockSpec((rows, depth), lambda i: (i, 0))
    by_columns = pl.BlockSpec((depth, rows), lambda i: (0, i))
    turned = jax.ShapeDtypeStruct((depth, total), jnp.bfloat16)
    return pl.pallas_call(
        turn_kernel,
        out_shape=[jax.ShapeDtypeStruct((total, depth), jnp.bfloat16), turned, turned],
        grid=(CHUNKS,),
        in_specs=[SCALAR, by_rows, by_rows],
        out_specs=[by_rows, by_columns, by_columns],
        compiler_params=params(),
        cost_estimate=cost(total * depth, 10 * total * depth),
    )(length, cotangent, normed)


def project_kernel(x_ref, w_ref, cos_ref, sin_ref, _, out_ref):
    store_turned(out_ref, 0, dot32(x_ref[...], w_ref[...]), cos_ref, sin_ref)


def project(normed, weights, cosines, sines, qkv):
    rows, depth = normed.shape
    width = weights.shape[1]
    steps = width // KV_WIDE
    first = steps // 4
    return pl.pallas_call(
        project_kernel,
        out_shape=jax.ShapeDtypeStruct((rows, width), jnp.bfloat16),
        grid=(steps - first,),
        in_specs=[
            whole(normed),
            pl.BlockSpec((depth, KV_WIDE), lambda i: (0, i + first)),
            whole(cosines),
            whole(sines),
            pl.BlockSpec(memory_space=pl.ANY),
        ],
        out_specs=pl.BlockSpec((rows, KV_WIDE), lambda i: (0, i + first)),
        input_output_aliases={4: 0},
        compiler_params=params(),
        cost_estimate=cost(
            2 * rows * depth * width, 2 * (rows * depth + depth * width + rows * width)
        ),
    )(normed, weights, cosines, sines, qkv)


def attend_kernel(start, length_ref, q_ref, kv_ref, strip_ref, out_ref):
    rows = q_ref.shape[0]
    keys = kv_ref.shape[0]
    length = length_ref[0]
    row_ids = start + lax.broadcasted_iota(jnp.int32, (1, rows), 1)
    limit = jnp.minimum(row_ids, length - 1)
    allowed = lax.broadcasted_iota(jnp.int32, (keys, rows), 0) <= limit
    mixed = []
    sums = []
    for kv in range(kv_ref.shape[1] // KV_WIDE):
        base = kv * KV_WIDE
        at = base + GROUP * LANES
        key = kv_ref[:, at : at + LANES]
        value_t = kv_ref[:, at + LANES : at + 2 * LANES].T
        for g in range(GROUP):
            query = q_ref[:, base + g * LANES : base + (g + 1) * LANES]
            raw = jnp.where(allowed, dot32_nt(key, query), masked_score)
            peak = jnp.max(raw, axis=0, keepdims=True)
            expo = jnp.exp2((raw - peak) * score_scale_log2)
            total = jnp.sum(expo, axis=0, keepdims=True)
            probs = (expo * (1.0 / total)).astype(jnp.bfloat16)
            mixed.append(dot32(value_t, probs).T)
            log_sum = peak * score_scale_log2 + jnp.log2(total)
            sums.append(jnp.where(row_ids < length, log_sum, far_away))
    out_ref[:rows, :] = dot_split(jnp.concatenate(mixed, 1), strip_ref[...])
    out_ref[rows:, :] = jnp.zeros((EXTRA, out_ref.shape[1]), jnp.float32)
    out_ref[rows : rows + len(sums), :rows] = jnp.concatenate(sums, 0)


def attend(length, qkv, strip, index, rows):
    keys = (index + 1) * rows
    width = qkv.shape[1] // 4
    heads = width // KV_WIDE * GROUP
    shape = (rows + EXTRA, strip.shape[1])
    return pl.pallas_call(
        functools.partial(attend_kernel, index * rows),
        out_shape=jax.ShapeDtypeStruct(shape, jnp.float32),
        grid=(1,),
        in_specs=[
            SCALAR,
            pl.BlockSpec((rows, width), lambda i: (index, 0)),
            pl.BlockSpec((keys, width), lambda i: (0, 0)),
            whole(strip),
        ],
        out_specs=pl.BlockSpec(shape, lambda i: (0, 0)),
        compiler_params=params(),
        cost_estimate=cost(
            4 * heads * rows * keys * LANES, 2 * (rows + keys) * width, heads * rows * keys
        ),
    )(length, qkv, qkv, strip)


def forward_kernel(level_ref, part_ref, other_ref, across_ref, outer_ref, *refs):
    x_ref, dout_ref, wo_ref, gain_ref, wg_ref, wu_ref, wd_ref = refs[:7]
    hidden_ref, normed_t_ref, activ_ref, dgate_ref, dup_ref, mlp_ref, dn_ref = refs[7:14]
    normed_ref = refs[14]
    rows = x_ref.shape[0]

    @pl.when(pl.program_id(0) == 0)
    def _():
        level = level_ref[0]
        inner = (level == 1) | (level == 2)
        width = part_ref.shape[1]
        second = jnp.where(inner, across_ref[:rows, width:], outer_ref[:rows, :width])
        third = jnp.where(inner, across_ref[:rows, :width], outer_ref[:rows, width:])
        mixed = jnp.concatenate([part_ref[:rows, :], other_ref[:rows, :], second, third], 1)
        hidden = x_ref[...].astype(jnp.float32) + dot32_nt(mixed.astype(jnp.bfloat16), wo_ref[...])
        hidden_ref[...] = hidden
        rms = lax.rsqrt(jnp.mean(hidden * hidden, -1, keepdims=True) + norm_eps)
        normed = (hidden * rms * gain_ref[...]).astype(jnp.bfloat16)
        normed_ref[...] = normed
        normed_t_ref[...] = normed.T
        mlp_ref[...] = jnp.zeros_like(mlp_ref)
        dn_ref[...] = jnp.zeros_like(dn_ref)

    normed = normed_ref[...]
    gate = dot32(normed, wg_ref[...])
    up = dot32(normed, wu_ref[...])
    dact = dot32_nt(dout_ref[...], wd_ref[...])
    sigmoid = jax.nn.sigmoid(gate)
    silu = gate * sigmoid
    activ = (silu * up).astype(jnp.bfloat16)
    dgate = (dact * up * sigmoid * (1.0 + gate * (1.0 - sigmoid))).astype(jnp.bfloat16)
    dup = (dact * silu).astype(jnp.bfloat16)
    activ_ref[...] = activ
    dgate_ref[...] = dgate
    dup_ref[...] = dup
    mlp_ref[...] += dot32(activ, wd_ref[...])
    dn_ref[:rows, :] += dot32_nt(dgate, wg_ref[...]) + dot32_nt(dup, wu_ref[...])


def forward_chunk(level, gathered, tokens, dout, w_out, gain, w_gate, w_up, w_down, index, rows):
    depth = tokens.shape[1]
    units = w_gate.shape[1]
    block = 512
    own_rows = pl.BlockSpec((rows, depth), lambda i: (index, 0))
    by_units = pl.BlockSpec((depth, block), lambda i: (0, i))
    gain = gain[None, :]
    f32, bf16 = jnp.float32, jnp.bfloat16
    outs = [
        jax.ShapeDtypeStruct((rows, depth), f32),
        jax.ShapeDtypeStruct((depth, rows), bf16),
        jax.ShapeDtypeStruct((rows, units), bf16),
        jax.ShapeDtypeStruct((rows, units), bf16),
        jax.ShapeDtypeStruct((rows, units), bf16),
        jax.ShapeDtypeStruct((rows, depth), f32),
        jax.ShapeDtypeStruct((rows + EXTRA, depth), f32),
    ]
    unit_out = pl.BlockSpec((rows, block), lambda i: (0, i))
    return pl.pallas_call(
        forward_kernel,
        out_shape=outs,
        grid=(units // block,),
        in_specs=[SCALAR]
        + [whole(array) for array in gathered]
        + [own_rows, own_rows, whole(w_out), whole(gain), by_units, by_units]
        + [pl.BlockSpec((block, depth), lambda i: (i, 0))],
        out_specs=[
            whole(outs[0]),
            whole(outs[1]),
            unit_out,
            unit_out,
            unit_out,
            whole(outs[5]),
            whole(outs[6]),
        ],
        scratch_shapes=[pltpu.VMEM((rows, depth), bf16)],
        compiler_params=params(),
        cost_estimate=cost(
            2 * rows * depth * (6 * units + w_out.shape[1]),
            2 * depth * (3 * units + w_out.shape[1]) + 22 * rows * depth,
            rows * units,
        ),
    )(level, *gathered, tokens, dout, w_out, gain, w_gate, w_up, w_down)


def hidden_grad(inner, total_ref, final_ref, hidden_ref, dout_ref, gain_ref):
    dnormed = jnp.where(inner, total_ref[...], final_ref[...])
    hidden = hidden_ref[...]
    rms = lax.rsqrt(jnp.mean(hidden * hidden, -1, keepdims=True) + norm_eps)
    scaled = dnormed * gain_ref[...]
    shift = jnp.mean(scaled * hidden, -1, keepdims=True)
    dhid = dout_ref[...].astype(jnp.float32) + (rms * scaled - hidden * (rms**3 * shift))
    return dhid, dnormed * (hidden * rms)


def backward_kernel(start, full, level_ref, total_ref, final_ref, hidden_ref, dout_ref, x_ref, *refs):
    gain_one_ref, gain_two_ref, wo_ref, q_ref = refs[:4]
    kv_here = q_ref.shape[1] // KV_WIDE
    refs = refs[4:]
    kv_refs, refs = refs[: 2 * kv_here], refs[2 * kv_here :]
    part_ref, other_ref, across_ref, outer_ref, place_ref, strip_ref = refs[:6]
    cos_ref, sin_ref = refs[6:8]
    dhid_ref, low_ref, dn_ref = refs[-3:]
    outs = refs[8:-3]
    if full:
        w_ref, outs = outs[0], outs[1:]
    count = (5 if start > 0 else 4) if full else 2
    acc_ref = outs[0] if len(outs) > count else None
    outs = outs[-count:]
    dhid_t_ref, dqkv_ref = outs[:2]
    if full:
        input_grad_ref, gains_ref = outs[2:4]
    rows = q_ref.shape[0]
    keys = kv_refs[0].shape[0]
    shard = pl.program_id(0)
    level = level_ref[0]
    inner = (level == 1) | (level == 2)

    @pl.when(shard == 0)
    def _():
        dhid, dgain = hidden_grad(
            inner, total_ref, final_ref, hidden_ref, dout_ref, gain_two_ref
        )
        dhid_ref[...] = dhid
        low = dhid.astype(jnp.bfloat16)
        low_ref[...] = low
        dhid_t_ref[...] = low.T
        if full:
            gains_ref[...] = jnp.zeros_like(gains_ref)
            gains_ref[1:2, :] = jnp.sum(dgain, 0, keepdims=True)
            dn_ref[...] = jnp.zeros_like(dn_ref)

    def rotate_back(grads):
        turned = grads * cos_ref[...] - pltpu.roll(grads, LANES // 2, 1) * sin_ref[...]
        return turned.astype(jnp.bfloat16)

    dmixed_all = dot32(low_ref[...], wo_ref[...]).astype(jnp.bfloat16)
    mixed = jnp.where(
        shard == 0,
        part_ref[...],
        jnp.where(shard == 1, other_ref[...], jnp.where(inner, across_ref[...], outer_ref[...])),
    )
    products = dmixed_all.astype(jnp.float32) * dot_split(mixed[:rows], place_ref[...])
    causal = lax.broadcasted_iota(jnp.int32, (rows, rows), 0) <= lax.broadcasted_iota(
        jnp.int32, (rows, rows), 1
    )
    grads = []
    for kv in range(kv_here):
        key_ref, value_ref = kv_refs[2 * kv : 2 * kv + 2]
        heads = range(kv * GROUP, (kv + 1) * GROUP)
        lanes = {h: slice(h * LANES, (h + 1) * LANES) for h in heads}
        row_dots = {h: jnp.sum(products[:, lanes[h]].T, axis=0, keepdims=True) for h in heads}
        log_sums = {h: mixed[rows + h : rows + h + 1, :rows] for h in heads}
        dqueries = dict.fromkeys(heads)
        here = slice(2 * kv * LANES, (2 * kv + 1) * LANES)
        there = slice((2 * kv + 1) * LANES, (2 * kv + 2) * LANES)
        for tile in range(keys // rows):
            span = slice(tile * rows, (tile + 1) * rows)
            key = key_ref[span, :]
            value = value_ref[span, :]
            key_t = key.T
            dkey = None if acc_ref is None else acc_ref[span, here]
            dvalue = None if acc_ref is None else acc_ref[span, there]
            last = tile * rows == start
            for h in heads:
                at = kv * KV_WIDE + (h % GROUP) * LANES
                query = q_ref[:, at : at + LANES]
                dmixed = dmixed_all[:, lanes[h]]
                raw = dot32_nt(key, query)
                probs = jnp.exp2(raw * score_scale_log2 - log_sums[h])
                if last:
                    probs = jnp.where(causal, probs, 0.0)
                dprobs = dot32_nt(value, dmixed)
                dscores = (probs * (dprobs - row_dots[h])).astype(jnp.bfloat16)
                dquery = dot32(key_t, dscores)
                dqueries[h] = dquery if dqueries[h] is None else dqueries[h] + dquery
                dkey_one = dot32(dscores, query)
                dvalue_one = dot32(probs.astype(jnp.bfloat16), dmixed)
                dkey = dkey_one if dkey is None else dkey + dkey_one
                dvalue = dvalue_one if dvalue is None else dvalue + dvalue_one
            if full and not last:
                outs[4][span, here] = dkey
                outs[4][span, there] = dvalue
        grads += [rotate_back(dqueries[h].T * score_scale) for h in heads]
        grads.append(rotate_back(dkey * score_scale))
        grads.append(dvalue.astype(jnp.bfloat16))
    grads = jnp.concatenate(grads, 1)
    if full:
        dn_ref[...] += dot32_nt(grads, w_ref[...])

    @pl.when(shard == 0)
    def _():
        wide = strip_ref.shape[1]
        for kv in range(kv_here):
            dqkv_ref[:, kv * wide : (kv + 1) * wide] = dot32(
                grads[:, kv * KV_WIDE : (kv + 1) * KV_WIDE], strip_ref[...]
            ).astype(jnp.bfloat16)

    if not full:
        return

    @pl.when(shard == pl.num_programs(0) - 1)
    def _():
        dnormed = dn_ref[...]
        inputs = x_ref[...].astype(jnp.float32)
        rms = lax.rsqrt(jnp.mean(inputs * inputs, -1, keepdims=True) + norm_eps)
        scaled = dnormed * gain_one_ref[...]
        shift = jnp.mean(scaled * inputs, -1, keepdims=True)
        grad = dhid_ref[...] + (rms * scaled - inputs * (rms**3 * shift))
        input_grad_ref[...] = grad.astype(jnp.bfloat16)
        gains_ref[0:1, :] = jnp.sum(dnormed * (inputs * rms), 0, keepdims=True)


def backward_chunk(
    level, sums_two, hidden, dout, tokens, gains, weights, qkv, gathered, places, tables, acc,
    index, rows, full=True
):
    start = index * rows
    keys = start + rows
    depth = tokens.shape[1]
    out_pad, qkv_pad = weights
    place_out, strip = places
    far_rows, width = gathered[0].shape
    out_wide = place_out.shape[1]
    kv_here = out_wide // (GROUP * LANES)
    wide = kv_here * KV_WIDE
    levels = qkv.shape[1] // wide
    own_rows = pl.BlockSpec((rows, depth), lambda t: (index, 0))
    table = pl.BlockSpec((rows, LANES), lambda t: (index, 0))
    gains = [gain[None, :] for gain in gains]
    key_value = lambda at: pl.BlockSpec(
        (keys, LANES), lambda t: (0, (wide // LANES) * t + at)
    )
    across = pl.BlockSpec((far_rows, width), lambda t: (0, jnp.where(t == 2, 1, 0)))
    outer = pl.BlockSpec((far_rows, width), lambda t: (0, jnp.where(t == 3, 1, 0)))
    in_specs = [
        SCALAR,
        whole(hidden),
        whole(hidden),
        whole(hidden),
        own_rows,
        own_rows,
        whole(gains[0]),
        whole(gains[1]),
        pl.BlockSpec((depth, out_wide), lambda t: (0, t)),
        pl.BlockSpec((rows, wide), lambda t: (index, t)),
    ]
    for kv in range(kv_here):
        at = kv * (KV_WIDE // LANES) + GROUP
        in_specs += [key_value(at), key_value(at + 1)]
    in_specs += [
        whole(gathered[0]),
        whole(gathered[1]),
        across,
        outer,
        whole(place_out),
        whole(strip),
        table,
        table,
    ]
    args = [level, *sums_two, hidden, dout, tokens, *gains, out_pad]
    args += [qkv] * (1 + 2 * kv_here)
    args += [*gathered, place_out, strip, *tables]
    sums_wide = 2 * kv_here * LANES
    if full:
        in_specs.append(pl.BlockSpec((depth, wide), lambda t: (0, t)))
        args.append(qkv_pad)
    if acc is not None:
        in_specs.append(pl.BlockSpec((keys, sums_wide), lambda t: (0, t)))
        args.append(acc)
    f32, bf16 = jnp.float32, jnp.bfloat16
    outs = [
        jax.ShapeDtypeStruct((depth, rows), bf16),
        jax.ShapeDtypeStruct((rows, kv_here * strip.shape[1]), bf16),
        jax.ShapeDtypeStruct((rows, depth), bf16),
        jax.ShapeDtypeStruct((8, depth), f32),
    ]
    outs = outs if full else outs[:2]
    out_specs = [whole(out) for out in outs]
    if full and start > 0:
        outs.append(jax.ShapeDtypeStruct((start, levels * sums_wide), f32))
        out_specs.append(pl.BlockSpec((start, sums_wide), lambda t: (0, t)))
    results = pl.pallas_call(
        functools.partial(backward_kernel, start, full),
        out_shape=outs,
        grid=(levels if full else 1,),
        in_specs=in_specs,
        out_specs=out_specs,
        scratch_shapes=[
            pltpu.VMEM((rows, depth), f32),
            pltpu.VMEM((rows, depth), bf16),
            pltpu.VMEM((rows, depth), f32),
        ],
        compiler_params=params(),
        cost_estimate=cost(
            levels * rows * (20 * kv_here * keys * LANES + 2 * depth * (out_wide + wide)),
            2 * depth * levels * (out_wide + wide) + 16 * rows * depth,
            levels * kv_here * GROUP * rows * keys,
        ),
    )(*args)
    return results[:4], (results[4] if full and start > 0 else None)


def rows_kernel(lefts, groups, adding, picked, together, side_ref, *refs):
    refs = list(refs)
    held_ref = refs.pop()
    out_refs = refs[-len(picked) :]
    refs = refs[: -len(picked)]
    recv_ref = refs.pop() if adding else None
    step = pl.program_id(0)
    left_refs = []
    for count in lefts:
        left_refs.append(refs[:count])
        refs = refs[count:]
    rights = []
    for _ in groups:
        rights.append(refs[:CHUNKS])
        refs = refs[CHUNKS:]
    rows = left_refs[0][0].shape[0]
    blocks = held_ref.shape[1] // rows

    @pl.when(step == 0)
    def _():
        for which, pieces in enumerate(left_refs):
            for n, ref in enumerate(pieces):
                m, j = n % blocks, n // blocks
                wide = ref.shape[1]
                held_ref[which, m * rows : (m + 1) * rows, j * wide : (j + 1) * wide] = ref[...]

    chunk = held_ref.shape[2] // CHUNKS
    whole_columns = slice(0, out_refs[0].shape[1])

    def give(group, left, columns):
        right = jnp.concatenate([ref[:chunk, :].astype(jnp.bfloat16) for ref in group], 0)
        total = dot32(held_ref[left], right)
        if recv_ref is not None:
            total = total + recv_ref[:, columns]
        for out_ref, parts in zip(out_refs, picked):
            at = 0
            for start, size in parts:
                out_ref[at : at + size, columns] = total[start : start + size]
                at += size

    begin = 0
    for group, (left, first, steps) in zip(rights, groups):
        if together:
            width = group[0].shape[1]
            give(group, left, slice(begin, begin + width))
            begin += width
        else:

            @pl.when((step >= first) & (step < first + steps))
            def _(group=group, left=left):
                give(group, left, whole_columns)


def rows_of(lefts, groups, side, rows, blocks, step, recv=None, picked=None):
    if picked is None:
        picked = [[(0, rows * blocks)]]
    at = lambda m: lambda i, side: ((m ^ side[2]) * side[1] + side[0], 0)
    specs = []
    args = []
    counts = []
    for left in lefts:
        pieces = left if isinstance(left, list) else [left]
        counts.append(len(pieces) * blocks)
        for piece in pieces:
            for m in range(blocks):
                specs.append(pl.BlockSpec((rows, piece.shape[1]), at(m)))
                args.append(piece)
    tokens = sum(piece.shape[1] for piece in pieces)
    first = 0
    plan = []
    together = step is None
    for which, rights in groups:
        if together:
            plan.append((which, 0, 1))
            specs += [whole(right) for right in rights]
            args += rights
            first += rights[0].shape[1]
            continue
        steps = rights[0].shape[1] // step
        plan.append((which, first, steps))
        for right in rights:
            pick = lambda i, side, first=first, steps=steps: (0, jnp.clip(i - first, 0, steps - 1))
            specs.append(pl.BlockSpec((right.shape[0], step), pick))
            args.append(right)
        first += steps
    if together:
        first, step = 1, first
    total = first * step
    block = lambda height: pl.BlockSpec((height, step), lambda i, side: (0, i))
    if recv is not None:
        specs.append(block(rows * blocks))
        args.append(recv)
    heights = [sum(size for _, size in parts) for parts in picked]
    results = pl.pallas_call(
        functools.partial(rows_kernel, counts, plan, recv is not None, picked, together),
        out_shape=[jax.ShapeDtypeStruct((height, total), jnp.float32) for height in heights],
        grid_spec=pltpu.PrefetchScalarGridSpec(
            num_scalar_prefetch=1,
            grid=(first,),
            in_specs=specs,
            out_specs=[block(height) for height in heights],
            scratch_shapes=[pltpu.VMEM((len(lefts), rows * blocks, tokens), jnp.bfloat16)],
        ),
        compiler_params=params(),
        cost_estimate=cost(
            2 * rows * blocks * tokens * total,
            4 * rows * blocks * total + 2 * tokens * (total + rows * blocks),
        ),
    )(side, *args)
    return results[0] if len(picked) == 1 else results


def shards(
    tokens,
    lengths,
    positions,
    cotangent,
    norm_gain,
    w_query,
    w_key,
    w_value,
    w_out,
    mlp_gain,
    w_gate,
    w_up,
    w_down,
):
    seq_rows, depth = tokens.shape
    chips = lax.axis_size("chip")
    dp = chips * 2
    tp = lax.axis_size("tp")
    chip = lax.axis_index("chip")
    core = lax.axis_index("core")
    level = lax.axis_index("tp")
    low = level < 2
    inner = (level == 1) | (level == 2)
    heads_here = w_query.shape[1] // HD
    kv_here = w_key.shape[1] // HD
    rows = seq_rows // CHUNKS
    slice_rows = depth // dp
    level_ref = level.astype(jnp.int32).reshape(1)
    by_hand = dp == 8
    swap = lambda array: lax.ppermute(array, "core", [(0, 1), (1, 0)])
    to_level = lambda array, s: along(array, [(t, t ^ s) for t in range(tp)])

    at_row = (chip * 2 + core) * slice_rows
    cols = lambda w: lax.dynamic_slice_in_dim(w, at_row, slice_rows, 1).astype(jnp.float32).T
    (out_slice,) = fence(cols(w_out))
    qkv_slice = jnp.concatenate(
        [
            lax.dynamic_slice_in_dim(w_query, at_row, slice_rows, 0).astype(jnp.float32),
            cols(w_key.T),
            cols(w_value.T),
        ],
        1,
    )
    out_slice, qkv_slice = fence(out_slice, qkv_slice)
    out_near = along(out_slice, PAIRS)
    qkv_near = along(qkv_slice, PAIRS)
    meta = jnp.stack([chip, core]).astype(jnp.int32)

    pq = place_query(heads_here)
    pkv = place_key_value(kv_here)
    p_all = place_all(heads_here, kv_here)
    strip_one = place_all(GROUP, 1).T
    p_out = place_plain(heads_here)
    strip_out = p_out.T

    half_dim = HD // 2
    freqs = rope_base ** (-(jnp.arange(half_dim).astype(jnp.float32) * 2.0 / HD))
    freqs = jnp.pad(freqs, (0, LANES // 2 - half_dim))
    angles = positions.astype(jnp.float32)[:, None] * jnp.concatenate([freqs, freqs])[None, :]
    cosines = jnp.cos(angles)
    sines = jnp.sin(angles) * jnp.where(jnp.arange(LANES) < LANES // 2, -1.0, 1.0)

    cosines, sines, out_near = fence(cosines, sines, out_near)
    out_across = along(jnp.stack([out_slice, out_near]), MIDDLE)
    qkv_own, normed_one, own_pad = start(
        tokens, norm_gain, w_query, w_key.T, w_value.T, pq, pkv, cosines, sines
    )

    def far_slices(near, across, outer):
        return jnp.stack(
            [
                near,
                jnp.where(inner, across[1], outer[0]),
                jnp.where(inner, across[0], outer[1]),
            ]
        )

    order = list(reversed(range(CHUNKS)))
    c0, c1, c2, c3 = order
    own, other, across, outer = {}, {}, {}, {}
    part, total, final = {}, {}, {}

    def hop_1(j):
        other[j] = along(own[j], PAIRS)

    def hop_2(j):
        across[j] = along(jnp.concatenate([own[j], other[j]], 1), MIDDLE)

    def hop_3(j):
        outer[j] = along(across[j], OUTWARD)

    coming = {}

    def add_1(j):
        coming[j] = along(part[j], INWARD)

    def add_2(j):
        total[j] = part[j][:rows] + coming[j][:rows]
        coming[j] = along(total[j], MIDDLE)

    def add_3(j, inward, extra=0):
        both = jnp.where(inner, total[j] + coming[j], inward)
        total[j] = jnp.pad(both, ((0, extra), (0, 0)))
        final[j] = along(total[j], PAIRS)
        return final[j][:rows]

    def to_chip(array, m):
        return lax.ppermute(array, "chip", [(i, i ^ m) for i in range(chips)])

    def over_chips_1(piece):
        cut = piece.shape[1] // 2
        one, two = piece[:, :cut], piece[:, cut:]
        return jnp.stack([one, to_chip(one, 1)]), jnp.stack([two, to_chip(two, 2)])

    def over_chips_2(one, two):
        return one, to_chip(one, 2), two, to_chip(two, 1)

    def over_chips_3(one, one_far, two, two_far):
        upper = jnp.stack([one[0], one[1], one_far[0], one_far[1]])
        lower = jnp.stack([two[0], two_far[0], two[1], two_far[1]])
        return jnp.concatenate([upper, lower], 2)

    qkv_own, out_across, qkv_near = fence(qkv_own, out_across, qkv_near)
    out_outer = along(out_across, OUTWARD)
    qkv_across = along(jnp.stack([qkv_slice, qkv_near]), MIDDLE)
    own[c0] = attend(lengths, qkv_own, strip_out, c0, rows)
    own, qkv_own, out_outer = fence(own, qkv_own, out_outer)
    hop_1(c0)
    out_far = far_slices(out_near, out_across, out_outer)
    out_mine = over_chips_1(out_far) if by_hand else out_far
    own[c1] = attend(lengths, qkv_own, strip_out, c1, rows)
    own[c1], qkv_own = fence(own[c1], qkv_own)
    hop_1(c1)
    own[c2] = attend(lengths, qkv_own, strip_out, c2, rows)
    own, other[c0], normed_one, w_out, out_mine, qkv_across, qkv_own = fence(
        own, other[c0], normed_one, w_out, out_mine, qkv_across, qkv_own
    )
    own[c3] = attend(lengths, qkv_own, strip_out, c3, rows)
    qkv_outer = along(qkv_across, OUTWARD)
    if by_hand:
        out_mine = over_chips_2(*out_mine)
    else:
        out_mine = lax.all_gather(out_mine, ("chip", "core"))
    hop_2(c0)
    dout, dout_t, normed_one_t = turn(lengths, cotangent, normed_one)
    w_out_t = w_out.T
    own, other, across, dout, dout_t, normed_one_t, w_out_t, out_mine, qkv_outer = fence(
        own, other, across, dout, dout_t, normed_one_t, w_out_t, out_mine, qkv_outer
    )
    hop_1(c2)
    hop_3(c0)
    hop_2(c1)
    qkv_far = lax.all_gather(far_slices(qkv_near, qkv_across, qkv_outer), ("chip", "core"))
    if by_hand:
        out_mine = over_chips_3(*out_mine)
        out_theirs = swap(out_mine)
        out_pad, out_plain = spread(
            spread_out_kernel,
            meta,
            w_out_t,
            [p_out],
            out_mine,
            out_theirs,
            [4 * p_out.shape[1], 4 * p_out.shape[0]],
        )
    else:
        plain = [w_out_t] + [
            out_mine[:, s].reshape(depth, -1).astype(jnp.bfloat16) for s in range(tp - 1)
        ]
        out_plain = jnp.concatenate(plain, 1)
        out_pad = jnp.concatenate([dot32(w, p_out).astype(jnp.bfloat16) for w in plain], 1)
    hidden, normed_t, activ, dgate, dup, mlp_part = {}, {}, {}, {}, {}, {}

    def feed(j):
        gathered = (own[j], other[j], across[j], outer[j])
        (hidden[j], normed_t[j], activ[j], dgate[j], dup[j], mlp_part[j], part[j]) = forward_chunk(
            level_ref, gathered, tokens, dout, out_plain, mlp_gain, w_gate, w_up, w_down, j, rows
        )

    own, other, across, outer, out_pad, out_plain = fence(
        own, other, across, outer, out_pad, out_plain
    )
    hop_1(c3)
    hop_3(c1)
    hop_2(c2)
    feed(c0)
    part, other = fence(part, other)
    add_1(c0)
    own, other, across, outer, part, hidden = fence(own, other, across, outer, part, hidden)
    hop_3(c2)
    hop_2(c3)
    feed(c1)
    qkv_far, hidden[c1] = fence(qkv_far, hidden[c1])
    qkv_pad = spread_qkv(own_pad, pq, pkv, qkv_far)
    own, other, across, outer, part, total, coming, hidden, qkv_pad = fence(
        own, other, across, outer, part, total, coming, hidden, qkv_pad
    )
    add_1(c1)
    hop_3(c3)
    add_2(c0)
    feed(c2)
    qkv_pad, hidden[c2] = fence(qkv_pad, hidden[c2])
    qkv = project(normed_one, qkv_pad, cosines, sines, qkv_own)
    own, other, across, outer, part, total, coming, hidden, qkv = fence(
        own, other, across, outer, part, total, coming, hidden, qkv
    )
    coming[c2] = add_3(c0, part[c2][:rows])
    add_2(c1)
    feed(c3)

    listed = lambda pieces: [pieces[j] for j in range(CHUNKS)]
    keep_side = jnp.stack([core, 2, 0]).astype(jnp.int32)
    keep_turned = jnp.stack([core, 2, chip]).astype(jnp.int32)
    send_side = jnp.stack([1 - core, 2, 0]).astype(jnp.int32)
    send_turned = jnp.stack([1 - core, 2, chip]).astype(jnp.int32)
    all_rows = jnp.array([0, 1, 0], jnp.int32)

    def send_rows(lefts, groups, step, side=send_side):
        if not by_hand:
            return rows_of(lefts, groups, all_rows, depth // 4, 4, step)
        return rows_of(lefts, groups, side, slice_rows, chips, step)

    def keep_rows(lefts, groups, received, step, side=keep_side, picked=None):
        if not by_hand:
            return received
        return rows_of(lefts, groups, side, slice_rows, chips, step, received, picked)

    def swap_rows(array):
        return swap(array) if by_hand else array

    def scatter(array, axes):
        return lax.psum_scatter(array, axes, scatter_dimension=0, tiled=True)

    units = w_gate.shape[1]
    mlp_args = (
        [listed(normed_t), dout_t],
        [(0, listed(dgate)), (0, listed(dup)), (1, listed(activ))],
    )
    acc = None
    dhid_t, dqkv_own, input_grad, gains = {}, {}, {}, {}

    def back(j):
        nonlocal acc
        (dhid_t[j], dqkv_own[j], input_grad[j], gains[j]), acc = back_some(j, True)

    def back_own(j):
        return back_some(j, False)[0]

    def back_some(j, full):
        return backward_chunk(
            level_ref,
            (total[j], final[j]),
            hidden[j],
            dout,
            tokens,
            (norm_gain, mlp_gain),
            (out_pad, qkv_pad),
            qkv,
            (own[j], other[j], across[j], outer[j]),
            (p_out, strip_one),
            (cosines, sines),
            acc,
            j,
            rows,
            full,
        )

    grad_mlp = rows_of(*mlp_args, all_rows, depth // 4, 4, units // 2)
    own, other, across, outer, part, total, coming, final, hidden, grad_mlp = fence(
        own, other, across, outer, part, total, coming, final, hidden, grad_mlp
    )
    grad_mlp = scatter(grad_mlp, ("chip", "core"))
    coming[c3] = add_3(c1, part[c3][:rows])
    add_2(c2)
    back(c0)

    near = lambda: jnp.where(low, mlp_part[1], mlp_part[2])
    edge = lambda: jnp.where(low, mlp_part[0], mlp_part[3])
    leave_far = lambda: jnp.where(low, mlp_part[3], mlp_part[0])
    leave_near = lambda: jnp.where(low, mlp_part[2], mlp_part[1])
    total, coming, final, hidden, mlp_part, acc, dhid_t = fence(
        total, coming, final, hidden, mlp_part, acc, dhid_t
    )
    far_sum = add_3(c2, leave_far())
    add_2(c3)
    back(c1)
    total, coming, final, hidden, mlp_part, far_sum, acc, dhid_t = fence(
        total, coming, final, hidden, mlp_part, far_sum, acc, dhid_t
    )
    near_sum = add_3(c3, leave_near(), EXTRA)
    far_in = along(leave_far() + far_sum, MIDDLE)
    back(c2)
    total, final, hidden, mlp_part, near_sum, far_in, acc, dhid_t = fence(
        total, final, hidden, mlp_part, near_sum, far_in, acc, dhid_t
    )
    last = along(jnp.where(inner, edge() + far_in, near()), PAIRS)
    near_in = along(leave_near() + near_sum, MIDDLE)
    dhid_t[c3], dqkv_own[c3] = back_own(c3)
    q_cols = heads_here * HD
    attn_args = (
        [listed(dhid_t), normed_one_t],
        [(0, listed(own)), (1, listed(dqkv_own))],
    )
    sent = swap_rows(send_rows(*attn_args, None, send_turned))
    total, final, hidden, acc, sent = fence(total, final, hidden, acc, sent)
    if by_hand:
        half = slice_rows // 2
        upper = lambda m: (m * slice_rows, half)
        lower = lambda m: (m * slice_rows + half, half)
        picked = [
            [upper(1), upper(3)],
            [upper(0), upper(2)],
            [lower(2), lower(3)],
            [lower(0), lower(1)],
        ]
        pieces = keep_rows(*attn_args, sent, None, keep_turned, picked)
        pieces, hidden = fence(pieces, hidden)
        one_away, one, two_away, two = pieces
        pieces = (one, to_chip(one_away, 1), two, to_chip(two_away, 2))
    else:
        pieces = scatter(sent, ("chip", "core"))
    back(c3)
    pieces, gains, input_grad, last, near_in = fence(pieces, gains, input_grad, last, near_in)
    gain_sums = gains[0] + gains[1] + gains[2] + gains[3]
    gain_sums = gain_sums + swap(gain_sums)
    if by_hand:
        others = [to_chip(gain_sums, m) for m in range(1, chips)]
        gain_sums = sum(others, gain_sums)
        one = pieces[0] + pieces[1]
        two = pieces[2] + pieces[3]
        one = one[:half] + to_chip(one[half:], 2)
        two = two[:half] + to_chip(two[half:], 1)
        attn = jnp.concatenate([one, two], 0)
    else:
        gain_sums = lax.psum(gain_sums, "chip")
        attn = pieces
    gain_rows = lax.dynamic_slice_in_dim(gain_sums, at_row, slice_rows, 1)
    grad_out, grad_qkv = attn[:, :q_cols], attn[:, q_cols:]
    mlp_rows = jnp.where(inner, near() + near_in, edge()) + last
    hidden_rows = jnp.where(
        low,
        jnp.where(level == 0, hidden[0], hidden[1]),
        jnp.where(level == 2, hidden[2], hidden[3]),
    )
    layer_out = (hidden_rows + mlp_rows).astype(jnp.bfloat16)
    one = strip_one.shape[1]
    picked = lambda at, width: jnp.concatenate(
        [grad_qkv[:, kv * one + at : kv * one + at + width] for kv in range(kv_here)], 1
    )
    return (
        layer_out,
        jnp.concatenate(listed(input_grad), 0),
        gain_rows[0],
        picked(0, GROUP * HD),
        picked(GROUP * HD, HD),
        picked((GROUP + 1) * HD, HD),
        grad_out.T,
        gain_rows[1],
        grad_mlp[:, :units],
        grad_mlp[:, units : 2 * units],
        grad_mlp[:, 2 * units :].T,
    )


def solution(mesh):
    devices = mesh.devices
    dp, tp = devices.shape
    split = Mesh(devices.reshape(dp // 2, 2, tp), ("chip", "core", "tp"))
    data = ("chip", "core")
    return jax.shard_map(
        shards,
        mesh=split,
        in_specs=(
            P(data, None),
            P(data),
            P(data),
            P(data, None),
            P(),
            P(None, "tp"),
            P(None, "tp"),
            P(None, "tp"),
            P("tp", None),
            P(),
            P(None, "tp"),
            P(None, "tp"),
            P("tp", None),
        ),
        out_specs=(
            P(("chip", "core", "tp"), None),
            P(data, None),
            P(data),
            P(data, "tp"),
            P(data, "tp"),
            P(data, "tp"),
            P("tp", data),
            P(data),
            P(data, "tp"),
            P(data, "tp"),
            P("tp", data),
        ),
        check_vma=False,
    )
```

```python
import functools

import jax
import jax.numpy as jnp
from jax import lax
from jax.experimental import pallas as pl
from jax.experimental.pallas import tpu as pltpu
from jax.sharding import Mesh
from jax.sharding import PartitionSpec as P

HD = 96
LANES = 128
GROUP = 2
KV_WIDE = (GROUP + 2) * LANES
rope_base = 100000.0
norm_eps = 1e-05
masked_score = -1e30
far_away = 1e30
score_scale = HD ** (-0.5)
score_scale_log2 = score_scale * 1.4426950408889634
CHUNKS = 4
EXTRA = 8
VMEM_BYTES = 56 * 1024 * 1024
NT = (((1,), (1,)), ((), ()))


def params():
    return pltpu.CompilerParams(vmem_limit_bytes=VMEM_BYTES)


def cost(flops, moved, exps=0):
    return pl.CostEstimate(
        flops=flops // 1024, bytes_accessed=moved // 1024, transcendentals=exps // 1024
    )


def dot32(a, b):
    return jnp.dot(a, b, preferred_element_type=jnp.float32)


def dot32_nt(a, b):
    return lax.dot_general(a, b, NT, preferred_element_type=jnp.float32)


def dot_split(a, places):
    high = a.astype(jnp.bfloat16)
    rest = (a - high.astype(jnp.float32)).astype(jnp.bfloat16)
    return dot32(high, places) + dot32(rest, places)


def fence(*trees):
    return lax.optimization_barrier(trees)


def whole(array, buffers=None):
    zeros = (0,) * len(array.shape)
    return pl.BlockSpec(array.shape, lambda *_: zeros)


SCALAR = pl.BlockSpec(memory_space=pltpu.SMEM)


def halves(entry):
    half_dim = HD // 2
    return (entry // half_dim) * (LANES // 2) + entry % half_dim


def placement(lanes, width):
    return (lanes[:, None] == jnp.arange(width)[None, :]).astype(jnp.bfloat16)


def place_query(heads):
    source = jnp.arange(heads * HD)
    return placement((source // HD) * LANES + halves(source % HD), heads * LANES)


def place_key_value(kv_heads):
    source = jnp.arange(kv_heads * HD)
    head = source // HD
    keys = head * 2 * LANES + halves(source % HD)
    values = head * 2 * LANES + LANES + source % HD
    return placement(jnp.concatenate([keys, values]), kv_heads * 2 * LANES)


def place_all(heads, kv_heads):
    source = jnp.arange(heads * HD)
    head = source // HD
    query = (head // GROUP) * KV_WIDE + (head % GROUP) * LANES + halves(source % HD)
    source = jnp.arange(kv_heads * HD)
    base = (source // HD) * KV_WIDE + GROUP * LANES
    keys = base + halves(source % HD)
    values = base + LANES + source % HD
    return placement(jnp.concatenate([query, keys, values]), kv_heads * KV_WIDE)


def place_plain(heads):
    source = jnp.arange(heads * HD)
    return placement((source // HD) * LANES + source % HD, heads * LANES)


PAIRS = [(0, 1), (1, 0), (2, 3), (3, 2)]
INWARD = [(0, 1), (3, 2)]
MIDDLE = [(1, 2), (2, 1)]
OUTWARD = [(1, 0), (2, 3)]


def along(part, pairs):
    return lax.ppermute(part, "tp", pairs)


def store_qkv(out_ref, here, base, query, key_value):
    wide = GROUP * LANES
    for kv in range(key_value.shape[1] // (2 * LANES)):
        at = base + kv * KV_WIDE
        there = slice(kv * 2 * LANES, (kv + 1) * 2 * LANES)
        out_ref[here, at : at + wide] = query[:, kv * wide : (kv + 1) * wide]
        out_ref[here, at + wide : at + KV_WIDE] = key_value[:, there]


def store_turned(out_ref, at, lin, cos_ref, sin_ref):
    for h in range(GROUP + 2):
        one = lin[:, h * LANES : (h + 1) * LANES]
        if h < GROUP + 1:
            one = one * cos_ref[...] + pltpu.roll(one, LANES // 2, 1) * sin_ref[...]
        out_ref[:, at + h * LANES : at + (h + 1) * LANES] = one.astype(jnp.bfloat16)


def spread_out_kernel(meta_ref, own_ref, p_ref, mine_ref, theirs_ref, pad_ref, plain_ref):
    rows, width = mine_ref.shape[2:]
    wide = p_ref.shape[1]
    for side, ref in enumerate((mine_ref, theirs_ref)):
        here = pl.ds(pl.multiple_of((meta_ref[1] ^ side) * rows, rows), rows)
        for s in range(4):
            block = own_ref[here, :] if s == 0 else ref[0, s - 1].astype(jnp.bfloat16)
            plain_ref[here, s * width : (s + 1) * width] = block
            pad_ref[here, s * wide : (s + 1) * wide] = dot32(block, p_ref[...]).astype(
                jnp.bfloat16
            )


def spread_qkv_kernel(pq_ref, pkv_ref, near_ref, far_ref, _, out_ref):
    parts, _, rows, width = far_ref.shape
    split = pq_ref.shape[0]
    block = jnp.where(pl.program_id(1) == 0, near_ref[:, 0], far_ref[:, 0])
    block = block.reshape(parts * rows, width).astype(jnp.bfloat16)
    query = dot32(block[:, :split], pq_ref[...]).astype(jnp.bfloat16)
    key_value = dot32(block[:, split:], pkv_ref[...]).astype(jnp.bfloat16)
    store_qkv(out_ref, slice(None), 0, query, key_value)


def spread_qkv(padded, pq, pkv, near, far):
    total = padded.shape[0]
    dp, others, rows, width = far.shape
    wide = padded.shape[1] // (others + 2)
    parts = max(1, dp // 2)
    block = parts * rows
    return pl.pallas_call(
        spread_qkv_kernel,
        out_shape=jax.ShapeDtypeStruct(padded.shape, jnp.bfloat16),
        grid=(total // block, others + 1),
        in_specs=[
            whole(pq),
            whole(pkv),
            pl.BlockSpec((parts, 1, rows, width), lambda i, s: (i, 0, 0, 0)),
            pl.BlockSpec((parts, 1, rows, width), lambda i, s: (i, jnp.maximum(s - 1, 0), 0, 0)),
            pl.BlockSpec(memory_space=pl.ANY),
        ],
        out_specs=pl.BlockSpec((block, wide), lambda i, s: (i, s + 1)),
        input_output_aliases={4: 0},
        compiler_params=params(),
        cost_estimate=cost(8 * total * width * 512, 20 * total * wide),
    )(pq, pkv, near, far, padded)


def spread(kernel, meta, own, places, mine, theirs, widths):
    chips, others, rows, width = mine.shape
    total = own.shape[0]
    row_block = lambda m, meta: (meta[0] ^ m, 0)
    piece = pl.BlockSpec((1, others, rows, width), lambda m, meta: (m, 0, 0, 0))
    return pl.pallas_call(
        kernel,
        out_shape=[jax.ShapeDtypeStruct((total, wide), jnp.bfloat16) for wide in widths],
        grid_spec=pltpu.PrefetchScalarGridSpec(
            num_scalar_prefetch=1,
            grid=(chips,),
            in_specs=[pl.BlockSpec((2 * rows, own.shape[1]), row_block)]
            + [whole(place) for place in places]
            + [piece, piece],
            out_specs=[pl.BlockSpec((2 * rows, wide), row_block) for wide in widths],
        ),
        compiler_params=params(),
        cost_estimate=cost(
            8 * total * width * 512, total * (12 * width + 2 * sum(widths))
        ),
    )(meta, own, *places, mine, theirs)


def start_kernel(x_ref, gain_ref, q_ref, k_ref, v_ref, pq_ref, pkv_ref, cos_ref, sin_ref, *outs):
    qkv_ref, normed_ref, pad_ref = outs

    @pl.when(pl.program_id(0) == 0)
    def _():
        split = k_ref.shape[0]
        query = dot32(q_ref[...], pq_ref[...]).astype(jnp.bfloat16)
        key_value = dot32(k_ref[...].T, pkv_ref[:split, :])
        key_value = key_value + dot32(v_ref[...].T, pkv_ref[split:, :])
        store_qkv(pad_ref, slice(None), 0, query, key_value.astype(jnp.bfloat16))

    inputs = x_ref[...].astype(jnp.float32)
    rms = lax.rsqrt(jnp.mean(inputs * inputs, -1, keepdims=True) + norm_eps)
    normed = (inputs * rms * gain_ref[...]).astype(jnp.bfloat16)
    normed_ref[...] = normed
    for kv in range(pad_ref.shape[1] // KV_WIDE):
        at = kv * KV_WIDE
        store_turned(qkv_ref, at, dot32(normed, pad_ref[:, at : at + KV_WIDE]), cos_ref, sin_ref)


def start(tokens, gain, w_query, w_key_t, w_value_t, pq, pkv, cosines, sines):
    total, depth = tokens.shape
    rows = total // CHUNKS
    wide = pq.shape[1] + pkv.shape[1]
    gain = gain[None, :]
    by_rows = lambda width: pl.BlockSpec((rows, width), lambda i: (i, 0))
    arrays = [w_query, w_key_t, w_value_t, pq, pkv]
    shapes = [
        jax.ShapeDtypeStruct((total, 4 * wide), jnp.bfloat16),
        jax.ShapeDtypeStruct((total, depth), jnp.bfloat16),
        jax.ShapeDtypeStruct((depth, 4 * wide), jnp.bfloat16),
    ]
    return pl.pallas_call(
        start_kernel,
        out_shape=shapes,
        grid=(CHUNKS,),
        in_specs=[by_rows(depth), whole(gain)]
        + [whole(array) for array in arrays]
        + [by_rows(LANES), by_rows(LANES)],
        out_specs=[
            by_rows(wide),
            by_rows(depth),
            pl.BlockSpec((depth, wide), lambda i: (0, 0)),
        ],
        compiler_params=params(),
        cost_estimate=cost(2 * total * depth * wide, 12 * total * depth),
    )(tokens, gain, *arrays, cosines, sines)


def turn_kernel(length_ref, cot_ref, normed_ref, dout_ref, dout_t_ref, normed_t_ref):
    rows = cot_ref.shape[0]
    at = pl.program_id(0) * rows + lax.broadcasted_iota(jnp.int32, cot_ref.shape, 0)
    dout = jnp.where(at < length_ref[0], cot_ref[...].astype(jnp.float32), 0.0)
    dout = dout.astype(jnp.bfloat16)
    dout_ref[...] = dout
    dout_t_ref[...] = dout.T
    normed_t_ref[...] = normed_ref[...].T


def turn(length, cotangent, normed):
    total, depth = cotangent.shape
    rows = total // CHUNKS
    by_rows = pl.BlockSpec((rows, depth), lambda i: (i, 0))
    by_columns = pl.BlockSpec((depth, rows), lambda i: (0, i))
    turned = jax.ShapeDtypeStruct((depth, total), jnp.bfloat16)
    return pl.pallas_call(
        turn_kernel,
        out_shape=[jax.ShapeDtypeStruct((total, depth), jnp.bfloat16), turned, turned],
        grid=(CHUNKS,),
        in_specs=[SCALAR, by_rows, by_rows],
        out_specs=[by_rows, by_columns, by_columns],
        compiler_params=params(),
        cost_estimate=cost(total * depth, 10 * total * depth),
    )(length, cotangent, normed)


def project_kernel(x_ref, w_ref, cos_ref, sin_ref, _, out_ref):
    store_turned(out_ref, 0, dot32(x_ref[...], w_ref[...]), cos_ref, sin_ref)


def project(normed, weights, cosines, sines, qkv):
    rows, depth = normed.shape
    width = weights.shape[1]
    steps = width // KV_WIDE
    first = steps // 4
    return pl.pallas_call(
        project_kernel,
        out_shape=jax.ShapeDtypeStruct((rows, width), jnp.bfloat16),
        grid=(steps - first,),
        in_specs=[
            whole(normed),
            pl.BlockSpec((depth, KV_WIDE), lambda i: (0, i + first)),
            whole(cosines),
            whole(sines),
            pl.BlockSpec(memory_space=pl.ANY),
        ],
        out_specs=pl.BlockSpec((rows, KV_WIDE), lambda i: (0, i + first)),
        input_output_aliases={4: 0},
        compiler_params=params(),
        cost_estimate=cost(
            2 * rows * depth * width, 2 * (rows * depth + depth * width + rows * width)
        ),
    )(normed, weights, cosines, sines, qkv)


def attend_kernel(start, length_ref, q_ref, kv_ref, strip_ref, out_ref):
    rows = q_ref.shape[0]
    keys = kv_ref.shape[0]
    length = length_ref[0]
    row_ids = start + lax.broadcasted_iota(jnp.int32, (1, rows), 1)
    limit = jnp.minimum(row_ids, length - 1)
    allowed = lax.broadcasted_iota(jnp.int32, (keys, rows), 0) <= limit
    mixed = []
    sums = []
    for kv in range(kv_ref.shape[1] // KV_WIDE):
        base = kv * KV_WIDE
        at = base + GROUP * LANES
        key = kv_ref[:, at : at + LANES]
        value_t = kv_ref[:, at + LANES : at + 2 * LANES].T
        for g in range(GROUP):
            query = q_ref[:, base + g * LANES : base + (g + 1) * LANES]
            raw = jnp.where(allowed, dot32_nt(key, query), masked_score)
            peak = jnp.max(raw, axis=0, keepdims=True)
            expo = jnp.exp2((raw - peak) * score_scale_log2)
            total = jnp.sum(expo, axis=0, keepdims=True)
            probs = (expo * (1.0 / total)).astype(jnp.bfloat16)
            mixed.append(dot32(value_t, probs).T)
            log_sum = peak * score_scale_log2 + jnp.log2(total)
            sums.append(jnp.where(row_ids < length, log_sum, far_away))
    out_ref[:rows, :] = dot_split(jnp.concatenate(mixed, 1), strip_ref[...])
    out_ref[rows:, :] = jnp.zeros((EXTRA, out_ref.shape[1]), jnp.float32)
    out_ref[rows : rows + len(sums), :rows] = jnp.concatenate(sums, 0)


def attend(length, qkv, strip, index, rows):
    keys = (index + 1) * rows
    width = qkv.shape[1] // 4
    heads = width // KV_WIDE * GROUP
    shape = (rows + EXTRA, strip.shape[1])
    return pl.pallas_call(
        functools.partial(attend_kernel, index * rows),
        out_shape=jax.ShapeDtypeStruct(shape, jnp.float32),
        grid=(1,),
        in_specs=[
            SCALAR,
            pl.BlockSpec((rows, width), lambda i: (index, 0)),
            pl.BlockSpec((keys, width), lambda i: (0, 0)),
            whole(strip),
        ],
        out_specs=pl.BlockSpec(shape, lambda i: (0, 0)),
        compiler_params=params(),
        cost_estimate=cost(
            4 * heads * rows * keys * LANES, 2 * (rows + keys) * width, heads * rows * keys
        ),
    )(length, qkv, qkv, strip)


def forward_kernel(level_ref, part_ref, other_ref, across_ref, outer_ref, *refs):
    x_ref, dout_ref, wo_ref, gain_ref, wg_ref, wu_ref, wd_ref = refs[:7]
    hidden_ref, normed_t_ref, activ_ref, dgate_ref, dup_ref, mlp_ref, dn_ref = refs[7:14]
    normed_ref = refs[14]
    rows = x_ref.shape[0]

    @pl.when(pl.program_id(0) == 0)
    def _():
        level = level_ref[0]
        inner = (level == 1) | (level == 2)
        width = part_ref.shape[1]
        second = jnp.where(inner, across_ref[:rows, width:], outer_ref[:rows, :width])
        third = jnp.where(inner, across_ref[:rows, :width], outer_ref[:rows, width:])
        mixed = jnp.concatenate([part_ref[:rows, :], other_ref[:rows, :], second, third], 1)
        hidden = x_ref[...].astype(jnp.float32) + dot32_nt(mixed.astype(jnp.bfloat16), wo_ref[...])
        hidden_ref[...] = hidden
        rms = lax.rsqrt(jnp.mean(hidden * hidden, -1, keepdims=True) + norm_eps)
        normed = (hidden * rms * gain_ref[...]).astype(jnp.bfloat16)
        normed_ref[...] = normed
        normed_t_ref[...] = normed.T
        mlp_ref[...] = jnp.zeros_like(mlp_ref)
        dn_ref[...] = jnp.zeros_like(dn_ref)

    normed = normed_ref[...]
    gate = dot32(normed, wg_ref[...])
    up = dot32(normed, wu_ref[...])
    dact = dot32_nt(dout_ref[...], wd_ref[...])
    sigmoid = jax.nn.sigmoid(gate)
    silu = gate * sigmoid
    activ = (silu * up).astype(jnp.bfloat16)
    dgate = (dact * up * sigmoid * (1.0 + gate * (1.0 - sigmoid))).astype(jnp.bfloat16)
    dup = (dact * silu).astype(jnp.bfloat16)
    activ_ref[...] = activ
    dgate_ref[...] = dgate
    dup_ref[...] = dup
    mlp_ref[...] += dot32(activ, wd_ref[...])
    dn_ref[:rows, :] += dot32_nt(dgate, wg_ref[...]) + dot32_nt(dup, wu_ref[...])


def forward_chunk(level, gathered, tokens, dout, w_out, gain, w_gate, w_up, w_down, index, rows):
    depth = tokens.shape[1]
    units = w_gate.shape[1]
    block = 512
    own_rows = pl.BlockSpec((rows, depth), lambda i: (index, 0))
    by_units = pl.BlockSpec((depth, block), lambda i: (0, i))
    gain = gain[None, :]
    f32, bf16 = jnp.float32, jnp.bfloat16
    outs = [
        jax.ShapeDtypeStruct((rows, depth), f32),
        jax.ShapeDtypeStruct((depth, rows), bf16),
        jax.ShapeDtypeStruct((rows, units), bf16),
        jax.ShapeDtypeStruct((rows, units), bf16),
        jax.ShapeDtypeStruct((rows, units), bf16),
        jax.ShapeDtypeStruct((rows, depth), f32),
        jax.ShapeDtypeStruct((rows + EXTRA, depth), f32),
    ]
    unit_out = pl.BlockSpec((rows, block), lambda i: (0, i))
    return pl.pallas_call(
        forward_kernel,
        out_shape=outs,
        grid=(units // block,),
        in_specs=[SCALAR]
        + [whole(array) for array in gathered]
        + [own_rows, own_rows, whole(w_out), whole(gain), by_units, by_units]
        + [pl.BlockSpec((block, depth), lambda i: (i, 0))],
        out_specs=[
            whole(outs[0]),
            whole(outs[1]),
            unit_out,
            unit_out,
            unit_out,
            whole(outs[5]),
            whole(outs[6]),
        ],
        scratch_shapes=[pltpu.VMEM((rows, depth), bf16)],
        compiler_params=params(),
        cost_estimate=cost(
            2 * rows * depth * (6 * units + w_out.shape[1]),
            2 * depth * (3 * units + w_out.shape[1]) + 22 * rows * depth,
            rows * units,
        ),
    )(level, *gathered, tokens, dout, w_out, gain, w_gate, w_up, w_down)


def hidden_grad(inner, total_ref, final_ref, hidden_ref, dout_ref, gain_ref):
    dnormed = jnp.where(inner, total_ref[...], final_ref[...])
    hidden = hidden_ref[...]
    rms = lax.rsqrt(jnp.mean(hidden * hidden, -1, keepdims=True) + norm_eps)
    scaled = dnormed * gain_ref[...]
    shift = jnp.mean(scaled * hidden, -1, keepdims=True)
    dhid = dout_ref[...].astype(jnp.float32) + (rms * scaled - hidden * (rms**3 * shift))
    return dhid, dnormed * (hidden * rms)


def backward_kernel(start, full, level_ref, total_ref, final_ref, hidden_ref, dout_ref, x_ref, *refs):
    gain_one_ref, gain_two_ref, wo_ref, q_ref = refs[:4]
    kv_here = q_ref.shape[1] // KV_WIDE
    refs = refs[4:]
    kv_refs, refs = refs[: 2 * kv_here], refs[2 * kv_here :]
    part_ref, other_ref, across_ref, outer_ref, place_ref, strip_ref = refs[:6]
    cos_ref, sin_ref = refs[6:8]
    dhid_ref, low_ref, dn_ref = refs[-3:]
    outs = refs[8:-3]
    if full:
        w_ref, outs = outs[0], outs[1:]
    count = (5 if start > 0 else 4) if full else 2
    acc_ref = outs[0] if len(outs) > count else None
    outs = outs[-count:]
    dhid_t_ref, dqkv_ref = outs[:2]
    if full:
        input_grad_ref, gains_ref = outs[2:4]
    rows = q_ref.shape[0]
    keys = kv_refs[0].shape[0]
    shard = pl.program_id(0)
    level = level_ref[0]
    inner = (level == 1) | (level == 2)

    @pl.when(shard == 0)
    def _():
        dhid, dgain = hidden_grad(
            inner, total_ref, final_ref, hidden_ref, dout_ref, gain_two_ref
        )
        dhid_ref[...] = dhid
        low = dhid.astype(jnp.bfloat16)
        low_ref[...] = low
        dhid_t_ref[...] = low.T
        if full:
            gains_ref[...] = jnp.zeros_like(gains_ref)
            gains_ref[1:2, :] = jnp.sum(dgain, 0, keepdims=True)
            dn_ref[...] = jnp.zeros_like(dn_ref)

    def rotate_back(grads):
        turned = grads * cos_ref[...] - pltpu.roll(grads, LANES // 2, 1) * sin_ref[...]
        return turned.astype(jnp.bfloat16)

    dmixed_all = dot32(low_ref[...], wo_ref[...]).astype(jnp.bfloat16)
    mixed = jnp.where(
        shard == 0,
        part_ref[...],
        jnp.where(shard == 1, other_ref[...], jnp.where(inner, across_ref[...], outer_ref[...])),
    )
    products = dmixed_all.astype(jnp.float32) * dot_split(mixed[:rows], place_ref[...])
    causal = lax.broadcasted_iota(jnp.int32, (rows, rows), 0) <= lax.broadcasted_iota(
        jnp.int32, (rows, rows), 1
    )
    grads = []
    for kv in range(kv_here):
        key_ref, value_ref = kv_refs[2 * kv : 2 * kv + 2]
        heads = range(kv * GROUP, (kv + 1) * GROUP)
        lanes = {h: slice(h * LANES, (h + 1) * LANES) for h in heads}
        row_dots = {h: jnp.sum(products[:, lanes[h]].T, axis=0, keepdims=True) for h in heads}
        log_sums = {h: mixed[rows + h : rows + h + 1, :rows] for h in heads}
        dqueries = dict.fromkeys(heads)
        here = slice(2 * kv * LANES, (2 * kv + 1) * LANES)
        there = slice((2 * kv + 1) * LANES, (2 * kv + 2) * LANES)
        for tile in range(keys // rows):
            span = slice(tile * rows, (tile + 1) * rows)
            key = key_ref[span, :]
            value = value_ref[span, :]
            key_t = key.T
            dkey = None if acc_ref is None else acc_ref[span, here]
            dvalue = None if acc_ref is None else acc_ref[span, there]
            last = tile * rows == start
            for h in heads:
                at = kv * KV_WIDE + (h % GROUP) * LANES
                query = q_ref[:, at : at + LANES]
                dmixed = dmixed_all[:, lanes[h]]
                raw = dot32_nt(key, query)
                probs = jnp.exp2(raw * score_scale_log2 - log_sums[h])
                if last:
                    probs = jnp.where(causal, probs, 0.0)
                dprobs = dot32_nt(value, dmixed)
                dscores = (probs * (dprobs - row_dots[h])).astype(jnp.bfloat16)
                dquery = dot32(key_t, dscores)
                dqueries[h] = dquery if dqueries[h] is None else dqueries[h] + dquery
                dkey_one = dot32(dscores, query)
                dvalue_one = dot32(probs.astype(jnp.bfloat16), dmixed)
                dkey = dkey_one if dkey is None else dkey + dkey_one
                dvalue = dvalue_one if dvalue is None else dvalue + dvalue_one
            if full and not last:
                outs[4][span, here] = dkey
                outs[4][span, there] = dvalue
        grads += [rotate_back(dqueries[h].T * score_scale) for h in heads]
        grads.append(rotate_back(dkey * score_scale))
        grads.append(dvalue.astype(jnp.bfloat16))
    grads = jnp.concatenate(grads, 1)
    if full:
        dn_ref[...] += dot32_nt(grads, w_ref[...])

    @pl.when(shard == 0)
    def _():
        wide = strip_ref.shape[1]
        for kv in range(kv_here):
            dqkv_ref[:, kv * wide : (kv + 1) * wide] = dot32(
                grads[:, kv * KV_WIDE : (kv + 1) * KV_WIDE], strip_ref[...]
            ).astype(jnp.bfloat16)

    if not full:
        return

    @pl.when(shard == pl.num_programs(0) - 1)
    def _():
        dnormed = dn_ref[...]
        inputs = x_ref[...].astype(jnp.float32)
        rms = lax.rsqrt(jnp.mean(inputs * inputs, -1, keepdims=True) + norm_eps)
        scaled = dnormed * gain_one_ref[...]
        shift = jnp.mean(scaled * inputs, -1, keepdims=True)
        grad = dhid_ref[...] + (rms * scaled - inputs * (rms**3 * shift))
        input_grad_ref[...] = grad.astype(jnp.bfloat16)
        gains_ref[0:1, :] = jnp.sum(dnormed * (inputs * rms), 0, keepdims=True)


def backward_chunk(
    level, sums_two, hidden, dout, tokens, gains, weights, qkv, gathered, places, tables, acc,
    index, rows, full=True
):
    start = index * rows
    keys = start + rows
    depth = tokens.shape[1]
    out_pad, qkv_pad = weights
    place_out, strip = places
    far_rows, width = gathered[0].shape
    out_wide = place_out.shape[1]
    kv_here = out_wide // (GROUP * LANES)
    wide = kv_here * KV_WIDE
    levels = qkv.shape[1] // wide
    own_rows = pl.BlockSpec((rows, depth), lambda t: (index, 0))
    table = pl.BlockSpec((rows, LANES), lambda t: (index, 0))
    gains = [gain[None, :] for gain in gains]
    key_value = lambda at: pl.BlockSpec(
        (keys, LANES), lambda t: (0, (wide // LANES) * t + at)
    )
    across = pl.BlockSpec((far_rows, width), lambda t: (0, jnp.where(t == 2, 1, 0)))
    outer = pl.BlockSpec((far_rows, width), lambda t: (0, jnp.where(t == 3, 1, 0)))
    in_specs = [
        SCALAR,
        whole(hidden),
        whole(hidden),
        whole(hidden),
        own_rows,
        own_rows,
        whole(gains[0]),
        whole(gains[1]),
        pl.BlockSpec((depth, out_wide), lambda t: (0, t)),
        pl.BlockSpec((rows, wide), lambda t: (index, t)),
    ]
    for kv in range(kv_here):
        at = kv * (KV_WIDE // LANES) + GROUP
        in_specs += [key_value(at), key_value(at + 1)]
    in_specs += [
        whole(gathered[0]),
        whole(gathered[1]),
        across,
        outer,
        whole(place_out),
        whole(strip),
        table,
        table,
    ]
    args = [level, *sums_two, hidden, dout, tokens, *gains, out_pad]
    args += [qkv] * (1 + 2 * kv_here)
    args += [*gathered, place_out, strip, *tables]
    sums_wide = 2 * kv_here * LANES
    if full:
        in_specs.append(pl.BlockSpec((depth, wide), lambda t: (0, t)))
        args.append(qkv_pad)
    if acc is not None:
        in_specs.append(pl.BlockSpec((keys, sums_wide), lambda t: (0, t)))
        args.append(acc)
    f32, bf16 = jnp.float32, jnp.bfloat16
    outs = [
        jax.ShapeDtypeStruct((depth, rows), bf16),
        jax.ShapeDtypeStruct((rows, kv_here * strip.shape[1]), bf16),
        jax.ShapeDtypeStruct((rows, depth), bf16),
        jax.ShapeDtypeStruct((8, depth), f32),
    ]
    outs = outs if full else outs[:2]
    out_specs = [whole(out) for out in outs]
    if full and start > 0:
        outs.append(jax.ShapeDtypeStruct((start, levels * sums_wide), f32))
        out_specs.append(pl.BlockSpec((start, sums_wide), lambda t: (0, t)))
    results = pl.pallas_call(
        functools.partial(backward_kernel, start, full),
        out_shape=outs,
        grid=(levels if full else 1,),
        in_specs=in_specs,
        out_specs=out_specs,
        scratch_shapes=[
            pltpu.VMEM((rows, depth), f32),
            pltpu.VMEM((rows, depth), bf16),
            pltpu.VMEM((rows, depth), f32),
        ],
        compiler_params=params(),
        cost_estimate=cost(
            levels * rows * (20 * kv_here * keys * LANES + 2 * depth * (out_wide + wide)),
            2 * depth * levels * (out_wide + wide) + 16 * rows * depth,
            levels * kv_here * GROUP * rows * keys,
        ),
    )(*args)
    return results[:4], (results[4] if full and start > 0 else None)


def rows_kernel(lefts, groups, adding, picked, together, side_ref, *refs):
    refs = list(refs)
    held_ref = refs.pop()
    out_refs = refs[-len(picked) :]
    refs = refs[: -len(picked)]
    recv_ref = refs.pop() if adding else None
    step = pl.program_id(0)
    left_refs = []
    for count in lefts:
        left_refs.append(refs[:count])
        refs = refs[count:]
    rights = []
    for _ in groups:
        rights.append(refs[:CHUNKS])
        refs = refs[CHUNKS:]
    rows = left_refs[0][0].shape[0]
    blocks = held_ref.shape[1] // rows

    @pl.when(step == 0)
    def _():
        for which, pieces in enumerate(left_refs):
            for n, ref in enumerate(pieces):
                m, j = n % blocks, n // blocks
                wide = ref.shape[1]
                held_ref[which, m * rows : (m + 1) * rows, j * wide : (j + 1) * wide] = ref[...]

    chunk = held_ref.shape[2] // CHUNKS
    whole_columns = slice(0, out_refs[0].shape[1])

    def give(group, left, columns):
        right = jnp.concatenate([ref[:chunk, :].astype(jnp.bfloat16) for ref in group], 0)
        total = dot32(held_ref[left], right)
        if recv_ref is not None:
            total = total + recv_ref[:, columns]
        for out_ref, parts in zip(out_refs, picked):
            at = 0
            for start, size in parts:
                out_ref[at : at + size, columns] = total[start : start + size]
                at += size

    begin = 0
    for group, (left, first, steps) in zip(rights, groups):
        if together:
            width = group[0].shape[1]
            give(group, left, slice(begin, begin + width))
            begin += width
        else:

            @pl.when((step >= first) & (step < first + steps))
            def _(group=group, left=left):
                give(group, left, whole_columns)


def rows_of(lefts, groups, side, rows, blocks, step, recv=None, picked=None):
    if picked is None:
        picked = [[(0, rows * blocks)]]
    at = lambda m: lambda i, side: ((m ^ side[2]) * side[1] + side[0], 0)
    specs = []
    args = []
    counts = []
    for left in lefts:
        pieces = left if isinstance(left, list) else [left]
        counts.append(len(pieces) * blocks)
        for piece in pieces:
            for m in range(blocks):
                specs.append(pl.BlockSpec((rows, piece.shape[1]), at(m)))
                args.append(piece)
    tokens = sum(piece.shape[1] for piece in pieces)
    first = 0
    plan = []
    together = step is None
    for which, rights in groups:
        if together:
            plan.append((which, 0, 1))
            specs += [whole(right) for right in rights]
            args += rights
            first += rights[0].shape[1]
            continue
        steps = rights[0].shape[1] // step
        plan.append((which, first, steps))
        for right in rights:
            pick = lambda i, side, first=first, steps=steps: (0, jnp.clip(i - first, 0, steps - 1))
            specs.append(pl.BlockSpec((right.shape[0], step), pick))
            args.append(right)
        first += steps
    if together:
        first, step = 1, first
    total = first * step
    block = lambda height: pl.BlockSpec((height, step), lambda i, side: (0, i))
    if recv is not None:
        specs.append(block(rows * blocks))
        args.append(recv)
    heights = [sum(size for _, size in parts) for parts in picked]
    results = pl.pallas_call(
        functools.partial(rows_kernel, counts, plan, recv is not None, picked, together),
        out_shape=[jax.ShapeDtypeStruct((height, total), jnp.float32) for height in heights],
        grid_spec=pltpu.PrefetchScalarGridSpec(
            num_scalar_prefetch=1,
            grid=(first,),
            in_specs=specs,
            out_specs=[block(height) for height in heights],
            scratch_shapes=[pltpu.VMEM((len(lefts), rows * blocks, tokens), jnp.bfloat16)],
        ),
        compiler_params=params(),
        cost_estimate=cost(
            2 * rows * blocks * tokens * total,
            4 * rows * blocks * total + 2 * tokens * (total + rows * blocks),
        ),
    )(side, *args)
    return results[0] if len(picked) == 1 else results


def shards(
    tokens,
    lengths,
    positions,
    cotangent,
    norm_gain,
    w_query,
    w_key,
    w_value,
    w_out,
    mlp_gain,
    w_gate,
    w_up,
    w_down,
):
    seq_rows, depth = tokens.shape
    chips = lax.axis_size("chip")
    dp = chips * 2
    tp = lax.axis_size("tp")
    chip = lax.axis_index("chip")
    core = lax.axis_index("core")
    level = lax.axis_index("tp")
    low = level < 2
    inner = (level == 1) | (level == 2)
    heads_here = w_query.shape[1] // HD
    kv_here = w_key.shape[1] // HD
    rows = seq_rows // CHUNKS
    slice_rows = depth // dp
    level_ref = level.astype(jnp.int32).reshape(1)
    by_hand = dp == 8
    swap = lambda array: lax.ppermute(array, "core", [(0, 1), (1, 0)])
    to_level = lambda array, s: along(array, [(t, t ^ s) for t in range(tp)])

    at_row = (chip * 2 + core) * slice_rows
    cols = lambda w: lax.dynamic_slice_in_dim(w, at_row, slice_rows, 1).astype(jnp.float32).T
    (out_slice,) = fence(cols(w_out))
    qkv_slice = jnp.concatenate(
        [
            lax.dynamic_slice_in_dim(w_query, at_row, slice_rows, 0).astype(jnp.float32),
            cols(w_key.T),
            cols(w_value.T),
        ],
        1,
    )
    out_slice, qkv_slice = fence(out_slice, qkv_slice)
    out_far = [to_level(out_slice, s) for s in (1, 2, 3)]
    qkv_near = along(qkv_slice, PAIRS)
    meta = jnp.stack([chip, core]).astype(jnp.int32)

    pq = place_query(heads_here)
    pkv = place_key_value(kv_here)
    p_all = place_all(heads_here, kv_here)
    strip_one = place_all(GROUP, 1).T
    p_out = place_plain(heads_here)
    strip_out = p_out.T

    half_dim = HD // 2
    freqs = rope_base ** (-(jnp.arange(half_dim).astype(jnp.float32) * 2.0 / HD))
    freqs = jnp.pad(freqs, (0, LANES // 2 - half_dim))
    angles = positions.astype(jnp.float32)[:, None] * jnp.concatenate([freqs, freqs])[None, :]
    cosines = jnp.cos(angles)
    sines = jnp.sin(angles) * jnp.where(jnp.arange(LANES) < LANES // 2, -1.0, 1.0)

    qkv_own, normed_one, own_pad = start(
        tokens, norm_gain, w_query, w_key.T, w_value.T, pq, pkv, cosines, sines
    )

    def far_slices(across, outer):
        return jnp.stack(
            [
                jnp.where(inner, across[1], outer[0]),
                jnp.where(inner, across[0], outer[1]),
            ]
        )

    order = list(reversed(range(CHUNKS)))
    c0, c1, c2, c3 = order
    own, other, across, outer = {}, {}, {}, {}
    part, total, final = {}, {}, {}

    def hop_1(j):
        other[j] = along(own[j], PAIRS)

    def hop_2(j):
        across[j] = along(jnp.concatenate([own[j], other[j]], 1), MIDDLE)

    def hop_3(j):
        outer[j] = along(across[j], OUTWARD)

    coming = {}

    def add_1(j):
        coming[j] = along(part[j], INWARD)

    def add_2(j):
        total[j] = part[j][:rows] + coming[j][:rows]
        coming[j] = along(total[j], MIDDLE)

    def add_3(j, inward, extra=0):
        both = jnp.where(inner, total[j] + coming[j], inward)
        total[j] = jnp.pad(both, ((0, extra), (0, 0)))
        final[j] = along(total[j], PAIRS)
        return final[j][:rows]

    def to_chip(array, m):
        return lax.ppermute(array, "chip", [(i, i ^ m) for i in range(chips)])

    def over_chips_1(piece):
        cut = piece.shape[1] // 2
        one, two = piece[:, :cut], piece[:, cut:]
        return jnp.stack([one, to_chip(one, 1)]), jnp.stack([two, to_chip(two, 2)])

    def over_chips_2(one, two):
        return one, to_chip(one, 2), two, to_chip(two, 1)

    def over_chips_3(one, one_far, two, two_far):
        upper = jnp.stack([one[0], one[1], one_far[0], one_far[1]])
        lower = jnp.stack([two[0], two_far[0], two[1], two_far[1]])
        return jnp.concatenate([upper, lower], 2)

    data = ("chip", "core")
    own[c0] = attend(lengths, qkv_own, strip_out, c0, rows)
    own, qkv_own, out_far = fence(own, qkv_own, out_far)
    hop_1(c0)
    out_far = jnp.stack(out_far)
    out_mine = over_chips_1(out_far) if by_hand else out_far
    own[c1] = attend(lengths, qkv_own, strip_out, c1, rows)
    own[c2] = attend(lengths, qkv_own, strip_out, c2, rows)
    own, other, qkv_own, normed_one, w_out, out_mine, qkv_near = fence(
        own, other, qkv_own, normed_one, w_out, out_mine, qkv_near
    )
    hop_2(c0)
    others = along(jnp.concatenate([own[c1], own[c2]], 0), PAIRS)
    other[c1], other[c2] = others[: rows + EXTRA], others[rows + EXTRA :]
    if by_hand:
        out_mine = over_chips_2(*out_mine)
    else:
        out_mine = lax.all_gather(out_mine, data)
    near_all = lax.all_gather(qkv_near[None], data)
    own[c3] = attend(lengths, qkv_own, strip_out, c3, rows)
    dout, dout_t, normed_one_t = turn(lengths, cotangent, normed_one)
    w_out_t = w_out.T
    own, other, across, dout, dout_t, normed_one_t, w_out_t, out_mine, qkv_near = fence(
        own, other, across, dout, dout_t, normed_one_t, w_out_t, out_mine, qkv_near
    )
    hop_3(c0)
    hop_2(c1)
    hop_1(c3)
    qkv_across = along(jnp.stack([qkv_slice, qkv_near]), MIDDLE)
    if by_hand:
        out_mine = over_chips_3(*out_mine)
        out_theirs = swap(out_mine)
        out_pad, out_plain = spread(
            spread_out_kernel,
            meta,
            w_out_t,
            [p_out],
            out_mine,
            out_theirs,
            [4 * p_out.shape[1], 4 * p_out.shape[0]],
        )
    else:
        plain = [w_out_t] + [
            out_mine[:, s].reshape(depth, -1).astype(jnp.bfloat16) for s in range(tp - 1)
        ]
        out_plain = jnp.concatenate(plain, 1)
        out_pad = jnp.concatenate([dot32(w, p_out).astype(jnp.bfloat16) for w in plain], 1)
    hidden, normed_t, activ, dgate, dup, mlp_part = {}, {}, {}, {}, {}, {}

    def feed(j):
        gathered = (own[j], other[j], across[j], outer[j])
        (hidden[j], normed_t[j], activ[j], dgate[j], dup[j], mlp_part[j], part[j]) = forward_chunk(
            level_ref, gathered, tokens, dout, out_plain, mlp_gain, w_gate, w_up, w_down, j, rows
        )

    own, other[c2], across, outer, out_pad, out_plain = fence(
        own, other[c2], across, outer, out_pad, out_plain
    )
    hop_3(c1)
    hop_2(c2)
    feed(c0)
    own, other, across, outer, part, hidden, qkv_across = fence(
        own, other, across, outer, part, hidden, qkv_across
    )
    add_1(c0)
    qkv_outer = along(qkv_across, OUTWARD)
    hop_3(c2)
    hop_2(c3)
    feed(c1)
    own, other, across, outer, part, coming, hidden, qkv_across, qkv_outer = fence(
        own, other, across, outer, part, coming, hidden, qkv_across, qkv_outer
    )
    far_all = lax.all_gather(far_slices(qkv_across, qkv_outer), data)
    add_1(c1)
    hop_3(c3)
    add_2(c0)
    feed(c2)
    own, other, across, outer, part, total, coming, hidden = fence(
        own, other, across, outer, part, total, coming, hidden
    )
    coming[c2] = add_3(c0, part[c2][:rows])
    add_2(c1)
    feed(c3)
    near_all, far_all, hidden[c3] = fence(near_all, far_all, hidden[c3])
    qkv_pad = spread_qkv(own_pad, pq, pkv, near_all, far_all)
    qkv = project(normed_one, qkv_pad, cosines, sines, qkv_own)

    listed = lambda pieces: [pieces[j] for j in range(CHUNKS)]
    keep_side = jnp.stack([core, 2, 0]).astype(jnp.int32)
    keep_turned = jnp.stack([core, 2, chip]).astype(jnp.int32)
    send_side = jnp.stack([1 - core, 2, 0]).astype(jnp.int32)
    send_turned = jnp.stack([1 - core, 2, chip]).astype(jnp.int32)
    all_rows = jnp.array([0, 1, 0], jnp.int32)

    def send_rows(lefts, groups, step, side=send_side):
        if not by_hand:
            return rows_of(lefts, groups, all_rows, depth // 4, 4, step)
        return rows_of(lefts, groups, side, slice_rows, chips, step)

    def keep_rows(lefts, groups, received, step, side=keep_side, picked=None):
        if not by_hand:
            return received
        return rows_of(lefts, groups, side, slice_rows, chips, step, received, picked)

    def swap_rows(array):
        return swap(array) if by_hand else array

    def scatter(array, axes):
        return lax.psum_scatter(array, axes, scatter_dimension=0, tiled=True)

    units = w_gate.shape[1]
    acc = None
    dhid_t, dqkv_own, input_grad, gains = {}, {}, {}, {}

    def back(j):
        nonlocal acc
        (dhid_t[j], dqkv_own[j], input_grad[j], gains[j]), acc = back_some(j, True)

    def back_own(j):
        return back_some(j, False)[0]

    def back_some(j, full):
        return backward_chunk(
            level_ref,
            (total[j], final[j]),
            hidden[j],
            dout,
            tokens,
            (norm_gain, mlp_gain),
            (out_pad, qkv_pad),
            qkv,
            (own[j], other[j], across[j], outer[j]),
            (p_out, strip_one),
            (cosines, sines),
            acc,
            j,
            rows,
            full,
        )

    own, other, across, outer, part, total, coming, final, hidden, mlp_in, qkv = fence(
        own, other, across, outer, part, total, coming, final, hidden,
        (normed_t, activ, dgate, dup), qkv,
    )
    normed_t, activ, dgate, dup = mlp_in
    coming[c3] = add_3(c1, part[c3][:rows])
    add_2(c2)
    mlp_args = (
        [listed(normed_t), dout_t],
        [(0, listed(dgate)), (0, listed(dup)), (1, listed(activ))],
    )
    grad_mlp = rows_of(*mlp_args, all_rows, depth // 4, 4, units // 2)
    hidden, grad_mlp = fence(hidden, grad_mlp)
    grad_mlp = scatter(grad_mlp, data)
    back(c0)

    near = lambda: jnp.where(low, mlp_part[1], mlp_part[2])
    edge = lambda: jnp.where(low, mlp_part[0], mlp_part[3])
    leave_far = lambda: jnp.where(low, mlp_part[3], mlp_part[0])
    leave_near = lambda: jnp.where(low, mlp_part[2], mlp_part[1])
    total, coming, final, hidden, mlp_part, acc, dhid_t = fence(
        total, coming, final, hidden, mlp_part, acc, dhid_t
    )
    far_sum = add_3(c2, leave_far())
    add_2(c3)
    back(c1)
    total, coming, final, hidden, mlp_part, far_sum, acc, dhid_t = fence(
        total, coming, final, hidden, mlp_part, far_sum, acc, dhid_t
    )
    near_sum = add_3(c3, leave_near(), EXTRA)
    far_in = along(leave_far() + far_sum, MIDDLE)
    back(c2)
    total, final, hidden, mlp_part, near_sum, far_in, acc, dhid_t = fence(
        total, final, hidden, mlp_part, near_sum, far_in, acc, dhid_t
    )
    last = along(jnp.where(inner, edge() + far_in, near()), PAIRS)
    near_in = along(leave_near() + near_sum, MIDDLE)
    dhid_t[c3], dqkv_own[c3] = back_own(c3)
    q_cols = heads_here * HD
    attn_args = (
        [listed(dhid_t), normed_one_t],
        [(0, listed(own)), (1, listed(dqkv_own))],
    )
    sent = swap_rows(send_rows(*attn_args, None, send_turned))
    total, final, hidden, acc, sent = fence(total, final, hidden, acc, sent)
    if by_hand:
        half = slice_rows // 2
        upper = lambda m: (m * slice_rows, half)
        lower = lambda m: (m * slice_rows + half, half)
        picked = [
            [upper(1), upper(3)],
            [upper(0), upper(2)],
            [lower(2), lower(3)],
            [lower(0), lower(1)],
        ]
        pieces = keep_rows(*attn_args, sent, None, keep_turned, picked)
        pieces, hidden = fence(pieces, hidden)
        one_away, one, two_away, two = pieces
        pieces = (one, to_chip(one_away, 1), two, to_chip(two_away, 2))
    else:
        pieces = scatter(sent, ("chip", "core"))
    back(c3)
    pieces, gains, input_grad, last, near_in = fence(pieces, gains, input_grad, last, near_in)
    gain_sums = gains[0] + gains[1] + gains[2] + gains[3]
    gain_sums = gain_sums + swap(gain_sums)
    if by_hand:
        others = [to_chip(gain_sums, m) for m in range(1, chips)]
        gain_sums = sum(others, gain_sums)
        one = pieces[0] + pieces[1]
        two = pieces[2] + pieces[3]
        one = one[:half] + to_chip(one[half:], 2)
        two = two[:half] + to_chip(two[half:], 1)
        attn = jnp.concatenate([one, two], 0)
    else:
        gain_sums = lax.psum(gain_sums, "chip")
        attn = pieces
    gain_rows = lax.dynamic_slice_in_dim(gain_sums, at_row, slice_rows, 1)
    grad_out, grad_qkv = attn[:, :q_cols], attn[:, q_cols:]
    mlp_rows = jnp.where(inner, near() + near_in, edge()) + last
    hidden_rows = jnp.where(
        low,
        jnp.where(level == 0, hidden[0], hidden[1]),
        jnp.where(level == 2, hidden[2], hidden[3]),
    )
    layer_out = (hidden_rows + mlp_rows).astype(jnp.bfloat16)
    one = strip_one.shape[1]
    picked = lambda at, width: jnp.concatenate(
        [grad_qkv[:, kv * one + at : kv * one + at + width] for kv in range(kv_here)], 1
    )
    return (
        layer_out,
        jnp.concatenate(listed(input_grad), 0),
        gain_rows[0],
        picked(0, GROUP * HD),
        picked(GROUP * HD, HD),
        picked((GROUP + 1) * HD, HD),
        grad_out.T,
        gain_rows[1],
        grad_mlp[:, :units],
        grad_mlp[:, units : 2 * units],
        grad_mlp[:, 2 * units :].T,
    )


def solution(mesh):
    devices = mesh.devices
    dp, tp = devices.shape
    split = Mesh(devices.reshape(dp // 2, 2, tp), ("chip", "core", "tp"))
    data = ("chip", "core")
    return jax.shard_map(
        shards,
        mesh=split,
        in_specs=(
            P(data, None),
            P(data),
            P(data),
            P(data, None),
            P(),
            P(None, "tp"),
            P(None, "tp"),
            P(None, "tp"),
            P("tp", None),
            P(),
            P(None, "tp"),
            P(None, "tp"),
            P("tp", None),
        ),
        out_specs=(
            P(("chip", "core", "tp"), None),
            P(data, None),
            P(data),
            P(data, "tp"),
            P(data, "tp"),
            P(data, "tp"),
            P("tp", data),
            P(data),
            P(data, "tp"),
            P(data, "tp"),
            P("tp", data),
        ),
        check_vma=False,
    )
```

```python
import functools

import jax
import jax.numpy as jnp
from jax import lax
from jax.experimental import pallas as pl
from jax.experimental.pallas import tpu as pltpu
from jax.sharding import Mesh
from jax.sharding import PartitionSpec as P

HD = 96
LANES = 128
GROUP = 2
KV_WIDE = (GROUP + 2) * LANES
rope_base = 100000.0
norm_eps = 1e-05
masked_score = -1e30
far_away = 1e30
score_scale = HD ** (-0.5)
score_scale_log2 = score_scale * 1.4426950408889634
CHUNKS = 4
EXTRA = 8
VMEM_BYTES = 56 * 1024 * 1024
NT = (((1,), (1,)), ((), ()))


def params():
    return pltpu.CompilerParams(vmem_limit_bytes=VMEM_BYTES)


def cost(flops, moved, exps=0):
    return pl.CostEstimate(
        flops=flops // 1024, bytes_accessed=moved // 1024, transcendentals=exps // 1024
    )


def dot32(a, b):
    return jnp.dot(a, b, preferred_element_type=jnp.float32)


def dot32_nt(a, b):
    return lax.dot_general(a, b, NT, preferred_element_type=jnp.float32)


def dot_split(a, places):
    high = a.astype(jnp.bfloat16)
    rest = (a - high.astype(jnp.float32)).astype(jnp.bfloat16)
    return dot32(high, places) + dot32(rest, places)


def fence(*trees):
    return lax.optimization_barrier(trees)


def whole(array, buffers=None):
    zeros = (0,) * len(array.shape)
    return pl.BlockSpec(array.shape, lambda *_: zeros)


SCALAR = pl.BlockSpec(memory_space=pltpu.SMEM)


def halves(entry):
    half_dim = HD // 2
    return (entry // half_dim) * (LANES // 2) + entry % half_dim


def placement(lanes, width):
    return (lanes[:, None] == jnp.arange(width)[None, :]).astype(jnp.bfloat16)


def place_query(heads):
    source = jnp.arange(heads * HD)
    return placement((source // HD) * LANES + halves(source % HD), heads * LANES)


def place_key_value(kv_heads):
    source = jnp.arange(kv_heads * HD)
    head = source // HD
    keys = head * 2 * LANES + halves(source % HD)
    values = head * 2 * LANES + LANES + source % HD
    return placement(jnp.concatenate([keys, values]), kv_heads * 2 * LANES)


def place_all(heads, kv_heads):
    source = jnp.arange(heads * HD)
    head = source // HD
    query = (head // GROUP) * KV_WIDE + (head % GROUP) * LANES + halves(source % HD)
    source = jnp.arange(kv_heads * HD)
    base = (source // HD) * KV_WIDE + GROUP * LANES
    keys = base + halves(source % HD)
    values = base + LANES + source % HD
    return placement(jnp.concatenate([query, keys, values]), kv_heads * KV_WIDE)


def place_plain(heads):
    source = jnp.arange(heads * HD)
    return placement((source // HD) * LANES + source % HD, heads * LANES)


PAIRS = [(0, 1), (1, 0), (2, 3), (3, 2)]
INWARD = [(0, 1), (3, 2)]
MIDDLE = [(1, 2), (2, 1)]
OUTWARD = [(1, 0), (2, 3)]


def along(part, pairs):
    return lax.ppermute(part, "tp", pairs)


def chosen(refs, low):
    return refs[0][...] if len(refs) == 1 else jnp.where(low, refs[0][...], refs[1][...])


def sums_kernel(inwards, level_ref, total_ref, coming_ref, *refs):
    level = level_ref[0]
    inner = (level == 1) | (level == 2)
    low = level < 2
    pair_ref, middle_ref = refs[-2:]
    inward_refs, add_refs, other_ref = refs[:inwards], refs[inwards:-3], refs[-3]
    summed = total_ref[...] + coming_ref[...]
    pair_ref[...] = jnp.where(inner, summed, chosen(inward_refs, low))
    middle_ref[...] = chosen(add_refs, low) + other_ref[...]


def hop_sums(level, total, coming, inward, add, other, rows):
    depth = total.shape[1]
    shape = jax.ShapeDtypeStruct((rows, depth), jnp.float32)
    block = pl.BlockSpec((rows // 4, depth), lambda i: (i, 0))
    args = [total, coming, *inward, *add, other]
    return pl.pallas_call(
        functools.partial(sums_kernel, len(inward)),
        out_shape=[shape, shape],
        grid=(4,),
        in_specs=[SCALAR] + [block] * len(args),
        out_specs=[block, block],
        compiler_params=params(),
        cost_estimate=cost(4 * rows * depth, 28 * rows * depth),
    )(level, *args)


def far_slices_kernel(level_ref, near_ref, across_ref, outer_ref, out_ref):
    inner = (level_ref[0] == 1) | (level_ref[0] == 2)
    out_ref[0] = near_ref[...]
    out_ref[1] = jnp.where(inner, across_ref[1], outer_ref[0])
    out_ref[2] = jnp.where(inner, across_ref[0], outer_ref[1])


def far_slices(level, near, across, outer):
    shape = jax.ShapeDtypeStruct((3, *near.shape), jnp.float32)
    return pl.pallas_call(
        far_slices_kernel,
        out_shape=shape,
        grid=(1,),
        in_specs=[SCALAR, whole(near), whole(across), whole(outer)],
        out_specs=whole(shape),
        compiler_params=params(),
        cost_estimate=cost(0, 32 * near.shape[0] * near.shape[1]),
    )(level, near, across, outer)


def store_qkv(out_ref, here, base, query, key_value):
    wide = GROUP * LANES
    for kv in range(key_value.shape[1] // (2 * LANES)):
        at = base + kv * KV_WIDE
        there = slice(kv * 2 * LANES, (kv + 1) * 2 * LANES)
        out_ref[here, at : at + wide] = query[:, kv * wide : (kv + 1) * wide]
        out_ref[here, at + wide : at + KV_WIDE] = key_value[:, there]


def store_turned(out_ref, at, lin, cos_ref, sin_ref):
    for h in range(GROUP + 2):
        one = lin[:, h * LANES : (h + 1) * LANES]
        if h < GROUP + 1:
            one = one * cos_ref[...] + pltpu.roll(one, LANES // 2, 1) * sin_ref[...]
        out_ref[:, at + h * LANES : at + (h + 1) * LANES] = one.astype(jnp.bfloat16)


def spread_out_kernel(meta_ref, own_ref, p_ref, mine_ref, theirs_ref, pad_ref, plain_ref):
    rows, width = mine_ref.shape[2:]
    wide = p_ref.shape[1]
    for side, ref in enumerate((mine_ref, theirs_ref)):
        here = pl.ds(pl.multiple_of((meta_ref[1] ^ side) * rows, rows), rows)
        for s in range(4):
            block = own_ref[here, :] if s == 0 else ref[0, s - 1].astype(jnp.bfloat16)
            plain_ref[here, s * width : (s + 1) * width] = block
            pad_ref[here, s * wide : (s + 1) * wide] = dot32(block, p_ref[...]).astype(
                jnp.bfloat16
            )


def spread_qkv_kernel(pq_ref, pkv_ref, far_ref, _, out_ref):
    parts, _, rows, width = far_ref.shape
    split = pq_ref.shape[0]
    block = far_ref[:, 0].reshape(parts * rows, width).astype(jnp.bfloat16)
    query = dot32(block[:, :split], pq_ref[...]).astype(jnp.bfloat16)
    key_value = dot32(block[:, split:], pkv_ref[...]).astype(jnp.bfloat16)
    store_qkv(out_ref, slice(None), 0, query, key_value)


def spread_qkv(padded, pq, pkv, far):
    total = padded.shape[0]
    dp, others, rows, width = far.shape
    wide = padded.shape[1] // (others + 1)
    parts = max(1, dp // 2)
    block = parts * rows
    return pl.pallas_call(
        spread_qkv_kernel,
        out_shape=jax.ShapeDtypeStruct(padded.shape, jnp.bfloat16),
        grid=(total // block, others),
        in_specs=[
            whole(pq),
            whole(pkv),
            pl.BlockSpec((parts, 1, rows, width), lambda i, s: (i, s, 0, 0)),
            pl.BlockSpec(memory_space=pl.ANY),
        ],
        out_specs=pl.BlockSpec((block, wide), lambda i, s: (i, s + 1)),
        input_output_aliases={3: 0},
        compiler_params=params(),
        cost_estimate=cost(8 * total * width * 512, 20 * total * wide),
    )(pq, pkv, far, padded)


def spread(kernel, meta, own, places, mine, theirs, widths):
    chips, others, rows, width = mine.shape
    total = own.shape[0]
    row_block = lambda m, meta: (meta[0] ^ m, 0)
    piece = pl.BlockSpec((1, others, rows, width), lambda m, meta: (m, 0, 0, 0))
    return pl.pallas_call(
        kernel,
        out_shape=[jax.ShapeDtypeStruct((total, wide), jnp.bfloat16) for wide in widths],
        grid_spec=pltpu.PrefetchScalarGridSpec(
            num_scalar_prefetch=1,
            grid=(chips,),
            in_specs=[pl.BlockSpec((2 * rows, own.shape[1]), row_block)]
            + [whole(place) for place in places]
            + [piece, piece],
            out_specs=[pl.BlockSpec((2 * rows, wide), row_block) for wide in widths],
        ),
        compiler_params=params(),
        cost_estimate=cost(
            8 * total * width * 512, total * (12 * width + 2 * sum(widths))
        ),
    )(meta, own, *places, mine, theirs)


def start_kernel(x_ref, gain_ref, q_ref, k_ref, v_ref, pq_ref, pkv_ref, cos_ref, sin_ref, *outs):
    qkv_ref, normed_ref, pad_ref = outs

    @pl.when(pl.program_id(0) == 0)
    def _():
        split = k_ref.shape[0]
        query = dot32(q_ref[...], pq_ref[...]).astype(jnp.bfloat16)
        key_value = dot32(k_ref[...].T, pkv_ref[:split, :])
        key_value = key_value + dot32(v_ref[...].T, pkv_ref[split:, :])
        store_qkv(pad_ref, slice(None), 0, query, key_value.astype(jnp.bfloat16))

    inputs = x_ref[...].astype(jnp.float32)
    rms = lax.rsqrt(jnp.mean(inputs * inputs, -1, keepdims=True) + norm_eps)
    normed = (inputs * rms * gain_ref[...]).astype(jnp.bfloat16)
    normed_ref[...] = normed
    for kv in range(pad_ref.shape[1] // KV_WIDE):
        at = kv * KV_WIDE
        store_turned(qkv_ref, at, dot32(normed, pad_ref[:, at : at + KV_WIDE]), cos_ref, sin_ref)


def start(tokens, gain, w_query, w_key_t, w_value_t, pq, pkv, cosines, sines):
    total, depth = tokens.shape
    rows = total // CHUNKS
    wide = pq.shape[1] + pkv.shape[1]
    gain = gain[None, :]
    by_rows = lambda width: pl.BlockSpec((rows, width), lambda i: (i, 0))
    arrays = [w_query, w_key_t, w_value_t, pq, pkv]
    shapes = [
        jax.ShapeDtypeStruct((total, 4 * wide), jnp.bfloat16),
        jax.ShapeDtypeStruct((total, depth), jnp.bfloat16),
        jax.ShapeDtypeStruct((depth, 4 * wide), jnp.bfloat16),
    ]
    return pl.pallas_call(
        start_kernel,
        out_shape=shapes,
        grid=(CHUNKS,),
        in_specs=[by_rows(depth), whole(gain)]
        + [whole(array) for array in arrays]
        + [by_rows(LANES), by_rows(LANES)],
        out_specs=[
            by_rows(wide),
            by_rows(depth),
            pl.BlockSpec((depth, wide), lambda i: (0, 0)),
        ],
        compiler_params=params(),
        cost_estimate=cost(2 * total * depth * wide, 12 * total * depth),
    )(tokens, gain, *arrays, cosines, sines)


def turn_kernel(length_ref, cot_ref, normed_ref, dout_ref, dout_t_ref, normed_t_ref):
    rows = cot_ref.shape[0]
    at = pl.program_id(0) * rows + lax.broadcasted_iota(jnp.int32, cot_ref.shape, 0)
    dout = jnp.where(at < length_ref[0], cot_ref[...].astype(jnp.float32), 0.0)
    dout = dout.astype(jnp.bfloat16)
    dout_ref[...] = dout
    dout_t_ref[...] = dout.T
    normed_t_ref[...] = normed_ref[...].T


def turn(length, cotangent, normed):
    total, depth = cotangent.shape
    rows = total // CHUNKS
    by_rows = pl.BlockSpec((rows, depth), lambda i: (i, 0))
    by_columns = pl.BlockSpec((depth, rows), lambda i: (0, i))
    turned = jax.ShapeDtypeStruct((depth, total), jnp.bfloat16)
    return pl.pallas_call(
        turn_kernel,
        out_shape=[jax.ShapeDtypeStruct((total, depth), jnp.bfloat16), turned, turned],
        grid=(CHUNKS,),
        in_specs=[SCALAR, by_rows, by_rows],
        out_specs=[by_rows, by_columns, by_columns],
        compiler_params=params(),
        cost_estimate=cost(total * depth, 10 * total * depth),
    )(length, cotangent, normed)


def project_kernel(x_ref, w_ref, cos_ref, sin_ref, _, out_ref):
    store_turned(out_ref, 0, dot32(x_ref[...], w_ref[...]), cos_ref, sin_ref)


def project(normed, weights, cosines, sines, qkv):
    rows, depth = normed.shape
    width = weights.shape[1]
    steps = width // KV_WIDE
    first = steps // 4
    return pl.pallas_call(
        project_kernel,
        out_shape=jax.ShapeDtypeStruct((rows, width), jnp.bfloat16),
        grid=(steps - first,),
        in_specs=[
            whole(normed),
            pl.BlockSpec((depth, KV_WIDE), lambda i: (0, i + first)),
            whole(cosines),
            whole(sines),
            pl.BlockSpec(memory_space=pl.ANY),
        ],
        out_specs=pl.BlockSpec((rows, KV_WIDE), lambda i: (0, i + first)),
        input_output_aliases={4: 0},
        compiler_params=params(),
        cost_estimate=cost(
            2 * rows * depth * width, 2 * (rows * depth + depth * width + rows * width)
        ),
    )(normed, weights, cosines, sines, qkv)


def attend_kernel(start, length_ref, q_ref, kv_ref, strip_ref, out_ref):
    rows = q_ref.shape[0]
    keys = kv_ref.shape[0]
    length = length_ref[0]
    row_ids = start + lax.broadcasted_iota(jnp.int32, (1, rows), 1)
    limit = jnp.minimum(row_ids, length - 1)
    allowed = lax.broadcasted_iota(jnp.int32, (keys, rows), 0) <= limit
    mixed = []
    sums = []
    for kv in range(kv_ref.shape[1] // KV_WIDE):
        base = kv * KV_WIDE
        at = base + GROUP * LANES
        key = kv_ref[:, at : at + LANES]
        value_t = kv_ref[:, at + LANES : at + 2 * LANES].T
        for g in range(GROUP):
            query = q_ref[:, base + g * LANES : base + (g + 1) * LANES]
            raw = jnp.where(allowed, dot32_nt(key, query), masked_score)
            peak = jnp.max(raw, axis=0, keepdims=True)
            expo = jnp.exp2((raw - peak) * score_scale_log2)
            total = jnp.sum(expo, axis=0, keepdims=True)
            probs = (expo * (1.0 / total)).astype(jnp.bfloat16)
            mixed.append(dot32(value_t, probs).T)
            log_sum = peak * score_scale_log2 + jnp.log2(total)
            sums.append(jnp.where(row_ids < length, log_sum, far_away))
    out_ref[:rows, :] = dot_split(jnp.concatenate(mixed, 1), strip_ref[...])
    out_ref[rows:, :] = jnp.zeros((EXTRA, out_ref.shape[1]), jnp.float32)
    out_ref[rows : rows + len(sums), :rows] = jnp.concatenate(sums, 0)


def attend(length, qkv, strip, index, rows):
    keys = (index + 1) * rows
    width = qkv.shape[1] // 4
    heads = width // KV_WIDE * GROUP
    shape = (rows + EXTRA, strip.shape[1])
    return pl.pallas_call(
        functools.partial(attend_kernel, index * rows),
        out_shape=jax.ShapeDtypeStruct(shape, jnp.float32),
        grid=(1,),
        in_specs=[
            SCALAR,
            pl.BlockSpec((rows, width), lambda i: (index, 0)),
            pl.BlockSpec((keys, width), lambda i: (0, 0)),
            whole(strip),
        ],
        out_specs=pl.BlockSpec(shape, lambda i: (0, 0)),
        compiler_params=params(),
        cost_estimate=cost(
            4 * heads * rows * keys * LANES, 2 * (rows + keys) * width, heads * rows * keys
        ),
    )(length, qkv, qkv, strip)


def forward_kernel(level_ref, part_ref, other_ref, across_ref, outer_ref, *refs):
    x_ref, dout_ref, wo_ref, gain_ref, wg_ref, wu_ref, wd_ref = refs[:7]
    hidden_ref, normed_t_ref, activ_ref, dgate_ref, dup_ref, mlp_ref, dn_ref = refs[7:14]
    normed_ref = refs[14]
    rows = x_ref.shape[0]

    @pl.when(pl.program_id(0) == 0)
    def _():
        level = level_ref[0]
        inner = (level == 1) | (level == 2)
        width = part_ref.shape[1]
        second = jnp.where(inner, across_ref[:rows, width:], outer_ref[:rows, :width])
        third = jnp.where(inner, across_ref[:rows, :width], outer_ref[:rows, width:])
        mixed = jnp.concatenate([part_ref[:rows, :], other_ref[:rows, :], second, third], 1)
        hidden = x_ref[...].astype(jnp.float32) + dot32_nt(mixed.astype(jnp.bfloat16), wo_ref[...])
        hidden_ref[...] = hidden
        rms = lax.rsqrt(jnp.mean(hidden * hidden, -1, keepdims=True) + norm_eps)
        normed = (hidden * rms * gain_ref[...]).astype(jnp.bfloat16)
        normed_ref[...] = normed
        normed_t_ref[...] = normed.T
        mlp_ref[...] = jnp.zeros_like(mlp_ref)
        dn_ref[...] = jnp.zeros_like(dn_ref)

    normed = normed_ref[...]
    gate = dot32(normed, wg_ref[...])
    up = dot32(normed, wu_ref[...])
    dact = dot32_nt(dout_ref[...], wd_ref[...])
    sigmoid = jax.nn.sigmoid(gate)
    silu = gate * sigmoid
    activ = (silu * up).astype(jnp.bfloat16)
    dgate = (dact * up * sigmoid * (1.0 + gate * (1.0 - sigmoid))).astype(jnp.bfloat16)
    dup = (dact * silu).astype(jnp.bfloat16)
    activ_ref[...] = activ
    dgate_ref[...] = dgate
    dup_ref[...] = dup
    mlp_ref[...] += dot32(activ, wd_ref[...])
    dn_ref[:rows, :] += dot32_nt(dgate, wg_ref[...]) + dot32_nt(dup, wu_ref[...])


def forward_chunk(level, gathered, tokens, dout, w_out, gain, w_gate, w_up, w_down, index, rows):
    depth = tokens.shape[1]
    units = w_gate.shape[1]
    block = 512
    own_rows = pl.BlockSpec((rows, depth), lambda i: (index, 0))
    by_units = pl.BlockSpec((depth, block), lambda i: (0, i))
    gain = gain[None, :]
    f32, bf16 = jnp.float32, jnp.bfloat16
    outs = [
        jax.ShapeDtypeStruct((rows, depth), f32),
        jax.ShapeDtypeStruct((depth, rows), bf16),
        jax.ShapeDtypeStruct((rows, units), bf16),
        jax.ShapeDtypeStruct((rows, units), bf16),
        jax.ShapeDtypeStruct((rows, units), bf16),
        jax.ShapeDtypeStruct((rows, depth), f32),
        jax.ShapeDtypeStruct((rows + EXTRA, depth), f32),
    ]
    unit_out = pl.BlockSpec((rows, block), lambda i: (0, i))
    return pl.pallas_call(
        forward_kernel,
        out_shape=outs,
        grid=(units // block,),
        in_specs=[SCALAR]
        + [whole(array) for array in gathered]
        + [own_rows, own_rows, whole(w_out), whole(gain), by_units, by_units]
        + [pl.BlockSpec((block, depth), lambda i: (i, 0))],
        out_specs=[
            whole(outs[0]),
            whole(outs[1]),
            unit_out,
            unit_out,
            unit_out,
            whole(outs[5]),
            whole(outs[6]),
        ],
        scratch_shapes=[pltpu.VMEM((rows, depth), bf16)],
        compiler_params=params(),
        cost_estimate=cost(
            2 * rows * depth * (6 * units + w_out.shape[1]),
            2 * depth * (3 * units + w_out.shape[1]) + 22 * rows * depth,
            rows * units,
        ),
    )(level, *gathered, tokens, dout, w_out, gain, w_gate, w_up, w_down)


def hidden_grad(inner, total_ref, final_ref, hidden_ref, dout_ref, gain_ref):
    dnormed = jnp.where(inner, total_ref[...], final_ref[...])
    hidden = hidden_ref[...]
    rms = lax.rsqrt(jnp.mean(hidden * hidden, -1, keepdims=True) + norm_eps)
    scaled = dnormed * gain_ref[...]
    shift = jnp.mean(scaled * hidden, -1, keepdims=True)
    dhid = dout_ref[...].astype(jnp.float32) + (rms * scaled - hidden * (rms**3 * shift))
    return dhid, dnormed * (hidden * rms)


def backward_kernel(start, full, level_ref, total_ref, final_ref, hidden_ref, dout_ref, x_ref, *refs):
    gain_one_ref, gain_two_ref, wo_ref, q_ref = refs[:4]
    kv_here = q_ref.shape[1] // KV_WIDE
    refs = refs[4:]
    kv_refs, refs = refs[: 2 * kv_here], refs[2 * kv_here :]
    part_ref, other_ref, across_ref, outer_ref, place_ref, strip_ref = refs[:6]
    cos_ref, sin_ref = refs[6:8]
    dhid_ref, low_ref, dn_ref = refs[-3:]
    outs = refs[8:-3]
    if full:
        w_ref, outs = outs[0], outs[1:]
    count = (5 if start > 0 else 4) if full else 2
    acc_ref = outs[0] if len(outs) > count else None
    outs = outs[-count:]
    dhid_t_ref, dqkv_ref = outs[:2]
    if full:
        input_grad_ref, gains_ref = outs[2:4]
    rows = q_ref.shape[0]
    keys = kv_refs[0].shape[0]
    shard = pl.program_id(0)
    level = level_ref[0]
    inner = (level == 1) | (level == 2)

    @pl.when(shard == 0)
    def _():
        dhid, dgain = hidden_grad(
            inner, total_ref, final_ref, hidden_ref, dout_ref, gain_two_ref
        )
        dhid_ref[...] = dhid
        low = dhid.astype(jnp.bfloat16)
        low_ref[...] = low
        dhid_t_ref[...] = low.T
        if full:
            gains_ref[...] = jnp.zeros_like(gains_ref)
            gains_ref[1:2, :] = jnp.sum(dgain, 0, keepdims=True)
            dn_ref[...] = jnp.zeros_like(dn_ref)

    def rotate_back(grads):
        turned = grads * cos_ref[...] - pltpu.roll(grads, LANES // 2, 1) * sin_ref[...]
        return turned.astype(jnp.bfloat16)

    dmixed_all = dot32(low_ref[...], wo_ref[...]).astype(jnp.bfloat16)
    mixed = jnp.where(
        shard == 0,
        part_ref[...],
        jnp.where(shard == 1, other_ref[...], jnp.where(inner, across_ref[...], outer_ref[...])),
    )
    products = dmixed_all.astype(jnp.float32) * dot_split(mixed[:rows], place_ref[...])
    causal = lax.broadcasted_iota(jnp.int32, (rows, rows), 0) <= lax.broadcasted_iota(
        jnp.int32, (rows, rows), 1
    )
    grads = []
    for kv in range(kv_here):
        key_ref, value_ref = kv_refs[2 * kv : 2 * kv + 2]
        heads = range(kv * GROUP, (kv + 1) * GROUP)
        lanes = {h: slice(h * LANES, (h + 1) * LANES) for h in heads}
        row_dots = {h: jnp.sum(products[:, lanes[h]].T, axis=0, keepdims=True) for h in heads}
        log_sums = {h: mixed[rows + h : rows + h + 1, :rows] for h in heads}
        dqueries = dict.fromkeys(heads)
        here = slice(2 * kv * LANES, (2 * kv + 1) * LANES)
        there = slice((2 * kv + 1) * LANES, (2 * kv + 2) * LANES)
        for tile in range(keys // rows):
            span = slice(tile * rows, (tile + 1) * rows)
            key = key_ref[span, :]
            value = value_ref[span, :]
            key_t = key.T
            dkey = None if acc_ref is None else acc_ref[span, here]
            dvalue = None if acc_ref is None else acc_ref[span, there]
            last = tile * rows == start
            for h in heads:
                at = kv * KV_WIDE + (h % GROUP) * LANES
                query = q_ref[:, at : at + LANES]
                dmixed = dmixed_all[:, lanes[h]]
                raw = dot32_nt(key, query)
                probs = jnp.exp2(raw * score_scale_log2 - log_sums[h])
                if last:
                    probs = jnp.where(causal, probs, 0.0)
                dprobs = dot32_nt(value, dmixed)
                dscores = (probs * (dprobs - row_dots[h])).astype(jnp.bfloat16)
                dquery = dot32(key_t, dscores)
                dqueries[h] = dquery if dqueries[h] is None else dqueries[h] + dquery
                dkey_one = dot32(dscores, query)
                dvalue_one = dot32(probs.astype(jnp.bfloat16), dmixed)
                dkey = dkey_one if dkey is None else dkey + dkey_one
                dvalue = dvalue_one if dvalue is None else dvalue + dvalue_one
            if full and not last:
                outs[4][span, here] = dkey
                outs[4][span, there] = dvalue
        grads += [rotate_back(dqueries[h].T * score_scale) for h in heads]
        grads.append(rotate_back(dkey * score_scale))
        grads.append(dvalue.astype(jnp.bfloat16))
    grads = jnp.concatenate(grads, 1)
    if full:
        dn_ref[...] += dot32_nt(grads, w_ref[...])

    @pl.when(shard == 0)
    def _():
        wide = strip_ref.shape[1]
        for kv in range(kv_here):
            dqkv_ref[:, kv * wide : (kv + 1) * wide] = dot32(
                grads[:, kv * KV_WIDE : (kv + 1) * KV_WIDE], strip_ref[...]
            ).astype(jnp.bfloat16)

    if not full:
        return

    @pl.when(shard == pl.num_programs(0) - 1)
    def _():
        dnormed = dn_ref[...]
        inputs = x_ref[...].astype(jnp.float32)
        rms = lax.rsqrt(jnp.mean(inputs * inputs, -1, keepdims=True) + norm_eps)
        scaled = dnormed * gain_one_ref[...]
        shift = jnp.mean(scaled * inputs, -1, keepdims=True)
        grad = dhid_ref[...] + (rms * scaled - inputs * (rms**3 * shift))
        input_grad_ref[...] = grad.astype(jnp.bfloat16)
        gains_ref[0:1, :] = jnp.sum(dnormed * (inputs * rms), 0, keepdims=True)


def backward_chunk(
    level, sums_two, hidden, dout, tokens, gains, weights, qkv, gathered, places, tables, acc,
    index, rows, full=True
):
    start = index * rows
    keys = start + rows
    depth = tokens.shape[1]
    out_pad, qkv_pad = weights
    place_out, strip = places
    far_rows, width = gathered[0].shape
    out_wide = place_out.shape[1]
    kv_here = out_wide // (GROUP * LANES)
    wide = kv_here * KV_WIDE
    levels = qkv.shape[1] // wide
    own_rows = pl.BlockSpec((rows, depth), lambda t: (index, 0))
    table = pl.BlockSpec((rows, LANES), lambda t: (index, 0))
    gains = [gain[None, :] for gain in gains]
    key_value = lambda at: pl.BlockSpec(
        (keys, LANES), lambda t: (0, (wide // LANES) * t + at)
    )
    across = pl.BlockSpec((far_rows, width), lambda t: (0, jnp.where(t == 2, 1, 0)))
    outer = pl.BlockSpec((far_rows, width), lambda t: (0, jnp.where(t == 3, 1, 0)))
    in_specs = [
        SCALAR,
        whole(hidden),
        whole(hidden),
        whole(hidden),
        own_rows,
        own_rows,
        whole(gains[0]),
        whole(gains[1]),
        pl.BlockSpec((depth, out_wide), lambda t: (0, t)),
        pl.BlockSpec((rows, wide), lambda t: (index, t)),
    ]
    for kv in range(kv_here):
        at = kv * (KV_WIDE // LANES) + GROUP
        in_specs += [key_value(at), key_value(at + 1)]
    in_specs += [
        whole(gathered[0]),
        whole(gathered[1]),
        across,
        outer,
        whole(place_out),
        whole(strip),
        table,
        table,
    ]
    args = [level, *sums_two, hidden, dout, tokens, *gains, out_pad]
    args += [qkv] * (1 + 2 * kv_here)
    args += [*gathered, place_out, strip, *tables]
    sums_wide = 2 * kv_here * LANES
    if full:
        in_specs.append(pl.BlockSpec((depth, wide), lambda t: (0, t)))
        args.append(qkv_pad)
    if acc is not None:
        in_specs.append(pl.BlockSpec((keys, sums_wide), lambda t: (0, t)))
        args.append(acc)
    f32, bf16 = jnp.float32, jnp.bfloat16
    outs = [
        jax.ShapeDtypeStruct((depth, rows), bf16),
        jax.ShapeDtypeStruct((rows, kv_here * strip.shape[1]), bf16),
        jax.ShapeDtypeStruct((rows, depth), bf16),
        jax.ShapeDtypeStruct((8, depth), f32),
    ]
    outs = outs if full else outs[:2]
    out_specs = [whole(out) for out in outs]
    if full and start > 0:
        outs.append(jax.ShapeDtypeStruct((start, levels * sums_wide), f32))
        out_specs.append(pl.BlockSpec((start, sums_wide), lambda t: (0, t)))
    results = pl.pallas_call(
        functools.partial(backward_kernel, start, full),
        out_shape=outs,
        grid=(levels if full else 1,),
        in_specs=in_specs,
        out_specs=out_specs,
        scratch_shapes=[
            pltpu.VMEM((rows, depth), f32),
            pltpu.VMEM((rows, depth), bf16),
            pltpu.VMEM((rows, depth), f32),
        ],
        compiler_params=params(),
        cost_estimate=cost(
            levels * rows * (20 * kv_here * keys * LANES + 2 * depth * (out_wide + wide)),
            2 * depth * levels * (out_wide + wide) + 16 * rows * depth,
            levels * kv_here * GROUP * rows * keys,
        ),
    )(*args)
    return results[:4], (results[4] if full and start > 0 else None)


def rows_kernel(lefts, groups, adding, picked, together, side_ref, *refs):
    refs = list(refs)
    held_ref = refs.pop()
    out_refs = refs[-len(picked) :]
    refs = refs[: -len(picked)]
    recv_ref = refs.pop() if adding else None
    step = pl.program_id(0)
    left_refs = []
    for count in lefts:
        left_refs.append(refs[:count])
        refs = refs[count:]
    rights = []
    for _ in groups:
        rights.append(refs[:CHUNKS])
        refs = refs[CHUNKS:]
    rows = left_refs[0][0].shape[0]
    blocks = held_ref.shape[1] // rows

    @pl.when(step == 0)
    def _():
        for which, pieces in enumerate(left_refs):
            for n, ref in enumerate(pieces):
                m, j = n % blocks, n // blocks
                wide = ref.shape[1]
                held_ref[which, m * rows : (m + 1) * rows, j * wide : (j + 1) * wide] = ref[...]

    chunk = held_ref.shape[2] // CHUNKS
    whole_columns = slice(0, out_refs[0].shape[1])

    def give(group, left, columns):
        right = jnp.concatenate([ref[:chunk, :].astype(jnp.bfloat16) for ref in group], 0)
        total = dot32(held_ref[left], right)
        if recv_ref is not None:
            total = total + recv_ref[:, columns]
        for out_ref, parts in zip(out_refs, picked):
            at = 0
            for start, size in parts:
                out_ref[at : at + size, columns] = total[start : start + size]
                at += size

    begin = 0
    for group, (left, first, steps) in zip(rights, groups):
        if together:
            width = group[0].shape[1]
            give(group, left, slice(begin, begin + width))
            begin += width
        else:

            @pl.when((step >= first) & (step < first + steps))
            def _(group=group, left=left):
                give(group, left, whole_columns)


def rows_of(lefts, groups, side, rows, blocks, step, recv=None, picked=None):
    if picked is None:
        picked = [[(0, rows * blocks)]]
    at = lambda m: lambda i, side: ((m ^ side[2]) * side[1] + side[0], 0)
    specs = []
    args = []
    counts = []
    for left in lefts:
        pieces = left if isinstance(left, list) else [left]
        counts.append(len(pieces) * blocks)
        for piece in pieces:
            for m in range(blocks):
                specs.append(pl.BlockSpec((rows, piece.shape[1]), at(m)))
                args.append(piece)
    tokens = sum(piece.shape[1] for piece in pieces)
    first = 0
    plan = []
    together = step is None
    for which, rights in groups:
        if together:
            plan.append((which, 0, 1))
            specs += [whole(right) for right in rights]
            args += rights
            first += rights[0].shape[1]
            continue
        steps = rights[0].shape[1] // step
        plan.append((which, first, steps))
        for right in rights:
            pick = lambda i, side, first=first, steps=steps: (0, jnp.clip(i - first, 0, steps - 1))
            specs.append(pl.BlockSpec((right.shape[0], step), pick))
            args.append(right)
        first += steps
    if together:
        first, step = 1, first
    total = first * step
    block = lambda height: pl.BlockSpec((height, step), lambda i, side: (0, i))
    if recv is not None:
        specs.append(block(rows * blocks))
        args.append(recv)
    heights = [sum(size for _, size in parts) for parts in picked]
    results = pl.pallas_call(
        functools.partial(rows_kernel, counts, plan, recv is not None, picked, together),
        out_shape=[jax.ShapeDtypeStruct((height, total), jnp.float32) for height in heights],
        grid_spec=pltpu.PrefetchScalarGridSpec(
            num_scalar_prefetch=1,
            grid=(first,),
            in_specs=specs,
            out_specs=[block(height) for height in heights],
            scratch_shapes=[pltpu.VMEM((len(lefts), rows * blocks, tokens), jnp.bfloat16)],
        ),
        compiler_params=params(),
        cost_estimate=cost(
            2 * rows * blocks * tokens * total,
            4 * rows * blocks * total + 2 * tokens * (total + rows * blocks),
        ),
    )(side, *args)
    return results[0] if len(picked) == 1 else results


def shards(
    tokens,
    lengths,
    positions,
    cotangent,
    norm_gain,
    w_query,
    w_key,
    w_value,
    w_out,
    mlp_gain,
    w_gate,
    w_up,
    w_down,
):
    seq_rows, depth = tokens.shape
    chips = lax.axis_size("chip")
    dp = chips * 2
    tp = lax.axis_size("tp")
    chip = lax.axis_index("chip")
    core = lax.axis_index("core")
    level = lax.axis_index("tp")
    low = level < 2
    inner = (level == 1) | (level == 2)
    heads_here = w_query.shape[1] // HD
    kv_here = w_key.shape[1] // HD
    rows = seq_rows // CHUNKS
    slice_rows = depth // dp
    level_ref = level.astype(jnp.int32).reshape(1)
    by_hand = dp == 8
    swap = lambda array: lax.ppermute(array, "core", [(0, 1), (1, 0)])
    to_level = lambda array, s: along(array, [(t, t ^ s) for t in range(tp)])

    at_row = (chip * 2 + core) * slice_rows
    cols = lambda w: lax.dynamic_slice_in_dim(w, at_row, slice_rows, 1).astype(jnp.float32).T
    (out_slice,) = fence(cols(w_out))
    qkv_slice = jnp.concatenate(
        [
            lax.dynamic_slice_in_dim(w_query, at_row, slice_rows, 0).astype(jnp.float32),
            cols(w_key.T),
            cols(w_value.T),
        ],
        1,
    )
    out_slice, qkv_slice = fence(out_slice, qkv_slice)
    out_near = along(out_slice, PAIRS)
    qkv_near = along(qkv_slice, PAIRS)
    meta = jnp.stack([chip, core]).astype(jnp.int32)

    pq = place_query(heads_here)
    pkv = place_key_value(kv_here)
    p_all = place_all(heads_here, kv_here)
    strip_one = place_all(GROUP, 1).T
    p_out = place_plain(heads_here)
    strip_out = p_out.T

    half_dim = HD // 2
    freqs = rope_base ** (-(jnp.arange(half_dim).astype(jnp.float32) * 2.0 / HD))
    freqs = jnp.pad(freqs, (0, LANES // 2 - half_dim))
    angles = positions.astype(jnp.float32)[:, None] * jnp.concatenate([freqs, freqs])[None, :]
    cosines = jnp.cos(angles)
    sines = jnp.sin(angles) * jnp.where(jnp.arange(LANES) < LANES // 2, -1.0, 1.0)

    cosines, sines, out_near = fence(cosines, sines, out_near)
    out_across = along(jnp.stack([out_slice, out_near]), MIDDLE)
    qkv_own, normed_one, own_pad = start(
        tokens, norm_gain, w_query, w_key.T, w_value.T, pq, pkv, cosines, sines
    )

    order = list(reversed(range(CHUNKS)))
    c0, c1, c2, c3 = order
    own, other, across, outer = {}, {}, {}, {}
    part, total, final = {}, {}, {}

    def hop_1(j):
        other[j] = along(own[j], PAIRS)

    def hop_2(j):
        across[j] = along(jnp.concatenate([own[j], other[j]], 1), MIDDLE)

    def hop_3(j):
        outer[j] = along(across[j], OUTWARD)

    coming = {}

    def add_1(j):
        coming[j] = along(part[j], INWARD)

    def add_2(j):
        total[j] = part[j][:rows] + coming[j][:rows]
        coming[j] = along(total[j], MIDDLE)

    def two_hops(j, inward, add, other):
        total[j], middle = hop_sums(level_ref, total[j], coming[j], inward, add, other, rows)
        final[j] = along(total[j], PAIRS)
        return final[j], middle, along(middle, MIDDLE)

    def to_chip(array, m):
        return lax.ppermute(array, "chip", [(i, i ^ m) for i in range(chips)])

    def over_chips_1(piece):
        cut = piece.shape[1] // 2
        one, two = piece[:, :cut], piece[:, cut:]
        return jnp.stack([one, to_chip(one, 1)]), jnp.stack([two, to_chip(two, 2)])

    def over_chips_2(one, two):
        return one, to_chip(one, 2), two, to_chip(two, 1)

    def over_chips_3(one, one_far, two, two_far):
        upper = jnp.stack([one[0], one[1], one_far[0], one_far[1]])
        lower = jnp.stack([two[0], two_far[0], two[1], two_far[1]])
        return jnp.concatenate([upper, lower], 2)

    qkv_own, out_across, qkv_near = fence(qkv_own, out_across, qkv_near)
    out_outer = along(out_across, OUTWARD)
    qkv_across = along(jnp.stack([qkv_slice, qkv_near]), MIDDLE)
    own[c0] = attend(lengths, qkv_own, strip_out, c0, rows)
    own, qkv_own, out_outer = fence(own, qkv_own, out_outer)
    hop_1(c0)
    out_far = far_slices(level_ref, out_near, out_across, out_outer)
    out_mine = over_chips_1(out_far) if by_hand else out_far
    own[c1] = attend(lengths, qkv_own, strip_out, c1, rows)
    own[c1], qkv_own = fence(own[c1], qkv_own)
    hop_1(c1)
    own[c2] = attend(lengths, qkv_own, strip_out, c2, rows)
    own, other[c0], normed_one, w_out, out_mine, qkv_across, qkv_own = fence(
        own, other[c0], normed_one, w_out, out_mine, qkv_across, qkv_own
    )
    own[c3] = attend(lengths, qkv_own, strip_out, c3, rows)
    qkv_outer = along(qkv_across, OUTWARD)
    if by_hand:
        out_mine = over_chips_2(*out_mine)
    else:
        out_mine = lax.all_gather(out_mine, ("chip", "core"))
    hop_2(c0)
    dout, dout_t, normed_one_t = turn(lengths, cotangent, normed_one)
    w_out_t = w_out.T
    own, other, across, dout, dout_t, normed_one_t, w_out_t, out_mine, qkv_outer = fence(
        own, other, across, dout, dout_t, normed_one_t, w_out_t, out_mine, qkv_outer
    )
    hop_1(c2)
    hop_3(c0)
    hop_2(c1)
    qkv_far = far_slices(level_ref, qkv_near, qkv_across, qkv_outer)
    qkv_far = lax.all_gather(qkv_far, ("chip", "core"))
    if by_hand:
        out_mine = over_chips_3(*out_mine)
        out_theirs = swap(out_mine)
        out_pad, out_plain = spread(
            spread_out_kernel,
            meta,
            w_out_t,
            [p_out],
            out_mine,
            out_theirs,
            [4 * p_out.shape[1], 4 * p_out.shape[0]],
        )
    else:
        plain = [w_out_t] + [
            out_mine[:, s].reshape(depth, -1).astype(jnp.bfloat16) for s in range(tp - 1)
        ]
        out_plain = jnp.concatenate(plain, 1)
        out_pad = jnp.concatenate([dot32(w, p_out).astype(jnp.bfloat16) for w in plain], 1)
    hidden, normed_t, activ, dgate, dup, mlp_part = {}, {}, {}, {}, {}, {}

    def feed(j):
        gathered = (own[j], other[j], across[j], outer[j])
        (hidden[j], normed_t[j], activ[j], dgate[j], dup[j], mlp_part[j], part[j]) = forward_chunk(
            level_ref, gathered, tokens, dout, out_plain, mlp_gain, w_gate, w_up, w_down, j, rows
        )

    own, other, across, outer, out_pad, out_plain = fence(
        own, other, across, outer, out_pad, out_plain
    )
    hop_1(c3)
    hop_3(c1)
    hop_2(c2)
    feed(c0)
    part, other = fence(part, other)
    add_1(c0)
    own, other, across, outer, part, hidden = fence(own, other, across, outer, part, hidden)
    hop_3(c2)
    hop_2(c3)
    feed(c1)
    qkv_far, hidden[c1] = fence(qkv_far, hidden[c1])
    qkv_pad = spread_qkv(own_pad, pq, pkv, qkv_far)
    own, other, across, outer, part, total, coming, hidden, qkv_pad = fence(
        own, other, across, outer, part, total, coming, hidden, qkv_pad
    )
    add_1(c1)
    hop_3(c3)
    add_2(c0)
    feed(c2)
    qkv_pad, hidden[c2] = fence(qkv_pad, hidden[c2])
    qkv = project(normed_one, qkv_pad, cosines, sines, qkv_own)
    own, other, across, outer, part, total, coming, hidden, qkv = fence(
        own, other, across, outer, part, total, coming, hidden, qkv
    )
    coming[c2], total[c1], coming[c1] = two_hops(c0, [part[c2]], [part[c1]], coming[c1])
    feed(c3)

    listed = lambda pieces: [pieces[j] for j in range(CHUNKS)]
    keep_side = jnp.stack([core, 2, 0]).astype(jnp.int32)
    keep_turned = jnp.stack([core, 2, chip]).astype(jnp.int32)
    send_side = jnp.stack([1 - core, 2, 0]).astype(jnp.int32)
    send_turned = jnp.stack([1 - core, 2, chip]).astype(jnp.int32)
    all_rows = jnp.array([0, 1, 0], jnp.int32)

    def send_rows(lefts, groups, step, side=send_side):
        if not by_hand:
            return rows_of(lefts, groups, all_rows, depth // 4, 4, step)
        return rows_of(lefts, groups, side, slice_rows, chips, step)

    def keep_rows(lefts, groups, received, step, side=keep_side, picked=None):
        if not by_hand:
            return received
        return rows_of(lefts, groups, side, slice_rows, chips, step, received, picked)

    def swap_rows(array):
        return swap(array) if by_hand else array

    def scatter(array, axes):
        return lax.psum_scatter(array, axes, scatter_dimension=0, tiled=True)

    units = w_gate.shape[1]
    mlp_args = (
        [listed(normed_t), dout_t],
        [(0, listed(dgate)), (0, listed(dup)), (1, listed(activ))],
    )
    acc = None
    dhid_t, dqkv_own, input_grad, gains = {}, {}, {}, {}

    def back(j):
        nonlocal acc
        (dhid_t[j], dqkv_own[j], input_grad[j], gains[j]), acc = back_some(j, True)

    def back_own(j):
        return back_some(j, False)[0]

    def back_some(j, full):
        return backward_chunk(
            level_ref,
            (total[j], final[j]),
            hidden[j],
            dout,
            tokens,
            (norm_gain, mlp_gain),
            (out_pad, qkv_pad),
            qkv,
            (own[j], other[j], across[j], outer[j]),
            (p_out, strip_one),
            (cosines, sines),
            acc,
            j,
            rows,
            full,
        )

    grad_mlp = rows_of(*mlp_args, all_rows, depth // 4, 4, units // 2)
    own, other, across, outer, part, total, coming, final, hidden, grad_mlp = fence(
        own, other, across, outer, part, total, coming, final, hidden, grad_mlp
    )
    grad_mlp = scatter(grad_mlp, ("chip", "core"))
    coming[c3], total[c2], coming[c2] = two_hops(c1, [part[c3]], [part[c2]], coming[c2])
    back(c0)

    near = lambda: jnp.where(low, mlp_part[1], mlp_part[2])
    edge = lambda: jnp.where(low, mlp_part[0], mlp_part[3])
    total, coming, final, hidden, mlp_part, acc, dhid_t = fence(
        total, coming, final, hidden, mlp_part, acc, dhid_t
    )
    leave_far = [mlp_part[3], mlp_part[0]]
    leave_near = [mlp_part[2], mlp_part[1]]
    far_sum, total[c3], coming[c3] = two_hops(c2, leave_far, [part[c3]], coming[c3])
    back(c1)
    total, coming, final, hidden, mlp_part, far_sum, acc, dhid_t = fence(
        total, coming, final, hidden, mlp_part, far_sum, acc, dhid_t
    )
    near_sum, _, far_in = two_hops(c3, leave_near, leave_far, far_sum)
    back(c2)
    total, final, hidden, mlp_part, near_sum, far_in, acc, dhid_t = fence(
        total, final, hidden, mlp_part, near_sum, far_in, acc, dhid_t
    )
    last = along(jnp.where(inner, edge() + far_in, near()), PAIRS)
    near_in = along(jnp.where(low, *leave_near) + near_sum, MIDDLE)
    dhid_t[c3], dqkv_own[c3] = back_own(c3)
    q_cols = heads_here * HD
    attn_args = (
        [listed(dhid_t), normed_one_t],
        [(0, listed(own)), (1, listed(dqkv_own))],
    )
    sent = swap_rows(send_rows(*attn_args, None, send_turned))
    total, final, hidden, acc, sent = fence(total, final, hidden, acc, sent)
    if by_hand:
        half = slice_rows // 2
        upper = lambda m: (m * slice_rows, half)
        lower = lambda m: (m * slice_rows + half, half)
        picked = [
            [upper(1), upper(3)],
            [upper(0), upper(2)],
            [lower(2), lower(3)],
            [lower(0), lower(1)],
        ]
        pieces = keep_rows(*attn_args, sent, None, keep_turned, picked)
        pieces, hidden = fence(pieces, hidden)
        one_away, one, two_away, two = pieces
        pieces = (one, to_chip(one_away, 1), two, to_chip(two_away, 2))
    else:
        pieces = scatter(sent, ("chip", "core"))
    back(c3)
    pieces, gains, input_grad, last, near_in = fence(pieces, gains, input_grad, last, near_in)
    gain_sums = gains[0] + gains[1] + gains[2] + gains[3]
    gain_sums = gain_sums + swap(gain_sums)
    grad_gate = grad_mlp[:, :units]
    grad_up = grad_mlp[:, units : 2 * units]
    grad_down = grad_mlp[:, 2 * units :].T
    if by_hand:
        others = [to_chip(gain_sums, m) for m in range(1, chips)]
        gain_sums = sum(others, gain_sums)
        one = pieces[0] + pieces[1]
        two = pieces[2] + pieces[3]
        one_last = to_chip(one[half:], 2)
        two_last = to_chip(two[half:], 1)
        one_last, two_last, grad_gate, grad_up, grad_down = fence(
            one_last, two_last, grad_gate, grad_up, grad_down
        )
        attn = jnp.concatenate([one[:half] + one_last, two[:half] + two_last], 0)
    else:
        gain_sums = lax.psum(gain_sums, "chip")
        attn = pieces
    gain_rows = lax.dynamic_slice_in_dim(gain_sums, at_row, slice_rows, 1)
    grad_out, grad_qkv = attn[:, :q_cols], attn[:, q_cols:]
    mlp_rows = jnp.where(inner, near() + near_in, edge()) + last
    hidden_rows = jnp.where(
        low,
        jnp.where(level == 0, hidden[0], hidden[1]),
        jnp.where(level == 2, hidden[2], hidden[3]),
    )
    layer_out = (hidden_rows + mlp_rows).astype(jnp.bfloat16)
    one = strip_one.shape[1]
    picked = lambda at, width: jnp.concatenate(
        [grad_qkv[:, kv * one + at : kv * one + at + width] for kv in range(kv_here)], 1
    )
    return (
        layer_out,
        jnp.concatenate(listed(input_grad), 0),
        gain_rows[0],
        picked(0, GROUP * HD),
        picked(GROUP * HD, HD),
        picked((GROUP + 1) * HD, HD),
        grad_out.T,
        gain_rows[1],
        grad_gate,
        grad_up,
        grad_down,
    )


def solution(mesh):
    devices = mesh.devices
    dp, tp = devices.shape
    split = Mesh(devices.reshape(dp // 2, 2, tp), ("chip", "core", "tp"))
    data = ("chip", "core")
    return jax.shard_map(
        shards,
        mesh=split,
        in_specs=(
            P(data, None),
            P(data),
            P(data),
            P(data, None),
            P(),
            P(None, "tp"),
            P(None, "tp"),
            P(None, "tp"),
            P("tp", None),
            P(),
            P(None, "tp"),
            P(None, "tp"),
            P("tp", None),
        ),
        out_specs=(
            P(("chip", "core", "tp"), None),
            P(data, None),
            P(data),
            P(data, "tp"),
            P(data, "tp"),
            P(data, "tp"),
            P("tp", data),
            P(data),
            P(data, "tp"),
            P(data, "tp"),
            P("tp", data),
        ),
        check_vma=False,
    )
```

```python
import functools

import jax
import jax.numpy as jnp
from jax import lax
from jax.experimental import pallas as pl
from jax.experimental.pallas import tpu as pltpu
from jax.sharding import Mesh
from jax.sharding import PartitionSpec as P

HD = 96
LANES = 128
GROUP = 2
KV_WIDE = (GROUP + 2) * LANES
rope_base = 100000.0
norm_eps = 1e-05
masked_score = -1e30
far_away = 1e30
score_scale = HD ** (-0.5)
score_scale_log2 = score_scale * 1.4426950408889634
CHUNKS = 4
EXTRA = 8
VMEM_BYTES = 56 * 1024 * 1024
NT = (((1,), (1,)), ((), ()))


def params():
    return pltpu.CompilerParams(vmem_limit_bytes=VMEM_BYTES)


def cost(flops, moved, exps=0):
    return pl.CostEstimate(
        flops=flops // 1024, bytes_accessed=moved // 1024, transcendentals=exps // 1024
    )


def dot32(a, b):
    return jnp.dot(a, b, preferred_element_type=jnp.float32)


def dot32_nt(a, b):
    return lax.dot_general(a, b, NT, preferred_element_type=jnp.float32)


def dot_split(a, places):
    high = a.astype(jnp.bfloat16)
    rest = (a - high.astype(jnp.float32)).astype(jnp.bfloat16)
    return dot32(high, places) + dot32(rest, places)


def fence(*trees):
    return lax.optimization_barrier(trees)


def whole(array, buffers=None):
    zeros = (0,) * len(array.shape)
    return pl.BlockSpec(array.shape, lambda *_: zeros)


SCALAR = pl.BlockSpec(memory_space=pltpu.SMEM)


def halves(entry):
    half_dim = HD // 2
    return (entry // half_dim) * (LANES // 2) + entry % half_dim


def placement(lanes, width):
    return (lanes[:, None] == jnp.arange(width)[None, :]).astype(jnp.bfloat16)


def place_query(heads):
    source = jnp.arange(heads * HD)
    return placement((source // HD) * LANES + halves(source % HD), heads * LANES)


def place_key_value(kv_heads):
    source = jnp.arange(kv_heads * HD)
    head = source // HD
    keys = head * 2 * LANES + halves(source % HD)
    values = head * 2 * LANES + LANES + source % HD
    return placement(jnp.concatenate([keys, values]), kv_heads * 2 * LANES)


def place_all(heads, kv_heads):
    source = jnp.arange(heads * HD)
    head = source // HD
    query = (head // GROUP) * KV_WIDE + (head % GROUP) * LANES + halves(source % HD)
    source = jnp.arange(kv_heads * HD)
    base = (source // HD) * KV_WIDE + GROUP * LANES
    keys = base + halves(source % HD)
    values = base + LANES + source % HD
    return placement(jnp.concatenate([query, keys, values]), kv_heads * KV_WIDE)


def place_plain(heads):
    source = jnp.arange(heads * HD)
    return placement((source // HD) * LANES + source % HD, heads * LANES)


PAIRS = [(0, 1), (1, 0), (2, 3), (3, 2)]
INWARD = [(0, 1), (3, 2)]
MIDDLE = [(1, 2), (2, 1)]
OUTWARD = [(1, 0), (2, 3)]


def along(part, pairs):
    return lax.ppermute(part, "tp", pairs)


def store_qkv(out_ref, here, base, query, key_value):
    wide = GROUP * LANES
    for kv in range(key_value.shape[1] // (2 * LANES)):
        at = base + kv * KV_WIDE
        there = slice(kv * 2 * LANES, (kv + 1) * 2 * LANES)
        out_ref[here, at : at + wide] = query[:, kv * wide : (kv + 1) * wide]
        out_ref[here, at + wide : at + KV_WIDE] = key_value[:, there]


def store_turned(out_ref, at, lin, cos_ref, sin_ref):
    for h in range(GROUP + 2):
        one = lin[:, h * LANES : (h + 1) * LANES]
        if h < GROUP + 1:
            one = one * cos_ref[...] + pltpu.roll(one, LANES // 2, 1) * sin_ref[...]
        out_ref[:, at + h * LANES : at + (h + 1) * LANES] = one.astype(jnp.bfloat16)


def spread_out_kernel(meta_ref, own_ref, p_ref, mine_ref, theirs_ref, pad_ref, plain_ref):
    rows, width = mine_ref.shape[2:]
    wide = p_ref.shape[1]
    for side, ref in enumerate((mine_ref, theirs_ref)):
        here = pl.ds(pl.multiple_of((meta_ref[1] ^ side) * rows, rows), rows)
        for s in range(4):
            block = own_ref[here, :] if s == 0 else ref[0, s - 1].astype(jnp.bfloat16)
            plain_ref[here, s * width : (s + 1) * width] = block
            pad_ref[here, s * wide : (s + 1) * wide] = dot32(block, p_ref[...]).astype(
                jnp.bfloat16
            )


def spread_qkv_kernel(pq_ref, pkv_ref, far_ref, _, out_ref):
    parts, _, rows, width = far_ref.shape
    split = pq_ref.shape[0]
    block = far_ref[:, 0].reshape(parts * rows, width).astype(jnp.bfloat16)
    query = dot32(block[:, :split], pq_ref[...]).astype(jnp.bfloat16)
    key_value = dot32(block[:, split:], pkv_ref[...]).astype(jnp.bfloat16)
    store_qkv(out_ref, slice(None), 0, query, key_value)


def spread_qkv(padded, pq, pkv, far):
    total = padded.shape[0]
    dp, others, rows, width = far.shape
    wide = padded.shape[1] // (others + 1)
    parts = max(1, dp // 2)
    block = parts * rows
    return pl.pallas_call(
        spread_qkv_kernel,
        out_shape=jax.ShapeDtypeStruct(padded.shape, jnp.bfloat16),
        grid=(total // block, others),
        in_specs=[
            whole(pq),
            whole(pkv),
            pl.BlockSpec((parts, 1, rows, width), lambda i, s: (i, s, 0, 0)),
            pl.BlockSpec(memory_space=pl.ANY),
        ],
        out_specs=pl.BlockSpec((block, wide), lambda i, s: (i, s + 1)),
        input_output_aliases={3: 0},
        compiler_params=params(),
        cost_estimate=cost(8 * total * width * 512, 20 * total * wide),
    )(pq, pkv, far, padded)


def spread(kernel, meta, own, places, mine, theirs, widths):
    chips, others, rows, width = mine.shape
    total = own.shape[0]
    row_block = lambda m, meta: (meta[0] ^ m, 0)
    piece = pl.BlockSpec((1, others, rows, width), lambda m, meta: (m, 0, 0, 0))
    return pl.pallas_call(
        kernel,
        out_shape=[jax.ShapeDtypeStruct((total, wide), jnp.bfloat16) for wide in widths],
        grid_spec=pltpu.PrefetchScalarGridSpec(
            num_scalar_prefetch=1,
            grid=(chips,),
            in_specs=[pl.BlockSpec((2 * rows, own.shape[1]), row_block)]
            + [whole(place) for place in places]
            + [piece, piece],
            out_specs=[pl.BlockSpec((2 * rows, wide), row_block) for wide in widths],
        ),
        compiler_params=params(),
        cost_estimate=cost(
            8 * total * width * 512, total * (12 * width + 2 * sum(widths))
        ),
    )(meta, own, *places, mine, theirs)


def start_kernel(x_ref, gain_ref, q_ref, k_ref, v_ref, pq_ref, pkv_ref, cos_ref, sin_ref, *outs):
    qkv_ref, normed_ref, pad_ref = outs

    @pl.when(pl.program_id(0) == 0)
    def _():
        split = k_ref.shape[0]
        query = dot32(q_ref[...], pq_ref[...]).astype(jnp.bfloat16)
        key_value = dot32(k_ref[...].T, pkv_ref[:split, :])
        key_value = key_value + dot32(v_ref[...].T, pkv_ref[split:, :])
        store_qkv(pad_ref, slice(None), 0, query, key_value.astype(jnp.bfloat16))

    inputs = x_ref[...].astype(jnp.float32)
    rms = lax.rsqrt(jnp.mean(inputs * inputs, -1, keepdims=True) + norm_eps)
    normed = (inputs * rms * gain_ref[...]).astype(jnp.bfloat16)
    normed_ref[...] = normed
    for kv in range(pad_ref.shape[1] // KV_WIDE):
        at = kv * KV_WIDE
        store_turned(qkv_ref, at, dot32(normed, pad_ref[:, at : at + KV_WIDE]), cos_ref, sin_ref)


def start(tokens, gain, w_query, w_key_t, w_value_t, pq, pkv, cosines, sines):
    total, depth = tokens.shape
    rows = total // CHUNKS
    wide = pq.shape[1] + pkv.shape[1]
    gain = gain[None, :]
    by_rows = lambda width: pl.BlockSpec((rows, width), lambda i: (i, 0))
    arrays = [w_query, w_key_t, w_value_t, pq, pkv]
    shapes = [
        jax.ShapeDtypeStruct((total, 4 * wide), jnp.bfloat16),
        jax.ShapeDtypeStruct((total, depth), jnp.bfloat16),
        jax.ShapeDtypeStruct((depth, 4 * wide), jnp.bfloat16),
    ]
    return pl.pallas_call(
        start_kernel,
        out_shape=shapes,
        grid=(CHUNKS,),
        in_specs=[by_rows(depth), whole(gain)]
        + [whole(array) for array in arrays]
        + [by_rows(LANES), by_rows(LANES)],
        out_specs=[
            by_rows(wide),
            by_rows(depth),
            pl.BlockSpec((depth, wide), lambda i: (0, 0)),
        ],
        compiler_params=params(),
        cost_estimate=cost(2 * total * depth * wide, 12 * total * depth),
    )(tokens, gain, *arrays, cosines, sines)


def turn_kernel(length_ref, cot_ref, normed_ref, dout_ref, dout_t_ref, normed_t_ref):
    rows = cot_ref.shape[0]
    at = pl.program_id(0) * rows + lax.broadcasted_iota(jnp.int32, cot_ref.shape, 0)
    dout = jnp.where(at < length_ref[0], cot_ref[...].astype(jnp.float32), 0.0)
    dout = dout.astype(jnp.bfloat16)
    dout_ref[...] = dout
    dout_t_ref[...] = dout.T
    normed_t_ref[...] = normed_ref[...].T


def turn(length, cotangent, normed):
    total, depth = cotangent.shape
    rows = total // CHUNKS
    by_rows = pl.BlockSpec((rows, depth), lambda i: (i, 0))
    by_columns = pl.BlockSpec((depth, rows), lambda i: (0, i))
    turned = jax.ShapeDtypeStruct((depth, total), jnp.bfloat16)
    return pl.pallas_call(
        turn_kernel,
        out_shape=[jax.ShapeDtypeStruct((total, depth), jnp.bfloat16), turned, turned],
        grid=(CHUNKS,),
        in_specs=[SCALAR, by_rows, by_rows],
        out_specs=[by_rows, by_columns, by_columns],
        compiler_params=params(),
        cost_estimate=cost(total * depth, 10 * total * depth),
    )(length, cotangent, normed)


def project_kernel(x_ref, w_ref, cos_ref, sin_ref, _, out_ref):
    store_turned(out_ref, 0, dot32(x_ref[...], w_ref[...]), cos_ref, sin_ref)


def project(normed, weights, cosines, sines, qkv):
    rows, depth = normed.shape
    width = weights.shape[1]
    steps = width // KV_WIDE
    first = steps // 4
    return pl.pallas_call(
        project_kernel,
        out_shape=jax.ShapeDtypeStruct((rows, width), jnp.bfloat16),
        grid=(steps - first,),
        in_specs=[
            whole(normed),
            pl.BlockSpec((depth, KV_WIDE), lambda i: (0, i + first)),
            whole(cosines),
            whole(sines),
            pl.BlockSpec(memory_space=pl.ANY),
        ],
        out_specs=pl.BlockSpec((rows, KV_WIDE), lambda i: (0, i + first)),
        input_output_aliases={4: 0},
        compiler_params=params(),
        cost_estimate=cost(
            2 * rows * depth * width, 2 * (rows * depth + depth * width + rows * width)
        ),
    )(normed, weights, cosines, sines, qkv)


def attend_kernel(start, length_ref, q_ref, kv_ref, strip_ref, out_ref):
    rows = q_ref.shape[0]
    keys = kv_ref.shape[0]
    length = length_ref[0]
    row_ids = start + lax.broadcasted_iota(jnp.int32, (1, rows), 1)
    limit = jnp.minimum(row_ids, length - 1)
    allowed = lax.broadcasted_iota(jnp.int32, (keys, rows), 0) <= limit
    mixed = []
    sums = []
    for kv in range(kv_ref.shape[1] // KV_WIDE):
        base = kv * KV_WIDE
        at = base + GROUP * LANES
        key = kv_ref[:, at : at + LANES]
        value_t = kv_ref[:, at + LANES : at + 2 * LANES].T
        for g in range(GROUP):
            query = q_ref[:, base + g * LANES : base + (g + 1) * LANES]
            raw = jnp.where(allowed, dot32_nt(key, query), masked_score)
            peak = jnp.max(raw, axis=0, keepdims=True)
            expo = jnp.exp2((raw - peak) * score_scale_log2)
            total = jnp.sum(expo, axis=0, keepdims=True)
            probs = (expo * (1.0 / total)).astype(jnp.bfloat16)
            mixed.append(dot32(value_t, probs).T)
            log_sum = peak * score_scale_log2 + jnp.log2(total)
            sums.append(jnp.where(row_ids < length, log_sum, far_away))
    out_ref[:rows, :] = dot_split(jnp.concatenate(mixed, 1), strip_ref[...])
    out_ref[rows:, :] = jnp.zeros((EXTRA, out_ref.shape[1]), jnp.float32)
    out_ref[rows : rows + len(sums), :rows] = jnp.concatenate(sums, 0)


def attend(length, qkv, strip, index, rows):
    keys = (index + 1) * rows
    width = qkv.shape[1] // 4
    heads = width // KV_WIDE * GROUP
    shape = (rows + EXTRA, strip.shape[1])
    return pl.pallas_call(
        functools.partial(attend_kernel, index * rows),
        out_shape=jax.ShapeDtypeStruct(shape, jnp.float32),
        grid=(1,),
        in_specs=[
            SCALAR,
            pl.BlockSpec((rows, width), lambda i: (index, 0)),
            pl.BlockSpec((keys, width), lambda i: (0, 0)),
            whole(strip),
        ],
        out_specs=pl.BlockSpec(shape, lambda i: (0, 0)),
        compiler_params=params(),
        cost_estimate=cost(
            4 * heads * rows * keys * LANES, 2 * (rows + keys) * width, heads * rows * keys
        ),
    )(length, qkv, qkv, strip)


def forward_kernel(level_ref, part_ref, other_ref, across_ref, outer_ref, *refs):
    x_ref, dout_ref, wo_ref, gain_ref, wg_ref, wu_ref, wd_ref = refs[:7]
    hidden_ref, normed_t_ref, activ_ref, dgate_ref, dup_ref, mlp_ref, dn_ref = refs[7:14]
    normed_ref = refs[14]
    rows = x_ref.shape[0]

    @pl.when(pl.program_id(0) == 0)
    def _():
        level = level_ref[0]
        inner = (level == 1) | (level == 2)
        width = part_ref.shape[1]
        second = jnp.where(inner, across_ref[:rows, width:], outer_ref[:rows, :width])
        third = jnp.where(inner, across_ref[:rows, :width], outer_ref[:rows, width:])
        mixed = jnp.concatenate([part_ref[:rows, :], other_ref[:rows, :], second, third], 1)
        hidden = x_ref[...].astype(jnp.float32) + dot32_nt(mixed.astype(jnp.bfloat16), wo_ref[...])
        hidden_ref[...] = hidden
        rms = lax.rsqrt(jnp.mean(hidden * hidden, -1, keepdims=True) + norm_eps)
        normed = (hidden * rms * gain_ref[...]).astype(jnp.bfloat16)
        normed_ref[...] = normed
        normed_t_ref[...] = normed.T
        mlp_ref[...] = jnp.zeros_like(mlp_ref)
        dn_ref[...] = jnp.zeros_like(dn_ref)

    normed = normed_ref[...]
    gate = dot32(normed, wg_ref[...])
    up = dot32(normed, wu_ref[...])
    dact = dot32_nt(dout_ref[...], wd_ref[...])
    sigmoid = jax.nn.sigmoid(gate)
    silu = gate * sigmoid
    activ = (silu * up).astype(jnp.bfloat16)
    dgate = (dact * up * sigmoid * (1.0 + gate * (1.0 - sigmoid))).astype(jnp.bfloat16)
    dup = (dact * silu).astype(jnp.bfloat16)
    activ_ref[...] = activ
    dgate_ref[...] = dgate
    dup_ref[...] = dup
    mlp_ref[...] += dot32(activ, wd_ref[...])
    dn_ref[:rows, :] += dot32_nt(dgate, wg_ref[...]) + dot32_nt(dup, wu_ref[...])


def forward_chunk(level, gathered, tokens, dout, w_out, gain, w_gate, w_up, w_down, index, rows):
    depth = tokens.shape[1]
    units = w_gate.shape[1]
    block = 512
    own_rows = pl.BlockSpec((rows, depth), lambda i: (index, 0))
    by_units = pl.BlockSpec((depth, block), lambda i: (0, i))
    gain = gain[None, :]
    f32, bf16 = jnp.float32, jnp.bfloat16
    outs = [
        jax.ShapeDtypeStruct((rows, depth), f32),
        jax.ShapeDtypeStruct((depth, rows), bf16),
        jax.ShapeDtypeStruct((rows, units), bf16),
        jax.ShapeDtypeStruct((rows, units), bf16),
        jax.ShapeDtypeStruct((rows, units), bf16),
        jax.ShapeDtypeStruct((rows, depth), f32),
        jax.ShapeDtypeStruct((rows + EXTRA, depth), f32),
    ]
    unit_out = pl.BlockSpec((rows, block), lambda i: (0, i))
    return pl.pallas_call(
        forward_kernel,
        out_shape=outs,
        grid=(units // block,),
        in_specs=[SCALAR]
        + [whole(array) for array in gathered]
        + [own_rows, own_rows, whole(w_out), whole(gain), by_units, by_units]
        + [pl.BlockSpec((block, depth), lambda i: (i, 0))],
        out_specs=[
            whole(outs[0]),
            whole(outs[1]),
            unit_out,
            unit_out,
            unit_out,
            whole(outs[5]),
            whole(outs[6]),
        ],
        scratch_shapes=[pltpu.VMEM((rows, depth), bf16)],
        compiler_params=params(),
        cost_estimate=cost(
            2 * rows * depth * (6 * units + w_out.shape[1]),
            2 * depth * (3 * units + w_out.shape[1]) + 22 * rows * depth,
            rows * units,
        ),
    )(level, *gathered, tokens, dout, w_out, gain, w_gate, w_up, w_down)


def hidden_grad(inner, total_ref, final_ref, hidden_ref, dout_ref, gain_ref):
    dnormed = jnp.where(inner, total_ref[...], final_ref[...])
    hidden = hidden_ref[...]
    rms = lax.rsqrt(jnp.mean(hidden * hidden, -1, keepdims=True) + norm_eps)
    scaled = dnormed * gain_ref[...]
    shift = jnp.mean(scaled * hidden, -1, keepdims=True)
    dhid = dout_ref[...].astype(jnp.float32) + (rms * scaled - hidden * (rms**3 * shift))
    return dhid, dnormed * (hidden * rms)


def backward_kernel(start, full, level_ref, total_ref, final_ref, hidden_ref, dout_ref, *refs):
    gain_two_ref, wo_ref, q_ref = refs[:3]
    kv_here = q_ref.shape[1] // KV_WIDE
    refs = refs[3:]
    kv_refs, refs = refs[: 2 * kv_here], refs[2 * kv_here :]
    part_ref, place_ref, strip_ref, cos_ref, sin_ref = refs[:5]
    dhid_ref, low_ref, dn_ref = refs[-3:]
    outs = refs[5:-3]
    if full:
        x_ref, gain_one_ref, other_ref, across_ref, outer_ref, w_ref = outs[:6]
        outs = outs[6:]
    count = (5 if start > 0 else 4) if full else 2
    acc_ref = outs[0] if len(outs) > count else None
    outs = outs[-count:]
    dhid_t_ref, dqkv_ref = outs[:2]
    if full:
        input_grad_ref, gains_ref = outs[2:4]
    rows = q_ref.shape[0]
    keys = kv_refs[0].shape[0]
    shard = pl.program_id(0)
    level = level_ref[0]
    inner = (level == 1) | (level == 2)

    @pl.when(shard == 0)
    def _():
        dhid, dgain = hidden_grad(
            inner, total_ref, final_ref, hidden_ref, dout_ref, gain_two_ref
        )
        dhid_ref[...] = dhid
        low = dhid.astype(jnp.bfloat16)
        low_ref[...] = low
        dhid_t_ref[...] = low.T
        if full:
            gains_ref[...] = jnp.zeros_like(gains_ref)
            gains_ref[1:2, :] = jnp.sum(dgain, 0, keepdims=True)
            dn_ref[...] = jnp.zeros_like(dn_ref)

    def rotate_back(grads):
        turned = grads * cos_ref[...] - pltpu.roll(grads, LANES // 2, 1) * sin_ref[...]
        return turned.astype(jnp.bfloat16)

    dmixed_all = dot32(low_ref[...], wo_ref[...]).astype(jnp.bfloat16)
    mixed = part_ref[...]
    if full:
        far = jnp.where(inner, across_ref[...], outer_ref[...])
        far = jnp.where(shard == 1, other_ref[...], far)
        mixed = jnp.where(shard == 0, mixed, far)
    products = dmixed_all.astype(jnp.float32) * dot_split(mixed[:rows], place_ref[...])
    causal = lax.broadcasted_iota(jnp.int32, (rows, rows), 0) <= lax.broadcasted_iota(
        jnp.int32, (rows, rows), 1
    )
    grads = []
    for kv in range(kv_here):
        key_ref, value_ref = kv_refs[2 * kv : 2 * kv + 2]
        heads = range(kv * GROUP, (kv + 1) * GROUP)
        lanes = {h: slice(h * LANES, (h + 1) * LANES) for h in heads}
        row_dots = {h: jnp.sum(products[:, lanes[h]].T, axis=0, keepdims=True) for h in heads}
        log_sums = {h: mixed[rows + h : rows + h + 1, :rows] for h in heads}
        dqueries = dict.fromkeys(heads)
        here = slice(2 * kv * LANES, (2 * kv + 1) * LANES)
        there = slice((2 * kv + 1) * LANES, (2 * kv + 2) * LANES)
        for tile in range(keys // rows):
            span = slice(tile * rows, (tile + 1) * rows)
            key = key_ref[span, :]
            value = value_ref[span, :]
            key_t = key.T
            dkey = None if acc_ref is None else acc_ref[span, here]
            dvalue = None if acc_ref is None else acc_ref[span, there]
            last = tile * rows == start
            for h in heads:
                at = kv * KV_WIDE + (h % GROUP) * LANES
                query = q_ref[:, at : at + LANES]
                dmixed = dmixed_all[:, lanes[h]]
                raw = dot32_nt(key, query)
                probs = jnp.exp2(raw * score_scale_log2 - log_sums[h])
                if last:
                    probs = jnp.where(causal, probs, 0.0)
                dprobs = dot32_nt(value, dmixed)
                dscores = (probs * (dprobs - row_dots[h])).astype(jnp.bfloat16)
                dquery = dot32(key_t, dscores)
                dqueries[h] = dquery if dqueries[h] is None else dqueries[h] + dquery
                dkey_one = dot32(dscores, query)
                dvalue_one = dot32(probs.astype(jnp.bfloat16), dmixed)
                dkey = dkey_one if dkey is None else dkey + dkey_one
                dvalue = dvalue_one if dvalue is None else dvalue + dvalue_one
            if full and not last:
                outs[4][span, here] = dkey
                outs[4][span, there] = dvalue
        grads += [rotate_back(dqueries[h].T * score_scale) for h in heads]
        grads.append(rotate_back(dkey * score_scale))
        grads.append(dvalue.astype(jnp.bfloat16))
    grads = jnp.concatenate(grads, 1)
    if full:
        dn_ref[...] += dot32_nt(grads, w_ref[...])

    @pl.when(shard == 0)
    def _():
        wide = strip_ref.shape[1]
        for kv in range(kv_here):
            dqkv_ref[:, kv * wide : (kv + 1) * wide] = dot32(
                grads[:, kv * KV_WIDE : (kv + 1) * KV_WIDE], strip_ref[...]
            ).astype(jnp.bfloat16)

    if not full:
        return

    @pl.when(shard == pl.num_programs(0) - 1)
    def _():
        dnormed = dn_ref[...]
        inputs = x_ref[...].astype(jnp.float32)
        rms = lax.rsqrt(jnp.mean(inputs * inputs, -1, keepdims=True) + norm_eps)
        scaled = dnormed * gain_one_ref[...]
        shift = jnp.mean(scaled * inputs, -1, keepdims=True)
        grad = dhid_ref[...] + (rms * scaled - inputs * (rms**3 * shift))
        input_grad_ref[...] = grad.astype(jnp.bfloat16)
        gains_ref[0:1, :] = jnp.sum(dnormed * (inputs * rms), 0, keepdims=True)


def backward_chunk(
    level, sums_two, hidden, dout, tokens, gains, weights, qkv, gathered, places, tables, acc,
    index, rows, full=True
):
    start = index * rows
    keys = start + rows
    depth = tokens.shape[1]
    out_pad, qkv_pad = weights
    place_out, strip = places
    far_rows, width = gathered[0].shape
    out_wide = place_out.shape[1]
    kv_here = out_wide // (GROUP * LANES)
    wide = kv_here * KV_WIDE
    levels = qkv.shape[1] // wide
    own_rows = pl.BlockSpec((rows, depth), lambda t: (index, 0))
    table = pl.BlockSpec((rows, LANES), lambda t: (index, 0))
    gains = [gain[None, :] for gain in gains]
    key_value = lambda at: pl.BlockSpec(
        (keys, LANES), lambda t: (0, (wide // LANES) * t + at)
    )
    across = pl.BlockSpec((far_rows, width), lambda t: (0, jnp.where(t == 2, 1, 0)))
    outer = pl.BlockSpec((far_rows, width), lambda t: (0, jnp.where(t == 3, 1, 0)))
    in_specs = [
        SCALAR,
        whole(hidden),
        whole(hidden),
        whole(hidden),
        own_rows,
        whole(gains[1]),
        pl.BlockSpec((depth, out_wide), lambda t: (0, t)),
        pl.BlockSpec((rows, wide), lambda t: (index, t)),
    ]
    for kv in range(kv_here):
        at = kv * (KV_WIDE // LANES) + GROUP
        in_specs += [key_value(at), key_value(at + 1)]
    in_specs += [
        whole(gathered[0]),
        whole(place_out),
        whole(strip),
        table,
        table,
    ]
    args = [level, *sums_two, hidden, dout, gains[1], out_pad]
    args += [qkv] * (1 + 2 * kv_here)
    args += [gathered[0], place_out, strip, *tables]
    sums_wide = 2 * kv_here * LANES
    if full:
        in_specs += [own_rows, whole(gains[0]), whole(gathered[1]), across, outer]
        in_specs.append(pl.BlockSpec((depth, wide), lambda t: (0, t)))
        args += [tokens, gains[0], *gathered[1:], qkv_pad]
    if acc is not None:
        in_specs.append(pl.BlockSpec((keys, sums_wide), lambda t: (0, t)))
        args.append(acc)
    f32, bf16 = jnp.float32, jnp.bfloat16
    outs = [
        jax.ShapeDtypeStruct((depth, rows), bf16),
        jax.ShapeDtypeStruct((rows, kv_here * strip.shape[1]), bf16),
        jax.ShapeDtypeStruct((rows, depth), bf16),
        jax.ShapeDtypeStruct((8, depth), f32),
    ]
    outs = outs if full else outs[:2]
    out_specs = [whole(out) for out in outs]
    if full and start > 0:
        outs.append(jax.ShapeDtypeStruct((start, levels * sums_wide), f32))
        out_specs.append(pl.BlockSpec((start, sums_wide), lambda t: (0, t)))
    results = pl.pallas_call(
        functools.partial(backward_kernel, start, full),
        out_shape=outs,
        grid=(levels if full else 1,),
        in_specs=in_specs,
        out_specs=out_specs,
        scratch_shapes=[
            pltpu.VMEM((rows, depth), f32),
            pltpu.VMEM((rows, depth), bf16),
            pltpu.VMEM((rows, depth), f32),
        ],
        compiler_params=params(),
        cost_estimate=cost(
            levels * rows * (20 * kv_here * keys * LANES + 2 * depth * (out_wide + wide)),
            2 * depth * levels * (out_wide + wide) + 16 * rows * depth,
            levels * kv_here * GROUP * rows * keys,
        ),
    )(*args)
    return results[:4], (results[4] if full and start > 0 else None)


def rows_kernel(lefts, groups, adding, picked, together, side_ref, *refs):
    refs = list(refs)
    held_ref = refs.pop()
    out_refs = refs[-len(picked) :]
    refs = refs[: -len(picked)]
    recv_ref = refs.pop() if adding else None
    step = pl.program_id(0)
    left_refs = []
    for count in lefts:
        left_refs.append(refs[:count])
        refs = refs[count:]
    rights = []
    for _ in groups:
        rights.append(refs[:CHUNKS])
        refs = refs[CHUNKS:]
    rows = left_refs[0][0].shape[0]
    blocks = held_ref.shape[1] // rows

    @pl.when(step == 0)
    def _():
        for which, pieces in enumerate(left_refs):
            for n, ref in enumerate(pieces):
                m, j = n % blocks, n // blocks
                wide = ref.shape[1]
                held_ref[which, m * rows : (m + 1) * rows, j * wide : (j + 1) * wide] = ref[...]

    chunk = held_ref.shape[2] // CHUNKS
    whole_columns = slice(0, out_refs[0].shape[1])

    def give(group, left, columns):
        right = jnp.concatenate([ref[:chunk, :].astype(jnp.bfloat16) for ref in group], 0)
        total = dot32(held_ref[left], right)
        if recv_ref is not None:
            total = total + recv_ref[:, columns]
        for out_ref, parts in zip(out_refs, picked):
            at = 0
            for start, size in parts:
                out_ref[at : at + size, columns] = total[start : start + size]
                at += size

    begin = 0
    for group, (left, first, steps) in zip(rights, groups):
        if together:
            width = group[0].shape[1]
            give(group, left, slice(begin, begin + width))
            begin += width
        else:

            @pl.when((step >= first) & (step < first + steps))
            def _(group=group, left=left):
                give(group, left, whole_columns)


def rows_of(lefts, groups, side, rows, blocks, step, recv=None, picked=None):
    if picked is None:
        picked = [[(0, rows * blocks)]]
    at = lambda m: lambda i, side: ((m ^ side[2]) * side[1] + side[0], 0)
    specs = []
    args = []
    counts = []
    for left in lefts:
        pieces = left if isinstance(left, list) else [left]
        counts.append(len(pieces) * blocks)
        for piece in pieces:
            for m in range(blocks):
                specs.append(pl.BlockSpec((rows, piece.shape[1]), at(m)))
                args.append(piece)
    tokens = sum(piece.shape[1] for piece in pieces)
    first = 0
    plan = []
    together = step is None
    for which, rights in groups:
        if together:
            plan.append((which, 0, 1))
            specs += [whole(right) for right in rights]
            args += rights
            first += rights[0].shape[1]
            continue
        steps = rights[0].shape[1] // step
        plan.append((which, first, steps))
        for right in rights:
            pick = lambda i, side, first=first, steps=steps: (0, jnp.clip(i - first, 0, steps - 1))
            specs.append(pl.BlockSpec((right.shape[0], step), pick))
            args.append(right)
        first += steps
    if together:
        first, step = 1, first
    total = first * step
    block = lambda height: pl.BlockSpec((height, step), lambda i, side: (0, i))
    if recv is not None:
        specs.append(block(rows * blocks))
        args.append(recv)
    heights = [sum(size for _, size in parts) for parts in picked]
    results = pl.pallas_call(
        functools.partial(rows_kernel, counts, plan, recv is not None, picked, together),
        out_shape=[jax.ShapeDtypeStruct((height, total), jnp.float32) for height in heights],
        grid_spec=pltpu.PrefetchScalarGridSpec(
            num_scalar_prefetch=1,
            grid=(first,),
            in_specs=specs,
            out_specs=[block(height) for height in heights],
            scratch_shapes=[pltpu.VMEM((len(lefts), rows * blocks, tokens), jnp.bfloat16)],
        ),
        compiler_params=params(),
        cost_estimate=cost(
            2 * rows * blocks * tokens * total,
            4 * rows * blocks * total + 2 * tokens * (total + rows * blocks),
        ),
    )(side, *args)
    return results[0] if len(picked) == 1 else results


def shards(
    tokens,
    lengths,
    positions,
    cotangent,
    norm_gain,
    w_query,
    w_key,
    w_value,
    w_out,
    mlp_gain,
    w_gate,
    w_up,
    w_down,
):
    seq_rows, depth = tokens.shape
    chips = lax.axis_size("chip")
    dp = chips * 2
    tp = lax.axis_size("tp")
    chip = lax.axis_index("chip")
    core = lax.axis_index("core")
    level = lax.axis_index("tp")
    low = level < 2
    inner = (level == 1) | (level == 2)
    heads_here = w_query.shape[1] // HD
    kv_here = w_key.shape[1] // HD
    rows = seq_rows // CHUNKS
    slice_rows = depth // dp
    level_ref = level.astype(jnp.int32).reshape(1)
    by_hand = dp == 8
    swap = lambda array: lax.ppermute(array, "core", [(0, 1), (1, 0)])
    to_level = lambda array, s: along(array, [(t, t ^ s) for t in range(tp)])

    at_row = (chip * 2 + core) * slice_rows
    cols = lambda w: lax.dynamic_slice_in_dim(w, at_row, slice_rows, 1).astype(jnp.float32).T
    (out_slice,) = fence(cols(w_out))
    qkv_slice = jnp.concatenate(
        [
            lax.dynamic_slice_in_dim(w_query, at_row, slice_rows, 0).astype(jnp.float32),
            cols(w_key.T),
            cols(w_value.T),
        ],
        1,
    )
    out_slice, qkv_slice = fence(out_slice, qkv_slice)
    out_near = along(out_slice, PAIRS)
    qkv_near = along(qkv_slice, PAIRS)
    meta = jnp.stack([chip, core]).astype(jnp.int32)

    pq = place_query(heads_here)
    pkv = place_key_value(kv_here)
    p_all = place_all(heads_here, kv_here)
    strip_one = place_all(GROUP, 1).T
    p_out = place_plain(heads_here)
    strip_out = p_out.T

    half_dim = HD // 2
    freqs = rope_base ** (-(jnp.arange(half_dim).astype(jnp.float32) * 2.0 / HD))
    freqs = jnp.pad(freqs, (0, LANES // 2 - half_dim))
    angles = positions.astype(jnp.float32)[:, None] * jnp.concatenate([freqs, freqs])[None, :]
    cosines = jnp.cos(angles)
    sines = jnp.sin(angles) * jnp.where(jnp.arange(LANES) < LANES // 2, -1.0, 1.0)

    cosines, sines, out_near = fence(cosines, sines, out_near)
    out_across = along(jnp.stack([out_slice, out_near]), MIDDLE)
    qkv_own, normed_one, own_pad = start(
        tokens, norm_gain, w_query, w_key.T, w_value.T, pq, pkv, cosines, sines
    )

    def far_slices(near, across, outer):
        return jnp.stack(
            [
                near,
                jnp.where(inner, across[1], outer[0]),
                jnp.where(inner, across[0], outer[1]),
            ]
        )

    order = list(reversed(range(CHUNKS)))
    c0, c1, c2, c3 = order
    own, other, across, outer = {}, {}, {}, {}
    part, total, final = {}, {}, {}

    def hop_1(j):
        other[j] = along(own[j], PAIRS)

    def hop_2(j):
        across[j] = along(jnp.concatenate([own[j], other[j]], 1), MIDDLE)

    def hop_3(j):
        outer[j] = along(across[j], OUTWARD)

    coming = {}

    def add_1(j):
        coming[j] = along(part[j], INWARD)

    def add_2(j):
        total[j] = part[j][:rows] + coming[j][:rows]
        coming[j] = along(total[j], MIDDLE)

    def add_3(j, inward, extra=0):
        both = jnp.where(inner, total[j] + coming[j], inward)
        total[j] = jnp.pad(both, ((0, extra), (0, 0)))
        final[j] = along(total[j], PAIRS)
        return final[j][:rows]

    def to_chip(array, m):
        return lax.ppermute(array, "chip", [(i, i ^ m) for i in range(chips)])

    def over_chips_1(piece):
        cut = piece.shape[1] // 2
        one, two = piece[:, :cut], piece[:, cut:]
        return jnp.stack([one, to_chip(one, 1)]), jnp.stack([two, to_chip(two, 2)])

    def over_chips_2(one, two):
        return one, to_chip(one, 2), two, to_chip(two, 1)

    def over_chips_3(one, one_far, two, two_far):
        upper = jnp.stack([one[0], one[1], one_far[0], one_far[1]])
        lower = jnp.stack([two[0], two_far[0], two[1], two_far[1]])
        return jnp.concatenate([upper, lower], 2)

    qkv_own, out_across, qkv_near = fence(qkv_own, out_across, qkv_near)
    out_outer = along(out_across, OUTWARD)
    qkv_across = along(jnp.stack([qkv_slice, qkv_near]), MIDDLE)
    own[c0] = attend(lengths, qkv_own, strip_out, c0, rows)
    own[c1] = attend(lengths, qkv_own, strip_out, c1, rows)
    own, qkv_own, out_outer = fence(own, qkv_own, out_outer)
    others = along(jnp.concatenate([own[c0], own[c1]], 0), PAIRS)
    out_far = far_slices(out_near, out_across, out_outer)
    out_mine = over_chips_1(out_far) if by_hand else out_far
    own[c2] = attend(lengths, qkv_own, strip_out, c2, rows)
    own[c3] = attend(lengths, qkv_own, strip_out, c3, rows)
    own[c3], qkv_across = fence(own[c3], qkv_across)
    qkv_outer = along(qkv_across, OUTWARD)
    own, others, normed_one, w_out, out_mine = fence(own, others, normed_one, w_out, out_mine)
    other[c0], other[c1] = others[: rows + EXTRA], others[rows + EXTRA :]
    if by_hand:
        out_mine = over_chips_2(*out_mine)
    else:
        out_mine = lax.all_gather(out_mine, ("chip", "core"))
    hop_2(c0)
    dout, dout_t, normed_one_t = turn(lengths, cotangent, normed_one)
    w_out_t = w_out.T
    own, other, across, dout, dout_t, normed_one_t, w_out_t, out_mine, qkv_outer = fence(
        own, other, across, dout, dout_t, normed_one_t, w_out_t, out_mine, qkv_outer
    )
    hop_1(c2)
    hop_3(c0)
    hop_2(c1)
    qkv_far = lax.all_gather(far_slices(qkv_near, qkv_across, qkv_outer), ("chip", "core"))
    if by_hand:
        out_mine = over_chips_3(*out_mine)
        out_theirs = swap(out_mine)
        out_pad, out_plain = spread(
            spread_out_kernel,
            meta,
            w_out_t,
            [p_out],
            out_mine,
            out_theirs,
            [4 * p_out.shape[1], 4 * p_out.shape[0]],
        )
    else:
        plain = [w_out_t] + [
            out_mine[:, s].reshape(depth, -1).astype(jnp.bfloat16) for s in range(tp - 1)
        ]
        out_plain = jnp.concatenate(plain, 1)
        out_pad = jnp.concatenate([dot32(w, p_out).astype(jnp.bfloat16) for w in plain], 1)
    hidden, normed_t, activ, dgate, dup, mlp_part = {}, {}, {}, {}, {}, {}

    def feed(j):
        gathered = (own[j], other[j], across[j], outer[j])
        (hidden[j], normed_t[j], activ[j], dgate[j], dup[j], mlp_part[j], part[j]) = forward_chunk(
            level_ref, gathered, tokens, dout, out_plain, mlp_gain, w_gate, w_up, w_down, j, rows
        )

    own, other, across, outer, out_pad, out_plain = fence(
        own, other, across, outer, out_pad, out_plain
    )
    hop_1(c3)
    hop_3(c1)
    hop_2(c2)
    feed(c0)
    part, other = fence(part, other)
    add_1(c0)
    own, other, across, outer, part, hidden = fence(own, other, across, outer, part, hidden)
    hop_3(c2)
    hop_2(c3)
    feed(c1)
    qkv_far, hidden[c1] = fence(qkv_far, hidden[c1])
    qkv_pad = spread_qkv(own_pad, pq, pkv, qkv_far)
    own, other, across, outer, part, total, coming, hidden, qkv_pad = fence(
        own, other, across, outer, part, total, coming, hidden, qkv_pad
    )
    add_1(c1)
    hop_3(c3)
    add_2(c0)
    feed(c2)
    qkv_pad, hidden[c2] = fence(qkv_pad, hidden[c2])
    qkv = project(normed_one, qkv_pad, cosines, sines, qkv_own)
    own, other, across, outer, part, total, coming, hidden, qkv = fence(
        own, other, across, outer, part, total, coming, hidden, qkv
    )
    coming[c2] = add_3(c0, part[c2][:rows])
    add_2(c1)
    feed(c3)

    listed = lambda pieces: [pieces[j] for j in range(CHUNKS)]
    keep_side = jnp.stack([core, 2, 0]).astype(jnp.int32)
    keep_turned = jnp.stack([core, 2, chip]).astype(jnp.int32)
    send_side = jnp.stack([1 - core, 2, 0]).astype(jnp.int32)
    send_turned = jnp.stack([1 - core, 2, chip]).astype(jnp.int32)
    all_rows = jnp.array([0, 1, 0], jnp.int32)

    def send_rows(lefts, groups, step, side=send_side):
        if not by_hand:
            return rows_of(lefts, groups, all_rows, depth // 4, 4, step)
        return rows_of(lefts, groups, side, slice_rows, chips, step)

    def keep_rows(lefts, groups, received, step, side=keep_side, picked=None):
        if not by_hand:
            return received
        return rows_of(lefts, groups, side, slice_rows, chips, step, received, picked)

    def swap_rows(array):
        return swap(array) if by_hand else array

    def scatter(array, axes):
        return lax.psum_scatter(array, axes, scatter_dimension=0, tiled=True)

    units = w_gate.shape[1]
    mlp_args = (
        [listed(normed_t), dout_t],
        [(0, listed(dgate)), (0, listed(dup)), (1, listed(activ))],
    )
    acc = None
    dhid_t, dqkv_own, input_grad, gains = {}, {}, {}, {}

    def back(j):
        nonlocal acc
        (dhid_t[j], dqkv_own[j], input_grad[j], gains[j]), acc = back_some(j, True)

    def back_own(j):
        return back_some(j, False)[0]

    def back_some(j, full):
        return backward_chunk(
            level_ref,
            (total[j], final[j]),
            hidden[j],
            dout,
            tokens,
            (norm_gain, mlp_gain),
            (out_pad, qkv_pad),
            qkv,
            (own[j], other[j], across[j], outer[j]),
            (p_out, strip_one),
            (cosines, sines),
            acc,
            j,
            rows,
            full,
        )

    grad_mlp = rows_of(*mlp_args, all_rows, depth // 4, 4, units // 2)
    own, other, across, outer, part, total, coming, final, hidden, grad_mlp = fence(
        own, other, across, outer, part, total, coming, final, hidden, grad_mlp
    )
    coming[c3] = add_3(c1, part[c3][:rows])
    add_2(c2)
    back(c0)

    near = lambda: jnp.where(low, mlp_part[1], mlp_part[2])
    edge = lambda: jnp.where(low, mlp_part[0], mlp_part[3])
    leave_far = lambda: jnp.where(low, mlp_part[3], mlp_part[0])
    leave_near = lambda: jnp.where(low, mlp_part[2], mlp_part[1])
    total, coming, final, hidden, mlp_part, acc, dhid_t, grad_mlp = fence(
        total, coming, final, hidden, mlp_part, acc, dhid_t, grad_mlp
    )
    grad_mlp = scatter(grad_mlp, ("chip", "core"))
    far_sum = add_3(c2, leave_far())
    add_2(c3)
    back(c1)
    total, coming, final, hidden, mlp_part, far_sum, acc, dhid_t = fence(
        total, coming, final, hidden, mlp_part, far_sum, acc, dhid_t
    )
    near_sum = add_3(c3, leave_near(), EXTRA)
    far_in = along(leave_far() + far_sum, MIDDLE)
    back(c2)
    total, final, hidden, mlp_part, near_sum, far_in, acc, dhid_t = fence(
        total, final, hidden, mlp_part, near_sum, far_in, acc, dhid_t
    )
    last = along(jnp.where(inner, edge() + far_in, near()), PAIRS)
    near_in = along(leave_near() + near_sum, MIDDLE)
    dhid_t[c3], dqkv_own[c3] = back_own(c3)
    q_cols = heads_here * HD
    attn_args = (
        [listed(dhid_t), normed_one_t],
        [(0, listed(own)), (1, listed(dqkv_own))],
    )
    sent = swap_rows(send_rows(*attn_args, None, send_turned))
    total, final, hidden, acc, sent = fence(total, final, hidden, acc, sent)
    if by_hand:
        half = slice_rows // 2
        upper = lambda m: (m * slice_rows, half)
        lower = lambda m: (m * slice_rows + half, half)
        picked = [
            [upper(1), upper(3)],
            [upper(0), upper(2)],
            [lower(2), lower(3)],
            [lower(0), lower(1)],
        ]
        pieces = keep_rows(*attn_args, sent, None, keep_turned, picked)
        pieces, hidden = fence(pieces, hidden)
        one_away, one, two_away, two = pieces
        pieces = (one, to_chip(one_away, 1), two, to_chip(two_away, 2))
    else:
        pieces = scatter(sent, ("chip", "core"))
    back(c3)
    pieces, gains, input_grad, last, near_in = fence(pieces, gains, input_grad, last, near_in)
    gain_sums = gains[0] + gains[1] + gains[2] + gains[3]
    gain_sums = gain_sums + swap(gain_sums)
    if by_hand:
        others = [to_chip(gain_sums, m) for m in range(1, chips)]
        gain_sums = sum(others, gain_sums)
        one = pieces[0] + pieces[1]
        two = pieces[2] + pieces[3]
        one = one[:half] + to_chip(one[half:], 2)
        two = two[:half] + to_chip(two[half:], 1)
        attn = jnp.concatenate([one, two], 0)
    else:
        gain_sums = lax.psum(gain_sums, "chip")
        attn = pieces
    gain_rows = lax.dynamic_slice_in_dim(gain_sums, at_row, slice_rows, 1)
    grad_out, grad_qkv = attn[:, :q_cols], attn[:, q_cols:]
    mlp_rows = jnp.where(inner, near() + near_in, edge()) + last
    hidden_rows = jnp.where(
        low,
        jnp.where(level == 0, hidden[0], hidden[1]),
        jnp.where(level == 2, hidden[2], hidden[3]),
    )
    layer_out = (hidden_rows + mlp_rows).astype(jnp.bfloat16)
    one = strip_one.shape[1]
    picked = lambda at, width: jnp.concatenate(
        [grad_qkv[:, kv * one + at : kv * one + at + width] for kv in range(kv_here)], 1
    )
    return (
        layer_out,
        jnp.concatenate(listed(input_grad), 0),
        gain_rows[0],
        picked(0, GROUP * HD),
        picked(GROUP * HD, HD),
        picked((GROUP + 1) * HD, HD),
        grad_out.T,
        gain_rows[1],
        grad_mlp[:, :units],
        grad_mlp[:, units : 2 * units],
        grad_mlp[:, 2 * units :].T,
    )


def solution(mesh):
    devices = mesh.devices
    dp, tp = devices.shape
    split = Mesh(devices.reshape(dp // 2, 2, tp), ("chip", "core", "tp"))
    data = ("chip", "core")
    return jax.shard_map(
        shards,
        mesh=split,
        in_specs=(
            P(data, None),
            P(data),
            P(data),
            P(data, None),
            P(),
            P(None, "tp"),
            P(None, "tp"),
            P(None, "tp"),
            P("tp", None),
            P(),
            P(None, "tp"),
            P(None, "tp"),
            P("tp", None),
        ),
        out_specs=(
            P(("chip", "core", "tp"), None),
            P(data, None),
            P(data),
            P(data, "tp"),
            P(data, "tp"),
            P(data, "tp"),
            P("tp", data),
            P(data),
            P(data, "tp"),
            P(data, "tp"),
            P("tp", data),
        ),
        check_vma=False,
    )
```

```python
import functools

import jax
import jax.numpy as jnp
from jax import lax
from jax.experimental import pallas as pl
from jax.experimental.pallas import tpu as pltpu
from jax.sharding import Mesh
from jax.sharding import PartitionSpec as P

HD = 96
LANES = 128
GROUP = 2
KV_WIDE = (GROUP + 2) * LANES
rope_base = 100000.0
norm_eps = 1e-05
masked_score = -1e30
far_away = 1e30
score_scale = HD ** (-0.5)
score_scale_log2 = score_scale * 1.4426950408889634
CHUNKS = 4
EXTRA = 8
VMEM_BYTES = 56 * 1024 * 1024
NT = (((1,), (1,)), ((), ()))


def params():
    return pltpu.CompilerParams(vmem_limit_bytes=VMEM_BYTES)


def cost(flops, moved, exps=0):
    return pl.CostEstimate(
        flops=flops // 1024, bytes_accessed=moved // 1024, transcendentals=exps // 1024
    )


def dot32(a, b):
    return jnp.dot(a, b, preferred_element_type=jnp.float32)


def dot32_nt(a, b):
    return lax.dot_general(a, b, NT, preferred_element_type=jnp.float32)


def dot_split(a, places):
    high = a.astype(jnp.bfloat16)
    rest = (a - high.astype(jnp.float32)).astype(jnp.bfloat16)
    return dot32(high, places) + dot32(rest, places)


def fence(*trees):
    return lax.optimization_barrier(trees)


def whole(array, buffers=None):
    zeros = (0,) * len(array.shape)
    return pl.BlockSpec(array.shape, lambda *_: zeros)


SCALAR = pl.BlockSpec(memory_space=pltpu.SMEM)


def halves(entry):
    half_dim = HD // 2
    return (entry // half_dim) * (LANES // 2) + entry % half_dim


def placement(lanes, width):
    return (lanes[:, None] == jnp.arange(width)[None, :]).astype(jnp.bfloat16)


def place_query(heads):
    source = jnp.arange(heads * HD)
    return placement((source // HD) * LANES + halves(source % HD), heads * LANES)


def place_key_value(kv_heads):
    source = jnp.arange(kv_heads * HD)
    head = source // HD
    keys = head * 2 * LANES + halves(source % HD)
    values = head * 2 * LANES + LANES + source % HD
    return placement(jnp.concatenate([keys, values]), kv_heads * 2 * LANES)


def place_all(heads, kv_heads):
    source = jnp.arange(heads * HD)
    head = source // HD
    query = (head // GROUP) * KV_WIDE + (head % GROUP) * LANES + halves(source % HD)
    source = jnp.arange(kv_heads * HD)
    base = (source // HD) * KV_WIDE + GROUP * LANES
    keys = base + halves(source % HD)
    values = base + LANES + source % HD
    return placement(jnp.concatenate([query, keys, values]), kv_heads * KV_WIDE)


def place_plain(heads):
    source = jnp.arange(heads * HD)
    return placement((source // HD) * LANES + source % HD, heads * LANES)


PAIRS = [(0, 1), (1, 0), (2, 3), (3, 2)]
INWARD = [(0, 1), (3, 2)]
MIDDLE = [(1, 2), (2, 1)]
OUTWARD = [(1, 0), (2, 3)]


def along(part, pairs):
    return lax.ppermute(part, "tp", pairs)


def store_qkv(out_ref, here, base, query, key_value):
    wide = GROUP * LANES
    for kv in range(key_value.shape[1] // (2 * LANES)):
        at = base + kv * KV_WIDE
        there = slice(kv * 2 * LANES, (kv + 1) * 2 * LANES)
        out_ref[here, at : at + wide] = query[:, kv * wide : (kv + 1) * wide]
        out_ref[here, at + wide : at + KV_WIDE] = key_value[:, there]


def store_turned(out_ref, at, lin, cos_ref, sin_ref):
    for h in range(GROUP + 2):
        one = lin[:, h * LANES : (h + 1) * LANES]
        if h < GROUP + 1:
            one = one * cos_ref[...] + pltpu.roll(one, LANES // 2, 1) * sin_ref[...]
        out_ref[:, at + h * LANES : at + (h + 1) * LANES] = one.astype(jnp.bfloat16)


def spread_out_kernel(meta_ref, own_ref, p_ref, mine_ref, theirs_ref, pad_ref, plain_ref):
    rows, width = mine_ref.shape[2:]
    wide = p_ref.shape[1]
    for side, ref in enumerate((mine_ref, theirs_ref)):
        here = pl.ds(pl.multiple_of((meta_ref[1] ^ side) * rows, rows), rows)
        for s in range(4):
            block = own_ref[here, :] if s == 0 else ref[0, s - 1].astype(jnp.bfloat16)
            plain_ref[here, s * width : (s + 1) * width] = block
            pad_ref[here, s * wide : (s + 1) * wide] = dot32(block, p_ref[...]).astype(
                jnp.bfloat16
            )


def spread_qkv_kernel(pq_ref, pkv_ref, far_ref, _, out_ref):
    parts, _, rows, width = far_ref.shape
    split = pq_ref.shape[0]
    block = far_ref[:, 0].reshape(parts * rows, width).astype(jnp.bfloat16)
    query = dot32(block[:, :split], pq_ref[...]).astype(jnp.bfloat16)
    key_value = dot32(block[:, split:], pkv_ref[...]).astype(jnp.bfloat16)
    store_qkv(out_ref, slice(None), 0, query, key_value)


def spread_qkv(padded, pq, pkv, far):
    total = padded.shape[0]
    dp, others, rows, width = far.shape
    wide = padded.shape[1] // (others + 1)
    parts = max(1, dp // 2)
    block = parts * rows
    return pl.pallas_call(
        spread_qkv_kernel,
        out_shape=jax.ShapeDtypeStruct(padded.shape, jnp.bfloat16),
        grid=(total // block, others),
        in_specs=[
            whole(pq),
            whole(pkv),
            pl.BlockSpec((parts, 1, rows, width), lambda i, s: (i, s, 0, 0)),
            pl.BlockSpec(memory_space=pl.ANY),
        ],
        out_specs=pl.BlockSpec((block, wide), lambda i, s: (i, s + 1)),
        input_output_aliases={3: 0},
        compiler_params=params(),
        cost_estimate=cost(8 * total * width * 512, 20 * total * wide),
    )(pq, pkv, far, padded)


def spread(kernel, meta, own, places, mine, theirs, widths):
    chips, others, rows, width = mine.shape
    total = own.shape[0]
    row_block = lambda m, meta: (meta[0] ^ m, 0)
    piece = pl.BlockSpec((1, others, rows, width), lambda m, meta: (m, 0, 0, 0))
    return pl.pallas_call(
        kernel,
        out_shape=[jax.ShapeDtypeStruct((total, wide), jnp.bfloat16) for wide in widths],
        grid_spec=pltpu.PrefetchScalarGridSpec(
            num_scalar_prefetch=1,
            grid=(chips,),
            in_specs=[pl.BlockSpec((2 * rows, own.shape[1]), row_block)]
            + [whole(place) for place in places]
            + [piece, piece],
            out_specs=[pl.BlockSpec((2 * rows, wide), row_block) for wide in widths],
        ),
        compiler_params=params(),
        cost_estimate=cost(
            8 * total * width * 512, total * (12 * width + 2 * sum(widths))
        ),
    )(meta, own, *places, mine, theirs)


def start_kernel(x_ref, gain_ref, q_ref, k_ref, v_ref, pq_ref, pkv_ref, cos_ref, sin_ref, *outs):
    qkv_ref, normed_ref, pad_ref = outs

    @pl.when(pl.program_id(0) == 0)
    def _():
        split = k_ref.shape[0]
        query = dot32(q_ref[...], pq_ref[...]).astype(jnp.bfloat16)
        key_value = dot32(k_ref[...].T, pkv_ref[:split, :])
        key_value = key_value + dot32(v_ref[...].T, pkv_ref[split:, :])
        store_qkv(pad_ref, slice(None), 0, query, key_value.astype(jnp.bfloat16))

    inputs = x_ref[...].astype(jnp.float32)
    rms = lax.rsqrt(jnp.mean(inputs * inputs, -1, keepdims=True) + norm_eps)
    normed = (inputs * rms * gain_ref[...]).astype(jnp.bfloat16)
    normed_ref[...] = normed
    for kv in range(pad_ref.shape[1] // KV_WIDE):
        at = kv * KV_WIDE
        store_turned(qkv_ref, at, dot32(normed, pad_ref[:, at : at + KV_WIDE]), cos_ref, sin_ref)


def start(tokens, gain, w_query, w_key_t, w_value_t, pq, pkv, cosines, sines):
    total, depth = tokens.shape
    rows = total // CHUNKS
    wide = pq.shape[1] + pkv.shape[1]
    gain = gain[None, :]
    by_rows = lambda width: pl.BlockSpec((rows, width), lambda i: (i, 0))
    arrays = [w_query, w_key_t, w_value_t, pq, pkv]
    shapes = [
        jax.ShapeDtypeStruct((total, 4 * wide), jnp.bfloat16),
        jax.ShapeDtypeStruct((total, depth), jnp.bfloat16),
        jax.ShapeDtypeStruct((depth, 4 * wide), jnp.bfloat16),
    ]
    return pl.pallas_call(
        start_kernel,
        out_shape=shapes,
        grid=(CHUNKS,),
        in_specs=[by_rows(depth), whole(gain)]
        + [whole(array) for array in arrays]
        + [by_rows(LANES), by_rows(LANES)],
        out_specs=[
            by_rows(wide),
            by_rows(depth),
            pl.BlockSpec((depth, wide), lambda i: (0, 0)),
        ],
        compiler_params=params(),
        cost_estimate=cost(2 * total * depth * wide, 12 * total * depth),
    )(tokens, gain, *arrays, cosines, sines)


def turn_kernel(length_ref, cot_ref, normed_ref, dout_ref, dout_t_ref, normed_t_ref):
    rows = cot_ref.shape[0]
    at = pl.program_id(0) * rows + lax.broadcasted_iota(jnp.int32, cot_ref.shape, 0)
    dout = jnp.where(at < length_ref[0], cot_ref[...].astype(jnp.float32), 0.0)
    dout = dout.astype(jnp.bfloat16)
    dout_ref[...] = dout
    dout_t_ref[...] = dout.T
    normed_t_ref[...] = normed_ref[...].T


def turn(length, cotangent, normed):
    total, depth = cotangent.shape
    rows = total // CHUNKS
    by_rows = pl.BlockSpec((rows, depth), lambda i: (i, 0))
    by_columns = pl.BlockSpec((depth, rows), lambda i: (0, i))
    turned = jax.ShapeDtypeStruct((depth, total), jnp.bfloat16)
    return pl.pallas_call(
        turn_kernel,
        out_shape=[jax.ShapeDtypeStruct((total, depth), jnp.bfloat16), turned, turned],
        grid=(CHUNKS,),
        in_specs=[SCALAR, by_rows, by_rows],
        out_specs=[by_rows, by_columns, by_columns],
        compiler_params=params(),
        cost_estimate=cost(total * depth, 10 * total * depth),
    )(length, cotangent, normed)


def project_kernel(x_ref, w_ref, cos_ref, sin_ref, _, out_ref):
    store_turned(out_ref, 0, dot32(x_ref[...], w_ref[...]), cos_ref, sin_ref)


def project(normed, weights, cosines, sines, qkv):
    rows, depth = normed.shape
    width = weights.shape[1]
    steps = width // KV_WIDE
    first = steps // 4
    return pl.pallas_call(
        project_kernel,
        out_shape=jax.ShapeDtypeStruct((rows, width), jnp.bfloat16),
        grid=(steps - first,),
        in_specs=[
            whole(normed),
            pl.BlockSpec((depth, KV_WIDE), lambda i: (0, i + first)),
            whole(cosines),
            whole(sines),
            pl.BlockSpec(memory_space=pl.ANY),
        ],
        out_specs=pl.BlockSpec((rows, KV_WIDE), lambda i: (0, i + first)),
        input_output_aliases={4: 0},
        compiler_params=params(),
        cost_estimate=cost(
            2 * rows * depth * width, 2 * (rows * depth + depth * width + rows * width)
        ),
    )(normed, weights, cosines, sines, qkv)


def attend_kernel(start, length_ref, q_ref, kv_ref, strip_ref, out_ref):
    rows = q_ref.shape[0]
    keys = kv_ref.shape[0]
    length = length_ref[0]
    row_ids = start + lax.broadcasted_iota(jnp.int32, (1, rows), 1)
    limit = jnp.minimum(row_ids, length - 1)
    allowed = lax.broadcasted_iota(jnp.int32, (keys, rows), 0) <= limit
    mixed = []
    sums = []
    for kv in range(kv_ref.shape[1] // KV_WIDE):
        base = kv * KV_WIDE
        at = base + GROUP * LANES
        key = kv_ref[:, at : at + LANES]
        value_t = kv_ref[:, at + LANES : at + 2 * LANES].T
        for g in range(GROUP):
            query = q_ref[:, base + g * LANES : base + (g + 1) * LANES]
            raw = jnp.where(allowed, dot32_nt(key, query), masked_score)
            peak = jnp.max(raw, axis=0, keepdims=True)
            expo = jnp.exp2((raw - peak) * score_scale_log2)
            total = jnp.sum(expo, axis=0, keepdims=True)
            probs = (expo * (1.0 / total)).astype(jnp.bfloat16)
            mixed.append(dot32(value_t, probs).T)
            log_sum = peak * score_scale_log2 + jnp.log2(total)
            sums.append(jnp.where(row_ids < length, log_sum, far_away))
    out_ref[:rows, :] = dot_split(jnp.concatenate(mixed, 1), strip_ref[...])
    out_ref[rows:, :] = jnp.zeros((EXTRA, out_ref.shape[1]), jnp.float32)
    out_ref[rows : rows + len(sums), :rows] = jnp.concatenate(sums, 0)


def attend(length, qkv, strip, index, rows):
    keys = (index + 1) * rows
    width = qkv.shape[1] // 4
    heads = width // KV_WIDE * GROUP
    shape = (rows + EXTRA, strip.shape[1])
    return pl.pallas_call(
        functools.partial(attend_kernel, index * rows),
        out_shape=jax.ShapeDtypeStruct(shape, jnp.float32),
        grid=(1,),
        in_specs=[
            SCALAR,
            pl.BlockSpec((rows, width), lambda i: (index, 0)),
            pl.BlockSpec((keys, width), lambda i: (0, 0)),
            whole(strip),
        ],
        out_specs=pl.BlockSpec(shape, lambda i: (0, 0)),
        compiler_params=params(),
        cost_estimate=cost(
            4 * heads * rows * keys * LANES, 2 * (rows + keys) * width, heads * rows * keys
        ),
    )(length, qkv, qkv, strip)


def forward_kernel(level_ref, part_ref, other_ref, across_ref, outer_ref, *refs):
    x_ref, dout_ref, wo_ref, gain_ref, wg_ref, wu_ref, wd_ref = refs[:7]
    hidden_ref, normed_t_ref, activ_ref, dgate_ref, dup_ref, mlp_ref, dn_ref = refs[7:14]
    normed_ref = refs[14]
    rows = x_ref.shape[0]

    @pl.when(pl.program_id(0) == 0)
    def _():
        level = level_ref[0]
        inner = (level == 1) | (level == 2)
        width = part_ref.shape[1]
        second = jnp.where(inner, across_ref[:rows, width:], outer_ref[:rows, :width])
        third = jnp.where(inner, across_ref[:rows, :width], outer_ref[:rows, width:])
        mixed = jnp.concatenate([part_ref[:rows, :], other_ref[:rows, :], second, third], 1)
        hidden = x_ref[...].astype(jnp.float32) + dot32_nt(mixed.astype(jnp.bfloat16), wo_ref[...])
        hidden_ref[...] = hidden
        rms = lax.rsqrt(jnp.mean(hidden * hidden, -1, keepdims=True) + norm_eps)
        normed = (hidden * rms * gain_ref[...]).astype(jnp.bfloat16)
        normed_ref[...] = normed
        normed_t_ref[...] = normed.T
        mlp_ref[...] = jnp.zeros_like(mlp_ref)
        dn_ref[...] = jnp.zeros_like(dn_ref)

    normed = normed_ref[...]
    gate = dot32(normed, wg_ref[...])
    up = dot32(normed, wu_ref[...])
    dact = dot32_nt(dout_ref[...], wd_ref[...])
    sigmoid = jax.nn.sigmoid(gate)
    silu = gate * sigmoid
    activ = (silu * up).astype(jnp.bfloat16)
    dgate = (dact * up * sigmoid * (1.0 + gate * (1.0 - sigmoid))).astype(jnp.bfloat16)
    dup = (dact * silu).astype(jnp.bfloat16)
    activ_ref[...] = activ
    dgate_ref[...] = dgate
    dup_ref[...] = dup
    mlp_ref[...] += dot32(activ, wd_ref[...])
    dn_ref[:rows, :] += dot32_nt(dgate, wg_ref[...]) + dot32_nt(dup, wu_ref[...])


def forward_chunk(level, gathered, tokens, dout, w_out, gain, w_gate, w_up, w_down, index, rows):
    depth = tokens.shape[1]
    units = w_gate.shape[1]
    block = 512
    own_rows = pl.BlockSpec((rows, depth), lambda i: (index, 0))
    by_units = pl.BlockSpec((depth, block), lambda i: (0, i))
    gain = gain[None, :]
    f32, bf16 = jnp.float32, jnp.bfloat16
    outs = [
        jax.ShapeDtypeStruct((rows, depth), f32),
        jax.ShapeDtypeStruct((depth, rows), bf16),
        jax.ShapeDtypeStruct((rows, units), bf16),
        jax.ShapeDtypeStruct((rows, units), bf16),
        jax.ShapeDtypeStruct((rows, units), bf16),
        jax.ShapeDtypeStruct((rows, depth), f32),
        jax.ShapeDtypeStruct((rows + EXTRA, depth), f32),
    ]
    unit_out = pl.BlockSpec((rows, block), lambda i: (0, i))
    return pl.pallas_call(
        forward_kernel,
        out_shape=outs,
        grid=(units // block,),
        in_specs=[SCALAR]
        + [whole(array) for array in gathered]
        + [own_rows, own_rows, whole(w_out), whole(gain), by_units, by_units]
        + [pl.BlockSpec((block, depth), lambda i: (i, 0))],
        out_specs=[
            whole(outs[0]),
            whole(outs[1]),
            unit_out,
            unit_out,
            unit_out,
            whole(outs[5]),
            whole(outs[6]),
        ],
        scratch_shapes=[pltpu.VMEM((rows, depth), bf16)],
        compiler_params=params(),
        cost_estimate=cost(
            2 * rows * depth * (6 * units + w_out.shape[1]),
            2 * depth * (3 * units + w_out.shape[1]) + 22 * rows * depth,
            rows * units,
        ),
    )(level, *gathered, tokens, dout, w_out, gain, w_gate, w_up, w_down)


def hidden_grad(inner, total_ref, final_ref, hidden_ref, dout_ref, gain_ref):
    dnormed = jnp.where(inner, total_ref[...], final_ref[...])
    hidden = hidden_ref[...]
    rms = lax.rsqrt(jnp.mean(hidden * hidden, -1, keepdims=True) + norm_eps)
    scaled = dnormed * gain_ref[...]
    shift = jnp.mean(scaled * hidden, -1, keepdims=True)
    dhid = dout_ref[...].astype(jnp.float32) + (rms * scaled - hidden * (rms**3 * shift))
    return dhid, dnormed * (hidden * rms)


def backward_kernel(start, full, adding, level_ref, total_ref, final_ref, hidden_ref, dout_ref, *refs):
    gain_two_ref, wo_ref, q_ref = refs[:3]
    kv_here = q_ref.shape[1] // KV_WIDE
    refs = refs[3:]
    kv_refs, refs = refs[: 2 * kv_here], refs[2 * kv_here :]
    part_ref, place_ref, strip_ref, cos_ref, sin_ref = refs[:5]
    dhid_ref, low_ref, dn_ref = refs[-3:]
    outs = refs[5:-3]
    if full:
        x_ref, gain_one_ref, other_ref, across_ref, outer_ref, w_ref = outs[:6]
        outs = outs[6:]
    count = (5 if start > 0 else 4) if full else 2
    acc_ref = outs[0] if adding else None
    outs = outs[-count:]
    dhid_t_ref, dqkv_ref = outs[:2]
    if full:
        input_grad_ref, gains_ref = outs[2:4]
    rows = q_ref.shape[0]
    keys = kv_refs[0].shape[0]
    shard = pl.program_id(0)
    level = level_ref[0]
    inner = (level == 1) | (level == 2)

    @pl.when(shard == 0)
    def _():
        dhid, dgain = hidden_grad(
            inner, total_ref, final_ref, hidden_ref, dout_ref, gain_two_ref
        )
        dhid_ref[...] = dhid
        low = dhid.astype(jnp.bfloat16)
        low_ref[...] = low
        dhid_t_ref[...] = low.T
        if full:
            gains_ref[...] = jnp.zeros_like(gains_ref)
            gains_ref[1:2, :] = jnp.sum(dgain, 0, keepdims=True)
            dn_ref[...] = jnp.zeros_like(dn_ref)

    def rotate_back(grads):
        turned = grads * cos_ref[...] - pltpu.roll(grads, LANES // 2, 1) * sin_ref[...]
        return turned.astype(jnp.bfloat16)

    dmixed_all = dot32(low_ref[...], wo_ref[...]).astype(jnp.bfloat16)
    mixed = part_ref[...]
    if full:
        far = jnp.where(inner, across_ref[...], outer_ref[...])
        far = jnp.where(shard == 1, other_ref[...], far)
        mixed = jnp.where(shard == 0, mixed, far)
    products = dmixed_all.astype(jnp.float32) * dot_split(mixed[:rows], place_ref[...])
    causal = lax.broadcasted_iota(jnp.int32, (rows, rows), 0) <= lax.broadcasted_iota(
        jnp.int32, (rows, rows), 1
    )
    grads = []
    for kv in range(kv_here):
        key_ref, value_ref = kv_refs[2 * kv : 2 * kv + 2]
        heads = range(kv * GROUP, (kv + 1) * GROUP)
        lanes = {h: slice(h * LANES, (h + 1) * LANES) for h in heads}
        row_dots = {h: jnp.sum(products[:, lanes[h]].T, axis=0, keepdims=True) for h in heads}
        log_sums = {h: mixed[rows + h : rows + h + 1, :rows] for h in heads}
        dqueries = dict.fromkeys(heads)
        here = slice(2 * kv * LANES, (2 * kv + 1) * LANES)
        there = slice((2 * kv + 1) * LANES, (2 * kv + 2) * LANES)
        for tile in range(keys // rows):
            span = slice(tile * rows, (tile + 1) * rows)
            key = key_ref[span, :]
            value = value_ref[span, :]
            key_t = key.T
            dkey = None if acc_ref is None else acc_ref[span, here]
            dvalue = None if acc_ref is None else acc_ref[span, there]
            last = tile * rows == start
            for h in heads:
                at = kv * KV_WIDE + (h % GROUP) * LANES
                query = q_ref[:, at : at + LANES]
                dmixed = dmixed_all[:, lanes[h]]
                raw = dot32_nt(key, query)
                probs = jnp.exp2(raw * score_scale_log2 - log_sums[h])
                if last:
                    probs = jnp.where(causal, probs, 0.0)
                dprobs = dot32_nt(value, dmixed)
                dscores = (probs * (dprobs - row_dots[h])).astype(jnp.bfloat16)
                dquery = dot32(key_t, dscores)
                dqueries[h] = dquery if dqueries[h] is None else dqueries[h] + dquery
                dkey_one = dot32(dscores, query)
                dvalue_one = dot32(probs.astype(jnp.bfloat16), dmixed)
                dkey = dkey_one if dkey is None else dkey + dkey_one
                dvalue = dvalue_one if dvalue is None else dvalue + dvalue_one
            if full and not last:
                outs[4][span, here] = dkey
                outs[4][span, there] = dvalue
        grads += [rotate_back(dqueries[h].T * score_scale) for h in heads]
        grads.append(rotate_back(dkey * score_scale))
        grads.append(dvalue.astype(jnp.bfloat16))
    grads = jnp.concatenate(grads, 1)
    if full:
        dn_ref[...] += dot32_nt(grads, w_ref[...])

    @pl.when(shard == 0)
    def _():
        wide = strip_ref.shape[1]
        for kv in range(kv_here):
            dqkv_ref[:, kv * wide : (kv + 1) * wide] = dot32(
                grads[:, kv * KV_WIDE : (kv + 1) * KV_WIDE], strip_ref[...]
            ).astype(jnp.bfloat16)

    if not full:
        return

    @pl.when(shard == pl.num_programs(0) - 1)
    def _():
        dnormed = dn_ref[...]
        inputs = x_ref[...].astype(jnp.float32)
        rms = lax.rsqrt(jnp.mean(inputs * inputs, -1, keepdims=True) + norm_eps)
        scaled = dnormed * gain_one_ref[...]
        shift = jnp.mean(scaled * inputs, -1, keepdims=True)
        grad = dhid_ref[...] + (rms * scaled - inputs * (rms**3 * shift))
        input_grad_ref[...] = grad.astype(jnp.bfloat16)
        gains_ref[0:1, :] = jnp.sum(dnormed * (inputs * rms), 0, keepdims=True)


def backward_chunk(
    level, sums_two, hidden, dout, tokens, gains, weights, qkv, gathered, places, tables, acc,
    index, rows, full=True, grad_into=None
):
    start = index * rows
    keys = start + rows
    depth = tokens.shape[1]
    out_pad, qkv_pad = weights
    place_out, strip = places
    far_rows, width = gathered[0].shape
    out_wide = place_out.shape[1]
    kv_here = out_wide // (GROUP * LANES)
    wide = kv_here * KV_WIDE
    levels = qkv.shape[1] // wide
    own_rows = pl.BlockSpec((rows, depth), lambda t: (index, 0))
    table = pl.BlockSpec((rows, LANES), lambda t: (index, 0))
    gains = [gain[None, :] for gain in gains]
    key_value = lambda at: pl.BlockSpec(
        (keys, LANES), lambda t: (0, (wide // LANES) * t + at)
    )
    across = pl.BlockSpec((far_rows, width), lambda t: (0, jnp.where(t == 2, 1, 0)))
    outer = pl.BlockSpec((far_rows, width), lambda t: (0, jnp.where(t == 3, 1, 0)))
    in_specs = [
        SCALAR,
        whole(hidden),
        whole(hidden),
        whole(hidden),
        own_rows,
        whole(gains[1]),
        pl.BlockSpec((depth, out_wide), lambda t: (0, t)),
        pl.BlockSpec((rows, wide), lambda t: (index, t)),
    ]
    for kv in range(kv_here):
        at = kv * (KV_WIDE // LANES) + GROUP
        in_specs += [key_value(at), key_value(at + 1)]
    in_specs += [
        whole(gathered[0]),
        whole(place_out),
        whole(strip),
        table,
        table,
    ]
    args = [level, *sums_two, hidden, dout, gains[1], out_pad]
    args += [qkv] * (1 + 2 * kv_here)
    args += [gathered[0], place_out, strip, *tables]
    sums_wide = 2 * kv_here * LANES
    if full:
        in_specs += [own_rows, whole(gains[0]), whole(gathered[1]), across, outer]
        in_specs.append(pl.BlockSpec((depth, wide), lambda t: (0, t)))
        args += [tokens, gains[0], *gathered[1:], qkv_pad]
    if acc is not None:
        in_specs.append(pl.BlockSpec((keys, sums_wide), lambda t: (0, t)))
        args.append(acc)
    f32, bf16 = jnp.float32, jnp.bfloat16
    outs = [
        jax.ShapeDtypeStruct((depth, rows), bf16),
        jax.ShapeDtypeStruct((rows, kv_here * strip.shape[1]), bf16),
        jax.ShapeDtypeStruct(tokens.shape, bf16),
        jax.ShapeDtypeStruct((8, depth), f32),
    ]
    outs = outs if full else outs[:2]
    out_specs = [whole(out) for out in outs]
    aliases = {}
    if full:
        out_specs[2] = own_rows
        if grad_into is not None:
            aliases = {len(args): 2}
            in_specs.append(pl.BlockSpec(memory_space=pl.ANY))
            args.append(grad_into)
    if full and start > 0:
        outs.append(jax.ShapeDtypeStruct((start, levels * sums_wide), f32))
        out_specs.append(pl.BlockSpec((start, sums_wide), lambda t: (0, t)))
    results = pl.pallas_call(
        functools.partial(backward_kernel, start, full, acc is not None),
        out_shape=outs,
        grid=(levels if full else 1,),
        input_output_aliases=aliases,
        in_specs=in_specs,
        out_specs=out_specs,
        scratch_shapes=[
            pltpu.VMEM((rows, depth), f32),
            pltpu.VMEM((rows, depth), bf16),
            pltpu.VMEM((rows, depth), f32),
        ],
        compiler_params=params(),
        cost_estimate=cost(
            levels * rows * (20 * kv_here * keys * LANES + 2 * depth * (out_wide + wide)),
            2 * depth * levels * (out_wide + wide) + 16 * rows * depth,
            levels * kv_here * GROUP * rows * keys,
        ),
    )(*args)
    return results[:4], (results[4] if full and start > 0 else None)


def rows_kernel(lefts, groups, adding, picked, together, side_ref, *refs):
    refs = list(refs)
    held_ref = refs.pop()
    out_refs = refs[-len(picked) :]
    refs = refs[: -len(picked)]
    recv_ref = refs.pop() if adding else None
    step = pl.program_id(0)
    left_refs = []
    for count in lefts:
        left_refs.append(refs[:count])
        refs = refs[count:]
    rights = []
    for _ in groups:
        rights.append(refs[:CHUNKS])
        refs = refs[CHUNKS:]
    rows = left_refs[0][0].shape[0]
    blocks = held_ref.shape[1] // rows

    @pl.when(step == 0)
    def _():
        for which, pieces in enumerate(left_refs):
            for n, ref in enumerate(pieces):
                m, j = n % blocks, n // blocks
                wide = ref.shape[1]
                held_ref[which, m * rows : (m + 1) * rows, j * wide : (j + 1) * wide] = ref[...]

    chunk = held_ref.shape[2] // CHUNKS
    whole_columns = slice(0, out_refs[0].shape[1])

    def give(group, left, columns):
        right = jnp.concatenate([ref[:chunk, :].astype(jnp.bfloat16) for ref in group], 0)
        total = dot32(held_ref[left], right)
        if recv_ref is not None:
            total = total + recv_ref[:, columns]
        for out_ref, parts in zip(out_refs, picked):
            at = 0
            for start, size in parts:
                out_ref[at : at + size, columns] = total[start : start + size]
                at += size

    begin = 0
    for group, (left, first, steps) in zip(rights, groups):
        if together:
            width = group[0].shape[1]
            give(group, left, slice(begin, begin + width))
            begin += width
        else:

            @pl.when((step >= first) & (step < first + steps))
            def _(group=group, left=left):
                give(group, left, whole_columns)


def rows_of(lefts, groups, side, rows, blocks, step, recv=None, picked=None):
    if picked is None:
        picked = [[(0, rows * blocks)]]
    at = lambda m: lambda i, side: ((m ^ side[2]) * side[1] + side[0], 0)
    specs = []
    args = []
    counts = []
    for left in lefts:
        pieces = left if isinstance(left, list) else [left]
        counts.append(len(pieces) * blocks)
        for piece in pieces:
            for m in range(blocks):
                specs.append(pl.BlockSpec((rows, piece.shape[1]), at(m)))
                args.append(piece)
    tokens = sum(piece.shape[1] for piece in pieces)
    first = 0
    plan = []
    together = step is None
    for which, rights in groups:
        if together:
            plan.append((which, 0, 1))
            specs += [whole(right) for right in rights]
            args += rights
            first += rights[0].shape[1]
            continue
        steps = rights[0].shape[1] // step
        plan.append((which, first, steps))
        for right in rights:
            pick = lambda i, side, first=first, steps=steps: (0, jnp.clip(i - first, 0, steps - 1))
            specs.append(pl.BlockSpec((right.shape[0], step), pick))
            args.append(right)
        first += steps
    if together:
        first, step = 1, first
    total = first * step
    block = lambda height: pl.BlockSpec((height, step), lambda i, side: (0, i))
    if recv is not None:
        specs.append(block(rows * blocks))
        args.append(recv)
    heights = [sum(size for _, size in parts) for parts in picked]
    results = pl.pallas_call(
        functools.partial(rows_kernel, counts, plan, recv is not None, picked, together),
        out_shape=[jax.ShapeDtypeStruct((height, total), jnp.float32) for height in heights],
        grid_spec=pltpu.PrefetchScalarGridSpec(
            num_scalar_prefetch=1,
            grid=(first,),
            in_specs=specs,
            out_specs=[block(height) for height in heights],
            scratch_shapes=[pltpu.VMEM((len(lefts), rows * blocks, tokens), jnp.bfloat16)],
        ),
        compiler_params=params(),
        cost_estimate=cost(
            2 * rows * blocks * tokens * total,
            4 * rows * blocks * total + 2 * tokens * (total + rows * blocks),
        ),
    )(side, *args)
    return results[0] if len(picked) == 1 else results


def shards(
    tokens,
    lengths,
    positions,
    cotangent,
    norm_gain,
    w_query,
    w_key,
    w_value,
    w_out,
    mlp_gain,
    w_gate,
    w_up,
    w_down,
):
    seq_rows, depth = tokens.shape
    chips = lax.axis_size("chip")
    dp = chips * 2
    tp = lax.axis_size("tp")
    chip = lax.axis_index("chip")
    core = lax.axis_index("core")
    level = lax.axis_index("tp")
    low = level < 2
    inner = (level == 1) | (level == 2)
    heads_here = w_query.shape[1] // HD
    kv_here = w_key.shape[1] // HD
    rows = seq_rows // CHUNKS
    slice_rows = depth // dp
    level_ref = level.astype(jnp.int32).reshape(1)
    by_hand = dp == 8
    swap = lambda array: lax.ppermute(array, "core", [(0, 1), (1, 0)])
    to_level = lambda array, s: along(array, [(t, t ^ s) for t in range(tp)])

    at_row = (chip * 2 + core) * slice_rows
    cols = lambda w: lax.dynamic_slice_in_dim(w, at_row, slice_rows, 1).astype(jnp.float32).T
    (out_slice,) = fence(cols(w_out))
    qkv_slice = jnp.concatenate(
        [
            lax.dynamic_slice_in_dim(w_query, at_row, slice_rows, 0).astype(jnp.float32),
            cols(w_key.T),
            cols(w_value.T),
        ],
        1,
    )
    out_slice, qkv_slice = fence(out_slice, qkv_slice)
    out_near = along(out_slice, PAIRS)
    qkv_near = along(qkv_slice, PAIRS)
    meta = jnp.stack([chip, core]).astype(jnp.int32)

    pq = place_query(heads_here)
    pkv = place_key_value(kv_here)
    p_all = place_all(heads_here, kv_here)
    strip_one = place_all(GROUP, 1).T
    p_out = place_plain(heads_here)
    strip_out = p_out.T

    half_dim = HD // 2
    freqs = rope_base ** (-(jnp.arange(half_dim).astype(jnp.float32) * 2.0 / HD))
    freqs = jnp.pad(freqs, (0, LANES // 2 - half_dim))
    angles = positions.astype(jnp.float32)[:, None] * jnp.concatenate([freqs, freqs])[None, :]
    cosines = jnp.cos(angles)
    sines = jnp.sin(angles) * jnp.where(jnp.arange(LANES) < LANES // 2, -1.0, 1.0)

    cosines, sines, out_near = fence(cosines, sines, out_near)
    out_across = along(jnp.stack([out_slice, out_near]), MIDDLE)
    qkv_own, normed_one, own_pad = start(
        tokens, norm_gain, w_query, w_key.T, w_value.T, pq, pkv, cosines, sines
    )

    def far_slices(near, across, outer):
        return jnp.stack(
            [
                near,
                jnp.where(inner, across[1], outer[0]),
                jnp.where(inner, across[0], outer[1]),
            ]
        )

    order = list(reversed(range(CHUNKS)))
    c0, c1, c2, c3 = order
    own, other, across, outer = {}, {}, {}, {}
    part, total, final = {}, {}, {}

    def hop_1(j):
        other[j] = along(own[j], PAIRS)

    def hop_2(j):
        across[j] = along(jnp.concatenate([own[j], other[j]], 1), MIDDLE)

    def hop_3(j):
        outer[j] = along(across[j], OUTWARD)

    coming = {}

    def add_1(j):
        coming[j] = along(part[j], INWARD)

    def add_2(j):
        total[j] = part[j][:rows] + coming[j][:rows]
        coming[j] = along(total[j], MIDDLE)

    def add_3(j, inward, extra=0):
        both = jnp.where(inner, total[j] + coming[j], inward)
        total[j] = jnp.pad(both, ((0, extra), (0, 0)))
        final[j] = along(total[j], PAIRS)
        return final[j]

    def to_chip(array, m):
        return lax.ppermute(array, "chip", [(i, i ^ m) for i in range(chips)])

    def over_chips_1(piece):
        cut = piece.shape[1] // 2
        one, two = piece[:, :cut], piece[:, cut:]
        return jnp.stack([one, to_chip(one, 1)]), jnp.stack([two, to_chip(two, 2)])

    def over_chips_2(one, two):
        return one, to_chip(one, 2), two, to_chip(two, 1)

    def over_chips_3(one, one_far, two, two_far):
        upper = jnp.stack([one[0], one[1], one_far[0], one_far[1]])
        lower = jnp.stack([two[0], two_far[0], two[1], two_far[1]])
        return jnp.concatenate([upper, lower], 2)

    qkv_own, out_across, qkv_near = fence(qkv_own, out_across, qkv_near)
    out_outer = along(out_across, OUTWARD)
    qkv_across = along(jnp.stack([qkv_slice, qkv_near]), MIDDLE)
    own[c0] = attend(lengths, qkv_own, strip_out, c0, rows)
    own[c1] = attend(lengths, qkv_own, strip_out, c1, rows)
    own, qkv_own, out_outer = fence(own, qkv_own, out_outer)
    others = along(jnp.concatenate([own[c0], own[c1]], 0), PAIRS)
    out_far = far_slices(out_near, out_across, out_outer)
    out_mine = over_chips_1(out_far) if by_hand else out_far
    own[c2] = attend(lengths, qkv_own, strip_out, c2, rows)
    own[c3] = attend(lengths, qkv_own, strip_out, c3, rows)
    own[c3], qkv_across = fence(own[c3], qkv_across)
    qkv_outer = along(qkv_across, OUTWARD)
    own, others, normed_one, w_out, out_mine = fence(own, others, normed_one, w_out, out_mine)
    other[c0], other[c1] = others[: rows + EXTRA], others[rows + EXTRA :]
    if by_hand:
        out_mine = over_chips_2(*out_mine)
    else:
        out_mine = lax.all_gather(out_mine, ("chip", "core"))
    hop_2(c0)
    dout, dout_t, normed_one_t = turn(lengths, cotangent, normed_one)
    w_out_t = w_out.T
    own, other, across, dout, dout_t, normed_one_t, w_out_t, out_mine, qkv_outer = fence(
        own, other, across, dout, dout_t, normed_one_t, w_out_t, out_mine, qkv_outer
    )
    hop_1(c2)
    hop_3(c0)
    hop_2(c1)
    qkv_far = lax.all_gather(far_slices(qkv_near, qkv_across, qkv_outer), ("chip", "core"))
    if by_hand:
        out_mine = over_chips_3(*out_mine)
        out_theirs = swap(out_mine)
        out_pad, out_plain = spread(
            spread_out_kernel,
            meta,
            w_out_t,
            [p_out],
            out_mine,
            out_theirs,
            [4 * p_out.shape[1], 4 * p_out.shape[0]],
        )
    else:
        plain = [w_out_t] + [
            out_mine[:, s].reshape(depth, -1).astype(jnp.bfloat16) for s in range(tp - 1)
        ]
        out_plain = jnp.concatenate(plain, 1)
        out_pad = jnp.concatenate([dot32(w, p_out).astype(jnp.bfloat16) for w in plain], 1)
    hidden, normed_t, activ, dgate, dup, mlp_part = {}, {}, {}, {}, {}, {}

    def feed(j):
        gathered = (own[j], other[j], across[j], outer[j])
        (hidden[j], normed_t[j], activ[j], dgate[j], dup[j], mlp_part[j], part[j]) = forward_chunk(
            level_ref, gathered, tokens, dout, out_plain, mlp_gain, w_gate, w_up, w_down, j, rows
        )

    own, other, across, outer, out_pad, out_plain = fence(
        own, other, across, outer, out_pad, out_plain
    )
    hop_1(c3)
    hop_3(c1)
    hop_2(c2)
    feed(c0)
    part, other = fence(part, other)
    add_1(c0)
    own, other, across, outer, part, hidden = fence(own, other, across, outer, part, hidden)
    hop_3(c2)
    hop_2(c3)
    feed(c1)
    qkv_far, hidden[c1] = fence(qkv_far, hidden[c1])
    qkv_pad = spread_qkv(own_pad, pq, pkv, qkv_far)
    own, other, across, outer, part, total, coming, hidden, qkv_pad = fence(
        own, other, across, outer, part, total, coming, hidden, qkv_pad
    )
    add_1(c1)
    hop_3(c3)
    add_2(c0)
    feed(c2)
    qkv_pad, hidden[c2] = fence(qkv_pad, hidden[c2])
    qkv = project(normed_one, qkv_pad, cosines, sines, qkv_own)
    own, other, across, outer, part, total, coming, hidden, qkv = fence(
        own, other, across, outer, part, total, coming, hidden, qkv
    )
    coming[c2] = add_3(c0, part[c2][:rows])
    add_2(c1)
    feed(c3)

    listed = lambda pieces: [pieces[j] for j in range(CHUNKS)]
    keep_side = jnp.stack([core, 2, 0]).astype(jnp.int32)
    keep_turned = jnp.stack([core, 2, chip]).astype(jnp.int32)
    send_side = jnp.stack([1 - core, 2, 0]).astype(jnp.int32)
    send_turned = jnp.stack([1 - core, 2, chip]).astype(jnp.int32)
    all_rows = jnp.array([0, 1, 0], jnp.int32)

    def send_rows(lefts, groups, step, side=send_side):
        if not by_hand:
            return rows_of(lefts, groups, all_rows, depth // 4, 4, step)
        return rows_of(lefts, groups, side, slice_rows, chips, step)

    def keep_rows(lefts, groups, received, step, side=keep_side, picked=None):
        if not by_hand:
            return received
        return rows_of(lefts, groups, side, slice_rows, chips, step, received, picked)

    def swap_rows(array):
        return swap(array) if by_hand else array

    def scatter(array, axes):
        return lax.psum_scatter(array, axes, scatter_dimension=0, tiled=True)

    units = w_gate.shape[1]
    mlp_args = (
        [listed(normed_t), dout_t],
        [(0, listed(dgate)), (0, listed(dup)), (1, listed(activ))],
    )
    acc = None
    input_grad = None
    dhid_t, dqkv_own, gains = {}, {}, {}

    def back(j):
        nonlocal acc, input_grad
        (dhid_t[j], dqkv_own[j], input_grad, gains[j]), acc = back_some(j, True)

    def back_own(j):
        return back_some(j, False)[0]

    def back_some(j, full):
        return backward_chunk(
            level_ref,
            (total[j], final[j]),
            hidden[j],
            dout,
            tokens,
            (norm_gain, mlp_gain),
            (out_pad, qkv_pad),
            qkv,
            (own[j], other[j], across[j], outer[j]),
            (p_out, strip_one),
            (cosines, sines),
            acc,
            j,
            rows,
            full,
            input_grad,
        )

    grad_mlp = rows_of(*mlp_args, all_rows, depth // 4, 4, units // 2)
    own, other, across, outer, part, total, coming, final, hidden, grad_mlp = fence(
        own, other, across, outer, part, total, coming, final, hidden, grad_mlp
    )
    coming[c3] = add_3(c1, part[c3][:rows])
    add_2(c2)
    back(c0)

    near = lambda: jnp.where(low, mlp_part[1], mlp_part[2])
    edge = lambda: jnp.where(low, mlp_part[0], mlp_part[3])
    leave_far = lambda: jnp.where(low, mlp_part[3], mlp_part[0])
    leave_near = lambda: jnp.where(low, mlp_part[2], mlp_part[1])
    total, coming, final, hidden, mlp_part, acc, dhid_t, grad_mlp = fence(
        total, coming, final, hidden, mlp_part, acc, dhid_t, grad_mlp
    )
    grad_mlp = scatter(grad_mlp, ("chip", "core"))
    far_sum = add_3(c2, leave_far())
    add_2(c3)
    back(c1)
    total, coming, final, hidden, mlp_part, far_sum, acc, dhid_t = fence(
        total, coming, final, hidden, mlp_part, far_sum, acc, dhid_t
    )
    add_3(c3, leave_near(), EXTRA)
    far_in = along(leave_far() + far_sum, MIDDLE)
    back(c2)
    total, final, hidden, acc, dhid_t = fence(total, final, hidden, acc, dhid_t)
    dhid_t[c3], dqkv_own[c3] = back_own(c3)
    dhid_t, dqkv_own, far_in, mlp_part, final = fence(
        dhid_t, dqkv_own, far_in, mlp_part, final
    )
    last = along(jnp.where(inner, edge() + far_in, near()), PAIRS)
    near_in = along(leave_near() + final[c3][:rows], MIDDLE)
    q_cols = heads_here * HD
    attn_args = (
        [listed(dhid_t), normed_one_t],
        [(0, listed(own)), (1, listed(dqkv_own))],
    )
    sent = swap_rows(send_rows(*attn_args, None, send_turned))
    total, final, hidden, acc, sent = fence(total, final, hidden, acc, sent)
    if by_hand:
        half = slice_rows // 2
        upper = lambda m: (m * slice_rows, half)
        lower = lambda m: (m * slice_rows + half, half)
        picked = [
            [upper(1), upper(3)],
            [upper(0), upper(2)],
            [lower(2), lower(3)],
            [lower(0), lower(1)],
        ]
        pieces = keep_rows(*attn_args, sent, None, keep_turned, picked)
        pieces, hidden = fence(pieces, hidden)
        one_away, one, two_away, two = pieces
        pieces = (one, to_chip(one_away, 1), two, to_chip(two_away, 2))
    else:
        pieces = scatter(sent, ("chip", "core"))
    back(c3)
    pieces, gains, input_grad = fence(pieces, gains, input_grad)
    gain_sums = gains[0] + gains[1] + gains[2] + gains[3]
    gain_sums = gain_sums + swap(gain_sums)
    gain_sums, last, near_in = fence(gain_sums, last, near_in)
    if by_hand:
        others = [to_chip(gain_sums, m) for m in range(1, chips)]
        gain_sums = sum(others, gain_sums)
        one = pieces[0] + pieces[1]
        two = pieces[2] + pieces[3]
        one = one[:half] + to_chip(one[half:], 2)
        two = two[:half] + to_chip(two[half:], 1)
        attn = jnp.concatenate([one, two], 0)
    else:
        gain_sums = lax.psum(gain_sums, "chip")
        attn = pieces
    gain_rows = lax.dynamic_slice_in_dim(gain_sums, at_row, slice_rows, 1)
    grad_out, grad_qkv = attn[:, :q_cols], attn[:, q_cols:]
    mlp_rows = jnp.where(inner, near() + near_in, edge()) + last
    hidden_rows = jnp.where(
        low,
        jnp.where(level == 0, hidden[0], hidden[1]),
        jnp.where(level == 2, hidden[2], hidden[3]),
    )
    layer_out = (hidden_rows + mlp_rows).astype(jnp.bfloat16)
    one = strip_one.shape[1]
    picked = lambda at, width: jnp.concatenate(
        [grad_qkv[:, kv * one + at : kv * one + at + width] for kv in range(kv_here)], 1
    )
    return (
        layer_out,
        input_grad,
        gain_rows[0],
        picked(0, GROUP * HD),
        picked(GROUP * HD, HD),
        picked((GROUP + 1) * HD, HD),
        grad_out.T,
        gain_rows[1],
        grad_mlp[:, :units],
        grad_mlp[:, units : 2 * units],
        grad_mlp[:, 2 * units :].T,
    )


def solution(mesh):
    devices = mesh.devices
    dp, tp = devices.shape
    split = Mesh(devices.reshape(dp // 2, 2, tp), ("chip", "core", "tp"))
    data = ("chip", "core")
    return jax.shard_map(
        shards,
        mesh=split,
        in_specs=(
            P(data, None),
            P(data),
            P(data),
            P(data, None),
            P(),
            P(None, "tp"),
            P(None, "tp"),
            P(None, "tp"),
            P("tp", None),
            P(),
            P(None, "tp"),
            P(None, "tp"),
            P("tp", None),
        ),
        out_specs=(
            P(("chip", "core", "tp"), None),
            P(data, None),
            P(data),
            P(data, "tp"),
            P(data, "tp"),
            P(data, "tp"),
            P("tp", data),
            P(data),
            P(data, "tp"),
            P(data, "tp"),
            P("tp", data),
        ),
        check_vma=False,
    )
```

```python
import functools

import jax
import jax.numpy as jnp
from jax import lax
from jax.experimental import pallas as pl
from jax.experimental.pallas import tpu as pltpu
from jax.sharding import Mesh
from jax.sharding import PartitionSpec as P

HD = 96
LANES = 128
GROUP = 2
KV_WIDE = (GROUP + 2) * LANES
rope_base = 100000.0
norm_eps = 1e-05
masked_score = -1e30
far_away = 1e30
score_scale = HD ** (-0.5)
score_scale_log2 = score_scale * 1.4426950408889634
CHUNKS = 4
EXTRA = 8
VMEM_BYTES = 56 * 1024 * 1024
NT = (((1,), (1,)), ((), ()))


def params():
    return pltpu.CompilerParams(vmem_limit_bytes=VMEM_BYTES)


def cost(flops, moved, exps=0):
    return pl.CostEstimate(
        flops=flops // 1024, bytes_accessed=moved // 1024, transcendentals=exps // 1024
    )


def dot32(a, b):
    return jnp.dot(a, b, preferred_element_type=jnp.float32)


def dot32_nt(a, b):
    return lax.dot_general(a, b, NT, preferred_element_type=jnp.float32)


def dot_split(a, places):
    high = a.astype(jnp.bfloat16)
    rest = (a - high.astype(jnp.float32)).astype(jnp.bfloat16)
    return dot32(high, places) + dot32(rest, places)


def fence(*trees):
    return lax.optimization_barrier(trees)


def whole(array, buffers=None):
    zeros = (0,) * len(array.shape)
    return pl.BlockSpec(array.shape, lambda *_: zeros)


SCALAR = pl.BlockSpec(memory_space=pltpu.SMEM)
ANYWHERE = pl.BlockSpec(memory_space=pl.ANY)


def halves(entry):
    half_dim = HD // 2
    return (entry // half_dim) * (LANES // 2) + entry % half_dim


def placement(lanes, width):
    return (lanes[:, None] == jnp.arange(width)[None, :]).astype(jnp.bfloat16)


def place_query(heads):
    source = jnp.arange(heads * HD)
    return placement((source // HD) * LANES + halves(source % HD), heads * LANES)


def place_key_value(kv_heads):
    source = jnp.arange(kv_heads * HD)
    head = source // HD
    keys = head * 2 * LANES + halves(source % HD)
    values = head * 2 * LANES + LANES + source % HD
    return placement(jnp.concatenate([keys, values]), kv_heads * 2 * LANES)


def place_all(heads, kv_heads):
    source = jnp.arange(heads * HD)
    head = source // HD
    query = (head // GROUP) * KV_WIDE + (head % GROUP) * LANES + halves(source % HD)
    source = jnp.arange(kv_heads * HD)
    base = (source // HD) * KV_WIDE + GROUP * LANES
    keys = base + halves(source % HD)
    values = base + LANES + source % HD
    return placement(jnp.concatenate([query, keys, values]), kv_heads * KV_WIDE)


def place_plain(heads):
    source = jnp.arange(heads * HD)
    return placement((source // HD) * LANES + source % HD, heads * LANES)


PAIRS = [(0, 1), (1, 0), (2, 3), (3, 2)]
INWARD = [(0, 1), (3, 2)]
MIDDLE = [(1, 2), (2, 1)]
OUTWARD = [(1, 0), (2, 3)]


def along(part, pairs):
    return lax.ppermute(part, "tp", pairs)


def store_qkv(out_ref, here, base, query, key_value):
    wide = GROUP * LANES
    for kv in range(key_value.shape[1] // (2 * LANES)):
        at = base + kv * KV_WIDE
        there = slice(kv * 2 * LANES, (kv + 1) * 2 * LANES)
        out_ref[here, at : at + wide] = query[:, kv * wide : (kv + 1) * wide]
        out_ref[here, at + wide : at + KV_WIDE] = key_value[:, there]


def store_turned(out_ref, at, lin, cos_ref, sin_ref):
    for h in range(GROUP + 2):
        one = lin[:, h * LANES : (h + 1) * LANES]
        if h < GROUP + 1:
            one = one * cos_ref[...] + pltpu.roll(one, LANES // 2, 1) * sin_ref[...]
        out_ref[:, at + h * LANES : at + (h + 1) * LANES] = one.astype(jnp.bfloat16)


def spread_out_kernel(meta_ref, own_ref, p_ref, mine_ref, theirs_ref, pad_ref, plain_ref):
    rows, width = mine_ref.shape[2:]
    wide = p_ref.shape[1]
    for side, ref in enumerate((mine_ref, theirs_ref)):
        here = pl.ds(pl.multiple_of((meta_ref[1] ^ side) * rows, rows), rows)
        for s in range(4):
            block = own_ref[here, :] if s == 0 else ref[0, s - 1].astype(jnp.bfloat16)
            plain_ref[here, s * width : (s + 1) * width] = block
            pad_ref[here, s * wide : (s + 1) * wide] = dot32(block, p_ref[...]).astype(
                jnp.bfloat16
            )


def spread_qkv_kernel(pq_ref, pkv_ref, far_ref, _, out_ref):
    parts, _, rows, width = far_ref.shape
    split = pq_ref.shape[0]
    block = far_ref[:, 0].reshape(parts * rows, width).astype(jnp.bfloat16)
    query = dot32(block[:, :split], pq_ref[...]).astype(jnp.bfloat16)
    key_value = dot32(block[:, split:], pkv_ref[...]).astype(jnp.bfloat16)
    store_qkv(out_ref, slice(None), 0, query, key_value)


def spread_qkv(padded, pq, pkv, far):
    total = padded.shape[0]
    dp, others, rows, width = far.shape
    wide = padded.shape[1] // (others + 1)
    parts = max(1, dp // 2)
    block = parts * rows
    return pl.pallas_call(
        spread_qkv_kernel,
        out_shape=jax.ShapeDtypeStruct(padded.shape, jnp.bfloat16),
        grid=(total // block, others),
        in_specs=[
            whole(pq),
            whole(pkv),
            pl.BlockSpec((parts, 1, rows, width), lambda i, s: (i, s, 0, 0)),
            pl.BlockSpec(memory_space=pl.ANY),
        ],
        out_specs=pl.BlockSpec((block, wide), lambda i, s: (i, s + 1)),
        input_output_aliases={3: 0},
        compiler_params=params(),
        cost_estimate=cost(8 * total * width * 512, 20 * total * wide),
    )(pq, pkv, far, padded)


def spread(kernel, meta, own, places, mine, theirs, widths):
    chips, others, rows, width = mine.shape
    total = own.shape[0]
    row_block = lambda m, meta: (meta[0] ^ m, 0)
    piece = pl.BlockSpec((1, others, rows, width), lambda m, meta: (m, 0, 0, 0))
    return pl.pallas_call(
        kernel,
        out_shape=[jax.ShapeDtypeStruct((total, wide), jnp.bfloat16) for wide in widths],
        grid_spec=pltpu.PrefetchScalarGridSpec(
            num_scalar_prefetch=1,
            grid=(chips,),
            in_specs=[pl.BlockSpec((2 * rows, own.shape[1]), row_block)]
            + [whole(place) for place in places]
            + [piece, piece],
            out_specs=[pl.BlockSpec((2 * rows, wide), row_block) for wide in widths],
        ),
        compiler_params=params(),
        cost_estimate=cost(
            8 * total * width * 512, total * (12 * width + 2 * sum(widths))
        ),
    )(meta, own, *places, mine, theirs)


def start_kernel(x_ref, gain_ref, q_ref, k_ref, v_ref, pq_ref, pkv_ref, cos_ref, sin_ref, *outs):
    qkv_ref, normed_ref, pad_ref = outs

    @pl.when(pl.program_id(0) == 0)
    def _():
        split = k_ref.shape[0]
        query = dot32(q_ref[...], pq_ref[...]).astype(jnp.bfloat16)
        key_value = dot32(k_ref[...].T, pkv_ref[:split, :])
        key_value = key_value + dot32(v_ref[...].T, pkv_ref[split:, :])
        store_qkv(pad_ref, slice(None), 0, query, key_value.astype(jnp.bfloat16))

    inputs = x_ref[...].astype(jnp.float32)
    rms = lax.rsqrt(jnp.mean(inputs * inputs, -1, keepdims=True) + norm_eps)
    normed = (inputs * rms * gain_ref[...]).astype(jnp.bfloat16)
    normed_ref[...] = normed
    for kv in range(pad_ref.shape[1] // KV_WIDE):
        at = kv * KV_WIDE
        store_turned(qkv_ref, at, dot32(normed, pad_ref[:, at : at + KV_WIDE]), cos_ref, sin_ref)


def start(tokens, gain, w_query, w_key_t, w_value_t, pq, pkv, cosines, sines):
    total, depth = tokens.shape
    rows = total // CHUNKS
    wide = pq.shape[1] + pkv.shape[1]
    gain = gain[None, :]
    by_rows = lambda width: pl.BlockSpec((rows, width), lambda i: (i, 0))
    arrays = [w_query, w_key_t, w_value_t, pq, pkv]
    shapes = [
        jax.ShapeDtypeStruct((total, 4 * wide), jnp.bfloat16),
        jax.ShapeDtypeStruct((total, depth), jnp.bfloat16),
        jax.ShapeDtypeStruct((depth, 4 * wide), jnp.bfloat16),
    ]
    return pl.pallas_call(
        start_kernel,
        out_shape=shapes,
        grid=(CHUNKS,),
        in_specs=[by_rows(depth), whole(gain)]
        + [whole(array) for array in arrays]
        + [by_rows(LANES), by_rows(LANES)],
        out_specs=[
            by_rows(wide),
            by_rows(depth),
            pl.BlockSpec((depth, wide), lambda i: (0, 0)),
        ],
        compiler_params=params(),
        cost_estimate=cost(2 * total * depth * wide, 12 * total * depth),
    )(tokens, gain, *arrays, cosines, sines)


def turn_kernel(length_ref, cot_ref, normed_ref, dout_ref, dout_t_ref, normed_t_ref):
    rows = cot_ref.shape[0]
    at = pl.program_id(0) * rows + lax.broadcasted_iota(jnp.int32, cot_ref.shape, 0)
    dout = jnp.where(at < length_ref[0], cot_ref[...].astype(jnp.float32), 0.0)
    dout = dout.astype(jnp.bfloat16)
    dout_ref[...] = dout
    dout_t_ref[...] = dout.T
    normed_t_ref[...] = normed_ref[...].T


def turn(length, cotangent, normed):
    total, depth = cotangent.shape
    rows = total // CHUNKS
    by_rows = pl.BlockSpec((rows, depth), lambda i: (i, 0))
    by_columns = pl.BlockSpec((depth, rows), lambda i: (0, i))
    turned = jax.ShapeDtypeStruct((depth, total), jnp.bfloat16)
    return pl.pallas_call(
        turn_kernel,
        out_shape=[jax.ShapeDtypeStruct((total, depth), jnp.bfloat16), turned, turned],
        grid=(CHUNKS,),
        in_specs=[SCALAR, by_rows, by_rows],
        out_specs=[by_rows, by_columns, by_columns],
        compiler_params=params(),
        cost_estimate=cost(total * depth, 10 * total * depth),
    )(length, cotangent, normed)


def project_kernel(x_ref, w_ref, cos_ref, sin_ref, _, out_ref):
    store_turned(out_ref, 0, dot32(x_ref[...], w_ref[...]), cos_ref, sin_ref)


def project(normed, weights, cosines, sines, qkv):
    rows, depth = normed.shape
    width = weights.shape[1]
    steps = width // KV_WIDE
    first = steps // 4
    return pl.pallas_call(
        project_kernel,
        out_shape=jax.ShapeDtypeStruct((rows, width), jnp.bfloat16),
        grid=(steps - first,),
        in_specs=[
            whole(normed),
            pl.BlockSpec((depth, KV_WIDE), lambda i: (0, i + first)),
            whole(cosines),
            whole(sines),
            pl.BlockSpec(memory_space=pl.ANY),
        ],
        out_specs=pl.BlockSpec((rows, KV_WIDE), lambda i: (0, i + first)),
        input_output_aliases={4: 0},
        compiler_params=params(),
        cost_estimate=cost(
            2 * rows * depth * width, 2 * (rows * depth + depth * width + rows * width)
        ),
    )(normed, weights, cosines, sines, qkv)


def attend_kernel(start, length_ref, q_ref, kv_ref, strip_ref, out_ref):
    rows = q_ref.shape[0]
    keys = kv_ref.shape[0]
    length = length_ref[0]
    row_ids = start + lax.broadcasted_iota(jnp.int32, (1, rows), 1)
    limit = jnp.minimum(row_ids, length - 1)
    allowed = lax.broadcasted_iota(jnp.int32, (keys, rows), 0) <= limit
    mixed = []
    sums = []
    for kv in range(kv_ref.shape[1] // KV_WIDE):
        base = kv * KV_WIDE
        at = base + GROUP * LANES
        key = kv_ref[:, at : at + LANES]
        value_t = kv_ref[:, at + LANES : at + 2 * LANES].T
        for g in range(GROUP):
            query = q_ref[:, base + g * LANES : base + (g + 1) * LANES]
            raw = jnp.where(allowed, dot32_nt(key, query), masked_score)
            peak = jnp.max(raw, axis=0, keepdims=True)
            expo = jnp.exp2((raw - peak) * score_scale_log2)
            total = jnp.sum(expo, axis=0, keepdims=True)
            probs = (expo * (1.0 / total)).astype(jnp.bfloat16)
            mixed.append(dot32(value_t, probs).T)
            log_sum = peak * score_scale_log2 + jnp.log2(total)
            sums.append(jnp.where(row_ids < length, log_sum, far_away))
    out_ref[:rows, :] = dot_split(jnp.concatenate(mixed, 1), strip_ref[...])
    out_ref[rows:, :] = jnp.zeros((EXTRA, out_ref.shape[1]), jnp.float32)
    out_ref[rows : rows + len(sums), :rows] = jnp.concatenate(sums, 0)


def attend(length, qkv, strip, index, rows):
    keys = (index + 1) * rows
    width = qkv.shape[1] // 4
    heads = width // KV_WIDE * GROUP
    shape = (rows + EXTRA, strip.shape[1])
    return pl.pallas_call(
        functools.partial(attend_kernel, index * rows),
        out_shape=jax.ShapeDtypeStruct(shape, jnp.float32),
        grid=(1,),
        in_specs=[
            SCALAR,
            pl.BlockSpec((rows, width), lambda i: (index, 0)),
            pl.BlockSpec((keys, width), lambda i: (0, 0)),
            whole(strip),
        ],
        out_specs=pl.BlockSpec(shape, lambda i: (0, 0)),
        compiler_params=params(),
        cost_estimate=cost(
            4 * heads * rows * keys * LANES, 2 * (rows + keys) * width, heads * rows * keys
        ),
    )(length, qkv, qkv, strip)


def forward_kernel(level_ref, part_ref, other_ref, across_ref, outer_ref, *refs):
    x_ref, dout_ref, wo_ref, gain_ref, gate_any, up_any, down_any = refs[:7]
    hidden_ref, normed_t_ref, activ_ref, dgate_ref, dup_ref, mlp_ref, dn_ref = refs[7:14]
    normed_ref, gate_ref, up_ref, down_ref, sems = refs[14:]
    rows = x_ref.shape[0]
    steps, block = down_ref.shape[:2]
    step = pl.program_id(0)

    def fetched(at):
        here = pl.ds(pl.multiple_of(at * block, block), block)
        return [
            pltpu.make_async_copy(gate_any.at[:, here], gate_ref.at[at], sems.at[0, at]),
            pltpu.make_async_copy(up_any.at[:, here], up_ref.at[at], sems.at[1, at]),
            pltpu.make_async_copy(down_any.at[here, :], down_ref.at[at], sems.at[2, at]),
        ]

    @pl.when(step == 0)
    def _():
        for at in range(steps):
            for copy in fetched(at):
                copy.start()
        level = level_ref[0]
        inner = (level == 1) | (level == 2)
        width = part_ref.shape[1]
        second = jnp.where(inner, across_ref[:rows, width:], outer_ref[:rows, :width])
        third = jnp.where(inner, across_ref[:rows, :width], outer_ref[:rows, width:])
        mixed = jnp.concatenate([part_ref[:rows, :], other_ref[:rows, :], second, third], 1)
        hidden = x_ref[...].astype(jnp.float32) + dot32_nt(mixed.astype(jnp.bfloat16), wo_ref[...])
        hidden_ref[...] = hidden
        rms = lax.rsqrt(jnp.mean(hidden * hidden, -1, keepdims=True) + norm_eps)
        normed = (hidden * rms * gain_ref[...]).astype(jnp.bfloat16)
        normed_ref[...] = normed
        normed_t_ref[...] = normed.T
        mlp_ref[...] = jnp.zeros_like(mlp_ref)
        dn_ref[...] = jnp.zeros_like(dn_ref)

    for copy in fetched(step):
        copy.wait()
    wg_ref, wu_ref, wd_ref = gate_ref.at[step], up_ref.at[step], down_ref.at[step]
    normed = normed_ref[...]
    gate = dot32(normed, wg_ref[...])
    up = dot32(normed, wu_ref[...])
    dact = dot32_nt(dout_ref[...], wd_ref[...])
    sigmoid = jax.nn.sigmoid(gate)
    silu = gate * sigmoid
    activ = (silu * up).astype(jnp.bfloat16)
    dgate = (dact * up * sigmoid * (1.0 + gate * (1.0 - sigmoid))).astype(jnp.bfloat16)
    dup = (dact * silu).astype(jnp.bfloat16)
    activ_ref[...] = activ
    dgate_ref[...] = dgate
    dup_ref[...] = dup
    mlp_ref[...] += dot32(activ, wd_ref[...])
    dn_ref[:rows, :] += dot32_nt(dgate, wg_ref[...]) + dot32_nt(dup, wu_ref[...])


def forward_chunk(level, gathered, tokens, dout, w_out, gain, w_gate, w_up, w_down, index, rows):
    depth = tokens.shape[1]
    units = w_gate.shape[1]
    block = 512
    own_rows = pl.BlockSpec((rows, depth), lambda i: (index, 0))
    steps = units // block
    gain = gain[None, :]
    f32, bf16 = jnp.float32, jnp.bfloat16
    outs = [
        jax.ShapeDtypeStruct((rows, depth), f32),
        jax.ShapeDtypeStruct((depth, rows), bf16),
        jax.ShapeDtypeStruct((rows, units), bf16),
        jax.ShapeDtypeStruct((rows, units), bf16),
        jax.ShapeDtypeStruct((rows, units), bf16),
        jax.ShapeDtypeStruct((rows, depth), f32),
        jax.ShapeDtypeStruct((rows + EXTRA, depth), f32),
    ]
    unit_out = pl.BlockSpec((rows, block), lambda i: (0, i))
    return pl.pallas_call(
        forward_kernel,
        out_shape=outs,
        grid=(steps,),
        in_specs=[SCALAR]
        + [whole(array) for array in gathered]
        + [own_rows, own_rows, whole(w_out), whole(gain)]
        + [ANYWHERE] * 3,
        out_specs=[
            whole(outs[0]),
            whole(outs[1]),
            unit_out,
            unit_out,
            unit_out,
            whole(outs[5]),
            whole(outs[6]),
        ],
        scratch_shapes=[
            pltpu.VMEM((rows, depth), bf16),
            pltpu.VMEM((steps, depth, block), bf16),
            pltpu.VMEM((steps, depth, block), bf16),
            pltpu.VMEM((steps, block, depth), bf16),
            pltpu.SemaphoreType.DMA((3, steps)),
        ],
        compiler_params=params(),
        cost_estimate=cost(
            2 * rows * depth * (6 * units + w_out.shape[1]),
            2 * depth * (3 * units + w_out.shape[1]) + 22 * rows * depth,
            rows * units,
        ),
    )(level, *gathered, tokens, dout, w_out, gain, w_gate, w_up, w_down)


def hidden_grad(inner, total_ref, final_ref, hidden_ref, dout_ref, gain_ref):
    dnormed = jnp.where(inner, total_ref[...], final_ref[...])
    hidden = hidden_ref[...]
    rms = lax.rsqrt(jnp.mean(hidden * hidden, -1, keepdims=True) + norm_eps)
    scaled = dnormed * gain_ref[...]
    shift = jnp.mean(scaled * hidden, -1, keepdims=True)
    dhid = dout_ref[...].astype(jnp.float32) + (rms * scaled - hidden * (rms**3 * shift))
    return dhid, dnormed * (hidden * rms)


def backward_kernel(
    start, full, adding, steps, level_ref, total_ref, final_ref, hidden_ref, dout_ref, *refs
):
    gain_two_ref, wo_ref, q_ref = refs[:3]
    kv_here = q_ref.shape[1] // KV_WIDE
    refs = refs[3:]
    kv_refs, refs = refs[: 2 * kv_here], refs[2 * kv_here :]
    part_ref, place_ref, strip_ref, cos_ref, sin_ref = refs[:5]
    extra = (2 if full else 0) + (1 if adding else 0) + 1
    outs, scratch = refs[5 : -3 - extra], refs[-3 - extra :]
    dhid_ref, low_ref, dn_ref, sems = scratch[:4]
    if full:
        x_any, gain_one_ref, other_ref, across_ref, outer_ref, w_any = outs[:6]
        outs = outs[6:]
        x_ref, w_buffers = scratch[4:6]
        tokens_here = pltpu.make_async_copy(
            x_any.at[pl.ds(start, x_ref.shape[0]), :], x_ref, sems.at[4]
        )
    count = (5 if start > 0 else 4) if full else 2
    if adding:
        acc_any, acc_buffers = outs[0], scratch[-1]
    outs = outs[-count:]
    dhid_t_ref, dqkv_ref = outs[:2]
    if full:
        input_grad_ref, gains_ref = outs[2:4]
    rows = q_ref.shape[0]
    keys = kv_refs[0].shape[0]
    shard = pl.program_id(0)
    level = level_ref[0]
    inner = (level == 1) | (level == 2)

    def fetched(at, sums):
        source, buffers = (acc_any, acc_buffers) if sums else (w_any, w_buffers)
        lanes = buffers.shape[2]
        here = pl.ds(pl.multiple_of(at * lanes, lanes), lanes)
        slot = at % 2
        sem = sems.at[slot + 2] if sums else sems.at[slot]
        return pltpu.make_async_copy(source.at[:, here], buffers.at[slot], sem)

    def fetch(at):
        if adding:
            fetched(at, True).start()
        if full:
            fetched(at, False).start()

    @pl.when(shard == 0)
    def _():
        for at in range(min(2, steps)):
            fetch(at)
        if full:
            tokens_here.start()
        dhid, dgain = hidden_grad(
            inner, total_ref, final_ref, hidden_ref, dout_ref, gain_two_ref
        )
        dhid_ref[...] = dhid
        low = dhid.astype(jnp.bfloat16)
        low_ref[...] = low
        dhid_t_ref[...] = low.T
        if full:
            gains_ref[...] = jnp.zeros_like(gains_ref)
            gains_ref[1:2, :] = jnp.sum(dgain, 0, keepdims=True)
            dn_ref[...] = jnp.zeros_like(dn_ref)

    def rotate_back(grads):
        turned = grads * cos_ref[...] - pltpu.roll(grads, LANES // 2, 1) * sin_ref[...]
        return turned.astype(jnp.bfloat16)

    dmixed_all = dot32(low_ref[...], wo_ref[...]).astype(jnp.bfloat16)
    mixed = part_ref[...]
    if full:
        far = jnp.where(inner, across_ref[...], outer_ref[...])
        far = jnp.where(shard == 1, other_ref[...], far)
        mixed = jnp.where(shard == 0, mixed, far)
    products = dmixed_all.astype(jnp.float32) * dot_split(mixed[:rows], place_ref[...])
    causal = lax.broadcasted_iota(jnp.int32, (rows, rows), 0) <= lax.broadcasted_iota(
        jnp.int32, (rows, rows), 1
    )
    acc_ref = None
    if adding:
        fetched(shard, True).wait()
        acc_ref = acc_buffers.at[shard % 2]
    grads = []
    for kv in range(kv_here):
        key_ref, value_ref = kv_refs[2 * kv : 2 * kv + 2]
        heads = range(kv * GROUP, (kv + 1) * GROUP)
        lanes = {h: slice(h * LANES, (h + 1) * LANES) for h in heads}
        row_dots = {h: jnp.sum(products[:, lanes[h]].T, axis=0, keepdims=True) for h in heads}
        log_sums = {h: mixed[rows + h : rows + h + 1, :rows] for h in heads}
        dqueries = dict.fromkeys(heads)
        here = slice(2 * kv * LANES, (2 * kv + 1) * LANES)
        there = slice((2 * kv + 1) * LANES, (2 * kv + 2) * LANES)
        for tile in range(keys // rows):
            span = slice(tile * rows, (tile + 1) * rows)
            key = key_ref[span, :]
            value = value_ref[span, :]
            key_t = key.T
            dkey = None if acc_ref is None else acc_ref[span, here]
            dvalue = None if acc_ref is None else acc_ref[span, there]
            last = tile * rows == start
            for h in heads:
                at = kv * KV_WIDE + (h % GROUP) * LANES
                query = q_ref[:, at : at + LANES]
                dmixed = dmixed_all[:, lanes[h]]
                raw = dot32_nt(key, query)
                probs = jnp.exp2(raw * score_scale_log2 - log_sums[h])
                if last:
                    probs = jnp.where(causal, probs, 0.0)
                dprobs = dot32_nt(value, dmixed)
                dscores = (probs * (dprobs - row_dots[h])).astype(jnp.bfloat16)
                dquery = dot32(key_t, dscores)
                dqueries[h] = dquery if dqueries[h] is None else dqueries[h] + dquery
                dkey_one = dot32(dscores, query)
                dvalue_one = dot32(probs.astype(jnp.bfloat16), dmixed)
                dkey = dkey_one if dkey is None else dkey + dkey_one
                dvalue = dvalue_one if dvalue is None else dvalue + dvalue_one
            if full and not last:
                outs[4][span, here] = dkey
                outs[4][span, there] = dvalue
        grads += [rotate_back(dqueries[h].T * score_scale) for h in heads]
        grads.append(rotate_back(dkey * score_scale))
        grads.append(dvalue.astype(jnp.bfloat16))
    grads = jnp.concatenate(grads, 1)
    if full:
        fetched(shard, False).wait()
        dn_ref[...] += dot32_nt(grads, w_buffers[shard % 2])

        @pl.when(shard + 2 < steps)
        def _():
            fetch(shard + 2)

    @pl.when(shard == 0)
    def _():
        wide = strip_ref.shape[1]
        for kv in range(kv_here):
            dqkv_ref[:, kv * wide : (kv + 1) * wide] = dot32(
                grads[:, kv * KV_WIDE : (kv + 1) * KV_WIDE], strip_ref[...]
            ).astype(jnp.bfloat16)

    if not full:
        return

    @pl.when(shard == pl.num_programs(0) - 1)
    def _():
        tokens_here.wait()
        dnormed = dn_ref[...]
        inputs = x_ref[...].astype(jnp.float32)
        rms = lax.rsqrt(jnp.mean(inputs * inputs, -1, keepdims=True) + norm_eps)
        scaled = dnormed * gain_one_ref[...]
        shift = jnp.mean(scaled * inputs, -1, keepdims=True)
        grad = dhid_ref[...] + (rms * scaled - inputs * (rms**3 * shift))
        input_grad_ref[...] = grad.astype(jnp.bfloat16)
        gains_ref[0:1, :] = jnp.sum(dnormed * (inputs * rms), 0, keepdims=True)


def backward_chunk(
    level, sums_two, hidden, dout, tokens, gains, weights, qkv, gathered, places, tables, acc,
    index, rows, full=True, grad_into=None
):
    start = index * rows
    keys = start + rows
    depth = tokens.shape[1]
    out_pad, qkv_pad = weights
    place_out, strip = places
    far_rows, width = gathered[0].shape
    out_wide = place_out.shape[1]
    kv_here = out_wide // (GROUP * LANES)
    wide = kv_here * KV_WIDE
    levels = qkv.shape[1] // wide
    own_rows = pl.BlockSpec((rows, depth), lambda t: (index, 0))
    table = pl.BlockSpec((rows, LANES), lambda t: (index, 0))
    gains = [gain[None, :] for gain in gains]
    key_value = lambda at: pl.BlockSpec(
        (keys, LANES), lambda t: (0, (wide // LANES) * t + at)
    )
    across = pl.BlockSpec((far_rows, width), lambda t: (0, jnp.where(t == 2, 1, 0)))
    outer = pl.BlockSpec((far_rows, width), lambda t: (0, jnp.where(t == 3, 1, 0)))
    in_specs = [
        SCALAR,
        whole(hidden),
        whole(hidden),
        whole(hidden),
        own_rows,
        whole(gains[1]),
        pl.BlockSpec((depth, out_wide), lambda t: (0, t)),
        pl.BlockSpec((rows, wide), lambda t: (index, t)),
    ]
    for kv in range(kv_here):
        at = kv * (KV_WIDE // LANES) + GROUP
        in_specs += [key_value(at), key_value(at + 1)]
    in_specs += [
        whole(gathered[0]),
        whole(place_out),
        whole(strip),
        table,
        table,
    ]
    args = [level, *sums_two, hidden, dout, gains[1], out_pad]
    args += [qkv] * (1 + 2 * kv_here)
    args += [gathered[0], place_out, strip, *tables]
    sums_wide = 2 * kv_here * LANES
    if full:
        in_specs += [ANYWHERE, whole(gains[0]), whole(gathered[1]), across, outer]
        in_specs.append(ANYWHERE)
        args += [tokens, gains[0], *gathered[1:], qkv_pad]
    if acc is not None:
        in_specs.append(ANYWHERE)
        args.append(acc)
    f32, bf16 = jnp.float32, jnp.bfloat16
    outs = [
        jax.ShapeDtypeStruct((depth, rows), bf16),
        jax.ShapeDtypeStruct((rows, kv_here * strip.shape[1]), bf16),
        jax.ShapeDtypeStruct(tokens.shape, bf16),
        jax.ShapeDtypeStruct((8, depth), f32),
    ]
    outs = outs if full else outs[:2]
    out_specs = [whole(out) for out in outs]
    aliases = {}
    if full:
        out_specs[2] = own_rows
        if grad_into is not None:
            aliases = {len(args): 2}
            in_specs.append(ANYWHERE)
            args.append(grad_into)
    if full and start > 0:
        outs.append(jax.ShapeDtypeStruct((start, levels * sums_wide), f32))
        out_specs.append(pl.BlockSpec((start, sums_wide), lambda t: (0, t)))
    steps = levels if full else 1
    scratch = [
        pltpu.VMEM((rows, depth), f32),
        pltpu.VMEM((rows, depth), bf16),
        pltpu.VMEM((rows, depth), f32),
        pltpu.SemaphoreType.DMA((5,)),
    ]
    if full:
        scratch += [pltpu.VMEM((rows, depth), bf16), pltpu.VMEM((2, depth, wide), bf16)]
    if acc is not None:
        scratch.append(pltpu.VMEM((min(2, steps), keys, sums_wide), f32))
    results = pl.pallas_call(
        functools.partial(backward_kernel, start, full, acc is not None, steps),
        out_shape=outs,
        grid=(steps,),
        input_output_aliases=aliases,
        in_specs=in_specs,
        out_specs=out_specs,
        scratch_shapes=scratch,
        compiler_params=params(),
        cost_estimate=cost(
            levels * rows * (20 * kv_here * keys * LANES + 2 * depth * (out_wide + wide)),
            2 * depth * levels * (out_wide + wide) + 16 * rows * depth,
            levels * kv_here * GROUP * rows * keys,
        ),
    )(*args)
    return results[:4], (results[4] if full and start > 0 else None)


def rows_kernel(lefts, groups, adding, picked, together, side_ref, *refs):
    refs = list(refs)
    held_ref = refs.pop()
    out_refs = refs[-len(picked) :]
    refs = refs[: -len(picked)]
    recv_ref = refs.pop() if adding else None
    step = pl.program_id(0)
    left_refs = []
    for count in lefts:
        left_refs.append(refs[:count])
        refs = refs[count:]
    rights = []
    for _ in groups:
        rights.append(refs[:CHUNKS])
        refs = refs[CHUNKS:]
    rows = left_refs[0][0].shape[0]
    blocks = held_ref.shape[1] // rows

    @pl.when(step == 0)
    def _():
        for which, pieces in enumerate(left_refs):
            for n, ref in enumerate(pieces):
                m, j = n % blocks, n // blocks
                wide = ref.shape[1]
                held_ref[which, m * rows : (m + 1) * rows, j * wide : (j + 1) * wide] = ref[...]

    chunk = held_ref.shape[2] // CHUNKS
    whole_columns = slice(0, out_refs[0].shape[1])

    def give(group, left, columns):
        right = jnp.concatenate([ref[:chunk, :].astype(jnp.bfloat16) for ref in group], 0)
        total = dot32(held_ref[left], right)
        if recv_ref is not None:
            total = total + recv_ref[:, columns]
        for out_ref, parts in zip(out_refs, picked):
            at = 0
            for start, size in parts:
                out_ref[at : at + size, columns] = total[start : start + size]
                at += size

    begin = 0
    for group, (left, first, steps) in zip(rights, groups):
        if together:
            width = group[0].shape[1]
            give(group, left, slice(begin, begin + width))
            begin += width
        else:

            @pl.when((step >= first) & (step < first + steps))
            def _(group=group, left=left):
                give(group, left, whole_columns)


def rows_of(lefts, groups, side, rows, blocks, step, recv=None, picked=None):
    if picked is None:
        picked = [[(0, rows * blocks)]]
    at = lambda m: lambda i, side: ((m ^ side[2]) * side[1] + side[0], 0)
    specs = []
    args = []
    counts = []
    for left in lefts:
        pieces = left if isinstance(left, list) else [left]
        counts.append(len(pieces) * blocks)
        for piece in pieces:
            for m in range(blocks):
                specs.append(pl.BlockSpec((rows, piece.shape[1]), at(m)))
                args.append(piece)
    tokens = sum(piece.shape[1] for piece in pieces)
    first = 0
    plan = []
    together = step is None
    for which, rights in groups:
        if together:
            plan.append((which, 0, 1))
            specs += [whole(right) for right in rights]
            args += rights
            first += rights[0].shape[1]
            continue
        steps = rights[0].shape[1] // step
        plan.append((which, first, steps))
        for right in rights:
            pick = lambda i, side, first=first, steps=steps: (0, jnp.clip(i - first, 0, steps - 1))
            specs.append(pl.BlockSpec((right.shape[0], step), pick))
            args.append(right)
        first += steps
    if together:
        first, step = 1, first
    total = first * step
    block = lambda height: pl.BlockSpec((height, step), lambda i, side: (0, i))
    if recv is not None:
        specs.append(block(rows * blocks))
        args.append(recv)
    heights = [sum(size for _, size in parts) for parts in picked]
    results = pl.pallas_call(
        functools.partial(rows_kernel, counts, plan, recv is not None, picked, together),
        out_shape=[jax.ShapeDtypeStruct((height, total), jnp.float32) for height in heights],
        grid_spec=pltpu.PrefetchScalarGridSpec(
            num_scalar_prefetch=1,
            grid=(first,),
            in_specs=specs,
            out_specs=[block(height) for height in heights],
            scratch_shapes=[pltpu.VMEM((len(lefts), rows * blocks, tokens), jnp.bfloat16)],
        ),
        compiler_params=params(),
        cost_estimate=cost(
            2 * rows * blocks * tokens * total,
            4 * rows * blocks * total + 2 * tokens * (total + rows * blocks),
        ),
    )(side, *args)
    return results[0] if len(picked) == 1 else results


def shards(
    tokens,
    lengths,
    positions,
    cotangent,
    norm_gain,
    w_query,
    w_key,
    w_value,
    w_out,
    mlp_gain,
    w_gate,
    w_up,
    w_down,
):
    seq_rows, depth = tokens.shape
    chips = lax.axis_size("chip")
    dp = chips * 2
    tp = lax.axis_size("tp")
    chip = lax.axis_index("chip")
    core = lax.axis_index("core")
    level = lax.axis_index("tp")
    low = level < 2
    inner = (level == 1) | (level == 2)
    heads_here = w_query.shape[1] // HD
    kv_here = w_key.shape[1] // HD
    rows = seq_rows // CHUNKS
    slice_rows = depth // dp
    level_ref = level.astype(jnp.int32).reshape(1)
    by_hand = dp == 8
    swap = lambda array: lax.ppermute(array, "core", [(0, 1), (1, 0)])
    to_level = lambda array, s: along(array, [(t, t ^ s) for t in range(tp)])

    at_row = (chip * 2 + core) * slice_rows
    cols = lambda w: lax.dynamic_slice_in_dim(w, at_row, slice_rows, 1).astype(jnp.float32).T
    (out_slice,) = fence(cols(w_out))
    qkv_slice = jnp.concatenate(
        [
            lax.dynamic_slice_in_dim(w_query, at_row, slice_rows, 0).astype(jnp.float32),
            cols(w_key.T),
            cols(w_value.T),
        ],
        1,
    )
    out_slice, qkv_slice = fence(out_slice, qkv_slice)
    out_near = along(out_slice, PAIRS)
    qkv_near = along(qkv_slice, PAIRS)
    meta = jnp.stack([chip, core]).astype(jnp.int32)

    pq = place_query(heads_here)
    pkv = place_key_value(kv_here)
    p_all = place_all(heads_here, kv_here)
    strip_one = place_all(GROUP, 1).T
    p_out = place_plain(heads_here)
    strip_out = p_out.T

    half_dim = HD // 2
    freqs = rope_base ** (-(jnp.arange(half_dim).astype(jnp.float32) * 2.0 / HD))
    freqs = jnp.pad(freqs, (0, LANES // 2 - half_dim))
    angles = positions.astype(jnp.float32)[:, None] * jnp.concatenate([freqs, freqs])[None, :]
    cosines = jnp.cos(angles)
    sines = jnp.sin(angles) * jnp.where(jnp.arange(LANES) < LANES // 2, -1.0, 1.0)

    cosines, sines, out_near = fence(cosines, sines, out_near)
    out_across = along(jnp.stack([out_slice, out_near]), MIDDLE)
    qkv_own, normed_one, own_pad = start(
        tokens, norm_gain, w_query, w_key.T, w_value.T, pq, pkv, cosines, sines
    )

    def far_slices(near, across, outer):
        return jnp.stack(
            [
                near,
                jnp.where(inner, across[1], outer[0]),
                jnp.where(inner, across[0], outer[1]),
            ]
        )

    order = list(reversed(range(CHUNKS)))
    c0, c1, c2, c3 = order
    own, other, across, outer = {}, {}, {}, {}
    part, total, final = {}, {}, {}

    def hop_1(j):
        other[j] = along(own[j], PAIRS)

    def hop_2(j):
        across[j] = along(jnp.concatenate([own[j], other[j]], 1), MIDDLE)

    def hop_3(j):
        outer[j] = along(across[j], OUTWARD)

    coming = {}

    def add_1(j):
        coming[j] = along(part[j], INWARD)

    def add_2(j):
        total[j] = part[j][:rows] + coming[j][:rows]
        coming[j] = along(total[j], MIDDLE)

    def add_3(j, inward, extra=0):
        both = jnp.where(inner, total[j] + coming[j], inward)
        total[j] = jnp.pad(both, ((0, extra), (0, 0)))
        final[j] = along(total[j], PAIRS)
        return final[j]

    def to_chip(array, m):
        return lax.ppermute(array, "chip", [(i, i ^ m) for i in range(chips)])

    def over_chips_1(piece):
        cut = piece.shape[1] // 2
        one, two = piece[:, :cut], piece[:, cut:]
        return jnp.stack([one, to_chip(one, 1)]), jnp.stack([two, to_chip(two, 2)])

    def over_chips_2(one, two):
        return one, to_chip(one, 2), two, to_chip(two, 1)

    def over_chips_3(one, one_far, two, two_far):
        upper = jnp.stack([one[0], one[1], one_far[0], one_far[1]])
        lower = jnp.stack([two[0], two_far[0], two[1], two_far[1]])
        return jnp.concatenate([upper, lower], 2)

    qkv_own, out_across, qkv_near = fence(qkv_own, out_across, qkv_near)
    out_outer = along(out_across, OUTWARD)
    qkv_across = along(jnp.stack([qkv_slice, qkv_near]), MIDDLE)
    own[c0] = attend(lengths, qkv_own, strip_out, c0, rows)
    own[c1] = attend(lengths, qkv_own, strip_out, c1, rows)
    own, qkv_own, out_outer = fence(own, qkv_own, out_outer)
    others = along(jnp.concatenate([own[c0], own[c1]], 0), PAIRS)
    out_far = far_slices(out_near, out_across, out_outer)
    out_mine = over_chips_1(out_far) if by_hand else out_far
    own[c2] = attend(lengths, qkv_own, strip_out, c2, rows)
    own[c3] = attend(lengths, qkv_own, strip_out, c3, rows)
    own[c3], qkv_across = fence(own[c3], qkv_across)
    qkv_outer = along(qkv_across, OUTWARD)
    own, others, normed_one, w_out, out_mine = fence(own, others, normed_one, w_out, out_mine)
    other[c0], other[c1] = others[: rows + EXTRA], others[rows + EXTRA :]
    if by_hand:
        out_mine = over_chips_2(*out_mine)
    else:
        out_mine = lax.all_gather(out_mine, ("chip", "core"))
    hop_2(c0)
    dout, dout_t, normed_one_t = turn(lengths, cotangent, normed_one)
    w_out_t = w_out.T
    own, other, across, dout, dout_t, normed_one_t, w_out_t, out_mine, qkv_outer = fence(
        own, other, across, dout, dout_t, normed_one_t, w_out_t, out_mine, qkv_outer
    )
    hop_1(c2)
    hop_3(c0)
    hop_2(c1)
    qkv_far = lax.all_gather(far_slices(qkv_near, qkv_across, qkv_outer), ("chip", "core"))
    if by_hand:
        out_mine = over_chips_3(*out_mine)
        out_theirs = swap(out_mine)
        out_pad, out_plain = spread(
            spread_out_kernel,
            meta,
            w_out_t,
            [p_out],
            out_mine,
            out_theirs,
            [4 * p_out.shape[1], 4 * p_out.shape[0]],
        )
    else:
        plain = [w_out_t] + [
            out_mine[:, s].reshape(depth, -1).astype(jnp.bfloat16) for s in range(tp - 1)
        ]
        out_plain = jnp.concatenate(plain, 1)
        out_pad = jnp.concatenate([dot32(w, p_out).astype(jnp.bfloat16) for w in plain], 1)
    hidden, normed_t, activ, dgate, dup, mlp_part = {}, {}, {}, {}, {}, {}

    def feed(j):
        gathered = (own[j], other[j], across[j], outer[j])
        (hidden[j], normed_t[j], activ[j], dgate[j], dup[j], mlp_part[j], part[j]) = forward_chunk(
            level_ref, gathered, tokens, dout, out_plain, mlp_gain, w_gate, w_up, w_down, j, rows
        )

    own, other, across, outer, out_pad, out_plain = fence(
        own, other, across, outer, out_pad, out_plain
    )
    hop_1(c3)
    hop_3(c1)
    hop_2(c2)
    feed(c0)
    part, other = fence(part, other)
    add_1(c0)
    own, other, across, outer, part, hidden = fence(own, other, across, outer, part, hidden)
    hop_3(c2)
    hop_2(c3)
    feed(c1)
    qkv_far, hidden[c1] = fence(qkv_far, hidden[c1])
    qkv_pad = spread_qkv(own_pad, pq, pkv, qkv_far)
    own, other, across, outer, part, total, coming, hidden, qkv_pad = fence(
        own, other, across, outer, part, total, coming, hidden, qkv_pad
    )
    add_1(c1)
    hop_3(c3)
    add_2(c0)
    feed(c2)
    qkv_pad, hidden[c2] = fence(qkv_pad, hidden[c2])
    qkv = project(normed_one, qkv_pad, cosines, sines, qkv_own)
    own, other, across, outer, part, total, coming, hidden, qkv = fence(
        own, other, across, outer, part, total, coming, hidden, qkv
    )
    coming[c2] = add_3(c0, part[c2][:rows])
    add_2(c1)
    feed(c3)

    listed = lambda pieces: [pieces[j] for j in range(CHUNKS)]
    keep_side = jnp.stack([core, 2, 0]).astype(jnp.int32)
    keep_turned = jnp.stack([core, 2, chip]).astype(jnp.int32)
    send_side = jnp.stack([1 - core, 2, 0]).astype(jnp.int32)
    send_turned = jnp.stack([1 - core, 2, chip]).astype(jnp.int32)
    all_rows = jnp.array([0, 1, 0], jnp.int32)

    def send_rows(lefts, groups, step, side=send_side):
        if not by_hand:
            return rows_of(lefts, groups, all_rows, depth // 4, 4, step)
        return rows_of(lefts, groups, side, slice_rows, chips, step)

    def keep_rows(lefts, groups, received, step, side=keep_side, picked=None):
        if not by_hand:
            return received
        return rows_of(lefts, groups, side, slice_rows, chips, step, received, picked)

    def swap_rows(array):
        return swap(array) if by_hand else array

    def scatter(array, axes):
        return lax.psum_scatter(array, axes, scatter_dimension=0, tiled=True)

    units = w_gate.shape[1]
    mlp_args = (
        [listed(normed_t), dout_t],
        [(0, listed(dgate)), (0, listed(dup)), (1, listed(activ))],
    )
    acc = None
    input_grad = None
    dhid_t, dqkv_own, gains = {}, {}, {}

    def back(j):
        nonlocal acc, input_grad
        (dhid_t[j], dqkv_own[j], input_grad, gains[j]), acc = back_some(j, True)

    def back_own(j):
        return back_some(j, False)[0]

    def back_some(j, full):
        return backward_chunk(
            level_ref,
            (total[j], final[j]),
            hidden[j],
            dout,
            tokens,
            (norm_gain, mlp_gain),
            (out_pad, qkv_pad),
            qkv,
            (own[j], other[j], across[j], outer[j]),
            (p_out, strip_one),
            (cosines, sines),
            acc,
            j,
            rows,
            full,
            input_grad,
        )

    grad_mlp = rows_of(*mlp_args, all_rows, depth // 4, 4, units // 2)
    own, other, across, outer, part, total, coming, final, hidden, grad_mlp = fence(
        own, other, across, outer, part, total, coming, final, hidden, grad_mlp
    )
    grad_mlp = scatter(grad_mlp, ("chip", "core"))
    coming[c3] = add_3(c1, part[c3][:rows])
    add_2(c2)
    back(c0)

    near = lambda: jnp.where(low, mlp_part[1], mlp_part[2])
    edge = lambda: jnp.where(low, mlp_part[0], mlp_part[3])
    leave_far = lambda: jnp.where(low, mlp_part[3], mlp_part[0])
    leave_near = lambda: jnp.where(low, mlp_part[2], mlp_part[1])
    total, coming, final, hidden, mlp_part, acc, dhid_t = fence(
        total, coming, final, hidden, mlp_part, acc, dhid_t
    )
    far_sum = add_3(c2, leave_far())
    add_2(c3)
    back(c1)
    total, coming, final, hidden, mlp_part, far_sum, acc, dhid_t = fence(
        total, coming, final, hidden, mlp_part, far_sum, acc, dhid_t
    )
    add_3(c3, leave_near(), EXTRA)
    far_in = along(leave_far() + far_sum, MIDDLE)
    back(c2)
    total, final, hidden, acc, dhid_t = fence(total, final, hidden, acc, dhid_t)
    dhid_t[c3], dqkv_own[c3] = back_own(c3)
    dhid_t, dqkv_own, far_in, mlp_part, final = fence(
        dhid_t, dqkv_own, far_in, mlp_part, final
    )
    last = along(jnp.where(inner, edge() + far_in, near()), PAIRS)
    near_in = along(leave_near() + final[c3][:rows], MIDDLE)
    q_cols = heads_here * HD
    attn_args = (
        [listed(dhid_t), normed_one_t],
        [(0, listed(own)), (1, listed(dqkv_own))],
    )
    sent = swap_rows(send_rows(*attn_args, None, send_turned))
    total, final, hidden, acc, sent = fence(total, final, hidden, acc, sent)
    if by_hand:
        half = slice_rows // 2
        upper = lambda m: (m * slice_rows, half)
        lower = lambda m: (m * slice_rows + half, half)
        picked = [
            [upper(1), upper(3)],
            [upper(0), upper(2)],
            [lower(2), lower(3)],
            [lower(0), lower(1)],
        ]
        pieces = keep_rows(*attn_args, sent, None, keep_turned, picked)
        pieces, hidden = fence(pieces, hidden)
        one_away, one, two_away, two = pieces
        pieces = (one, to_chip(one_away, 1), two, to_chip(two_away, 2))
    else:
        pieces = scatter(sent, ("chip", "core"))
    back(c3)
    pieces, gains, input_grad = fence(pieces, gains, input_grad)
    gain_sums = gains[0] + gains[1] + gains[2] + gains[3]
    gain_sums = gain_sums + swap(gain_sums)
    gain_sums, last, near_in = fence(gain_sums, last, near_in)
    if by_hand:
        others = [to_chip(gain_sums, m) for m in range(1, chips)]
        gain_sums = sum(others, gain_sums)
        one = pieces[0] + pieces[1]
        two = pieces[2] + pieces[3]
        one = one[:half] + to_chip(one[half:], 2)
        two = two[:half] + to_chip(two[half:], 1)
        attn = jnp.concatenate([one, two], 0)
    else:
        gain_sums = lax.psum(gain_sums, "chip")
        attn = pieces
    gain_rows = lax.dynamic_slice_in_dim(gain_sums, at_row, slice_rows, 1)
    grad_out, grad_qkv = attn[:, :q_cols], attn[:, q_cols:]
    mlp_rows = jnp.where(inner, near() + near_in, edge()) + last
    hidden_rows = jnp.where(
        low,
        jnp.where(level == 0, hidden[0], hidden[1]),
        jnp.where(level == 2, hidden[2], hidden[3]),
    )
    layer_out = (hidden_rows + mlp_rows).astype(jnp.bfloat16)
    one = strip_one.shape[1]
    picked = lambda at, width: jnp.concatenate(
        [grad_qkv[:, kv * one + at : kv * one + at + width] for kv in range(kv_here)], 1
    )
    return (
        layer_out,
        input_grad,
        gain_rows[0],
        picked(0, GROUP * HD),
        picked(GROUP * HD, HD),
        picked((GROUP + 1) * HD, HD),
        grad_out.T,
        gain_rows[1],
        grad_mlp[:, :units],
        grad_mlp[:, units : 2 * units],
        grad_mlp[:, 2 * units :].T,
    )


def solution(mesh):
    devices = mesh.devices
    dp, tp = devices.shape
    split = Mesh(devices.reshape(dp // 2, 2, tp), ("chip", "core", "tp"))
    data = ("chip", "core")
    return jax.shard_map(
        shards,
        mesh=split,
        in_specs=(
            P(data, None),
            P(data),
            P(data),
            P(data, None),
            P(),
            P(None, "tp"),
            P(None, "tp"),
            P(None, "tp"),
            P("tp", None),
            P(),
            P(None, "tp"),
            P(None, "tp"),
            P("tp", None),
        ),
        out_specs=(
            P(("chip", "core", "tp"), None),
            P(data, None),
            P(data),
            P(data, "tp"),
            P(data, "tp"),
            P(data, "tp"),
            P("tp", data),
            P(data),
            P(data, "tp"),
            P(data, "tp"),
            P("tp", data),
        ),
        check_vma=False,
    )
```

```python
import functools

import jax
import jax.numpy as jnp
from jax import lax
from jax.experimental import pallas as pl
from jax.experimental.pallas import tpu as pltpu
from jax.sharding import Mesh
from jax.sharding import PartitionSpec as P

HD = 96
LANES = 128
GROUP = 2
KV_WIDE = (GROUP + 2) * LANES
rope_base = 100000.0
norm_eps = 1e-05
masked_score = -1e30
far_away = 1e30
score_scale = HD ** (-0.5)
score_scale_log2 = score_scale * 1.4426950408889634
CHUNKS = 4
EXTRA = 8
VMEM_BYTES = 56 * 1024 * 1024
NT = (((1,), (1,)), ((), ()))


def params():
    return pltpu.CompilerParams(vmem_limit_bytes=VMEM_BYTES)


def cost(flops, moved, exps=0):
    return pl.CostEstimate(
        flops=flops // 1024, bytes_accessed=moved // 1024, transcendentals=exps // 1024
    )


def dot32(a, b):
    return jnp.dot(a, b, preferred_element_type=jnp.float32)


def dot32_nt(a, b):
    return lax.dot_general(a, b, NT, preferred_element_type=jnp.float32)


def dot_split(a, places):
    high = a.astype(jnp.bfloat16)
    rest = (a - high.astype(jnp.float32)).astype(jnp.bfloat16)
    return dot32(high, places) + dot32(rest, places)


def fence(*trees):
    return lax.optimization_barrier(trees)


def whole(array, buffers=None):
    zeros = (0,) * len(array.shape)
    return pl.BlockSpec(array.shape, lambda *_: zeros)


SCALAR = pl.BlockSpec(memory_space=pltpu.SMEM)
ANYWHERE = pl.BlockSpec(memory_space=pl.ANY)


def halves(entry):
    half_dim = HD // 2
    return (entry // half_dim) * (LANES // 2) + entry % half_dim


def placement(lanes, width):
    return (lanes[:, None] == jnp.arange(width)[None, :]).astype(jnp.bfloat16)


def place_query(heads):
    source = jnp.arange(heads * HD)
    return placement((source // HD) * LANES + halves(source % HD), heads * LANES)


def place_key_value(kv_heads):
    source = jnp.arange(kv_heads * HD)
    head = source // HD
    keys = head * 2 * LANES + halves(source % HD)
    values = head * 2 * LANES + LANES + source % HD
    return placement(jnp.concatenate([keys, values]), kv_heads * 2 * LANES)


def place_all(heads, kv_heads):
    source = jnp.arange(heads * HD)
    head = source // HD
    query = (head // GROUP) * KV_WIDE + (head % GROUP) * LANES + halves(source % HD)
    source = jnp.arange(kv_heads * HD)
    base = (source // HD) * KV_WIDE + GROUP * LANES
    keys = base + halves(source % HD)
    values = base + LANES + source % HD
    return placement(jnp.concatenate([query, keys, values]), kv_heads * KV_WIDE)


def place_plain(heads):
    source = jnp.arange(heads * HD)
    return placement((source // HD) * LANES + source % HD, heads * LANES)


PAIRS = [(0, 1), (1, 0), (2, 3), (3, 2)]
INWARD = [(0, 1), (3, 2)]
MIDDLE = [(1, 2), (2, 1)]
OUTWARD = [(1, 0), (2, 3)]


def along(part, pairs):
    return lax.ppermute(part, "tp", pairs)


def store_qkv(out_ref, here, base, query, key_value):
    wide = GROUP * LANES
    for kv in range(key_value.shape[1] // (2 * LANES)):
        at = base + kv * KV_WIDE
        there = slice(kv * 2 * LANES, (kv + 1) * 2 * LANES)
        out_ref[here, at : at + wide] = query[:, kv * wide : (kv + 1) * wide]
        out_ref[here, at + wide : at + KV_WIDE] = key_value[:, there]


def store_turned(out_ref, at, lin, cos_ref, sin_ref):
    for h in range(GROUP + 2):
        one = lin[:, h * LANES : (h + 1) * LANES]
        if h < GROUP + 1:
            one = one * cos_ref[...] + pltpu.roll(one, LANES // 2, 1) * sin_ref[...]
        out_ref[:, at + h * LANES : at + (h + 1) * LANES] = one.astype(jnp.bfloat16)


def spread_out_kernel(meta_ref, own_ref, p_ref, mine_ref, theirs_ref, pad_ref, plain_ref):
    rows, width = mine_ref.shape[2:]
    wide = p_ref.shape[1]
    for side, ref in enumerate((mine_ref, theirs_ref)):
        here = pl.ds(pl.multiple_of((meta_ref[1] ^ side) * rows, rows), rows)
        for s in range(4):
            block = own_ref[here, :] if s == 0 else ref[0, s - 1].astype(jnp.bfloat16)
            plain_ref[here, s * width : (s + 1) * width] = block
            pad_ref[here, s * wide : (s + 1) * wide] = dot32(block, p_ref[...]).astype(
                jnp.bfloat16
            )


def spread_qkv_kernel(pq_ref, pkv_ref, far_ref, _, out_ref):
    parts, _, rows, width = far_ref.shape
    split = pq_ref.shape[0]
    block = far_ref[:, 0].reshape(parts * rows, width).astype(jnp.bfloat16)
    query = dot32(block[:, :split], pq_ref[...]).astype(jnp.bfloat16)
    key_value = dot32(block[:, split:], pkv_ref[...]).astype(jnp.bfloat16)
    store_qkv(out_ref, slice(None), 0, query, key_value)


def spread_qkv(padded, pq, pkv, far):
    total = padded.shape[0]
    dp, others, rows, width = far.shape
    wide = padded.shape[1] // (others + 1)
    parts = max(1, dp // 2)
    block = parts * rows
    return pl.pallas_call(
        spread_qkv_kernel,
        out_shape=jax.ShapeDtypeStruct(padded.shape, jnp.bfloat16),
        grid=(total // block, others),
        in_specs=[
            whole(pq),
            whole(pkv),
            pl.BlockSpec((parts, 1, rows, width), lambda i, s: (i, s, 0, 0)),
            pl.BlockSpec(memory_space=pl.ANY),
        ],
        out_specs=pl.BlockSpec((block, wide), lambda i, s: (i, s + 1)),
        input_output_aliases={3: 0},
        compiler_params=params(),
        cost_estimate=cost(8 * total * width * 512, 20 * total * wide),
    )(pq, pkv, far, padded)


def spread(kernel, meta, own, places, mine, theirs, widths):
    chips, others, rows, width = mine.shape
    total = own.shape[0]
    row_block = lambda m, meta: (meta[0] ^ m, 0)
    piece = pl.BlockSpec((1, others, rows, width), lambda m, meta: (m, 0, 0, 0))
    return pl.pallas_call(
        kernel,
        out_shape=[jax.ShapeDtypeStruct((total, wide), jnp.bfloat16) for wide in widths],
        grid_spec=pltpu.PrefetchScalarGridSpec(
            num_scalar_prefetch=1,
            grid=(chips,),
            in_specs=[pl.BlockSpec((2 * rows, own.shape[1]), row_block)]
            + [whole(place) for place in places]
            + [piece, piece],
            out_specs=[pl.BlockSpec((2 * rows, wide), row_block) for wide in widths],
        ),
        compiler_params=params(),
        cost_estimate=cost(
            8 * total * width * 512, total * (12 * width + 2 * sum(widths))
        ),
    )(meta, own, *places, mine, theirs)


def start_kernel(x_ref, gain_ref, q_ref, k_ref, v_ref, pq_ref, pkv_ref, cos_ref, sin_ref, *outs):
    qkv_ref, normed_ref, pad_ref = outs

    @pl.when(pl.program_id(0) == 0)
    def _():
        split = k_ref.shape[0]
        query = dot32(q_ref[...], pq_ref[...]).astype(jnp.bfloat16)
        key_value = dot32(k_ref[...].T, pkv_ref[:split, :])
        key_value = key_value + dot32(v_ref[...].T, pkv_ref[split:, :])
        store_qkv(pad_ref, slice(None), 0, query, key_value.astype(jnp.bfloat16))

    inputs = x_ref[...].astype(jnp.float32)
    rms = lax.rsqrt(jnp.mean(inputs * inputs, -1, keepdims=True) + norm_eps)
    normed = (inputs * rms * gain_ref[...]).astype(jnp.bfloat16)
    normed_ref[...] = normed
    for kv in range(pad_ref.shape[1] // KV_WIDE):
        at = kv * KV_WIDE
        store_turned(qkv_ref, at, dot32(normed, pad_ref[:, at : at + KV_WIDE]), cos_ref, sin_ref)


def start(tokens, gain, w_query, w_key_t, w_value_t, pq, pkv, cosines, sines):
    total, depth = tokens.shape
    rows = total // CHUNKS
    wide = pq.shape[1] + pkv.shape[1]
    gain = gain[None, :]
    by_rows = lambda width: pl.BlockSpec((rows, width), lambda i: (i, 0))
    arrays = [w_query, w_key_t, w_value_t, pq, pkv]
    shapes = [
        jax.ShapeDtypeStruct((total, 4 * wide), jnp.bfloat16),
        jax.ShapeDtypeStruct((total, depth), jnp.bfloat16),
        jax.ShapeDtypeStruct((depth, 4 * wide), jnp.bfloat16),
    ]
    return pl.pallas_call(
        start_kernel,
        out_shape=shapes,
        grid=(CHUNKS,),
        in_specs=[by_rows(depth), whole(gain)]
        + [whole(array) for array in arrays]
        + [by_rows(LANES), by_rows(LANES)],
        out_specs=[
            by_rows(wide),
            by_rows(depth),
            pl.BlockSpec((depth, wide), lambda i: (0, 0)),
        ],
        compiler_params=params(),
        cost_estimate=cost(2 * total * depth * wide, 12 * total * depth),
    )(tokens, gain, *arrays, cosines, sines)


def turn_kernel(length_ref, cot_ref, normed_ref, dout_ref, dout_t_ref, normed_t_ref):
    rows = cot_ref.shape[0]
    at = pl.program_id(0) * rows + lax.broadcasted_iota(jnp.int32, cot_ref.shape, 0)
    dout = jnp.where(at < length_ref[0], cot_ref[...].astype(jnp.float32), 0.0)
    dout = dout.astype(jnp.bfloat16)
    dout_ref[...] = dout
    dout_t_ref[...] = dout.T
    normed_t_ref[...] = normed_ref[...].T


def turn(length, cotangent, normed):
    total, depth = cotangent.shape
    rows = total // CHUNKS
    by_rows = pl.BlockSpec((rows, depth), lambda i: (i, 0))
    by_columns = pl.BlockSpec((depth, rows), lambda i: (0, i))
    turned = jax.ShapeDtypeStruct((depth, total), jnp.bfloat16)
    return pl.pallas_call(
        turn_kernel,
        out_shape=[jax.ShapeDtypeStruct((total, depth), jnp.bfloat16), turned, turned],
        grid=(CHUNKS,),
        in_specs=[SCALAR, by_rows, by_rows],
        out_specs=[by_rows, by_columns, by_columns],
        compiler_params=params(),
        cost_estimate=cost(total * depth, 10 * total * depth),
    )(length, cotangent, normed)


def project_kernel(x_ref, w_ref, cos_ref, sin_ref, _, out_ref):
    store_turned(out_ref, 0, dot32(x_ref[...], w_ref[...]), cos_ref, sin_ref)


def project(normed, weights, cosines, sines, qkv):
    rows, depth = normed.shape
    width = weights.shape[1]
    steps = width // KV_WIDE
    first = steps // 4
    return pl.pallas_call(
        project_kernel,
        out_shape=jax.ShapeDtypeStruct((rows, width), jnp.bfloat16),
        grid=(steps - first,),
        in_specs=[
            whole(normed),
            pl.BlockSpec((depth, KV_WIDE), lambda i: (0, i + first)),
            whole(cosines),
            whole(sines),
            pl.BlockSpec(memory_space=pl.ANY),
        ],
        out_specs=pl.BlockSpec((rows, KV_WIDE), lambda i: (0, i + first)),
        input_output_aliases={4: 0},
        compiler_params=params(),
        cost_estimate=cost(
            2 * rows * depth * width, 2 * (rows * depth + depth * width + rows * width)
        ),
    )(normed, weights, cosines, sines, qkv)


def attend_kernel(start, length_ref, q_ref, kv_ref, strip_ref, out_ref):
    rows = q_ref.shape[0]
    keys = kv_ref.shape[0]
    length = length_ref[0]
    row_ids = start + lax.broadcasted_iota(jnp.int32, (1, rows), 1)
    limit = jnp.minimum(row_ids, length - 1)
    allowed = lax.broadcasted_iota(jnp.int32, (keys, rows), 0) <= limit
    mixed = []
    sums = []
    for kv in range(kv_ref.shape[1] // KV_WIDE):
        base = kv * KV_WIDE
        at = base + GROUP * LANES
        key = kv_ref[:, at : at + LANES]
        value_t = kv_ref[:, at + LANES : at + 2 * LANES].T
        for g in range(GROUP):
            query = q_ref[:, base + g * LANES : base + (g + 1) * LANES]
            raw = jnp.where(allowed, dot32_nt(key, query), masked_score)
            peak = jnp.max(raw, axis=0, keepdims=True)
            expo = jnp.exp2((raw - peak) * score_scale_log2)
            total = jnp.sum(expo, axis=0, keepdims=True)
            probs = (expo * (1.0 / total)).astype(jnp.bfloat16)
            mixed.append(dot32(value_t, probs).T)
            log_sum = peak * score_scale_log2 + jnp.log2(total)
            sums.append(jnp.where(row_ids < length, log_sum, far_away))
    out_ref[:rows, :] = dot_split(jnp.concatenate(mixed, 1), strip_ref[...])
    out_ref[rows:, :] = jnp.zeros((EXTRA, out_ref.shape[1]), jnp.float32)
    out_ref[rows : rows + len(sums), :rows] = jnp.concatenate(sums, 0)


def attend(length, qkv, strip, index, rows):
    keys = (index + 1) * rows
    width = qkv.shape[1] // 4
    heads = width // KV_WIDE * GROUP
    shape = (rows + EXTRA, strip.shape[1])
    return pl.pallas_call(
        functools.partial(attend_kernel, index * rows),
        out_shape=jax.ShapeDtypeStruct(shape, jnp.float32),
        grid=(1,),
        in_specs=[
            SCALAR,
            pl.BlockSpec((rows, width), lambda i: (index, 0)),
            pl.BlockSpec((keys, width), lambda i: (0, 0)),
            whole(strip),
        ],
        out_specs=pl.BlockSpec(shape, lambda i: (0, 0)),
        compiler_params=params(),
        cost_estimate=cost(
            4 * heads * rows * keys * LANES, 2 * (rows + keys) * width, heads * rows * keys
        ),
    )(length, qkv, qkv, strip)


def forward_kernel(level_ref, part_ref, other_ref, across_ref, outer_ref, *refs):
    x_ref, dout_ref, wo_ref, gain_ref, gate_any, up_any, down_any = refs[:7]
    hidden_ref, normed_t_ref, activ_ref, dgate_ref, dup_ref, mlp_ref, dn_ref = refs[7:14]
    normed_ref, gate_ref, up_ref, down_ref, sems = refs[14:]
    rows = x_ref.shape[0]
    steps, block = down_ref.shape[:2]
    step = pl.program_id(0)

    def fetched(at):
        here = pl.ds(pl.multiple_of(at * block, block), block)
        return [
            pltpu.make_async_copy(gate_any.at[:, here], gate_ref.at[at], sems.at[0, at]),
            pltpu.make_async_copy(up_any.at[:, here], up_ref.at[at], sems.at[1, at]),
            pltpu.make_async_copy(down_any.at[here, :], down_ref.at[at], sems.at[2, at]),
        ]

    @pl.when(step == 0)
    def _():
        for at in range(steps):
            for copy in fetched(at):
                copy.start()
        level = level_ref[0]
        inner = (level == 1) | (level == 2)
        width = part_ref.shape[1]
        second = jnp.where(inner, across_ref[:rows, width:], outer_ref[:rows, :width])
        third = jnp.where(inner, across_ref[:rows, :width], outer_ref[:rows, width:])
        mixed = jnp.concatenate([part_ref[:rows, :], other_ref[:rows, :], second, third], 1)
        hidden = x_ref[...].astype(jnp.float32) + dot32_nt(mixed.astype(jnp.bfloat16), wo_ref[...])
        hidden_ref[...] = hidden
        rms = lax.rsqrt(jnp.mean(hidden * hidden, -1, keepdims=True) + norm_eps)
        normed = (hidden * rms * gain_ref[...]).astype(jnp.bfloat16)
        normed_ref[...] = normed
        normed_t_ref[...] = normed.T
        mlp_ref[...] = jnp.zeros_like(mlp_ref)
        dn_ref[...] = jnp.zeros_like(dn_ref)

    for copy in fetched(step):
        copy.wait()
    wg_ref, wu_ref, wd_ref = gate_ref.at[step], up_ref.at[step], down_ref.at[step]
    normed = normed_ref[...]
    gate = dot32(normed, wg_ref[...])
    up = dot32(normed, wu_ref[...])
    dact = dot32_nt(dout_ref[...], wd_ref[...])
    sigmoid = jax.nn.sigmoid(gate)
    silu = gate * sigmoid
    activ = (silu * up).astype(jnp.bfloat16)
    dgate = (dact * up * sigmoid * (1.0 + gate * (1.0 - sigmoid))).astype(jnp.bfloat16)
    dup = (dact * silu).astype(jnp.bfloat16)
    activ_ref[...] = activ
    dgate_ref[...] = dgate
    dup_ref[...] = dup
    mlp_ref[...] += dot32(activ, wd_ref[...])
    dn_ref[:rows, :] += dot32_nt(dgate, wg_ref[...]) + dot32_nt(dup, wu_ref[...])


def forward_chunk(level, gathered, tokens, dout, w_out, gain, w_gate, w_up, w_down, index, rows):
    depth = tokens.shape[1]
    units = w_gate.shape[1]
    block = 512
    own_rows = pl.BlockSpec((rows, depth), lambda i: (index, 0))
    steps = units // block
    gain = gain[None, :]
    f32, bf16 = jnp.float32, jnp.bfloat16
    outs = [
        jax.ShapeDtypeStruct((rows, depth), f32),
        jax.ShapeDtypeStruct((depth, rows), bf16),
        jax.ShapeDtypeStruct((rows, units), bf16),
        jax.ShapeDtypeStruct((rows, units), bf16),
        jax.ShapeDtypeStruct((rows, units), bf16),
        jax.ShapeDtypeStruct((rows, depth), f32),
        jax.ShapeDtypeStruct((rows + EXTRA, depth), f32),
    ]
    unit_out = pl.BlockSpec((rows, block), lambda i: (0, i))
    return pl.pallas_call(
        forward_kernel,
        out_shape=outs,
        grid=(steps,),
        in_specs=[SCALAR]
        + [whole(array) for array in gathered]
        + [own_rows, own_rows, whole(w_out), whole(gain)]
        + [ANYWHERE] * 3,
        out_specs=[
            whole(outs[0]),
            whole(outs[1]),
            unit_out,
            unit_out,
            unit_out,
            whole(outs[5]),
            whole(outs[6]),
        ],
        scratch_shapes=[
            pltpu.VMEM((rows, depth), bf16),
            pltpu.VMEM((steps, depth, block), bf16),
            pltpu.VMEM((steps, depth, block), bf16),
            pltpu.VMEM((steps, block, depth), bf16),
            pltpu.SemaphoreType.DMA((3, steps)),
        ],
        compiler_params=params(),
        cost_estimate=cost(
            2 * rows * depth * (6 * units + w_out.shape[1]),
            2 * depth * (3 * units + w_out.shape[1]) + 22 * rows * depth,
            rows * units,
        ),
    )(level, *gathered, tokens, dout, w_out, gain, w_gate, w_up, w_down)


def hidden_grad(inner, total_ref, final_ref, hidden_ref, dout_ref, gain_ref):
    dnormed = jnp.where(inner, total_ref[...], final_ref[...])
    hidden = hidden_ref[...]
    rms = lax.rsqrt(jnp.mean(hidden * hidden, -1, keepdims=True) + norm_eps)
    scaled = dnormed * gain_ref[...]
    shift = jnp.mean(scaled * hidden, -1, keepdims=True)
    dhid = dout_ref[...].astype(jnp.float32) + (rms * scaled - hidden * (rms**3 * shift))
    return dhid, dnormed * (hidden * rms)


def backward_kernel(
    start, full, adding, steps, level_ref, total_ref, final_ref, hidden_ref, dout_ref, *refs
):
    gain_two_ref, wo_ref, q_ref = refs[:3]
    kv_here = q_ref.shape[1] // KV_WIDE
    refs = refs[3:]
    kv_refs, refs = refs[: 2 * kv_here], refs[2 * kv_here :]
    part_ref, place_ref, strip_ref, cos_ref, sin_ref = refs[:5]
    extra = (2 if full else 0) + (1 if adding else 0) + 1
    outs, scratch = refs[5 : -3 - extra], refs[-3 - extra :]
    dhid_ref, low_ref, dn_ref, sems = scratch[:4]
    if full:
        x_any, gain_one_ref, other_ref, across_ref, outer_ref, w_any = outs[:6]
        outs = outs[6:]
        x_ref, w_buffers = scratch[4:6]
        tokens_here = pltpu.make_async_copy(
            x_any.at[pl.ds(start, x_ref.shape[0]), :], x_ref, sems.at[4]
        )
    count = (5 if start > 0 else 4) if full else 2
    if adding:
        acc_any, acc_buffers = outs[0], scratch[-1]
    outs = outs[-count:]
    dhid_t_ref, dqkv_ref = outs[:2]
    if full:
        input_grad_ref, gains_ref = outs[2:4]
    rows = q_ref.shape[0]
    keys = kv_refs[0].shape[0]
    shard = pl.program_id(0)
    level = level_ref[0]
    inner = (level == 1) | (level == 2)

    def fetched(at, sums):
        source, buffers = (acc_any, acc_buffers) if sums else (w_any, w_buffers)
        lanes = buffers.shape[2]
        here = pl.ds(pl.multiple_of(at * lanes, lanes), lanes)
        slot = at % 2
        sem = sems.at[slot + 2] if sums else sems.at[slot]
        return pltpu.make_async_copy(source.at[:, here], buffers.at[slot], sem)

    def fetch(at):
        if adding:
            fetched(at, True).start()
        if full:
            fetched(at, False).start()

    @pl.when(shard == 0)
    def _():
        for at in range(min(2, steps)):
            fetch(at)
        if full:
            tokens_here.start()
        dhid, dgain = hidden_grad(
            inner, total_ref, final_ref, hidden_ref, dout_ref, gain_two_ref
        )
        dhid_ref[...] = dhid
        low = dhid.astype(jnp.bfloat16)
        low_ref[...] = low
        dhid_t_ref[...] = low.T
        if full:
            gains_ref[...] = jnp.zeros_like(gains_ref)
            gains_ref[1:2, :] = jnp.sum(dgain, 0, keepdims=True)
            dn_ref[...] = jnp.zeros_like(dn_ref)

    def rotate_back(grads):
        turned = grads * cos_ref[...] - pltpu.roll(grads, LANES // 2, 1) * sin_ref[...]
        return turned.astype(jnp.bfloat16)

    dmixed_all = dot32(low_ref[...], wo_ref[...]).astype(jnp.bfloat16)
    mixed = part_ref[...]
    if full:
        far = jnp.where(inner, across_ref[...], outer_ref[...])
        far = jnp.where(shard == 1, other_ref[...], far)
        mixed = jnp.where(shard == 0, mixed, far)
    products = dmixed_all.astype(jnp.float32) * dot_split(mixed[:rows], place_ref[...])
    causal = lax.broadcasted_iota(jnp.int32, (rows, rows), 0) <= lax.broadcasted_iota(
        jnp.int32, (rows, rows), 1
    )
    acc_ref = None
    if adding:
        fetched(shard, True).wait()
        acc_ref = acc_buffers.at[shard % 2]
    grads = []
    for kv in range(kv_here):
        key_ref, value_ref = kv_refs[2 * kv : 2 * kv + 2]
        heads = range(kv * GROUP, (kv + 1) * GROUP)
        lanes = {h: slice(h * LANES, (h + 1) * LANES) for h in heads}
        row_dots = {h: jnp.sum(products[:, lanes[h]].T, axis=0, keepdims=True) for h in heads}
        log_sums = {h: mixed[rows + h : rows + h + 1, :rows] for h in heads}
        dqueries = dict.fromkeys(heads)
        here = slice(2 * kv * LANES, (2 * kv + 1) * LANES)
        there = slice((2 * kv + 1) * LANES, (2 * kv + 2) * LANES)
        for tile in range(keys // rows):
            span = slice(tile * rows, (tile + 1) * rows)
            key = key_ref[span, :]
            value = value_ref[span, :]
            key_t = key.T
            dkey = None if acc_ref is None else acc_ref[span, here]
            dvalue = None if acc_ref is None else acc_ref[span, there]
            last = tile * rows == start
            for h in heads:
                at = kv * KV_WIDE + (h % GROUP) * LANES
                query = q_ref[:, at : at + LANES]
                dmixed = dmixed_all[:, lanes[h]]
                raw = dot32_nt(key, query)
                probs = jnp.exp2(raw * score_scale_log2 - log_sums[h])
                if last:
                    probs = jnp.where(causal, probs, 0.0)
                dprobs = dot32_nt(value, dmixed)
                dscores = (probs * (dprobs - row_dots[h])).astype(jnp.bfloat16)
                dquery = dot32(key_t, dscores)
                dqueries[h] = dquery if dqueries[h] is None else dqueries[h] + dquery
                dkey_one = dot32(dscores, query)
                dvalue_one = dot32(probs.astype(jnp.bfloat16), dmixed)
                dkey = dkey_one if dkey is None else dkey + dkey_one
                dvalue = dvalue_one if dvalue is None else dvalue + dvalue_one
            if full and not last:
                outs[4][span, here] = dkey
                outs[4][span, there] = dvalue
        grads += [rotate_back(dqueries[h].T * score_scale) for h in heads]
        grads.append(rotate_back(dkey * score_scale))
        grads.append(dvalue.astype(jnp.bfloat16))
    grads = jnp.concatenate(grads, 1)
    if full:
        fetched(shard, False).wait()
        dn_ref[...] += dot32_nt(grads, w_buffers[shard % 2])

        @pl.when(shard + 2 < steps)
        def _():
            fetch(shard + 2)

    @pl.when(shard == 0)
    def _():
        wide = strip_ref.shape[1]
        for kv in range(kv_here):
            dqkv_ref[:, kv * wide : (kv + 1) * wide] = dot32(
                grads[:, kv * KV_WIDE : (kv + 1) * KV_WIDE], strip_ref[...]
            ).astype(jnp.bfloat16)

    if not full:
        return

    @pl.when(shard == pl.num_programs(0) - 1)
    def _():
        tokens_here.wait()
        dnormed = dn_ref[...]
        inputs = x_ref[...].astype(jnp.float32)
        rms = lax.rsqrt(jnp.mean(inputs * inputs, -1, keepdims=True) + norm_eps)
        scaled = dnormed * gain_one_ref[...]
        shift = jnp.mean(scaled * inputs, -1, keepdims=True)
        grad = dhid_ref[...] + (rms * scaled - inputs * (rms**3 * shift))
        input_grad_ref[...] = grad.astype(jnp.bfloat16)
        gains_ref[0:1, :] = jnp.sum(dnormed * (inputs * rms), 0, keepdims=True)


def backward_chunk(
    level, sums_two, hidden, dout, tokens, gains, weights, qkv, gathered, places, tables, acc,
    index, rows, full=True, grad_into=None
):
    start = index * rows
    keys = start + rows
    depth = tokens.shape[1]
    out_pad, qkv_pad = weights
    place_out, strip = places
    far_rows, width = gathered[0].shape
    out_wide = place_out.shape[1]
    kv_here = out_wide // (GROUP * LANES)
    wide = kv_here * KV_WIDE
    levels = qkv.shape[1] // wide
    own_rows = pl.BlockSpec((rows, depth), lambda t: (index, 0))
    table = pl.BlockSpec((rows, LANES), lambda t: (index, 0))
    gains = [gain[None, :] for gain in gains]
    key_value = lambda at: pl.BlockSpec(
        (keys, LANES), lambda t: (0, (wide // LANES) * t + at)
    )
    across = pl.BlockSpec((far_rows, width), lambda t: (0, jnp.where(t == 2, 1, 0)))
    outer = pl.BlockSpec((far_rows, width), lambda t: (0, jnp.where(t == 3, 1, 0)))
    in_specs = [
        SCALAR,
        whole(hidden),
        whole(hidden),
        whole(hidden),
        own_rows,
        whole(gains[1]),
        pl.BlockSpec((depth, out_wide), lambda t: (0, t)),
        pl.BlockSpec((rows, wide), lambda t: (index, t)),
    ]
    for kv in range(kv_here):
        at = kv * (KV_WIDE // LANES) + GROUP
        in_specs += [key_value(at), key_value(at + 1)]
    in_specs += [
        whole(gathered[0]),
        whole(place_out),
        whole(strip),
        table,
        table,
    ]
    args = [level, *sums_two, hidden, dout, gains[1], out_pad]
    args += [qkv] * (1 + 2 * kv_here)
    args += [gathered[0], place_out, strip, *tables]
    sums_wide = 2 * kv_here * LANES
    if full:
        in_specs += [ANYWHERE, whole(gains[0]), whole(gathered[1]), across, outer]
        in_specs.append(ANYWHERE)
        args += [tokens, gains[0], *gathered[1:], qkv_pad]
    if acc is not None:
        in_specs.append(ANYWHERE)
        args.append(acc)
    f32, bf16 = jnp.float32, jnp.bfloat16
    outs = [
        jax.ShapeDtypeStruct((depth, rows), bf16),
        jax.ShapeDtypeStruct((rows, kv_here * strip.shape[1]), bf16),
        jax.ShapeDtypeStruct(tokens.shape, bf16),
        jax.ShapeDtypeStruct((8, depth), f32),
    ]
    outs = outs if full else outs[:2]
    out_specs = [whole(out) for out in outs]
    aliases = {}
    if full:
        out_specs[2] = own_rows
        if grad_into is not None:
            aliases = {len(args): 2}
            in_specs.append(ANYWHERE)
            args.append(grad_into)
    if full and start > 0:
        outs.append(jax.ShapeDtypeStruct((start, levels * sums_wide), f32))
        out_specs.append(pl.BlockSpec((start, sums_wide), lambda t: (0, t)))
    steps = levels if full else 1
    scratch = [
        pltpu.VMEM((rows, depth), f32),
        pltpu.VMEM((rows, depth), bf16),
        pltpu.VMEM((rows, depth), f32),
        pltpu.SemaphoreType.DMA((5,)),
    ]
    if full:
        scratch += [pltpu.VMEM((rows, depth), bf16), pltpu.VMEM((2, depth, wide), bf16)]
    if acc is not None:
        scratch.append(pltpu.VMEM((min(2, steps), keys, sums_wide), f32))
    results = pl.pallas_call(
        functools.partial(backward_kernel, start, full, acc is not None, steps),
        out_shape=outs,
        grid=(steps,),
        input_output_aliases=aliases,
        in_specs=in_specs,
        out_specs=out_specs,
        scratch_shapes=scratch,
        compiler_params=params(),
        cost_estimate=cost(
            levels * rows * (20 * kv_here * keys * LANES + 2 * depth * (out_wide + wide)),
            2 * depth * levels * (out_wide + wide) + 16 * rows * depth,
            levels * kv_here * GROUP * rows * keys,
        ),
    )(*args)
    return results[:4], (results[4] if full and start > 0 else None)


def rows_kernel(lefts, groups, adding, picked, together, side_ref, *refs):
    refs = list(refs)
    held_ref = refs.pop()
    out_refs = refs[-len(picked) :]
    refs = refs[: -len(picked)]
    recv_ref = refs.pop() if adding else None
    step = pl.program_id(0)
    left_refs = []
    for count in lefts:
        left_refs.append(refs[:count])
        refs = refs[count:]
    rights = []
    for _ in groups:
        rights.append(refs[:CHUNKS])
        refs = refs[CHUNKS:]
    rows = left_refs[0][0].shape[0]
    blocks = held_ref.shape[1] // rows

    @pl.when(step == 0)
    def _():
        for which, pieces in enumerate(left_refs):
            for n, ref in enumerate(pieces):
                m, j = n % blocks, n // blocks
                wide = ref.shape[1]
                held_ref[which, m * rows : (m + 1) * rows, j * wide : (j + 1) * wide] = ref[...]

    chunk = held_ref.shape[2] // CHUNKS
    whole_columns = slice(0, out_refs[0].shape[1])

    def give(group, left, columns):
        right = jnp.concatenate([ref[:chunk, :].astype(jnp.bfloat16) for ref in group], 0)
        total = dot32(held_ref[left], right)
        if recv_ref is not None:
            total = total + recv_ref[:, columns]
        for out_ref, parts in zip(out_refs, picked):
            at = 0
            for start, size in parts:
                out_ref[at : at + size, columns] = total[start : start + size]
                at += size

    begin = 0
    for group, (left, first, steps) in zip(rights, groups):
        if together:
            width = group[0].shape[1]
            give(group, left, slice(begin, begin + width))
            begin += width
        else:

            @pl.when((step >= first) & (step < first + steps))
            def _(group=group, left=left):
                give(group, left, whole_columns)


def rows_of(lefts, groups, side, rows, blocks, step, recv=None, picked=None):
    if picked is None:
        picked = [[(0, rows * blocks)]]
    at = lambda m: lambda i, side: ((m ^ side[2]) * side[1] + side[0], 0)
    specs = []
    args = []
    counts = []
    for left in lefts:
        pieces = left if isinstance(left, list) else [left]
        counts.append(len(pieces) * blocks)
        for piece in pieces:
            for m in range(blocks):
                specs.append(pl.BlockSpec((rows, piece.shape[1]), at(m)))
                args.append(piece)
    tokens = sum(piece.shape[1] for piece in pieces)
    first = 0
    plan = []
    together = step is None
    for which, rights in groups:
        if together:
            plan.append((which, 0, 1))
            specs += [whole(right) for right in rights]
            args += rights
            first += rights[0].shape[1]
            continue
        steps = rights[0].shape[1] // step
        plan.append((which, first, steps))
        for right in rights:
            pick = lambda i, side, first=first, steps=steps: (0, jnp.clip(i - first, 0, steps - 1))
            specs.append(pl.BlockSpec((right.shape[0], step), pick))
            args.append(right)
        first += steps
    if together:
        first, step = 1, first
    total = first * step
    block = lambda height: pl.BlockSpec((height, step), lambda i, side: (0, i))
    if recv is not None:
        specs.append(block(rows * blocks))
        args.append(recv)
    heights = [sum(size for _, size in parts) for parts in picked]
    results = pl.pallas_call(
        functools.partial(rows_kernel, counts, plan, recv is not None, picked, together),
        out_shape=[jax.ShapeDtypeStruct((height, total), jnp.float32) for height in heights],
        grid_spec=pltpu.PrefetchScalarGridSpec(
            num_scalar_prefetch=1,
            grid=(first,),
            in_specs=specs,
            out_specs=[block(height) for height in heights],
            scratch_shapes=[pltpu.VMEM((len(lefts), rows * blocks, tokens), jnp.bfloat16)],
        ),
        compiler_params=params(),
        cost_estimate=cost(
            2 * rows * blocks * tokens * total,
            4 * rows * blocks * total + 2 * tokens * (total + rows * blocks),
        ),
    )(side, *args)
    return results[0] if len(picked) == 1 else results


def finish_kernel(*refs):
    query_ref, key_ref, value_ref, out_ref = refs[4:]
    kv_here = key_ref.shape[1] // HD
    q_cols = out_ref.shape[1]
    for at in range(2):
        kept_ref, far_ref = refs[2 * at : 2 * at + 2]
        half = far_ref.shape[0]
        sums = kept_ref[...] + far_ref[...]
        here = slice(at * half, (at + 1) * half)
        out_ref[here, :] = sums[:, :q_cols]
        start = q_cols
        cut = [[], [], []]
        for kv in range(kv_here):
            for i, width in enumerate((GROUP * HD, HD, HD)):
                cut[i].append(sums[:, start : start + width])
                start += width
        for ref, pieces in zip((query_ref, key_ref, value_ref), cut):
            ref[here, :] = jnp.concatenate(pieces, 1)


def finish(one, far_one, two, far_two, kv_here):
    half, columns = far_one.shape
    first = pl.BlockSpec((half, columns), lambda i: (0, 0))
    q_cols = kv_here * GROUP * HD
    outs = [
        jax.ShapeDtypeStruct((2 * half, width), jnp.float32)
        for width in (q_cols, kv_here * HD, kv_here * HD, q_cols)
    ]
    return pl.pallas_call(
        finish_kernel,
        out_shape=outs,
        grid=(1,),
        in_specs=[first] * 4,
        out_specs=[whole(out) for out in outs],
        compiler_params=params(),
        cost_estimate=cost(4 * half * columns, 32 * half * columns),
    )(one, far_one, two, far_two)


def shards(
    tokens,
    lengths,
    positions,
    cotangent,
    norm_gain,
    w_query,
    w_key,
    w_value,
    w_out,
    mlp_gain,
    w_gate,
    w_up,
    w_down,
):
    seq_rows, depth = tokens.shape
    chips = lax.axis_size("chip")
    dp = chips * 2
    tp = lax.axis_size("tp")
    chip = lax.axis_index("chip")
    core = lax.axis_index("core")
    level = lax.axis_index("tp")
    low = level < 2
    inner = (level == 1) | (level == 2)
    heads_here = w_query.shape[1] // HD
    kv_here = w_key.shape[1] // HD
    rows = seq_rows // CHUNKS
    slice_rows = depth // dp
    level_ref = level.astype(jnp.int32).reshape(1)
    by_hand = dp == 8
    swap = lambda array: lax.ppermute(array, "core", [(0, 1), (1, 0)])
    to_level = lambda array, s: along(array, [(t, t ^ s) for t in range(tp)])

    at_row = (chip * 2 + core) * slice_rows
    cols = lambda w: lax.dynamic_slice_in_dim(w, at_row, slice_rows, 1).astype(jnp.float32).T
    (out_slice,) = fence(cols(w_out))
    qkv_slice = jnp.concatenate(
        [
            lax.dynamic_slice_in_dim(w_query, at_row, slice_rows, 0).astype(jnp.float32),
            cols(w_key.T),
            cols(w_value.T),
        ],
        1,
    )
    out_slice, qkv_slice = fence(out_slice, qkv_slice)
    out_near = along(out_slice, PAIRS)
    qkv_near = along(qkv_slice, PAIRS)
    meta = jnp.stack([chip, core]).astype(jnp.int32)

    pq = place_query(heads_here)
    pkv = place_key_value(kv_here)
    p_all = place_all(heads_here, kv_here)
    strip_one = place_all(GROUP, 1).T
    p_out = place_plain(heads_here)
    strip_out = p_out.T

    half_dim = HD // 2
    freqs = rope_base ** (-(jnp.arange(half_dim).astype(jnp.float32) * 2.0 / HD))
    freqs = jnp.pad(freqs, (0, LANES // 2 - half_dim))
    angles = positions.astype(jnp.float32)[:, None] * jnp.concatenate([freqs, freqs])[None, :]
    cosines = jnp.cos(angles)
    sines = jnp.sin(angles) * jnp.where(jnp.arange(LANES) < LANES // 2, -1.0, 1.0)

    cosines, sines, out_near = fence(cosines, sines, out_near)
    out_across = along(jnp.stack([out_slice, out_near]), MIDDLE)
    qkv_own, normed_one, own_pad = start(
        tokens, norm_gain, w_query, w_key.T, w_value.T, pq, pkv, cosines, sines
    )

    def far_slices(near, across, outer):
        return jnp.stack(
            [
                near,
                jnp.where(inner, across[1], outer[0]),
                jnp.where(inner, across[0], outer[1]),
            ]
        )

    order = list(reversed(range(CHUNKS)))
    c0, c1, c2, c3 = order
    own, other, across, outer = {}, {}, {}, {}
    part, total, final = {}, {}, {}

    def hop_1(j):
        other[j] = along(own[j], PAIRS)

    def hop_2(j):
        across[j] = along(jnp.concatenate([own[j], other[j]], 1), MIDDLE)

    def hop_3(j):
        outer[j] = along(across[j], OUTWARD)

    coming = {}

    def add_1(j):
        coming[j] = along(part[j], INWARD)

    def add_2(j):
        total[j] = part[j][:rows] + coming[j][:rows]
        coming[j] = along(total[j], MIDDLE)

    def add_3(j, inward, extra=0):
        both = jnp.where(inner, total[j] + coming[j], inward)
        total[j] = jnp.pad(both, ((0, extra), (0, 0)))
        final[j] = along(total[j], PAIRS)
        return final[j]

    def to_chip(array, m):
        return lax.ppermute(array, "chip", [(i, i ^ m) for i in range(chips)])

    def over_chips_1(piece):
        cut = piece.shape[1] // 2
        one, two = piece[:, :cut], piece[:, cut:]
        return jnp.stack([one, to_chip(one, 1)]), jnp.stack([two, to_chip(two, 2)])

    def over_chips_2(one, two):
        return one, to_chip(one, 2), two, to_chip(two, 1)

    def over_chips_3(one, one_far, two, two_far):
        upper = jnp.stack([one[0], one[1], one_far[0], one_far[1]])
        lower = jnp.stack([two[0], two_far[0], two[1], two_far[1]])
        return jnp.concatenate([upper, lower], 2)

    qkv_own, out_across, qkv_near = fence(qkv_own, out_across, qkv_near)
    out_outer = along(out_across, OUTWARD)
    qkv_across = along(jnp.stack([qkv_slice, qkv_near]), MIDDLE)
    own[c0] = attend(lengths, qkv_own, strip_out, c0, rows)
    own[c1] = attend(lengths, qkv_own, strip_out, c1, rows)
    own, qkv_own, out_outer = fence(own, qkv_own, out_outer)
    others = along(jnp.concatenate([own[c0], own[c1]], 0), PAIRS)
    out_far = far_slices(out_near, out_across, out_outer)
    out_mine = over_chips_1(out_far) if by_hand else out_far
    own[c2] = attend(lengths, qkv_own, strip_out, c2, rows)
    own[c3] = attend(lengths, qkv_own, strip_out, c3, rows)
    own[c3], qkv_across = fence(own[c3], qkv_across)
    qkv_outer = along(qkv_across, OUTWARD)
    own, others, normed_one, w_out, out_mine = fence(own, others, normed_one, w_out, out_mine)
    other[c0], other[c1] = others[: rows + EXTRA], others[rows + EXTRA :]
    if by_hand:
        out_mine = over_chips_2(*out_mine)
    else:
        out_mine = lax.all_gather(out_mine, ("chip", "core"))
    hop_2(c0)
    dout, dout_t, normed_one_t = turn(lengths, cotangent, normed_one)
    w_out_t = w_out.T
    own, other, across, dout, dout_t, normed_one_t, w_out_t, out_mine, qkv_outer = fence(
        own, other, across, dout, dout_t, normed_one_t, w_out_t, out_mine, qkv_outer
    )
    hop_1(c2)
    hop_3(c0)
    hop_2(c1)
    qkv_far = lax.all_gather(far_slices(qkv_near, qkv_across, qkv_outer), ("chip", "core"))
    if by_hand:
        out_mine = over_chips_3(*out_mine)
        out_theirs = swap(out_mine)
        out_pad, out_plain = spread(
            spread_out_kernel,
            meta,
            w_out_t,
            [p_out],
            out_mine,
            out_theirs,
            [4 * p_out.shape[1], 4 * p_out.shape[0]],
        )
    else:
        plain = [w_out_t] + [
            out_mine[:, s].reshape(depth, -1).astype(jnp.bfloat16) for s in range(tp - 1)
        ]
        out_plain = jnp.concatenate(plain, 1)
        out_pad = jnp.concatenate([dot32(w, p_out).astype(jnp.bfloat16) for w in plain], 1)
    hidden, normed_t, activ, dgate, dup, mlp_part = {}, {}, {}, {}, {}, {}

    def feed(j):
        gathered = (own[j], other[j], across[j], outer[j])
        (hidden[j], normed_t[j], activ[j], dgate[j], dup[j], mlp_part[j], part[j]) = forward_chunk(
            level_ref, gathered, tokens, dout, out_plain, mlp_gain, w_gate, w_up, w_down, j, rows
        )

    own, other, across, outer, out_pad, out_plain = fence(
        own, other, across, outer, out_pad, out_plain
    )
    hop_1(c3)
    hop_3(c1)
    hop_2(c2)
    feed(c0)
    part, other = fence(part, other)
    add_1(c0)
    own, other, across, outer, part, hidden = fence(own, other, across, outer, part, hidden)
    hop_3(c2)
    hop_2(c3)
    feed(c1)
    qkv_far, hidden[c1] = fence(qkv_far, hidden[c1])
    qkv_pad = spread_qkv(own_pad, pq, pkv, qkv_far)
    own, other, across, outer, part, total, coming, hidden, qkv_pad = fence(
        own, other, across, outer, part, total, coming, hidden, qkv_pad
    )
    add_1(c1)
    hop_3(c3)
    add_2(c0)
    feed(c2)
    qkv_pad, hidden[c2] = fence(qkv_pad, hidden[c2])
    qkv = project(normed_one, qkv_pad, cosines, sines, qkv_own)
    own, other, across, outer, part, total, coming, hidden, qkv = fence(
        own, other, across, outer, part, total, coming, hidden, qkv
    )
    coming[c2] = add_3(c0, part[c2][:rows])
    add_2(c1)
    feed(c3)

    listed = lambda pieces: [pieces[j] for j in range(CHUNKS)]
    keep_side = jnp.stack([core, 2, 0]).astype(jnp.int32)
    keep_turned = jnp.stack([core, 2, chip]).astype(jnp.int32)
    send_side = jnp.stack([1 - core, 2, 0]).astype(jnp.int32)
    send_turned = jnp.stack([1 - core, 2, chip]).astype(jnp.int32)
    all_rows = jnp.array([0, 1, 0], jnp.int32)

    def send_rows(lefts, groups, step, side=send_side):
        if not by_hand:
            return rows_of(lefts, groups, all_rows, depth // 4, 4, step)
        return rows_of(lefts, groups, side, slice_rows, chips, step)

    def keep_rows(lefts, groups, received, step, side=keep_side, picked=None):
        if not by_hand:
            return received
        return rows_of(lefts, groups, side, slice_rows, chips, step, received, picked)

    def swap_rows(array):
        return swap(array) if by_hand else array

    def scatter(array, axes):
        return lax.psum_scatter(array, axes, scatter_dimension=0, tiled=True)

    units = w_gate.shape[1]
    mlp_args = (
        [listed(normed_t), dout_t],
        [(0, listed(dgate)), (0, listed(dup)), (1, listed(activ))],
    )
    acc = None
    input_grad = None
    dhid_t, dqkv_own, gains = {}, {}, {}

    def back(j):
        nonlocal acc, input_grad
        (dhid_t[j], dqkv_own[j], input_grad, gains[j]), acc = back_some(j, True)

    def back_own(j):
        return back_some(j, False)[0]

    def back_some(j, full):
        return backward_chunk(
            level_ref,
            (total[j], final[j]),
            hidden[j],
            dout,
            tokens,
            (norm_gain, mlp_gain),
            (out_pad, qkv_pad),
            qkv,
            (own[j], other[j], across[j], outer[j]),
            (p_out, strip_one),
            (cosines, sines),
            acc,
            j,
            rows,
            full,
            input_grad,
        )

    grad_mlp = rows_of(*mlp_args, all_rows, depth // 4, 4, units // 2)
    own, other, across, outer, part, total, coming, final, hidden, grad_mlp = fence(
        own, other, across, outer, part, total, coming, final, hidden, grad_mlp
    )
    grad_mlp = scatter(grad_mlp, ("chip", "core"))
    coming[c3] = add_3(c1, part[c3][:rows])
    add_2(c2)
    back(c0)

    near = lambda: jnp.where(low, mlp_part[1], mlp_part[2])
    edge = lambda: jnp.where(low, mlp_part[0], mlp_part[3])
    leave_far = lambda: jnp.where(low, mlp_part[3], mlp_part[0])
    leave_near = lambda: jnp.where(low, mlp_part[2], mlp_part[1])
    total, coming, final, hidden, mlp_part, acc, dhid_t = fence(
        total, coming, final, hidden, mlp_part, acc, dhid_t
    )
    far_sum = add_3(c2, leave_far())
    add_2(c3)
    back(c1)
    total, coming, final, hidden, mlp_part, far_sum, acc, dhid_t = fence(
        total, coming, final, hidden, mlp_part, far_sum, acc, dhid_t
    )
    add_3(c3, leave_near(), EXTRA)
    far_in = along(leave_far() + far_sum, MIDDLE)
    back(c2)
    total, final, hidden, acc, dhid_t = fence(total, final, hidden, acc, dhid_t)
    dhid_t[c3], dqkv_own[c3] = back_own(c3)
    dhid_t, dqkv_own, far_in, mlp_part, final = fence(
        dhid_t, dqkv_own, far_in, mlp_part, final
    )
    last = along(jnp.where(inner, edge() + far_in, near()), PAIRS)
    near_in = along(leave_near() + final[c3][:rows], MIDDLE)
    q_cols = heads_here * HD
    attn_args = (
        [listed(dhid_t), normed_one_t],
        [(0, listed(own)), (1, listed(dqkv_own))],
    )
    sent = swap_rows(send_rows(*attn_args, None, send_turned))
    total, final, hidden, acc, sent = fence(total, final, hidden, acc, sent)
    if by_hand:
        half = slice_rows // 2
        upper = lambda m: (m * slice_rows, half)
        lower = lambda m: (m * slice_rows + half, half)
        picked = [
            [upper(1), upper(3)],
            [upper(0), upper(2)],
            [lower(2), lower(3)],
            [lower(0), lower(1)],
        ]
        pieces = keep_rows(*attn_args, sent, None, keep_turned, picked)
        pieces, hidden = fence(pieces, hidden)
        one_away, one, two_away, two = pieces
        pieces = (one, to_chip(one_away, 1), two, to_chip(two_away, 2))
    else:
        pieces = scatter(sent, ("chip", "core"))
    back(c3)
    pieces, gains, input_grad = fence(pieces, gains, input_grad)
    gain_sums = gains[0] + gains[1] + gains[2] + gains[3]
    gain_sums = gain_sums + swap(gain_sums)
    gain_sums, last, near_in = fence(gain_sums, last, near_in)
    mlp_rows = jnp.where(inner, near() + near_in, edge()) + last
    hidden_rows = jnp.where(
        low,
        jnp.where(level == 0, hidden[0], hidden[1]),
        jnp.where(level == 2, hidden[2], hidden[3]),
    )
    layer_out = (hidden_rows + mlp_rows).astype(jnp.bfloat16)
    mlp_grads = [grad_mlp[:, at * units : (at + 1) * units] for at in range(3)]
    if by_hand:
        one = pieces[0] + pieces[1]
        two = pieces[2] + pieces[3]
        far_one = to_chip(one[half:], 2)
        far_two = to_chip(two[half:], 1)
        others = [to_chip(gain_sums, m) for m in range(1, chips)]
        far_one, far_two, mlp_grads, layer_out = fence(far_one, far_two, mlp_grads, layer_out)
        attn_grads = finish(one, far_one, two, far_two, kv_here)
        others, attn_grads = fence(others, attn_grads)
        gain_sums = sum(others, gain_sums)
    else:
        gain_sums = lax.psum(gain_sums, "chip")
        grad_qkv = pieces[:, q_cols:]
        one = strip_one.shape[1]
        picked = lambda at, width: jnp.concatenate(
            [grad_qkv[:, kv * one + at : kv * one + at + width] for kv in range(kv_here)], 1
        )
        attn_grads = (
            picked(0, GROUP * HD),
            picked(GROUP * HD, HD),
            picked((GROUP + 1) * HD, HD),
            pieces[:, :q_cols],
        )
    gain_rows = lax.dynamic_slice_in_dim(gain_sums, at_row, slice_rows, 1)
    grad_query, grad_key, grad_value, grad_out_t = attn_grads
    return (
        layer_out,
        input_grad,
        gain_rows[0],
        grad_query,
        grad_key,
        grad_value,
        grad_out_t.T,
        gain_rows[1],
        mlp_grads[0],
        mlp_grads[1],
        mlp_grads[2].T,
    )


def solution(mesh):
    devices = mesh.devices
    dp, tp = devices.shape
    split = Mesh(devices.reshape(dp // 2, 2, tp), ("chip", "core", "tp"))
    data = ("chip", "core")
    return jax.shard_map(
        shards,
        mesh=split,
        in_specs=(
            P(data, None),
            P(data),
            P(data),
            P(data, None),
            P(),
            P(None, "tp"),
            P(None, "tp"),
            P(None, "tp"),
            P("tp", None),
            P(),
            P(None, "tp"),
            P(None, "tp"),
            P("tp", None),
        ),
        out_specs=(
            P(("chip", "core", "tp"), None),
            P(data, None),
            P(data),
            P(data, "tp"),
            P(data, "tp"),
            P(data, "tp"),
            P("tp", data),
            P(data),
            P(data, "tp"),
            P(data, "tp"),
            P("tp", data),
        ),
        check_vma=False,
    )
```

```python
import functools

import jax
import jax.numpy as jnp
from jax import lax
from jax.experimental import pallas as pl
from jax.experimental.pallas import tpu as pltpu
from jax.sharding import Mesh
from jax.sharding import PartitionSpec as P

HD = 96
LANES = 128
GROUP = 2
KV_WIDE = (GROUP + 2) * LANES
rope_base = 100000.0
norm_eps = 1e-05
masked_score = -1e30
far_away = 1e30
score_scale = HD ** (-0.5)
score_scale_log2 = score_scale * 1.4426950408889634
CHUNKS = 4
EXTRA = 8
VMEM_BYTES = 40 * 1024 * 1024
NT = (((1,), (1,)), ((), ()))


def params():
    return pltpu.CompilerParams(vmem_limit_bytes=VMEM_BYTES)


def cost(flops, moved, exps=0):
    return pl.CostEstimate(
        flops=flops // 1024, bytes_accessed=moved // 1024, transcendentals=exps // 1024
    )


def dot32(a, b):
    return jnp.dot(a, b, preferred_element_type=jnp.float32)


def dot32_nt(a, b):
    return lax.dot_general(a, b, NT, preferred_element_type=jnp.float32)


def dot_split(a, places):
    high = a.astype(jnp.bfloat16)
    rest = (a - high.astype(jnp.float32)).astype(jnp.bfloat16)
    return dot32(high, places) + dot32(rest, places)


def fence(*trees):
    return lax.optimization_barrier(trees)


def whole(array, buffers=None):
    zeros = (0,) * len(array.shape)
    return pl.BlockSpec(array.shape, lambda *_: zeros)


SCALAR = pl.BlockSpec(memory_space=pltpu.SMEM)
ANYWHERE = pl.BlockSpec(memory_space=pl.ANY)


def halves(entry):
    half_dim = HD // 2
    return (entry // half_dim) * (LANES // 2) + entry % half_dim


def placement(lanes, width):
    return (lanes[:, None] == jnp.arange(width)[None, :]).astype(jnp.bfloat16)


def place_query(heads):
    source = jnp.arange(heads * HD)
    return placement((source // HD) * LANES + halves(source % HD), heads * LANES)


def place_key_value(kv_heads):
    source = jnp.arange(kv_heads * HD)
    head = source // HD
    keys = head * 2 * LANES + halves(source % HD)
    values = head * 2 * LANES + LANES + source % HD
    return placement(jnp.concatenate([keys, values]), kv_heads * 2 * LANES)


def place_all(heads, kv_heads):
    source = jnp.arange(heads * HD)
    head = source // HD
    query = (head // GROUP) * KV_WIDE + (head % GROUP) * LANES + halves(source % HD)
    source = jnp.arange(kv_heads * HD)
    base = (source // HD) * KV_WIDE + GROUP * LANES
    keys = base + halves(source % HD)
    values = base + LANES + source % HD
    return placement(jnp.concatenate([query, keys, values]), kv_heads * KV_WIDE)


def place_plain(heads):
    source = jnp.arange(heads * HD)
    return placement((source // HD) * LANES + source % HD, heads * LANES)


PAIRS = [(0, 1), (1, 0), (2, 3), (3, 2)]
INWARD = [(0, 1), (3, 2)]
MIDDLE = [(1, 2), (2, 1)]
OUTWARD = [(1, 0), (2, 3)]


def along(part, pairs):
    return lax.ppermute(part, "tp", pairs)


def store_qkv(out_ref, here, base, query, key_value):
    wide = GROUP * LANES
    for kv in range(key_value.shape[1] // (2 * LANES)):
        at = base + kv * KV_WIDE
        there = slice(kv * 2 * LANES, (kv + 1) * 2 * LANES)
        out_ref[here, at : at + wide] = query[:, kv * wide : (kv + 1) * wide]
        out_ref[here, at + wide : at + KV_WIDE] = key_value[:, there]


def store_turned(out_ref, at, lin, cos_ref, sin_ref):
    for h in range(GROUP + 2):
        one = lin[:, h * LANES : (h + 1) * LANES]
        if h < GROUP + 1:
            one = one * cos_ref[...] + pltpu.roll(one, LANES // 2, 1) * sin_ref[...]
        out_ref[:, at + h * LANES : at + (h + 1) * LANES] = one.astype(jnp.bfloat16)


def spread_out_kernel(meta_ref, own_ref, p_ref, mine_ref, theirs_ref, pad_ref, plain_ref):
    rows, width = mine_ref.shape[2:]
    wide = p_ref.shape[1]
    for side, ref in enumerate((mine_ref, theirs_ref)):
        here = pl.ds(pl.multiple_of((meta_ref[1] ^ side) * rows, rows), rows)
        for s in range(4):
            block = own_ref[here, :] if s == 0 else ref[0, s - 1].astype(jnp.bfloat16)
            plain_ref[here, s * width : (s + 1) * width] = block
            pad_ref[here, s * wide : (s + 1) * wide] = dot32(block, p_ref[...]).astype(
                jnp.bfloat16
            )


def spread_qkv_kernel(pq_ref, pkv_ref, far_ref, _, out_ref):
    parts, _, rows, width = far_ref.shape
    split = pq_ref.shape[0]
    block = far_ref[:, 0].reshape(parts * rows, width).astype(jnp.bfloat16)
    query = dot32(block[:, :split], pq_ref[...]).astype(jnp.bfloat16)
    key_value = dot32(block[:, split:], pkv_ref[...]).astype(jnp.bfloat16)
    store_qkv(out_ref, slice(None), 0, query, key_value)


def spread_qkv(padded, pq, pkv, far):
    total = padded.shape[0]
    dp, others, rows, width = far.shape
    wide = padded.shape[1] // (others + 1)
    parts = max(1, dp // 2)
    block = parts * rows
    return pl.pallas_call(
        spread_qkv_kernel,
        out_shape=jax.ShapeDtypeStruct(padded.shape, jnp.bfloat16),
        grid=(total // block, others),
        in_specs=[
            whole(pq),
            whole(pkv),
            pl.BlockSpec((parts, 1, rows, width), lambda i, s: (i, s, 0, 0)),
            pl.BlockSpec(memory_space=pl.ANY),
        ],
        out_specs=pl.BlockSpec((block, wide), lambda i, s: (i, s + 1)),
        input_output_aliases={3: 0},
        compiler_params=params(),
        cost_estimate=cost(8 * total * width * 512, 20 * total * wide),
    )(pq, pkv, far, padded)


def spread(kernel, meta, own, places, mine, theirs, widths):
    chips, others, rows, width = mine.shape
    total = own.shape[0]
    row_block = lambda m, meta: (meta[0] ^ m, 0)
    piece = pl.BlockSpec((1, others, rows, width), lambda m, meta: (m, 0, 0, 0))
    return pl.pallas_call(
        kernel,
        out_shape=[jax.ShapeDtypeStruct((total, wide), jnp.bfloat16) for wide in widths],
        grid_spec=pltpu.PrefetchScalarGridSpec(
            num_scalar_prefetch=1,
            grid=(chips,),
            in_specs=[pl.BlockSpec((2 * rows, own.shape[1]), row_block)]
            + [whole(place) for place in places]
            + [piece, piece],
            out_specs=[pl.BlockSpec((2 * rows, wide), row_block) for wide in widths],
        ),
        compiler_params=params(),
        cost_estimate=cost(
            8 * total * width * 512, total * (12 * width + 2 * sum(widths))
        ),
    )(meta, own, *places, mine, theirs)


def start_kernel(x_ref, gain_ref, q_ref, k_ref, v_ref, pq_ref, pkv_ref, cos_ref, sin_ref, *outs):
    qkv_ref, normed_ref, pad_ref = outs

    @pl.when(pl.program_id(0) == 0)
    def _():
        split = k_ref.shape[0]
        query = dot32(q_ref[...], pq_ref[...]).astype(jnp.bfloat16)
        key_value = dot32(k_ref[...].T, pkv_ref[:split, :])
        key_value = key_value + dot32(v_ref[...].T, pkv_ref[split:, :])
        store_qkv(pad_ref, slice(None), 0, query, key_value.astype(jnp.bfloat16))

    inputs = x_ref[...].astype(jnp.float32)
    rms = lax.rsqrt(jnp.mean(inputs * inputs, -1, keepdims=True) + norm_eps)
    normed = (inputs * rms * gain_ref[...]).astype(jnp.bfloat16)
    normed_ref[...] = normed
    for kv in range(pad_ref.shape[1] // KV_WIDE):
        at = kv * KV_WIDE
        store_turned(qkv_ref, at, dot32(normed, pad_ref[:, at : at + KV_WIDE]), cos_ref, sin_ref)


def start(tokens, gain, w_query, w_key_t, w_value_t, pq, pkv, cosines, sines):
    total, depth = tokens.shape
    rows = total // CHUNKS
    wide = pq.shape[1] + pkv.shape[1]
    gain = gain[None, :]
    by_rows = lambda width: pl.BlockSpec((rows, width), lambda i: (i, 0))
    arrays = [w_query, w_key_t, w_value_t, pq, pkv]
    shapes = [
        jax.ShapeDtypeStruct((total, 4 * wide), jnp.bfloat16),
        jax.ShapeDtypeStruct((total, depth), jnp.bfloat16),
        jax.ShapeDtypeStruct((depth, 4 * wide), jnp.bfloat16),
    ]
    return pl.pallas_call(
        start_kernel,
        out_shape=shapes,
        grid=(CHUNKS,),
        in_specs=[by_rows(depth), whole(gain)]
        + [whole(array) for array in arrays]
        + [by_rows(LANES), by_rows(LANES)],
        out_specs=[
            by_rows(wide),
            by_rows(depth),
            pl.BlockSpec((depth, wide), lambda i: (0, 0)),
        ],
        compiler_params=params(),
        cost_estimate=cost(2 * total * depth * wide, 12 * total * depth),
    )(tokens, gain, *arrays, cosines, sines)


def turn_kernel(length_ref, cot_ref, normed_ref, dout_ref, dout_t_ref, normed_t_ref):
    rows = cot_ref.shape[0]
    at = pl.program_id(0) * rows + lax.broadcasted_iota(jnp.int32, cot_ref.shape, 0)
    dout = jnp.where(at < length_ref[0], cot_ref[...].astype(jnp.float32), 0.0)
    dout = dout.astype(jnp.bfloat16)
    dout_ref[...] = dout
    dout_t_ref[...] = dout.T
    normed_t_ref[...] = normed_ref[...].T


def turn(length, cotangent, normed):
    total, depth = cotangent.shape
    rows = total // CHUNKS
    by_rows = pl.BlockSpec((rows, depth), lambda i: (i, 0))
    by_columns = pl.BlockSpec((depth, rows), lambda i: (0, i))
    turned = jax.ShapeDtypeStruct((depth, total), jnp.bfloat16)
    return pl.pallas_call(
        turn_kernel,
        out_shape=[jax.ShapeDtypeStruct((total, depth), jnp.bfloat16), turned, turned],
        grid=(CHUNKS,),
        in_specs=[SCALAR, by_rows, by_rows],
        out_specs=[by_rows, by_columns, by_columns],
        compiler_params=params(),
        cost_estimate=cost(total * depth, 10 * total * depth),
    )(length, cotangent, normed)


def project_kernel(x_ref, w_ref, cos_ref, sin_ref, _, out_ref):
    store_turned(out_ref, 0, dot32(x_ref[...], w_ref[...]), cos_ref, sin_ref)


def project(normed, weights, cosines, sines, qkv):
    rows, depth = normed.shape
    width = weights.shape[1]
    steps = width // KV_WIDE
    first = steps // 4
    return pl.pallas_call(
        project_kernel,
        out_shape=jax.ShapeDtypeStruct((rows, width), jnp.bfloat16),
        grid=(steps - first,),
        in_specs=[
            whole(normed),
            pl.BlockSpec((depth, KV_WIDE), lambda i: (0, i + first)),
            whole(cosines),
            whole(sines),
            pl.BlockSpec(memory_space=pl.ANY),
        ],
        out_specs=pl.BlockSpec((rows, KV_WIDE), lambda i: (0, i + first)),
        input_output_aliases={4: 0},
        compiler_params=params(),
        cost_estimate=cost(
            2 * rows * depth * width, 2 * (rows * depth + depth * width + rows * width)
        ),
    )(normed, weights, cosines, sines, qkv)


def attend_kernel(start, length_ref, q_ref, kv_ref, strip_ref, out_ref):
    rows = q_ref.shape[0]
    keys = kv_ref.shape[0]
    length = length_ref[0]
    row_ids = start + lax.broadcasted_iota(jnp.int32, (1, rows), 1)
    limit = jnp.minimum(row_ids, length - 1)
    allowed = lax.broadcasted_iota(jnp.int32, (keys, rows), 0) <= limit
    mixed = []
    sums = []
    for kv in range(kv_ref.shape[1] // KV_WIDE):
        base = kv * KV_WIDE
        at = base + GROUP * LANES
        key = kv_ref[:, at : at + LANES]
        value_t = kv_ref[:, at + LANES : at + 2 * LANES].T
        for g in range(GROUP):
            query = q_ref[:, base + g * LANES : base + (g + 1) * LANES]
            raw = jnp.where(allowed, dot32_nt(key, query), masked_score)
            peak = jnp.max(raw, axis=0, keepdims=True)
            expo = jnp.exp2((raw - peak) * score_scale_log2)
            total = jnp.sum(expo, axis=0, keepdims=True)
            probs = (expo * (1.0 / total)).astype(jnp.bfloat16)
            mixed.append(dot32(value_t, probs).T)
            log_sum = peak * score_scale_log2 + jnp.log2(total)
            sums.append(jnp.where(row_ids < length, log_sum, far_away))
    out_ref[:rows, :] = dot_split(jnp.concatenate(mixed, 1), strip_ref[...])
    out_ref[rows:, :] = jnp.zeros((EXTRA, out_ref.shape[1]), jnp.float32)
    out_ref[rows : rows + len(sums), :rows] = jnp.concatenate(sums, 0)


def attend(length, qkv, strip, index, rows):
    keys = (index + 1) * rows
    width = qkv.shape[1] // 4
    heads = width // KV_WIDE * GROUP
    shape = (rows + EXTRA, strip.shape[1])
    return pl.pallas_call(
        functools.partial(attend_kernel, index * rows),
        out_shape=jax.ShapeDtypeStruct(shape, jnp.float32),
        grid=(1,),
        in_specs=[
            SCALAR,
            pl.BlockSpec((rows, width), lambda i: (index, 0)),
            pl.BlockSpec((keys, width), lambda i: (0, 0)),
            whole(strip),
        ],
        out_specs=pl.BlockSpec(shape, lambda i: (0, 0)),
        compiler_params=params(),
        cost_estimate=cost(
            4 * heads * rows * keys * LANES, 2 * (rows + keys) * width, heads * rows * keys
        ),
    )(length, qkv, qkv, strip)


def forward_kernel(level_ref, part_ref, other_ref, across_ref, outer_ref, *refs):
    x_ref, dout_ref, wo_ref, gain_ref, gate_any, up_any, down_any = refs[:7]
    hidden_ref, normed_t_ref, activ_ref, dgate_ref, dup_ref, mlp_ref, dn_ref = refs[7:14]
    normed_ref, gate_ref, up_ref, down_ref, sems = refs[14:]
    rows = x_ref.shape[0]
    steps, block = down_ref.shape[:2]
    step = pl.program_id(0)

    def fetched(at):
        here = pl.ds(pl.multiple_of(at * block, block), block)
        return [
            pltpu.make_async_copy(gate_any.at[:, here], gate_ref.at[at], sems.at[0, at]),
            pltpu.make_async_copy(up_any.at[:, here], up_ref.at[at], sems.at[1, at]),
            pltpu.make_async_copy(down_any.at[here, :], down_ref.at[at], sems.at[2, at]),
        ]

    @pl.when(step == 0)
    def _():
        for at in range(steps):
            for copy in fetched(at):
                copy.start()
        level = level_ref[0]
        inner = (level == 1) | (level == 2)
        width = part_ref.shape[1]
        second = jnp.where(inner, across_ref[:rows, width:], outer_ref[:rows, :width])
        third = jnp.where(inner, across_ref[:rows, :width], outer_ref[:rows, width:])
        mixed = jnp.concatenate([part_ref[:rows, :], other_ref[:rows, :], second, third], 1)
        hidden = x_ref[...].astype(jnp.float32) + dot32_nt(mixed.astype(jnp.bfloat16), wo_ref[...])
        hidden_ref[...] = hidden
        rms = lax.rsqrt(jnp.mean(hidden * hidden, -1, keepdims=True) + norm_eps)
        normed = (hidden * rms * gain_ref[...]).astype(jnp.bfloat16)
        normed_ref[...] = normed
        normed_t_ref[...] = normed.T
        mlp_ref[...] = jnp.zeros_like(mlp_ref)
        dn_ref[...] = jnp.zeros_like(dn_ref)

    for copy in fetched(step):
        copy.wait()
    wg_ref, wu_ref, wd_ref = gate_ref.at[step], up_ref.at[step], down_ref.at[step]
    normed = normed_ref[...]
    gate = dot32(normed, wg_ref[...])
    up = dot32(normed, wu_ref[...])
    dact = dot32_nt(dout_ref[...], wd_ref[...])
    sigmoid = jax.nn.sigmoid(gate)
    silu = gate * sigmoid
    activ = (silu * up).astype(jnp.bfloat16)
    dgate = (dact * up * sigmoid * (1.0 + gate * (1.0 - sigmoid))).astype(jnp.bfloat16)
    dup = (dact * silu).astype(jnp.bfloat16)
    activ_ref[...] = activ
    dgate_ref[...] = dgate
    dup_ref[...] = dup
    mlp_ref[...] += dot32(activ, wd_ref[...])
    dn_ref[:rows, :] += dot32_nt(dgate, wg_ref[...]) + dot32_nt(dup, wu_ref[...])


def forward_chunk(level, gathered, tokens, dout, w_out, gain, w_gate, w_up, w_down, index, rows):
    depth = tokens.shape[1]
    units = w_gate.shape[1]
    block = 512
    own_rows = pl.BlockSpec((rows, depth), lambda i: (index, 0))
    steps = units // block
    gain = gain[None, :]
    f32, bf16 = jnp.float32, jnp.bfloat16
    outs = [
        jax.ShapeDtypeStruct((rows, depth), f32),
        jax.ShapeDtypeStruct((depth, rows), bf16),
        jax.ShapeDtypeStruct((rows, units), bf16),
        jax.ShapeDtypeStruct((rows, units), bf16),
        jax.ShapeDtypeStruct((rows, units), bf16),
        jax.ShapeDtypeStruct((rows, depth), f32),
        jax.ShapeDtypeStruct((rows + EXTRA, depth), f32),
    ]
    unit_out = pl.BlockSpec((rows, block), lambda i: (0, i))
    return pl.pallas_call(
        forward_kernel,
        out_shape=outs,
        grid=(steps,),
        in_specs=[SCALAR]
        + [whole(array) for array in gathered]
        + [own_rows, own_rows, whole(w_out), whole(gain)]
        + [ANYWHERE] * 3,
        out_specs=[
            whole(outs[0]),
            whole(outs[1]),
            unit_out,
            unit_out,
            unit_out,
            whole(outs[5]),
            whole(outs[6]),
        ],
        scratch_shapes=[
            pltpu.VMEM((rows, depth), bf16),
            pltpu.VMEM((steps, depth, block), bf16),
            pltpu.VMEM((steps, depth, block), bf16),
            pltpu.VMEM((steps, block, depth), bf16),
            pltpu.SemaphoreType.DMA((3, steps)),
        ],
        compiler_params=params(),
        cost_estimate=cost(
            2 * rows * depth * (6 * units + w_out.shape[1]),
            2 * depth * (3 * units + w_out.shape[1]) + 22 * rows * depth,
            rows * units,
        ),
    )(level, *gathered, tokens, dout, w_out, gain, w_gate, w_up, w_down)


def hidden_grad(inner, total_ref, final_ref, hidden_ref, dout_ref, gain_ref):
    dnormed = jnp.where(inner, total_ref[...], final_ref[...])
    hidden = hidden_ref[...]
    rms = lax.rsqrt(jnp.mean(hidden * hidden, -1, keepdims=True) + norm_eps)
    scaled = dnormed * gain_ref[...]
    shift = jnp.mean(scaled * hidden, -1, keepdims=True)
    dhid = dout_ref[...].astype(jnp.float32) + (rms * scaled - hidden * (rms**3 * shift))
    return dhid, dnormed * (hidden * rms)


def backward_kernel(
    start, full, adding, steps, level_ref, total_ref, final_ref, hidden_ref, dout_ref, *refs
):
    gain_two_ref, wo_ref, q_ref = refs[:3]
    kv_here = q_ref.shape[1] // KV_WIDE
    refs = refs[3:]
    kv_refs, refs = refs[: 2 * kv_here], refs[2 * kv_here :]
    part_ref, place_ref, strip_ref, cos_ref, sin_ref = refs[:5]
    extra = (2 if full else 0) + (1 if adding else 0) + 1
    outs, scratch = refs[5 : -3 - extra], refs[-3 - extra :]
    dhid_ref, low_ref, dn_ref, sems = scratch[:4]
    if full:
        x_any, gain_one_ref, other_ref, across_ref, outer_ref, w_any = outs[:6]
        outs = outs[6:]
        x_ref, w_buffers = scratch[4:6]
        tokens_here = pltpu.make_async_copy(
            x_any.at[pl.ds(start, x_ref.shape[0]), :], x_ref, sems.at[4]
        )
    count = (5 if start > 0 else 4) if full else 2
    if adding:
        acc_any, acc_buffers = outs[0], scratch[-1]
    outs = outs[-count:]
    dhid_t_ref, dqkv_ref = outs[:2]
    if full:
        input_grad_ref, gains_ref = outs[2:4]
    rows = q_ref.shape[0]
    keys = kv_refs[0].shape[0]
    shard = pl.program_id(0)
    level = level_ref[0]
    inner = (level == 1) | (level == 2)

    def fetched(at, sums):
        source, buffers = (acc_any, acc_buffers) if sums else (w_any, w_buffers)
        lanes = buffers.shape[2]
        here = pl.ds(pl.multiple_of(at * lanes, lanes), lanes)
        slot = at % 2
        sem = sems.at[slot + 2] if sums else sems.at[slot]
        return pltpu.make_async_copy(source.at[:, here], buffers.at[slot], sem)

    def fetch(at):
        if adding:
            fetched(at, True).start()
        if full:
            fetched(at, False).start()

    @pl.when(shard == 0)
    def _():
        for at in range(min(2, steps)):
            fetch(at)
        if full:
            tokens_here.start()
        dhid, dgain = hidden_grad(
            inner, total_ref, final_ref, hidden_ref, dout_ref, gain_two_ref
        )
        dhid_ref[...] = dhid
        low = dhid.astype(jnp.bfloat16)
        low_ref[...] = low
        dhid_t_ref[...] = low.T
        if full:
            gains_ref[...] = jnp.zeros_like(gains_ref)
            gains_ref[1:2, :] = jnp.sum(dgain, 0, keepdims=True)
            dn_ref[...] = jnp.zeros_like(dn_ref)

    def rotate_back(grads):
        turned = grads * cos_ref[...] - pltpu.roll(grads, LANES // 2, 1) * sin_ref[...]
        return turned.astype(jnp.bfloat16)

    dmixed_all = dot32(low_ref[...], wo_ref[...]).astype(jnp.bfloat16)
    mixed = part_ref[...]
    if full:
        far = jnp.where(inner, across_ref[...], outer_ref[...])
        far = jnp.where(shard == 1, other_ref[...], far)
        mixed = jnp.where(shard == 0, mixed, far)
    products = dmixed_all.astype(jnp.float32) * dot_split(mixed[:rows], place_ref[...])
    causal = lax.broadcasted_iota(jnp.int32, (rows, rows), 0) <= lax.broadcasted_iota(
        jnp.int32, (rows, rows), 1
    )
    acc_ref = None
    if adding:
        fetched(shard, True).wait()
        acc_ref = acc_buffers.at[shard % 2]
    grads = []
    for kv in range(kv_here):
        key_ref, value_ref = kv_refs[2 * kv : 2 * kv + 2]
        heads = range(kv * GROUP, (kv + 1) * GROUP)
        lanes = {h: slice(h * LANES, (h + 1) * LANES) for h in heads}
        row_dots = {h: jnp.sum(products[:, lanes[h]].T, axis=0, keepdims=True) for h in heads}
        log_sums = {h: mixed[rows + h : rows + h + 1, :rows] for h in heads}
        dqueries = dict.fromkeys(heads)
        here = slice(2 * kv * LANES, (2 * kv + 1) * LANES)
        there = slice((2 * kv + 1) * LANES, (2 * kv + 2) * LANES)
        for tile in range(keys // rows):
            span = slice(tile * rows, (tile + 1) * rows)
            key = key_ref[span, :]
            value = value_ref[span, :]
            key_t = key.T
            dkey = None if acc_ref is None else acc_ref[span, here]
            dvalue = None if acc_ref is None else acc_ref[span, there]
            last = tile * rows == start
            for h in heads:
                at = kv * KV_WIDE + (h % GROUP) * LANES
                query = q_ref[:, at : at + LANES]
                dmixed = dmixed_all[:, lanes[h]]
                raw = dot32_nt(key, query)
                probs = jnp.exp2(raw * score_scale_log2 - log_sums[h])
                if last:
                    probs = jnp.where(causal, probs, 0.0)
                dprobs = dot32_nt(value, dmixed)
                dscores = (probs * (dprobs - row_dots[h])).astype(jnp.bfloat16)
                dquery = dot32(key_t, dscores)
                dqueries[h] = dquery if dqueries[h] is None else dqueries[h] + dquery
                dkey_one = dot32(dscores, query)
                dvalue_one = dot32(probs.astype(jnp.bfloat16), dmixed)
                dkey = dkey_one if dkey is None else dkey + dkey_one
                dvalue = dvalue_one if dvalue is None else dvalue + dvalue_one
            if full and not last:
                outs[4][span, here] = dkey
                outs[4][span, there] = dvalue
        grads += [rotate_back(dqueries[h].T * score_scale) for h in heads]
        grads.append(rotate_back(dkey * score_scale))
        grads.append(dvalue.astype(jnp.bfloat16))
    grads = jnp.concatenate(grads, 1)
    if full:
        fetched(shard, False).wait()
        dn_ref[...] += dot32_nt(grads, w_buffers[shard % 2])

        @pl.when(shard + 2 < steps)
        def _():
            fetch(shard + 2)

    @pl.when(shard == 0)
    def _():
        wide = strip_ref.shape[1]
        for kv in range(kv_here):
            dqkv_ref[:, kv * wide : (kv + 1) * wide] = dot32(
                grads[:, kv * KV_WIDE : (kv + 1) * KV_WIDE], strip_ref[...]
            ).astype(jnp.bfloat16)

    if not full:
        return

    @pl.when(shard == pl.num_programs(0) - 1)
    def _():
        tokens_here.wait()
        dnormed = dn_ref[...]
        inputs = x_ref[...].astype(jnp.float32)
        rms = lax.rsqrt(jnp.mean(inputs * inputs, -1, keepdims=True) + norm_eps)
        scaled = dnormed * gain_one_ref[...]
        shift = jnp.mean(scaled * inputs, -1, keepdims=True)
        grad = dhid_ref[...] + (rms * scaled - inputs * (rms**3 * shift))
        input_grad_ref[...] = grad.astype(jnp.bfloat16)
        gains_ref[0:1, :] = jnp.sum(dnormed * (inputs * rms), 0, keepdims=True)


def backward_chunk(
    level, sums_two, hidden, dout, tokens, gains, weights, qkv, gathered, places, tables, acc,
    index, rows, full=True, grad_into=None
):
    start = index * rows
    keys = start + rows
    depth = tokens.shape[1]
    out_pad, qkv_pad = weights
    place_out, strip = places
    far_rows, width = gathered[0].shape
    out_wide = place_out.shape[1]
    kv_here = out_wide // (GROUP * LANES)
    wide = kv_here * KV_WIDE
    levels = qkv.shape[1] // wide
    own_rows = pl.BlockSpec((rows, depth), lambda t: (index, 0))
    table = pl.BlockSpec((rows, LANES), lambda t: (index, 0))
    gains = [gain[None, :] for gain in gains]
    key_value = lambda at: pl.BlockSpec(
        (keys, LANES), lambda t: (0, (wide // LANES) * t + at)
    )
    across = pl.BlockSpec((far_rows, width), lambda t: (0, jnp.where(t == 2, 1, 0)))
    outer = pl.BlockSpec((far_rows, width), lambda t: (0, jnp.where(t == 3, 1, 0)))
    in_specs = [
        SCALAR,
        whole(hidden),
        whole(hidden),
        whole(hidden),
        own_rows,
        whole(gains[1]),
        pl.BlockSpec((depth, out_wide), lambda t: (0, t)),
        pl.BlockSpec((rows, wide), lambda t: (index, t)),
    ]
    for kv in range(kv_here):
        at = kv * (KV_WIDE // LANES) + GROUP
        in_specs += [key_value(at), key_value(at + 1)]
    in_specs += [
        whole(gathered[0]),
        whole(place_out),
        whole(strip),
        table,
        table,
    ]
    args = [level, *sums_two, hidden, dout, gains[1], out_pad]
    args += [qkv] * (1 + 2 * kv_here)
    args += [gathered[0], place_out, strip, *tables]
    sums_wide = 2 * kv_here * LANES
    if full:
        in_specs += [ANYWHERE, whole(gains[0]), whole(gathered[1]), across, outer]
        in_specs.append(ANYWHERE)
        args += [tokens, gains[0], *gathered[1:], qkv_pad]
    if acc is not None:
        in_specs.append(ANYWHERE)
        args.append(acc)
    f32, bf16 = jnp.float32, jnp.bfloat16
    outs = [
        jax.ShapeDtypeStruct((depth, rows), bf16),
        jax.ShapeDtypeStruct((rows, kv_here * strip.shape[1]), bf16),
        jax.ShapeDtypeStruct(tokens.shape, bf16),
        jax.ShapeDtypeStruct((8, depth), f32),
    ]
    outs = outs if full else outs[:2]
    out_specs = [whole(out) for out in outs]
    aliases = {}
    if full:
        out_specs[2] = own_rows
        if grad_into is not None:
            aliases = {len(args): 2}
            in_specs.append(ANYWHERE)
            args.append(grad_into)
    if full and start > 0:
        outs.append(jax.ShapeDtypeStruct((start, levels * sums_wide), f32))
        out_specs.append(pl.BlockSpec((start, sums_wide), lambda t: (0, t)))
    steps = levels if full else 1
    scratch = [
        pltpu.VMEM((rows, depth), f32),
        pltpu.VMEM((rows, depth), bf16),
        pltpu.VMEM((rows, depth), f32),
        pltpu.SemaphoreType.DMA((5,)),
    ]
    if full:
        scratch += [pltpu.VMEM((rows, depth), bf16), pltpu.VMEM((2, depth, wide), bf16)]
    if acc is not None:
        scratch.append(pltpu.VMEM((min(2, steps), keys, sums_wide), f32))
    results = pl.pallas_call(
        functools.partial(backward_kernel, start, full, acc is not None, steps),
        out_shape=outs,
        grid=(steps,),
        input_output_aliases=aliases,
        in_specs=in_specs,
        out_specs=out_specs,
        scratch_shapes=scratch,
        compiler_params=params(),
        cost_estimate=cost(
            levels * rows * (20 * kv_here * keys * LANES + 2 * depth * (out_wide + wide)),
            2 * depth * levels * (out_wide + wide) + 16 * rows * depth,
            levels * kv_here * GROUP * rows * keys,
        ),
    )(*args)
    return results[:4], (results[4] if full and start > 0 else None)


def rows_kernel(lefts, groups, adding, picked, together, side_ref, *refs):
    refs = list(refs)
    held_ref = refs.pop()
    out_refs = refs[-len(picked) :]
    refs = refs[: -len(picked)]
    recv_ref = refs.pop() if adding else None
    step = pl.program_id(0)
    left_refs = []
    for count in lefts:
        left_refs.append(refs[:count])
        refs = refs[count:]
    rights = []
    for _ in groups:
        rights.append(refs[:CHUNKS])
        refs = refs[CHUNKS:]
    rows = left_refs[0][0].shape[0]
    blocks = held_ref.shape[1] // rows

    @pl.when(step == 0)
    def _():
        for which, pieces in enumerate(left_refs):
            for n, ref in enumerate(pieces):
                m, j = n % blocks, n // blocks
                wide = ref.shape[1]
                held_ref[which, m * rows : (m + 1) * rows, j * wide : (j + 1) * wide] = ref[...]

    chunk = held_ref.shape[2] // CHUNKS
    whole_columns = slice(0, out_refs[0].shape[1])

    def give(group, left, columns):
        right = jnp.concatenate([ref[:chunk, :].astype(jnp.bfloat16) for ref in group], 0)
        total = dot32(held_ref[left], right)
        if recv_ref is not None:
            total = total + recv_ref[:, columns]
        for out_ref, parts in zip(out_refs, picked):
            at = 0
            for start, size in parts:
                out_ref[at : at + size, columns] = total[start : start + size]
                at += size

    begin = 0
    for group, (left, first, steps) in zip(rights, groups):
        if together:
            width = group[0].shape[1]
            give(group, left, slice(begin, begin + width))
            begin += width
        else:

            @pl.when((step >= first) & (step < first + steps))
            def _(group=group, left=left):
                give(group, left, whole_columns)


def rows_of(lefts, groups, side, rows, blocks, step, recv=None, picked=None):
    if picked is None:
        picked = [[(0, rows * blocks)]]
    at = lambda m: lambda i, side: ((m ^ side[2]) * side[1] + side[0], 0)
    specs = []
    args = []
    counts = []
    for left in lefts:
        pieces = left if isinstance(left, list) else [left]
        counts.append(len(pieces) * blocks)
        for piece in pieces:
            for m in range(blocks):
                specs.append(pl.BlockSpec((rows, piece.shape[1]), at(m)))
                args.append(piece)
    tokens = sum(piece.shape[1] for piece in pieces)
    first = 0
    plan = []
    together = step is None
    for which, rights in groups:
        if together:
            plan.append((which, 0, 1))
            specs += [whole(right) for right in rights]
            args += rights
            first += rights[0].shape[1]
            continue
        steps = rights[0].shape[1] // step
        plan.append((which, first, steps))
        for right in rights:
            pick = lambda i, side, first=first, steps=steps: (0, jnp.clip(i - first, 0, steps - 1))
            specs.append(pl.BlockSpec((right.shape[0], step), pick))
            args.append(right)
        first += steps
    if together:
        first, step = 1, first
    total = first * step
    block = lambda height: pl.BlockSpec((height, step), lambda i, side: (0, i))
    if recv is not None:
        specs.append(block(rows * blocks))
        args.append(recv)
    heights = [sum(size for _, size in parts) for parts in picked]
    results = pl.pallas_call(
        functools.partial(rows_kernel, counts, plan, recv is not None, picked, together),
        out_shape=[jax.ShapeDtypeStruct((height, total), jnp.float32) for height in heights],
        grid_spec=pltpu.PrefetchScalarGridSpec(
            num_scalar_prefetch=1,
            grid=(first,),
            in_specs=specs,
            out_specs=[block(height) for height in heights],
            scratch_shapes=[pltpu.VMEM((len(lefts), rows * blocks, tokens), jnp.bfloat16)],
        ),
        compiler_params=params(),
        cost_estimate=cost(
            2 * rows * blocks * tokens * total,
            4 * rows * blocks * total + 2 * tokens * (total + rows * blocks),
        ),
    )(side, *args)
    return results[0] if len(picked) == 1 else results


def finish_kernel(*refs):
    query_ref, key_ref, value_ref, out_ref = refs[4:]
    kv_here = key_ref.shape[1] // HD
    q_cols = out_ref.shape[1]
    for at in range(2):
        kept_ref, far_ref = refs[2 * at : 2 * at + 2]
        half = far_ref.shape[0]
        sums = kept_ref[...] + far_ref[...]
        here = slice(at * half, (at + 1) * half)
        out_ref[here, :] = sums[:, :q_cols]
        start = q_cols
        cut = [[], [], []]
        for kv in range(kv_here):
            for i, width in enumerate((GROUP * HD, HD, HD)):
                cut[i].append(sums[:, start : start + width])
                start += width
        for ref, pieces in zip((query_ref, key_ref, value_ref), cut):
            ref[here, :] = jnp.concatenate(pieces, 1)


def finish(one, far_one, two, far_two, kv_here):
    half, columns = far_one.shape
    first = pl.BlockSpec((half, columns), lambda i: (0, 0))
    q_cols = kv_here * GROUP * HD
    outs = [
        jax.ShapeDtypeStruct((2 * half, width), jnp.float32)
        for width in (q_cols, kv_here * HD, kv_here * HD, q_cols)
    ]
    return pl.pallas_call(
        finish_kernel,
        out_shape=outs,
        grid=(1,),
        in_specs=[first] * 4,
        out_specs=[whole(out) for out in outs],
        compiler_params=params(),
        cost_estimate=cost(4 * half * columns, 32 * half * columns),
    )(one, far_one, two, far_two)


def shards(
    tokens,
    lengths,
    positions,
    cotangent,
    norm_gain,
    w_query,
    w_key,
    w_value,
    w_out,
    mlp_gain,
    w_gate,
    w_up,
    w_down,
):
    seq_rows, depth = tokens.shape
    chips = lax.axis_size("chip")
    dp = chips * 2
    tp = lax.axis_size("tp")
    chip = lax.axis_index("chip")
    core = lax.axis_index("core")
    level = lax.axis_index("tp")
    low = level < 2
    inner = (level == 1) | (level == 2)
    heads_here = w_query.shape[1] // HD
    kv_here = w_key.shape[1] // HD
    rows = seq_rows // CHUNKS
    slice_rows = depth // dp
    level_ref = level.astype(jnp.int32).reshape(1)
    by_hand = dp == 8
    swap = lambda array: lax.ppermute(array, "core", [(0, 1), (1, 0)])
    to_level = lambda array, s: along(array, [(t, t ^ s) for t in range(tp)])

    at_row = (chip * 2 + core) * slice_rows
    cols = lambda w: lax.dynamic_slice_in_dim(w, at_row, slice_rows, 1).astype(jnp.float32).T
    (out_slice,) = fence(cols(w_out))
    qkv_slice = jnp.concatenate(
        [
            lax.dynamic_slice_in_dim(w_query, at_row, slice_rows, 0).astype(jnp.float32),
            cols(w_key.T),
            cols(w_value.T),
        ],
        1,
    )
    out_slice, qkv_slice = fence(out_slice, qkv_slice)
    out_near = along(out_slice, PAIRS)
    qkv_near = along(qkv_slice, PAIRS)
    meta = jnp.stack([chip, core]).astype(jnp.int32)

    pq = place_query(heads_here)
    pkv = place_key_value(kv_here)
    p_all = place_all(heads_here, kv_here)
    strip_one = place_all(GROUP, 1).T
    p_out = place_plain(heads_here)
    strip_out = p_out.T

    half_dim = HD // 2
    freqs = rope_base ** (-(jnp.arange(half_dim).astype(jnp.float32) * 2.0 / HD))
    freqs = jnp.pad(freqs, (0, LANES // 2 - half_dim))
    angles = positions.astype(jnp.float32)[:, None] * jnp.concatenate([freqs, freqs])[None, :]
    cosines = jnp.cos(angles)
    sines = jnp.sin(angles) * jnp.where(jnp.arange(LANES) < LANES // 2, -1.0, 1.0)

    cosines, sines, out_near = fence(cosines, sines, out_near)
    out_across = along(jnp.stack([out_slice, out_near]), MIDDLE)
    qkv_own, normed_one, own_pad = start(
        tokens, norm_gain, w_query, w_key.T, w_value.T, pq, pkv, cosines, sines
    )

    def far_slices(near, across, outer):
        return jnp.stack(
            [
                near,
                jnp.where(inner, across[1], outer[0]),
                jnp.where(inner, across[0], outer[1]),
            ]
        )

    order = list(reversed(range(CHUNKS)))
    c0, c1, c2, c3 = order
    own, other, across, outer = {}, {}, {}, {}
    part, total, final = {}, {}, {}

    def hop_1(j):
        other[j] = along(own[j], PAIRS)

    def hop_2(j):
        across[j] = along(jnp.concatenate([own[j], other[j]], 1), MIDDLE)

    def hop_3(j):
        outer[j] = along(across[j], OUTWARD)

    coming = {}

    def add_1(j):
        coming[j] = along(part[j], INWARD)

    def add_2(j):
        total[j] = part[j][:rows] + coming[j][:rows]
        coming[j] = along(total[j], MIDDLE)

    def add_3(j, inward, extra=0):
        both = jnp.where(inner, total[j] + coming[j], inward)
        total[j] = jnp.pad(both, ((0, extra), (0, 0)))
        final[j] = along(total[j], PAIRS)
        return final[j]

    def to_chip(array, m):
        return lax.ppermute(array, "chip", [(i, i ^ m) for i in range(chips)])

    def over_chips_1(piece):
        cut = piece.shape[1] // 2
        one, two = piece[:, :cut], piece[:, cut:]
        return jnp.stack([one, to_chip(one, 1)]), jnp.stack([two, to_chip(two, 2)])

    def over_chips_2(one, two):
        return one, to_chip(one, 2), two, to_chip(two, 1)

    def over_chips_3(one, one_far, two, two_far):
        upper = jnp.stack([one[0], one[1], one_far[0], one_far[1]])
        lower = jnp.stack([two[0], two_far[0], two[1], two_far[1]])
        return jnp.concatenate([upper, lower], 2)

    qkv_own, out_across, qkv_near = fence(qkv_own, out_across, qkv_near)
    out_outer = along(out_across, OUTWARD)
    qkv_across = along(jnp.stack([qkv_slice, qkv_near]), MIDDLE)
    own[c0] = attend(lengths, qkv_own, strip_out, c0, rows)
    own[c1] = attend(lengths, qkv_own, strip_out, c1, rows)
    own, qkv_own, out_outer = fence(own, qkv_own, out_outer)
    others = along(jnp.concatenate([own[c0], own[c1]], 0), PAIRS)
    out_far = far_slices(out_near, out_across, out_outer)
    out_mine = over_chips_1(out_far) if by_hand else out_far
    own[c2] = attend(lengths, qkv_own, strip_out, c2, rows)
    own[c3] = attend(lengths, qkv_own, strip_out, c3, rows)
    own[c3], qkv_across = fence(own[c3], qkv_across)
    qkv_outer = along(qkv_across, OUTWARD)
    own, others, normed_one, w_out, out_mine = fence(own, others, normed_one, w_out, out_mine)
    other[c0], other[c1] = others[: rows + EXTRA], others[rows + EXTRA :]
    if by_hand:
        out_mine = over_chips_2(*out_mine)
    else:
        out_mine = lax.all_gather(out_mine, ("chip", "core"))
    hop_2(c0)
    dout, dout_t, normed_one_t = turn(lengths, cotangent, normed_one)
    w_out_t = w_out.T
    own, other, across, dout, dout_t, normed_one_t, w_out_t, out_mine, qkv_outer = fence(
        own, other, across, dout, dout_t, normed_one_t, w_out_t, out_mine, qkv_outer
    )
    hop_1(c2)
    hop_3(c0)
    hop_2(c1)
    qkv_far = lax.all_gather(far_slices(qkv_near, qkv_across, qkv_outer), ("chip", "core"))
    if by_hand:
        out_mine = over_chips_3(*out_mine)
        out_theirs = swap(out_mine)
        out_pad, out_plain = spread(
            spread_out_kernel,
            meta,
            w_out_t,
            [p_out],
            out_mine,
            out_theirs,
            [4 * p_out.shape[1], 4 * p_out.shape[0]],
        )
    else:
        plain = [w_out_t] + [
            out_mine[:, s].reshape(depth, -1).astype(jnp.bfloat16) for s in range(tp - 1)
        ]
        out_plain = jnp.concatenate(plain, 1)
        out_pad = jnp.concatenate([dot32(w, p_out).astype(jnp.bfloat16) for w in plain], 1)
    hidden, normed_t, activ, dgate, dup, mlp_part = {}, {}, {}, {}, {}, {}

    def feed(j):
        gathered = (own[j], other[j], across[j], outer[j])
        (hidden[j], normed_t[j], activ[j], dgate[j], dup[j], mlp_part[j], part[j]) = forward_chunk(
            level_ref, gathered, tokens, dout, out_plain, mlp_gain, w_gate, w_up, w_down, j, rows
        )

    own, other, across, outer, out_pad, out_plain = fence(
        own, other, across, outer, out_pad, out_plain
    )
    hop_1(c3)
    hop_3(c1)
    hop_2(c2)
    feed(c0)
    part, other = fence(part, other)
    add_1(c0)
    own, other, across, outer, part, hidden = fence(own, other, across, outer, part, hidden)
    hop_3(c2)
    hop_2(c3)
    feed(c1)
    qkv_far, hidden[c1] = fence(qkv_far, hidden[c1])
    qkv_pad = spread_qkv(own_pad, pq, pkv, qkv_far)
    own, other, across, outer, part, total, coming, hidden, qkv_pad = fence(
        own, other, across, outer, part, total, coming, hidden, qkv_pad
    )
    add_1(c1)
    hop_3(c3)
    add_2(c0)
    feed(c2)
    qkv_pad, hidden[c2] = fence(qkv_pad, hidden[c2])
    qkv = project(normed_one, qkv_pad, cosines, sines, qkv_own)
    own, other, across, outer, part, total, coming, hidden, qkv = fence(
        own, other, across, outer, part, total, coming, hidden, qkv
    )
    coming[c2] = add_3(c0, part[c2][:rows])
    add_2(c1)
    feed(c3)

    listed = lambda pieces: [pieces[j] for j in range(CHUNKS)]
    keep_side = jnp.stack([core, 2, 0]).astype(jnp.int32)
    keep_turned = jnp.stack([core, 2, chip]).astype(jnp.int32)
    send_side = jnp.stack([1 - core, 2, 0]).astype(jnp.int32)
    send_turned = jnp.stack([1 - core, 2, chip]).astype(jnp.int32)
    all_rows = jnp.array([0, 1, 0], jnp.int32)

    def send_rows(lefts, groups, step, side=send_side):
        if not by_hand:
            return rows_of(lefts, groups, all_rows, depth // 4, 4, step)
        return rows_of(lefts, groups, side, slice_rows, chips, step)

    def keep_rows(lefts, groups, received, step, side=keep_side, picked=None):
        if not by_hand:
            return received
        return rows_of(lefts, groups, side, slice_rows, chips, step, received, picked)

    def swap_rows(array):
        return swap(array) if by_hand else array

    def scatter(array, axes):
        return lax.psum_scatter(array, axes, scatter_dimension=0, tiled=True)

    units = w_gate.shape[1]
    mlp_args = (
        [listed(normed_t), dout_t],
        [(0, listed(dgate)), (0, listed(dup)), (1, listed(activ))],
    )
    acc = None
    input_grad = None
    dhid_t, dqkv_own, gains = {}, {}, {}

    def back(j):
        nonlocal acc, input_grad
        (dhid_t[j], dqkv_own[j], input_grad, gains[j]), acc = back_some(j, True)

    def back_own(j):
        return back_some(j, False)[0]

    def back_some(j, full):
        return backward_chunk(
            level_ref,
            (total[j], final[j]),
            hidden[j],
            dout,
            tokens,
            (norm_gain, mlp_gain),
            (out_pad, qkv_pad),
            qkv,
            (own[j], other[j], across[j], outer[j]),
            (p_out, strip_one),
            (cosines, sines),
            acc,
            j,
            rows,
            full,
            input_grad,
        )

    grad_mlp = rows_of(*mlp_args, all_rows, depth // 4, 4, units // 2)
    own, other, across, outer, part, total, coming, final, hidden, grad_mlp = fence(
        own, other, across, outer, part, total, coming, final, hidden, grad_mlp
    )
    grad_mlp = scatter(grad_mlp, ("chip", "core"))
    coming[c3] = add_3(c1, part[c3][:rows])
    add_2(c2)
    back(c0)

    near = lambda: jnp.where(low, mlp_part[1], mlp_part[2])
    edge = lambda: jnp.where(low, mlp_part[0], mlp_part[3])
    leave_far = lambda: jnp.where(low, mlp_part[3], mlp_part[0])
    leave_near = lambda: jnp.where(low, mlp_part[2], mlp_part[1])
    total, coming, final, hidden, mlp_part, acc, dhid_t = fence(
        total, coming, final, hidden, mlp_part, acc, dhid_t
    )
    far_sum = add_3(c2, leave_far())
    add_2(c3)
    back(c1)
    total, coming, final, hidden, mlp_part, far_sum, acc, dhid_t = fence(
        total, coming, final, hidden, mlp_part, far_sum, acc, dhid_t
    )
    add_3(c3, leave_near(), EXTRA)
    far_in = along(leave_far() + far_sum, MIDDLE)
    back(c2)
    total, final, hidden, acc, dhid_t = fence(total, final, hidden, acc, dhid_t)
    dhid_t[c3], dqkv_own[c3] = back_own(c3)
    dhid_t, dqkv_own, far_in, mlp_part, final = fence(
        dhid_t, dqkv_own, far_in, mlp_part, final
    )
    last = along(jnp.where(inner, edge() + far_in, near()), PAIRS)
    near_in = along(leave_near() + final[c3][:rows], MIDDLE)
    q_cols = heads_here * HD
    attn_args = (
        [listed(dhid_t), normed_one_t],
        [(0, listed(own)), (1, listed(dqkv_own))],
    )
    sent = swap_rows(send_rows(*attn_args, None, send_turned))
    total, final, hidden, acc, sent = fence(total, final, hidden, acc, sent)
    if by_hand:
        half = slice_rows // 2
        upper = lambda m: (m * slice_rows, half)
        lower = lambda m: (m * slice_rows + half, half)
        picked = [
            [upper(1), upper(3)],
            [upper(0), upper(2)],
            [lower(2), lower(3)],
            [lower(0), lower(1)],
        ]
        pieces = keep_rows(*attn_args, sent, None, keep_turned, picked)
        pieces, hidden = fence(pieces, hidden)
        one_away, one, two_away, two = pieces
        pieces = (one, to_chip(one_away, 1), two, to_chip(two_away, 2))
    else:
        pieces = scatter(sent, ("chip", "core"))
    back(c3)
    pieces, gains, input_grad = fence(pieces, gains, input_grad)
    gain_sums = gains[0] + gains[1] + gains[2] + gains[3]
    gain_sums = gain_sums + swap(gain_sums)
    gain_sums, last, near_in = fence(gain_sums, last, near_in)
    mlp_rows = jnp.where(inner, near() + near_in, edge()) + last
    hidden_rows = jnp.where(
        low,
        jnp.where(level == 0, hidden[0], hidden[1]),
        jnp.where(level == 2, hidden[2], hidden[3]),
    )
    layer_out = (hidden_rows + mlp_rows).astype(jnp.bfloat16)
    mlp_grads = [grad_mlp[:, at * units : (at + 1) * units] for at in range(3)]
    if by_hand:
        one = pieces[0] + pieces[1]
        two = pieces[2] + pieces[3]
        far_one = to_chip(one[half:], 2)
        far_two = to_chip(two[half:], 1)
        others = [to_chip(gain_sums, m) for m in range(1, chips)]
        far_one, far_two, mlp_grads, layer_out = fence(far_one, far_two, mlp_grads, layer_out)
        attn_grads = finish(one, far_one, two, far_two, kv_here)
        others, attn_grads = fence(others, attn_grads)
        gain_sums = sum(others, gain_sums)
    else:
        gain_sums = lax.psum(gain_sums, "chip")
        grad_qkv = pieces[:, q_cols:]
        one = strip_one.shape[1]
        picked = lambda at, width: jnp.concatenate(
            [grad_qkv[:, kv * one + at : kv * one + at + width] for kv in range(kv_here)], 1
        )
        attn_grads = (
            picked(0, GROUP * HD),
            picked(GROUP * HD, HD),
            picked((GROUP + 1) * HD, HD),
            pieces[:, :q_cols],
        )
    gain_rows = lax.dynamic_slice_in_dim(gain_sums, at_row, slice_rows, 1)
    grad_query, grad_key, grad_value, grad_out_t = attn_grads
    return (
        layer_out,
        input_grad,
        gain_rows[0],
        grad_query,
        grad_key,
        grad_value,
        grad_out_t.T,
        gain_rows[1],
        mlp_grads[0],
        mlp_grads[1],
        mlp_grads[2].T,
    )


def solution(mesh):
    devices = mesh.devices
    dp, tp = devices.shape
    split = Mesh(devices.reshape(dp // 2, 2, tp), ("chip", "core", "tp"))
    data = ("chip", "core")
    return jax.shard_map(
        shards,
        mesh=split,
        in_specs=(
            P(data, None),
            P(data),
            P(data),
            P(data, None),
            P(),
            P(None, "tp"),
            P(None, "tp"),
            P(None, "tp"),
            P("tp", None),
            P(),
            P(None, "tp"),
            P(None, "tp"),
            P("tp", None),
        ),
        out_specs=(
            P(("chip", "core", "tp"), None),
            P(data, None),
            P(data),
            P(data, "tp"),
            P(data, "tp"),
            P(data, "tp"),
            P("tp", data),
            P(data),
            P(data, "tp"),
            P(data, "tp"),
            P("tp", data),
        ),
        check_vma=False,
    )
```

```python
import functools

import jax
import jax.numpy as jnp
from jax import lax
from jax.experimental import pallas as pl
from jax.experimental.pallas import tpu as pltpu
from jax.sharding import Mesh
from jax.sharding import PartitionSpec as P

HD = 96
LANES = 128
GROUP = 2
KV_WIDE = (GROUP + 2) * LANES
rope_base = 100000.0
norm_eps = 1e-05
masked_score = -1e30
far_away = 1e30
score_scale = HD ** (-0.5)
score_scale_log2 = score_scale * 1.4426950408889634
CHUNKS = 4
EXTRA = 8
VMEM_BYTES = 56 * 1024 * 1024
LATE_VMEM_BYTES = 40 * 1024 * 1024
NT = (((1,), (1,)), ((), ()))


def params(vmem=VMEM_BYTES):
    return pltpu.CompilerParams(vmem_limit_bytes=vmem)


def cost(flops, moved, exps=0):
    return pl.CostEstimate(
        flops=flops // 1024, bytes_accessed=moved // 1024, transcendentals=exps // 1024
    )


def dot32(a, b):
    return jnp.dot(a, b, preferred_element_type=jnp.float32)


def dot32_nt(a, b):
    return lax.dot_general(a, b, NT, preferred_element_type=jnp.float32)


def dot_split(a, places):
    high = a.astype(jnp.bfloat16)
    rest = (a - high.astype(jnp.float32)).astype(jnp.bfloat16)
    return dot32(high, places) + dot32(rest, places)


def fence(*trees):
    return lax.optimization_barrier(trees)


def whole(array, buffers=None):
    zeros = (0,) * len(array.shape)
    return pl.BlockSpec(array.shape, lambda *_: zeros)


SCALAR = pl.BlockSpec(memory_space=pltpu.SMEM)
ANYWHERE = pl.BlockSpec(memory_space=pl.ANY)


def halves(entry):
    half_dim = HD // 2
    return (entry // half_dim) * (LANES // 2) + entry % half_dim


def placement(lanes, width):
    return (lanes[:, None] == jnp.arange(width)[None, :]).astype(jnp.bfloat16)


def place_query(heads):
    source = jnp.arange(heads * HD)
    return placement((source // HD) * LANES + halves(source % HD), heads * LANES)


def place_key_value(kv_heads):
    source = jnp.arange(kv_heads * HD)
    head = source // HD
    keys = head * 2 * LANES + halves(source % HD)
    values = head * 2 * LANES + LANES + source % HD
    return placement(jnp.concatenate([keys, values]), kv_heads * 2 * LANES)


def place_all(heads, kv_heads):
    source = jnp.arange(heads * HD)
    head = source // HD
    query = (head // GROUP) * KV_WIDE + (head % GROUP) * LANES + halves(source % HD)
    source = jnp.arange(kv_heads * HD)
    base = (source // HD) * KV_WIDE + GROUP * LANES
    keys = base + halves(source % HD)
    values = base + LANES + source % HD
    return placement(jnp.concatenate([query, keys, values]), kv_heads * KV_WIDE)


def place_plain(heads):
    source = jnp.arange(heads * HD)
    return placement((source // HD) * LANES + source % HD, heads * LANES)


PAIRS = [(0, 1), (1, 0), (2, 3), (3, 2)]
INWARD = [(0, 1), (3, 2)]
MIDDLE = [(1, 2), (2, 1)]
OUTWARD = [(1, 0), (2, 3)]


def along(part, pairs):
    return lax.ppermute(part, "tp", pairs)


def store_qkv(out_ref, here, base, query, key_value):
    wide = GROUP * LANES
    for kv in range(key_value.shape[1] // (2 * LANES)):
        at = base + kv * KV_WIDE
        there = slice(kv * 2 * LANES, (kv + 1) * 2 * LANES)
        out_ref[here, at : at + wide] = query[:, kv * wide : (kv + 1) * wide]
        out_ref[here, at + wide : at + KV_WIDE] = key_value[:, there]


def store_turned(out_ref, at, lin, cos_ref, sin_ref):
    for h in range(GROUP + 2):
        one = lin[:, h * LANES : (h + 1) * LANES]
        if h < GROUP + 1:
            one = one * cos_ref[...] + pltpu.roll(one, LANES // 2, 1) * sin_ref[...]
        out_ref[:, at + h * LANES : at + (h + 1) * LANES] = one.astype(jnp.bfloat16)


def spread_out_kernel(meta_ref, own_ref, p_ref, mine_ref, theirs_ref, pad_ref, plain_ref):
    rows, width = mine_ref.shape[2:]
    wide = p_ref.shape[1]
    for side, ref in enumerate((mine_ref, theirs_ref)):
        here = pl.ds(pl.multiple_of((meta_ref[1] ^ side) * rows, rows), rows)
        for s in range(4):
            block = own_ref[here, :] if s == 0 else ref[0, s - 1].astype(jnp.bfloat16)
            plain_ref[here, s * width : (s + 1) * width] = block
            pad_ref[here, s * wide : (s + 1) * wide] = dot32(block, p_ref[...]).astype(
                jnp.bfloat16
            )


def spread_qkv_kernel(pq_ref, pkv_ref, far_ref, _, out_ref):
    parts, _, rows, width = far_ref.shape
    split = pq_ref.shape[0]
    block = far_ref[:, 0].reshape(parts * rows, width).astype(jnp.bfloat16)
    query = dot32(block[:, :split], pq_ref[...]).astype(jnp.bfloat16)
    key_value = dot32(block[:, split:], pkv_ref[...]).astype(jnp.bfloat16)
    store_qkv(out_ref, slice(None), 0, query, key_value)


def spread_qkv(padded, pq, pkv, far):
    total = padded.shape[0]
    dp, others, rows, width = far.shape
    wide = padded.shape[1] // (others + 1)
    parts = max(1, dp // 2)
    block = parts * rows
    return pl.pallas_call(
        spread_qkv_kernel,
        out_shape=jax.ShapeDtypeStruct(padded.shape, jnp.bfloat16),
        grid=(total // block, others),
        in_specs=[
            whole(pq),
            whole(pkv),
            pl.BlockSpec((parts, 1, rows, width), lambda i, s: (i, s, 0, 0)),
            pl.BlockSpec(memory_space=pl.ANY),
        ],
        out_specs=pl.BlockSpec((block, wide), lambda i, s: (i, s + 1)),
        input_output_aliases={3: 0},
        compiler_params=params(),
        cost_estimate=cost(8 * total * width * 512, 20 * total * wide),
    )(pq, pkv, far, padded)


def spread(kernel, meta, own, places, mine, theirs, widths):
    chips, others, rows, width = mine.shape
    total = own.shape[0]
    row_block = lambda m, meta: (meta[0] ^ m, 0)
    piece = pl.BlockSpec((1, others, rows, width), lambda m, meta: (m, 0, 0, 0))
    return pl.pallas_call(
        kernel,
        out_shape=[jax.ShapeDtypeStruct((total, wide), jnp.bfloat16) for wide in widths],
        grid_spec=pltpu.PrefetchScalarGridSpec(
            num_scalar_prefetch=1,
            grid=(chips,),
            in_specs=[pl.BlockSpec((2 * rows, own.shape[1]), row_block)]
            + [whole(place) for place in places]
            + [piece, piece],
            out_specs=[pl.BlockSpec((2 * rows, wide), row_block) for wide in widths],
        ),
        compiler_params=params(),
        cost_estimate=cost(
            8 * total * width * 512, total * (12 * width + 2 * sum(widths))
        ),
    )(meta, own, *places, mine, theirs)


def start_kernel(x_ref, gain_ref, q_ref, k_ref, v_ref, pq_ref, pkv_ref, cos_ref, sin_ref, *outs):
    qkv_ref, normed_ref, pad_ref = outs

    @pl.when(pl.program_id(0) == 0)
    def _():
        split = k_ref.shape[0]
        query = dot32(q_ref[...], pq_ref[...]).astype(jnp.bfloat16)
        key_value = dot32(k_ref[...].T, pkv_ref[:split, :])
        key_value = key_value + dot32(v_ref[...].T, pkv_ref[split:, :])
        store_qkv(pad_ref, slice(None), 0, query, key_value.astype(jnp.bfloat16))

    inputs = x_ref[...].astype(jnp.float32)
    rms = lax.rsqrt(jnp.mean(inputs * inputs, -1, keepdims=True) + norm_eps)
    normed = (inputs * rms * gain_ref[...]).astype(jnp.bfloat16)
    normed_ref[...] = normed
    for kv in range(pad_ref.shape[1] // KV_WIDE):
        at = kv * KV_WIDE
        store_turned(qkv_ref, at, dot32(normed, pad_ref[:, at : at + KV_WIDE]), cos_ref, sin_ref)


def start(tokens, gain, w_query, w_key_t, w_value_t, pq, pkv, cosines, sines):
    total, depth = tokens.shape
    rows = total // CHUNKS
    wide = pq.shape[1] + pkv.shape[1]
    gain = gain[None, :]
    by_rows = lambda width: pl.BlockSpec((rows, width), lambda i: (i, 0))
    arrays = [w_query, w_key_t, w_value_t, pq, pkv]
    shapes = [
        jax.ShapeDtypeStruct((total, 4 * wide), jnp.bfloat16),
        jax.ShapeDtypeStruct((total, depth), jnp.bfloat16),
        jax.ShapeDtypeStruct((depth, 4 * wide), jnp.bfloat16),
    ]
    return pl.pallas_call(
        start_kernel,
        out_shape=shapes,
        grid=(CHUNKS,),
        in_specs=[by_rows(depth), whole(gain)]
        + [whole(array) for array in arrays]
        + [by_rows(LANES), by_rows(LANES)],
        out_specs=[
            by_rows(wide),
            by_rows(depth),
            pl.BlockSpec((depth, wide), lambda i: (0, 0)),
        ],
        compiler_params=params(),
        cost_estimate=cost(2 * total * depth * wide, 12 * total * depth),
    )(tokens, gain, *arrays, cosines, sines)


def turn_kernel(length_ref, cot_ref, normed_ref, dout_ref, dout_t_ref, normed_t_ref):
    rows = cot_ref.shape[0]
    at = pl.program_id(0) * rows + lax.broadcasted_iota(jnp.int32, cot_ref.shape, 0)
    dout = jnp.where(at < length_ref[0], cot_ref[...].astype(jnp.float32), 0.0)
    dout = dout.astype(jnp.bfloat16)
    dout_ref[...] = dout
    dout_t_ref[...] = dout.T
    normed_t_ref[...] = normed_ref[...].T


def turn(length, cotangent, normed):
    total, depth = cotangent.shape
    rows = total // CHUNKS
    by_rows = pl.BlockSpec((rows, depth), lambda i: (i, 0))
    by_columns = pl.BlockSpec((depth, rows), lambda i: (0, i))
    turned = jax.ShapeDtypeStruct((depth, total), jnp.bfloat16)
    return pl.pallas_call(
        turn_kernel,
        out_shape=[jax.ShapeDtypeStruct((total, depth), jnp.bfloat16), turned, turned],
        grid=(CHUNKS,),
        in_specs=[SCALAR, by_rows, by_rows],
        out_specs=[by_rows, by_columns, by_columns],
        compiler_params=params(),
        cost_estimate=cost(total * depth, 10 * total * depth),
    )(length, cotangent, normed)


def project_kernel(x_ref, w_ref, cos_ref, sin_ref, _, out_ref):
    store_turned(out_ref, 0, dot32(x_ref[...], w_ref[...]), cos_ref, sin_ref)


def project(normed, weights, cosines, sines, qkv):
    rows, depth = normed.shape
    width = weights.shape[1]
    steps = width // KV_WIDE
    first = steps // 4
    return pl.pallas_call(
        project_kernel,
        out_shape=jax.ShapeDtypeStruct((rows, width), jnp.bfloat16),
        grid=(steps - first,),
        in_specs=[
            whole(normed),
            pl.BlockSpec((depth, KV_WIDE), lambda i: (0, i + first)),
            whole(cosines),
            whole(sines),
            pl.BlockSpec(memory_space=pl.ANY),
        ],
        out_specs=pl.BlockSpec((rows, KV_WIDE), lambda i: (0, i + first)),
        input_output_aliases={4: 0},
        compiler_params=params(),
        cost_estimate=cost(
            2 * rows * depth * width, 2 * (rows * depth + depth * width + rows * width)
        ),
    )(normed, weights, cosines, sines, qkv)


def attend_kernel(start, length_ref, q_ref, kv_ref, strip_ref, out_ref):
    rows = q_ref.shape[0]
    keys = kv_ref.shape[0]
    length = length_ref[0]
    row_ids = start + lax.broadcasted_iota(jnp.int32, (1, rows), 1)
    limit = jnp.minimum(row_ids, length - 1)
    allowed = lax.broadcasted_iota(jnp.int32, (keys, rows), 0) <= limit
    mixed = []
    sums = []
    for kv in range(kv_ref.shape[1] // KV_WIDE):
        base = kv * KV_WIDE
        at = base + GROUP * LANES
        key = kv_ref[:, at : at + LANES]
        value_t = kv_ref[:, at + LANES : at + 2 * LANES].T
        for g in range(GROUP):
            query = q_ref[:, base + g * LANES : base + (g + 1) * LANES]
            raw = jnp.where(allowed, dot32_nt(key, query), masked_score)
            peak = jnp.max(raw, axis=0, keepdims=True)
            expo = jnp.exp2((raw - peak) * score_scale_log2)
            total = jnp.sum(expo, axis=0, keepdims=True)
            probs = (expo * (1.0 / total)).astype(jnp.bfloat16)
            mixed.append(dot32(value_t, probs).T)
            log_sum = peak * score_scale_log2 + jnp.log2(total)
            sums.append(jnp.where(row_ids < length, log_sum, far_away))
    out_ref[:rows, :] = dot_split(jnp.concatenate(mixed, 1), strip_ref[...])
    out_ref[rows:, :] = jnp.zeros((EXTRA, out_ref.shape[1]), jnp.float32)
    out_ref[rows : rows + len(sums), :rows] = jnp.concatenate(sums, 0)


def attend(length, qkv, strip, index, rows):
    keys = (index + 1) * rows
    width = qkv.shape[1] // 4
    heads = width // KV_WIDE * GROUP
    shape = (rows + EXTRA, strip.shape[1])
    return pl.pallas_call(
        functools.partial(attend_kernel, index * rows),
        out_shape=jax.ShapeDtypeStruct(shape, jnp.float32),
        grid=(1,),
        in_specs=[
            SCALAR,
            pl.BlockSpec((rows, width), lambda i: (index, 0)),
            pl.BlockSpec((keys, width), lambda i: (0, 0)),
            whole(strip),
        ],
        out_specs=pl.BlockSpec(shape, lambda i: (0, 0)),
        compiler_params=params(),
        cost_estimate=cost(
            4 * heads * rows * keys * LANES, 2 * (rows + keys) * width, heads * rows * keys
        ),
    )(length, qkv, qkv, strip)


def forward_kernel(level_ref, part_ref, other_ref, across_ref, outer_ref, *refs):
    x_ref, dout_ref, wo_ref, gain_ref, gate_any, up_any, down_any = refs[:7]
    hidden_ref, normed_t_ref, activ_ref, dgate_ref, dup_ref, mlp_ref, dn_ref = refs[7:14]
    normed_ref, gate_ref, up_ref, down_ref, sems = refs[14:]
    rows = x_ref.shape[0]
    steps, block = down_ref.shape[:2]
    step = pl.program_id(0)

    def fetched(at):
        here = pl.ds(pl.multiple_of(at * block, block), block)
        return [
            pltpu.make_async_copy(gate_any.at[:, here], gate_ref.at[at], sems.at[0, at]),
            pltpu.make_async_copy(up_any.at[:, here], up_ref.at[at], sems.at[1, at]),
            pltpu.make_async_copy(down_any.at[here, :], down_ref.at[at], sems.at[2, at]),
        ]

    @pl.when(step == 0)
    def _():
        for at in range(steps):
            for copy in fetched(at):
                copy.start()
        level = level_ref[0]
        inner = (level == 1) | (level == 2)
        width = part_ref.shape[1]
        second = jnp.where(inner, across_ref[:rows, width:], outer_ref[:rows, :width])
        third = jnp.where(inner, across_ref[:rows, :width], outer_ref[:rows, width:])
        mixed = jnp.concatenate([part_ref[:rows, :], other_ref[:rows, :], second, third], 1)
        hidden = x_ref[...].astype(jnp.float32) + dot32_nt(mixed.astype(jnp.bfloat16), wo_ref[...])
        hidden_ref[...] = hidden
        rms = lax.rsqrt(jnp.mean(hidden * hidden, -1, keepdims=True) + norm_eps)
        normed = (hidden * rms * gain_ref[...]).astype(jnp.bfloat16)
        normed_ref[...] = normed
        normed_t_ref[...] = normed.T
        mlp_ref[...] = jnp.zeros_like(mlp_ref)
        dn_ref[...] = jnp.zeros_like(dn_ref)

    for copy in fetched(step):
        copy.wait()
    wg_ref, wu_ref, wd_ref = gate_ref.at[step], up_ref.at[step], down_ref.at[step]
    normed = normed_ref[...]
    gate = dot32(normed, wg_ref[...])
    up = dot32(normed, wu_ref[...])
    dact = dot32_nt(dout_ref[...], wd_ref[...])
    sigmoid = jax.nn.sigmoid(gate)
    silu = gate * sigmoid
    activ = (silu * up).astype(jnp.bfloat16)
    dgate = (dact * up * sigmoid * (1.0 + gate * (1.0 - sigmoid))).astype(jnp.bfloat16)
    dup = (dact * silu).astype(jnp.bfloat16)
    activ_ref[...] = activ
    dgate_ref[...] = dgate
    dup_ref[...] = dup
    mlp_ref[...] += dot32(activ, wd_ref[...])
    dn_ref[:rows, :] += dot32_nt(dgate, wg_ref[...]) + dot32_nt(dup, wu_ref[...])


def forward_chunk(level, gathered, tokens, dout, w_out, gain, w_gate, w_up, w_down, index, rows):
    depth = tokens.shape[1]
    units = w_gate.shape[1]
    block = 512
    own_rows = pl.BlockSpec((rows, depth), lambda i: (index, 0))
    steps = units // block
    gain = gain[None, :]
    f32, bf16 = jnp.float32, jnp.bfloat16
    outs = [
        jax.ShapeDtypeStruct((rows, depth), f32),
        jax.ShapeDtypeStruct((depth, rows), bf16),
        jax.ShapeDtypeStruct((rows, units), bf16),
        jax.ShapeDtypeStruct((rows, units), bf16),
        jax.ShapeDtypeStruct((rows, units), bf16),
        jax.ShapeDtypeStruct((rows, depth), f32),
        jax.ShapeDtypeStruct((rows + EXTRA, depth), f32),
    ]
    unit_out = pl.BlockSpec((rows, block), lambda i: (0, i))
    return pl.pallas_call(
        forward_kernel,
        out_shape=outs,
        grid=(steps,),
        in_specs=[SCALAR]
        + [whole(array) for array in gathered]
        + [own_rows, own_rows, whole(w_out), whole(gain)]
        + [ANYWHERE] * 3,
        out_specs=[
            whole(outs[0]),
            whole(outs[1]),
            unit_out,
            unit_out,
            unit_out,
            whole(outs[5]),
            whole(outs[6]),
        ],
        scratch_shapes=[
            pltpu.VMEM((rows, depth), bf16),
            pltpu.VMEM((steps, depth, block), bf16),
            pltpu.VMEM((steps, depth, block), bf16),
            pltpu.VMEM((steps, block, depth), bf16),
            pltpu.SemaphoreType.DMA((3, steps)),
        ],
        compiler_params=params(),
        cost_estimate=cost(
            2 * rows * depth * (6 * units + w_out.shape[1]),
            2 * depth * (3 * units + w_out.shape[1]) + 22 * rows * depth,
            rows * units,
        ),
    )(level, *gathered, tokens, dout, w_out, gain, w_gate, w_up, w_down)


def hidden_grad(inner, total_ref, final_ref, hidden_ref, dout_ref, gain_ref):
    dnormed = jnp.where(inner, total_ref[...], final_ref[...])
    hidden = hidden_ref[...]
    rms = lax.rsqrt(jnp.mean(hidden * hidden, -1, keepdims=True) + norm_eps)
    scaled = dnormed * gain_ref[...]
    shift = jnp.mean(scaled * hidden, -1, keepdims=True)
    dhid = dout_ref[...].astype(jnp.float32) + (rms * scaled - hidden * (rms**3 * shift))
    return dhid, dnormed * (hidden * rms)


def backward_kernel(
    start, full, adding, steps, level_ref, total_ref, final_ref, hidden_ref, dout_ref, *refs
):
    gain_two_ref, wo_ref, q_ref = refs[:3]
    kv_here = q_ref.shape[1] // KV_WIDE
    refs = refs[3:]
    kv_refs, refs = refs[: 2 * kv_here], refs[2 * kv_here :]
    part_ref, place_ref, strip_ref, cos_ref, sin_ref = refs[:5]
    extra = (2 if full else 0) + (1 if adding else 0) + 1
    outs, scratch = refs[5 : -3 - extra], refs[-3 - extra :]
    dhid_ref, low_ref, dn_ref, sems = scratch[:4]
    if full:
        x_any, gain_one_ref, other_ref, across_ref, outer_ref, w_any = outs[:6]
        outs = outs[6:]
        x_ref, w_buffers = scratch[4:6]
        tokens_here = pltpu.make_async_copy(
            x_any.at[pl.ds(start, x_ref.shape[0]), :], x_ref, sems.at[4]
        )
    count = (5 if start > 0 else 4) if full else 2
    if adding:
        acc_any, acc_buffers = outs[0], scratch[-1]
    outs = outs[-count:]
    dhid_t_ref, dqkv_ref = outs[:2]
    if full:
        input_grad_ref, gains_ref = outs[2:4]
    rows = q_ref.shape[0]
    keys = kv_refs[0].shape[0]
    shard = pl.program_id(0)
    level = level_ref[0]
    inner = (level == 1) | (level == 2)

    def fetched(at, sums):
        source, buffers = (acc_any, acc_buffers) if sums else (w_any, w_buffers)
        lanes = buffers.shape[2]
        here = pl.ds(pl.multiple_of(at * lanes, lanes), lanes)
        slot = at % 2
        sem = sems.at[slot + 2] if sums else sems.at[slot]
        return pltpu.make_async_copy(source.at[:, here], buffers.at[slot], sem)

    def fetch(at):
        if adding:
            fetched(at, True).start()
        if full:
            fetched(at, False).start()

    @pl.when(shard == 0)
    def _():
        for at in range(min(2, steps)):
            fetch(at)
        if full:
            tokens_here.start()
        dhid, dgain = hidden_grad(
            inner, total_ref, final_ref, hidden_ref, dout_ref, gain_two_ref
        )
        dhid_ref[...] = dhid
        low = dhid.astype(jnp.bfloat16)
        low_ref[...] = low
        dhid_t_ref[...] = low.T
        if full:
            gains_ref[...] = jnp.zeros_like(gains_ref)
            gains_ref[1:2, :] = jnp.sum(dgain, 0, keepdims=True)
            dn_ref[...] = jnp.zeros_like(dn_ref)

    def rotate_back(grads):
        turned = grads * cos_ref[...] - pltpu.roll(grads, LANES // 2, 1) * sin_ref[...]
        return turned.astype(jnp.bfloat16)

    dmixed_all = dot32(low_ref[...], wo_ref[...]).astype(jnp.bfloat16)
    mixed = part_ref[...]
    if full:
        far = jnp.where(inner, across_ref[...], outer_ref[...])
        far = jnp.where(shard == 1, other_ref[...], far)
        mixed = jnp.where(shard == 0, mixed, far)
    products = dmixed_all.astype(jnp.float32) * dot_split(mixed[:rows], place_ref[...])
    causal = lax.broadcasted_iota(jnp.int32, (rows, rows), 0) <= lax.broadcasted_iota(
        jnp.int32, (rows, rows), 1
    )
    acc_ref = None
    if adding:
        fetched(shard, True).wait()
        acc_ref = acc_buffers.at[shard % 2]
    grads = []
    for kv in range(kv_here):
        key_ref, value_ref = kv_refs[2 * kv : 2 * kv + 2]
        heads = range(kv * GROUP, (kv + 1) * GROUP)
        lanes = {h: slice(h * LANES, (h + 1) * LANES) for h in heads}
        row_dots = {h: jnp.sum(products[:, lanes[h]].T, axis=0, keepdims=True) for h in heads}
        log_sums = {h: mixed[rows + h : rows + h + 1, :rows] for h in heads}
        dqueries = dict.fromkeys(heads)
        here = slice(2 * kv * LANES, (2 * kv + 1) * LANES)
        there = slice((2 * kv + 1) * LANES, (2 * kv + 2) * LANES)
        for tile in range(keys // rows):
            span = slice(tile * rows, (tile + 1) * rows)
            key = key_ref[span, :]
            value = value_ref[span, :]
            key_t = key.T
            dkey = None if acc_ref is None else acc_ref[span, here]
            dvalue = None if acc_ref is None else acc_ref[span, there]
            last = tile * rows == start
            for h in heads:
                at = kv * KV_WIDE + (h % GROUP) * LANES
                query = q_ref[:, at : at + LANES]
                dmixed = dmixed_all[:, lanes[h]]
                raw = dot32_nt(key, query)
                probs = jnp.exp2(raw * score_scale_log2 - log_sums[h])
                if last:
                    probs = jnp.where(causal, probs, 0.0)
                dprobs = dot32_nt(value, dmixed)
                dscores = (probs * (dprobs - row_dots[h])).astype(jnp.bfloat16)
                dquery = dot32(key_t, dscores)
                dqueries[h] = dquery if dqueries[h] is None else dqueries[h] + dquery
                dkey_one = dot32(dscores, query)
                dvalue_one = dot32(probs.astype(jnp.bfloat16), dmixed)
                dkey = dkey_one if dkey is None else dkey + dkey_one
                dvalue = dvalue_one if dvalue is None else dvalue + dvalue_one
            if full and not last:
                outs[4][span, here] = dkey
                outs[4][span, there] = dvalue
        grads += [rotate_back(dqueries[h].T * score_scale) for h in heads]
        grads.append(rotate_back(dkey * score_scale))
        grads.append(dvalue.astype(jnp.bfloat16))
    grads = jnp.concatenate(grads, 1)
    if full:
        fetched(shard, False).wait()
        dn_ref[...] += dot32_nt(grads, w_buffers[shard % 2])

        @pl.when(shard + 2 < steps)
        def _():
            fetch(shard + 2)

    @pl.when(shard == 0)
    def _():
        wide = strip_ref.shape[1]
        for kv in range(kv_here):
            dqkv_ref[:, kv * wide : (kv + 1) * wide] = dot32(
                grads[:, kv * KV_WIDE : (kv + 1) * KV_WIDE], strip_ref[...]
            ).astype(jnp.bfloat16)

    if not full:
        return

    @pl.when(shard == pl.num_programs(0) - 1)
    def _():
        tokens_here.wait()
        dnormed = dn_ref[...]
        inputs = x_ref[...].astype(jnp.float32)
        rms = lax.rsqrt(jnp.mean(inputs * inputs, -1, keepdims=True) + norm_eps)
        scaled = dnormed * gain_one_ref[...]
        shift = jnp.mean(scaled * inputs, -1, keepdims=True)
        grad = dhid_ref[...] + (rms * scaled - inputs * (rms**3 * shift))
        input_grad_ref[...] = grad.astype(jnp.bfloat16)
        gains_ref[0:1, :] = jnp.sum(dnormed * (inputs * rms), 0, keepdims=True)


def backward_chunk(
    level, sums_two, hidden, dout, tokens, gains, weights, qkv, gathered, places, tables, acc,
    index, rows, full=True, grad_into=None
):
    start = index * rows
    keys = start + rows
    depth = tokens.shape[1]
    out_pad, qkv_pad = weights
    place_out, strip = places
    far_rows, width = gathered[0].shape
    out_wide = place_out.shape[1]
    kv_here = out_wide // (GROUP * LANES)
    wide = kv_here * KV_WIDE
    levels = qkv.shape[1] // wide
    own_rows = pl.BlockSpec((rows, depth), lambda t: (index, 0))
    table = pl.BlockSpec((rows, LANES), lambda t: (index, 0))
    gains = [gain[None, :] for gain in gains]
    key_value = lambda at: pl.BlockSpec(
        (keys, LANES), lambda t: (0, (wide // LANES) * t + at)
    )
    across = pl.BlockSpec((far_rows, width), lambda t: (0, jnp.where(t == 2, 1, 0)))
    outer = pl.BlockSpec((far_rows, width), lambda t: (0, jnp.where(t == 3, 1, 0)))
    in_specs = [
        SCALAR,
        whole(hidden),
        whole(hidden),
        whole(hidden),
        own_rows,
        whole(gains[1]),
        pl.BlockSpec((depth, out_wide), lambda t: (0, t)),
        pl.BlockSpec((rows, wide), lambda t: (index, t)),
    ]
    for kv in range(kv_here):
        at = kv * (KV_WIDE // LANES) + GROUP
        in_specs += [key_value(at), key_value(at + 1)]
    in_specs += [
        whole(gathered[0]),
        whole(place_out),
        whole(strip),
        table,
        table,
    ]
    args = [level, *sums_two, hidden, dout, gains[1], out_pad]
    args += [qkv] * (1 + 2 * kv_here)
    args += [gathered[0], place_out, strip, *tables]
    sums_wide = 2 * kv_here * LANES
    if full:
        in_specs += [ANYWHERE, whole(gains[0]), whole(gathered[1]), across, outer]
        in_specs.append(ANYWHERE)
        args += [tokens, gains[0], *gathered[1:], qkv_pad]
    if acc is not None:
        in_specs.append(ANYWHERE)
        args.append(acc)
    f32, bf16 = jnp.float32, jnp.bfloat16
    outs = [
        jax.ShapeDtypeStruct((depth, rows), bf16),
        jax.ShapeDtypeStruct((rows, kv_here * strip.shape[1]), bf16),
        jax.ShapeDtypeStruct(tokens.shape, bf16),
        jax.ShapeDtypeStruct((8, depth), f32),
    ]
    outs = outs if full else outs[:2]
    out_specs = [whole(out) for out in outs]
    aliases = {}
    if full:
        out_specs[2] = own_rows
        if grad_into is not None:
            aliases = {len(args): 2}
            in_specs.append(ANYWHERE)
            args.append(grad_into)
    if full and start > 0:
        outs.append(jax.ShapeDtypeStruct((start, levels * sums_wide), f32))
        out_specs.append(pl.BlockSpec((start, sums_wide), lambda t: (0, t)))
    steps = levels if full else 1
    scratch = [
        pltpu.VMEM((rows, depth), f32),
        pltpu.VMEM((rows, depth), bf16),
        pltpu.VMEM((rows, depth), f32),
        pltpu.SemaphoreType.DMA((5,)),
    ]
    if full:
        scratch += [pltpu.VMEM((rows, depth), bf16), pltpu.VMEM((2, depth, wide), bf16)]
    if acc is not None:
        scratch.append(pltpu.VMEM((min(2, steps), keys, sums_wide), f32))
    results = pl.pallas_call(
        functools.partial(backward_kernel, start, full, acc is not None, steps),
        out_shape=outs,
        grid=(steps,),
        input_output_aliases=aliases,
        in_specs=in_specs,
        out_specs=out_specs,
        scratch_shapes=scratch,
        compiler_params=params(VMEM_BYTES if start else LATE_VMEM_BYTES),
        cost_estimate=cost(
            levels * rows * (20 * kv_here * keys * LANES + 2 * depth * (out_wide + wide)),
            2 * depth * levels * (out_wide + wide) + 16 * rows * depth,
            levels * kv_here * GROUP * rows * keys,
        ),
    )(*args)
    return results[:4], (results[4] if full and start > 0 else None)


def rows_kernel(lefts, groups, adding, picked, together, side_ref, *refs):
    refs = list(refs)
    held_ref = refs.pop()
    out_refs = refs[-len(picked) :]
    refs = refs[: -len(picked)]
    recv_ref = refs.pop() if adding else None
    step = pl.program_id(0)
    left_refs = []
    for count in lefts:
        left_refs.append(refs[:count])
        refs = refs[count:]
    rights = []
    for _ in groups:
        rights.append(refs[:CHUNKS])
        refs = refs[CHUNKS:]
    rows = left_refs[0][0].shape[0]
    blocks = held_ref.shape[1] // rows

    @pl.when(step == 0)
    def _():
        for which, pieces in enumerate(left_refs):
            for n, ref in enumerate(pieces):
                m, j = n % blocks, n // blocks
                wide = ref.shape[1]
                held_ref[which, m * rows : (m + 1) * rows, j * wide : (j + 1) * wide] = ref[...]

    chunk = held_ref.shape[2] // CHUNKS
    whole_columns = slice(0, out_refs[0].shape[1])

    def give(group, left, columns):
        right = jnp.concatenate([ref[:chunk, :].astype(jnp.bfloat16) for ref in group], 0)
        total = dot32(held_ref[left], right)
        if recv_ref is not None:
            total = total + recv_ref[:, columns]
        for out_ref, parts in zip(out_refs, picked):
            at = 0
            for start, size in parts:
                out_ref[at : at + size, columns] = total[start : start + size]
                at += size

    begin = 0
    for group, (left, first, steps) in zip(rights, groups):
        if together:
            width = group[0].shape[1]
            give(group, left, slice(begin, begin + width))
            begin += width
        else:

            @pl.when((step >= first) & (step < first + steps))
            def _(group=group, left=left):
                give(group, left, whole_columns)


def rows_of(
    lefts, groups, side, rows, blocks, step, recv=None, picked=None, vmem=LATE_VMEM_BYTES
):
    if picked is None:
        picked = [[(0, rows * blocks)]]
    at = lambda m: lambda i, side: ((m ^ side[2]) * side[1] + side[0], 0)
    specs = []
    args = []
    counts = []
    for left in lefts:
        pieces = left if isinstance(left, list) else [left]
        counts.append(len(pieces) * blocks)
        for piece in pieces:
            for m in range(blocks):
                specs.append(pl.BlockSpec((rows, piece.shape[1]), at(m)))
                args.append(piece)
    tokens = sum(piece.shape[1] for piece in pieces)
    first = 0
    plan = []
    together = step is None
    for which, rights in groups:
        if together:
            plan.append((which, 0, 1))
            specs += [whole(right) for right in rights]
            args += rights
            first += rights[0].shape[1]
            continue
        steps = rights[0].shape[1] // step
        plan.append((which, first, steps))
        for right in rights:
            pick = lambda i, side, first=first, steps=steps: (0, jnp.clip(i - first, 0, steps - 1))
            specs.append(pl.BlockSpec((right.shape[0], step), pick))
            args.append(right)
        first += steps
    if together:
        first, step = 1, first
    total = first * step
    block = lambda height: pl.BlockSpec((height, step), lambda i, side: (0, i))
    if recv is not None:
        specs.append(block(rows * blocks))
        args.append(recv)
    heights = [sum(size for _, size in parts) for parts in picked]
    results = pl.pallas_call(
        functools.partial(rows_kernel, counts, plan, recv is not None, picked, together),
        out_shape=[jax.ShapeDtypeStruct((height, total), jnp.float32) for height in heights],
        grid_spec=pltpu.PrefetchScalarGridSpec(
            num_scalar_prefetch=1,
            grid=(first,),
            in_specs=specs,
            out_specs=[block(height) for height in heights],
            scratch_shapes=[pltpu.VMEM((len(lefts), rows * blocks, tokens), jnp.bfloat16)],
        ),
        compiler_params=params(vmem),
        cost_estimate=cost(
            2 * rows * blocks * tokens * total,
            4 * rows * blocks * total + 2 * tokens * (total + rows * blocks),
        ),
    )(side, *args)
    return results[0] if len(picked) == 1 else results


def finish_kernel(*refs):
    query_ref, key_ref, value_ref, out_ref = refs[4:]
    kv_here = key_ref.shape[1] // HD
    q_cols = out_ref.shape[1]
    for at in range(2):
        kept_ref, far_ref = refs[2 * at : 2 * at + 2]
        half = far_ref.shape[0]
        sums = kept_ref[...] + far_ref[...]
        here = slice(at * half, (at + 1) * half)
        out_ref[here, :] = sums[:, :q_cols]
        start = q_cols
        cut = [[], [], []]
        for kv in range(kv_here):
            for i, width in enumerate((GROUP * HD, HD, HD)):
                cut[i].append(sums[:, start : start + width])
                start += width
        for ref, pieces in zip((query_ref, key_ref, value_ref), cut):
            ref[here, :] = jnp.concatenate(pieces, 1)


def finish(one, far_one, two, far_two, kv_here):
    half, columns = far_one.shape
    first = pl.BlockSpec((half, columns), lambda i: (0, 0))
    q_cols = kv_here * GROUP * HD
    outs = [
        jax.ShapeDtypeStruct((2 * half, width), jnp.float32)
        for width in (q_cols, kv_here * HD, kv_here * HD, q_cols)
    ]
    return pl.pallas_call(
        finish_kernel,
        out_shape=outs,
        grid=(1,),
        in_specs=[first] * 4,
        out_specs=[whole(out) for out in outs],
        compiler_params=params(LATE_VMEM_BYTES),
        cost_estimate=cost(4 * half * columns, 32 * half * columns),
    )(one, far_one, two, far_two)


def shards(
    tokens,
    lengths,
    positions,
    cotangent,
    norm_gain,
    w_query,
    w_key,
    w_value,
    w_out,
    mlp_gain,
    w_gate,
    w_up,
    w_down,
):
    seq_rows, depth = tokens.shape
    chips = lax.axis_size("chip")
    dp = chips * 2
    tp = lax.axis_size("tp")
    chip = lax.axis_index("chip")
    core = lax.axis_index("core")
    level = lax.axis_index("tp")
    low = level < 2
    inner = (level == 1) | (level == 2)
    heads_here = w_query.shape[1] // HD
    kv_here = w_key.shape[1] // HD
    rows = seq_rows // CHUNKS
    slice_rows = depth // dp
    level_ref = level.astype(jnp.int32).reshape(1)
    by_hand = dp == 8
    swap = lambda array: lax.ppermute(array, "core", [(0, 1), (1, 0)])
    to_level = lambda array, s: along(array, [(t, t ^ s) for t in range(tp)])

    at_row = (chip * 2 + core) * slice_rows
    cols = lambda w: lax.dynamic_slice_in_dim(w, at_row, slice_rows, 1).astype(jnp.float32).T
    (out_slice,) = fence(cols(w_out))
    qkv_slice = jnp.concatenate(
        [
            lax.dynamic_slice_in_dim(w_query, at_row, slice_rows, 0).astype(jnp.float32),
            cols(w_key.T),
            cols(w_value.T),
        ],
        1,
    )
    out_slice, qkv_slice = fence(out_slice, qkv_slice)
    out_near = along(out_slice, PAIRS)
    qkv_near = along(qkv_slice, PAIRS)
    meta = jnp.stack([chip, core]).astype(jnp.int32)

    pq = place_query(heads_here)
    pkv = place_key_value(kv_here)
    p_all = place_all(heads_here, kv_here)
    strip_one = place_all(GROUP, 1).T
    p_out = place_plain(heads_here)
    strip_out = p_out.T

    half_dim = HD // 2
    freqs = rope_base ** (-(jnp.arange(half_dim).astype(jnp.float32) * 2.0 / HD))
    freqs = jnp.pad(freqs, (0, LANES // 2 - half_dim))
    angles = positions.astype(jnp.float32)[:, None] * jnp.concatenate([freqs, freqs])[None, :]
    cosines = jnp.cos(angles)
    sines = jnp.sin(angles) * jnp.where(jnp.arange(LANES) < LANES // 2, -1.0, 1.0)

    cosines, sines, out_near = fence(cosines, sines, out_near)
    out_across = along(jnp.stack([out_slice, out_near]), MIDDLE)
    qkv_own, normed_one, own_pad = start(
        tokens, norm_gain, w_query, w_key.T, w_value.T, pq, pkv, cosines, sines
    )

    def far_slices(near, across, outer):
        return jnp.stack(
            [
                near,
                jnp.where(inner, across[1], outer[0]),
                jnp.where(inner, across[0], outer[1]),
            ]
        )

    order = list(reversed(range(CHUNKS)))
    c0, c1, c2, c3 = order
    own, other, across, outer = {}, {}, {}, {}
    part, total, final = {}, {}, {}

    def hop_1(j):
        other[j] = along(own[j], PAIRS)

    def hop_2(j):
        across[j] = along(jnp.concatenate([own[j], other[j]], 1), MIDDLE)

    def hop_3(j):
        outer[j] = along(across[j], OUTWARD)

    coming = {}

    def add_1(j):
        coming[j] = along(part[j], INWARD)

    def add_2(j):
        total[j] = part[j][:rows] + coming[j][:rows]
        coming[j] = along(total[j], MIDDLE)

    def add_3(j, inward, extra=0):
        both = jnp.where(inner, total[j] + coming[j], inward)
        total[j] = jnp.pad(both, ((0, extra), (0, 0)))
        final[j] = along(total[j], PAIRS)
        return final[j]

    def to_chip(array, m):
        return lax.ppermute(array, "chip", [(i, i ^ m) for i in range(chips)])

    def over_chips_1(piece):
        cut = piece.shape[1] // 2
        one, two = piece[:, :cut], piece[:, cut:]
        return jnp.stack([one, to_chip(one, 1)]), jnp.stack([two, to_chip(two, 2)])

    def over_chips_2(one, two):
        return one, to_chip(one, 2), two, to_chip(two, 1)

    def over_chips_3(one, one_far, two, two_far):
        upper = jnp.stack([one[0], one[1], one_far[0], one_far[1]])
        lower = jnp.stack([two[0], two_far[0], two[1], two_far[1]])
        return jnp.concatenate([upper, lower], 2)

    qkv_own, out_across, qkv_near = fence(qkv_own, out_across, qkv_near)
    out_outer = along(out_across, OUTWARD)
    qkv_across = along(jnp.stack([qkv_slice, qkv_near]), MIDDLE)
    own[c0] = attend(lengths, qkv_own, strip_out, c0, rows)
    own[c1] = attend(lengths, qkv_own, strip_out, c1, rows)
    own, qkv_own, out_outer = fence(own, qkv_own, out_outer)
    others = along(jnp.concatenate([own[c0], own[c1]], 0), PAIRS)
    out_far = far_slices(out_near, out_across, out_outer)
    out_mine = over_chips_1(out_far) if by_hand else out_far
    own[c2] = attend(lengths, qkv_own, strip_out, c2, rows)
    own[c3] = attend(lengths, qkv_own, strip_out, c3, rows)
    own[c3], qkv_across = fence(own[c3], qkv_across)
    qkv_outer = along(qkv_across, OUTWARD)
    own, others, normed_one, w_out, out_mine = fence(own, others, normed_one, w_out, out_mine)
    other[c0], other[c1] = others[: rows + EXTRA], others[rows + EXTRA :]
    if by_hand:
        out_mine = over_chips_2(*out_mine)
    else:
        out_mine = lax.all_gather(out_mine, ("chip", "core"))
    hop_2(c0)
    dout, dout_t, normed_one_t = turn(lengths, cotangent, normed_one)
    w_out_t = w_out.T
    own, other, across, dout, dout_t, normed_one_t, w_out_t, out_mine, qkv_outer = fence(
        own, other, across, dout, dout_t, normed_one_t, w_out_t, out_mine, qkv_outer
    )
    hop_1(c2)
    hop_3(c0)
    hop_2(c1)
    qkv_far = lax.all_gather(far_slices(qkv_near, qkv_across, qkv_outer), ("chip", "core"))
    if by_hand:
        out_mine = over_chips_3(*out_mine)
        out_theirs = swap(out_mine)
        out_pad, out_plain = spread(
            spread_out_kernel,
            meta,
            w_out_t,
            [p_out],
            out_mine,
            out_theirs,
            [4 * p_out.shape[1], 4 * p_out.shape[0]],
        )
    else:
        plain = [w_out_t] + [
            out_mine[:, s].reshape(depth, -1).astype(jnp.bfloat16) for s in range(tp - 1)
        ]
        out_plain = jnp.concatenate(plain, 1)
        out_pad = jnp.concatenate([dot32(w, p_out).astype(jnp.bfloat16) for w in plain], 1)
    hidden, normed_t, activ, dgate, dup, mlp_part = {}, {}, {}, {}, {}, {}

    def feed(j):
        gathered = (own[j], other[j], across[j], outer[j])
        (hidden[j], normed_t[j], activ[j], dgate[j], dup[j], mlp_part[j], part[j]) = forward_chunk(
            level_ref, gathered, tokens, dout, out_plain, mlp_gain, w_gate, w_up, w_down, j, rows
        )

    own, other, across, outer, out_pad, out_plain = fence(
        own, other, across, outer, out_pad, out_plain
    )
    hop_1(c3)
    hop_3(c1)
    hop_2(c2)
    feed(c0)
    part, other = fence(part, other)
    add_1(c0)
    own, other, across, outer, part, hidden = fence(own, other, across, outer, part, hidden)
    hop_3(c2)
    hop_2(c3)
    feed(c1)
    qkv_far, hidden[c1] = fence(qkv_far, hidden[c1])
    qkv_pad = spread_qkv(own_pad, pq, pkv, qkv_far)
    own, other, across, outer, part, total, coming, hidden, qkv_pad = fence(
        own, other, across, outer, part, total, coming, hidden, qkv_pad
    )
    add_1(c1)
    hop_3(c3)
    add_2(c0)
    feed(c2)
    qkv_pad, hidden[c2] = fence(qkv_pad, hidden[c2])
    qkv = project(normed_one, qkv_pad, cosines, sines, qkv_own)
    own, other, across, outer, part, total, coming, hidden, qkv = fence(
        own, other, across, outer, part, total, coming, hidden, qkv
    )
    coming[c2] = add_3(c0, part[c2][:rows])
    add_2(c1)
    feed(c3)

    listed = lambda pieces: [pieces[j] for j in range(CHUNKS)]
    keep_side = jnp.stack([core, 2, 0]).astype(jnp.int32)
    keep_turned = jnp.stack([core, 2, chip]).astype(jnp.int32)
    send_side = jnp.stack([1 - core, 2, 0]).astype(jnp.int32)
    send_turned = jnp.stack([1 - core, 2, chip]).astype(jnp.int32)
    all_rows = jnp.array([0, 1, 0], jnp.int32)

    def send_rows(lefts, groups, step, side=send_side):
        if not by_hand:
            return rows_of(lefts, groups, all_rows, depth // 4, 4, step)
        return rows_of(lefts, groups, side, slice_rows, chips, step)

    def keep_rows(lefts, groups, received, step, side=keep_side, picked=None):
        if not by_hand:
            return received
        return rows_of(lefts, groups, side, slice_rows, chips, step, received, picked)

    def swap_rows(array):
        return swap(array) if by_hand else array

    def scatter(array, axes):
        return lax.psum_scatter(array, axes, scatter_dimension=0, tiled=True)

    units = w_gate.shape[1]
    mlp_args = (
        [listed(normed_t), dout_t],
        [(0, listed(dgate)), (0, listed(dup)), (1, listed(activ))],
    )
    acc = None
    input_grad = None
    dhid_t, dqkv_own, gains = {}, {}, {}

    def back(j):
        nonlocal acc, input_grad
        (dhid_t[j], dqkv_own[j], input_grad, gains[j]), acc = back_some(j, True)

    def back_own(j):
        return back_some(j, False)[0]

    def back_some(j, full):
        return backward_chunk(
            level_ref,
            (total[j], final[j]),
            hidden[j],
            dout,
            tokens,
            (norm_gain, mlp_gain),
            (out_pad, qkv_pad),
            qkv,
            (own[j], other[j], across[j], outer[j]),
            (p_out, strip_one),
            (cosines, sines),
            acc,
            j,
            rows,
            full,
            input_grad,
        )

    grad_mlp = rows_of(
        *mlp_args, all_rows, depth // 4, 4, units // 2, vmem=VMEM_BYTES
    )
    own, other, across, outer, part, total, coming, final, hidden, grad_mlp = fence(
        own, other, across, outer, part, total, coming, final, hidden, grad_mlp
    )
    grad_mlp = scatter(grad_mlp, ("chip", "core"))
    coming[c3] = add_3(c1, part[c3][:rows])
    add_2(c2)
    back(c0)

    near = lambda: jnp.where(low, mlp_part[1], mlp_part[2])
    edge = lambda: jnp.where(low, mlp_part[0], mlp_part[3])
    leave_far = lambda: jnp.where(low, mlp_part[3], mlp_part[0])
    leave_near = lambda: jnp.where(low, mlp_part[2], mlp_part[1])
    total, coming, final, hidden, mlp_part, acc, dhid_t = fence(
        total, coming, final, hidden, mlp_part, acc, dhid_t
    )
    far_sum = add_3(c2, leave_far())
    add_2(c3)
    back(c1)
    total, coming, final, hidden, mlp_part, far_sum, acc, dhid_t = fence(
        total, coming, final, hidden, mlp_part, far_sum, acc, dhid_t
    )
    add_3(c3, leave_near(), EXTRA)
    far_in = along(leave_far() + far_sum, MIDDLE)
    back(c2)
    total, final, hidden, acc, dhid_t = fence(total, final, hidden, acc, dhid_t)
    dhid_t[c3], dqkv_own[c3] = back_own(c3)
    dhid_t, dqkv_own, far_in, mlp_part, final = fence(
        dhid_t, dqkv_own, far_in, mlp_part, final
    )
    last = along(jnp.where(inner, edge() + far_in, near()), PAIRS)
    near_in = along(leave_near() + final[c3][:rows], MIDDLE)
    q_cols = heads_here * HD
    attn_args = (
        [listed(dhid_t), normed_one_t],
        [(0, listed(own)), (1, listed(dqkv_own))],
    )
    sent = swap_rows(send_rows(*attn_args, None, send_turned))
    total, final, hidden, acc, sent = fence(total, final, hidden, acc, sent)
    if by_hand:
        half = slice_rows // 2
        upper = lambda m: (m * slice_rows, half)
        lower = lambda m: (m * slice_rows + half, half)
        picked = [
            [upper(1), upper(3)],
            [upper(0), upper(2)],
            [lower(2), lower(3)],
            [lower(0), lower(1)],
        ]
        pieces = keep_rows(*attn_args, sent, None, keep_turned, picked)
        pieces, hidden = fence(pieces, hidden)
        one_away, one, two_away, two = pieces
        pieces = (one, to_chip(one_away, 1), two, to_chip(two_away, 2))
    else:
        pieces = scatter(sent, ("chip", "core"))
    back(c3)
    pieces, gains, input_grad = fence(pieces, gains, input_grad)
    gain_sums = gains[0] + gains[1] + gains[2] + gains[3]
    gain_sums = gain_sums + swap(gain_sums)
    gain_sums, last, near_in = fence(gain_sums, last, near_in)
    mlp_rows = jnp.where(inner, near() + near_in, edge()) + last
    hidden_rows = jnp.where(
        low,
        jnp.where(level == 0, hidden[0], hidden[1]),
        jnp.where(level == 2, hidden[2], hidden[3]),
    )
    layer_out = (hidden_rows + mlp_rows).astype(jnp.bfloat16)
    mlp_grads = [grad_mlp[:, at * units : (at + 1) * units] for at in range(3)]
    if by_hand:
        one = pieces[0] + pieces[1]
        two = pieces[2] + pieces[3]
        far_one = to_chip(one[half:], 2)
        far_two = to_chip(two[half:], 1)
        others = [to_chip(gain_sums, m) for m in range(1, chips)]
        far_one, far_two, mlp_grads, layer_out = fence(far_one, far_two, mlp_grads, layer_out)
        attn_grads = finish(one, far_one, two, far_two, kv_here)
        others, attn_grads = fence(others, attn_grads)
        gain_sums = sum(others, gain_sums)
    else:
        gain_sums = lax.psum(gain_sums, "chip")
        grad_qkv = pieces[:, q_cols:]
        one = strip_one.shape[1]
        picked = lambda at, width: jnp.concatenate(
            [grad_qkv[:, kv * one + at : kv * one + at + width] for kv in range(kv_here)], 1
        )
        attn_grads = (
            picked(0, GROUP * HD),
            picked(GROUP * HD, HD),
            picked((GROUP + 1) * HD, HD),
            pieces[:, :q_cols],
        )
    gain_rows = lax.dynamic_slice_in_dim(gain_sums, at_row, slice_rows, 1)
    grad_query, grad_key, grad_value, grad_out_t = attn_grads
    return (
        layer_out,
        input_grad,
        gain_rows[0],
        grad_query,
        grad_key,
        grad_value,
        grad_out_t.T,
        gain_rows[1],
        mlp_grads[0],
        mlp_grads[1],
        mlp_grads[2].T,
    )


def solution(mesh):
    devices = mesh.devices
    dp, tp = devices.shape
    split = Mesh(devices.reshape(dp // 2, 2, tp), ("chip", "core", "tp"))
    data = ("chip", "core")
    return jax.shard_map(
        shards,
        mesh=split,
        in_specs=(
            P(data, None),
            P(data),
            P(data),
            P(data, None),
            P(),
            P(None, "tp"),
            P(None, "tp"),
            P(None, "tp"),
            P("tp", None),
            P(),
            P(None, "tp"),
            P(None, "tp"),
            P("tp", None),
        ),
        out_specs=(
            P(("chip", "core", "tp"), None),
            P(data, None),
            P(data),
            P(data, "tp"),
            P(data, "tp"),
            P(data, "tp"),
            P("tp", data),
            P(data),
            P(data, "tp"),
            P(data, "tp"),
            P("tp", data),
        ),
        check_vma=False,
    )
```

```python
import functools

import jax
import jax.numpy as jnp
from jax import lax
from jax.experimental import pallas as pl
from jax.experimental.pallas import tpu as pltpu
from jax.sharding import Mesh
from jax.sharding import PartitionSpec as P

HD = 96
LANES = 128
GROUP = 2
KV_WIDE = (GROUP + 2) * LANES
rope_base = 100000.0
norm_eps = 1e-05
masked_score = -1e30
far_away = 1e30
score_scale = HD ** (-0.5)
score_scale_log2 = score_scale * 1.4426950408889634
CHUNKS = 4
EXTRA = 8
VMEM_BYTES = 56 * 1024 * 1024
LATE_VMEM_BYTES = 40 * 1024 * 1024
NT = (((1,), (1,)), ((), ()))


def params(vmem=VMEM_BYTES):
    return pltpu.CompilerParams(vmem_limit_bytes=vmem)


def cost(flops, moved, exps=0):
    return pl.CostEstimate(
        flops=flops // 1024, bytes_accessed=moved // 1024, transcendentals=exps // 1024
    )


def dot32(a, b):
    return jnp.dot(a, b, preferred_element_type=jnp.float32)


def dot32_nt(a, b):
    return lax.dot_general(a, b, NT, preferred_element_type=jnp.float32)


def dot_split(a, places):
    high = a.astype(jnp.bfloat16)
    rest = (a - high.astype(jnp.float32)).astype(jnp.bfloat16)
    return dot32(high, places) + dot32(rest, places)


def fence(*trees):
    return lax.optimization_barrier(trees)


def whole(array, buffers=None):
    zeros = (0,) * len(array.shape)
    return pl.BlockSpec(array.shape, lambda *_: zeros)


SCALAR = pl.BlockSpec(memory_space=pltpu.SMEM)
ANYWHERE = pl.BlockSpec(memory_space=pl.ANY)


def halves(entry):
    half_dim = HD // 2
    return (entry // half_dim) * (LANES // 2) + entry % half_dim


def placement(lanes, width):
    return (lanes[:, None] == jnp.arange(width)[None, :]).astype(jnp.bfloat16)


def place_query(heads):
    source = jnp.arange(heads * HD)
    return placement((source // HD) * LANES + halves(source % HD), heads * LANES)


def place_key_value(kv_heads):
    source = jnp.arange(kv_heads * HD)
    head = source // HD
    keys = head * 2 * LANES + halves(source % HD)
    values = head * 2 * LANES + LANES + source % HD
    return placement(jnp.concatenate([keys, values]), kv_heads * 2 * LANES)


def place_all(heads, kv_heads):
    source = jnp.arange(heads * HD)
    head = source // HD
    query = (head // GROUP) * KV_WIDE + (head % GROUP) * LANES + halves(source % HD)
    source = jnp.arange(kv_heads * HD)
    base = (source // HD) * KV_WIDE + GROUP * LANES
    keys = base + halves(source % HD)
    values = base + LANES + source % HD
    return placement(jnp.concatenate([query, keys, values]), kv_heads * KV_WIDE)


def place_plain(heads):
    source = jnp.arange(heads * HD)
    return placement((source // HD) * LANES + source % HD, heads * LANES)


PAIRS = [(0, 1), (1, 0), (2, 3), (3, 2)]
INWARD = [(0, 1), (3, 2)]
MIDDLE = [(1, 2), (2, 1)]
OUTWARD = [(1, 0), (2, 3)]


def along(part, pairs):
    return lax.ppermute(part, "tp", pairs)


def store_qkv(out_ref, here, base, query, key_value):
    wide = GROUP * LANES
    for kv in range(key_value.shape[1] // (2 * LANES)):
        at = base + kv * KV_WIDE
        there = slice(kv * 2 * LANES, (kv + 1) * 2 * LANES)
        out_ref[here, at : at + wide] = query[:, kv * wide : (kv + 1) * wide]
        out_ref[here, at + wide : at + KV_WIDE] = key_value[:, there]


def store_turned(out_ref, at, lin, cos_ref, sin_ref):
    for h in range(GROUP + 2):
        one = lin[:, h * LANES : (h + 1) * LANES]
        if h < GROUP + 1:
            one = one * cos_ref[...] + pltpu.roll(one, LANES // 2, 1) * sin_ref[...]
        out_ref[:, at + h * LANES : at + (h + 1) * LANES] = one.astype(jnp.bfloat16)


def spread_out_kernel(meta_ref, own_ref, p_ref, mine_ref, theirs_ref, pad_ref, plain_ref):
    rows, width = mine_ref.shape[2:]
    wide = p_ref.shape[1]
    for side, ref in enumerate((mine_ref, theirs_ref)):
        here = pl.ds(pl.multiple_of((meta_ref[1] ^ side) * rows, rows), rows)
        for s in range(4):
            block = own_ref[here, :] if s == 0 else ref[0, s - 1].astype(jnp.bfloat16)
            plain_ref[here, s * width : (s + 1) * width] = block
            pad_ref[here, s * wide : (s + 1) * wide] = dot32(block, p_ref[...]).astype(
                jnp.bfloat16
            )


def spread_qkv_kernel(pq_ref, pkv_ref, far_ref, _, out_ref):
    parts, _, rows, width = far_ref.shape
    split = pq_ref.shape[0]
    block = far_ref[:, 0].reshape(parts * rows, width).astype(jnp.bfloat16)
    query = dot32(block[:, :split], pq_ref[...]).astype(jnp.bfloat16)
    key_value = dot32(block[:, split:], pkv_ref[...]).astype(jnp.bfloat16)
    store_qkv(out_ref, slice(None), 0, query, key_value)


def spread_qkv(padded, pq, pkv, far):
    total = padded.shape[0]
    dp, others, rows, width = far.shape
    wide = padded.shape[1] // (others + 1)
    parts = max(1, dp // 2)
    block = parts * rows
    return pl.pallas_call(
        spread_qkv_kernel,
        out_shape=jax.ShapeDtypeStruct(padded.shape, jnp.bfloat16),
        grid=(total // block, others),
        in_specs=[
            whole(pq),
            whole(pkv),
            pl.BlockSpec((parts, 1, rows, width), lambda i, s: (i, s, 0, 0)),
            pl.BlockSpec(memory_space=pl.ANY),
        ],
        out_specs=pl.BlockSpec((block, wide), lambda i, s: (i, s + 1)),
        input_output_aliases={3: 0},
        compiler_params=params(),
        cost_estimate=cost(8 * total * width * 512, 20 * total * wide),
    )(pq, pkv, far, padded)


def spread(kernel, meta, own, places, mine, theirs, widths):
    chips, others, rows, width = mine.shape
    total = own.shape[0]
    row_block = lambda m, meta: (meta[0] ^ m, 0)
    piece = pl.BlockSpec((1, others, rows, width), lambda m, meta: (m, 0, 0, 0))
    return pl.pallas_call(
        kernel,
        out_shape=[jax.ShapeDtypeStruct((total, wide), jnp.bfloat16) for wide in widths],
        grid_spec=pltpu.PrefetchScalarGridSpec(
            num_scalar_prefetch=1,
            grid=(chips,),
            in_specs=[pl.BlockSpec((2 * rows, own.shape[1]), row_block)]
            + [whole(place) for place in places]
            + [piece, piece],
            out_specs=[pl.BlockSpec((2 * rows, wide), row_block) for wide in widths],
        ),
        compiler_params=params(),
        cost_estimate=cost(
            8 * total * width * 512, total * (12 * width + 2 * sum(widths))
        ),
    )(meta, own, *places, mine, theirs)


def start_kernel(x_ref, gain_ref, q_ref, k_ref, v_ref, pq_ref, pkv_ref, cos_ref, sin_ref, *outs):
    qkv_ref, normed_ref, pad_ref = outs

    @pl.when(pl.program_id(0) == 0)
    def _():
        split = k_ref.shape[0]
        query = dot32(q_ref[...], pq_ref[...]).astype(jnp.bfloat16)
        key_value = dot32(k_ref[...].T, pkv_ref[:split, :])
        key_value = key_value + dot32(v_ref[...].T, pkv_ref[split:, :])
        store_qkv(pad_ref, slice(None), 0, query, key_value.astype(jnp.bfloat16))

    inputs = x_ref[...].astype(jnp.float32)
    rms = lax.rsqrt(jnp.mean(inputs * inputs, -1, keepdims=True) + norm_eps)
    normed = (inputs * rms * gain_ref[...]).astype(jnp.bfloat16)
    normed_ref[...] = normed
    for kv in range(pad_ref.shape[1] // KV_WIDE):
        at = kv * KV_WIDE
        store_turned(qkv_ref, at, dot32(normed, pad_ref[:, at : at + KV_WIDE]), cos_ref, sin_ref)


def start(tokens, gain, w_query, w_key_t, w_value_t, pq, pkv, cosines, sines):
    total, depth = tokens.shape
    rows = total // CHUNKS
    wide = pq.shape[1] + pkv.shape[1]
    gain = gain[None, :]
    by_rows = lambda width: pl.BlockSpec((rows, width), lambda i: (i, 0))
    arrays = [w_query, w_key_t, w_value_t, pq, pkv]
    shapes = [
        jax.ShapeDtypeStruct((total, 4 * wide), jnp.bfloat16),
        jax.ShapeDtypeStruct((total, depth), jnp.bfloat16),
        jax.ShapeDtypeStruct((depth, 4 * wide), jnp.bfloat16),
    ]
    return pl.pallas_call(
        start_kernel,
        out_shape=shapes,
        grid=(CHUNKS,),
        in_specs=[by_rows(depth), whole(gain)]
        + [whole(array) for array in arrays]
        + [by_rows(LANES), by_rows(LANES)],
        out_specs=[
            by_rows(wide),
            by_rows(depth),
            pl.BlockSpec((depth, wide), lambda i: (0, 0)),
        ],
        compiler_params=params(),
        cost_estimate=cost(2 * total * depth * wide, 12 * total * depth),
    )(tokens, gain, *arrays, cosines, sines)


def turn_kernel(length_ref, cot_ref, normed_ref, dout_ref, dout_t_ref, normed_t_ref):
    rows = cot_ref.shape[0]
    at = pl.program_id(0) * rows + lax.broadcasted_iota(jnp.int32, cot_ref.shape, 0)
    dout = jnp.where(at < length_ref[0], cot_ref[...].astype(jnp.float32), 0.0)
    dout = dout.astype(jnp.bfloat16)
    dout_ref[...] = dout
    dout_t_ref[...] = dout.T
    normed_t_ref[...] = normed_ref[...].T


def turn(length, cotangent, normed):
    total, depth = cotangent.shape
    rows = total // CHUNKS
    by_rows = pl.BlockSpec((rows, depth), lambda i: (i, 0))
    by_columns = pl.BlockSpec((depth, rows), lambda i: (0, i))
    turned = jax.ShapeDtypeStruct((depth, total), jnp.bfloat16)
    return pl.pallas_call(
        turn_kernel,
        out_shape=[jax.ShapeDtypeStruct((total, depth), jnp.bfloat16), turned, turned],
        grid=(CHUNKS,),
        in_specs=[SCALAR, by_rows, by_rows],
        out_specs=[by_rows, by_columns, by_columns],
        compiler_params=params(),
        cost_estimate=cost(total * depth, 10 * total * depth),
    )(length, cotangent, normed)


def project_kernel(x_ref, w_ref, cos_ref, sin_ref, _, out_ref):
    store_turned(out_ref, 0, dot32(x_ref[...], w_ref[...]), cos_ref, sin_ref)


def project(normed, weights, cosines, sines, qkv):
    rows, depth = normed.shape
    width = weights.shape[1]
    steps = width // KV_WIDE
    first = steps // 4
    return pl.pallas_call(
        project_kernel,
        out_shape=jax.ShapeDtypeStruct((rows, width), jnp.bfloat16),
        grid=(steps - first,),
        in_specs=[
            whole(normed),
            pl.BlockSpec((depth, KV_WIDE), lambda i: (0, i + first)),
            whole(cosines),
            whole(sines),
            pl.BlockSpec(memory_space=pl.ANY),
        ],
        out_specs=pl.BlockSpec((rows, KV_WIDE), lambda i: (0, i + first)),
        input_output_aliases={4: 0},
        compiler_params=params(),
        cost_estimate=cost(
            2 * rows * depth * width, 2 * (rows * depth + depth * width + rows * width)
        ),
    )(normed, weights, cosines, sines, qkv)


def attend_kernel(start, length_ref, q_ref, kv_ref, strip_ref, out_ref):
    rows = q_ref.shape[0]
    keys = kv_ref.shape[0]
    length = length_ref[0]
    row_ids = start + lax.broadcasted_iota(jnp.int32, (1, rows), 1)
    limit = jnp.minimum(row_ids, length - 1)
    allowed = lax.broadcasted_iota(jnp.int32, (keys, rows), 0) <= limit
    mixed = []
    sums = []
    for kv in range(kv_ref.shape[1] // KV_WIDE):
        base = kv * KV_WIDE
        at = base + GROUP * LANES
        key = kv_ref[:, at : at + LANES]
        value_t = kv_ref[:, at + LANES : at + 2 * LANES].T
        for g in range(GROUP):
            query = q_ref[:, base + g * LANES : base + (g + 1) * LANES]
            raw = jnp.where(allowed, dot32_nt(key, query), masked_score)
            peak = jnp.max(raw, axis=0, keepdims=True)
            expo = jnp.exp2((raw - peak) * score_scale_log2)
            total = jnp.sum(expo, axis=0, keepdims=True)
            probs = (expo * (1.0 / total)).astype(jnp.bfloat16)
            mixed.append(dot32(value_t, probs).T)
            log_sum = peak * score_scale_log2 + jnp.log2(total)
            sums.append(jnp.where(row_ids < length, log_sum, far_away))
    out_ref[:rows, :] = dot_split(jnp.concatenate(mixed, 1), strip_ref[...])
    out_ref[rows:, :] = jnp.zeros((EXTRA, out_ref.shape[1]), jnp.float32)
    out_ref[rows : rows + len(sums), :rows] = jnp.concatenate(sums, 0)


def attend(length, qkv, strip, index, rows):
    keys = (index + 1) * rows
    width = qkv.shape[1] // 4
    heads = width // KV_WIDE * GROUP
    shape = (rows + EXTRA, strip.shape[1])
    return pl.pallas_call(
        functools.partial(attend_kernel, index * rows),
        out_shape=jax.ShapeDtypeStruct(shape, jnp.float32),
        grid=(1,),
        in_specs=[
            SCALAR,
            pl.BlockSpec((rows, width), lambda i: (index, 0)),
            pl.BlockSpec((keys, width), lambda i: (0, 0)),
            whole(strip),
        ],
        out_specs=pl.BlockSpec(shape, lambda i: (0, 0)),
        compiler_params=params(),
        cost_estimate=cost(
            4 * heads * rows * keys * LANES, 2 * (rows + keys) * width, heads * rows * keys
        ),
    )(length, qkv, qkv, strip)


def forward_kernel(level_ref, part_ref, other_ref, across_ref, outer_ref, *refs):
    x_ref, dout_ref, wo_ref, gain_ref, gate_any, up_any, down_any = refs[:7]
    hidden_ref, normed_t_ref, activ_ref, dgate_ref, dup_ref, mlp_ref, dn_ref = refs[7:14]
    normed_ref, gate_ref, up_ref, down_ref, sems = refs[14:]
    rows = x_ref.shape[0]
    steps, block = down_ref.shape[:2]
    step = pl.program_id(0)

    def fetched(at):
        here = pl.ds(pl.multiple_of(at * block, block), block)
        return [
            pltpu.make_async_copy(gate_any.at[:, here], gate_ref.at[at], sems.at[0, at]),
            pltpu.make_async_copy(up_any.at[:, here], up_ref.at[at], sems.at[1, at]),
            pltpu.make_async_copy(down_any.at[here, :], down_ref.at[at], sems.at[2, at]),
        ]

    @pl.when(step == 0)
    def _():
        for at in range(steps):
            for copy in fetched(at):
                copy.start()
        level = level_ref[0]
        inner = (level == 1) | (level == 2)
        width = part_ref.shape[1]
        second = jnp.where(inner, across_ref[:rows, width:], outer_ref[:rows, :width])
        third = jnp.where(inner, across_ref[:rows, :width], outer_ref[:rows, width:])
        mixed = jnp.concatenate([part_ref[:rows, :], other_ref[:rows, :], second, third], 1)
        hidden = x_ref[...].astype(jnp.float32) + dot32_nt(mixed.astype(jnp.bfloat16), wo_ref[...])
        hidden_ref[...] = hidden
        rms = lax.rsqrt(jnp.mean(hidden * hidden, -1, keepdims=True) + norm_eps)
        normed = (hidden * rms * gain_ref[...]).astype(jnp.bfloat16)
        normed_ref[...] = normed
        normed_t_ref[...] = normed.T
        mlp_ref[...] = jnp.zeros_like(mlp_ref)
        dn_ref[...] = jnp.zeros_like(dn_ref)

    for copy in fetched(step):
        copy.wait()
    wg_ref, wu_ref, wd_ref = gate_ref.at[step], up_ref.at[step], down_ref.at[step]
    normed = normed_ref[...]
    gate = dot32(normed, wg_ref[...])
    up = dot32(normed, wu_ref[...])
    dact = dot32_nt(dout_ref[...], wd_ref[...])
    sigmoid = jax.nn.sigmoid(gate)
    silu = gate * sigmoid
    activ = (silu * up).astype(jnp.bfloat16)
    dgate = (dact * up * sigmoid * (1.0 + gate * (1.0 - sigmoid))).astype(jnp.bfloat16)
    dup = (dact * silu).astype(jnp.bfloat16)
    activ_ref[...] = activ
    dgate_ref[...] = dgate
    dup_ref[...] = dup
    mlp_ref[...] += dot32(activ, wd_ref[...])
    dn_ref[:rows, :] += dot32_nt(dgate, wg_ref[...]) + dot32_nt(dup, wu_ref[...])


def forward_chunk(level, gathered, tokens, dout, w_out, gain, w_gate, w_up, w_down, index, rows):
    depth = tokens.shape[1]
    units = w_gate.shape[1]
    block = 512
    own_rows = pl.BlockSpec((rows, depth), lambda i: (index, 0))
    steps = units // block
    gain = gain[None, :]
    f32, bf16 = jnp.float32, jnp.bfloat16
    outs = [
        jax.ShapeDtypeStruct((rows, depth), f32),
        jax.ShapeDtypeStruct((depth, rows), bf16),
        jax.ShapeDtypeStruct((rows, units), bf16),
        jax.ShapeDtypeStruct((rows, units), bf16),
        jax.ShapeDtypeStruct((rows, units), bf16),
        jax.ShapeDtypeStruct((rows, depth), f32),
        jax.ShapeDtypeStruct((rows + EXTRA, depth), f32),
    ]
    unit_out = pl.BlockSpec((rows, block), lambda i: (0, i))
    return pl.pallas_call(
        forward_kernel,
        out_shape=outs,
        grid=(steps,),
        in_specs=[SCALAR]
        + [whole(array) for array in gathered]
        + [own_rows, own_rows, whole(w_out), whole(gain)]
        + [ANYWHERE] * 3,
        out_specs=[
            whole(outs[0]),
            whole(outs[1]),
            unit_out,
            unit_out,
            unit_out,
            whole(outs[5]),
            whole(outs[6]),
        ],
        scratch_shapes=[
            pltpu.VMEM((rows, depth), bf16),
            pltpu.VMEM((steps, depth, block), bf16),
            pltpu.VMEM((steps, depth, block), bf16),
            pltpu.VMEM((steps, block, depth), bf16),
            pltpu.SemaphoreType.DMA((3, steps)),
        ],
        compiler_params=params(),
        cost_estimate=cost(
            2 * rows * depth * (6 * units + w_out.shape[1]),
            2 * depth * (3 * units + w_out.shape[1]) + 22 * rows * depth,
            rows * units,
        ),
    )(level, *gathered, tokens, dout, w_out, gain, w_gate, w_up, w_down)


def hidden_grad(inner, total_ref, final_ref, hidden_ref, dout_ref, gain_ref):
    dnormed = jnp.where(inner, total_ref[...], final_ref[...])
    hidden = hidden_ref[...]
    rms = lax.rsqrt(jnp.mean(hidden * hidden, -1, keepdims=True) + norm_eps)
    scaled = dnormed * gain_ref[...]
    shift = jnp.mean(scaled * hidden, -1, keepdims=True)
    dhid = dout_ref[...].astype(jnp.float32) + (rms * scaled - hidden * (rms**3 * shift))
    return dhid, dnormed * (hidden * rms)


def backward_kernel(
    start, full, adding, steps, level_ref, total_ref, final_ref, hidden_ref, dout_ref, *refs
):
    gain_two_ref, wo_ref, q_ref = refs[:3]
    kv_here = q_ref.shape[1] // KV_WIDE
    refs = refs[3:]
    kv_refs, refs = refs[: 2 * kv_here], refs[2 * kv_here :]
    part_ref, place_ref, strip_ref, cos_ref, sin_ref = refs[:5]
    extra = (2 if full else 0) + (1 if adding else 0) + 1
    outs, scratch = refs[5 : -3 - extra], refs[-3 - extra :]
    dhid_ref, low_ref, dn_ref, sems = scratch[:4]
    if full:
        x_any, gain_one_ref, other_ref, across_ref, outer_ref, w_any = outs[:6]
        outs = outs[6:]
        x_ref, w_buffers = scratch[4:6]
        tokens_here = pltpu.make_async_copy(
            x_any.at[pl.ds(start, x_ref.shape[0]), :], x_ref, sems.at[4]
        )
    count = (5 if start > 0 else 4) if full else 2
    if adding:
        acc_any, acc_buffers = outs[0], scratch[-1]
    outs = outs[-count:]
    dhid_t_ref, dqkv_ref = outs[:2]
    if full:
        input_grad_ref, gains_ref = outs[2:4]
    rows = q_ref.shape[0]
    keys = kv_refs[0].shape[0]
    shard = pl.program_id(0)
    level = level_ref[0]
    inner = (level == 1) | (level == 2)

    def fetched(at, sums):
        source, buffers = (acc_any, acc_buffers) if sums else (w_any, w_buffers)
        lanes = buffers.shape[2]
        here = pl.ds(pl.multiple_of(at * lanes, lanes), lanes)
        slot = at % 2
        sem = sems.at[slot + 2] if sums else sems.at[slot]
        return pltpu.make_async_copy(source.at[:, here], buffers.at[slot], sem)

    def fetch(at):
        if adding:
            fetched(at, True).start()
        if full:
            fetched(at, False).start()

    @pl.when(shard == 0)
    def _():
        for at in range(min(2, steps)):
            fetch(at)
        if full:
            tokens_here.start()
        dhid, dgain = hidden_grad(
            inner, total_ref, final_ref, hidden_ref, dout_ref, gain_two_ref
        )
        dhid_ref[...] = dhid
        low = dhid.astype(jnp.bfloat16)
        low_ref[...] = low
        dhid_t_ref[...] = low.T
        if full:
            gains_ref[...] = jnp.zeros_like(gains_ref)
            gains_ref[1:2, :] = jnp.sum(dgain, 0, keepdims=True)
            dn_ref[...] = jnp.zeros_like(dn_ref)

    def rotate_back(grads):
        turned = grads * cos_ref[...] - pltpu.roll(grads, LANES // 2, 1) * sin_ref[...]
        return turned.astype(jnp.bfloat16)

    dmixed_all = dot32(low_ref[...], wo_ref[...]).astype(jnp.bfloat16)
    mixed = part_ref[...]
    if full:
        far = jnp.where(inner, across_ref[...], outer_ref[...])
        far = jnp.where(shard == 1, other_ref[...], far)
        mixed = jnp.where(shard == 0, mixed, far)
    products = dmixed_all.astype(jnp.float32) * dot_split(mixed[:rows], place_ref[...])
    causal = lax.broadcasted_iota(jnp.int32, (rows, rows), 0) <= lax.broadcasted_iota(
        jnp.int32, (rows, rows), 1
    )
    acc_ref = None
    if adding:
        fetched(shard, True).wait()
        acc_ref = acc_buffers.at[shard % 2]
    grads = []
    for kv in range(kv_here):
        key_ref, value_ref = kv_refs[2 * kv : 2 * kv + 2]
        heads = range(kv * GROUP, (kv + 1) * GROUP)
        lanes = {h: slice(h * LANES, (h + 1) * LANES) for h in heads}
        row_dots = {h: jnp.sum(products[:, lanes[h]].T, axis=0, keepdims=True) for h in heads}
        log_sums = {h: mixed[rows + h : rows + h + 1, :rows] for h in heads}
        dqueries = dict.fromkeys(heads)
        here = slice(2 * kv * LANES, (2 * kv + 1) * LANES)
        there = slice((2 * kv + 1) * LANES, (2 * kv + 2) * LANES)
        for tile in range(keys // rows):
            span = slice(tile * rows, (tile + 1) * rows)
            key = key_ref[span, :]
            value = value_ref[span, :]
            key_t = key.T
            dkey = None if acc_ref is None else acc_ref[span, here]
            dvalue = None if acc_ref is None else acc_ref[span, there]
            last = tile * rows == start
            for h in heads:
                at = kv * KV_WIDE + (h % GROUP) * LANES
                query = q_ref[:, at : at + LANES]
                dmixed = dmixed_all[:, lanes[h]]
                raw = dot32_nt(key, query)
                probs = jnp.exp2(raw * score_scale_log2 - log_sums[h])
                if last:
                    probs = jnp.where(causal, probs, 0.0)
                dprobs = dot32_nt(value, dmixed)
                dscores = (probs * (dprobs - row_dots[h])).astype(jnp.bfloat16)
                dquery = dot32(key_t, dscores)
                dqueries[h] = dquery if dqueries[h] is None else dqueries[h] + dquery
                dkey_one = dot32(dscores, query)
                dvalue_one = dot32(probs.astype(jnp.bfloat16), dmixed)
                dkey = dkey_one if dkey is None else dkey + dkey_one
                dvalue = dvalue_one if dvalue is None else dvalue + dvalue_one
            if full and not last:
                outs[4][span, here] = dkey
                outs[4][span, there] = dvalue
        grads += [rotate_back(dqueries[h].T * score_scale) for h in heads]
        grads.append(rotate_back(dkey * score_scale))
        grads.append(dvalue.astype(jnp.bfloat16))
    grads = jnp.concatenate(grads, 1)
    if full:
        fetched(shard, False).wait()
        dn_ref[...] += dot32_nt(grads, w_buffers[shard % 2])

        @pl.when(shard + 2 < steps)
        def _():
            fetch(shard + 2)

    @pl.when(shard == 0)
    def _():
        wide = strip_ref.shape[1]
        for kv in range(kv_here):
            dqkv_ref[:, kv * wide : (kv + 1) * wide] = dot32(
                grads[:, kv * KV_WIDE : (kv + 1) * KV_WIDE], strip_ref[...]
            ).astype(jnp.bfloat16)

    if not full:
        return

    @pl.when(shard == pl.num_programs(0) - 1)
    def _():
        tokens_here.wait()
        dnormed = dn_ref[...]
        inputs = x_ref[...].astype(jnp.float32)
        rms = lax.rsqrt(jnp.mean(inputs * inputs, -1, keepdims=True) + norm_eps)
        scaled = dnormed * gain_one_ref[...]
        shift = jnp.mean(scaled * inputs, -1, keepdims=True)
        grad = dhid_ref[...] + (rms * scaled - inputs * (rms**3 * shift))
        input_grad_ref[...] = grad.astype(jnp.bfloat16)
        gains_ref[0:1, :] = jnp.sum(dnormed * (inputs * rms), 0, keepdims=True)


def backward_chunk(
    level, sums_two, hidden, dout, tokens, gains, weights, qkv, gathered, places, tables, acc,
    index, rows, full=True, grad_into=None
):
    start = index * rows
    keys = start + rows
    depth = tokens.shape[1]
    out_pad, qkv_pad = weights
    place_out, strip = places
    far_rows, width = gathered[0].shape
    out_wide = place_out.shape[1]
    kv_here = out_wide // (GROUP * LANES)
    wide = kv_here * KV_WIDE
    levels = qkv.shape[1] // wide
    own_rows = pl.BlockSpec((rows, depth), lambda t: (index, 0))
    table = pl.BlockSpec((rows, LANES), lambda t: (index, 0))
    gains = [gain[None, :] for gain in gains]
    key_value = lambda at: pl.BlockSpec(
        (keys, LANES), lambda t: (0, (wide // LANES) * t + at)
    )
    across = pl.BlockSpec((far_rows, width), lambda t: (0, jnp.where(t == 2, 1, 0)))
    outer = pl.BlockSpec((far_rows, width), lambda t: (0, jnp.where(t == 3, 1, 0)))
    in_specs = [
        SCALAR,
        whole(hidden),
        whole(hidden),
        whole(hidden),
        own_rows,
        whole(gains[1]),
        pl.BlockSpec((depth, out_wide), lambda t: (0, t)),
        pl.BlockSpec((rows, wide), lambda t: (index, t)),
    ]
    for kv in range(kv_here):
        at = kv * (KV_WIDE // LANES) + GROUP
        in_specs += [key_value(at), key_value(at + 1)]
    in_specs += [
        whole(gathered[0]),
        whole(place_out),
        whole(strip),
        table,
        table,
    ]
    args = [level, *sums_two, hidden, dout, gains[1], out_pad]
    args += [qkv] * (1 + 2 * kv_here)
    args += [gathered[0], place_out, strip, *tables]
    sums_wide = 2 * kv_here * LANES
    if full:
        in_specs += [ANYWHERE, whole(gains[0]), whole(gathered[1]), across, outer]
        in_specs.append(ANYWHERE)
        args += [tokens, gains[0], *gathered[1:], qkv_pad]
    if acc is not None:
        in_specs.append(ANYWHERE)
        args.append(acc)
    f32, bf16 = jnp.float32, jnp.bfloat16
    outs = [
        jax.ShapeDtypeStruct((depth, rows), bf16),
        jax.ShapeDtypeStruct((rows, kv_here * strip.shape[1]), bf16),
        jax.ShapeDtypeStruct(tokens.shape, bf16),
        jax.ShapeDtypeStruct((8, depth), f32),
    ]
    outs = outs if full else outs[:2]
    out_specs = [whole(out) for out in outs]
    aliases = {}
    if full:
        out_specs[2] = own_rows
        if grad_into is not None:
            aliases = {len(args): 2}
            in_specs.append(ANYWHERE)
            args.append(grad_into)
    if full and start > 0:
        outs.append(jax.ShapeDtypeStruct((start, levels * sums_wide), f32))
        out_specs.append(pl.BlockSpec((start, sums_wide), lambda t: (0, t)))
    steps = levels if full else 1
    scratch = [
        pltpu.VMEM((rows, depth), f32),
        pltpu.VMEM((rows, depth), bf16),
        pltpu.VMEM((rows, depth), f32),
        pltpu.SemaphoreType.DMA((5,)),
    ]
    if full:
        scratch += [pltpu.VMEM((rows, depth), bf16), pltpu.VMEM((2, depth, wide), bf16)]
    if acc is not None:
        scratch.append(pltpu.VMEM((min(2, steps), keys, sums_wide), f32))
    results = pl.pallas_call(
        functools.partial(backward_kernel, start, full, acc is not None, steps),
        out_shape=outs,
        grid=(steps,),
        input_output_aliases=aliases,
        in_specs=in_specs,
        out_specs=out_specs,
        scratch_shapes=scratch,
        compiler_params=params(),
        cost_estimate=cost(
            levels * rows * (20 * kv_here * keys * LANES + 2 * depth * (out_wide + wide)),
            2 * depth * levels * (out_wide + wide) + 16 * rows * depth,
            levels * kv_here * GROUP * rows * keys,
        ),
    )(*args)
    return results[:4], (results[4] if full and start > 0 else None)


def rows_kernel(lefts, groups, adding, picked, together, side_ref, *refs):
    refs = list(refs)
    held_ref = refs.pop()
    out_refs = refs[-len(picked) :]
    refs = refs[: -len(picked)]
    recv_ref = refs.pop() if adding else None
    step = pl.program_id(0)
    left_refs = []
    for count in lefts:
        left_refs.append(refs[:count])
        refs = refs[count:]
    rights = []
    for _ in groups:
        rights.append(refs[:CHUNKS])
        refs = refs[CHUNKS:]
    rows = left_refs[0][0].shape[0]
    blocks = held_ref.shape[1] // rows

    @pl.when(step == 0)
    def _():
        for which, pieces in enumerate(left_refs):
            for n, ref in enumerate(pieces):
                m, j = n % blocks, n // blocks
                wide = ref.shape[1]
                held_ref[which, m * rows : (m + 1) * rows, j * wide : (j + 1) * wide] = ref[...]

    chunk = held_ref.shape[2] // CHUNKS
    whole_columns = slice(0, out_refs[0].shape[1])

    def give(group, left, columns):
        right = jnp.concatenate([ref[:chunk, :].astype(jnp.bfloat16) for ref in group], 0)
        total = dot32(held_ref[left], right)
        if recv_ref is not None:
            total = total + recv_ref[:, columns]
        for out_ref, parts in zip(out_refs, picked):
            at = 0
            for start, size in parts:
                out_ref[at : at + size, columns] = total[start : start + size]
                at += size

    begin = 0
    for group, (left, first, steps) in zip(rights, groups):
        if together:
            width = group[0].shape[1]
            give(group, left, slice(begin, begin + width))
            begin += width
        else:

            @pl.when((step >= first) & (step < first + steps))
            def _(group=group, left=left):
                give(group, left, whole_columns)


def rows_of(
    lefts, groups, side, rows, blocks, step, recv=None, picked=None, vmem=LATE_VMEM_BYTES
):
    if picked is None:
        picked = [[(0, rows * blocks)]]
    at = lambda m: lambda i, side: ((m ^ side[2]) * side[1] + side[0], 0)
    specs = []
    args = []
    counts = []
    for left in lefts:
        pieces = left if isinstance(left, list) else [left]
        counts.append(len(pieces) * blocks)
        for piece in pieces:
            for m in range(blocks):
                specs.append(pl.BlockSpec((rows, piece.shape[1]), at(m)))
                args.append(piece)
    tokens = sum(piece.shape[1] for piece in pieces)
    first = 0
    plan = []
    together = step is None
    for which, rights in groups:
        if together:
            plan.append((which, 0, 1))
            specs += [whole(right) for right in rights]
            args += rights
            first += rights[0].shape[1]
            continue
        steps = rights[0].shape[1] // step
        plan.append((which, first, steps))
        for right in rights:
            pick = lambda i, side, first=first, steps=steps: (0, jnp.clip(i - first, 0, steps - 1))
            specs.append(pl.BlockSpec((right.shape[0], step), pick))
            args.append(right)
        first += steps
    if together:
        first, step = 1, first
    total = first * step
    block = lambda height: pl.BlockSpec((height, step), lambda i, side: (0, i))
    if recv is not None:
        specs.append(block(rows * blocks))
        args.append(recv)
    heights = [sum(size for _, size in parts) for parts in picked]
    results = pl.pallas_call(
        functools.partial(rows_kernel, counts, plan, recv is not None, picked, together),
        out_shape=[jax.ShapeDtypeStruct((height, total), jnp.float32) for height in heights],
        grid_spec=pltpu.PrefetchScalarGridSpec(
            num_scalar_prefetch=1,
            grid=(first,),
            in_specs=specs,
            out_specs=[block(height) for height in heights],
            scratch_shapes=[pltpu.VMEM((len(lefts), rows * blocks, tokens), jnp.bfloat16)],
        ),
        compiler_params=params(vmem),
        cost_estimate=cost(
            2 * rows * blocks * tokens * total,
            4 * rows * blocks * total + 2 * tokens * (total + rows * blocks),
        ),
    )(side, *args)
    return results[0] if len(picked) == 1 else results


def finish_kernel(*refs):
    query_ref, key_ref, value_ref, out_ref = refs[4:]
    kv_here = key_ref.shape[1] // HD
    q_cols = out_ref.shape[1]
    for at in range(2):
        kept_ref, far_ref = refs[2 * at : 2 * at + 2]
        half = far_ref.shape[0]
        sums = kept_ref[...] + far_ref[...]
        here = slice(at * half, (at + 1) * half)
        out_ref[here, :] = sums[:, :q_cols]
        start = q_cols
        cut = [[], [], []]
        for kv in range(kv_here):
            for i, width in enumerate((GROUP * HD, HD, HD)):
                cut[i].append(sums[:, start : start + width])
                start += width
        for ref, pieces in zip((query_ref, key_ref, value_ref), cut):
            ref[here, :] = jnp.concatenate(pieces, 1)


def finish(one, far_one, two, far_two, kv_here):
    half, columns = far_one.shape
    first = pl.BlockSpec((half, columns), lambda i: (0, 0))
    q_cols = kv_here * GROUP * HD
    outs = [
        jax.ShapeDtypeStruct((2 * half, width), jnp.float32)
        for width in (q_cols, kv_here * HD, kv_here * HD, q_cols)
    ]
    return pl.pallas_call(
        finish_kernel,
        out_shape=outs,
        grid=(1,),
        in_specs=[first] * 4,
        out_specs=[whole(out) for out in outs],
        compiler_params=params(LATE_VMEM_BYTES),
        cost_estimate=cost(4 * half * columns, 32 * half * columns),
    )(one, far_one, two, far_two)


def shards(
    tokens,
    lengths,
    positions,
    cotangent,
    norm_gain,
    w_query,
    w_key,
    w_value,
    w_out,
    mlp_gain,
    w_gate,
    w_up,
    w_down,
):
    seq_rows, depth = tokens.shape
    chips = lax.axis_size("chip")
    dp = chips * 2
    tp = lax.axis_size("tp")
    chip = lax.axis_index("chip")
    core = lax.axis_index("core")
    level = lax.axis_index("tp")
    low = level < 2
    inner = (level == 1) | (level == 2)
    heads_here = w_query.shape[1] // HD
    kv_here = w_key.shape[1] // HD
    rows = seq_rows // CHUNKS
    slice_rows = depth // dp
    level_ref = level.astype(jnp.int32).reshape(1)
    by_hand = dp == 8
    swap = lambda array: lax.ppermute(array, "core", [(0, 1), (1, 0)])
    to_level = lambda array, s: along(array, [(t, t ^ s) for t in range(tp)])

    at_row = (chip * 2 + core) * slice_rows
    cols = lambda w: lax.dynamic_slice_in_dim(w, at_row, slice_rows, 1).astype(jnp.float32).T
    (out_slice,) = fence(cols(w_out))
    qkv_slice = jnp.concatenate(
        [
            lax.dynamic_slice_in_dim(w_query, at_row, slice_rows, 0).astype(jnp.float32),
            cols(w_key.T),
            cols(w_value.T),
        ],
        1,
    )
    out_slice, qkv_slice = fence(out_slice, qkv_slice)
    out_near = along(out_slice, PAIRS)
    qkv_near = along(qkv_slice, PAIRS)
    meta = jnp.stack([chip, core]).astype(jnp.int32)

    pq = place_query(heads_here)
    pkv = place_key_value(kv_here)
    p_all = place_all(heads_here, kv_here)
    strip_one = place_all(GROUP, 1).T
    p_out = place_plain(heads_here)
    strip_out = p_out.T

    half_dim = HD // 2
    freqs = rope_base ** (-(jnp.arange(half_dim).astype(jnp.float32) * 2.0 / HD))
    freqs = jnp.pad(freqs, (0, LANES // 2 - half_dim))
    angles = positions.astype(jnp.float32)[:, None] * jnp.concatenate([freqs, freqs])[None, :]
    cosines = jnp.cos(angles)
    sines = jnp.sin(angles) * jnp.where(jnp.arange(LANES) < LANES // 2, -1.0, 1.0)

    cosines, sines, out_near = fence(cosines, sines, out_near)
    out_across = along(jnp.stack([out_slice, out_near]), MIDDLE)
    qkv_own, normed_one, own_pad = start(
        tokens, norm_gain, w_query, w_key.T, w_value.T, pq, pkv, cosines, sines
    )

    def far_slices(near, across, outer):
        return jnp.stack(
            [
                near,
                jnp.where(inner, across[1], outer[0]),
                jnp.where(inner, across[0], outer[1]),
            ]
        )

    order = list(reversed(range(CHUNKS)))
    c0, c1, c2, c3 = order
    own, other, across, outer = {}, {}, {}, {}
    part, total, final = {}, {}, {}

    def hop_1(j):
        other[j] = along(own[j], PAIRS)

    def hop_2(j):
        across[j] = along(jnp.concatenate([own[j], other[j]], 1), MIDDLE)

    def hop_3(j):
        outer[j] = along(across[j], OUTWARD)

    coming = {}

    def add_1(j):
        coming[j] = along(part[j], INWARD)

    def add_2(j):
        total[j] = part[j][:rows] + coming[j][:rows]
        coming[j] = along(total[j], MIDDLE)

    def add_3(j, inward, extra=0):
        both = jnp.where(inner, total[j] + coming[j], inward)
        total[j] = jnp.pad(both, ((0, extra), (0, 0)))
        final[j] = along(total[j], PAIRS)
        return final[j]

    def to_chip(array, m):
        return lax.ppermute(array, "chip", [(i, i ^ m) for i in range(chips)])

    def over_chips_1(piece):
        cut = piece.shape[1] // 2
        one, two = piece[:, :cut], piece[:, cut:]
        return jnp.stack([one, to_chip(one, 1)]), jnp.stack([two, to_chip(two, 2)])

    def over_chips_2(one, two):
        return one, to_chip(one, 2), two, to_chip(two, 1)

    def over_chips_3(one, one_far, two, two_far):
        upper = jnp.stack([one[0], one[1], one_far[0], one_far[1]])
        lower = jnp.stack([two[0], two_far[0], two[1], two_far[1]])
        return jnp.concatenate([upper, lower], 2)

    qkv_own, out_across, qkv_near = fence(qkv_own, out_across, qkv_near)
    out_outer = along(out_across, OUTWARD)
    qkv_across = along(jnp.stack([qkv_slice, qkv_near]), MIDDLE)
    own[c0] = attend(lengths, qkv_own, strip_out, c0, rows)
    own[c1] = attend(lengths, qkv_own, strip_out, c1, rows)
    own, qkv_own, out_outer = fence(own, qkv_own, out_outer)
    others = along(jnp.concatenate([own[c0], own[c1]], 0), PAIRS)
    out_far = far_slices(out_near, out_across, out_outer)
    out_mine = over_chips_1(out_far) if by_hand else out_far
    own[c2] = attend(lengths, qkv_own, strip_out, c2, rows)
    own[c3] = attend(lengths, qkv_own, strip_out, c3, rows)
    own[c3], qkv_across = fence(own[c3], qkv_across)
    qkv_outer = along(qkv_across, OUTWARD)
    own, others, normed_one, w_out, out_mine = fence(own, others, normed_one, w_out, out_mine)
    other[c0], other[c1] = others[: rows + EXTRA], others[rows + EXTRA :]
    if by_hand:
        out_mine = over_chips_2(*out_mine)
    else:
        out_mine = lax.all_gather(out_mine, ("chip", "core"))
    hop_2(c0)
    dout, dout_t, normed_one_t = turn(lengths, cotangent, normed_one)
    w_out_t = w_out.T
    own, other, across, dout, dout_t, normed_one_t, w_out_t, out_mine, qkv_outer = fence(
        own, other, across, dout, dout_t, normed_one_t, w_out_t, out_mine, qkv_outer
    )
    hop_1(c2)
    hop_3(c0)
    hop_2(c1)
    qkv_far = lax.all_gather(far_slices(qkv_near, qkv_across, qkv_outer), ("chip", "core"))
    if by_hand:
        out_mine = over_chips_3(*out_mine)
        out_theirs = swap(out_mine)
        out_pad, out_plain = spread(
            spread_out_kernel,
            meta,
            w_out_t,
            [p_out],
            out_mine,
            out_theirs,
            [4 * p_out.shape[1], 4 * p_out.shape[0]],
        )
    else:
        plain = [w_out_t] + [
            out_mine[:, s].reshape(depth, -1).astype(jnp.bfloat16) for s in range(tp - 1)
        ]
        out_plain = jnp.concatenate(plain, 1)
        out_pad = jnp.concatenate([dot32(w, p_out).astype(jnp.bfloat16) for w in plain], 1)
    hidden, normed_t, activ, dgate, dup, mlp_part = {}, {}, {}, {}, {}, {}

    def feed(j):
        gathered = (own[j], other[j], across[j], outer[j])
        (hidden[j], normed_t[j], activ[j], dgate[j], dup[j], mlp_part[j], part[j]) = forward_chunk(
            level_ref, gathered, tokens, dout, out_plain, mlp_gain, w_gate, w_up, w_down, j, rows
        )

    own, other, across, outer, out_pad, out_plain = fence(
        own, other, across, outer, out_pad, out_plain
    )
    hop_1(c3)
    hop_3(c1)
    hop_2(c2)
    feed(c0)
    part, other = fence(part, other)
    add_1(c0)
    own, other, across, outer, part, hidden = fence(own, other, across, outer, part, hidden)
    hop_3(c2)
    hop_2(c3)
    feed(c1)
    qkv_far, hidden[c1] = fence(qkv_far, hidden[c1])
    qkv_pad = spread_qkv(own_pad, pq, pkv, qkv_far)
    own, other, across, outer, part, total, coming, hidden, qkv_pad = fence(
        own, other, across, outer, part, total, coming, hidden, qkv_pad
    )
    add_1(c1)
    hop_3(c3)
    add_2(c0)
    feed(c2)
    qkv_pad, hidden[c2] = fence(qkv_pad, hidden[c2])
    qkv = project(normed_one, qkv_pad, cosines, sines, qkv_own)
    own, other, across, outer, part, total, coming, hidden, qkv = fence(
        own, other, across, outer, part, total, coming, hidden, qkv
    )
    coming[c2] = add_3(c0, part[c2][:rows])
    add_2(c1)
    feed(c3)

    listed = lambda pieces: [pieces[j] for j in range(CHUNKS)]
    keep_side = jnp.stack([core, 2, 0]).astype(jnp.int32)
    keep_turned = jnp.stack([core, 2, chip]).astype(jnp.int32)
    send_side = jnp.stack([1 - core, 2, 0]).astype(jnp.int32)
    send_turned = jnp.stack([1 - core, 2, chip]).astype(jnp.int32)
    all_rows = jnp.array([0, 1, 0], jnp.int32)

    def send_rows(lefts, groups, step, side=send_side):
        if not by_hand:
            return rows_of(lefts, groups, all_rows, depth // 4, 4, step)
        return rows_of(lefts, groups, side, slice_rows, chips, step)

    def keep_rows(lefts, groups, received, step, side=keep_side, picked=None):
        if not by_hand:
            return received
        return rows_of(lefts, groups, side, slice_rows, chips, step, received, picked)

    def swap_rows(array):
        return swap(array) if by_hand else array

    def scatter(array, axes):
        return lax.psum_scatter(array, axes, scatter_dimension=0, tiled=True)

    units = w_gate.shape[1]
    mlp_args = (
        [listed(normed_t), dout_t],
        [(0, listed(dgate)), (0, listed(dup)), (1, listed(activ))],
    )
    acc = None
    input_grad = None
    dhid_t, dqkv_own, gains = {}, {}, {}

    def back(j):
        nonlocal acc, input_grad
        (dhid_t[j], dqkv_own[j], input_grad, gains[j]), acc = back_some(j, True)

    def back_own(j):
        return back_some(j, False)[0]

    def back_some(j, full):
        return backward_chunk(
            level_ref,
            (total[j], final[j]),
            hidden[j],
            dout,
            tokens,
            (norm_gain, mlp_gain),
            (out_pad, qkv_pad),
            qkv,
            (own[j], other[j], across[j], outer[j]),
            (p_out, strip_one),
            (cosines, sines),
            acc,
            j,
            rows,
            full,
            input_grad,
        )

    grad_mlp = rows_of(
        *mlp_args, all_rows, depth // 4, 4, units // 2, vmem=VMEM_BYTES
    )
    own, other, across, outer, part, total, coming, final, hidden, grad_mlp = fence(
        own, other, across, outer, part, total, coming, final, hidden, grad_mlp
    )
    grad_mlp = scatter(grad_mlp, ("chip", "core"))
    coming[c3] = add_3(c1, part[c3][:rows])
    add_2(c2)
    back(c0)

    near = lambda: jnp.where(low, mlp_part[1], mlp_part[2])
    edge = lambda: jnp.where(low, mlp_part[0], mlp_part[3])
    leave_far = lambda: jnp.where(low, mlp_part[3], mlp_part[0])
    leave_near = lambda: jnp.where(low, mlp_part[2], mlp_part[1])
    total, coming, final, hidden, mlp_part, acc, dhid_t = fence(
        total, coming, final, hidden, mlp_part, acc, dhid_t
    )
    far_sum = add_3(c2, leave_far())
    add_2(c3)
    back(c1)
    total, coming, final, hidden, mlp_part, far_sum, acc, dhid_t = fence(
        total, coming, final, hidden, mlp_part, far_sum, acc, dhid_t
    )
    add_3(c3, leave_near(), EXTRA)
    far_in = along(leave_far() + far_sum, MIDDLE)
    back(c2)
    total, final, hidden, acc, dhid_t = fence(total, final, hidden, acc, dhid_t)
    dhid_t[c3], dqkv_own[c3] = back_own(c3)
    dhid_t, dqkv_own, far_in, mlp_part, final = fence(
        dhid_t, dqkv_own, far_in, mlp_part, final
    )
    last = along(jnp.where(inner, edge() + far_in, near()), PAIRS)
    near_in = along(leave_near() + final[c3][:rows], MIDDLE)
    q_cols = heads_here * HD
    attn_args = (
        [listed(dhid_t), normed_one_t],
        [(0, listed(own)), (1, listed(dqkv_own))],
    )
    sent = swap_rows(send_rows(*attn_args, None, send_turned))
    total, final, hidden, acc, sent = fence(total, final, hidden, acc, sent)
    if by_hand:
        half = slice_rows // 2
        upper = lambda m: (m * slice_rows, half)
        lower = lambda m: (m * slice_rows + half, half)
        picked = [
            [upper(1), upper(3)],
            [upper(0), upper(2)],
            [lower(2), lower(3)],
            [lower(0), lower(1)],
        ]
        pieces = keep_rows(*attn_args, sent, None, keep_turned, picked)
        pieces, hidden = fence(pieces, hidden)
        one_away, one, two_away, two = pieces
        pieces = (one, to_chip(one_away, 1), two, to_chip(two_away, 2))
    else:
        pieces = scatter(sent, ("chip", "core"))
    back(c3)
    pieces, gains, input_grad = fence(pieces, gains, input_grad)
    gain_sums = gains[0] + gains[1] + gains[2] + gains[3]
    gain_sums = gain_sums + swap(gain_sums)
    gain_sums, last, near_in = fence(gain_sums, last, near_in)
    mlp_rows = jnp.where(inner, near() + near_in, edge()) + last
    hidden_rows = jnp.where(
        low,
        jnp.where(level == 0, hidden[0], hidden[1]),
        jnp.where(level == 2, hidden[2], hidden[3]),
    )
    layer_out = (hidden_rows + mlp_rows).astype(jnp.bfloat16)
    mlp_grads = [grad_mlp[:, at * units : (at + 1) * units] for at in range(3)]
    if by_hand:
        one = pieces[0] + pieces[1]
        two = pieces[2] + pieces[3]
        far_one = to_chip(one[half:], 2)
        far_two = to_chip(two[half:], 1)
        others = [to_chip(gain_sums, m) for m in range(1, chips)]
        far_one, far_two, mlp_grads, layer_out = fence(far_one, far_two, mlp_grads, layer_out)
        attn_grads = finish(one, far_one, two, far_two, kv_here)
        others, attn_grads = fence(others, attn_grads)
        gain_sums = sum(others, gain_sums)
    else:
        gain_sums = lax.psum(gain_sums, "chip")
        grad_qkv = pieces[:, q_cols:]
        one = strip_one.shape[1]
        picked = lambda at, width: jnp.concatenate(
            [grad_qkv[:, kv * one + at : kv * one + at + width] for kv in range(kv_here)], 1
        )
        attn_grads = (
            picked(0, GROUP * HD),
            picked(GROUP * HD, HD),
            picked((GROUP + 1) * HD, HD),
            pieces[:, :q_cols],
        )
    gain_rows = lax.dynamic_slice_in_dim(gain_sums, at_row, slice_rows, 1)
    grad_query, grad_key, grad_value, grad_out_t = attn_grads
    return (
        layer_out,
        input_grad,
        gain_rows[0],
        grad_query,
        grad_key,
        grad_value,
        grad_out_t.T,
        gain_rows[1],
        mlp_grads[0],
        mlp_grads[1],
        mlp_grads[2].T,
    )


def solution(mesh):
    devices = mesh.devices
    dp, tp = devices.shape
    split = Mesh(devices.reshape(dp // 2, 2, tp), ("chip", "core", "tp"))
    data = ("chip", "core")
    return jax.shard_map(
        shards,
        mesh=split,
        in_specs=(
            P(data, None),
            P(data),
            P(data),
            P(data, None),
            P(),
            P(None, "tp"),
            P(None, "tp"),
            P(None, "tp"),
            P("tp", None),
            P(),
            P(None, "tp"),
            P(None, "tp"),
            P("tp", None),
        ),
        out_specs=(
            P(("chip", "core", "tp"), None),
            P(data, None),
            P(data),
            P(data, "tp"),
            P(data, "tp"),
            P(data, "tp"),
            P("tp", data),
            P(data),
            P(data, "tp"),
            P(data, "tp"),
            P("tp", data),
        ),
        check_vma=False,
    )
```
